32 devices in a mesh: dp: 8 (over y, x, core), tensor: 4 (over z).
Axes of the slice: x: 2, y: 2, z: 4, core: 2. Of those that a mesh axis runs over, the one named last changes fastest.
Arguments:
- tokens: bfloat16 [4096, 2048], P(('dp', 'tensor')), may hold values from -6 to 6
- picture_ids: int32 [4096], P('dp'), may hold values from 0 to 1, as said below
- routes: int32 [4096, 4], P('dp'), may hold values from 0 to 7, as said below
- slot_order: int32 [4096, 4], P('dp'), may hold values from 0 to 319, as said below
- norm_gains: bfloat16 [2, 2048], P(None, ('dp', 'tensor')), may hold values from 0.5 to 1.5
- w_query: bfloat16 [2048, 2048], P('dp', 'tensor'), may hold values from -0.125 to 0.125
- w_key: bfloat16 [2048, 2048], P('dp', 'tensor'), may hold values from -0.125 to 0.125
- w_value: bfloat16 [2048, 2048], P('dp', 'tensor'), may hold values from -0.125 to 0.125
- w_out: bfloat16 [2048, 2048], P('tensor', 'dp'), may hold values from -0.75 to 0.75
- qkv_bias: bfloat16 [3, 16, 128], P(None, 'tensor', 'dp'), may hold values from -3 to 3
- router: bfloat16 [2048, 9], P('dp'), may hold values from -0.06591797 to 0.06591797
- shared_gate: bfloat16 [2048, 5632], P('dp', 'tensor'), may hold values from -0.125 to 0.125
- shared_up: bfloat16 [2048, 5632], P('dp', 'tensor'), may hold values from -0.125 to 0.125
- shared_down: bfloat16 [5632, 2048], P('tensor', 'dp'), may hold values from -0.21875 to 0.21875
- expert_gate: bfloat16 [8, 2048, 1408], P(None, 'dp', 'tensor'), may hold values from -0.125 to 0.125
- expert_up: bfloat16 [8, 2048, 1408], P(None, 'dp', 'tensor'), may hold values from -0.125 to 0.125
- expert_down: bfloat16 [8, 1408, 2048], P(None, 'tensor', 'dp'), may hold values from -0.625 to 0.625
- out_grad: bfloat16 [4096, 2048], P(('dp', 'tensor')), may hold values from -6 to 6
Outputs:
- output: bfloat16 [4096, 2048], P(('dp', 'tensor'))
- input_grad: bfloat16 [4096, 2048], P(('dp', 'tensor'))
- gains_grad: float32 [2, 2048], P(None, ('dp', 'tensor'))
- query_grad: float32 [2048, 2048], P('dp', 'tensor')
- key_grad: float32 [2048, 2048], P('dp', 'tensor')
- value_grad: float32 [2048, 2048], P('dp', 'tensor')
- out_proj_grad: float32 [2048, 2048], P('tensor', 'dp')
- bias_grad: float32 [3, 16, 128], P(None, 'tensor', 'dp')
- router_grad: float32 [2048, 9], P('dp')
- shared_gate_grad: float32 [2048, 5632], P('dp', 'tensor')
- shared_up_grad: float32 [2048, 5632], P('dp', 'tensor')
- shared_down_grad: float32 [5632, 2048], P('tensor', 'dp')
- expert_gate_grad: float32 [8, 2048, 1408], P(None, 'dp', 'tensor')
- expert_up_grad: float32 [8, 2048, 1408], P(None, 'dp', 'tensor')
- expert_down_grad: float32 [8, 1408, 2048], P(None, 'tensor', 'dp')
The draws below stay inside these ranges and needn't reach their ends.
Inputs may be any that keep to these rules, and one draw needn't show every extreme that they name: `picture_ids`: each sequence of 512 tokens holds exactly one run of 256 consecutive tokens numbered 1; all its other tokens are 0. `routes`: each token names 4 different experts. Within one sequence no expert is named by more than 320 tokens, and one expert by exactly 320. Within one sequence, the tokens that name an expert hold its slots 0 to one less than their number, each once; slot_order[t, k] belongs to the expert routes[t, k].
All inputs are finite; a program needn't handle non-finite values.
Results may differ from the reference program's by a relative error of at most 0.029.
Values may be sent and summed in bfloat16 or wider, within the bound.
A program may use at most 320 MiB of HBM per device.

```python
import jax
import jax.numpy as jnp
from jax import lax

D = 2048
H = 16
HD = 128
FFE = 1408
FFS = 5632
E = 8
K = 4
PIECE = 256
SEQ = 512
TOKENS = 4096
CAP = 320


def route_table(key):
    sequences = TOKENS // SEQ

    def one_sequence(seq_key):
        busy_key, turn_key, flag_key, order_key = jax.random.split(seq_key, 4)
        busiest = jax.random.randint(busy_key, (), 0, E)
        rotation = jax.random.randint(turn_key, (), 0, E - 1)
        flag_order = jax.random.permutation(flag_key, SEQ)
        position = jnp.zeros((SEQ,), jnp.int32).at[flag_order].set(jnp.arange(SEQ, dtype=jnp.int32))
        flagged = position < CAP
        first_pick = jnp.where(flagged, position * (K - 1) % (E - 1), (position - CAP) * K % (E - 1))
        column = jnp.arange(K, dtype=jnp.int32)
        offset = jnp.where(flagged[:, None], first_pick[:, None] + column[None, :] - 1, first_pick[:, None] + column[None, :])
        others = (busiest + 1 + (offset + rotation) % (E - 1)) % E
        chosen = jnp.where(jnp.logical_and(flagged[:, None], column[None, :] == 0), busiest, others).astype(jnp.int32)
        ranking = jax.random.permutation(order_key, SEQ)
        counts = jnp.sum((chosen[:, :, None] == jnp.arange(E, dtype=jnp.int32)[None, None, :]).astype(jnp.int32), axis=1)
        ordered = counts[ranking]
        before = jnp.cumsum(ordered, axis=0) - ordered
        slot_table = jnp.zeros((SEQ, E), jnp.int32).at[ranking].set(before)
        slot_ids = jnp.take_along_axis(slot_table, chosen, axis=1)
        return (chosen, slot_ids)
    chosen, slot_ids = jax.vmap(one_sequence)(jax.random.split(key, sequences))
    return (chosen.reshape(TOKENS, K).astype(jnp.int32), slot_ids.reshape(TOKENS, K).astype(jnp.int32))


def draw_routes(key, part):
    chosen, slot_ids = route_table(key)
    return chosen


def draw_slot_order(key, part):
    chosen, slot_ids = route_table(key)
    return slot_ids


def draw_picture_ids(key, part):
    key = jax.random.fold_in(key, 5)
    sequences = TOKENS // SEQ
    offsets = jax.random.randint(key, (sequences,), 0, SEQ - PIECE + 1)
    position = jnp.arange(SEQ, dtype=jnp.int32)
    inside = jnp.logical_and(position[None, :] >= offsets[:, None], position[None, :] < offsets[:, None] + PIECE)
    return inside.astype(jnp.int32).reshape(TOKENS)


def steps_of(rng, extent, cuts, low, top_value):
    loudness = 1.0
    for dim, shards_of in cuts:
        steps = jax.random.uniform(jax.random.fold_in(jax.random.fold_in(rng, 6), dim), (shards_of,), jnp.float32, low / len(cuts), top_value / len(cuts))
        loudness = loudness * jnp.repeat(jnp.exp(steps), extent[dim] // shards_of).reshape((-1,) + (1,) * (len(extent) - 1 - dim))
    return loudness


def bell_draw(rng, dims, scale, most, pieces=(), held_as=jnp.bfloat16):
    entries = scale * jax.random.normal(rng, dims, jnp.float32)
    if pieces:
        entries = entries * steps_of(rng, dims, pieces, -0.22, 0.18)
    return jnp.clip(entries, -most, most).astype(held_as)


def setup_inputs(seed: int = 0) -> dict:
    splits = jax.random.split(jax.random.key(seed), 19)
    return {
        "tokens": bell_draw(splits[0], (TOKENS, D), 1.0, 6.0, ((0, 32),)),
        "picture_ids": draw_picture_ids(jax.random.fold_in(splits[18], 71), 0),
        "routes": draw_routes(jax.random.fold_in(splits[18], 71), 0),
        "slot_order": draw_slot_order(jax.random.fold_in(splits[18], 71), 0),
        "norm_gains": jnp.clip(1.0 + 0.1 * jax.random.normal(splits[4], (2, D), jnp.float32), 0.5, 1.5).astype(jnp.bfloat16),
        "w_query": bell_draw(splits[5], (D, H * HD), D ** -0.5, 0.125, ((0, 8), (1, 4))),
        "w_key": bell_draw(splits[6], (D, H * HD), D ** -0.5, 0.125, ((0, 8), (1, 4))),
        "w_value": bell_draw(splits[7], (D, H * HD), D ** -0.5, 0.125, ((0, 8), (1, 4))),
        "w_out": bell_draw(splits[8], (H * HD, D), (H * HD // 32) ** -0.5, 0.75, ((0, 4), (1, 8))),
        "qkv_bias": bell_draw(splits[9], (3, H, HD), 0.5, 3.0, ((1, 4), (2, 8))),
        "router": bell_draw(splits[10], (D, E + 1), 0.011, 0.06591797, ((0, 8),)),
        "shared_gate": bell_draw(splits[11], (D, FFS), D ** -0.5, 0.125, ((0, 8), (1, 4))),
        "shared_up": bell_draw(splits[12], (D, FFS), D ** -0.5, 0.125, ((0, 8), (1, 4))),
        "shared_down": bell_draw(splits[13], (FFS, D), (FFS // 8) ** -0.5, 0.21875, ((0, 4), (1, 8))),
        "expert_gate": bell_draw(splits[14], (E, D, FFE), D ** -0.5, 0.125, ((1, 8), (2, 4))),
        "expert_up": bell_draw(splits[15], (E, D, FFE), D ** -0.5, 0.125, ((1, 8), (2, 4))),
        "expert_down": bell_draw(splits[16], (E, FFE, D), (FFE // 16) ** -0.5, 0.625, ((1, 4), (2, 8))),
        "out_grad": bell_draw(splits[17], (TOKENS, D), 1.0, 6.0, ((0, 32),)),
    }


@jax.custom_vjp
def low(v):
    return lax.optimization_barrier(v.astype(jnp.bfloat16)).astype(jnp.float32)

@jax.custom_vjp
def low_back(v):
    return v

def low_keep(v):
    return (low(v), None)

def low_pass(kept, grad):
    return (grad,)

def back_keep(v):
    return (v, None)

def back_low(kept, grad):
    return (low(grad),)
low.defvjp(low_keep, low_pass)
low_back.defvjp(back_keep, back_low)
EPS = 1e-06
THETA = 1000000.0

def product(left, right):
    return jnp.dot(left, right, precision=lax.Precision.HIGHEST)

def rope_tables():
    half_width = HD // 2
    inverse = THETA ** (-(2.0 * jnp.arange(half_width, dtype=jnp.float32)) / HD)
    angles = jnp.arange(SEQ, dtype=jnp.float32)[:, None] * inverse[None, :]
    return (jnp.cos(angles), jnp.sin(angles))

def rotate(field_in, cos_part, sin_part):
    half_width = field_in.shape[-1] // 2
    lower_half = field_in[..., :half_width]
    upper_half = field_in[..., half_width:]
    cos_rows = cos_part[:, None, :]
    sin_rows = sin_part[:, None, :]
    return jnp.concatenate([lower_half * cos_rows - upper_half * sin_rows, upper_half * cos_rows + lower_half * sin_rows], axis=-1)

def rms_norm(values_in, gain_row):
    scale_rows = lax.rsqrt(lax.optimization_barrier(jnp.mean(values_in * values_in, axis=-1, keepdims=True)) + EPS)
    return values_in * scale_rows * gain_row

def layer(inputs, allowed, route_rows, slot_rows, gains, w_query, w_key, w_value, w_out, qkv_bias, router, shared_gate, shared_up, shared_down, expert_gate, expert_up, expert_down):
    first_norm = low(rms_norm(inputs, gains[0]))
    cos_part, sin_part = rope_tables()
    query_pre = low_back(product(first_norm, w_query) + qkv_bias[0].reshape(-1))
    key_pre = low_back(product(first_norm, w_key) + qkv_bias[1].reshape(-1))
    value_pre = low(low_back(product(first_norm, w_value) + qkv_bias[2].reshape(-1)))
    queries = low(rotate(query_pre.reshape(SEQ, H, HD), cos_part, sin_part))
    keys_in = low(rotate(key_pre.reshape(SEQ, H, HD), cos_part, sin_part))
    values_in = value_pre.reshape(SEQ, H, HD)

    def one_head(operands):
        head_query, head_key, head_value = operands
        scores = low_back(product(head_query, head_key.T) * HD ** (-0.5))
        scores = jnp.where(allowed, scores, -1e+30)
        row_max = lax.optimization_barrier(jnp.max(scores, axis=-1, keepdims=True))
        weights = jnp.exp(scores - row_max)
        softmax_probs = weights / lax.optimization_barrier(jnp.sum(weights, axis=-1, keepdims=True))
        return product(low(softmax_probs), head_value)
    head_mix = lax.map(jax.checkpoint(one_head), (queries.transpose(1, 0, 2), keys_in.transpose(1, 0, 2), values_in.transpose(1, 0, 2)))
    heads_out = low(low_back(head_mix.transpose(1, 0, 2).reshape(SEQ, H * HD)))
    attention = low_back(product(heads_out, w_out))
    hidden = inputs + attention
    second_norm = low(rms_norm(hidden, gains[1]))
    logits = low_back(product(second_norm, router))
    expert_probs = jax.nn.softmax(logits[:, :E], axis=-1)
    shared_weight = jax.nn.sigmoid(logits[:, E])
    gate_probs = jnp.take_along_axis(expert_probs, route_rows, axis=1)
    matches = route_rows[None] == jnp.arange(E, dtype=jnp.int32)[:, None, None]
    present = jnp.any(matches, axis=-1)
    slot_table = lax.optimization_barrier(jnp.sum(jnp.where(matches, slot_rows[None], 0), axis=-1))
    onehot = jnp.logical_and(jnp.arange(CAP, dtype=jnp.int32)[None, :, None] == slot_table[:, None, :], present[:, None, :]).astype(jnp.float32)
    slot_placed_rows = jnp.einsum('ect,td->ecd', onehot, second_norm, precision=lax.Precision.HIGHEST)
    gate_in = low_back(jnp.einsum('tuk,tkb->tub', slot_placed_rows, expert_gate, precision=lax.Precision.HIGHEST))
    up_projection_input = low_back(jnp.einsum('tuk,tkb->tub', slot_placed_rows, expert_up, precision=lax.Precision.HIGHEST))
    expert_act = low(jax.nn.silu(gate_in) * up_projection_input)
    expert_out = low_back(jnp.einsum('ecf,efd->ecd', expert_act, expert_down, precision=lax.Precision.HIGHEST))
    slot_index = route_rows * CAP + slot_rows
    picked = jnp.take(expert_out.reshape(E * CAP, D), slot_index, axis=0)
    expert_mix = lax.optimization_barrier(jnp.sum(gate_probs[:, :, None] * picked, axis=1))
    shared_gate_in = low_back(product(second_norm, shared_gate))
    shared_up_in = low_back(product(second_norm, shared_up))
    shared_act = low(jax.nn.silu(shared_gate_in) * shared_up_in)
    shared_out = low_back(product(shared_act, shared_down))
    return hidden + shared_weight[:, None] * shared_out + expert_mix

def reference(tokens, picture_ids, routes, slot_order, norm_gains, w_query, w_key, w_value, w_out, qkv_bias, router, shared_gate, shared_up, shared_down, expert_gate, expert_up, expert_down, out_grad):
    sequences = TOKENS // SEQ
    weights = tuple((w.astype(jnp.float32) for w in (norm_gains, w_query, w_key, w_value, w_out, qkv_bias, router, shared_gate, shared_up, shared_down, expert_gate, expert_up, expert_down)))
    inputs = tokens.astype(jnp.float32).reshape(sequences, SEQ, D)
    cotangent = out_grad.astype(jnp.float32).reshape(sequences, SEQ, D)
    pictures = picture_ids.reshape(sequences, SEQ)
    route_all = routes.reshape(sequences, SEQ, K)
    slot_all = slot_order.reshape(sequences, SEQ, K)
    positions = jnp.arange(SEQ, dtype=jnp.int32)

    def one_sequence(totals, operands):
        seq_input, seq_grad, seq_picture, seq_routes, seq_slots = operands
        allowed = jnp.logical_or(positions[None, :] <= positions[:, None], seq_picture[:, None] * seq_picture[None, :] > 0)

        def apply_layer(layer_input, *params):
            return layer(layer_input, allowed, seq_routes, seq_slots, *params)
        result, pullback = jax.vjp(apply_layer, seq_input, *weights)
        grads = pullback(seq_grad)
        totals = tuple((total + grad_term for total, grad_term in zip(totals, grads[1:])))
        return (totals, (result.astype(jnp.bfloat16), grads[0].astype(jnp.bfloat16)))
    empty_sums = tuple((jnp.zeros(w.shape, jnp.float32) for w in weights))
    totals, (results, input_grads) = lax.scan(one_sequence, empty_sums, (inputs, cotangent, pictures, route_all, slot_all))
    return (results.reshape(TOKENS, D), input_grads.reshape(TOKENS, D), totals[0], totals[1], totals[2], totals[3], totals[4], totals[5], totals[6], totals[7], totals[8], totals[9], totals[10], totals[11], totals[12])
```

```python
import functools

import jax
import jax.numpy as jnp
from jax import lax
from jax.experimental import pallas as pl
from jax.experimental.pallas import tpu as pltpu
from jax.sharding import PartitionSpec as P

EPS = 1e-06
THETA = 1000000.0
BF = jnp.bfloat16
F32 = jnp.float32


def rope_tables(length, width):
    half_width = width // 2
    inverse = THETA ** (-(2.0 * jnp.arange(half_width, dtype=F32)) / width)
    angles = jnp.arange(length, dtype=F32)[:, None] * inverse[None, :]
    return jnp.cos(angles), jnp.sin(angles)


def rotate(field_in, cos_part, sin_part):
    half_width = field_in.shape[-1] // 2
    low, high = field_in[..., :half_width], field_in[..., half_width:]
    cos_rows, sin_rows = cos_part[:, None, :], sin_part[:, None, :]
    return jnp.concatenate(
        [low * cos_rows - high * sin_rows, high * cos_rows + low * sin_rows], axis=-1
    )


def einsum(spec, *args):
    return jnp.einsum(spec, *args, preferred_element_type=F32)


def silu_parts(gate_in):
    gate_sig = jax.nn.sigmoid(gate_in)
    return gate_in * gate_sig, gate_sig * (1.0 + gate_in * (1.0 - gate_sig))


def after(array, *others):
    return lax.optimization_barrier((array,) + others)[0]


def pick(array, index, axis):
    return lax.dynamic_index_in_dim(array, index, axis, keepdims=False)


VMEM_LIMIT = 58 * 2**20


def dot(left, right, left_dim=1, right_dim=0):
    return lax.dot_general(
        left, right, (((left_dim,), (right_dim,)), ((), ())), preferred_element_type=F32
    )


def call(body, grid, in_specs, out_specs, out_shape, flops, moved, scratch=()):
    return pl.pallas_call(
        body,
        grid=grid,
        in_specs=in_specs,
        out_specs=out_specs,
        out_shape=out_shape,
        scratch_shapes=scratch,
        cost_estimate=pl.CostEstimate(flops=flops, bytes_accessed=moved, transcendentals=0),
        compiler_params=pltpu.CompilerParams(vmem_limit_bytes=VMEM_LIMIT),
    )


def act_body(
    experts,
    units,
    group_ref,
    slot_ref,
    rows_ref,
    grads_ref,
    router_ref,
    gateup_ref,
    down_ref,
    slotted_ref,
    slotgrad_ref,
    pair_ref,
    act_ref,
    terms_ref,
    pair_s_ref,
    act_s_ref,
    inner_s_ref,
    probs_ref,
):
    unit = pl.program_id(1)
    half = gateup_ref.shape[1] // 2
    seq_len = rows_ref.shape[1]
    capacity = slotted_ref.shape[2]

    @pl.when(unit == 0)
    def _():
        logits = dot(router_ref[...], rows_ref[0], 1, 1)
        row = lax.broadcasted_iota(jnp.int32, logits.shape, 0)
        routed = jnp.where(row < experts, logits, -1e30)
        raised = jnp.exp(routed - jnp.max(routed, axis=0, keepdims=True))
        soft = raised / jnp.sum(raised, axis=0, keepdims=True)
        probs_ref[0] = jnp.where(row < experts, soft, jax.nn.sigmoid(logits))

    def parts(data, cot, weight):
        both = dot(data, gateup_ref[0], 1, 1)
        cot_in = dot(cot, down_ref[0], 1, 1)
        gate_in, up_in = both[:, :half], both[:, half:]
        gate_act, gate_slope = silu_parts(gate_in)
        act = gate_act * up_in
        inner = jnp.sum(act.astype(BF).astype(F32) * cot_in, axis=1, keepdims=True)
        cot_in = cot_in * weight
        return (
            (act * weight).astype(BF),
            (cot_in * up_in * gate_slope).astype(BF),
            (cot_in * gate_act).astype(BF),
            inner,
        )

    @pl.when(unit < units - 1)
    def _():
        slot = slot_ref[0, pl.ds(unit, 1), :]
        mask = lax.broadcasted_iota(jnp.int32, (capacity, seq_len), 0) == slot
        onehot = mask.astype(F32).astype(BF)
        slotted_ref[0, 0] = dot(onehot, rows_ref[0]).astype(BF)
        slotgrad_ref[0, 0] = dot(onehot, grads_ref[0]).astype(BF)
        probs = probs_ref[0]
        row = lax.broadcasted_iota(jnp.int32, probs.shape, 0)
        expert = group_ref[0] * (units - 1) + unit
        gate = jnp.sum(jnp.where(row == expert, probs, 0.0), axis=0, keepdims=True)
        weight = jnp.sum(jnp.where(mask, gate, 0.0), axis=1, keepdims=True)
        act, gate_grad, up_grad, inner = parts(slotted_ref[0, 0], slotgrad_ref[0, 0], weight)
        act_ref[0, 0] = act
        pair_ref[0, 0, :, :half] = gate_grad
        pair_ref[0, 0, :, half:] = up_grad
        terms_ref[0, pl.ds(unit, 1), :] = jnp.sum(
            jnp.where(mask, inner, 0.0), axis=0, keepdims=True
        )

    @pl.when(unit == units - 1)
    def _():
        logits = dot(rows_ref[0], router_ref[...], 1, 1)
        weight = jax.nn.sigmoid(logits[:, experts : experts + 1])
        act, gate_grad, up_grad, inner = parts(rows_ref[0], grads_ref[0], weight)
        act_s_ref[0] = act
        pair_s_ref[0, :, :half] = gate_grad
        pair_s_ref[0, :, half:] = up_grad
        inner_s_ref[0] = inner


def act_call(experts, capacity, group, slots, rows, grads, router, gateup, down):
    count, seq_len, width = rows.shape
    units, wide, _ = gateup.shape
    half = wide // 2
    routed = units - 1

    def seq(s, u):
        return (s, 0, 0)

    def unit(s, u):
        return (u, 0, 0)

    def slot(s, u):
        return (jnp.minimum(u, routed - 1), s, 0, 0)

    work = count * (routed * capacity + seq_len) * width
    return call(
        functools.partial(act_body, experts, units),
        (count, units),
        [
            pl.BlockSpec(memory_space=pltpu.SMEM),
            pl.BlockSpec((1, routed, seq_len), seq),
            pl.BlockSpec((1, seq_len, width), seq),
            pl.BlockSpec((1, seq_len, width), seq),
            pl.BlockSpec(router.shape, lambda s, u: (0, 0)),
            pl.BlockSpec((1, wide, width), unit),
            pl.BlockSpec((1, half, width), unit),
        ],
        [
            pl.BlockSpec((1, 1, capacity, width), slot),
            pl.BlockSpec((1, 1, capacity, width), slot),
            pl.BlockSpec((1, 1, capacity, wide), slot),
            pl.BlockSpec((1, 1, capacity, half), slot),
            pl.BlockSpec((1, routed, seq_len), seq),
            pl.BlockSpec((1, seq_len, wide), seq),
            pl.BlockSpec((1, seq_len, half), seq),
            pl.BlockSpec((1, seq_len, 1), seq),
            pl.BlockSpec((1,) + (router.shape[0], seq_len), seq),
        ],
        [
            jax.ShapeDtypeStruct((routed, count, capacity, width), BF),
            jax.ShapeDtypeStruct((routed, count, capacity, width), BF),
            jax.ShapeDtypeStruct((routed, count, capacity, wide), BF),
            jax.ShapeDtypeStruct((routed, count, capacity, half), BF),
            jax.ShapeDtypeStruct((count, routed, seq_len), F32),
            jax.ShapeDtypeStruct((count, seq_len, wide), BF),
            jax.ShapeDtypeStruct((count, seq_len, half), BF),
            jax.ShapeDtypeStruct((count, seq_len, 1), F32),
            jax.ShapeDtypeStruct((count, router.shape[0], seq_len), F32),
        ],
        2 * work * 3 * half + 4 * count * routed * capacity * seq_len * width,
        8 * count * seq_len * width * 2,
    )(group, slots, rows, grads, router, gateup, down)


def back_body(slot_ref, routed_ref, shared_ref, weight_ref, out_ref):
    routed, _, capacity, _ = routed_ref.shape
    seq_len = shared_ref.shape[1]
    total = dot(shared_ref[0], weight_ref[routed])
    lane = lax.broadcasted_iota(jnp.int32, (seq_len, capacity), 1)
    for e in range(routed):
        slot_rows = dot(routed_ref[e, 0], weight_ref[e]).astype(BF)
        onehot = (lane == slot_ref[0, e]).astype(F32).astype(BF)
        total = total + dot(onehot, slot_rows)
    out_ref[0] = total.astype(BF)


def back_call(slots, routed, shared, weight):
    units, wide, width = weight.shape
    count, seq_len, _ = shared.shape
    capacity = routed.shape[2]
    block = min(width, 512)
    work = count * ((units - 1) * capacity + seq_len) * width
    return call(
        back_body,
        (width // block, count),
        [
            pl.BlockSpec((1, units - 1, seq_len, 1), lambda j, s: (s, 0, 0, 0)),
            pl.BlockSpec((units - 1, 1, capacity, wide), lambda j, s: (0, s, 0, 0)),
            pl.BlockSpec((1, seq_len, wide), lambda j, s: (s, 0, 0)),
            pl.BlockSpec((units, wide, block), lambda j, s: (0, 0, j)),
        ],
        pl.BlockSpec((1, seq_len, block), lambda j, s: (s, 0, j)),
        jax.ShapeDtypeStruct((count, seq_len, width), BF),
        2 * work * wide + 2 * count * (units - 1) * capacity * seq_len * width,
        units * wide * width * 2 + count * seq_len * width * 2,
    )(slots, routed, shared, weight)


def outer_body(keep, pad, left_a, right_a, left_b, right_b, out_ref):
    total = dot(left_a[0], right_a[0], 0, 0) + dot(left_b[0], right_b[0], 0, 0)
    total = total.astype(BF)
    blocks, _, rows, slice_width = out_ref.shape
    for part in range(rows // keep):
        for k in range(blocks):
            out_ref[k, 0, part * keep : (part + 1) * keep] = total[
                part * pad : part * pad + keep, k * slice_width : (k + 1) * slice_width
            ]


def outer_call(keep, pad, dp, pairs):
    (left_a, right_a), (left_b, right_b) = pairs
    units, rows, wide = left_a.shape
    width = right_a.shape[2]
    slice_width = width // dp
    blocks = max(1, 512 // slice_width)
    kept = wide // pad * keep

    def left(n):
        return pl.BlockSpec((1, n, wide), lambda u, j: (u, 0, 0))

    def right(n):
        return pl.BlockSpec((1, n, blocks * slice_width), lambda u, j: (u, 0, j))

    return call(
        functools.partial(outer_body, keep, pad),
        (units, dp // blocks),
        [left(rows), right(rows), left(rows), right(rows)],
        pl.BlockSpec((blocks, 1, kept, slice_width), lambda u, j: (j, u, 0, 0)),
        jax.ShapeDtypeStruct((dp, units, kept, slice_width), BF),
        4 * units * rows * wide * width,
        units * rows * (wide + width) * 4,
    )(left_a, right_a, left_b, right_b)


def local(
    dp,
    tokens,
    picture_ids,
    routes,
    slot_order,
    norm_gains,
    w_query,
    w_key,
    w_value,
    w_out,
    qkv_bias,
    router,
    shared_gate,
    shared_up,
    shared_down,
    expert_gate,
    expert_up,
    expert_down,
    out_grad,
):
    seq_len = picture_ids.shape[0]
    local_rows = tokens.shape[0]
    width = tokens.shape[1]
    experts, slice_width, hidden_units = expert_gate.shape
    top_count = routes.shape[1]
    capacity = 5 * seq_len * top_count // (4 * experts)
    heads_local = qkv_bias.shape[1]
    head_width = w_query.shape[1] // heads_local
    pair_heads = heads_local // 2
    pair_width = pair_heads * head_width
    mine_experts = experts // 4
    hidden_pad = -(-hidden_units // 128) * 128

    me = lax.axis_index("dp")
    zi = lax.axis_index("tensor")
    core, xi = me % 2, (me // 2) % 2
    group = me % 4
    bits = []
    while 2 ** (len(bits) + 1) <= dp:
        bits.append(2 ** len(bits))
    upper = bits[2:]

    def swap(array, bit):
        return lax.ppermute(array, "dp", [(i, i ^ bit) for i in range(dp)])

    def bit_of(bit):
        return (me // bit) % 2

    def join(mine, theirs, bit, axis):
        n = mine.shape[axis]
        shape = list(mine.shape)
        shape[axis] = 2 * n
        out = jnp.zeros(shape, mine.dtype)
        out = lax.dynamic_update_slice_in_dim(out, mine, n * bit_of(bit), axis)
        return lax.dynamic_update_slice_in_dim(out, theirs, n * (1 - bit_of(bit)), axis)

    def half(array, which, axis):
        n = array.shape[axis] // 2
        return lax.dynamic_slice_in_dim(array, which * n, n, axis)

    gains_z = lax.all_gather(norm_gains, "tensor", axis=1, tiled=True)
    misc_rows = 16
    bias_width = 3 * pair_heads * qkv_bias.shape[2]
    bias_cores = qkv_bias.reshape(3, 2, -1).swapaxes(0, 1).reshape(2, bias_width)

    def misc_pack(core_bias):
        wide = jnp.zeros((misc_rows, 2 * pair_width), BF)
        wide = wide.at[: experts + 1, :slice_width].set(router.T)
        wide = wide.at[experts + 1, :bias_width].set(core_bias)
        return wide.at[experts + 2 : experts + 4, :slice_width].set(gains_z)

    qk = jnp.concatenate(
        [w.reshape(slice_width, 2, pair_width) for w in (w_query, w_key)], axis=2
    )
    qk = jnp.concatenate(
        [qk, jnp.stack([misc_pack(bias_cores[0]), misc_pack(bias_cores[1])], axis=1)], axis=0
    )
    vo = jnp.concatenate(
        [w.reshape(slice_width, 2, pair_width) for w in (w_value, w_out.T)], axis=2
    )
    tokens_z = lax.all_gather(tokens, "tensor", axis=0, tiled=True)

    def gather_attention(pack, order):
        dims = (1,) * len(bits[1:])
        both = join(pick(pack, core, 1)[None], swap(pick(pack, 1 - core, 1), 1)[None], 1, 0)
        both = both.reshape(dims + both.shape)
        for bit in order:
            axis = len(bits) - 1 - bits.index(bit)
            both = join(both, swap(both, bit), bit, axis)
        return both.reshape((dp,) + both.shape[-2:])

    qk_all = gather_attention(qk, bits[1:])
    vo_full = gather_attention(vo, bits[:0:-1]).reshape(width, 2 * pair_width)
    qk_full = qk_all[:, :slice_width].reshape(width, 2 * pair_width)
    misc = qk_all[:, slice_width:]
    router_full = misc[:, : experts + 1, :slice_width].swapaxes(1, 2).reshape(width, -1)
    gain_rows = misc[:, experts + 2 : experts + 4, :slice_width].swapaxes(0, 1)
    gain_rows = gain_rows.reshape(2, width).astype(F32)
    bias = misc[:, experts + 1, :bias_width].astype(F32)
    bias = bias.reshape(dp, 3 * pair_heads, -1).swapaxes(0, 1).reshape(3, pair_width)

    tokens_sib = swap(tokens_z, 1)
    grad_z = lax.all_gather(out_grad, "tensor", axis=0, tiled=True)

    codes = jnp.concatenate([routes, slot_order], axis=1).T
    codes_x = swap(codes, 2)
    both_codes = swap(jnp.stack([codes, codes_x]), 1)
    codes_a = jnp.stack([codes, both_codes[0]])
    codes_b = jnp.stack([codes_x, both_codes[1]])
    pictures = jnp.stack([picture_ids, swap(picture_ids, 1)])

    def core_units(routed, shared):
        routed = routed.reshape(2, 2, mine_experts, hidden_units, slice_width)
        shared = shared.reshape(2, 2, 1, hidden_units, slice_width)

        def cut(which):
            return jnp.concatenate([pick(routed, which, 1), pick(shared, which, 1)], axis=1)

        return join(cut(core), swap(cut(1 - core), 1), 1, 3)

    def x_units(held):
        return join(pick(held, xi, 0), swap(pick(held, 1 - xi, 0), 2), 2, 2)

    def upper_units(held):
        for bit in upper[:-1]:
            held = join(held, swap(held, bit), bit, 2)
        return held, swap(held, upper[-1])

    def padded(*pairs):
        n = pairs[0][0].shape[-1]
        out = jnp.zeros((mine_experts + 1, len(pairs) * hidden_pad, 2 * n), BF)
        zero = jnp.int32(0)
        for k, (mine, theirs) in enumerate(pairs):
            row = jnp.int32(k * hidden_pad)
            out = lax.dynamic_update_slice(out, mine, (zero, row, n * bit_of(upper[-1])))
            out = lax.dynamic_update_slice(out, theirs, (zero, row, n * (1 - bit_of(upper[-1]))))
        return out

    down_c = core_units(expert_down, shared_down)
    gate_c = core_units(expert_gate.swapaxes(1, 2), shared_gate.T)
    up_c = core_units(expert_up.swapaxes(1, 2), shared_up.T)
    down_x = x_units(down_c)
    gate_x = x_units(gate_c)
    up_x = x_units(up_c)
    grad_x = swap(after(grad_z, up_x), 2)
    down_y = upper_units(down_x)
    gate_y = upper_units(gate_x)
    up_y = upper_units(up_x)

    rows_f = jnp.stack([tokens_z, tokens_sib]).astype(F32)
    qk_full = after(qk_full, down_c, gate_c, up_c)
    first_scale = lax.rsqrt(jnp.mean(rows_f * rows_f, axis=-1, keepdims=True) + EPS)
    first_norm = (rows_f * first_scale * gain_rows[0]).astype(BF)
    qk_pre = einsum("std,df->stf", first_norm, qk_full) + jnp.concatenate([bias[0], bias[1]])
    values = (einsum("std,df->stf", first_norm, vo_full[:, :pair_width]) + bias[2]).astype(BF)
    cos_part, sin_part = rope_tables(seq_len, head_width)
    qk_rot = rotate(
        qk_pre.reshape(2, seq_len, 2 * pair_heads, head_width), cos_part, sin_part
    ).astype(BF)
    qk_rot = after(qk_rot, down_x)
    queries, keys = qk_rot[:, :, :pair_heads], qk_rot[:, :, pair_heads:]
    values = values.reshape(2, seq_len, pair_heads, head_width)
    positions = jnp.arange(seq_len, dtype=jnp.int32)
    allowed = jnp.logical_or(
        positions[None, None, :] <= positions[None, :, None],
        pictures[:, :, None] * pictures[:, None, :] > 0,
    )
    score_scale = head_width ** (-0.5)
    scores = einsum("sqhd,skhd->shqk", queries, keys) * score_scale
    scores = jnp.where(allowed[:, None], scores, -1e30)
    weights = jnp.exp(scores - jnp.max(scores, axis=-1, keepdims=True))
    probs = weights / jnp.sum(weights, axis=-1, keepdims=True)
    probs_low = probs.astype(BF)
    head_mix = einsum("shqk,skhd->sqhd", probs_low, values).astype(BF)
    heads_out = after(head_mix.reshape(2, seq_len, pair_width), gate_x)
    out_weight = vo_full[:, pair_width:]
    attn_part = einsum("sqf,df->sqd", heads_out, out_weight)

    def core_sum(own, sibling):
        return own + swap(sibling.astype(BF), 1).astype(F32)

    def z_scatter(array):
        return lax.psum_scatter(
            array.astype(BF), "tensor", scatter_dimension=0, tiled=True
        ).astype(F32)

    inputs = tokens.astype(F32)
    hidden = inputs + z_scatter(core_sum(attn_part[0], attn_part[1]))
    hidden = after(hidden, up_x, down_y[1])
    second_scale = lax.rsqrt(jnp.mean(hidden * hidden, axis=-1, keepdims=True) + EPS)
    second_unit = hidden * second_scale
    second_norm = (second_unit * gain_rows[1]).astype(BF)
    norm_z = lax.all_gather(second_norm, "tensor", axis=0, tiled=True)
    norm_z = after(norm_z, gate_y[1], grad_x)
    down_all = padded(down_y)
    gateup_all = padded(gate_y, up_y)

    norm_x = swap(norm_z, 2)
    norm_a = jnp.stack([norm_z, swap(norm_z, 1)])
    norm_b = jnp.stack([norm_x, swap(norm_x, 1)])
    grad_a = jnp.stack([grad_z, swap(grad_z, 1)])
    grad_b = jnp.stack([grad_x, swap(grad_x, 1)])

    expert_ids = group * mine_experts + jnp.arange(mine_experts, dtype=jnp.int32)

    router_rows = jnp.pad(router_full.T, ((0, 16 - experts - 1), (0, 0)))
    group_ids = group.astype(jnp.int32).reshape(1)

    def slots_of(codes_in):
        routes_in, slots_in = codes_in[:, None, :top_count], codes_in[:, None, top_count:]
        matches = routes_in == expert_ids[None, :, None, None]
        return jnp.max(jnp.where(matches, slots_in, -1), axis=2)

    def feed(slots, rows, grads):
        slotted, slot_grad, pair, act, terms, pair_s, act_s, inner_s, probs_out = act_call(
            experts, capacity, group_ids, slots, rows, grads, router_rows, gateup_all, down_all
        )
        terms = jnp.concatenate([terms.swapaxes(1, 2), inner_s], axis=-1)
        flat = [a.reshape(mine_experts, -1, a.shape[-1]) for a in (slotted, slot_grad, pair, act)]
        shared = [a.reshape(1, -1, a.shape[-1]) for a in (rows, grads, pair_s, act_s)]
        return (pair, pair_s), (act, act_s), terms, (flat, shared), probs_out

    slots_a, slots_b = slots_of(codes_a), slots_of(codes_b)
    fed_a = feed(slots_a, norm_a, grad_a)
    fed_b = feed(slots_b, norm_b, grad_b)
    columns_a, columns_b = slots_a[..., None], slots_b[..., None]
    row_grad_b = back_call(columns_b, *fed_b[0], gateup_all)
    row_grad_a = back_call(after(columns_a, row_grad_b), *fed_a[0], gateup_all)
    row_out_b = back_call(after(columns_b, row_grad_a), *fed_b[1], down_all)
    row_out_a = back_call(columns_a, *fed_a[1], down_all)

    def spread(terms):
        wide = jnp.zeros(terms.shape[:-1] + (128,), F32)
        wide = lax.dynamic_update_slice_in_dim(
            wide, terms[..., :mine_experts], group * mine_experts, terms.ndim - 1
        )
        return wide.at[..., experts].set(terms[..., mine_experts])

    def group_sum(a, b):
        across = b[0].astype(F32) + swap(b[1].astype(BF), 1).astype(F32)
        near = a[0].astype(F32) + swap(a[1].astype(BF), 1).astype(F32)
        return near + swap(across.astype(BF), 2).astype(F32)

    grad_sum = group_sum(row_grad_a, row_grad_b)
    term_sum = group_sum(spread(fed_a[2]), spread(fed_b[2]))
    packed = z_scatter(jnp.concatenate([grad_sum, term_sum], axis=-1))
    second_grad, gate_sums = packed[:, :width], packed[:, width:]

    data_a, data_b = fed_a[3], fed_b[3]

    def unit_grads(left, right):
        return jnp.concatenate(
            [
                outer_call(
                    hidden_units,
                    hidden_pad,
                    dp,
                    [(data[k][left], data[k][right]) for data in (data_a, data_b)],
                )
                for k in range(2)
            ],
            axis=1,
        )

    def scatter_units(total):
        total = total.reshape((2,) * len(bits) + total.shape[1:])
        for bit in reversed(upper):
            axis = len(bits) - 1 - bits.index(bit)
            sent = half(total, 1 - bit_of(bit), axis)
            kept = half(total, bit_of(bit), axis)
            total = (kept.astype(F32) + swap(sent, bit).astype(F32)).astype(BF)
        total = total.reshape((2, 2) + total.shape[len(bits) :])
        held = join(pick(total, xi, 0)[None], swap(pick(total, 1 - xi, 0), 2)[None], 2, 0)
        return join(pick(held, core, 1)[:, None], swap(pick(held, 1 - core, 1), 1)[:, None], 1, 1)

    def split_units(held):
        routed = held[:, :, :mine_experts].reshape(experts, -1, slice_width)
        shared = held[:, :, mine_experts]
        return routed.astype(F32), shared.astype(F32)

    gateup_sum = scatter_units(unit_grads(2, 0))
    down_sum = scatter_units(unit_grads(3, 1))
    routed_gu, shared_gu = split_units(gateup_sum)
    routed_down, shared_down_sum = split_units(down_sum)
    shared_gu = shared_gu.reshape(4, 2, hidden_units, slice_width)
    egate_sum = routed_gu[:, :hidden_units].swapaxes(1, 2)
    eup_sum = routed_gu[:, hidden_units:].swapaxes(1, 2)
    sgate_sum = shared_gu[:, 0].reshape(-1, slice_width).T
    sup_sum = shared_gu[:, 1].reshape(-1, slice_width).T
    sdown_sum = shared_down_sum.reshape(-1, slice_width)

    row_start = zi * local_rows
    probs_local = lax.dynamic_slice_in_dim(fed_a[4][0], row_start, local_rows, 1).T
    probs_mine, weight_mine = probs_local[:, :experts], probs_local[:, experts]
    route_grad = gate_sums[:, :experts]
    expert_logit_grad = probs_mine * (
        route_grad - jnp.sum(probs_mine * route_grad, axis=-1, keepdims=True)
    )
    weight_logit_grad = gate_sums[:, experts] * weight_mine * (1.0 - weight_mine)
    logits_grad = jnp.concatenate([expert_logit_grad, weight_logit_grad[:, None]], axis=1).astype(
        BF
    )
    second_grad = second_grad + einsum("tf,df->td", logits_grad, router_full)
    gain_two_grad = jnp.sum(second_grad * second_unit, axis=0)
    unit_two = second_grad * gain_rows[1]
    hidden_grad = out_grad.astype(F32) + second_scale * (
        unit_two - second_unit * jnp.mean(unit_two * second_unit, axis=-1, keepdims=True)
    )
    attention_grad = hidden_grad.astype(BF)
    wide_logits = jnp.pad(logits_grad, ((0, 0), (0, 128 - experts - 1)))
    back_z = lax.all_gather(
        jnp.concatenate([attention_grad, wide_logits], axis=1), "tensor", axis=0, tiled=True
    )
    out_sum = after(group_sum(row_out_a, row_out_b), back_z)
    output = (hidden + z_scatter(out_sum)).astype(BF)
    logits_z = back_z[:, width : width + 16]
    back_own = back_z[:, :width]
    back_rows = jnp.stack([back_own, swap(back_own, 1)])

    router_part = einsum("tf,td->fd", logits_z, norm_z)[: experts + 1]

    out_proj = einsum("std,stf->df", back_rows, heads_out)
    mix_grad = einsum("std,df->stf", back_rows, out_weight).astype(BF)
    mix_grad = mix_grad.reshape(2, seq_len, pair_heads, head_width)
    prob_grad = einsum("sqhd,skhd->shqk", mix_grad, values)
    score_grad = (
        probs * (prob_grad - jnp.sum(probs * prob_grad, axis=-1, keepdims=True))
    ).astype(BF)
    query_rot = einsum("shqk,skhd->sqhd", score_grad, keys) * score_scale
    key_rot = einsum("shqk,sqhd->skhd", score_grad, queries) * score_scale
    value_grad = einsum("shqk,sqhd->skhd", probs_low, mix_grad)
    qk_grad = rotate(jnp.concatenate([query_rot, key_rot], axis=2), cos_part, -sin_part)
    qk_grad = qk_grad.astype(BF).reshape(2, seq_len, 2 * pair_width)
    v_grad = value_grad.astype(BF).reshape(2, seq_len, pair_width)
    first_part = einsum("stf,df->std", qk_grad, qk_full) + einsum(
        "stf,df->std", v_grad, vo_full[:, :pair_width]
    )
    first_grad = z_scatter(core_sum(first_part[0], first_part[1]))

    gain_one_grad = jnp.sum(first_part * (rows_f * first_scale), axis=(0, 1))
    bias_part = jnp.concatenate(
        [jnp.sum(qk_grad.astype(F32), axis=(0, 1)), jnp.sum(v_grad.astype(F32), axis=(0, 1))]
    )
    bias_part = bias_part.reshape(3 * pair_heads, dp, -1).swapaxes(0, 1).reshape(dp, 1, -1)
    gain_part = jnp.stack([gain_one_grad, gain_two_grad]).reshape(2, dp, slice_width)

    def wide_rows(rows):
        return jnp.pad(rows, ((0, 0), (0, 0), (0, 2 * pair_width - rows.shape[2])))

    misc_part = jnp.concatenate(
        [
            wide_rows(router_part.reshape(experts + 1, dp, slice_width).swapaxes(0, 1)),
            wide_rows(bias_part),
            wide_rows(gain_part.swapaxes(0, 1)),
            jnp.zeros((dp, misc_rows - experts - 4, 2 * pair_width), F32),
        ],
        axis=1,
    )
    qk_total = einsum("std,stf->df", first_norm, qk_grad).reshape(dp, slice_width, -1)
    qk_total = jnp.concatenate([qk_total, misc_part], axis=1)
    vo_total = jnp.concatenate([einsum("std,stf->df", first_norm, v_grad), out_proj], axis=1)
    vo_total = vo_total.reshape(dp, slice_width, -1)

    def scatter_attention(total, order):
        total = total.reshape((2,) * len(bits) + total.shape[1:])
        for bit in order:
            axis = len(bits) - 1 - bits.index(bit)
            sent = half(total, 1 - bit_of(bit), axis).astype(BF)
            total = half(total, bit_of(bit), axis) + swap(sent, bit).astype(F32)
        total = total.reshape((2,) + total.shape[-2:]).astype(BF)
        return pick(total, core, 0), swap(pick(total, 1 - core, 0), 1)

    def columns_of(mine, theirs):
        held = join(mine[:slice_width, None], theirs[:slice_width, None], 1, 1)
        first, second = held[..., :pair_width], held[..., pair_width:]
        return (
            first.reshape(slice_width, -1).astype(F32),
            second.reshape(slice_width, -1).astype(F32),
        )

    qk_mine, qk_theirs = scatter_attention(qk_total, bits[:0:-1])
    vo_mine, vo_theirs = scatter_attention(vo_total, bits[1:])
    qk_sums = columns_of(qk_mine, qk_theirs)
    vo_sums = columns_of(vo_mine, vo_theirs)
    misc_mine = qk_mine[slice_width:].astype(F32)
    misc_theirs = qk_theirs[slice_width:].astype(F32)
    misc_sum = misc_mine + misc_theirs
    router_sum = misc_sum[: experts + 1, :slice_width].T
    bias_sums = join(
        misc_mine[experts + 1, :bias_width].reshape(3, 1, pair_heads, -1),
        misc_theirs[experts + 1, :bias_width].reshape(3, 1, pair_heads, -1),
        1,
        1,
    ).reshape(3, heads_local, -1)
    gain_sums = lax.all_gather(
        misc_sum[experts + 2 : experts + 4, :slice_width], "tensor", axis=0, tiled=False
    )
    tensor = gain_sums.shape[0]
    gain_sums = jnp.sum(gain_sums, axis=0).reshape(2, tensor, -1)
    gain_sums = pick(gain_sums, zi, 1)

    unit_mine = inputs * lax.rsqrt(jnp.mean(inputs * inputs, axis=-1, keepdims=True) + EPS)
    scale_mine = lax.rsqrt(jnp.mean(inputs * inputs, axis=-1, keepdims=True) + EPS)
    unit_one = first_grad * gain_rows[0]
    input_grad = hidden_grad + scale_mine * (
        unit_one - unit_mine * jnp.mean(unit_one * unit_mine, axis=-1, keepdims=True)
    )
    return (
        output,
        input_grad.astype(BF),
        gain_sums,
        qk_sums[0],
        qk_sums[1],
        vo_sums[0],
        vo_sums[1].T,
        bias_sums,
        router_sum,
        sgate_sum,
        sup_sum,
        sdown_sum,
        egate_sum,
        eup_sum,
        routed_down,
    )


def solution(mesh):
    return jax.shard_map(
        functools.partial(local, mesh.shape["dp"]),
        mesh=mesh,
        in_specs=(
            P(("dp", "tensor"), None),
            P("dp"),
            P("dp", None),
            P("dp", None),
            P(None, ("dp", "tensor")),
            P("dp", "tensor"),
            P("dp", "tensor"),
            P("dp", "tensor"),
            P("tensor", "dp"),
            P(None, "tensor", "dp"),
            P("dp", None),
            P("dp", "tensor"),
            P("dp", "tensor"),
            P("tensor", "dp"),
            P(None, "dp", "tensor"),
            P(None, "dp", "tensor"),
            P(None, "tensor", "dp"),
            P(("dp", "tensor"), None),
        ),
        out_specs=(
            P(("dp", "tensor"), None),
            P(("dp", "tensor"), None),
            P(None, ("dp", "tensor")),
            P("dp", "tensor"),
            P("dp", "tensor"),
            P("dp", "tensor"),
            P("tensor", "dp"),
            P(None, "tensor", "dp"),
            P("dp", None),
            P("dp", "tensor"),
            P("dp", "tensor"),
            P("tensor", "dp"),
            P(None, "dp", "tensor"),
            P(None, "dp", "tensor"),
            P(None, "tensor", "dp"),
        ),
        check_vma=False,
    )
```

```python
import functools

import jax
import jax.numpy as jnp
from jax import lax
from jax.experimental import pallas as pl
from jax.experimental.pallas import tpu as pltpu
from jax.sharding import PartitionSpec as P

EPS = 1e-06
THETA = 1000000.0
BF = jnp.bfloat16
F32 = jnp.float32


def rope_tables(length, width):
    half_width = width // 2
    inverse = THETA ** (-(2.0 * jnp.arange(half_width, dtype=F32)) / width)
    angles = jnp.arange(length, dtype=F32)[:, None] * inverse[None, :]
    return jnp.cos(angles), jnp.sin(angles)


def rotate(field_in, cos_part, sin_part):
    half_width = field_in.shape[-1] // 2
    low, high = field_in[..., :half_width], field_in[..., half_width:]
    cos_rows, sin_rows = cos_part[:, None, :], sin_part[:, None, :]
    return jnp.concatenate(
        [low * cos_rows - high * sin_rows, high * cos_rows + low * sin_rows], axis=-1
    )


def einsum(spec, *args):
    return jnp.einsum(spec, *args, preferred_element_type=F32)


def silu_parts(gate_in):
    gate_sig = jax.nn.sigmoid(gate_in)
    return gate_in * gate_sig, gate_sig * (1.0 + gate_in * (1.0 - gate_sig))


def after(array, *others):
    return lax.optimization_barrier((array,) + others)[0]


def pick(array, index, axis):
    return lax.dynamic_index_in_dim(array, index, axis, keepdims=False)


VMEM_LIMIT = 58 * 2**20


def dot(left, right, left_dim=1, right_dim=0):
    return lax.dot_general(
        left, right, (((left_dim,), (right_dim,)), ((), ())), preferred_element_type=F32
    )


def call(body, grid, in_specs, out_specs, out_shape, flops, moved, scratch=()):
    return pl.pallas_call(
        body,
        grid=grid,
        in_specs=in_specs,
        out_specs=out_specs,
        out_shape=out_shape,
        scratch_shapes=scratch,
        cost_estimate=pl.CostEstimate(flops=flops, bytes_accessed=moved, transcendentals=0),
        compiler_params=pltpu.CompilerParams(vmem_limit_bytes=VMEM_LIMIT),
    )


def act_body(
    experts,
    units,
    group_ref,
    slot_ref,
    rows_ref,
    grads_ref,
    router_ref,
    gateup_ref,
    down_ref,
    slotted_ref,
    slotgrad_ref,
    pair_ref,
    act_ref,
    terms_ref,
    pair_s_ref,
    act_s_ref,
    inner_s_ref,
    probs_ref,
):
    unit = pl.program_id(1)
    half = gateup_ref.shape[1] // 2
    seq_len = rows_ref.shape[1]
    capacity = slotted_ref.shape[2]

    @pl.when(unit == 0)
    def _():
        logits = dot(router_ref[...], rows_ref[0], 1, 1)
        row = lax.broadcasted_iota(jnp.int32, logits.shape, 0)
        routed = jnp.where(row < experts, logits, -1e30)
        raised = jnp.exp(routed - jnp.max(routed, axis=0, keepdims=True))
        soft = raised / jnp.sum(raised, axis=0, keepdims=True)
        probs_ref[0] = jnp.where(row < experts, soft, jax.nn.sigmoid(logits))

    def parts(data, cot, weight):
        both = dot(data, gateup_ref[0], 1, 1)
        cot_in = dot(cot, down_ref[0], 1, 1)
        gate_in, up_in = both[:, :half], both[:, half:]
        gate_act, gate_slope = silu_parts(gate_in)
        act = gate_act * up_in
        inner = jnp.sum(act.astype(BF).astype(F32) * cot_in, axis=1, keepdims=True)
        cot_in = cot_in * weight
        return (
            (act * weight).astype(BF),
            (cot_in * up_in * gate_slope).astype(BF),
            (cot_in * gate_act).astype(BF),
            inner,
        )

    @pl.when(unit < units - 1)
    def _():
        slot = slot_ref[0, pl.ds(unit, 1), :]
        mask = lax.broadcasted_iota(jnp.int32, (capacity, seq_len), 0) == slot
        onehot = mask.astype(F32).astype(BF)
        slotted_ref[0, 0] = dot(onehot, rows_ref[0]).astype(BF)
        slotgrad_ref[0, 0] = dot(onehot, grads_ref[0]).astype(BF)
        probs = probs_ref[0]
        row = lax.broadcasted_iota(jnp.int32, probs.shape, 0)
        expert = group_ref[0] * (units - 1) + unit
        gate = jnp.sum(jnp.where(row == expert, probs, 0.0), axis=0, keepdims=True)
        weight = jnp.sum(jnp.where(mask, gate, 0.0), axis=1, keepdims=True)
        act, gate_grad, up_grad, inner = parts(slotted_ref[0, 0], slotgrad_ref[0, 0], weight)
        act_ref[0, 0] = act
        pair_ref[0, 0, :, :half] = gate_grad
        pair_ref[0, 0, :, half:] = up_grad
        terms_ref[0, pl.ds(unit, 1), :] = jnp.sum(
            jnp.where(mask, inner, 0.0), axis=0, keepdims=True
        )

    @pl.when(unit == units - 1)
    def _():
        logits = dot(rows_ref[0], router_ref[...], 1, 1)
        weight = jax.nn.sigmoid(logits[:, experts : experts + 1])
        act, gate_grad, up_grad, inner = parts(rows_ref[0], grads_ref[0], weight)
        act_s_ref[0] = act
        pair_s_ref[0, :, :half] = gate_grad
        pair_s_ref[0, :, half:] = up_grad
        inner_s_ref[0] = inner


def act_call(experts, capacity, group, slots, rows, grads, router, gateup, down):
    count, seq_len, width = rows.shape
    units, wide, _ = gateup.shape
    half = wide // 2
    routed = units - 1

    def seq(s, u):
        return (s, 0, 0)

    def unit(s, u):
        return (u, 0, 0)

    def slot(s, u):
        return (jnp.minimum(u, routed - 1), s, 0, 0)

    work = count * (routed * capacity + seq_len) * width
    return call(
        functools.partial(act_body, experts, units),
        (count, units),
        [
            pl.BlockSpec(memory_space=pltpu.SMEM),
            pl.BlockSpec((1, routed, seq_len), seq),
            pl.BlockSpec((1, seq_len, width), seq),
            pl.BlockSpec((1, seq_len, width), seq),
            pl.BlockSpec(router.shape, lambda s, u: (0, 0)),
            pl.BlockSpec((1, wide, width), unit),
            pl.BlockSpec((1, half, width), unit),
        ],
        [
            pl.BlockSpec((1, 1, capacity, width), slot),
            pl.BlockSpec((1, 1, capacity, width), slot),
            pl.BlockSpec((1, 1, capacity, wide), slot),
            pl.BlockSpec((1, 1, capacity, half), slot),
            pl.BlockSpec((1, routed, seq_len), seq),
            pl.BlockSpec((1, seq_len, wide), seq),
            pl.BlockSpec((1, seq_len, half), seq),
            pl.BlockSpec((1, seq_len, 1), seq),
            pl.BlockSpec((1,) + (router.shape[0], seq_len), seq),
        ],
        [
            jax.ShapeDtypeStruct((routed, count, capacity, width), BF),
            jax.ShapeDtypeStruct((routed, count, capacity, width), BF),
            jax.ShapeDtypeStruct((routed, count, capacity, wide), BF),
            jax.ShapeDtypeStruct((routed, count, capacity, half), BF),
            jax.ShapeDtypeStruct((count, routed, seq_len), F32),
            jax.ShapeDtypeStruct((count, seq_len, wide), BF),
            jax.ShapeDtypeStruct((count, seq_len, half), BF),
            jax.ShapeDtypeStruct((count, seq_len, 1), F32),
            jax.ShapeDtypeStruct((count, router.shape[0], seq_len), F32),
        ],
        2 * work * 3 * half + 4 * count * routed * capacity * seq_len * width,
        8 * count * seq_len * width * 2,
    )(group, slots, rows, grads, router, gateup, down)


def back_body(slot_ref, routed_ref, shared_ref, weight_ref, out_ref):
    routed, _, capacity, _ = routed_ref.shape
    seq_len = shared_ref.shape[1]
    total = dot(shared_ref[0], weight_ref[routed])
    lane = lax.broadcasted_iota(jnp.int32, (seq_len, capacity), 1)
    for e in range(routed):
        slot_rows = dot(routed_ref[e, 0], weight_ref[e]).astype(BF)
        onehot = (lane == slot_ref[0, e]).astype(F32).astype(BF)
        total = total + dot(onehot, slot_rows)
    out_ref[0] = total.astype(BF)


def back_call(slots, routed, shared, weight):
    units, wide, width = weight.shape
    count, seq_len, _ = shared.shape
    capacity = routed.shape[2]
    block = min(width, 512)
    work = count * ((units - 1) * capacity + seq_len) * width
    return call(
        back_body,
        (width // block, count),
        [
            pl.BlockSpec((1, units - 1, seq_len, 1), lambda j, s: (s, 0, 0, 0)),
            pl.BlockSpec((units - 1, 1, capacity, wide), lambda j, s: (0, s, 0, 0)),
            pl.BlockSpec((1, seq_len, wide), lambda j, s: (s, 0, 0)),
            pl.BlockSpec((units, wide, block), lambda j, s: (0, 0, j)),
        ],
        pl.BlockSpec((1, seq_len, block), lambda j, s: (s, 0, j)),
        jax.ShapeDtypeStruct((count, seq_len, width), BF),
        2 * work * wide + 2 * count * (units - 1) * capacity * seq_len * width,
        units * wide * width * 2 + count * seq_len * width * 2,
    )(slots, routed, shared, weight)


def outer_body(keep, pad, left_a, right_a, left_b, right_b, out_ref):
    total = dot(left_a[0], right_a[0], 0, 0) + dot(left_b[0], right_b[0], 0, 0)
    total = total.astype(BF)
    blocks, _, rows, slice_width = out_ref.shape
    for part in range(rows // keep):
        for k in range(blocks):
            out_ref[k, 0, part * keep : (part + 1) * keep] = total[
                part * pad : part * pad + keep, k * slice_width : (k + 1) * slice_width
            ]


def outer_call(keep, pad, dp, pairs):
    (left_a, right_a), (left_b, right_b) = pairs
    units, rows, wide = left_a.shape
    width = right_a.shape[2]
    slice_width = width // dp
    blocks = max(1, 512 // slice_width)
    kept = wide // pad * keep

    def left(n):
        return pl.BlockSpec((1, n, wide), lambda u, j: (u, 0, 0))

    def right(n):
        return pl.BlockSpec((1, n, blocks * slice_width), lambda u, j: (u, 0, j))

    return call(
        functools.partial(outer_body, keep, pad),
        (units, dp // blocks),
        [left(rows), right(rows), left(rows), right(rows)],
        pl.BlockSpec((blocks, 1, kept, slice_width), lambda u, j: (j, u, 0, 0)),
        jax.ShapeDtypeStruct((dp, units, kept, slice_width), BF),
        4 * units * rows * wide * width,
        units * rows * (wide + width) * 4,
    )(left_a, right_a, left_b, right_b)


MESH = pl.DeviceIdType.MESH


class Copies:
    def __init__(self, send, recv, here):
        self.send, self.recv, self.here = send, recv, here
        self.remote_count = self.local_count = 0

    def remote(self, src, dst, **device):
        k = self.remote_count
        self.remote_count += 1
        return pltpu.make_async_remote_copy(
            src_ref=src,
            dst_ref=dst,
            send_sem=self.send.at[k],
            recv_sem=self.recv.at[k],
            device_id=device,
            device_id_type=MESH,
        )

    def local(self, src, dst):
        k = self.local_count
        self.local_count += 1
        return pltpu.make_async_copy(src, dst, self.here.at[k])


class Line:
    def __init__(self, copies, buffer, z, depth, rows):
        self.z, self.depth = z, depth

        def piece(p):
            return buffer.at[pl.ds(pl.multiple_of(p * rows, rows), rows)]

        def make(k, sign):
            p = z - sign * k
            return copies.remote(piece(p), piece(p), tensor=z + sign)

        self.ups = [make(k, 1) for k in range(depth - 1)]
        self.downs = [make(k, -1) for k in range(depth - 1)]

    def sends(self, k):
        z, top = self.z, self.depth - 1
        return (
            (self.ups[k], jnp.logical_and(z < top, z >= k)),
            (self.downs[k], jnp.logical_and(z > 0, z + k <= top)),
        )

    def begin(self):
        for copy, there in self.sends(0):
            pl.when(there)(copy.start)

    def step(self, k, each=None):
        z, top = self.z, self.depth - 1
        arrivals = (
            (self.ups[k - 1], z >= k, z - k),
            (self.downs[k - 1], z + k <= top, z + k),
        )
        onward = self.sends(k) if k < top else (None, None)
        for (copy, there, p), further in zip(arrivals, onward):

            def arrive(copy=copy, p=p):
                copy.wait_recv()
                if each is not None:
                    each(k, p)

            pl.when(there)(arrive)
            if further is not None:
                pl.when(further[1])(further[0].start)

    def finish(self):
        for k in range(self.depth - 1):
            for copy, there in self.sends(k):
                pl.when(there)(copy.wait_send)


def peer_of(me, r):
    out, bit = me, 1
    while bit <= r:
        if r & bit:
            out = out + bit - 2 * bit * (me // bit % 2)
        bit *= 2
    return out


def greet(me, z, dp, depth):
    barrier = pltpu.get_barrier_semaphore()
    for r in range(1, dp):
        pl.semaphore_signal(barrier, inc=1, device_id={"dp": peer_of(me, r)}, device_id_type=MESH)
    for r in range(1, depth):
        pl.semaphore_signal(
            barrier, inc=1, device_id={"tensor": (z + r) % depth}, device_id_type=MESH
        )
    pl.semaphore_wait(barrier, dp - 1 + depth - 1)


def spin(field, cos_rows, sin_rows):
    return field * cos_rows + pltpu.roll(field, field.shape[-1] // 2, 1) * sin_rows


def forward_body(
    sizes,
    codes_ref,
    misc_ref,
    gains_ref,
    cos_ref,
    sin_ref,
    tokens_ref,
    outgrad_ref,
    wq_ref,
    wk_ref,
    wv_ref,
    wo_ref,
    eg_ref,
    eu_ref,
    ed_ref,
    sg_ref,
    su_ref,
    sd_ref,
    hidden_ref,
    norm_ref,
    grads_ref,
    gateup_ref,
    down_ref,
    codes_all,
    misc_all,
    gain_rows,
    tok,
    weights,
    qkv_ref,
    probs_ref,
    mix_ref,
    fnorm,
    part,
    part_in,
    scatter_in,
    gains_all,
    zeros,
    send,
    recv,
    here,
):
    dp, depth, experts, hidden_units, head = sizes
    me, z = lax.axis_index("dp"), lax.axis_index("tensor")
    core, x = me % 2, (me // 2) % 2
    bits = [2**k for k in range(dp.bit_length() - 1)]
    upper = bits[2:]
    rows, width = tokens_ref.shape
    seq_len = rows * depth
    slice_width = width // dp
    routed = experts // 4
    c = Copies(send, recv, here)

    def bit_of(bit):
        return (me // bit) % 2

    greet(me, z, dp, depth)

    first = []
    own_codes = c.local(codes_ref, codes_all.at[0])
    own_misc = c.local(misc_ref, misc_all.at[me])
    own_gains = c.local(gains_ref, gains_all.at[z, me])
    for copy in (own_codes, own_misc, own_gains):
        copy.start()
    for r in range(1, 4):
        first.append(c.remote(codes_ref, codes_all.at[r], dp=peer_of(me, r)))
    gain_copies = [c.remote(gains_ref, gains_all.at[z, me], dp=peer_of(me, r)) for r in range(1, dp)]
    misc_copies = [c.remote(misc_ref, misc_all.at[me], dp=peer_of(me, r)) for r in range(1, dp)]
    for copy in gain_copies + misc_copies + first:
        copy.start()

    def piece(buffer, p):
        return buffer.at[pl.ds(pl.multiple_of(p * rows, rows), rows)]

    own_tok = c.local(tokens_ref, piece(tok.at[0], z))
    own_tok.start()
    own_grad = c.local(outgrad_ref, piece(grads_ref.at[0], z))
    own_grad.start()

    def columns(k, n):
        return pl.ds(pl.multiple_of(k * n, n), n)

    pair = wq_ref.shape[1] // 2
    own_at = tuple(bit_of(bit) for bit in reversed(bits))
    core_copies = []
    for k, w in enumerate((wq_ref, wk_ref, wv_ref, wo_ref)):
        place = weights.at[own_at + (slice(None), pl.ds(k * pair, pair))]
        core_copies.append(c.remote(w.at[:, columns(1 - core, pair)], place, dp=peer_of(me, 1)))
        core_copies.append(c.local(w.at[:, columns(core, pair)], place))
    for copy in core_copies:
        copy.start()

    own_tok.wait()
    tok_line = Line(c, tok.at[0], z, depth, rows)
    tok_line.begin()
    tok_pass = [c.remote(tokens_ref, piece(tok.at[1], z), dp=peer_of(me, 1))]
    tok_pass[0].start()

    zeros[...] = jnp.zeros_like(zeros)
    pad = zeros.shape[1]
    pads = [c.local(zeros, down_ref.at[:, 0, pl.ds(hidden_units, pad)])]
    pads += [c.local(zeros, gateup_ref.at[:, k, pl.ds(hidden_units, pad)]) for k in range(2)]
    matrices = ((ed_ref, sd_ref, down_ref, 0), (eg_ref, sg_ref, gateup_ref, 0), (eu_ref, su_ref, gateup_ref, 1))
    slab = columns(me, slice_width)

    def group_copies(routed_src, shared_src, dst, k, r):
        group = (peer_of(me, r)) % 4
        many = (
            routed_src.at[pl.ds(group * routed, routed)],
            dst.at[pl.ds(0, routed), k, pl.ds(0, hidden_units), slab],
        )
        one = (shared_src.at[group], dst.at[routed, k, pl.ds(0, hidden_units), slab])
        if r == 0:
            return [c.local(*many), c.local(*one)]
        return [c.remote(*many, dp=peer_of(me, r)), c.remote(*one, dp=peer_of(me, r))]

    near = [[copy for r in (0, 1) for copy in group_copies(*m, r)] for m in matrices]
    far = [[copy for r in (2, 3) for copy in group_copies(*m, r)] for m in matrices]

    def upper_copies(dst, k):
        copies = []
        for bit in upper:
            n = bit * slice_width
            cols = pl.ds(pl.multiple_of(me // bit * n, n), n)
            place = dst.at[:, k, pl.ds(0, hidden_units), cols]
            copies.append(c.remote(place, place, dp=peer_of(me, bit)))
        return copies

    over = [upper_copies(m[2], m[3]) for m in matrices]

    for copy in core_copies:
        copy.wait()

    def weight_copies(order, half):
        have, copies = [1], []
        for bit in order:
            index = tuple(
                pl.ds(0, 2) if b in have else pl.ds(bit_of(b), 1) for b in reversed(bits)
            )
            place = weights.at[index + (slice(None), pl.ds(half * 2 * pair, 2 * pair))]
            copies.append(c.remote(place, place, dp=peer_of(me, bit)))
            have.append(bit)
        return copies

    qk_copies = weight_copies(bits[1:], 0)
    vo_copies = weight_copies(bits[:0:-1], 1)
    qk_copies[0].start()
    vo_copies[0].start()
    for copy in pads + [copy for m in near for copy in m]:
        copy.start()

    own_gains.wait()
    for copy in gain_copies:
        copy.wait_recv()
    gain_spread = [
        c.remote(gains_all.at[z], gains_all.at[z], tensor=(z + r) % depth) for r in range(1, depth)
    ]
    for copy in gain_spread:
        copy.start()

    def pass_on(buffer_from, buffer_to, passed):
        ups = [c.remote(piece(buffer_from, z - k), piece(buffer_to, z - k), dp=peer_of(me, 1)) for k in range(1, depth)]
        downs = [c.remote(piece(buffer_from, z + k), piece(buffer_to, z + k), dp=peer_of(me, 1)) for k in range(1, depth)]
        for k in range(1, depth):
            passed.append((ups[k - 1], z >= k))
            passed.append((downs[k - 1], z + k <= depth - 1))

        def each(k, p, up):
            (ups if up else downs)[k - 1].start()

        return each

    tok_passed = []
    pass_tok = pass_on(tok.at[0], tok.at[1], tok_passed)

    def line_step(line, k, each):
        top = depth - 1
        onward = line.sends(k) if k < top else (None, None)
        for up, copy, there, further in (
            (True, line.ups[k - 1], z >= k, onward[0]),
            (False, line.downs[k - 1], z + k <= top, onward[1]),
        ):
            pl.when(there)(copy.wait_recv)
            if further is not None:
                pl.when(further[1])(further[0].start)
            if each is not None:
                pl.when(there)(functools.partial(each, k, None, up))

    line_step(tok_line, 1, pass_tok)
    for k in range(1, len(bits) - 1):
        qk_copies[k - 1].wait_recv()
        qk_copies[k].start()
        vo_copies[k - 1].wait_recv()
        vo_copies[k].start()
    for m in far:
        for copy in m:
            copy.start()
    own_grad.wait()
    grad_line = Line(c, grads_ref.at[0], z, depth, rows)
    for k in range(2, depth):
        line_step(tok_line, k, pass_tok)
    grad_line.begin()

    for copy in gain_spread:
        copy.wait_recv()
    for d in range(dp):
        total = gains_all[0, d]
        for t in range(1, depth):
            total = total + gains_all[t, d]
        gain_rows[:, d * slice_width : (d + 1) * slice_width] = total

    def norm_rows(s):
        def block(i, carry):
            at = pl.ds(pl.multiple_of(i * rows, rows), rows)
            data = tok[s, at, :].astype(F32)
            scale = lax.rsqrt(jnp.mean(data * data, axis=-1, keepdims=True) + EPS)
            fnorm[at, :] = (data * scale * gain_rows[0:1, :]).astype(BF)
            return carry

        lax.fori_loop(0, depth, block, 0)

    own_misc.wait()
    for copy in misc_copies:
        copy.wait_recv()
    bias_in = jnp.zeros(misc_ref.shape, F32)
    sub = lax.broadcasted_iota(jnp.int32, misc_ref.shape, 0)
    for d in range(dp):
        bias_in = jnp.where(sub == d, misc_all[d, pl.ds(experts + 1 + core, 1), :], bias_in)
    bias_in = bias_in.astype(BF)
    heads3 = 3 * pair
    head_slice = head // dp
    lane = lax.broadcasted_iota(jnp.int32, (bias_in.shape[1], heads3), 1)
    sub = lax.broadcasted_iota(jnp.int32, (bias_in.shape[1], heads3), 0)
    place = (lane // head * head_slice + lane % head_slice == sub).astype(F32).astype(BF)
    spread = dot(bias_in, place)
    lane = lax.broadcasted_iota(jnp.int32, spread.shape, 1)
    sub = lax.broadcasted_iota(jnp.int32, spread.shape, 0)
    bias = jnp.sum(jnp.where(lane % head // head_slice == sub, spread, 0.0), axis=0, keepdims=True)

    qk_copies[-1].wait_recv()
    vo_copies[-1].wait_recv()
    pairs = pair // head

    def project(s):
        def block(i, carry):
            at = pl.ds(pl.multiple_of(i * 2 * rows, 2 * rows), 2 * rows)
            full = weights[...].reshape(width, 4 * pair)
            pre = dot(fnorm[at, :], full[:, : 3 * pair]) + bias
            cos_rows, sin_rows = cos_ref[at, :], sin_ref[at, :]
            for kind in range(3):
                for h in range(pairs):
                    a = (kind * pairs + h) * head
                    field = pre[:, a : a + head]
                    if kind < 2:
                        field = spin(field, cos_rows, sin_rows)
                    qkv_ref[kind, s * pairs + h, at, :] = field.astype(BF)
            return carry

        lax.fori_loop(0, depth // 2, block, 0)

    norm_rows(0)
    project(0)
    line_step(grad_line, 1, None)
    for copy in near[0]:
        copy.wait()
    for copy in far[0]:
        copy.wait_recv()
    over[0][0].start()
    tok_pass[0].wait()
    for copy, there in tok_passed:
        pl.when(there)(copy.wait)
    norm_rows(1)
    project(1)

    own_codes.wait()
    for copy in first:
        copy.wait()
    causal_block = seq_len // 2

    def attend(s):
        flags = codes_all[s]
        sub = lax.broadcasted_iota(jnp.int32, flags.shape, 0)
        flags = jnp.where(sub == 8, flags, 0).astype(F32).astype(BF)
        for h in range(pairs):
            for b in range(2):
                at = slice(b * causal_block, (b + 1) * causal_block)
                seen = dot(flags[:, at], flags, 0, 0)
                row = lax.broadcasted_iota(jnp.int32, seen.shape, 0) + b * causal_block
                col = lax.broadcasted_iota(jnp.int32, seen.shape, 1)
                scores = dot(qkv_ref[0, s * pairs + h, at, :], qkv_ref[1, s * pairs + h], 1, 1)
                scores = scores * head ** (-0.5)
                scores = jnp.where(jnp.logical_or(col <= row, seen > 0.5), scores, -1e30)
                raised = jnp.exp(scores - jnp.max(scores, axis=1, keepdims=True))
                probs = raised / jnp.sum(raised, axis=1, keepdims=True)
                probs = probs.astype(BF)
                probs_ref[s * pairs + h, at, :] = probs
                mixed = dot(probs, qkv_ref[2, s * pairs + h])
                mix_ref[s, at, h * head : (h + 1) * head] = mixed.astype(BF)

    def project_out(s):
        for d in range(dp):
            index = tuple(d // bit % 2 for bit in reversed(bits))
            block = weights[index + (slice(None), slice(3 * pair, 4 * pair))]
            at = slice(d * slice_width, (d + 1) * slice_width)
            part[s, :, at] = dot(mix_ref[s], block, 1, 1).astype(BF)

    attend(1)
    if depth > 2:
        line_step(grad_line, 2, None)
    project_out(1)
    part_pass = c.remote(part.at[1], part_in, dp=peer_of(me, 1))
    part_pass.start()
    attend(0)
    project_out(0)
    for copy in near[1]:
        copy.wait()
    for copy in far[1]:
        copy.wait_recv()
    over[1][0].start()
    part_pass.wait_recv()

    scatter = []
    for r in list(range(1, depth)) + [0]:
        at = pl.ds(pl.multiple_of((z + r) % depth * rows, rows), rows)
        total = part[0, at, :].astype(F32) + part_in[at, :].astype(F32)
        if r:
            part[0, at, :] = total.astype(BF)
            copy = c.remote(part.at[0, at], scatter_in.at[r - 1], tensor=(z + r) % depth)
            copy.start()
            scatter.append(copy)
        else:
            hidden_ref[...] = total + tok[0, at, :].astype(F32)

    for k in range(3, depth):
        line_step(grad_line, k, None)
    x_grad = c.remote(grads_ref.at[0], grads_ref.at[2], dp=peer_of(me, 2))
    x_grad.start()
    own_pass = c.remote(grads_ref.at[0], grads_ref.at[1], dp=peer_of(me, 1))
    own_pass.start()
    for copy in near[2]:
        copy.wait()
    for copy in far[2]:
        copy.wait_recv()
    over[2][0].start()

    for copy in scatter:
        copy.wait_recv()
    total = hidden_ref[...]
    for r in range(1, depth):
        total = total + scatter_in[r - 1].astype(F32)
    hidden_ref[...] = total
    scale = lax.rsqrt(jnp.mean(total * total, axis=-1, keepdims=True) + EPS)
    norm_ref[0, pl.ds(pl.multiple_of(z * rows, rows), rows), :] = (
        total * scale * gain_rows[1:2, :]
    ).astype(BF)
    norm_line = Line(c, norm_ref.at[0], z, depth, rows)
    norm_line.begin()
    norm_own = c.remote(piece(norm_ref.at[0], z), piece(norm_ref.at[1], z), dp=peer_of(me, 1))
    norm_own.start()
    norm_passed = []
    pass_norm = pass_on(norm_ref.at[0], norm_ref.at[1], norm_passed)
    for k in range(1, depth):
        line_step(norm_line, k, pass_norm)

    x_grad.wait_recv()
    grad_pass = c.remote(grads_ref.at[2], grads_ref.at[3], dp=peer_of(me, 1))
    grad_pass.start()
    for k in range(1, len(upper)):
        for chain in over:
            chain[k - 1].wait_recv()
            chain[k].start()
    for chain in over:
        chain[-1].wait_recv()
    norm_own.wait()
    for copy, there in norm_passed:
        pl.when(there)(copy.wait)
    own_pass.wait()
    grad_pass.wait()
    for line in (tok_line, grad_line, norm_line):
        line.finish()
    for copy in pads:
        copy.wait()
    for copy in gain_copies + misc_copies + gain_spread + qk_copies + vo_copies + scatter:
        copy.wait_send()
    for copy in [part_pass, x_grad] + [y for m in far for y in m] + [y for m in over for y in m]:
        copy.wait_send()


def forward_call(dp, depth, experts, head, small, arrays, units):
    codes, misc, gains, cos_rows, sin_rows = small
    tokens, pair = arrays[0], arrays[2].shape[1] // 2
    rows, width = tokens.shape
    seq_len = rows * depth
    hidden_units = units[0].shape[1]
    hidden_pad = -(-hidden_units // 128) * 128
    routed = experts // 4
    bits = dp.bit_length() - 1
    pairs = pair // head
    vmem, hbm = pl.BlockSpec(memory_space=pltpu.VMEM), pl.BlockSpec(memory_space=pl.ANY)
    shape = jax.ShapeDtypeStruct
    return pl.pallas_call(
        functools.partial(forward_body, (dp, depth, experts, hidden_units, head)),
        in_specs=[vmem] * 5 + [hbm] * 12,
        out_specs=[vmem, vmem, hbm, hbm, hbm] + [vmem] * 8,
        out_shape=[
            shape((rows, width), F32),
            shape((2, seq_len, width), BF),
            shape((4, seq_len, width), BF),
            shape((routed + 1, 2, hidden_pad, width), BF),
            shape((routed + 1, 1, hidden_pad, width), BF),
            shape((4,) + codes.shape, codes.dtype),
            shape((dp,) + misc.shape, F32),
            shape((8, width), F32),
            shape((2, seq_len, width), BF),
            shape((2,) * bits + (width // dp, 4 * pair), BF),
            shape((3, 2 * pairs, seq_len, head), BF),
            shape((2 * pairs, seq_len, seq_len), BF),
            shape((2, seq_len, pair), BF),
        ],
        scratch_shapes=[
            pltpu.VMEM((seq_len, width), BF),
            pltpu.VMEM((2, seq_len, width), BF),
            pltpu.VMEM((seq_len, width), BF),
            pltpu.VMEM((depth - 1, rows, width), BF),
            pltpu.VMEM((depth, dp) + gains.shape, F32),
            pltpu.VMEM((routed + 1, hidden_pad - hidden_units, width), BF),
            pltpu.SemaphoreType.DMA((160,)),
            pltpu.SemaphoreType.DMA((160,)),
            pltpu.SemaphoreType.DMA((32,)),
        ],
        compiler_params=pltpu.CompilerParams(
            collective_id=0, has_side_effects=True, vmem_limit_bytes=VMEM_LIMIT
        ),
    )(codes, misc, gains, cos_rows, sin_rows, *arrays, *units)


def local_plain(
    dp,
    tokens,
    picture_ids,
    routes,
    slot_order,
    norm_gains,
    w_query,
    w_key,
    w_value,
    w_out,
    qkv_bias,
    router,
    shared_gate,
    shared_up,
    shared_down,
    expert_gate,
    expert_up,
    expert_down,
    out_grad,
):
    seq_len = picture_ids.shape[0]
    local_rows = tokens.shape[0]
    width = tokens.shape[1]
    experts, slice_width, hidden_units = expert_gate.shape
    top_count = routes.shape[1]
    capacity = 5 * seq_len * top_count // (4 * experts)
    heads_local = qkv_bias.shape[1]
    head_width = w_query.shape[1] // heads_local
    pair_heads = heads_local // 2
    pair_width = pair_heads * head_width
    mine_experts = experts // 4
    hidden_pad = -(-hidden_units // 128) * 128

    me = lax.axis_index("dp")
    zi = lax.axis_index("tensor")
    core, xi = me % 2, (me // 2) % 2
    group = me % 4
    bits = []
    while 2 ** (len(bits) + 1) <= dp:
        bits.append(2 ** len(bits))
    upper = bits[2:]

    def swap(array, bit):
        return lax.ppermute(array, "dp", [(i, i ^ bit) for i in range(dp)])

    def bit_of(bit):
        return (me // bit) % 2

    def join(mine, theirs, bit, axis):
        n = mine.shape[axis]
        shape = list(mine.shape)
        shape[axis] = 2 * n
        out = jnp.zeros(shape, mine.dtype)
        out = lax.dynamic_update_slice_in_dim(out, mine, n * bit_of(bit), axis)
        return lax.dynamic_update_slice_in_dim(out, theirs, n * (1 - bit_of(bit)), axis)

    def half(array, which, axis):
        n = array.shape[axis] // 2
        return lax.dynamic_slice_in_dim(array, which * n, n, axis)

    gains_z = lax.all_gather(norm_gains, "tensor", axis=1, tiled=True)
    misc_rows = 16
    bias_width = 3 * pair_heads * qkv_bias.shape[2]
    bias_cores = qkv_bias.reshape(3, 2, -1).swapaxes(0, 1).reshape(2, bias_width)

    def misc_pack(core_bias):
        wide = jnp.zeros((misc_rows, 2 * pair_width), BF)
        wide = wide.at[: experts + 1, :slice_width].set(router.T)
        wide = wide.at[experts + 1, :bias_width].set(core_bias)
        return wide.at[experts + 2 : experts + 4, :slice_width].set(gains_z)

    qk = jnp.concatenate(
        [w.reshape(slice_width, 2, pair_width) for w in (w_query, w_key)], axis=2
    )
    qk = jnp.concatenate(
        [qk, jnp.stack([misc_pack(bias_cores[0]), misc_pack(bias_cores[1])], axis=1)], axis=0
    )
    vo = jnp.concatenate(
        [w.reshape(slice_width, 2, pair_width) for w in (w_value, w_out.T)], axis=2
    )
    tokens_z = lax.all_gather(tokens, "tensor", axis=0, tiled=True)

    def gather_attention(pack, order):
        dims = (1,) * len(bits[1:])
        both = join(pick(pack, core, 1)[None], swap(pick(pack, 1 - core, 1), 1)[None], 1, 0)
        both = both.reshape(dims + both.shape)
        for bit in order:
            axis = len(bits) - 1 - bits.index(bit)
            both = join(both, swap(both, bit), bit, axis)
        return both.reshape((dp,) + both.shape[-2:])

    qk_all = gather_attention(qk, bits[1:])
    vo_full = gather_attention(vo, bits[:0:-1]).reshape(width, 2 * pair_width)
    qk_full = qk_all[:, :slice_width].reshape(width, 2 * pair_width)
    misc = qk_all[:, slice_width:]
    router_full = misc[:, : experts + 1, :slice_width].swapaxes(1, 2).reshape(width, -1)
    gain_rows = misc[:, experts + 2 : experts + 4, :slice_width].swapaxes(0, 1)
    gain_rows = gain_rows.reshape(2, width).astype(F32)
    bias = misc[:, experts + 1, :bias_width].astype(F32)
    bias = bias.reshape(dp, 3 * pair_heads, -1).swapaxes(0, 1).reshape(3, pair_width)

    tokens_sib = swap(tokens_z, 1)
    grad_z = lax.all_gather(out_grad, "tensor", axis=0, tiled=True)

    codes = jnp.concatenate([routes, slot_order], axis=1).T
    codes_x = swap(codes, 2)
    both_codes = swap(jnp.stack([codes, codes_x]), 1)
    codes_a = jnp.stack([codes, both_codes[0]])
    codes_b = jnp.stack([codes_x, both_codes[1]])
    pictures = jnp.stack([picture_ids, swap(picture_ids, 1)])

    def core_units(routed, shared):
        routed = routed.reshape(2, 2, mine_experts, hidden_units, slice_width)
        shared = shared.reshape(2, 2, 1, hidden_units, slice_width)

        def cut(which):
            return jnp.concatenate([pick(routed, which, 1), pick(shared, which, 1)], axis=1)

        return join(cut(core), swap(cut(1 - core), 1), 1, 3)

    def x_units(held):
        return join(pick(held, xi, 0), swap(pick(held, 1 - xi, 0), 2), 2, 2)

    def upper_units(held):
        for bit in upper[:-1]:
            held = join(held, swap(held, bit), bit, 2)
        return held, swap(held, upper[-1])

    def padded(*pairs):
        n = pairs[0][0].shape[-1]
        out = jnp.zeros((mine_experts + 1, len(pairs) * hidden_pad, 2 * n), BF)
        zero = jnp.int32(0)
        for k, (mine, theirs) in enumerate(pairs):
            row = jnp.int32(k * hidden_pad)
            out = lax.dynamic_update_slice(out, mine, (zero, row, n * bit_of(upper[-1])))
            out = lax.dynamic_update_slice(out, theirs, (zero, row, n * (1 - bit_of(upper[-1]))))
        return out

    down_c = core_units(expert_down, shared_down)
    gate_c = core_units(expert_gate.swapaxes(1, 2), shared_gate.T)
    up_c = core_units(expert_up.swapaxes(1, 2), shared_up.T)
    down_x = x_units(down_c)
    gate_x = x_units(gate_c)
    up_x = x_units(up_c)
    grad_x = swap(after(grad_z, up_x), 2)
    down_y = upper_units(down_x)
    gate_y = upper_units(gate_x)
    up_y = upper_units(up_x)

    rows_f = jnp.stack([tokens_z, tokens_sib]).astype(F32)
    qk_full = after(qk_full, down_c, gate_c, up_c)
    first_scale = lax.rsqrt(jnp.mean(rows_f * rows_f, axis=-1, keepdims=True) + EPS)
    first_norm = (rows_f * first_scale * gain_rows[0]).astype(BF)
    qk_pre = einsum("std,df->stf", first_norm, qk_full) + jnp.concatenate([bias[0], bias[1]])
    values = (einsum("std,df->stf", first_norm, vo_full[:, :pair_width]) + bias[2]).astype(BF)
    cos_part, sin_part = rope_tables(seq_len, head_width)
    qk_rot = rotate(
        qk_pre.reshape(2, seq_len, 2 * pair_heads, head_width), cos_part, sin_part
    ).astype(BF)
    qk_rot = after(qk_rot, down_x)
    queries, keys = qk_rot[:, :, :pair_heads], qk_rot[:, :, pair_heads:]
    values = values.reshape(2, seq_len, pair_heads, head_width)
    positions = jnp.arange(seq_len, dtype=jnp.int32)
    allowed = jnp.logical_or(
        positions[None, None, :] <= positions[None, :, None],
        pictures[:, :, None] * pictures[:, None, :] > 0,
    )
    score_scale = head_width ** (-0.5)
    scores = einsum("sqhd,skhd->shqk", queries, keys) * score_scale
    scores = jnp.where(allowed[:, None], scores, -1e30)
    weights = jnp.exp(scores - jnp.max(scores, axis=-1, keepdims=True))
    probs = weights / jnp.sum(weights, axis=-1, keepdims=True)
    probs_low = probs.astype(BF)
    head_mix = einsum("shqk,skhd->sqhd", probs_low, values).astype(BF)
    heads_out = after(head_mix.reshape(2, seq_len, pair_width), gate_x)
    out_weight = vo_full[:, pair_width:]
    attn_part = einsum("sqf,df->sqd", heads_out, out_weight)

    def core_sum(own, sibling):
        return own + swap(sibling.astype(BF), 1).astype(F32)

    def z_scatter(array):
        return lax.psum_scatter(
            array.astype(BF), "tensor", scatter_dimension=0, tiled=True
        ).astype(F32)

    inputs = tokens.astype(F32)
    hidden = inputs + z_scatter(core_sum(attn_part[0], attn_part[1]))
    hidden = after(hidden, up_x, down_y[1])
    second_scale = lax.rsqrt(jnp.mean(hidden * hidden, axis=-1, keepdims=True) + EPS)
    second_unit = hidden * second_scale
    second_norm = (second_unit * gain_rows[1]).astype(BF)
    norm_z = lax.all_gather(second_norm, "tensor", axis=0, tiled=True)
    norm_z = after(norm_z, gate_y[1], grad_x)
    down_all = padded(down_y)
    gateup_all = padded(gate_y, up_y)

    norm_x = swap(norm_z, 2)
    norm_a = jnp.stack([norm_z, swap(norm_z, 1)])
    norm_b = jnp.stack([norm_x, swap(norm_x, 1)])
    grad_a = jnp.stack([grad_z, swap(grad_z, 1)])
    grad_b = jnp.stack([grad_x, swap(grad_x, 1)])

    expert_ids = group * mine_experts + jnp.arange(mine_experts, dtype=jnp.int32)

    router_rows = jnp.pad(router_full.T, ((0, 16 - experts - 1), (0, 0)))
    group_ids = group.astype(jnp.int32).reshape(1)

    def slots_of(codes_in):
        routes_in, slots_in = codes_in[:, None, :top_count], codes_in[:, None, top_count:]
        matches = routes_in == expert_ids[None, :, None, None]
        return jnp.max(jnp.where(matches, slots_in, -1), axis=2)

    def feed(slots, rows, grads):
        slotted, slot_grad, pair, act, terms, pair_s, act_s, inner_s, probs_out = act_call(
            experts, capacity, group_ids, slots, rows, grads, router_rows, gateup_all, down_all
        )
        terms = jnp.concatenate([terms.swapaxes(1, 2), inner_s], axis=-1)
        flat = [a.reshape(mine_experts, -1, a.shape[-1]) for a in (slotted, slot_grad, pair, act)]
        shared = [a.reshape(1, -1, a.shape[-1]) for a in (rows, grads, pair_s, act_s)]
        return (pair, pair_s), (act, act_s), terms, (flat, shared), probs_out

    slots_a, slots_b = slots_of(codes_a), slots_of(codes_b)
    fed_a = feed(slots_a, norm_a, grad_a)
    fed_b = feed(slots_b, norm_b, grad_b)
    columns_a, columns_b = slots_a[..., None], slots_b[..., None]
    row_grad_b = back_call(columns_b, *fed_b[0], gateup_all)
    row_grad_a = back_call(after(columns_a, row_grad_b), *fed_a[0], gateup_all)
    row_out_b = back_call(after(columns_b, row_grad_a), *fed_b[1], down_all)
    row_out_a = back_call(columns_a, *fed_a[1], down_all)

    def spread(terms):
        wide = jnp.zeros(terms.shape[:-1] + (128,), F32)
        wide = lax.dynamic_update_slice_in_dim(
            wide, terms[..., :mine_experts], group * mine_experts, terms.ndim - 1
        )
        return wide.at[..., experts].set(terms[..., mine_experts])

    def group_sum(a, b):
        across = b[0].astype(F32) + swap(b[1].astype(BF), 1).astype(F32)
        near = a[0].astype(F32) + swap(a[1].astype(BF), 1).astype(F32)
        return near + swap(across.astype(BF), 2).astype(F32)

    grad_sum = group_sum(row_grad_a, row_grad_b)
    term_sum = group_sum(spread(fed_a[2]), spread(fed_b[2]))
    packed = z_scatter(jnp.concatenate([grad_sum, term_sum], axis=-1))
    second_grad, gate_sums = packed[:, :width], packed[:, width:]

    data_a, data_b = fed_a[3], fed_b[3]

    def unit_grads(left, right):
        return jnp.concatenate(
            [
                outer_call(
                    hidden_units,
                    hidden_pad,
                    dp,
                    [(data[k][left], data[k][right]) for data in (data_a, data_b)],
                )
                for k in range(2)
            ],
            axis=1,
        )

    def scatter_units(total):
        total = total.reshape((2,) * len(bits) + total.shape[1:])
        for bit in reversed(upper):
            axis = len(bits) - 1 - bits.index(bit)
            sent = half(total, 1 - bit_of(bit), axis)
            kept = half(total, bit_of(bit), axis)
            total = (kept.astype(F32) + swap(sent, bit).astype(F32)).astype(BF)
        total = total.reshape((2, 2) + total.shape[len(bits) :])
        held = join(pick(total, xi, 0)[None], swap(pick(total, 1 - xi, 0), 2)[None], 2, 0)
        return join(pick(held, core, 1)[:, None], swap(pick(held, 1 - core, 1), 1)[:, None], 1, 1)

    def split_units(held):
        routed = held[:, :, :mine_experts].reshape(experts, -1, slice_width)
        shared = held[:, :, mine_experts]
        return routed.astype(F32), shared.astype(F32)

    gateup_sum = scatter_units(unit_grads(2, 0))
    down_sum = scatter_units(unit_grads(3, 1))
    routed_gu, shared_gu = split_units(gateup_sum)
    routed_down, shared_down_sum = split_units(down_sum)
    shared_gu = shared_gu.reshape(4, 2, hidden_units, slice_width)
    egate_sum = routed_gu[:, :hidden_units].swapaxes(1, 2)
    eup_sum = routed_gu[:, hidden_units:].swapaxes(1, 2)
    sgate_sum = shared_gu[:, 0].reshape(-1, slice_width).T
    sup_sum = shared_gu[:, 1].reshape(-1, slice_width).T
    sdown_sum = shared_down_sum.reshape(-1, slice_width)

    row_start = zi * local_rows
    probs_local = lax.dynamic_slice_in_dim(fed_a[4][0], row_start, local_rows, 1).T
    probs_mine, weight_mine = probs_local[:, :experts], probs_local[:, experts]
    route_grad = gate_sums[:, :experts]
    expert_logit_grad = probs_mine * (
        route_grad - jnp.sum(probs_mine * route_grad, axis=-1, keepdims=True)
    )
    weight_logit_grad = gate_sums[:, experts] * weight_mine * (1.0 - weight_mine)
    logits_grad = jnp.concatenate([expert_logit_grad, weight_logit_grad[:, None]], axis=1).astype(
        BF
    )
    second_grad = second_grad + einsum("tf,df->td", logits_grad, router_full)
    gain_two_grad = jnp.sum(second_grad * second_unit, axis=0)
    unit_two = second_grad * gain_rows[1]
    hidden_grad = out_grad.astype(F32) + second_scale * (
        unit_two - second_unit * jnp.mean(unit_two * second_unit, axis=-1, keepdims=True)
    )
    attention_grad = hidden_grad.astype(BF)
    wide_logits = jnp.pad(logits_grad, ((0, 0), (0, 128 - experts - 1)))
    back_z = lax.all_gather(
        jnp.concatenate([attention_grad, wide_logits], axis=1), "tensor", axis=0, tiled=True
    )
    out_sum = after(group_sum(row_out_a, row_out_b), back_z)
    output = (hidden + z_scatter(out_sum)).astype(BF)
    logits_z = back_z[:, width : width + 16]
    back_own = back_z[:, :width]
    back_rows = jnp.stack([back_own, swap(back_own, 1)])

    router_part = einsum("tf,td->fd", logits_z, norm_z)[: experts + 1]

    out_proj = einsum("std,stf->df", back_rows, heads_out)
    mix_grad = einsum("std,df->stf", back_rows, out_weight).astype(BF)
    mix_grad = mix_grad.reshape(2, seq_len, pair_heads, head_width)
    prob_grad = einsum("sqhd,skhd->shqk", mix_grad, values)
    score_grad = (
        probs * (prob_grad - jnp.sum(probs * prob_grad, axis=-1, keepdims=True))
    ).astype(BF)
    query_rot = einsum("shqk,skhd->sqhd", score_grad, keys) * score_scale
    key_rot = einsum("shqk,sqhd->skhd", score_grad, queries) * score_scale
    value_grad = einsum("shqk,sqhd->skhd", probs_low, mix_grad)
    qk_grad = rotate(jnp.concatenate([query_rot, key_rot], axis=2), cos_part, -sin_part)
    qk_grad = qk_grad.astype(BF).reshape(2, seq_len, 2 * pair_width)
    v_grad = value_grad.astype(BF).reshape(2, seq_len, pair_width)
    first_part = einsum("stf,df->std", qk_grad, qk_full) + einsum(
        "stf,df->std", v_grad, vo_full[:, :pair_width]
    )
    first_grad = z_scatter(core_sum(first_part[0], first_part[1]))

    gain_one_grad = jnp.sum(first_part * (rows_f * first_scale), axis=(0, 1))
    bias_part = jnp.concatenate(
        [jnp.sum(qk_grad.astype(F32), axis=(0, 1)), jnp.sum(v_grad.astype(F32), axis=(0, 1))]
    )
    bias_part = bias_part.reshape(3 * pair_heads, dp, -1).swapaxes(0, 1).reshape(dp, 1, -1)
    gain_part = jnp.stack([gain_one_grad, gain_two_grad]).reshape(2, dp, slice_width)

    def wide_rows(rows):
        return jnp.pad(rows, ((0, 0), (0, 0), (0, 2 * pair_width - rows.shape[2])))

    misc_part = jnp.concatenate(
        [
            wide_rows(router_part.reshape(experts + 1, dp, slice_width).swapaxes(0, 1)),
            wide_rows(bias_part),
            wide_rows(gain_part.swapaxes(0, 1)),
            jnp.zeros((dp, misc_rows - experts - 4, 2 * pair_width), F32),
        ],
        axis=1,
    )
    qk_total = einsum("std,stf->df", first_norm, qk_grad).reshape(dp, slice_width, -1)
    qk_total = jnp.concatenate([qk_total, misc_part], axis=1)
    vo_total = jnp.concatenate([einsum("std,stf->df", first_norm, v_grad), out_proj], axis=1)
    vo_total = vo_total.reshape(dp, slice_width, -1)

    def scatter_attention(total, order):
        total = total.reshape((2,) * len(bits) + total.shape[1:])
        for bit in order:
            axis = len(bits) - 1 - bits.index(bit)
            sent = half(total, 1 - bit_of(bit), axis).astype(BF)
            total = half(total, bit_of(bit), axis) + swap(sent, bit).astype(F32)
        total = total.reshape((2,) + total.shape[-2:]).astype(BF)
        return pick(total, core, 0), swap(pick(total, 1 - core, 0), 1)

    def columns_of(mine, theirs):
        held = join(mine[:slice_width, None], theirs[:slice_width, None], 1, 1)
        first, second = held[..., :pair_width], held[..., pair_width:]
        return (
            first.reshape(slice_width, -1).astype(F32),
            second.reshape(slice_width, -1).astype(F32),
        )

    qk_mine, qk_theirs = scatter_attention(qk_total, bits[:0:-1])
    vo_mine, vo_theirs = scatter_attention(vo_total, bits[1:])
    qk_sums = columns_of(qk_mine, qk_theirs)
    vo_sums = columns_of(vo_mine, vo_theirs)
    misc_mine = qk_mine[slice_width:].astype(F32)
    misc_theirs = qk_theirs[slice_width:].astype(F32)
    misc_sum = misc_mine + misc_theirs
    router_sum = misc_sum[: experts + 1, :slice_width].T
    bias_sums = join(
        misc_mine[experts + 1, :bias_width].reshape(3, 1, pair_heads, -1),
        misc_theirs[experts + 1, :bias_width].reshape(3, 1, pair_heads, -1),
        1,
        1,
    ).reshape(3, heads_local, -1)
    gain_sums = lax.all_gather(
        misc_sum[experts + 2 : experts + 4, :slice_width], "tensor", axis=0, tiled=False
    )
    tensor = gain_sums.shape[0]
    gain_sums = jnp.sum(gain_sums, axis=0).reshape(2, tensor, -1)
    gain_sums = pick(gain_sums, zi, 1)

    unit_mine = inputs * lax.rsqrt(jnp.mean(inputs * inputs, axis=-1, keepdims=True) + EPS)
    scale_mine = lax.rsqrt(jnp.mean(inputs * inputs, axis=-1, keepdims=True) + EPS)
    unit_one = first_grad * gain_rows[0]
    input_grad = hidden_grad + scale_mine * (
        unit_one - unit_mine * jnp.mean(unit_one * unit_mine, axis=-1, keepdims=True)
    )
    return (
        output,
        input_grad.astype(BF),
        gain_sums,
        qk_sums[0],
        qk_sums[1],
        vo_sums[0],
        vo_sums[1].T,
        bias_sums,
        router_sum,
        sgate_sum,
        sup_sum,
        sdown_sum,
        egate_sum,
        eup_sum,
        routed_down,
    )


def local_fused(
    dp,
    depth,
    tokens,
    picture_ids,
    routes,
    slot_order,
    norm_gains,
    w_query,
    w_key,
    w_value,
    w_out,
    qkv_bias,
    router,
    shared_gate,
    shared_up,
    shared_down,
    expert_gate,
    expert_up,
    expert_down,
    out_grad,
):
    seq_len = picture_ids.shape[0]
    local_rows = tokens.shape[0]
    width = tokens.shape[1]
    experts, slice_width, hidden_units = expert_gate.shape
    top_count = routes.shape[1]
    capacity = 5 * seq_len * top_count // (4 * experts)
    heads_local = qkv_bias.shape[1]
    head_width = w_query.shape[1] // heads_local
    pair_heads = heads_local // 2
    pair_width = pair_heads * head_width
    mine_experts = experts // 4
    hidden_pad = -(-hidden_units // 128) * 128

    me = lax.axis_index("dp")
    zi = lax.axis_index("tensor")
    core, xi = me % 2, (me // 2) % 2
    group = me % 4
    bits = []
    while 2 ** (len(bits) + 1) <= dp:
        bits.append(2 ** len(bits))
    upper = bits[2:]

    def swap(array, bit):
        return lax.ppermute(array, "dp", [(i, i ^ bit) for i in range(dp)])

    def bit_of(bit):
        return (me // bit) % 2

    def join(mine, theirs, bit, axis):
        n = mine.shape[axis]
        shape = list(mine.shape)
        shape[axis] = 2 * n
        out = jnp.zeros(shape, mine.dtype)
        out = lax.dynamic_update_slice_in_dim(out, mine, n * bit_of(bit), axis)
        return lax.dynamic_update_slice_in_dim(out, theirs, n * (1 - bit_of(bit)), axis)

    def half(array, which, axis):
        n = array.shape[axis] // 2
        return lax.dynamic_slice_in_dim(array, which * n, n, axis)

    codes = jnp.concatenate([routes.T, slot_order.T, picture_ids[None]], axis=0)
    codes = jnp.pad(codes, ((0, 16 - codes.shape[0]), (0, 0)))
    bias_cores = qkv_bias.reshape(3, 2, -1).swapaxes(0, 1).reshape(2, -1)
    bias_width = bias_cores.shape[1]
    misc = jnp.zeros((16, slice_width), F32)
    misc = misc.at[: experts + 1].set(router.T.astype(F32))
    misc = misc.at[experts + 1 : experts + 3, :bias_width].set(bias_cores.astype(F32))
    gains = lax.dynamic_update_slice(
        jnp.zeros((8, slice_width), F32),
        norm_gains.astype(F32),
        (jnp.int32(0), zi * norm_gains.shape[1]),
    )
    cos_part, sin_part = rope_tables(seq_len, head_width)
    cos_rows = jnp.concatenate([cos_part, cos_part], axis=1)
    sin_rows = jnp.concatenate([-sin_part, sin_part], axis=1)
    (
        hidden,
        norm_own,
        grads_all,
        gateup_all,
        down_all,
        codes_all,
        misc_all,
        gain_rows,
        tok,
        attn_weights,
        qkv,
        probs_low,
        heads_out,
    ) = forward_call(
        dp,
        depth,
        experts,
        head_width,
        (codes, misc, gains, cos_rows, sin_rows),
        (tokens, out_grad, w_query, w_key, w_value, w_out.T),
        (
            expert_gate.swapaxes(1, 2),
            expert_up.swapaxes(1, 2),
            expert_down,
            shared_gate.T.reshape(4, hidden_units, slice_width),
            shared_up.T.reshape(4, hidden_units, slice_width),
            shared_down.reshape(4, hidden_units, slice_width),
        ),
    )
    gateup_all = gateup_all.reshape(mine_experts + 1, 2 * hidden_pad, width)
    down_all = down_all.reshape(mine_experts + 1, hidden_pad, width)
    attn_weights = attn_weights.reshape(width, 4 * pair_width)
    qk_full, vo_full = attn_weights[:, : 2 * pair_width], attn_weights[:, 2 * pair_width :]
    out_weight = vo_full[:, pair_width:]
    router_rows = jnp.concatenate([misc_all[d] for d in range(dp)], axis=1)
    router_rows = jnp.where(jnp.arange(16)[:, None] <= experts, router_rows, 0.0).astype(BF)
    router_full = router_rows[: experts + 1].T
    codes_all = codes_all[:, : 2 * top_count]
    codes_a, codes_b = codes_all[:2], codes_all[2:]
    misc_rows = 16
    rows_f = tok.astype(F32)
    first_scale = lax.rsqrt(jnp.mean(rows_f * rows_f, axis=-1, keepdims=True) + EPS)
    score_scale = head_width ** (-0.5)
    inputs = tokens.astype(F32)
    second_scale = lax.rsqrt(jnp.mean(hidden * hidden, axis=-1, keepdims=True) + EPS)
    second_unit = hidden * second_scale

    def core_sum(own, sibling):
        return own + swap(sibling.astype(BF), 1).astype(F32)

    def z_scatter(array):
        return lax.psum_scatter(
            array.astype(BF), "tensor", scatter_dimension=0, tiled=True
        ).astype(F32)

    norm_z = norm_own[0]
    norm_a = norm_own
    norm_x = swap(norm_z, 2)
    norm_b = jnp.stack([norm_x, swap(norm_x, 1)])
    grad_a, grad_b = grads_all[:2], grads_all[2:]

    expert_ids = group * mine_experts + jnp.arange(mine_experts, dtype=jnp.int32)

    group_ids = group.astype(jnp.int32).reshape(1)

    def slots_of(codes_in):
        routes_in, slots_in = codes_in[:, None, :top_count], codes_in[:, None, top_count:]
        matches = routes_in == expert_ids[None, :, None, None]
        return jnp.max(jnp.where(matches, slots_in, -1), axis=2)

    def feed(slots, rows, grads):
        slotted, slot_grad, pair, act, terms, pair_s, act_s, inner_s, probs_out = act_call(
            experts, capacity, group_ids, slots, rows, grads, router_rows, gateup_all, down_all
        )
        terms = jnp.concatenate([terms.swapaxes(1, 2), inner_s], axis=-1)
        flat = [a.reshape(mine_experts, -1, a.shape[-1]) for a in (slotted, slot_grad, pair, act)]
        shared = [a.reshape(1, -1, a.shape[-1]) for a in (rows, grads, pair_s, act_s)]
        return (pair, pair_s), (act, act_s), terms, (flat, shared), probs_out

    slots_a, slots_b = slots_of(codes_a), slots_of(codes_b)
    fed_a = feed(slots_a, norm_a, grad_a)
    fed_b = feed(slots_b, norm_b, grad_b)
    columns_a, columns_b = slots_a[..., None], slots_b[..., None]
    row_grad_b = back_call(columns_b, *fed_b[0], gateup_all)
    row_grad_a = back_call(after(columns_a, row_grad_b), *fed_a[0], gateup_all)
    row_out_b = back_call(after(columns_b, row_grad_a), *fed_b[1], down_all)
    row_out_a = back_call(columns_a, *fed_a[1], down_all)

    def spread(terms):
        wide = jnp.zeros(terms.shape[:-1] + (128,), F32)
        wide = lax.dynamic_update_slice_in_dim(
            wide, terms[..., :mine_experts], group * mine_experts, terms.ndim - 1
        )
        return wide.at[..., experts].set(terms[..., mine_experts])

    def group_sum(a, b):
        across = b[0].astype(F32) + swap(b[1].astype(BF), 1).astype(F32)
        near = a[0].astype(F32) + swap(a[1].astype(BF), 1).astype(F32)
        return near + swap(across.astype(BF), 2).astype(F32)

    grad_sum = group_sum(row_grad_a, row_grad_b)
    term_sum = group_sum(spread(fed_a[2]), spread(fed_b[2]))
    packed = z_scatter(jnp.concatenate([grad_sum, term_sum], axis=-1))
    second_grad, gate_sums = packed[:, :width], packed[:, width:]

    data_a, data_b = fed_a[3], fed_b[3]

    def unit_grads(left, right):
        return jnp.concatenate(
            [
                outer_call(
                    hidden_units,
                    hidden_pad,
                    dp,
                    [(data[k][left], data[k][right]) for data in (data_a, data_b)],
                )
                for k in range(2)
            ],
            axis=1,
        )

    def scatter_units(total):
        total = total.reshape((2,) * len(bits) + total.shape[1:])
        for bit in reversed(upper):
            axis = len(bits) - 1 - bits.index(bit)
            sent = half(total, 1 - bit_of(bit), axis)
            kept = half(total, bit_of(bit), axis)
            total = (kept.astype(F32) + swap(sent, bit).astype(F32)).astype(BF)
        total = total.reshape((2, 2) + total.shape[len(bits) :])
        held = join(pick(total, xi, 0)[None], swap(pick(total, 1 - xi, 0), 2)[None], 2, 0)
        return join(pick(held, core, 1)[:, None], swap(pick(held, 1 - core, 1), 1)[:, None], 1, 1)

    def split_units(held):
        routed = held[:, :, :mine_experts].reshape(experts, -1, slice_width)
        shared = held[:, :, mine_experts]
        return routed.astype(F32), shared.astype(F32)

    gateup_sum = scatter_units(unit_grads(2, 0))
    down_sum = scatter_units(unit_grads(3, 1))
    routed_gu, shared_gu = split_units(gateup_sum)
    routed_down, shared_down_sum = split_units(down_sum)
    shared_gu = shared_gu.reshape(4, 2, hidden_units, slice_width)
    egate_sum = routed_gu[:, :hidden_units].swapaxes(1, 2)
    eup_sum = routed_gu[:, hidden_units:].swapaxes(1, 2)
    sgate_sum = shared_gu[:, 0].reshape(-1, slice_width).T
    sup_sum = shared_gu[:, 1].reshape(-1, slice_width).T
    sdown_sum = shared_down_sum.reshape(-1, slice_width)

    row_start = zi * local_rows
    probs_local = lax.dynamic_slice_in_dim(fed_a[4][0], row_start, local_rows, 1).T
    probs_mine, weight_mine = probs_local[:, :experts], probs_local[:, experts]
    route_grad = gate_sums[:, :experts]
    expert_logit_grad = probs_mine * (
        route_grad - jnp.sum(probs_mine * route_grad, axis=-1, keepdims=True)
    )
    weight_logit_grad = gate_sums[:, experts] * weight_mine * (1.0 - weight_mine)
    logits_grad = jnp.concatenate([expert_logit_grad, weight_logit_grad[:, None]], axis=1).astype(
        BF
    )
    second_grad = second_grad + einsum("tf,df->td", logits_grad, router_full)
    gain_two_grad = jnp.sum(second_grad * second_unit, axis=0)
    unit_two = second_grad * gain_rows[1]
    hidden_grad = out_grad.astype(F32) + second_scale * (
        unit_two - second_unit * jnp.mean(unit_two * second_unit, axis=-1, keepdims=True)
    )
    attention_grad = hidden_grad.astype(BF)
    wide_logits = jnp.pad(logits_grad, ((0, 0), (0, 128 - experts - 1)))
    back_z = lax.all_gather(
        jnp.concatenate([attention_grad, wide_logits], axis=1), "tensor", axis=0, tiled=True
    )
    out_sum = after(group_sum(row_out_a, row_out_b), back_z)
    output = (hidden + z_scatter(out_sum)).astype(BF)
    logits_z = back_z[:, width : width + 16]
    back_own = back_z[:, :width]
    back_rows = jnp.stack([back_own, swap(back_own, 1)])

    router_part = einsum("tf,td->fd", logits_z, norm_z)[: experts + 1]

    first_norm = (rows_f * first_scale * gain_rows[0]).astype(BF)
    out_proj = einsum("std,stf->df", back_rows, heads_out)
    mix_grad = einsum("std,df->stf", back_rows, out_weight).astype(BF)
    mix_grad = mix_grad.reshape(2, seq_len, pair_heads, head_width).swapaxes(1, 2)
    mix_grad = mix_grad.reshape(2 * pair_heads, seq_len, head_width)
    queries, keys, values = qkv[0], qkv[1], qkv[2]
    prob_grad = einsum("nqd,nkd->nqk", mix_grad, values)
    probs = probs_low.astype(F32)
    score_grad = (
        probs * (prob_grad - jnp.sum(probs * prob_grad, axis=-1, keepdims=True))
    ).astype(BF)
    query_rot = einsum("nqk,nkd->nqd", score_grad, keys) * score_scale
    key_rot = einsum("nqk,nqd->nkd", score_grad, queries) * score_scale
    value_grad = einsum("nqk,nqd->nkd", probs_low, mix_grad)

    def unspin(field):
        return field * cos_rows - jnp.roll(field, head_width // 2, axis=-1) * sin_rows

    def lanes_of(field):
        field = field.reshape(2, pair_heads, seq_len, head_width).swapaxes(1, 2)
        return field.astype(BF).reshape(2, seq_len, pair_width)

    qk_grad = jnp.concatenate([lanes_of(unspin(query_rot)), lanes_of(unspin(key_rot))], axis=-1)
    v_grad = lanes_of(value_grad)
    first_part = einsum("stf,df->std", qk_grad, qk_full) + einsum(
        "stf,df->std", v_grad, vo_full[:, :pair_width]
    )
    first_grad = z_scatter(core_sum(first_part[0], first_part[1]))

    gain_one_grad = jnp.sum(first_part * (rows_f * first_scale), axis=(0, 1))
    bias_part = jnp.concatenate(
        [jnp.sum(qk_grad.astype(F32), axis=(0, 1)), jnp.sum(v_grad.astype(F32), axis=(0, 1))]
    )
    bias_part = bias_part.reshape(3 * pair_heads, dp, -1).swapaxes(0, 1).reshape(dp, 1, -1)
    gain_part = jnp.stack([gain_one_grad, gain_two_grad]).reshape(2, dp, slice_width)

    def wide_rows(rows):
        return jnp.pad(rows, ((0, 0), (0, 0), (0, 2 * pair_width - rows.shape[2])))

    misc_part = jnp.concatenate(
        [
            wide_rows(router_part.reshape(experts + 1, dp, slice_width).swapaxes(0, 1)),
            wide_rows(bias_part),
            wide_rows(gain_part.swapaxes(0, 1)),
            jnp.zeros((dp, misc_rows - experts - 4, 2 * pair_width), F32),
        ],
        axis=1,
    )
    qk_total = einsum("std,stf->df", first_norm, qk_grad).reshape(dp, slice_width, -1)
    qk_total = jnp.concatenate([qk_total, misc_part], axis=1)
    vo_total = jnp.concatenate([einsum("std,stf->df", first_norm, v_grad), out_proj], axis=1)
    vo_total = vo_total.reshape(dp, slice_width, -1)

    def scatter_attention(total, order):
        total = total.reshape((2,) * len(bits) + total.shape[1:])
        for bit in order:
            axis = len(bits) - 1 - bits.index(bit)
            sent = half(total, 1 - bit_of(bit), axis).astype(BF)
            total = half(total, bit_of(bit), axis) + swap(sent, bit).astype(F32)
        total = total.reshape((2,) + total.shape[-2:]).astype(BF)
        return pick(total, core, 0), swap(pick(total, 1 - core, 0), 1)

    def columns_of(mine, theirs):
        held = join(mine[:slice_width, None], theirs[:slice_width, None], 1, 1)
        first, second = held[..., :pair_width], held[..., pair_width:]
        return (
            first.reshape(slice_width, -1).astype(F32),
            second.reshape(slice_width, -1).astype(F32),
        )

    qk_mine, qk_theirs = scatter_attention(qk_total, bits[:0:-1])
    vo_mine, vo_theirs = scatter_attention(vo_total, bits[1:])
    qk_sums = columns_of(qk_mine, qk_theirs)
    vo_sums = columns_of(vo_mine, vo_theirs)
    misc_mine = qk_mine[slice_width:].astype(F32)
    misc_theirs = qk_theirs[slice_width:].astype(F32)
    misc_sum = misc_mine + misc_theirs
    router_sum = misc_sum[: experts + 1, :slice_width].T
    bias_sums = join(
        misc_mine[experts + 1, :bias_width].reshape(3, 1, pair_heads, -1),
        misc_theirs[experts + 1, :bias_width].reshape(3, 1, pair_heads, -1),
        1,
        1,
    ).reshape(3, heads_local, -1)
    gain_sums = lax.all_gather(
        misc_sum[experts + 2 : experts + 4, :slice_width], "tensor", axis=0, tiled=False
    )
    tensor = gain_sums.shape[0]
    gain_sums = jnp.sum(gain_sums, axis=0).reshape(2, tensor, -1)
    gain_sums = pick(gain_sums, zi, 1)

    unit_mine = inputs * lax.rsqrt(jnp.mean(inputs * inputs, axis=-1, keepdims=True) + EPS)
    scale_mine = lax.rsqrt(jnp.mean(inputs * inputs, axis=-1, keepdims=True) + EPS)
    unit_one = first_grad * gain_rows[0]
    input_grad = hidden_grad + scale_mine * (
        unit_one - unit_mine * jnp.mean(unit_one * unit_mine, axis=-1, keepdims=True)
    )
    return (
        output,
        input_grad.astype(BF),
        gain_sums,
        qk_sums[0],
        qk_sums[1],
        vo_sums[0],
        vo_sums[1].T,
        bias_sums,
        router_sum,
        sgate_sum,
        sup_sum,
        sdown_sum,
        egate_sum,
        eup_sum,
        routed_down,
    )


def solution(mesh):
    dp, depth = mesh.shape["dp"], mesh.shape["tensor"]

    def body(*arrays):
        if arrays[5].shape[0] % 128 == 0 and dp == 8 and depth == 4:
            return local_fused(dp, depth, *arrays)
        return local_plain(dp, *arrays)

    return jax.shard_map(
        body,
        mesh=mesh,
        in_specs=(
            P(("dp", "tensor"), None),
            P("dp"),
            P("dp", None),
            P("dp", None),
            P(None, ("dp", "tensor")),
            P("dp", "tensor"),
            P("dp", "tensor"),
            P("dp", "tensor"),
            P("tensor", "dp"),
            P(None, "tensor", "dp"),
            P("dp", None),
            P("dp", "tensor"),
            P("dp", "tensor"),
            P("tensor", "dp"),
            P(None, "dp", "tensor"),
            P(None, "dp", "tensor"),
            P(None, "tensor", "dp"),
            P(("dp", "tensor"), None),
        ),
        out_specs=(
            P(("dp", "tensor"), None),
            P(("dp", "tensor"), None),
            P(None, ("dp", "tensor")),
            P("dp", "tensor"),
            P("dp", "tensor"),
            P("dp", "tensor"),
            P("tensor", "dp"),
            P(None, "tensor", "dp"),
            P("dp", None),
            P("dp", "tensor"),
            P("dp", "tensor"),
            P("tensor", "dp"),
            P(None, "dp", "tensor"),
            P(None, "dp", "tensor"),
            P(None, "tensor", "dp"),
        ),
        check_vma=False,
    )
```

```python
import functools

import jax
import jax.numpy as jnp
from jax import lax
from jax.experimental import pallas as pl
from jax.experimental.pallas import tpu as pltpu
from jax.sharding import PartitionSpec as P

EPS = 1e-06
THETA = 1000000.0
BF = jnp.bfloat16
F32 = jnp.float32


def rope_tables(length, width):
    half_width = width // 2
    inverse = THETA ** (-(2.0 * jnp.arange(half_width, dtype=F32)) / width)
    angles = jnp.arange(length, dtype=F32)[:, None] * inverse[None, :]
    return jnp.cos(angles), jnp.sin(angles)


def rotate(field_in, cos_part, sin_part):
    half_width = field_in.shape[-1] // 2
    low, high = field_in[..., :half_width], field_in[..., half_width:]
    cos_rows, sin_rows = cos_part[:, None, :], sin_part[:, None, :]
    return jnp.concatenate(
        [low * cos_rows - high * sin_rows, high * cos_rows + low * sin_rows], axis=-1
    )


def einsum(spec, *args):
    return jnp.einsum(spec, *args, preferred_element_type=F32)


def silu_parts(gate_in):
    gate_sig = jax.nn.sigmoid(gate_in)
    return gate_in * gate_sig, gate_sig * (1.0 + gate_in * (1.0 - gate_sig))


def after(array, *others):
    return lax.optimization_barrier((array,) + others)[0]


def pick(array, index, axis):
    return lax.dynamic_index_in_dim(array, index, axis, keepdims=False)


VMEM_LIMIT = 58 * 2**20


def dot(left, right, left_dim=1, right_dim=0):
    return lax.dot_general(
        left, right, (((left_dim,), (right_dim,)), ((), ())), preferred_element_type=F32
    )


def call(body, grid, in_specs, out_specs, out_shape, flops, moved, scratch=()):
    return pl.pallas_call(
        body,
        grid=grid,
        in_specs=in_specs,
        out_specs=out_specs,
        out_shape=out_shape,
        scratch_shapes=scratch,
        cost_estimate=pl.CostEstimate(flops=flops, bytes_accessed=moved, transcendentals=0),
        compiler_params=pltpu.CompilerParams(vmem_limit_bytes=VMEM_LIMIT),
    )


def act_body(
    experts,
    units,
    group_ref,
    slot_ref,
    rows_ref,
    grads_ref,
    router_ref,
    gateup_ref,
    down_ref,
    slotted_ref,
    slotgrad_ref,
    pair_ref,
    act_ref,
    terms_ref,
    pair_s_ref,
    act_s_ref,
    inner_s_ref,
    probs_ref,
):
    unit = pl.program_id(1)
    half = gateup_ref.shape[1] // 2
    seq_len = rows_ref.shape[1]
    capacity = slotted_ref.shape[2]

    @pl.when(unit == 0)
    def _():
        logits = dot(router_ref[...], rows_ref[0], 1, 1)
        row = lax.broadcasted_iota(jnp.int32, logits.shape, 0)
        routed = jnp.where(row < experts, logits, -1e30)
        raised = jnp.exp(routed - jnp.max(routed, axis=0, keepdims=True))
        soft = raised / jnp.sum(raised, axis=0, keepdims=True)
        probs_ref[0] = jnp.where(row < experts, soft, jax.nn.sigmoid(logits))

    def parts(data, cot, weight):
        both = dot(data, gateup_ref[0], 1, 1)
        cot_in = dot(cot, down_ref[0], 1, 1)
        gate_in, up_in = both[:, :half], both[:, half:]
        gate_act, gate_slope = silu_parts(gate_in)
        act = gate_act * up_in
        inner = jnp.sum(act.astype(BF).astype(F32) * cot_in, axis=1, keepdims=True)
        cot_in = cot_in * weight
        return (
            (act * weight).astype(BF),
            (cot_in * up_in * gate_slope).astype(BF),
            (cot_in * gate_act).astype(BF),
            inner,
        )

    @pl.when(unit < units - 1)
    def _():
        slot = slot_ref[0, pl.ds(unit, 1), :]
        mask = lax.broadcasted_iota(jnp.int32, (capacity, seq_len), 0) == slot
        onehot = mask.astype(F32).astype(BF)
        slotted_ref[0, 0] = dot(onehot, rows_ref[0]).astype(BF)
        slotgrad_ref[0, 0] = dot(onehot, grads_ref[0]).astype(BF)
        probs = probs_ref[0]
        row = lax.broadcasted_iota(jnp.int32, probs.shape, 0)
        expert = group_ref[0] * (units - 1) + unit
        gate = jnp.sum(jnp.where(row == expert, probs, 0.0), axis=0, keepdims=True)
        weight = jnp.sum(jnp.where(mask, gate, 0.0), axis=1, keepdims=True)
        act, gate_grad, up_grad, inner = parts(slotted_ref[0, 0], slotgrad_ref[0, 0], weight)
        act_ref[0, 0] = act
        pair_ref[0, 0, :, :half] = gate_grad
        pair_ref[0, 0, :, half:] = up_grad
        terms_ref[0, pl.ds(unit, 1), :] = jnp.sum(
            jnp.where(mask, inner, 0.0), axis=0, keepdims=True
        )

    @pl.when(unit == units - 1)
    def _():
        logits = dot(rows_ref[0], router_ref[...], 1, 1)
        weight = jax.nn.sigmoid(logits[:, experts : experts + 1])
        act, gate_grad, up_grad, inner = parts(rows_ref[0], grads_ref[0], weight)
        act_s_ref[0] = act
        pair_s_ref[0, :, :half] = gate_grad
        pair_s_ref[0, :, half:] = up_grad
        inner_s_ref[0] = inner


def act_call(experts, capacity, group, slots, rows, grads, router, gateup, down):
    count, seq_len, width = rows.shape
    units, wide, _ = gateup.shape
    half = wide // 2
    routed = units - 1

    def seq(s, u):
        return (s, 0, 0)

    def unit(s, u):
        return (u, 0, 0)

    def slot(s, u):
        return (jnp.minimum(u, routed - 1), s, 0, 0)

    work = count * (routed * capacity + seq_len) * width
    return call(
        functools.partial(act_body, experts, units),
        (count, units),
        [
            pl.BlockSpec(memory_space=pltpu.SMEM),
            pl.BlockSpec((1, routed, seq_len), seq),
            pl.BlockSpec((1, seq_len, width), seq),
            pl.BlockSpec((1, seq_len, width), seq),
            pl.BlockSpec(router.shape, lambda s, u: (0, 0)),
            pl.BlockSpec((1, wide, width), unit),
            pl.BlockSpec((1, half, width), unit),
        ],
        [
            pl.BlockSpec((1, 1, capacity, width), slot),
            pl.BlockSpec((1, 1, capacity, width), slot),
            pl.BlockSpec((1, 1, capacity, wide), slot),
            pl.BlockSpec((1, 1, capacity, half), slot),
            pl.BlockSpec((1, routed, seq_len), seq),
            pl.BlockSpec((1, seq_len, wide), seq),
            pl.BlockSpec((1, seq_len, half), seq),
            pl.BlockSpec((1, seq_len, 1), seq),
            pl.BlockSpec((1,) + (router.shape[0], seq_len), seq),
        ],
        [
            jax.ShapeDtypeStruct((routed, count, capacity, width), BF),
            jax.ShapeDtypeStruct((routed, count, capacity, width), BF),
            jax.ShapeDtypeStruct((routed, count, capacity, wide), BF),
            jax.ShapeDtypeStruct((routed, count, capacity, half), BF),
            jax.ShapeDtypeStruct((count, routed, seq_len), F32),
            jax.ShapeDtypeStruct((count, seq_len, wide), BF),
            jax.ShapeDtypeStruct((count, seq_len, half), BF),
            jax.ShapeDtypeStruct((count, seq_len, 1), F32),
            jax.ShapeDtypeStruct((count, router.shape[0], seq_len), F32),
        ],
        2 * work * 3 * half + 4 * count * routed * capacity * seq_len * width,
        8 * count * seq_len * width * 2,
    )(group, slots, rows, grads, router, gateup, down)


def back_body(slot_ref, routed_ref, shared_ref, weight_ref, out_ref):
    routed, _, capacity, _ = routed_ref.shape
    seq_len = shared_ref.shape[1]
    total = dot(shared_ref[0], weight_ref[routed])
    lane = lax.broadcasted_iota(jnp.int32, (seq_len, capacity), 1)
    for e in range(routed):
        slot_rows = dot(routed_ref[e, 0], weight_ref[e]).astype(BF)
        onehot = (lane == slot_ref[0, e]).astype(F32).astype(BF)
        total = total + dot(onehot, slot_rows)
    out_ref[0] = total.astype(BF)


def back_call(slots, routed, shared, weight):
    units, wide, width = weight.shape
    count, seq_len, _ = shared.shape
    capacity = routed.shape[2]
    block = min(width, 512)
    work = count * ((units - 1) * capacity + seq_len) * width
    return call(
        back_body,
        (width // block, count),
        [
            pl.BlockSpec((1, units - 1, seq_len, 1), lambda j, s: (s, 0, 0, 0)),
            pl.BlockSpec((units - 1, 1, capacity, wide), lambda j, s: (0, s, 0, 0)),
            pl.BlockSpec((1, seq_len, wide), lambda j, s: (s, 0, 0)),
            pl.BlockSpec((units, wide, block), lambda j, s: (0, 0, j)),
        ],
        pl.BlockSpec((1, seq_len, block), lambda j, s: (s, 0, j)),
        jax.ShapeDtypeStruct((count, seq_len, width), BF),
        2 * work * wide + 2 * count * (units - 1) * capacity * seq_len * width,
        units * wide * width * 2 + count * seq_len * width * 2,
    )(slots, routed, shared, weight)


def outer_body(keep, pad, left_a, right_a, left_b, right_b, out_ref):
    total = dot(left_a[0], right_a[0], 0, 0) + dot(left_b[0], right_b[0], 0, 0)
    total = total.astype(BF)
    blocks, _, rows, slice_width = out_ref.shape
    for part in range(rows // keep):
        for k in range(blocks):
            out_ref[k, 0, part * keep : (part + 1) * keep] = total[
                part * pad : part * pad + keep, k * slice_width : (k + 1) * slice_width
            ]


def outer_call(keep, pad, dp, pairs):
    (left_a, right_a), (left_b, right_b) = pairs
    units, rows, wide = left_a.shape
    width = right_a.shape[2]
    slice_width = width // dp
    blocks = max(1, 512 // slice_width)
    kept = wide // pad * keep

    def left(n):
        return pl.BlockSpec((1, n, wide), lambda u, j: (u, 0, 0))

    def right(n):
        return pl.BlockSpec((1, n, blocks * slice_width), lambda u, j: (u, 0, j))

    return call(
        functools.partial(outer_body, keep, pad),
        (units, dp // blocks),
        [left(rows), right(rows), left(rows), right(rows)],
        pl.BlockSpec((blocks, 1, kept, slice_width), lambda u, j: (j, u, 0, 0)),
        jax.ShapeDtypeStruct((dp, units, kept, slice_width), BF),
        4 * units * rows * wide * width,
        units * rows * (wide + width) * 4,
    )(left_a, right_a, left_b, right_b)


def units_body(keep, pad, *refs):
    lefts, rights, outs = refs[:4], refs[4:8], refs[8:]
    unit, units = pl.program_id(0), pl.num_programs(0)

    def store(first, second):
        total = dot(lefts[first][0], rights[first][0], 0, 0)
        total = (total + dot(lefts[second][0], rights[second][0], 0, 0)).astype(BF)
        for part, out_ref in enumerate(outs):
            blocks, _, _, slice_width = out_ref.shape
            for k in range(blocks):
                out_ref[k, 0] = total[
                    part * pad : part * pad + keep, k * slice_width : (k + 1) * slice_width
                ]

    @pl.when(unit < units - 1)
    def _():
        store(0, 1)

    @pl.when(unit == units - 1)
    def _():
        store(2, 3)


def units_call(keep, pad, dp, routed, shared):
    lefts = [pair[0] for pair in routed + shared]
    rights = [pair[1] for pair in routed + shared]
    many, _, wide = lefts[0].shape
    width = rights[0].shape[2]
    slice_width = width // dp
    blocks = max(1, 512 // slice_width)
    parts = wide // pad
    last = dp // blocks - 1

    def spec(array, cols, shared_unit):
        def where(u, j):
            mine = (u == many) if shared_unit else (u < many)
            unit = 0 if shared_unit else jnp.minimum(u, many - 1)
            if cols:
                return (unit, 0, jnp.where(mine, j, 0 if shared_unit else last))
            return (unit, 0, 0)

        return pl.BlockSpec((1, array.shape[1], cols or wide), where)

    cols = blocks * slice_width
    return call(
        functools.partial(units_body, keep, pad),
        (many + 1, dp // blocks),
        [spec(a, 0, n > 1) for n, a in enumerate(lefts)]
        + [spec(a, cols, n > 1) for n, a in enumerate(rights)],
        [pl.BlockSpec((blocks, 1, keep, slice_width), lambda u, j: (j, u, 0, 0))] * parts,
        [jax.ShapeDtypeStruct((dp, many + 1, keep, slice_width), BF)] * parts,
        4 * (many * lefts[0].shape[1] + lefts[2].shape[1]) * wide * width,
        (many * lefts[0].shape[1] + lefts[2].shape[1]) * (wide + width) * 4,
    )(*lefts, *rights)


MESH = pl.DeviceIdType.MESH


class Copies:
    def __init__(self, send, recv, here):
        self.send, self.recv, self.here = send, recv, here
        self.remote_count = self.local_count = 0

    def remote(self, src, dst, **device):
        k = self.remote_count
        self.remote_count += 1
        return pltpu.make_async_remote_copy(
            src_ref=src,
            dst_ref=dst,
            send_sem=self.send.at[k],
            recv_sem=self.recv.at[k],
            device_id=device,
            device_id_type=MESH,
        )

    def local(self, src, dst):
        k = self.local_count
        self.local_count += 1
        return pltpu.make_async_copy(src, dst, self.here.at[k])


class Line:
    def __init__(self, copies, buffer, z, depth, rows):
        self.z, self.depth = z, depth

        def piece(p):
            return buffer.at[pl.ds(pl.multiple_of(p * rows, rows), rows)]

        def make(k, sign):
            p = z - sign * k
            return copies.remote(piece(p), piece(p), tensor=z + sign)

        self.ups = [make(k, 1) for k in range(depth - 1)]
        self.downs = [make(k, -1) for k in range(depth - 1)]

    def sends(self, k):
        z, top = self.z, self.depth - 1
        return (
            (self.ups[k], jnp.logical_and(z < top, z >= k)),
            (self.downs[k], jnp.logical_and(z > 0, z + k <= top)),
        )

    def begin(self):
        for copy, there in self.sends(0):
            pl.when(there)(copy.start)

    def finish(self):
        for k in range(self.depth - 1):
            for copy, there in self.sends(k):
                pl.when(there)(copy.wait_send)


def peer_of(me, r):
    out, bit = me, 1
    while bit <= r:
        if r & bit:
            out = out + bit - 2 * bit * (me // bit % 2)
        bit *= 2
    return out


def greet(me, z, dp, depth):
    barrier = pltpu.get_barrier_semaphore()
    for r in range(1, dp):
        pl.semaphore_signal(barrier, inc=1, device_id={"dp": peer_of(me, r)}, device_id_type=MESH)
    for r in range(1, depth):
        pl.semaphore_signal(
            barrier, inc=1, device_id={"tensor": (z + r) % depth}, device_id_type=MESH
        )
    pl.semaphore_wait(barrier, dp - 1 + depth - 1)


def spin(field, cos_rows, sin_rows):
    return field * cos_rows + pltpu.roll(field, field.shape[-1] // 2, 1) * sin_rows


def piece_of(buffer, p, rows):
    return buffer.at[pl.ds(pl.multiple_of(p * rows, rows), rows)]


def pass_on(c, source, target, z, depth, rows, sibling, passed):
    def make(p):
        return c.remote(piece_of(source, p, rows), piece_of(target, p, rows), dp=sibling)

    ups = [make(z - k) for k in range(1, depth)]
    downs = [make(z + k) for k in range(1, depth)]
    for k in range(1, depth):
        passed.append((ups[k - 1], z >= k))
        passed.append((downs[k - 1], z + k <= depth - 1))

    def each(k, up):
        (ups if up else downs)[k - 1].start()

    return each


def line_step(line, k, each=None):
    z, top = line.z, line.depth - 1
    onward = line.sends(k) if k < top else (None, None)
    for up, copy, there, further in (
        (True, line.ups[k - 1], z >= k, onward[0]),
        (False, line.downs[k - 1], z + k <= top, onward[1]),
    ):
        pl.when(there)(copy.wait_recv)
        if further is not None:
            pl.when(further[1])(further[0].start)
        if each is not None:
            pl.when(there)(functools.partial(each, k, up))


def forward_body(
    sizes,
    codes_ref,
    misc_ref,
    gains_ref,
    cos_ref,
    sin_ref,
    tokens_ref,
    outgrad_ref,
    wq_ref,
    wk_ref,
    wv_ref,
    wo_ref,
    eg_ref,
    eu_ref,
    ed_ref,
    sg_ref,
    su_ref,
    sd_ref,
    hidden_ref,
    norm_ref,
    grads_ref,
    gateup_ref,
    down_ref,
    codes_all,
    misc_all,
    gain_rows,
    tok,
    weights,
    qkv_ref,
    probs_ref,
    mix_ref,
    fnorm,
    part,
    part_in,
    scatter_in,
    gains_all,
    zeros,
    send,
    recv,
    here,
):
    dp, depth, experts, hidden_units, head = sizes
    me, z = lax.axis_index("dp"), lax.axis_index("tensor")
    core, x = me % 2, (me // 2) % 2
    bits = [2**k for k in range(dp.bit_length() - 1)]
    upper = bits[2:]
    rows, width = tokens_ref.shape
    seq_len = rows * depth
    slice_width = width // dp
    routed = experts // 4
    c = Copies(send, recv, here)

    def bit_of(bit):
        return (me // bit) % 2

    greet(me, z, dp, depth)

    first = []
    own_codes = c.local(codes_ref, codes_all.at[0])
    own_misc = c.local(misc_ref, misc_all.at[me])
    own_gains = c.local(gains_ref, gains_all.at[z, me])
    for copy in (own_codes, own_misc, own_gains):
        copy.start()
    for r in range(1, 4):
        first.append(c.remote(codes_ref, codes_all.at[r], dp=peer_of(me, r)))
    gain_copies = [c.remote(gains_ref, gains_all.at[z, me], dp=peer_of(me, r)) for r in range(1, dp)]
    misc_copies = [c.remote(misc_ref, misc_all.at[me], dp=peer_of(me, r)) for r in range(1, dp)]
    for copy in gain_copies + misc_copies + first:
        copy.start()

    def piece(buffer, p):
        return buffer.at[pl.ds(pl.multiple_of(p * rows, rows), rows)]

    own_tok = c.local(tokens_ref, piece(tok.at[0], z))
    own_tok.start()
    own_grad = c.local(outgrad_ref, piece(grads_ref.at[0], z))
    own_grad.start()

    def columns(k, n):
        return pl.ds(pl.multiple_of(k * n, n), n)

    pair = wq_ref.shape[1] // 2
    own_at = tuple(bit_of(bit) for bit in reversed(bits))
    core_copies = []
    for k, w in enumerate((wq_ref, wk_ref, wv_ref, wo_ref)):
        place = weights.at[own_at + (slice(None), pl.ds(k * pair, pair))]
        core_copies.append(c.remote(w.at[:, columns(1 - core, pair)], place, dp=peer_of(me, 1)))
        core_copies.append(c.local(w.at[:, columns(core, pair)], place))
    for copy in core_copies:
        copy.start()

    own_tok.wait()
    tok_line = Line(c, tok.at[0], z, depth, rows)
    tok_line.begin()
    tok_pass = [c.remote(tokens_ref, piece(tok.at[1], z), dp=peer_of(me, 1))]
    tok_pass[0].start()

    zeros[...] = jnp.zeros_like(zeros)
    pad = zeros.shape[1]
    pads = [c.local(zeros, down_ref.at[:, 0, pl.ds(hidden_units, pad)])]
    pads += [c.local(zeros, gateup_ref.at[:, k, pl.ds(hidden_units, pad)]) for k in range(2)]
    matrices = ((ed_ref, sd_ref, down_ref, 0), (eg_ref, sg_ref, gateup_ref, 0), (eu_ref, su_ref, gateup_ref, 1))
    slab = columns(me, slice_width)

    def group_copies(routed_src, shared_src, dst, k, r):
        group = (peer_of(me, r)) % 4
        many = (
            routed_src.at[pl.ds(group * routed, routed)],
            dst.at[pl.ds(0, routed), k, pl.ds(0, hidden_units), slab],
        )
        one = (shared_src.at[group], dst.at[routed, k, pl.ds(0, hidden_units), slab])
        if r == 0:
            return [c.local(*many), c.local(*one)]
        return [c.remote(*many, dp=peer_of(me, r)), c.remote(*one, dp=peer_of(me, r))]

    near = [[copy for r in (0, 1) for copy in group_copies(*m, r)] for m in matrices]
    far = [[copy for r in (2, 3) for copy in group_copies(*m, r)] for m in matrices]

    def upper_copies(dst, k):
        copies = []
        for bit in upper:
            n = bit * slice_width
            cols = pl.ds(pl.multiple_of(me // bit * n, n), n)
            place = dst.at[:, k, pl.ds(0, hidden_units), cols]
            copies.append(c.remote(place, place, dp=peer_of(me, bit)))
        return copies

    over = [upper_copies(m[2], m[3]) for m in matrices]

    for copy in core_copies:
        copy.wait()

    def weight_copies(order, half):
        have, copies = [1], []
        for bit in order:
            index = tuple(
                pl.ds(0, 2) if b in have else pl.ds(bit_of(b), 1) for b in reversed(bits)
            )
            place = weights.at[index + (slice(None), pl.ds(half * 2 * pair, 2 * pair))]
            copies.append(c.remote(place, place, dp=peer_of(me, bit)))
            have.append(bit)
        return copies

    qk_copies = weight_copies(bits[1:], 0)
    vo_copies = weight_copies(bits[:0:-1], 1)
    qk_copies[0].start()
    vo_copies[0].start()
    for copy in pads + [copy for m in near for copy in m]:
        copy.start()

    own_gains.wait()
    for copy in gain_copies:
        copy.wait_recv()
    gain_spread = [
        c.remote(gains_all.at[z], gains_all.at[z], tensor=(z + r) % depth) for r in range(1, depth)
    ]
    for copy in gain_spread:
        copy.start()

    tok_passed = []
    sibling = peer_of(me, 1)
    pass_tok = pass_on(c, tok.at[0], tok.at[1], z, depth, rows, sibling, tok_passed)

    line_step(tok_line, 1, pass_tok)
    for k in range(1, len(bits) - 1):
        qk_copies[k - 1].wait_recv()
        qk_copies[k].start()
        vo_copies[k - 1].wait_recv()
        vo_copies[k].start()
    for m in far:
        for copy in m:
            copy.start()
    own_grad.wait()
    grad_line = Line(c, grads_ref.at[0], z, depth, rows)
    for k in range(2, depth):
        line_step(tok_line, k, pass_tok)
    grad_line.begin()

    for copy in gain_spread:
        copy.wait_recv()
    for d in range(dp):
        total = gains_all[0, d]
        for t in range(1, depth):
            total = total + gains_all[t, d]
        gain_rows[:, d * slice_width : (d + 1) * slice_width] = total

    def norm_rows(s):
        def block(i, carry):
            at = pl.ds(pl.multiple_of(i * rows, rows), rows)
            data = tok[s, at, :].astype(F32)
            scale = lax.rsqrt(jnp.mean(data * data, axis=-1, keepdims=True) + EPS)
            fnorm[at, :] = (data * scale * gain_rows[0:1, :]).astype(BF)
            return carry

        lax.fori_loop(0, depth, block, 0)

    own_misc.wait()
    for copy in misc_copies:
        copy.wait_recv()
    bias_in = jnp.zeros(misc_ref.shape, F32)
    sub = lax.broadcasted_iota(jnp.int32, misc_ref.shape, 0)
    for d in range(dp):
        bias_in = jnp.where(sub == d, misc_all[d, pl.ds(experts + 1 + core, 1), :], bias_in)
    bias_in = bias_in.astype(BF)
    heads3 = 3 * pair
    head_slice = head // dp
    lane = lax.broadcasted_iota(jnp.int32, (bias_in.shape[1], heads3), 1)
    sub = lax.broadcasted_iota(jnp.int32, (bias_in.shape[1], heads3), 0)
    place = (lane // head * head_slice + lane % head_slice == sub).astype(F32).astype(BF)
    spread = dot(bias_in, place)
    lane = lax.broadcasted_iota(jnp.int32, spread.shape, 1)
    sub = lax.broadcasted_iota(jnp.int32, spread.shape, 0)
    bias = jnp.sum(jnp.where(lane % head // head_slice == sub, spread, 0.0), axis=0, keepdims=True)

    qk_copies[-1].wait_recv()
    vo_copies[-1].wait_recv()
    pairs = pair // head

    def project(s):
        def block(i, carry):
            at = pl.ds(pl.multiple_of(i * 2 * rows, 2 * rows), 2 * rows)
            full = weights[...].reshape(width, 4 * pair)
            pre = dot(fnorm[at, :], full[:, : 3 * pair]) + bias
            cos_rows, sin_rows = cos_ref[at, :], sin_ref[at, :]
            for kind in range(3):
                for h in range(pairs):
                    a = (kind * pairs + h) * head
                    field = pre[:, a : a + head]
                    if kind < 2:
                        field = spin(field, cos_rows, sin_rows)
                    qkv_ref[kind, s * pairs + h, at, :] = field.astype(BF)
            return carry

        lax.fori_loop(0, depth // 2, block, 0)

    norm_rows(0)
    project(0)
    line_step(grad_line, 1)
    for copy in near[0]:
        copy.wait()
    for copy in far[0]:
        copy.wait_recv()
    over[0][0].start()
    tok_pass[0].wait()
    for copy, there in tok_passed:
        pl.when(there)(copy.wait)
    norm_rows(1)
    project(1)

    own_codes.wait()
    for copy in first:
        copy.wait()
    causal_block = seq_len // 2

    def attend(s):
        flags = codes_all[s]
        sub = lax.broadcasted_iota(jnp.int32, flags.shape, 0)
        flags = jnp.where(sub == 8, flags, 0).astype(F32).astype(BF)
        for h in range(pairs):
            for b in range(2):
                at = slice(b * causal_block, (b + 1) * causal_block)
                seen = dot(flags[:, at], flags, 0, 0)
                row = lax.broadcasted_iota(jnp.int32, seen.shape, 0) + b * causal_block
                col = lax.broadcasted_iota(jnp.int32, seen.shape, 1)
                scores = dot(qkv_ref[0, s * pairs + h, at, :], qkv_ref[1, s * pairs + h], 1, 1)
                scores = scores * head ** (-0.5)
                scores = jnp.where(jnp.logical_or(col <= row, seen > 0.5), scores, -1e30)
                raised = jnp.exp(scores - jnp.max(scores, axis=1, keepdims=True))
                probs = raised / jnp.sum(raised, axis=1, keepdims=True)
                probs = probs.astype(BF)
                probs_ref[s * pairs + h, at, :] = probs
                mixed = dot(probs, qkv_ref[2, s * pairs + h])
                mix_ref[s, at, h * head : (h + 1) * head] = mixed.astype(BF)

    def project_out(s):
        for d in range(dp):
            index = tuple(d // bit % 2 for bit in reversed(bits))
            block = weights[index + (slice(None), slice(3 * pair, 4 * pair))]
            at = slice(d * slice_width, (d + 1) * slice_width)
            part[s, :, at] = dot(mix_ref[s], block, 1, 1).astype(BF)

    attend(1)
    if depth > 2:
        line_step(grad_line, 2)
    project_out(1)
    part_pass = c.remote(part.at[1], part_in, dp=peer_of(me, 1))
    part_pass.start()
    attend(0)
    project_out(0)
    for copy in near[1]:
        copy.wait()
    for copy in far[1]:
        copy.wait_recv()
    over[1][0].start()
    part_pass.wait_recv()

    scatter = []
    for r in list(range(1, depth)) + [0]:
        at = pl.ds(pl.multiple_of((z + r) % depth * rows, rows), rows)
        total = part[0, at, :].astype(F32) + part_in[at, :].astype(F32)
        if r:
            part[0, at, :] = total.astype(BF)
            copy = c.remote(part.at[0, at], scatter_in.at[r - 1], tensor=(z + r) % depth)
            copy.start()
            scatter.append(copy)
        else:
            hidden_ref[...] = total + tok[0, at, :].astype(F32)

    for k in range(3, depth):
        line_step(grad_line, k)
    x_grad = c.remote(grads_ref.at[0], grads_ref.at[2], dp=peer_of(me, 2))
    x_grad.start()
    own_pass = c.remote(grads_ref.at[0], grads_ref.at[1], dp=peer_of(me, 1))
    own_pass.start()
    for copy in near[2]:
        copy.wait()
    for copy in far[2]:
        copy.wait_recv()
    over[2][0].start()

    for copy in scatter:
        copy.wait_recv()
    total = hidden_ref[...]
    for r in range(1, depth):
        total = total + scatter_in[r - 1].astype(F32)
    hidden_ref[...] = total
    scale = lax.rsqrt(jnp.mean(total * total, axis=-1, keepdims=True) + EPS)
    norm_ref[0, pl.ds(pl.multiple_of(z * rows, rows), rows), :] = (
        total * scale * gain_rows[1:2, :]
    ).astype(BF)
    norm_line = Line(c, norm_ref.at[0], z, depth, rows)
    norm_line.begin()
    norm_own = c.remote(piece(norm_ref.at[0], z), piece(norm_ref.at[1], z), dp=peer_of(me, 1))
    norm_own.start()
    norm_passed = []
    pass_norm = pass_on(
        c, norm_ref.at[0], norm_ref.at[1], z, depth, rows, sibling, norm_passed
    )
    for k in range(1, depth):
        line_step(norm_line, k, pass_norm)

    x_grad.wait_recv()
    grad_pass = c.remote(grads_ref.at[2], grads_ref.at[3], dp=peer_of(me, 1))
    grad_pass.start()
    for k in range(1, len(upper)):
        for chain in over:
            chain[k - 1].wait_recv()
            chain[k].start()
    for chain in over:
        chain[-1].wait_recv()
    norm_own.wait()
    for copy, there in norm_passed:
        pl.when(there)(copy.wait)
    own_pass.wait()
    grad_pass.wait()
    for line in (tok_line, grad_line, norm_line):
        line.finish()
    for copy in pads:
        copy.wait()
    for copy in gain_copies + misc_copies + gain_spread + qk_copies + vo_copies + scatter:
        copy.wait_send()
    for copy in [part_pass, x_grad] + [y for m in far for y in m] + [y for m in over for y in m]:
        copy.wait_send()


def forward_call(dp, depth, experts, head, small, arrays, units):
    codes, misc, gains, cos_rows, sin_rows = small
    tokens, pair = arrays[0], arrays[2].shape[1] // 2
    rows, width = tokens.shape
    seq_len = rows * depth
    hidden_units = units[0].shape[1]
    hidden_pad = -(-hidden_units // 128) * 128
    routed = experts // 4
    bits = dp.bit_length() - 1
    pairs = pair // head
    vmem, hbm = pl.BlockSpec(memory_space=pltpu.VMEM), pl.BlockSpec(memory_space=pl.ANY)
    shape = jax.ShapeDtypeStruct
    return pl.pallas_call(
        functools.partial(forward_body, (dp, depth, experts, hidden_units, head)),
        in_specs=[vmem] * 5 + [hbm] * 12,
        out_specs=[vmem, vmem, hbm, hbm, hbm] + [vmem] * 8,
        out_shape=[
            shape((rows, width), F32),
            shape((2, seq_len, width), BF),
            shape((4, seq_len, width), BF),
            shape((routed + 1, 2, hidden_pad, width), BF),
            shape((routed + 1, 1, hidden_pad, width), BF),
            shape((4,) + codes.shape, codes.dtype),
            shape((dp,) + misc.shape, F32),
            shape((8, width), F32),
            shape((2, seq_len, width), BF),
            shape((2,) * bits + (width // dp, 4 * pair), BF),
            shape((3, 2 * pairs, seq_len, head), BF),
            shape((2 * pairs, seq_len, seq_len), BF),
            shape((2, seq_len, pair), BF),
        ],
        scratch_shapes=[
            pltpu.VMEM((seq_len, width), BF),
            pltpu.VMEM((2, seq_len, width), BF),
            pltpu.VMEM((seq_len, width), BF),
            pltpu.VMEM((depth - 1, rows, width), BF),
            pltpu.VMEM((depth, dp) + gains.shape, F32),
            pltpu.VMEM((routed + 1, hidden_pad - hidden_units, width), BF),
            pltpu.SemaphoreType.DMA((160,)),
            pltpu.SemaphoreType.DMA((160,)),
            pltpu.SemaphoreType.DMA((32,)),
        ],
        compiler_params=pltpu.CompilerParams(
            collective_id=0, has_side_effects=True, vmem_limit_bytes=VMEM_LIMIT
        ),
    )(codes, misc, gains, cos_rows, sin_rows, *arrays, *units)


def backward_body(
    sizes,
    terms_ref,
    probs_mine_ref,
    router_ref,
    gain_rows,
    cos_ref,
    sin_ref,
    hidden_ref,
    outgrad_ref,
    grad_a_ref,
    grad_b_ref,
    grad_c_ref,
    out_a_ref,
    out_b_ref,
    out_c_ref,
    down_ref,
    gate_ref,
    up_ref,
    tok_hbm,
    weights_hbm,
    qkv_hbm,
    probs_hbm,
    mix_hbm,
    norm_hbm,
    output_ref,
    input_ref,
    down_out,
    gate_out,
    up_out,
    attn_out,
    misc_out,
    gains_out,
    own_sum,
    arrived,
    three,
    scatter_in,
    terms_sum,
    terms_in,
    back,
    tok,
    weights,
    qkv,
    probs_ref,
    mix_ref,
    scales,
    qkv_grad,
    part_in,
    keep,
    total_a,
    first_qk,
    first_vo,
    second_in,
    misc_part,
    misc_in,
    gains_in,
    vectors,
    send,
    recv,
    here,
):
    dp, depth, experts, head = sizes
    me, z = lax.axis_index("dp"), lax.axis_index("tensor")
    core, x, y = me % 2, (me // 2) % 2, me // 4
    rows, width = output_ref.shape
    seq_len = rows * depth
    slice_width = width // dp
    pair = mix_ref.shape[2]
    pairs = pair // head
    bits = [1, 2, 4]
    c = Copies(send, recv, here)

    greet(me, z, dp, depth)

    matrices = ((gate_ref, gate_out), (up_ref, up_out), (down_ref, down_out))
    over = []
    for m, (source, _) in enumerate(matrices):
        other = source.at[pl.ds((1 - y) * 4, 4)]
        over.append(c.remote(other, arrived.at[m], dp=peer_of(me, 4)))
        over[m].start()
    grads = (grad_a_ref.at[0], grad_b_ref, grad_c_ref)
    loads = [c.local(grads[k], three.at[k]) for k in range(3)]
    for copy in loads:
        copy.start()
    own_loads = [
        c.local(source.at[pl.ds(y * 4, 4)], own_sum) for source, _ in matrices
    ]
    inputs = [
        c.local(a, b)
        for a, b in (
            (weights_hbm, weights),
            (mix_hbm, mix_ref),
            (qkv_hbm, qkv),
            (probs_hbm, probs_ref),
            (tok_hbm, tok),
        )
    ]
    own_loads[0].start()
    for copy in inputs:
        copy.start()

    def at_of(p):
        return pl.ds(pl.multiple_of(p * rows, rows), rows)

    for copy in loads:
        copy.wait()
    scatter, small = [], []
    for r in list(range(1, depth)) + [0]:
        at = at_of((z + r) % depth)
        total = three[0, at, :].astype(F32) + three[1, at, :].astype(F32)
        total = total + three[2, at, :].astype(F32)
        extra = terms_ref[0, at, :] + terms_ref[1, at, :] + terms_ref[2, at, :]
        if r:
            three[0, at, :] = total.astype(BF)
            terms_sum[at, :] = extra
            peer = (z + r) % depth
            scatter.append(c.remote(three.at[0, at], scatter_in.at[0, r - 1], tensor=peer))
            small.append(c.remote(terms_sum.at[at], terms_in.at[r - 1], tensor=peer))
            scatter[-1].start()
            small[-1].start()
        else:
            keep[0] = total
            terms_sum[at, :] = extra

    def add_over(m):
        own_loads[m].wait()
        over[m].wait_recv()
        copies = []
        for r in (2, 3, 1, 0):
            k = peer_of(me, r) % 4
            for unit in range(own_sum.shape[1]):
                arrived[m, k, unit] = (
                    own_sum[k, unit].astype(F32) + arrived[m, k, unit].astype(F32)
                ).astype(BF)
            place = matrices[m][1].at[me % 4]
            if r:
                copies.append(c.remote(arrived.at[m, k], place, dp=peer_of(me, r)))
            else:
                copies.append(c.local(arrived.at[m, k], place))
            copies[-1].start()
        if m + 1 < len(own_loads):
            own_loads[m + 1].start()
        return copies

    for copy in scatter:
        copy.wait_recv()
    for copy in small:
        copy.wait_recv()
    route = terms_sum[at_of(z), :]
    grad = keep[0]
    for r in range(1, depth):
        grad = grad + scatter_in[0, r - 1].astype(F32)
        route = route + terms_in[r - 1]
    probs_mine = probs_mine_ref[...]
    lane = lax.broadcasted_iota(jnp.int32, route.shape, 1)
    inner = jnp.sum(jnp.where(lane < experts, probs_mine * route, 0.0), axis=1, keepdims=True)
    logits = jnp.where(
        lane < experts,
        probs_mine * (route - inner),
        jnp.where(lane == experts, route * probs_mine * (1.0 - probs_mine), 0.0),
    ).astype(BF)
    grad = grad + dot(logits, router_ref[...])
    hidden = hidden_ref[...]
    scale = lax.rsqrt(jnp.mean(hidden * hidden, axis=-1, keepdims=True) + EPS)
    unit = hidden * scale
    vectors[1:2, :] = jnp.sum(grad * unit, axis=0, keepdims=True)
    grad = grad * gain_rows[1:2, :]
    grad = outgrad_ref[...].astype(F32) + scale * (
        grad - unit * jnp.mean(grad * unit, axis=-1, keepdims=True)
    )
    keep[0] = grad
    back[0, at_of(z), :width] = grad.astype(BF)
    back[0, at_of(z), width:] = logits

    line = Line(c, back.at[0], z, depth, rows)
    line.begin()
    sibling = peer_of(me, 1)
    back_own = c.remote(piece_of(back.at[0], z, rows), piece_of(back.at[1], z, rows), dp=sibling)
    back_own.start()
    passed = []
    pass_back = pass_on(c, back.at[0], back.at[1], z, depth, rows, sibling, passed)
    for copy in scatter:
        copy.wait_send()
    outs = (out_a_ref.at[0], out_b_ref, out_c_ref)
    out_loads = [c.local(outs[k], three.at[k]) for k in range(3)]
    for copy in out_loads:
        copy.start()
    units = add_over(0)
    line_step(line, 1, pass_back)

    for copy in inputs:
        copy.wait()

    def scale_rows(i, carry):
        at = at_of(i)
        for s in range(2):
            data = tok[s, at, :].astype(F32)
            scales[s, at, :] = lax.rsqrt(jnp.mean(data * data, axis=-1, keepdims=True) + EPS)
        return carry

    lax.fori_loop(0, depth, scale_rows, 0)
    line_step(line, 2, pass_back)
    for copy in out_loads:
        copy.wait()
    out_scatter = []
    for r in list(range(1, depth)) + [0]:
        at = at_of((z + r) % depth)
        total = three[0, at, :].astype(F32) + three[1, at, :].astype(F32)
        total = total + three[2, at, :].astype(F32)
        if r:
            three[0, at, :] = total.astype(BF)
            peer = (z + r) % depth
            out_scatter.append(c.remote(three.at[0, at], scatter_in.at[1, r - 1], tensor=peer))
        else:
            keep[1] = total + hidden_ref[...]
    line_step(line, 3, pass_back)
    back_own.wait()
    for copy, there in passed:
        pl.when(there)(copy.wait)
    for copy in out_scatter:
        copy.start()

    def block_of(d):
        return tuple(d // bit % 2 for bit in reversed(bits))

    def slab(d):
        return slice(d * slice_width, (d + 1) * slice_width)

    def attention(s):
        mixed = jnp.zeros((seq_len, pair), F32)
        for d in range(dp):
            block = weights[block_of(d) + (slice(None), slice(3 * pair, 4 * pair))]
            mixed = mixed + dot(back[s, :, slab(d)], block)
        mixed = mixed.astype(BF)
        for h in range(pairs):
            n = s * pairs + h
            cot = mixed[:, h * head : (h + 1) * head]
            key_total = jnp.zeros((seq_len, head), F32)
            value_total = jnp.zeros((seq_len, head), F32)
            for b in range(2):
                at = slice(b * seq_len // 2, (b + 1) * seq_len // 2)
                p_low = probs_ref[n, at, :]
                p = p_low.astype(F32)
                p_grad = dot(cot[at], qkv[2, n], 1, 1)
                s_grad = p * (p_grad - jnp.sum(p * p_grad, axis=1, keepdims=True))
                s_grad = s_grad.astype(BF)
                q_grad = dot(s_grad, qkv[1, n]) * head ** (-0.5)
                q_grad = spin(q_grad, cos_ref[at, :], -sin_ref[at, :])
                qkv_grad[s, at, h * head : (h + 1) * head] = q_grad.astype(BF)
                key_total = key_total + dot(s_grad, qkv[0, n, at, :], 0, 0)
                value_total = value_total + dot(p_low, cot[at], 0, 0)
            k_grad = spin(key_total * head ** (-0.5), cos_ref[...], -sin_ref[...])
            a = pair + h * head
            qkv_grad[s, :, a : a + head] = k_grad.astype(BF)
            qkv_grad[s, :, a + pair : a + pair + head] = value_total.astype(BF)

    def first_grad(s):
        for d in range(dp):
            block = weights[block_of(d) + (slice(None), slice(0, 3 * pair))]
            total = dot(qkv_grad[s], block, 1, 1)
            three[1 + s, :, slab(d)] = total.astype(BF)
            unit_block = tok[s, :, slab(d)].astype(F32) * scales[s]
            row = jnp.sum(total * unit_block, axis=0, keepdims=True)
            vectors[2 + s : 3 + s, slab(d)] = row

    attention(1)
    first_grad(1)
    part_pass = c.remote(three.at[2], part_in, dp=sibling)
    part_pass.start()
    units += add_over(1)
    attention(0)
    first_grad(0)
    part_pass.wait_recv()
    first_scatter = []
    for r in list(range(1, depth)) + [0]:
        at = at_of((z + r) % depth)
        total = three[1, at, :].astype(F32) + part_in[at, :].astype(F32)
        if r:
            three[1, at, :] = total.astype(BF)
            peer = (z + r) % depth
            copy = c.remote(three.at[1, at], scatter_in.at[2, r - 1], tensor=peer)
            copy.start()
            first_scatter.append(copy)
        else:
            keep[2] = total

    for d in range(dp):
        total = jnp.zeros((slice_width, 3 * pair), F32)
        out_total = jnp.zeros((slice_width, pair), F32)
        for s in range(2):
            data = tok[s, :, slab(d)].astype(F32) * scales[s] * gain_rows[0:1, slab(d)]
            total = total + dot(data.astype(BF), qkv_grad[s], 0, 0)
            out_total = out_total + dot(back[s, :, slab(d)], mix_ref[s], 0, 0)
        total_a[block_of(d) + (slice(None), slice(0, 3 * pair))] = total.astype(BF)
        total_a[block_of(d) + (slice(None), slice(3 * pair, 4 * pair))] = out_total.astype(BF)

    half = 2 * pair

    def index(y_at, x_at, k):
        return (y_at, x_at, slice(None), slice(None), pl.ds(k * half, half))

    every = pl.ds(0, 2)
    qk_first = c.remote(
        total_a.at[index(pl.ds(1 - y, 1), every, 0)], first_qk, dp=peer_of(me, 4)
    )
    vo_first = c.remote(
        total_a.at[index(every, pl.ds(1 - x, 1), 1)], first_vo, dp=peer_of(me, 2)
    )
    qk_first.start()
    vo_first.start()

    for copy in out_scatter:
        copy.wait_send()
    norm_load = c.local(norm_hbm.at[0], three.at[0])
    norm_load.start()
    norm_load.wait()
    router_part = dot(back[0, :, width:], three[0], 0, 0)
    ones = jnp.ones((16, seq_len), BF)
    bias_row = dot(ones, qkv_grad[0]) + dot(ones, qkv_grad[1])
    lane = lax.broadcasted_iota(jnp.int32, bias_row.shape, 1)
    sub = lax.broadcasted_iota(jnp.int32, bias_row.shape, 0)
    head_slice = head // dp
    bias_rows = jnp.where(lane % head // head_slice == sub, bias_row, 0.0)
    high = bias_rows.astype(BF)
    low = (bias_rows - high.astype(F32)).astype(BF)
    lane = lax.broadcasted_iota(jnp.int32, (3 * pair, slice_width), 1)
    sub = lax.broadcasted_iota(jnp.int32, (3 * pair, slice_width), 0)
    place = (sub // head * head_slice + sub % head_slice == lane).astype(F32).astype(BF)
    bias_rows = dot(high, place) + dot(low, place)
    sub = lax.broadcasted_iota(jnp.int32, (16, slice_width), 0)
    misc_copies = []
    for d in range(dp):
        tile = jnp.where(sub <= experts, router_part[:16, slab(d)], 0.0)
        tile = jnp.where(sub == experts + 1 + core, bias_rows[d : d + 1], tile)
        gain_one = vectors[2:3, slab(d)] + vectors[3:4, slab(d)]
        tile = jnp.where(sub == experts + 3, gain_one, tile)
        tile = jnp.where(sub == experts + 4, vectors[1:2, slab(d)], tile)
        misc_part[d] = tile
    for r in range(1, dp):
        to = peer_of(me, r)
        misc_copies.append(c.remote(misc_part.at[to], misc_in.at[r - 1], dp=to))
        misc_copies[-1].start()
    units += add_over(2)

    qk_first.wait()
    mine = index(pl.ds(y, 1), every, 0)
    total_a[mine] = (total_a[mine].astype(F32) + first_qk[...].astype(F32)).astype(BF)
    qk_second = c.remote(
        total_a.at[index(pl.ds(y, 1), pl.ds(1 - x, 1), 0)], second_in.at[0], dp=peer_of(me, 2)
    )
    qk_second.start()
    vo_first.wait()
    mine = index(every, pl.ds(x, 1), 1)
    total_a[mine] = (total_a[mine].astype(F32) + first_vo[...].astype(F32)).astype(BF)
    vo_second = c.remote(
        total_a.at[index(pl.ds(1 - y, 1), pl.ds(x, 1), 1)], second_in.at[1], dp=peer_of(me, 4)
    )
    vo_second.start()

    total = misc_part[me]
    for r, copy in enumerate(misc_copies):
        copy.wait_recv()
        total = total + misc_in[r]
    misc_out[...] = total
    gain_copies = []
    for r in range(1, depth):
        peer = (z + r) % depth
        gain_copies.append(c.remote(misc_out.at[8:16], gains_in.at[r - 1], tensor=peer))
        gain_copies[-1].start()

    finals = []
    for k, copy in enumerate((qk_second, vo_second)):
        copy.wait()
        mine = (y, x, slice(None), slice(None), pl.ds(k * half, half))
        total_a[mine] = (
            total_a[mine].astype(F32) + second_in[k, 0, 0].astype(F32)
        ).astype(BF)
        for other in (True, False):
            to = 1 - core if other else core
            source = total_a.at[y, x, to, :, pl.ds(k * half, half)]
            place = attn_out.at[core, :, pl.ds(k * half, half)]
            finals.append(c.remote(source, place, dp=sibling) if other else c.local(source, place))
            finals[-1].start()

    for copy in out_scatter:
        copy.wait_recv()
    total = keep[1]
    for r in range(1, depth):
        total = total + scatter_in[1, r - 1].astype(F32)
    output_ref[...] = total.astype(BF)
    for copy in first_scatter:
        copy.wait_recv()
    total = keep[2]
    for r in range(1, depth):
        total = total + scatter_in[2, r - 1].astype(F32)
    total = total * gain_rows[0:1, :]
    scale = scales[0, at_of(z), :]
    unit = tok[0, at_of(z), :].astype(F32) * scale
    total = keep[0] + scale * (total - unit * jnp.mean(total * unit, axis=-1, keepdims=True))
    input_ref[...] = total.astype(BF)

    total = misc_out[8:16, :]
    for r, copy in enumerate(gain_copies):
        copy.wait()
        total = total + gains_in[r]
    gains_out[...] = total
    for copy in finals + units:
        copy.wait()
    line.finish()
    for copy in over + small + first_scatter + misc_copies + [part_pass]:
        copy.wait_send()


def backward_call(dp, depth, experts, head, in_vmem, in_hbm):
    output_rows, width = in_vmem[6].shape
    seq_len = output_rows * depth
    slice_width = width // dp
    units = in_hbm[6].shape[1:]
    pair = in_hbm[13].shape[2]
    pairs = pair // head
    vmem, hbm = pl.BlockSpec(memory_space=pltpu.VMEM), pl.BlockSpec(memory_space=pl.ANY)
    shape = jax.ShapeDtypeStruct
    final = shape((4,) + units, BF)
    return pl.pallas_call(
        functools.partial(backward_body, (dp, depth, experts, head)),
        in_specs=[vmem] * len(in_vmem) + [hbm] * len(in_hbm),
        out_specs=[vmem, vmem, hbm, hbm, hbm, vmem, vmem, vmem],
        out_shape=[
            shape((output_rows, width), BF),
            shape((output_rows, width), BF),
            final,
            final,
            final,
            shape((2, slice_width, 4 * pair), BF),
            shape((16, slice_width), F32),
            shape((8, slice_width), F32),
        ],
        scratch_shapes=[
            pltpu.VMEM((4,) + units, BF),
            pltpu.VMEM((3, 4) + units, BF),
            pltpu.VMEM((3, seq_len, width), BF),
            pltpu.VMEM((3, depth - 1, output_rows, width), BF),
            pltpu.VMEM((seq_len, 128), F32),
            pltpu.VMEM((depth - 1, output_rows, 128), F32),
            pltpu.VMEM((2, seq_len, width + 128), BF),
            pltpu.VMEM((2, seq_len, width), BF),
            pltpu.VMEM((2, 2, 2, slice_width, 4 * pair), BF),
            pltpu.VMEM((3, 2 * pairs, seq_len, head), BF),
            pltpu.VMEM((2 * pairs, seq_len, seq_len), BF),
            pltpu.VMEM((2, seq_len, pair), BF),
            pltpu.VMEM((2, seq_len, 1), F32),
            pltpu.VMEM((2, seq_len, 3 * pair), BF),
            pltpu.VMEM((seq_len, width), BF),
            pltpu.VMEM((3, output_rows, width), F32),
            pltpu.VMEM((2, 2, 2, slice_width, 4 * pair), BF),
            pltpu.VMEM((1, 2, 2, slice_width, 2 * pair), BF),
            pltpu.VMEM((2, 1, 2, slice_width, 2 * pair), BF),
            pltpu.VMEM((2, 1, 1, 2, slice_width, 2 * pair), BF),
            pltpu.VMEM((dp, 16, slice_width), F32),
            pltpu.VMEM((dp - 1, 16, slice_width), F32),
            pltpu.VMEM((depth - 1, 8, slice_width), F32),
            pltpu.VMEM((8, width), F32),
            pltpu.SemaphoreType.DMA((96,)),
            pltpu.SemaphoreType.DMA((96,)),
            pltpu.SemaphoreType.DMA((40,)),
        ],
        compiler_params=pltpu.CompilerParams(
            collective_id=1, has_side_effects=True, vmem_limit_bytes=62 * 2**20
        ),
    )(*in_vmem, *in_hbm)


def local_plain(
    dp,
    tokens,
    picture_ids,
    routes,
    slot_order,
    norm_gains,
    w_query,
    w_key,
    w_value,
    w_out,
    qkv_bias,
    router,
    shared_gate,
    shared_up,
    shared_down,
    expert_gate,
    expert_up,
    expert_down,
    out_grad,
):
    seq_len = picture_ids.shape[0]
    local_rows = tokens.shape[0]
    width = tokens.shape[1]
    experts, slice_width, hidden_units = expert_gate.shape
    top_count = routes.shape[1]
    capacity = 5 * seq_len * top_count // (4 * experts)
    heads_local = qkv_bias.shape[1]
    head_width = w_query.shape[1] // heads_local
    pair_heads = heads_local // 2
    pair_width = pair_heads * head_width
    mine_experts = experts // 4
    hidden_pad = -(-hidden_units // 128) * 128

    me = lax.axis_index("dp")
    zi = lax.axis_index("tensor")
    core, xi = me % 2, (me // 2) % 2
    group = me % 4
    bits = []
    while 2 ** (len(bits) + 1) <= dp:
        bits.append(2 ** len(bits))
    upper = bits[2:]

    def swap(array, bit):
        return lax.ppermute(array, "dp", [(i, i ^ bit) for i in range(dp)])

    def bit_of(bit):
        return (me // bit) % 2

    def join(mine, theirs, bit, axis):
        n = mine.shape[axis]
        shape = list(mine.shape)
        shape[axis] = 2 * n
        out = jnp.zeros(shape, mine.dtype)
        out = lax.dynamic_update_slice_in_dim(out, mine, n * bit_of(bit), axis)
        return lax.dynamic_update_slice_in_dim(out, theirs, n * (1 - bit_of(bit)), axis)

    def half(array, which, axis):
        n = array.shape[axis] // 2
        return lax.dynamic_slice_in_dim(array, which * n, n, axis)

    gains_z = lax.all_gather(norm_gains, "tensor", axis=1, tiled=True)
    misc_rows = 16
    bias_width = 3 * pair_heads * qkv_bias.shape[2]
    bias_cores = qkv_bias.reshape(3, 2, -1).swapaxes(0, 1).reshape(2, bias_width)

    def misc_pack(core_bias):
        wide = jnp.zeros((misc_rows, 2 * pair_width), BF)
        wide = wide.at[: experts + 1, :slice_width].set(router.T)
        wide = wide.at[experts + 1, :bias_width].set(core_bias)
        return wide.at[experts + 2 : experts + 4, :slice_width].set(gains_z)

    qk = jnp.concatenate(
        [w.reshape(slice_width, 2, pair_width) for w in (w_query, w_key)], axis=2
    )
    qk = jnp.concatenate(
        [qk, jnp.stack([misc_pack(bias_cores[0]), misc_pack(bias_cores[1])], axis=1)], axis=0
    )
    vo = jnp.concatenate(
        [w.reshape(slice_width, 2, pair_width) for w in (w_value, w_out.T)], axis=2
    )
    tokens_z = lax.all_gather(tokens, "tensor", axis=0, tiled=True)

    def gather_attention(pack, order):
        dims = (1,) * len(bits[1:])
        both = join(pick(pack, core, 1)[None], swap(pick(pack, 1 - core, 1), 1)[None], 1, 0)
        both = both.reshape(dims + both.shape)
        for bit in order:
            axis = len(bits) - 1 - bits.index(bit)
            both = join(both, swap(both, bit), bit, axis)
        return both.reshape((dp,) + both.shape[-2:])

    qk_all = gather_attention(qk, bits[1:])
    vo_full = gather_attention(vo, bits[:0:-1]).reshape(width, 2 * pair_width)
    qk_full = qk_all[:, :slice_width].reshape(width, 2 * pair_width)
    misc = qk_all[:, slice_width:]
    router_full = misc[:, : experts + 1, :slice_width].swapaxes(1, 2).reshape(width, -1)
    gain_rows = misc[:, experts + 2 : experts + 4, :slice_width].swapaxes(0, 1)
    gain_rows = gain_rows.reshape(2, width).astype(F32)
    bias = misc[:, experts + 1, :bias_width].astype(F32)
    bias = bias.reshape(dp, 3 * pair_heads, -1).swapaxes(0, 1).reshape(3, pair_width)

    tokens_sib = swap(tokens_z, 1)
    grad_z = lax.all_gather(out_grad, "tensor", axis=0, tiled=True)

    codes = jnp.concatenate([routes, slot_order], axis=1).T
    codes_x = swap(codes, 2)
    both_codes = swap(jnp.stack([codes, codes_x]), 1)
    codes_a = jnp.stack([codes, both_codes[0]])
    codes_b = jnp.stack([codes_x, both_codes[1]])
    pictures = jnp.stack([picture_ids, swap(picture_ids, 1)])

    def core_units(routed, shared):
        routed = routed.reshape(2, 2, mine_experts, hidden_units, slice_width)
        shared = shared.reshape(2, 2, 1, hidden_units, slice_width)

        def cut(which):
            return jnp.concatenate([pick(routed, which, 1), pick(shared, which, 1)], axis=1)

        return join(cut(core), swap(cut(1 - core), 1), 1, 3)

    def x_units(held):
        return join(pick(held, xi, 0), swap(pick(held, 1 - xi, 0), 2), 2, 2)

    def upper_units(held):
        for bit in upper[:-1]:
            held = join(held, swap(held, bit), bit, 2)
        return held, swap(held, upper[-1])

    def padded(*pairs):
        n = pairs[0][0].shape[-1]
        out = jnp.zeros((mine_experts + 1, len(pairs) * hidden_pad, 2 * n), BF)
        zero = jnp.int32(0)
        for k, (mine, theirs) in enumerate(pairs):
            row = jnp.int32(k * hidden_pad)
            out = lax.dynamic_update_slice(out, mine, (zero, row, n * bit_of(upper[-1])))
            out = lax.dynamic_update_slice(out, theirs, (zero, row, n * (1 - bit_of(upper[-1]))))
        return out

    down_c = core_units(expert_down, shared_down)
    gate_c = core_units(expert_gate.swapaxes(1, 2), shared_gate.T)
    up_c = core_units(expert_up.swapaxes(1, 2), shared_up.T)
    down_x = x_units(down_c)
    gate_x = x_units(gate_c)
    up_x = x_units(up_c)
    grad_x = swap(after(grad_z, up_x), 2)
    down_y = upper_units(down_x)
    gate_y = upper_units(gate_x)
    up_y = upper_units(up_x)

    rows_f = jnp.stack([tokens_z, tokens_sib]).astype(F32)
    qk_full = after(qk_full, down_c, gate_c, up_c)
    first_scale = lax.rsqrt(jnp.mean(rows_f * rows_f, axis=-1, keepdims=True) + EPS)
    first_norm = (rows_f * first_scale * gain_rows[0]).astype(BF)
    qk_pre = einsum("std,df->stf", first_norm, qk_full) + jnp.concatenate([bias[0], bias[1]])
    values = (einsum("std,df->stf", first_norm, vo_full[:, :pair_width]) + bias[2]).astype(BF)
    cos_part, sin_part = rope_tables(seq_len, head_width)
    qk_rot = rotate(
        qk_pre.reshape(2, seq_len, 2 * pair_heads, head_width), cos_part, sin_part
    ).astype(BF)
    qk_rot = after(qk_rot, down_x)
    queries, keys = qk_rot[:, :, :pair_heads], qk_rot[:, :, pair_heads:]
    values = values.reshape(2, seq_len, pair_heads, head_width)
    positions = jnp.arange(seq_len, dtype=jnp.int32)
    allowed = jnp.logical_or(
        positions[None, None, :] <= positions[None, :, None],
        pictures[:, :, None] * pictures[:, None, :] > 0,
    )
    score_scale = head_width ** (-0.5)
    scores = einsum("sqhd,skhd->shqk", queries, keys) * score_scale
    scores = jnp.where(allowed[:, None], scores, -1e30)
    weights = jnp.exp(scores - jnp.max(scores, axis=-1, keepdims=True))
    probs = weights / jnp.sum(weights, axis=-1, keepdims=True)
    probs_low = probs.astype(BF)
    head_mix = einsum("shqk,skhd->sqhd", probs_low, values).astype(BF)
    heads_out = after(head_mix.reshape(2, seq_len, pair_width), gate_x)
    out_weight = vo_full[:, pair_width:]
    attn_part = einsum("sqf,df->sqd", heads_out, out_weight)

    def core_sum(own, sibling):
        return own + swap(sibling.astype(BF), 1).astype(F32)

    def z_scatter(array):
        return lax.psum_scatter(
            array.astype(BF), "tensor", scatter_dimension=0, tiled=True
        ).astype(F32)

    inputs = tokens.astype(F32)
    hidden = inputs + z_scatter(core_sum(attn_part[0], attn_part[1]))
    hidden = after(hidden, up_x, down_y[1])
    second_scale = lax.rsqrt(jnp.mean(hidden * hidden, axis=-1, keepdims=True) + EPS)
    second_unit = hidden * second_scale
    second_norm = (second_unit * gain_rows[1]).astype(BF)
    norm_z = lax.all_gather(second_norm, "tensor", axis=0, tiled=True)
    norm_z = after(norm_z, gate_y[1], grad_x)
    down_all = padded(down_y)
    gateup_all = padded(gate_y, up_y)

    norm_x = swap(norm_z, 2)
    norm_a = jnp.stack([norm_z, swap(norm_z, 1)])
    norm_b = jnp.stack([norm_x, swap(norm_x, 1)])
    grad_a = jnp.stack([grad_z, swap(grad_z, 1)])
    grad_b = jnp.stack([grad_x, swap(grad_x, 1)])

    expert_ids = group * mine_experts + jnp.arange(mine_experts, dtype=jnp.int32)

    router_rows = jnp.pad(router_full.T, ((0, 16 - experts - 1), (0, 0)))
    group_ids = group.astype(jnp.int32).reshape(1)

    def slots_of(codes_in):
        routes_in, slots_in = codes_in[:, None, :top_count], codes_in[:, None, top_count:]
        matches = routes_in == expert_ids[None, :, None, None]
        return jnp.max(jnp.where(matches, slots_in, -1), axis=2)

    def feed(slots, rows, grads):
        slotted, slot_grad, pair, act, terms, pair_s, act_s, inner_s, probs_out = act_call(
            experts, capacity, group_ids, slots, rows, grads, router_rows, gateup_all, down_all
        )
        terms = jnp.concatenate([terms.swapaxes(1, 2), inner_s], axis=-1)
        flat = [a.reshape(mine_experts, -1, a.shape[-1]) for a in (slotted, slot_grad, pair, act)]
        shared = [a.reshape(1, -1, a.shape[-1]) for a in (rows, grads, pair_s, act_s)]
        return (pair, pair_s), (act, act_s), terms, (flat, shared), probs_out

    slots_a, slots_b = slots_of(codes_a), slots_of(codes_b)
    fed_a = feed(slots_a, norm_a, grad_a)
    fed_b = feed(slots_b, norm_b, grad_b)
    columns_a, columns_b = slots_a[..., None], slots_b[..., None]
    row_grad_b = back_call(columns_b, *fed_b[0], gateup_all)
    row_grad_a = back_call(after(columns_a, row_grad_b), *fed_a[0], gateup_all)
    row_out_b = back_call(after(columns_b, row_grad_a), *fed_b[1], down_all)
    row_out_a = back_call(columns_a, *fed_a[1], down_all)

    def spread(terms):
        wide = jnp.zeros(terms.shape[:-1] + (128,), F32)
        wide = lax.dynamic_update_slice_in_dim(
            wide, terms[..., :mine_experts], group * mine_experts, terms.ndim - 1
        )
        return wide.at[..., experts].set(terms[..., mine_experts])

    def group_sum(a, b):
        across = b[0].astype(F32) + swap(b[1].astype(BF), 1).astype(F32)
        near = a[0].astype(F32) + swap(a[1].astype(BF), 1).astype(F32)
        return near + swap(across.astype(BF), 2).astype(F32)

    grad_sum = group_sum(row_grad_a, row_grad_b)
    term_sum = group_sum(spread(fed_a[2]), spread(fed_b[2]))
    packed = z_scatter(jnp.concatenate([grad_sum, term_sum], axis=-1))
    second_grad, gate_sums = packed[:, :width], packed[:, width:]

    data_a, data_b = fed_a[3], fed_b[3]

    def unit_grads(left, right):
        return jnp.concatenate(
            [
                outer_call(
                    hidden_units,
                    hidden_pad,
                    dp,
                    [(data[k][left], data[k][right]) for data in (data_a, data_b)],
                )
                for k in range(2)
            ],
            axis=1,
        )

    def scatter_units(total):
        total = total.reshape((2,) * len(bits) + total.shape[1:])
        for bit in reversed(upper):
            axis = len(bits) - 1 - bits.index(bit)
            sent = half(total, 1 - bit_of(bit), axis)
            kept = half(total, bit_of(bit), axis)
            total = (kept.astype(F32) + swap(sent, bit).astype(F32)).astype(BF)
        total = total.reshape((2, 2) + total.shape[len(bits) :])
        held = join(pick(total, xi, 0)[None], swap(pick(total, 1 - xi, 0), 2)[None], 2, 0)
        return join(pick(held, core, 1)[:, None], swap(pick(held, 1 - core, 1), 1)[:, None], 1, 1)

    def split_units(held):
        routed = held[:, :, :mine_experts].reshape(experts, -1, slice_width)
        shared = held[:, :, mine_experts]
        return routed.astype(F32), shared.astype(F32)

    gateup_sum = scatter_units(unit_grads(2, 0))
    down_sum = scatter_units(unit_grads(3, 1))
    routed_gu, shared_gu = split_units(gateup_sum)
    routed_down, shared_down_sum = split_units(down_sum)
    shared_gu = shared_gu.reshape(4, 2, hidden_units, slice_width)
    egate_sum = routed_gu[:, :hidden_units].swapaxes(1, 2)
    eup_sum = routed_gu[:, hidden_units:].swapaxes(1, 2)
    sgate_sum = shared_gu[:, 0].reshape(-1, slice_width).T
    sup_sum = shared_gu[:, 1].reshape(-1, slice_width).T
    sdown_sum = shared_down_sum.reshape(-1, slice_width)

    row_start = zi * local_rows
    probs_local = lax.dynamic_slice_in_dim(fed_a[4][0], row_start, local_rows, 1).T
    probs_mine, weight_mine = probs_local[:, :experts], probs_local[:, experts]
    route_grad = gate_sums[:, :experts]
    expert_logit_grad = probs_mine * (
        route_grad - jnp.sum(probs_mine * route_grad, axis=-1, keepdims=True)
    )
    weight_logit_grad = gate_sums[:, experts] * weight_mine * (1.0 - weight_mine)
    logits_grad = jnp.concatenate([expert_logit_grad, weight_logit_grad[:, None]], axis=1).astype(
        BF
    )
    second_grad = second_grad + einsum("tf,df->td", logits_grad, router_full)
    gain_two_grad = jnp.sum(second_grad * second_unit, axis=0)
    unit_two = second_grad * gain_rows[1]
    hidden_grad = out_grad.astype(F32) + second_scale * (
        unit_two - second_unit * jnp.mean(unit_two * second_unit, axis=-1, keepdims=True)
    )
    attention_grad = hidden_grad.astype(BF)
    wide_logits = jnp.pad(logits_grad, ((0, 0), (0, 128 - experts - 1)))
    back_z = lax.all_gather(
        jnp.concatenate([attention_grad, wide_logits], axis=1), "tensor", axis=0, tiled=True
    )
    out_sum = after(group_sum(row_out_a, row_out_b), back_z)
    output = (hidden + z_scatter(out_sum)).astype(BF)
    logits_z = back_z[:, width : width + 16]
    back_own = back_z[:, :width]
    back_rows = jnp.stack([back_own, swap(back_own, 1)])

    router_part = einsum("tf,td->fd", logits_z, norm_z)[: experts + 1]

    out_proj = einsum("std,stf->df", back_rows, heads_out)
    mix_grad = einsum("std,df->stf", back_rows, out_weight).astype(BF)
    mix_grad = mix_grad.reshape(2, seq_len, pair_heads, head_width)
    prob_grad = einsum("sqhd,skhd->shqk", mix_grad, values)
    score_grad = (
        probs * (prob_grad - jnp.sum(probs * prob_grad, axis=-1, keepdims=True))
    ).astype(BF)
    query_rot = einsum("shqk,skhd->sqhd", score_grad, keys) * score_scale
    key_rot = einsum("shqk,sqhd->skhd", score_grad, queries) * score_scale
    value_grad = einsum("shqk,sqhd->skhd", probs_low, mix_grad)
    qk_grad = rotate(jnp.concatenate([query_rot, key_rot], axis=2), cos_part, -sin_part)
    qk_grad = qk_grad.astype(BF).reshape(2, seq_len, 2 * pair_width)
    v_grad = value_grad.astype(BF).reshape(2, seq_len, pair_width)
    first_part = einsum("stf,df->std", qk_grad, qk_full) + einsum(
        "stf,df->std", v_grad, vo_full[:, :pair_width]
    )
    first_grad = z_scatter(core_sum(first_part[0], first_part[1]))

    gain_one_grad = jnp.sum(first_part * (rows_f * first_scale), axis=(0, 1))
    bias_part = jnp.concatenate(
        [jnp.sum(qk_grad.astype(F32), axis=(0, 1)), jnp.sum(v_grad.astype(F32), axis=(0, 1))]
    )
    bias_part = bias_part.reshape(3 * pair_heads, dp, -1).swapaxes(0, 1).reshape(dp, 1, -1)
    gain_part = jnp.stack([gain_one_grad, gain_two_grad]).reshape(2, dp, slice_width)

    def wide_rows(rows):
        return jnp.pad(rows, ((0, 0), (0, 0), (0, 2 * pair_width - rows.shape[2])))

    misc_part = jnp.concatenate(
        [
            wide_rows(router_part.reshape(experts + 1, dp, slice_width).swapaxes(0, 1)),
            wide_rows(bias_part),
            wide_rows(gain_part.swapaxes(0, 1)),
            jnp.zeros((dp, misc_rows - experts - 4, 2 * pair_width), F32),
        ],
        axis=1,
    )
    qk_total = einsum("std,stf->df", first_norm, qk_grad).reshape(dp, slice_width, -1)
    qk_total = jnp.concatenate([qk_total, misc_part], axis=1)
    vo_total = jnp.concatenate([einsum("std,stf->df", first_norm, v_grad), out_proj], axis=1)
    vo_total = vo_total.reshape(dp, slice_width, -1)

    def scatter_attention(total, order):
        total = total.reshape((2,) * len(bits) + total.shape[1:])
        for bit in order:
            axis = len(bits) - 1 - bits.index(bit)
            sent = half(total, 1 - bit_of(bit), axis).astype(BF)
            total = half(total, bit_of(bit), axis) + swap(sent, bit).astype(F32)
        total = total.reshape((2,) + total.shape[-2:]).astype(BF)
        return pick(total, core, 0), swap(pick(total, 1 - core, 0), 1)

    def columns_of(mine, theirs):
        held = join(mine[:slice_width, None], theirs[:slice_width, None], 1, 1)
        first, second = held[..., :pair_width], held[..., pair_width:]
        return (
            first.reshape(slice_width, -1).astype(F32),
            second.reshape(slice_width, -1).astype(F32),
        )

    qk_mine, qk_theirs = scatter_attention(qk_total, bits[:0:-1])
    vo_mine, vo_theirs = scatter_attention(vo_total, bits[1:])
    qk_sums = columns_of(qk_mine, qk_theirs)
    vo_sums = columns_of(vo_mine, vo_theirs)
    misc_mine = qk_mine[slice_width:].astype(F32)
    misc_theirs = qk_theirs[slice_width:].astype(F32)
    misc_sum = misc_mine + misc_theirs
    router_sum = misc_sum[: experts + 1, :slice_width].T
    bias_sums = join(
        misc_mine[experts + 1, :bias_width].reshape(3, 1, pair_heads, -1),
        misc_theirs[experts + 1, :bias_width].reshape(3, 1, pair_heads, -1),
        1,
        1,
    ).reshape(3, heads_local, -1)
    gain_sums = lax.all_gather(
        misc_sum[experts + 2 : experts + 4, :slice_width], "tensor", axis=0, tiled=False
    )
    tensor = gain_sums.shape[0]
    gain_sums = jnp.sum(gain_sums, axis=0).reshape(2, tensor, -1)
    gain_sums = pick(gain_sums, zi, 1)

    unit_mine = inputs * lax.rsqrt(jnp.mean(inputs * inputs, axis=-1, keepdims=True) + EPS)
    scale_mine = lax.rsqrt(jnp.mean(inputs * inputs, axis=-1, keepdims=True) + EPS)
    unit_one = first_grad * gain_rows[0]
    input_grad = hidden_grad + scale_mine * (
        unit_one - unit_mine * jnp.mean(unit_one * unit_mine, axis=-1, keepdims=True)
    )
    return (
        output,
        input_grad.astype(BF),
        gain_sums,
        qk_sums[0],
        qk_sums[1],
        vo_sums[0],
        vo_sums[1].T,
        bias_sums,
        router_sum,
        sgate_sum,
        sup_sum,
        sdown_sum,
        egate_sum,
        eup_sum,
        routed_down,
    )


def local_fused(
    dp,
    depth,
    tokens,
    picture_ids,
    routes,
    slot_order,
    norm_gains,
    w_query,
    w_key,
    w_value,
    w_out,
    qkv_bias,
    router,
    shared_gate,
    shared_up,
    shared_down,
    expert_gate,
    expert_up,
    expert_down,
    out_grad,
):
    seq_len = picture_ids.shape[0]
    local_rows = tokens.shape[0]
    width = tokens.shape[1]
    experts, slice_width, hidden_units = expert_gate.shape
    top_count = routes.shape[1]
    capacity = 5 * seq_len * top_count // (4 * experts)
    heads_local = qkv_bias.shape[1]
    head_width = w_query.shape[1] // heads_local
    pair_heads = heads_local // 2
    pair_width = pair_heads * head_width
    mine_experts = experts // 4
    hidden_pad = -(-hidden_units // 128) * 128

    me = lax.axis_index("dp")
    zi = lax.axis_index("tensor")
    core, xi = me % 2, (me // 2) % 2
    group = me % 4
    bits = []
    while 2 ** (len(bits) + 1) <= dp:
        bits.append(2 ** len(bits))
    upper = bits[2:]

    def swap(array, bit):
        return lax.ppermute(array, "dp", [(i, i ^ bit) for i in range(dp)])

    def bit_of(bit):
        return (me // bit) % 2

    def join(mine, theirs, bit, axis):
        n = mine.shape[axis]
        shape = list(mine.shape)
        shape[axis] = 2 * n
        out = jnp.zeros(shape, mine.dtype)
        out = lax.dynamic_update_slice_in_dim(out, mine, n * bit_of(bit), axis)
        return lax.dynamic_update_slice_in_dim(out, theirs, n * (1 - bit_of(bit)), axis)

    def half(array, which, axis):
        n = array.shape[axis] // 2
        return lax.dynamic_slice_in_dim(array, which * n, n, axis)

    codes = jnp.concatenate([routes.T, slot_order.T, picture_ids[None]], axis=0)
    codes = jnp.pad(codes, ((0, 16 - codes.shape[0]), (0, 0)))
    bias_cores = qkv_bias.reshape(3, 2, -1).swapaxes(0, 1).reshape(2, -1)
    bias_width = bias_cores.shape[1]
    misc = jnp.zeros((16, slice_width), F32)
    misc = misc.at[: experts + 1].set(router.T.astype(F32))
    misc = misc.at[experts + 1 : experts + 3, :bias_width].set(bias_cores.astype(F32))
    gains = lax.dynamic_update_slice(
        jnp.zeros((8, slice_width), F32),
        norm_gains.astype(F32),
        (jnp.int32(0), zi * norm_gains.shape[1]),
    )
    cos_part, sin_part = rope_tables(seq_len, head_width)
    cos_rows = jnp.concatenate([cos_part, cos_part], axis=1)
    sin_rows = jnp.concatenate([-sin_part, sin_part], axis=1)
    (
        hidden,
        norm_own,
        grads_all,
        gateup_all,
        down_all,
        codes_all,
        misc_all,
        gain_rows,
        tok,
        attn_weights,
        qkv,
        probs_low,
        heads_out,
    ) = forward_call(
        dp,
        depth,
        experts,
        head_width,
        (codes, misc, gains, cos_rows, sin_rows),
        (tokens, out_grad, w_query, w_key, w_value, w_out.T),
        (
            expert_gate.swapaxes(1, 2),
            expert_up.swapaxes(1, 2),
            expert_down,
            shared_gate.T.reshape(4, hidden_units, slice_width),
            shared_up.T.reshape(4, hidden_units, slice_width),
            shared_down.reshape(4, hidden_units, slice_width),
        ),
    )
    gateup_all = gateup_all.reshape(mine_experts + 1, 2 * hidden_pad, width)
    down_all = down_all.reshape(mine_experts + 1, hidden_pad, width)
    router_rows = jnp.concatenate([misc_all[d] for d in range(dp)], axis=1)
    router_rows = jnp.where(jnp.arange(16)[:, None] <= experts, router_rows, 0.0).astype(BF)
    router_full = router_rows[: experts + 1].T
    codes_all = codes_all[:, : 2 * top_count]
    codes_a, codes_b = codes_all[:2], codes_all[2:]
    norm_z = norm_own[0]
    norm_a = norm_own
    norm_x = swap(norm_z, 2)
    norm_b = jnp.stack([norm_x, swap(norm_x, 1)])
    grad_a, grad_b = grads_all[:2], grads_all[2:]

    expert_ids = group * mine_experts + jnp.arange(mine_experts, dtype=jnp.int32)

    group_ids = group.astype(jnp.int32).reshape(1)

    def slots_of(codes_in):
        routes_in, slots_in = codes_in[:, None, :top_count], codes_in[:, None, top_count:]
        matches = routes_in == expert_ids[None, :, None, None]
        return jnp.max(jnp.where(matches, slots_in, -1), axis=2)

    def feed(slots, rows, grads):
        slotted, slot_grad, pair, act, terms, pair_s, act_s, inner_s, probs_out = act_call(
            experts, capacity, group_ids, slots, rows, grads, router_rows, gateup_all, down_all
        )
        terms = jnp.concatenate([terms.swapaxes(1, 2), inner_s], axis=-1)
        flat = [a.reshape(mine_experts, -1, a.shape[-1]) for a in (slotted, slot_grad, pair, act)]
        shared = [a.reshape(1, -1, a.shape[-1]) for a in (rows, grads, pair_s, act_s)]
        return (pair, pair_s), (act, act_s), terms, (flat, shared), probs_out

    slots_a, slots_b = slots_of(codes_a), slots_of(codes_b)
    fed_a = feed(slots_a, norm_a, grad_a)
    fed_b = feed(slots_b, norm_b, grad_b)
    columns_a, columns_b = slots_a[..., None], slots_b[..., None]
    row_grad_b = back_call(columns_b, *fed_b[0], gateup_all)
    row_grad_a = back_call(after(columns_a, row_grad_b), *fed_a[0], gateup_all)
    row_out_b = back_call(after(columns_b, row_grad_a), *fed_b[1], down_all)
    row_out_a = back_call(columns_a, *fed_a[1], down_all)

    def spread(terms):
        wide = jnp.zeros(terms.shape[:-1] + (128,), F32)
        wide = lax.dynamic_update_slice_in_dim(
            wide, terms[..., :mine_experts], group * mine_experts, terms.ndim - 1
        )
        return wide.at[..., experts].set(terms[..., mine_experts])

    def over_group(a, b):
        across = b[0].astype(F32) + swap(b[1], 1).astype(F32)
        return a, swap(a[1], 1), swap(across.astype(b.dtype), 2)

    grad_parts = over_group(row_grad_a, row_grad_b)
    terms_a, terms_b, terms_c = over_group(spread(fed_a[2]), spread(fed_b[2]))
    terms = jnp.stack([terms_a[0], terms_b, terms_c])
    out_parts = over_group(row_out_a, row_out_b)

    data_a, data_b = fed_a[3], fed_b[3]

    def unit_grads(left, right):
        pairs = [[(data[k][left], data[k][right]) for data in (data_a, data_b)] for k in range(2)]
        return units_call(hidden_units, hidden_pad, dp, *pairs)

    gate_total, up_total = unit_grads(2, 0)
    down_total = unit_grads(3, 1)[0]
    probs_mine = lax.dynamic_slice_in_dim(fed_a[4][0], zi * local_rows, local_rows, 1).T
    probs_mine = jnp.pad(probs_mine, ((0, 0), (0, 128 - probs_mine.shape[1])))
    router_wide = jnp.pad(router_rows, ((0, 128 - router_rows.shape[0]), (0, 0)))
    output, input_grad, down_sum, gate_sum, up_sum, attn_sum, misc_sum, gains_sum = backward_call(
        dp,
        depth,
        experts,
        head_width,
        (terms, probs_mine, router_wide, gain_rows, cos_rows, sin_rows, hidden, out_grad),
        grad_parts
        + out_parts
        + (down_total, gate_total, up_total, tok, attn_weights, qkv, probs_low, heads_out, norm_own),
    )

    def split_units(held):
        routed = held[:, :mine_experts].reshape(experts, hidden_units, slice_width)
        shared = held[:, mine_experts].reshape(-1, slice_width)
        return routed.astype(F32), shared.astype(F32)

    egate_sum, sgate_sum = split_units(gate_sum)
    eup_sum, sup_sum = split_units(up_sum)
    edown_sum, sdown_sum = split_units(down_sum)

    def columns_of(kind):
        held = attn_sum[:, :, kind * pair_width : (kind + 1) * pair_width].swapaxes(0, 1)
        return held.reshape(slice_width, -1).astype(F32)

    bias_sums = misc_sum[experts + 1 : experts + 3, :bias_width].reshape(2, 3, pair_heads, -1)
    bias_sums = bias_sums.swapaxes(0, 1).reshape(3, heads_local, -1)
    piece = norm_gains.shape[1]
    gain_sums = lax.dynamic_slice(gains_sum[3:5], (jnp.int32(0), zi * piece), (2, piece))
    return (
        output,
        input_grad,
        gain_sums,
        columns_of(0),
        columns_of(1),
        columns_of(2),
        columns_of(3).T,
        bias_sums,
        misc_sum[: experts + 1].T,
        sgate_sum.T,
        sup_sum.T,
        sdown_sum,
        egate_sum.swapaxes(1, 2),
        eup_sum.swapaxes(1, 2),
        edown_sum,
    )


def solution(mesh):
    dp, depth = mesh.shape["dp"], mesh.shape["tensor"]

    def body(*arrays):
        if arrays[5].shape[0] % 128 == 0 and dp == 8 and depth == 4:
            return local_fused(dp, depth, *arrays)
        return local_plain(dp, *arrays)

    return jax.shard_map(
        body,
        mesh=mesh,
        in_specs=(
            P(("dp", "tensor"), None),
            P("dp"),
            P("dp", None),
            P("dp", None),
            P(None, ("dp", "tensor")),
            P("dp", "tensor"),
            P("dp", "tensor"),
            P("dp", "tensor"),
            P("tensor", "dp"),
            P(None, "tensor", "dp"),
            P("dp", None),
            P("dp", "tensor"),
            P("dp", "tensor"),
            P("tensor", "dp"),
            P(None, "dp", "tensor"),
            P(None, "dp", "tensor"),
            P(None, "tensor", "dp"),
            P(("dp", "tensor"), None),
        ),
        out_specs=(
            P(("dp", "tensor"), None),
            P(("dp", "tensor"), None),
            P(None, ("dp", "tensor")),
            P("dp", "tensor"),
            P("dp", "tensor"),
            P("dp", "tensor"),
            P("tensor", "dp"),
            P(None, "tensor", "dp"),
            P("dp", None),
            P("dp", "tensor"),
            P("dp", "tensor"),
            P("tensor", "dp"),
            P(None, "dp", "tensor"),
            P(None, "dp", "tensor"),
            P(None, "tensor", "dp"),
        ),
        check_vma=False,
    )
```

```python
import functools

import jax
import jax.numpy as jnp
from jax import lax
from jax.experimental import pallas as pl
from jax.experimental.pallas import tpu as pltpu
from jax.sharding import PartitionSpec as P

EPS = 1e-06
THETA = 1000000.0
BF = jnp.bfloat16
F32 = jnp.float32


def rope_tables(length, width):
    half_width = width // 2
    inverse = THETA ** (-(2.0 * jnp.arange(half_width, dtype=F32)) / width)
    angles = jnp.arange(length, dtype=F32)[:, None] * inverse[None, :]
    return jnp.cos(angles), jnp.sin(angles)


def rotate(field_in, cos_part, sin_part):
    half_width = field_in.shape[-1] // 2
    low, high = field_in[..., :half_width], field_in[..., half_width:]
    cos_rows, sin_rows = cos_part[:, None, :], sin_part[:, None, :]
    return jnp.concatenate(
        [low * cos_rows - high * sin_rows, high * cos_rows + low * sin_rows], axis=-1
    )


def einsum(spec, *args):
    return jnp.einsum(spec, *args, preferred_element_type=F32)


def silu_parts(gate_in):
    gate_sig = jax.nn.sigmoid(gate_in)
    return gate_in * gate_sig, gate_sig * (1.0 + gate_in * (1.0 - gate_sig))


def after(array, *others):
    return lax.optimization_barrier((array,) + others)[0]


def pick(array, index, axis):
    return lax.dynamic_index_in_dim(array, index, axis, keepdims=False)


VMEM_LIMIT = 58 * 2**20


def dot(left, right, left_dim=1, right_dim=0):
    return lax.dot_general(
        left, right, (((left_dim,), (right_dim,)), ((), ())), preferred_element_type=F32
    )


def call(body, grid, in_specs, out_specs, out_shape, flops, moved, scratch=()):
    return pl.pallas_call(
        body,
        grid=grid,
        in_specs=in_specs,
        out_specs=out_specs,
        out_shape=out_shape,
        scratch_shapes=scratch,
        cost_estimate=pl.CostEstimate(flops=flops, bytes_accessed=moved, transcendentals=0),
        compiler_params=pltpu.CompilerParams(vmem_limit_bytes=VMEM_LIMIT),
    )


def plain_act_body(
    experts,
    units,
    group_ref,
    slot_ref,
    rows_ref,
    grads_ref,
    router_ref,
    gateup_ref,
    down_ref,
    slotted_ref,
    slotgrad_ref,
    pair_ref,
    act_ref,
    terms_ref,
    pair_s_ref,
    act_s_ref,
    inner_s_ref,
    probs_ref,
):
    unit = pl.program_id(1)
    half = gateup_ref.shape[1] // 2
    seq_len = rows_ref.shape[1]
    capacity = slotted_ref.shape[2]

    @pl.when(unit == 0)
    def _():
        logits = dot(router_ref[...], rows_ref[0], 1, 1)
        row = lax.broadcasted_iota(jnp.int32, logits.shape, 0)
        routed = jnp.where(row < experts, logits, -1e30)
        raised = jnp.exp(routed - jnp.max(routed, axis=0, keepdims=True))
        soft = raised / jnp.sum(raised, axis=0, keepdims=True)
        probs_ref[0] = jnp.where(row < experts, soft, jax.nn.sigmoid(logits))

    def parts(data, cot, weight):
        both = dot(data, gateup_ref[0], 1, 1)
        cot_in = dot(cot, down_ref[0], 1, 1)
        gate_in, up_in = both[:, :half], both[:, half:]
        gate_act, gate_slope = silu_parts(gate_in)
        act = gate_act * up_in
        inner = jnp.sum(act.astype(BF).astype(F32) * cot_in, axis=1, keepdims=True)
        cot_in = cot_in * weight
        return (
            (act * weight).astype(BF),
            (cot_in * up_in * gate_slope).astype(BF),
            (cot_in * gate_act).astype(BF),
            inner,
        )

    @pl.when(unit < units - 1)
    def _():
        slot = slot_ref[0, pl.ds(unit, 1), :]
        mask = lax.broadcasted_iota(jnp.int32, (capacity, seq_len), 0) == slot
        onehot = mask.astype(F32).astype(BF)
        slotted_ref[0, 0] = dot(onehot, rows_ref[0]).astype(BF)
        slotgrad_ref[0, 0] = dot(onehot, grads_ref[0]).astype(BF)
        probs = probs_ref[0]
        row = lax.broadcasted_iota(jnp.int32, probs.shape, 0)
        expert = group_ref[0] * (units - 1) + unit
        gate = jnp.sum(jnp.where(row == expert, probs, 0.0), axis=0, keepdims=True)
        weight = jnp.sum(jnp.where(mask, gate, 0.0), axis=1, keepdims=True)
        act, gate_grad, up_grad, inner = parts(slotted_ref[0, 0], slotgrad_ref[0, 0], weight)
        act_ref[0, 0] = act
        pair_ref[0, 0, :, :half] = gate_grad
        pair_ref[0, 0, :, half:] = up_grad
        terms_ref[0, pl.ds(unit, 1), :] = jnp.sum(
            jnp.where(mask, inner, 0.0), axis=0, keepdims=True
        )

    @pl.when(unit == units - 1)
    def _():
        logits = dot(rows_ref[0], router_ref[...], 1, 1)
        weight = jax.nn.sigmoid(logits[:, experts : experts + 1])
        act, gate_grad, up_grad, inner = parts(rows_ref[0], grads_ref[0], weight)
        act_s_ref[0] = act
        pair_s_ref[0, :, :half] = gate_grad
        pair_s_ref[0, :, half:] = up_grad
        inner_s_ref[0] = inner


def plain_act_call(experts, capacity, group, slots, rows, grads, router, gateup, down):
    count, seq_len, width = rows.shape
    units, wide, _ = gateup.shape
    half = wide // 2
    routed = units - 1

    def seq(s, u):
        return (s, 0, 0)

    def unit(s, u):
        return (u, 0, 0)

    def slot(s, u):
        return (jnp.minimum(u, routed - 1), s, 0, 0)

    work = count * (routed * capacity + seq_len) * width
    return call(
        functools.partial(plain_act_body, experts, units),
        (count, units),
        [
            pl.BlockSpec(memory_space=pltpu.SMEM),
            pl.BlockSpec((1, routed, seq_len), seq),
            pl.BlockSpec((1, seq_len, width), seq),
            pl.BlockSpec((1, seq_len, width), seq),
            pl.BlockSpec(router.shape, lambda s, u: (0, 0)),
            pl.BlockSpec((1, wide, width), unit),
            pl.BlockSpec((1, half, width), unit),
        ],
        [
            pl.BlockSpec((1, 1, capacity, width), slot),
            pl.BlockSpec((1, 1, capacity, width), slot),
            pl.BlockSpec((1, 1, capacity, wide), slot),
            pl.BlockSpec((1, 1, capacity, half), slot),
            pl.BlockSpec((1, routed, seq_len), seq),
            pl.BlockSpec((1, seq_len, wide), seq),
            pl.BlockSpec((1, seq_len, half), seq),
            pl.BlockSpec((1, seq_len, 1), seq),
            pl.BlockSpec((1,) + (router.shape[0], seq_len), seq),
        ],
        [
            jax.ShapeDtypeStruct((routed, count, capacity, width), BF),
            jax.ShapeDtypeStruct((routed, count, capacity, width), BF),
            jax.ShapeDtypeStruct((routed, count, capacity, wide), BF),
            jax.ShapeDtypeStruct((routed, count, capacity, half), BF),
            jax.ShapeDtypeStruct((count, routed, seq_len), F32),
            jax.ShapeDtypeStruct((count, seq_len, wide), BF),
            jax.ShapeDtypeStruct((count, seq_len, half), BF),
            jax.ShapeDtypeStruct((count, seq_len, 1), F32),
            jax.ShapeDtypeStruct((count, router.shape[0], seq_len), F32),
        ],
        2 * work * 3 * half + 4 * count * routed * capacity * seq_len * width,
        8 * count * seq_len * width * 2,
    )(group, slots, rows, grads, router, gateup, down)


def plain_back_body(slot_ref, routed_ref, shared_ref, weight_ref, out_ref):
    routed, _, capacity, _ = routed_ref.shape
    seq_len = shared_ref.shape[1]
    total = dot(shared_ref[0], weight_ref[routed])
    lane = lax.broadcasted_iota(jnp.int32, (seq_len, capacity), 1)
    for e in range(routed):
        slot_rows = dot(routed_ref[e, 0], weight_ref[e]).astype(BF)
        onehot = (lane == slot_ref[0, e]).astype(F32).astype(BF)
        total = total + dot(onehot, slot_rows)
    out_ref[0] = total.astype(BF)


def plain_back_call(slots, routed, shared, weight):
    units, wide, width = weight.shape
    count, seq_len, _ = shared.shape
    capacity = routed.shape[2]
    block = min(width, 512)
    work = count * ((units - 1) * capacity + seq_len) * width
    return call(
        plain_back_body,
        (width // block, count),
        [
            pl.BlockSpec((1, units - 1, seq_len, 1), lambda j, s: (s, 0, 0, 0)),
            pl.BlockSpec((units - 1, 1, capacity, wide), lambda j, s: (0, s, 0, 0)),
            pl.BlockSpec((1, seq_len, wide), lambda j, s: (s, 0, 0)),
            pl.BlockSpec((units, wide, block), lambda j, s: (0, 0, j)),
        ],
        pl.BlockSpec((1, seq_len, block), lambda j, s: (s, 0, j)),
        jax.ShapeDtypeStruct((count, seq_len, width), BF),
        2 * work * wide + 2 * count * (units - 1) * capacity * seq_len * width,
        units * wide * width * 2 + count * seq_len * width * 2,
    )(slots, routed, shared, weight)


def plain_outer_body(keep, pad, left_a, right_a, left_b, right_b, out_ref):
    total = dot(left_a[0], right_a[0], 0, 0) + dot(left_b[0], right_b[0], 0, 0)
    total = total.astype(BF)
    blocks, _, rows, slice_width = out_ref.shape
    for part in range(rows // keep):
        for k in range(blocks):
            out_ref[k, 0, part * keep : (part + 1) * keep] = total[
                part * pad : part * pad + keep, k * slice_width : (k + 1) * slice_width
            ]


def plain_outer_call(keep, pad, dp, pairs):
    (left_a, right_a), (left_b, right_b) = pairs
    units, rows, wide = left_a.shape
    width = right_a.shape[2]
    slice_width = width // dp
    blocks = max(1, 512 // slice_width)
    kept = wide // pad * keep

    def left(n):
        return pl.BlockSpec((1, n, wide), lambda u, j: (u, 0, 0))

    def right(n):
        return pl.BlockSpec((1, n, blocks * slice_width), lambda u, j: (u, 0, j))

    return call(
        functools.partial(plain_outer_body, keep, pad),
        (units, dp // blocks),
        [left(rows), right(rows), left(rows), right(rows)],
        pl.BlockSpec((blocks, 1, kept, slice_width), lambda u, j: (j, u, 0, 0)),
        jax.ShapeDtypeStruct((dp, units, kept, slice_width), BF),
        4 * units * rows * wide * width,
        units * rows * (wide + width) * 4,
    )(left_a, right_a, left_b, right_b)


def act_body(
    experts,
    top_count,
    group_ref,
    codes_ref,
    rows_ref,
    grads_ref,
    router_ref,
    gateup_ref,
    down_ref,
    slotted_ref,
    slotgrad_ref,
    pair_ref,
    act_ref,
    pair_s_ref,
    act_s_ref,
    terms_ref,
    probs_ref,
):
    unit, units = pl.program_id(0), pl.num_programs(0)
    half = gateup_ref.shape[1] // 2
    count, seq_len, width = rows_ref.shape
    capacity = slotted_ref.shape[2]

    @pl.when(unit == 0)
    def _():
        for s in range(count):
            logits = dot(router_ref[...], rows_ref[s], 1, 1)
            row = lax.broadcasted_iota(jnp.int32, logits.shape, 0)
            routed = jnp.where(row < experts, logits, -1e30)
            raised = jnp.exp(routed - jnp.max(routed, axis=0, keepdims=True))
            soft = raised / jnp.sum(raised, axis=0, keepdims=True)
            probs_ref[s] = jnp.where(row < experts, soft, jax.nn.sigmoid(logits))
        terms_ref[...] = jnp.zeros_like(terms_ref)

    def parts(data, cot, weight):
        both = dot(data, gateup_ref[0], 1, 1)
        cot_in = dot(cot, down_ref[0], 1, 1)
        gate_in, up_in = both[:, :half], both[:, half:]
        gate_act, gate_slope = silu_parts(gate_in)
        act = gate_act * up_in
        inner = jnp.sum(act.astype(BF).astype(F32) * cot_in, axis=1, keepdims=True)
        cot_in = cot_in * weight
        return (
            (act * weight).astype(BF),
            (cot_in * up_in * gate_slope).astype(BF),
            (cot_in * gate_act).astype(BF),
            inner,
        )

    @pl.when(unit < units - 1)
    def _():
        expert = group_ref[0] * (units - 1) + unit
        masks, weights = [], []
        for s in range(count):
            mask = slot_mask(codes_ref, s, expert, top_count, capacity)
            onehot = mask.astype(F32).astype(BF)
            slotted_ref[0, s] = dot(onehot, rows_ref[s]).astype(BF)
            slotgrad_ref[0, s] = dot(onehot, grads_ref[s]).astype(BF)
            probs = probs_ref[s]
            row = lax.broadcasted_iota(jnp.int32, probs.shape, 0)
            gate = jnp.sum(jnp.where(row == expert, probs, 0.0), axis=0, keepdims=True)
            weights.append(jnp.sum(jnp.where(mask, gate, 0.0), axis=1, keepdims=True))
            masks.append(onehot)
        act, gate_grad, up_grad, inner = parts(
            slotted_ref[0].reshape(count * capacity, width),
            slotgrad_ref[0].reshape(count * capacity, width),
            jnp.concatenate(weights, axis=0),
        )
        lane = lax.broadcasted_iota(jnp.int32, (capacity, terms_ref.shape[2]), 1)
        for s in range(count):
            at = slice(s * capacity, (s + 1) * capacity)
            act_ref[0, s] = act[at]
            pair_ref[0, s, :, :half] = gate_grad[at]
            pair_ref[0, s, :, half:] = up_grad[at]
            placed = jnp.where(lane == expert, inner[at], 0.0)
            high = placed.astype(BF)
            low = (placed - high.astype(F32)).astype(BF)
            terms_ref[s] += dot(masks[s], high, 0, 0) + dot(masks[s], low, 0, 0)

    @pl.when(unit == units - 1)
    def _():
        data = rows_ref[...].reshape(count * seq_len, width)
        logits = dot(data, router_ref[...], 1, 1)
        weight = jax.nn.sigmoid(logits[:, experts : experts + 1])
        act, gate_grad, up_grad, inner = parts(
            data, grads_ref[...].reshape(count * seq_len, width), weight
        )
        lane = lax.broadcasted_iota(jnp.int32, (seq_len, terms_ref.shape[2]), 1)
        for s in range(count):
            at = slice(s * seq_len, (s + 1) * seq_len)
            act_s_ref[s] = act[at]
            pair_s_ref[s, :, :half] = gate_grad[at]
            pair_s_ref[s, :, half:] = up_grad[at]
            terms_ref[s] += jnp.where(lane == experts, inner[at], 0.0)


def slot_mask(codes_ref, s, expert, top_count, capacity):
    codes = codes_ref[s]
    slot = jnp.full((1, codes.shape[1]), -1, jnp.int32)
    for k in range(top_count):
        slot = jnp.where(codes[k : k + 1] == expert, codes[top_count + k : top_count + k + 1], slot)
    return lax.broadcasted_iota(jnp.int32, (capacity, codes.shape[1]), 0) == slot


def act_call(experts, top_count, capacity, chunk, group, codes, rows, grads, router, gateup, down):
    _, seq_len, width = rows.shape
    units, wide, _ = gateup.shape
    half = wide // 2
    routed, count = units - 1, 2

    def unit(u):
        return (u, 0, 0)

    def slot(u):
        return (jnp.minimum(u, routed - 1), 0, 0, 0)

    def whole(*shape):
        return pl.BlockSpec(shape, lambda u: (0,) * len(shape))

    def part(*shape):
        return pl.BlockSpec(
            shape,
            lambda u: (chunk,) + (0,) * (len(shape) - 1),
            pipeline_mode=pl.Buffered(1),
        )

    work = count * (routed * capacity + seq_len) * width
    return call(
        functools.partial(act_body, experts, top_count),
        (units,),
        [
            pl.BlockSpec(memory_space=pltpu.SMEM),
            part(count, codes.shape[1], seq_len),
            part(count, seq_len, width),
            part(count, seq_len, width),
            whole(*router.shape),
            pl.BlockSpec((1, wide, width), unit),
            pl.BlockSpec((1, half, width), unit),
        ],
        [
            pl.BlockSpec((1, count, capacity, width), slot),
            pl.BlockSpec((1, count, capacity, width), slot),
            pl.BlockSpec((1, count, capacity, wide), slot),
            pl.BlockSpec((1, count, capacity, half), slot),
            whole(count, seq_len, wide),
            whole(count, seq_len, half),
            whole(count, seq_len, 128),
            whole(count, router.shape[0], seq_len),
        ],
        [
            jax.ShapeDtypeStruct((routed, count, capacity, width), BF),
            jax.ShapeDtypeStruct((routed, count, capacity, width), BF),
            jax.ShapeDtypeStruct((routed, count, capacity, wide), BF),
            jax.ShapeDtypeStruct((routed, count, capacity, half), BF),
            jax.ShapeDtypeStruct((count, seq_len, wide), BF),
            jax.ShapeDtypeStruct((count, seq_len, half), BF),
            jax.ShapeDtypeStruct((count, seq_len, 128), F32),
            jax.ShapeDtypeStruct((count, router.shape[0], seq_len), F32),
        ],
        2 * work * 3 * half + 4 * count * routed * capacity * seq_len * width,
        8 * count * seq_len * width * 2,
    )(group, codes, rows, grads, router, gateup, down)


def back_body(top_count, group_ref, codes_ref, routed_ref, shared_ref, weight_ref, *refs):
    out_refs, onehot_ref = refs[:-1], refs[-1]
    routed, count, capacity, wide = routed_ref.shape
    seq_len = shared_ref.shape[1]
    cols = weight_ref.shape[2]

    @pl.when(pl.program_id(0) == 0)
    def _():
        for s in range(count):
            for e in range(routed):
                mask = slot_mask(codes_ref, s, group_ref[0] * routed + e, top_count, capacity)
                onehot_ref[s, e * capacity : (e + 1) * capacity] = mask.astype(F32).astype(BF)

    shared = dot(shared_ref[...].reshape(count * seq_len, wide), weight_ref[routed])
    slots = [
        dot(routed_ref[e].reshape(count * capacity, wide), weight_ref[e])
        .astype(BF)
        .reshape(count, capacity, cols)
        for e in range(routed)
    ]
    for s in range(count):
        total = dot(onehot_ref[s], jnp.concatenate([rows[s] for rows in slots], axis=0), 0, 0)
        out_refs[s][...] = (total + shared[s * seq_len : (s + 1) * seq_len]).astype(BF)


def back_call(top_count, chunk, group, codes, routed, shared, weight):
    units, wide, width = weight.shape
    count, seq_len, _ = shared.shape
    capacity = routed.shape[2]
    block = min(width, 512)
    work = count * ((units - 1) * capacity + seq_len) * width

    def whole(*shape):
        return pl.BlockSpec(
            shape, lambda j: (0,) * len(shape), pipeline_mode=pl.Buffered(1)
        )

    return call(
        functools.partial(back_body, top_count),
        (width // block,),
        [
            pl.BlockSpec(memory_space=pltpu.SMEM),
            pl.BlockSpec((count, codes.shape[1], seq_len), lambda j: (chunk, 0, 0)),
            whole(*routed.shape),
            whole(*shared.shape),
            pl.BlockSpec((units, wide, block), lambda j: (0, 0, j)),
        ],
        [pl.BlockSpec((seq_len, block), lambda j: (0, j))] * count,
        [jax.ShapeDtypeStruct((seq_len, width), BF)] * count,
        2 * work * wide + 2 * count * (units - 1) * capacity * seq_len * width,
        units * wide * width * 2 + count * seq_len * width * 2,
        [pltpu.VMEM((count, (units - 1) * capacity, seq_len), BF)],
    )(group, codes, routed, shared, weight)


def units_body(keep, pad, *refs):
    lefts, rights, outs = refs[:4], refs[4:8], refs[8:]
    unit, units = pl.program_id(0), pl.num_programs(0)

    def store(first, second):
        total = dot(lefts[first][0], rights[first][0], 0, 0)
        total = (total + dot(lefts[second][0], rights[second][0], 0, 0)).astype(BF)
        for part, out_ref in enumerate(outs):
            blocks, _, _, slice_width = out_ref.shape
            for k in range(blocks):
                out_ref[k, 0] = total[
                    part * pad : part * pad + keep, k * slice_width : (k + 1) * slice_width
                ]

    @pl.when(unit < units - 1)
    def _():
        store(0, 1)

    @pl.when(unit == units - 1)
    def _():
        store(2, 3)


def units_call(keep, pad, dp, routed, shared):
    lefts = [pair[0] for pair in routed] + [entry[0] for entry in shared]
    rights = [pair[1] for pair in routed] + [entry[1] for entry in shared]
    chunks = [0, 0] + [entry[2] for entry in shared]
    many, _, wide = lefts[0].shape
    width = rights[0].shape[2]
    slice_width = width // dp
    blocks = max(1, 1024 // slice_width)
    parts = wide // pad
    last = dp // blocks - 1

    def spec(n, array, cols):
        def where(u, j):
            of_shared = n > 1
            mine = (u == many) if of_shared else (u < many)
            unit = chunks[n] if of_shared else jnp.minimum(u, many - 1)
            if cols:
                return (unit, 0, jnp.where(mine, j, 0 if of_shared else last))
            return (0 if of_shared else unit, 0, 0)

        return pl.BlockSpec((1, array.shape[1], cols or wide), where)

    cols = blocks * slice_width
    rows = many * lefts[0].shape[1] + lefts[2].shape[1]
    return call(
        functools.partial(units_body, keep, pad),
        (many + 1, dp // blocks),
        [spec(n, a, 0) for n, a in enumerate(lefts)]
        + [spec(n, a, cols) for n, a in enumerate(rights)],
        [pl.BlockSpec((blocks, 1, keep, slice_width), lambda u, j: (j, u, 0, 0))] * parts,
        [jax.ShapeDtypeStruct((dp, many + 1, keep, slice_width), BF)] * parts,
        4 * rows * wide * width,
        rows * (wide + width) * 4,
    )(*lefts, *rights)


MESH = pl.DeviceIdType.MESH


class Copies:
    def __init__(self, send, recv, here):
        self.send, self.recv, self.here = send, recv, here
        self.remote_count = self.local_count = 0

    def remote(self, src, dst, **device):
        k = self.remote_count
        self.remote_count += 1
        return pltpu.make_async_remote_copy(
            src_ref=src,
            dst_ref=dst,
            send_sem=self.send.at[k],
            recv_sem=self.recv.at[k],
            device_id=device,
            device_id_type=MESH,
        )

    def local(self, src, dst):
        k = self.local_count
        self.local_count += 1
        return pltpu.make_async_copy(src, dst, self.here.at[k])


class Line:
    def __init__(self, copies, buffer, z, depth, rows):
        self.z, self.depth = z, depth

        def piece(p):
            return buffer.at[pl.ds(pl.multiple_of(p * rows, rows), rows)]

        def make(k, sign):
            p = z - sign * k
            return copies.remote(piece(p), piece(p), tensor=z + sign)

        self.ups = [make(k, 1) for k in range(depth - 1)]
        self.downs = [make(k, -1) for k in range(depth - 1)]

    def sends(self, k):
        z, top = self.z, self.depth - 1
        return (
            (self.ups[k], jnp.logical_and(z < top, z >= k)),
            (self.downs[k], jnp.logical_and(z > 0, z + k <= top)),
        )

    def begin(self):
        for copy, there in self.sends(0):
            pl.when(there)(copy.start)

    def finish(self):
        for k in range(self.depth - 1):
            for copy, there in self.sends(k):
                pl.when(there)(copy.wait_send)


def peer_of(me, r):
    out, bit = me, 1
    while bit <= r:
        if r & bit:
            out = out + bit - 2 * bit * (me // bit % 2)
        bit *= 2
    return out


def greet(me, z, dp, depth):
    barrier = pltpu.get_barrier_semaphore()
    for r in range(1, dp):
        pl.semaphore_signal(barrier, inc=1, device_id={"dp": peer_of(me, r)}, device_id_type=MESH)
    for r in range(1, depth):
        pl.semaphore_signal(
            barrier, inc=1, device_id={"tensor": (z + r) % depth}, device_id_type=MESH
        )
    pl.semaphore_wait(barrier, dp - 1 + depth - 1)


def spin(field, cos_rows, sin_rows):
    return field * cos_rows + pltpu.roll(field, field.shape[-1] // 2, 1) * sin_rows


def piece_of(buffer, p, rows):
    return buffer.at[pl.ds(pl.multiple_of(p * rows, rows), rows)]


def pass_on(c, source, target, z, depth, rows, sibling, passed):
    def make(p):
        return c.remote(piece_of(source, p, rows), piece_of(target, p, rows), dp=sibling)

    ups = [make(z - k) for k in range(1, depth)]
    downs = [make(z + k) for k in range(1, depth)]
    for k in range(1, depth):
        passed.append((ups[k - 1], z >= k))
        passed.append((downs[k - 1], z + k <= depth - 1))

    def each(k, up):
        (ups if up else downs)[k - 1].start()

    return each


def line_step(line, k, each=None):
    z, top = line.z, line.depth - 1
    onward = line.sends(k) if k < top else (None, None)
    for up, copy, there, further in (
        (True, line.ups[k - 1], z >= k, onward[0]),
        (False, line.downs[k - 1], z + k <= top, onward[1]),
    ):
        pl.when(there)(copy.wait_recv)
        if further is not None:
            pl.when(further[1])(further[0].start)
        if each is not None:
            pl.when(there)(functools.partial(each, k, up))


def forward_body(
    sizes,
    codes_ref,
    misc_ref,
    gains_ref,
    cos_ref,
    sin_ref,
    tokens_ref,
    outgrad_ref,
    wq_ref,
    wk_ref,
    wv_ref,
    wo_ref,
    eg_ref,
    eu_ref,
    ed_ref,
    sg_ref,
    su_ref,
    sd_ref,
    hidden_ref,
    norm_ref,
    grads_ref,
    gateup_ref,
    down_ref,
    codes_all,
    misc_all,
    gain_rows,
    tok,
    weights,
    qkv_ref,
    probs_ref,
    mix_ref,
    fnorm,
    part,
    part_in,
    scatter_in,
    gains_all,
    zeros,
    send,
    recv,
    here,
):
    dp, depth, experts, hidden_units, head = sizes
    me, z = lax.axis_index("dp"), lax.axis_index("tensor")
    core, x = me % 2, (me // 2) % 2
    bits = [2**k for k in range(dp.bit_length() - 1)]
    upper = bits[2:]
    rows, width = tokens_ref.shape
    seq_len = rows * depth
    slice_width = width // dp
    routed = experts // 4
    c = Copies(send, recv, here)

    def bit_of(bit):
        return (me // bit) % 2

    greet(me, z, dp, depth)

    first = []
    own_codes = c.local(codes_ref, codes_all.at[0])
    own_misc = c.local(misc_ref, misc_all.at[me])
    own_gains = c.local(gains_ref, gains_all.at[z, me])
    for copy in (own_codes, own_misc, own_gains):
        copy.start()
    for r in range(1, 4):
        first.append(c.remote(codes_ref, codes_all.at[r], dp=peer_of(me, r)))
    gain_copies = [c.remote(gains_ref, gains_all.at[z, me], dp=peer_of(me, r)) for r in range(1, dp)]
    misc_copies = [c.remote(misc_ref, misc_all.at[me], dp=peer_of(me, r)) for r in range(1, dp)]
    for copy in gain_copies + misc_copies + first:
        copy.start()

    def piece(buffer, p):
        return buffer.at[pl.ds(pl.multiple_of(p * rows, rows), rows)]

    own_tok = c.local(tokens_ref, piece(tok.at[0], z))
    own_tok.start()
    own_grad = c.local(outgrad_ref, piece(grads_ref.at[0], z))
    own_grad.start()

    def columns(k, n):
        return pl.ds(pl.multiple_of(k * n, n), n)

    pair = wq_ref.shape[1] // 2
    own_at = tuple(bit_of(bit) for bit in reversed(bits))
    core_copies = []
    for k, w in enumerate((wq_ref, wk_ref, wv_ref, wo_ref)):
        place = weights.at[own_at + (slice(None), pl.ds(k * pair, pair))]
        core_copies.append(c.remote(w.at[:, columns(1 - core, pair)], place, dp=peer_of(me, 1)))
        core_copies.append(c.local(w.at[:, columns(core, pair)], place))
    for copy in core_copies:
        copy.start()

    own_tok.wait()
    tok_line = Line(c, tok.at[0], z, depth, rows)
    tok_line.begin()
    tok_pass = [c.remote(tokens_ref, piece(tok.at[1], z), dp=peer_of(me, 1))]
    tok_pass[0].start()

    zeros[...] = jnp.zeros_like(zeros)
    pad = zeros.shape[1]
    pads = [c.local(zeros, down_ref.at[:, 0, pl.ds(hidden_units, pad)])]
    pads += [c.local(zeros, gateup_ref.at[:, k, pl.ds(hidden_units, pad)]) for k in range(2)]
    matrices = ((ed_ref, sd_ref, down_ref, 0), (eg_ref, sg_ref, gateup_ref, 0), (eu_ref, su_ref, gateup_ref, 1))
    slab = columns(me, slice_width)

    def group_copies(routed_src, shared_src, dst, k, r):
        group = (peer_of(me, r)) % 4
        many = (
            routed_src.at[pl.ds(group * routed, routed)],
            dst.at[pl.ds(0, routed), k, pl.ds(0, hidden_units), slab],
        )
        one = (shared_src.at[group], dst.at[routed, k, pl.ds(0, hidden_units), slab])
        if r == 0:
            return [c.local(*many), c.local(*one)]
        return [c.remote(*many, dp=peer_of(me, r)), c.remote(*one, dp=peer_of(me, r))]

    near = [[copy for r in (0, 1) for copy in group_copies(*m, r)] for m in matrices]
    far = [[copy for r in (2, 3) for copy in group_copies(*m, r)] for m in matrices]

    def upper_copies(dst, k):
        copies = []
        for bit in upper:
            n = bit * slice_width
            cols = pl.ds(pl.multiple_of(me // bit * n, n), n)
            place = dst.at[:, k, pl.ds(0, hidden_units), cols]
            copies.append(c.remote(place, place, dp=peer_of(me, bit)))
        return copies

    over = [upper_copies(m[2], m[3]) for m in matrices]

    for copy in core_copies:
        copy.wait()

    def weight_copies(order, half):
        have, copies = [1], []
        for bit in order:
            index = tuple(
                pl.ds(0, 2) if b in have else pl.ds(bit_of(b), 1) for b in reversed(bits)
            )
            place = weights.at[index + (slice(None), pl.ds(half * 2 * pair, 2 * pair))]
            copies.append(c.remote(place, place, dp=peer_of(me, bit)))
            have.append(bit)
        return copies

    qk_copies = weight_copies(bits[1:], 0)
    vo_copies = weight_copies(bits[:0:-1], 1)
    qk_copies[0].start()
    vo_copies[0].start()
    for copy in pads + [copy for m in near for copy in m]:
        copy.start()

    own_gains.wait()
    for copy in gain_copies:
        copy.wait_recv()
    gain_spread = [
        c.remote(gains_all.at[z], gains_all.at[z], tensor=(z + r) % depth) for r in range(1, depth)
    ]
    for copy in gain_spread:
        copy.start()

    tok_passed = []
    sibling = peer_of(me, 1)
    pass_tok = pass_on(c, tok.at[0], tok.at[1], z, depth, rows, sibling, tok_passed)

    line_step(tok_line, 1, pass_tok)
    for k in range(1, len(bits) - 1):
        qk_copies[k - 1].wait_recv()
        qk_copies[k].start()
        vo_copies[k - 1].wait_recv()
        vo_copies[k].start()
    for m in far:
        for copy in m:
            copy.start()
    own_grad.wait()
    grad_line = Line(c, grads_ref.at[0], z, depth, rows)
    for k in range(2, depth):
        line_step(tok_line, k, pass_tok)
    grad_line.begin()

    for copy in gain_spread:
        copy.wait_recv()
    for d in range(dp):
        total = gains_all[0, d]
        for t in range(1, depth):
            total = total + gains_all[t, d]
        gain_rows[:, d * slice_width : (d + 1) * slice_width] = total

    def norm_rows(s):
        def block(i, carry):
            at = pl.ds(pl.multiple_of(i * rows, rows), rows)
            data = tok[s, at, :].astype(F32)
            scale = lax.rsqrt(jnp.mean(data * data, axis=-1, keepdims=True) + EPS)
            fnorm[at, :] = (data * scale * gain_rows[0:1, :]).astype(BF)
            return carry

        lax.fori_loop(0, depth, block, 0)

    own_misc.wait()
    for copy in misc_copies:
        copy.wait_recv()
    bias_in = jnp.zeros(misc_ref.shape, F32)
    sub = lax.broadcasted_iota(jnp.int32, misc_ref.shape, 0)
    for d in range(dp):
        bias_in = jnp.where(sub == d, misc_all[d, pl.ds(experts + 1 + core, 1), :], bias_in)
    bias_in = bias_in.astype(BF)
    heads3 = 3 * pair
    head_slice = head // dp
    lane = lax.broadcasted_iota(jnp.int32, (bias_in.shape[1], heads3), 1)
    sub = lax.broadcasted_iota(jnp.int32, (bias_in.shape[1], heads3), 0)
    place = (lane // head * head_slice + lane % head_slice == sub).astype(F32).astype(BF)
    spread = dot(bias_in, place)
    lane = lax.broadcasted_iota(jnp.int32, spread.shape, 1)
    sub = lax.broadcasted_iota(jnp.int32, spread.shape, 0)
    bias = jnp.sum(jnp.where(lane % head // head_slice == sub, spread, 0.0), axis=0, keepdims=True)

    qk_copies[-1].wait_recv()
    vo_copies[-1].wait_recv()
    pairs = pair // head

    def project(s):
        def block(i, carry):
            at = pl.ds(pl.multiple_of(i * 2 * rows, 2 * rows), 2 * rows)
            full = weights[...].reshape(width, 4 * pair)
            pre = dot(fnorm[at, :], full[:, : 3 * pair]) + bias
            cos_rows, sin_rows = cos_ref[at, :], sin_ref[at, :]
            for kind in range(3):
                for h in range(pairs):
                    a = (kind * pairs + h) * head
                    field = pre[:, a : a + head]
                    if kind < 2:
                        field = spin(field, cos_rows, sin_rows)
                    qkv_ref[kind, s * pairs + h, at, :] = field.astype(BF)
            return carry

        lax.fori_loop(0, depth // 2, block, 0)

    norm_rows(0)
    project(0)
    line_step(grad_line, 1)
    for copy in near[0]:
        copy.wait()
    for copy in far[0]:
        copy.wait_recv()
    over[0][0].start()
    tok_pass[0].wait()
    for copy, there in tok_passed:
        pl.when(there)(copy.wait)
    norm_rows(1)
    project(1)

    own_codes.wait()
    for copy in first:
        copy.wait()
    causal_block = seq_len // 2

    def attend(s):
        flags = codes_all[s]
        sub = lax.broadcasted_iota(jnp.int32, flags.shape, 0)
        flags = jnp.where(sub == 8, flags, 0).astype(F32).astype(BF)
        for h in range(pairs):
            for b in range(2):
                at = slice(b * causal_block, (b + 1) * causal_block)
                seen = dot(flags[:, at], flags, 0, 0)
                row = lax.broadcasted_iota(jnp.int32, seen.shape, 0) + b * causal_block
                col = lax.broadcasted_iota(jnp.int32, seen.shape, 1)
                scores = dot(qkv_ref[0, s * pairs + h, at, :], qkv_ref[1, s * pairs + h], 1, 1)
                scores = scores * head ** (-0.5)
                scores = jnp.where(jnp.logical_or(col <= row, seen > 0.5), scores, -1e30)
                raised = jnp.exp(scores - jnp.max(scores, axis=1, keepdims=True))
                probs = raised / jnp.sum(raised, axis=1, keepdims=True)
                probs = probs.astype(BF)
                probs_ref[s * pairs + h, at, :] = probs
                mixed = dot(probs, qkv_ref[2, s * pairs + h])
                mix_ref[s, at, h * head : (h + 1) * head] = mixed.astype(BF)

    def project_out(s):
        for d in range(dp):
            index = tuple(d // bit % 2 for bit in reversed(bits))
            block = weights[index + (slice(None), slice(3 * pair, 4 * pair))]
            at = slice(d * slice_width, (d + 1) * slice_width)
            part[s, :, at] = dot(mix_ref[s], block, 1, 1).astype(BF)

    attend(1)
    if depth > 2:
        line_step(grad_line, 2)
    project_out(1)
    part_pass = c.remote(part.at[1], part_in, dp=peer_of(me, 1))
    part_pass.start()
    attend(0)
    project_out(0)
    for copy in near[1]:
        copy.wait()
    for copy in far[1]:
        copy.wait_recv()
    over[1][0].start()
    part_pass.wait_recv()

    scatter = []
    for r in list(range(1, depth)) + [0]:
        at = pl.ds(pl.multiple_of((z + r) % depth * rows, rows), rows)
        total = part[0, at, :].astype(F32) + part_in[at, :].astype(F32)
        if r:
            part[0, at, :] = total.astype(BF)
            copy = c.remote(part.at[0, at], scatter_in.at[r - 1], tensor=(z + r) % depth)
            copy.start()
            scatter.append(copy)
        else:
            hidden_ref[...] = total + tok[0, at, :].astype(F32)

    for k in range(3, depth):
        line_step(grad_line, k)
    x_grad = c.remote(grads_ref.at[0], grads_ref.at[2], dp=peer_of(me, 2))
    x_grad.start()
    own_pass = c.remote(grads_ref.at[0], grads_ref.at[1], dp=peer_of(me, 1))
    own_pass.start()
    for copy in near[2]:
        copy.wait()
    for copy in far[2]:
        copy.wait_recv()
    over[2][0].start()

    for copy in scatter:
        copy.wait_recv()
    total = hidden_ref[...]
    for r in range(1, depth):
        total = total + scatter_in[r - 1].astype(F32)
    hidden_ref[...] = total
    scale = lax.rsqrt(jnp.mean(total * total, axis=-1, keepdims=True) + EPS)
    norm_ref[0, pl.ds(pl.multiple_of(z * rows, rows), rows), :] = (
        total * scale * gain_rows[1:2, :]
    ).astype(BF)
    norm_line = Line(c, norm_ref.at[0], z, depth, rows)
    norm_line.begin()
    beside = peer_of(me, 2)
    norm_own = c.remote(piece(norm_ref.at[0], z), piece(norm_ref.at[1], z), dp=sibling)
    norm_far = c.remote(piece(norm_ref.at[0], z), piece(norm_ref.at[2], z), dp=beside)
    norm_far.start()
    norm_own.start()
    norm_passed, far_passed = [], []
    pass_norm = pass_on(
        c, norm_ref.at[0], norm_ref.at[1], z, depth, rows, sibling, norm_passed
    )
    pass_far = pass_on(c, norm_ref.at[0], norm_ref.at[2], z, depth, rows, beside, far_passed)

    def pass_both(k, up):
        pass_far(k, up)
        pass_norm(k, up)

    for k in range(1, depth):
        line_step(norm_line, k, pass_both)

    x_grad.wait_recv()
    grad_pass = c.remote(grads_ref.at[2], grads_ref.at[3], dp=peer_of(me, 1))
    grad_pass.start()
    for k in range(1, len(upper)):
        for chain in over:
            chain[k - 1].wait_recv()
            chain[k].start()
    for chain in over:
        chain[-1].wait_recv()
    norm_far.wait()
    for copy, there in far_passed:
        pl.when(there)(copy.wait)
    norm_pass = c.remote(norm_ref.at[2], norm_ref.at[3], dp=sibling)
    norm_pass.start()
    norm_own.wait()
    for copy, there in norm_passed:
        pl.when(there)(copy.wait)
    norm_pass.wait()
    own_pass.wait()
    grad_pass.wait()
    for line in (tok_line, grad_line, norm_line):
        line.finish()
    for copy in pads:
        copy.wait()
    for copy in gain_copies + misc_copies + gain_spread + qk_copies + vo_copies + scatter:
        copy.wait_send()
    for copy in [part_pass, x_grad] + [y for m in far for y in m] + [y for m in over for y in m]:
        copy.wait_send()


def forward_call(dp, depth, experts, head, small, arrays, units):
    codes, misc, gains, cos_rows, sin_rows = small
    tokens, pair = arrays[0], arrays[2].shape[1] // 2
    rows, width = tokens.shape
    seq_len = rows * depth
    hidden_units = units[0].shape[1]
    hidden_pad = -(-hidden_units // 128) * 128
    routed = experts // 4
    bits = dp.bit_length() - 1
    pairs = pair // head
    vmem, hbm = pl.BlockSpec(memory_space=pltpu.VMEM), pl.BlockSpec(memory_space=pl.ANY)
    shape = jax.ShapeDtypeStruct
    return pl.pallas_call(
        functools.partial(forward_body, (dp, depth, experts, hidden_units, head)),
        in_specs=[vmem] * 5 + [hbm] * 12,
        out_specs=[vmem, vmem, hbm, hbm, hbm] + [vmem] * 8,
        out_shape=[
            shape((rows, width), F32),
            shape((4, seq_len, width), BF),
            shape((4, seq_len, width), BF),
            shape((routed + 1, 2, hidden_pad, width), BF),
            shape((routed + 1, 1, hidden_pad, width), BF),
            shape((4,) + codes.shape, codes.dtype),
            shape((dp,) + misc.shape, F32),
            shape((8, width), F32),
            shape((2, seq_len, width), BF),
            shape((2,) * bits + (width // dp, 4 * pair), BF),
            shape((3, 2 * pairs, seq_len, head), BF),
            shape((2 * pairs, seq_len, seq_len), BF),
            shape((2, seq_len, pair), BF),
        ],
        scratch_shapes=[
            pltpu.VMEM((seq_len, width), BF),
            pltpu.VMEM((2, seq_len, width), BF),
            pltpu.VMEM((seq_len, width), BF),
            pltpu.VMEM((depth - 1, rows, width), BF),
            pltpu.VMEM((depth, dp) + gains.shape, F32),
            pltpu.VMEM((routed + 1, hidden_pad - hidden_units, width), BF),
            pltpu.SemaphoreType.DMA((160,)),
            pltpu.SemaphoreType.DMA((160,)),
            pltpu.SemaphoreType.DMA((32,)),
        ],
        compiler_params=pltpu.CompilerParams(
            collective_id=0, has_side_effects=True, vmem_limit_bytes=VMEM_LIMIT
        ),
    )(codes, misc, gains, cos_rows, sin_rows, *arrays, *units)


def backward_body(
    sizes,
    terms_ref,
    probs_mine_ref,
    router_ref,
    gain_rows,
    cos_ref,
    sin_ref,
    hidden_ref,
    outgrad_ref,
    grad_a_ref,
    grad_b_ref,
    grad_c_ref,
    out_a_ref,
    out_b_ref,
    out_far_ref,
    gate_in_ref,
    gate_ref,
    up_ref,
    down_ref,
    tok_hbm,
    weights_hbm,
    qkv_hbm,
    probs_hbm,
    mix_hbm,
    norm_hbm,
    output_ref,
    input_ref,
    gate_out,
    up_out,
    down_out,
    out_c_ref,
    attn_out,
    misc_out,
    gains_out,
    own_sum,
    arrived,
    three,
    scatter_in,
    terms_sum,
    terms_in,
    back,
    tok,
    weights,
    qkv,
    probs_ref,
    mix_ref,
    scales,
    qkv_grad,
    part_in,
    keep,
    total_a,
    first_qk,
    first_vo,
    second_in,
    misc_part,
    misc_in,
    gains_in,
    vectors,
    send,
    recv,
    here,
):
    dp, depth, experts, head = sizes
    me, z = lax.axis_index("dp"), lax.axis_index("tensor")
    core, x, y = me % 2, (me // 2) % 2, me // 4
    rows, width = output_ref.shape
    seq_len = rows * depth
    slice_width = width // dp
    pair = mix_ref.shape[2]
    pairs = pair // head
    bits = [1, 2, 4]
    c = Copies(send, recv, here)

    greet(me, z, dp, depth)

    matrices = ((gate_ref, gate_out), (up_ref, up_out), (down_ref, down_out))
    over = [None]
    for m in (1, 2):
        other = matrices[m][0].at[pl.ds((1 - y) * 4, 4)]
        over.append(c.remote(other, arrived.at[m], dp=peer_of(me, 4)))
        over[m].start()
    out_far = c.remote(out_far_ref, out_c_ref, dp=peer_of(me, 2))
    out_far.start()
    gate_in = c.local(gate_in_ref, arrived.at[0])
    grads = (grad_a_ref, grad_b_ref, grad_c_ref)
    loads = [c.local(grads[k], three.at[k]) for k in range(3)]
    for copy in loads:
        copy.start()
    own_loads = [
        c.local(source.at[pl.ds(y * 4, 4)], own_sum) for source, _ in matrices
    ]
    inputs = [
        c.local(a, b)
        for a, b in (
            (weights_hbm, weights),
            (mix_hbm, mix_ref),
            (qkv_hbm, qkv),
            (probs_hbm, probs_ref),
            (tok_hbm, tok),
        )
    ]
    own_loads[0].start()
    gate_in.start()
    for copy in inputs:
        copy.start()

    def at_of(p):
        return pl.ds(pl.multiple_of(p * rows, rows), rows)

    for copy in loads:
        copy.wait()
    scatter, small = [], []
    for r in list(range(1, depth)) + [0]:
        at = at_of((z + r) % depth)
        total = three[0, at, :].astype(F32) + three[1, at, :].astype(F32)
        total = total + three[2, at, :].astype(F32)
        extra = terms_ref[0, at, :] + terms_ref[1, at, :] + terms_ref[2, at, :]
        if r:
            three[0, at, :] = total.astype(BF)
            terms_sum[at, :] = extra
            peer = (z + r) % depth
            scatter.append(c.remote(three.at[0, at], scatter_in.at[0, r - 1], tensor=peer))
            small.append(c.remote(terms_sum.at[at], terms_in.at[r - 1], tensor=peer))
            scatter[-1].start()
            small[-1].start()
        else:
            keep[0] = total
            terms_sum[at, :] = extra

    def add_over(m):
        own_loads[m].wait()
        if m:
            over[m].wait_recv()
        else:
            gate_in.wait()
        copies = []
        for r in (2, 3, 1, 0):
            k = peer_of(me, r) % 4
            for unit in range(own_sum.shape[1]):
                arrived[m, k, unit] = (
                    own_sum[k, unit].astype(F32) + arrived[m, k, unit].astype(F32)
                ).astype(BF)
            place = matrices[m][1].at[me % 4]
            if r:
                copies.append(c.remote(arrived.at[m, k], place, dp=peer_of(me, r)))
            else:
                copies.append(c.local(arrived.at[m, k], place))
            copies[-1].start()
        if m + 1 < len(own_loads):
            own_loads[m + 1].start()
        return copies

    units = add_over(0)
    for copy in scatter:
        copy.wait_recv()
    for copy in small:
        copy.wait_recv()
    route = terms_sum[at_of(z), :]
    grad = keep[0]
    for r in range(1, depth):
        grad = grad + scatter_in[0, r - 1].astype(F32)
        route = route + terms_in[r - 1]
    probs_mine = probs_mine_ref[...]
    lane = lax.broadcasted_iota(jnp.int32, route.shape, 1)
    inner = jnp.sum(jnp.where(lane < experts, probs_mine * route, 0.0), axis=1, keepdims=True)
    logits = jnp.where(
        lane < experts,
        probs_mine * (route - inner),
        jnp.where(lane == experts, route * probs_mine * (1.0 - probs_mine), 0.0),
    ).astype(BF)
    grad = grad + dot(logits, router_ref[...])
    hidden = hidden_ref[...]
    scale = lax.rsqrt(jnp.mean(hidden * hidden, axis=-1, keepdims=True) + EPS)
    unit = hidden * scale
    vectors[1:2, :] = jnp.sum(grad * unit, axis=0, keepdims=True)
    grad = grad * gain_rows[1:2, :]
    grad = outgrad_ref[...].astype(F32) + scale * (
        grad - unit * jnp.mean(grad * unit, axis=-1, keepdims=True)
    )
    keep[0] = grad
    back[0, at_of(z), :width] = grad.astype(BF)
    back[0, at_of(z), width:] = logits

    line = Line(c, back.at[0], z, depth, rows)
    line.begin()
    sibling = peer_of(me, 1)
    back_own = c.remote(piece_of(back.at[0], z, rows), piece_of(back.at[1], z, rows), dp=sibling)
    back_own.start()
    passed = []
    pass_back = pass_on(c, back.at[0], back.at[1], z, depth, rows, sibling, passed)
    for copy in scatter:
        copy.wait_send()
    outs = (out_a_ref, out_b_ref, out_c_ref)
    out_loads = [c.local(outs[k], three.at[k]) for k in range(3)]
    for copy in out_loads[:2]:
        copy.start()
    line_step(line, 1, pass_back)
    out_far.wait_recv()
    out_loads[2].start()

    for copy in inputs:
        copy.wait()

    def scale_rows(i, carry):
        at = at_of(i)
        for s in range(2):
            data = tok[s, at, :].astype(F32)
            scales[s, at, :] = lax.rsqrt(jnp.mean(data * data, axis=-1, keepdims=True) + EPS)
        return carry

    lax.fori_loop(0, depth, scale_rows, 0)
    line_step(line, 2, pass_back)
    units += add_over(1)
    for copy in out_loads:
        copy.wait()
    out_scatter = []
    for r in list(range(1, depth)) + [0]:
        at = at_of((z + r) % depth)
        total = three[0, at, :].astype(F32) + three[1, at, :].astype(F32)
        total = total + three[2, at, :].astype(F32)
        if r:
            three[0, at, :] = total.astype(BF)
            peer = (z + r) % depth
            out_scatter.append(c.remote(three.at[0, at], scatter_in.at[1, r - 1], tensor=peer))
        else:
            keep[1] = total + hidden_ref[...]
    line_step(line, 3, pass_back)
    back_own.wait()
    for copy, there in passed:
        pl.when(there)(copy.wait)
    for copy in out_scatter:
        copy.start()

    def block_of(d):
        return tuple(d // bit % 2 for bit in reversed(bits))

    def slab(d):
        return slice(d * slice_width, (d + 1) * slice_width)

    def attention(s):
        mixed = jnp.zeros((seq_len, pair), F32)
        for d in range(dp):
            block = weights[block_of(d) + (slice(None), slice(3 * pair, 4 * pair))]
            mixed = mixed + dot(back[s, :, slab(d)], block)
        mixed = mixed.astype(BF)
        for h in range(pairs):
            n = s * pairs + h
            cot = mixed[:, h * head : (h + 1) * head]
            key_total = jnp.zeros((seq_len, head), F32)
            value_total = jnp.zeros((seq_len, head), F32)
            for b in range(2):
                at = slice(b * seq_len // 2, (b + 1) * seq_len // 2)
                p_low = probs_ref[n, at, :]
                p = p_low.astype(F32)
                p_grad = dot(cot[at], qkv[2, n], 1, 1)
                s_grad = p * (p_grad - jnp.sum(p * p_grad, axis=1, keepdims=True))
                s_grad = s_grad.astype(BF)
                q_grad = dot(s_grad, qkv[1, n]) * head ** (-0.5)
                q_grad = spin(q_grad, cos_ref[at, :], -sin_ref[at, :])
                qkv_grad[s, at, h * head : (h + 1) * head] = q_grad.astype(BF)
                key_total = key_total + dot(s_grad, qkv[0, n, at, :], 0, 0)
                value_total = value_total + dot(p_low, cot[at], 0, 0)
            k_grad = spin(key_total * head ** (-0.5), cos_ref[...], -sin_ref[...])
            a = pair + h * head
            qkv_grad[s, :, a : a + head] = k_grad.astype(BF)
            qkv_grad[s, :, a + pair : a + pair + head] = value_total.astype(BF)

    def first_grad(s):
        for d in range(dp):
            block = weights[block_of(d) + (slice(None), slice(0, 3 * pair))]
            total = dot(qkv_grad[s], block, 1, 1)
            three[1 + s, :, slab(d)] = total.astype(BF)
            unit_block = tok[s, :, slab(d)].astype(F32) * scales[s]
            row = jnp.sum(total * unit_block, axis=0, keepdims=True)
            vectors[2 + s : 3 + s, slab(d)] = row

    attention(1)
    first_grad(1)
    part_pass = c.remote(three.at[2], part_in, dp=sibling)
    part_pass.start()
    units += add_over(2)
    attention(0)
    first_grad(0)
    part_pass.wait_recv()
    first_scatter = []
    for r in list(range(1, depth)) + [0]:
        at = at_of((z + r) % depth)
        total = three[1, at, :].astype(F32) + part_in[at, :].astype(F32)
        if r:
            three[1, at, :] = total.astype(BF)
            peer = (z + r) % depth
            copy = c.remote(three.at[1, at], scatter_in.at[2, r - 1], tensor=peer)
            copy.start()
            first_scatter.append(copy)
        else:
            keep[2] = total

    for d in range(dp):
        total = jnp.zeros((slice_width, 3 * pair), F32)
        out_total = jnp.zeros((slice_width, pair), F32)
        for s in range(2):
            data = tok[s, :, slab(d)].astype(F32) * scales[s] * gain_rows[0:1, slab(d)]
            total = total + dot(data.astype(BF), qkv_grad[s], 0, 0)
            out_total = out_total + dot(back[s, :, slab(d)], mix_ref[s], 0, 0)
        total_a[block_of(d) + (slice(None), slice(0, 3 * pair))] = total.astype(BF)
        total_a[block_of(d) + (slice(None), slice(3 * pair, 4 * pair))] = out_total.astype(BF)

    half = 2 * pair

    def index(y_at, x_at, k):
        return (y_at, x_at, slice(None), slice(None), pl.ds(k * half, half))

    every = pl.ds(0, 2)
    qk_first = c.remote(
        total_a.at[index(pl.ds(1 - y, 1), every, 0)], first_qk, dp=peer_of(me, 4)
    )
    vo_first = c.remote(
        total_a.at[index(every, pl.ds(1 - x, 1), 1)], first_vo, dp=peer_of(me, 2)
    )
    qk_first.start()
    vo_first.start()

    for copy in out_scatter:
        copy.wait_send()
    norm_load = c.local(norm_hbm.at[0], three.at[0])
    norm_load.start()
    norm_load.wait()
    router_part = dot(back[0, :, width:], three[0], 0, 0)
    ones = jnp.ones((16, seq_len), BF)
    bias_row = dot(ones, qkv_grad[0]) + dot(ones, qkv_grad[1])
    lane = lax.broadcasted_iota(jnp.int32, bias_row.shape, 1)
    sub = lax.broadcasted_iota(jnp.int32, bias_row.shape, 0)
    head_slice = head // dp
    bias_rows = jnp.where(lane % head // head_slice == sub, bias_row, 0.0)
    high = bias_rows.astype(BF)
    low = (bias_rows - high.astype(F32)).astype(BF)
    lane = lax.broadcasted_iota(jnp.int32, (3 * pair, slice_width), 1)
    sub = lax.broadcasted_iota(jnp.int32, (3 * pair, slice_width), 0)
    place = (sub // head * head_slice + sub % head_slice == lane).astype(F32).astype(BF)
    bias_rows = dot(high, place) + dot(low, place)
    sub = lax.broadcasted_iota(jnp.int32, (16, slice_width), 0)
    misc_copies = []
    for d in range(dp):
        tile = jnp.where(sub <= experts, router_part[:16, slab(d)], 0.0)
        tile = jnp.where(sub == experts + 1 + core, bias_rows[d : d + 1], tile)
        gain_one = vectors[2:3, slab(d)] + vectors[3:4, slab(d)]
        tile = jnp.where(sub == experts + 3, gain_one, tile)
        tile = jnp.where(sub == experts + 4, vectors[1:2, slab(d)], tile)
        misc_part[d] = tile
    for r in range(1, dp):
        to = peer_of(me, r)
        misc_copies.append(c.remote(misc_part.at[to], misc_in.at[r - 1], dp=to))
        misc_copies[-1].start()

    qk_first.wait()
    mine = index(pl.ds(y, 1), every, 0)
    total_a[mine] = (total_a[mine].astype(F32) + first_qk[...].astype(F32)).astype(BF)
    qk_second = c.remote(
        total_a.at[index(pl.ds(y, 1), pl.ds(1 - x, 1), 0)], second_in.at[0], dp=peer_of(me, 2)
    )
    qk_second.start()
    vo_first.wait()
    mine = index(every, pl.ds(x, 1), 1)
    total_a[mine] = (total_a[mine].astype(F32) + first_vo[...].astype(F32)).astype(BF)
    vo_second = c.remote(
        total_a.at[index(pl.ds(1 - y, 1), pl.ds(x, 1), 1)], second_in.at[1], dp=peer_of(me, 4)
    )
    vo_second.start()

    total = misc_part[me]
    for r, copy in enumerate(misc_copies):
        copy.wait_recv()
        total = total + misc_in[r]
    misc_out[...] = total
    gain_copies = []
    for r in range(1, depth):
        peer = (z + r) % depth
        gain_copies.append(c.remote(misc_out.at[8:16], gains_in.at[r - 1], tensor=peer))
        gain_copies[-1].start()

    finals = []
    for k, copy in enumerate((qk_second, vo_second)):
        copy.wait()
        mine = (y, x, slice(None), slice(None), pl.ds(k * half, half))
        total_a[mine] = (
            total_a[mine].astype(F32) + second_in[k, 0, 0].astype(F32)
        ).astype(BF)
        for other in (True, False):
            to = 1 - core if other else core
            source = total_a.at[y, x, to, :, pl.ds(k * half, half)]
            place = attn_out.at[core, :, pl.ds(k * half, half)]
            finals.append(c.remote(source, place, dp=sibling) if other else c.local(source, place))
            finals[-1].start()

    for copy in out_scatter:
        copy.wait_recv()
    total = keep[1]
    for r in range(1, depth):
        total = total + scatter_in[1, r - 1].astype(F32)
    output_ref[...] = total.astype(BF)
    for copy in first_scatter:
        copy.wait_recv()
    total = keep[2]
    for r in range(1, depth):
        total = total + scatter_in[2, r - 1].astype(F32)
    total = total * gain_rows[0:1, :]
    scale = scales[0, at_of(z), :]
    unit = tok[0, at_of(z), :].astype(F32) * scale
    total = keep[0] + scale * (total - unit * jnp.mean(total * unit, axis=-1, keepdims=True))
    input_ref[...] = total.astype(BF)

    total = misc_out[8:16, :]
    for r, copy in enumerate(gain_copies):
        copy.wait()
        total = total + gains_in[r]
    gains_out[...] = total
    for copy in finals + units:
        copy.wait()
    line.finish()
    for copy in over[1:] + small + first_scatter + misc_copies + [part_pass, out_far]:
        copy.wait_send()


def backward_call(dp, depth, experts, head, in_vmem, in_hbm):
    output_rows, width = in_vmem[6].shape
    seq_len = output_rows * depth
    slice_width = width // dp
    units = in_hbm[6].shape[1:]
    pair = in_hbm[14].shape[2]
    pairs = pair // head
    vmem, hbm = pl.BlockSpec(memory_space=pltpu.VMEM), pl.BlockSpec(memory_space=pl.ANY)
    shape = jax.ShapeDtypeStruct
    final = shape((4,) + units, BF)
    return pl.pallas_call(
        functools.partial(backward_body, (dp, depth, experts, head)),
        in_specs=[vmem] * len(in_vmem) + [hbm] * len(in_hbm),
        out_specs=[vmem, vmem, hbm, hbm, hbm, hbm, vmem, vmem, vmem],
        out_shape=[
            shape((output_rows, width), BF),
            shape((output_rows, width), BF),
            final,
            final,
            final,
            shape((seq_len, width), BF),
            shape((2, slice_width, 4 * pair), BF),
            shape((16, slice_width), F32),
            shape((8, slice_width), F32),
        ],
        scratch_shapes=[
            pltpu.VMEM((4,) + units, BF),
            pltpu.VMEM((3, 4) + units, BF),
            pltpu.VMEM((3, seq_len, width), BF),
            pltpu.VMEM((3, depth - 1, output_rows, width), BF),
            pltpu.VMEM((seq_len, 128), F32),
            pltpu.VMEM((depth - 1, output_rows, 128), F32),
            pltpu.VMEM((2, seq_len, width + 128), BF),
            pltpu.VMEM((2, seq_len, width), BF),
            pltpu.VMEM((2, 2, 2, slice_width, 4 * pair), BF),
            pltpu.VMEM((3, 2 * pairs, seq_len, head), BF),
            pltpu.VMEM((2 * pairs, seq_len, seq_len), BF),
            pltpu.VMEM((2, seq_len, pair), BF),
            pltpu.VMEM((2, seq_len, 1), F32),
            pltpu.VMEM((2, seq_len, 3 * pair), BF),
            pltpu.VMEM((seq_len, width), BF),
            pltpu.VMEM((3, output_rows, width), F32),
            pltpu.VMEM((2, 2, 2, slice_width, 4 * pair), BF),
            pltpu.VMEM((1, 2, 2, slice_width, 2 * pair), BF),
            pltpu.VMEM((2, 1, 2, slice_width, 2 * pair), BF),
            pltpu.VMEM((2, 1, 1, 2, slice_width, 2 * pair), BF),
            pltpu.VMEM((dp, 16, slice_width), F32),
            pltpu.VMEM((dp - 1, 16, slice_width), F32),
            pltpu.VMEM((depth - 1, 8, slice_width), F32),
            pltpu.VMEM((8, width), F32),
            pltpu.SemaphoreType.DMA((96,)),
            pltpu.SemaphoreType.DMA((96,)),
            pltpu.SemaphoreType.DMA((40,)),
        ],
        compiler_params=pltpu.CompilerParams(
            collective_id=1, has_side_effects=True, vmem_limit_bytes=62 * 2**20
        ),
    )(*in_vmem, *in_hbm)


def local_plain(
    dp,
    tokens,
    picture_ids,
    routes,
    slot_order,
    norm_gains,
    w_query,
    w_key,
    w_value,
    w_out,
    qkv_bias,
    router,
    shared_gate,
    shared_up,
    shared_down,
    expert_gate,
    expert_up,
    expert_down,
    out_grad,
):
    seq_len = picture_ids.shape[0]
    local_rows = tokens.shape[0]
    width = tokens.shape[1]
    experts, slice_width, hidden_units = expert_gate.shape
    top_count = routes.shape[1]
    capacity = 5 * seq_len * top_count // (4 * experts)
    heads_local = qkv_bias.shape[1]
    head_width = w_query.shape[1] // heads_local
    pair_heads = heads_local // 2
    pair_width = pair_heads * head_width
    mine_experts = experts // 4
    hidden_pad = -(-hidden_units // 128) * 128

    me = lax.axis_index("dp")
    zi = lax.axis_index("tensor")
    core, xi = me % 2, (me // 2) % 2
    group = me % 4
    bits = []
    while 2 ** (len(bits) + 1) <= dp:
        bits.append(2 ** len(bits))
    upper = bits[2:]

    def swap(array, bit):
        return lax.ppermute(array, "dp", [(i, i ^ bit) for i in range(dp)])

    def bit_of(bit):
        return (me // bit) % 2

    def join(mine, theirs, bit, axis):
        n = mine.shape[axis]
        shape = list(mine.shape)
        shape[axis] = 2 * n
        out = jnp.zeros(shape, mine.dtype)
        out = lax.dynamic_update_slice_in_dim(out, mine, n * bit_of(bit), axis)
        return lax.dynamic_update_slice_in_dim(out, theirs, n * (1 - bit_of(bit)), axis)

    def half(array, which, axis):
        n = array.shape[axis] // 2
        return lax.dynamic_slice_in_dim(array, which * n, n, axis)

    gains_z = lax.all_gather(norm_gains, "tensor", axis=1, tiled=True)
    misc_rows = 16
    bias_width = 3 * pair_heads * qkv_bias.shape[2]
    bias_cores = qkv_bias.reshape(3, 2, -1).swapaxes(0, 1).reshape(2, bias_width)

    def misc_pack(core_bias):
        wide = jnp.zeros((misc_rows, 2 * pair_width), BF)
        wide = wide.at[: experts + 1, :slice_width].set(router.T)
        wide = wide.at[experts + 1, :bias_width].set(core_bias)
        return wide.at[experts + 2 : experts + 4, :slice_width].set(gains_z)

    qk = jnp.concatenate(
        [w.reshape(slice_width, 2, pair_width) for w in (w_query, w_key)], axis=2
    )
    qk = jnp.concatenate(
        [qk, jnp.stack([misc_pack(bias_cores[0]), misc_pack(bias_cores[1])], axis=1)], axis=0
    )
    vo = jnp.concatenate(
        [w.reshape(slice_width, 2, pair_width) for w in (w_value, w_out.T)], axis=2
    )
    tokens_z = lax.all_gather(tokens, "tensor", axis=0, tiled=True)

    def gather_attention(pack, order):
        dims = (1,) * len(bits[1:])
        both = join(pick(pack, core, 1)[None], swap(pick(pack, 1 - core, 1), 1)[None], 1, 0)
        both = both.reshape(dims + both.shape)
        for bit in order:
            axis = len(bits) - 1 - bits.index(bit)
            both = join(both, swap(both, bit), bit, axis)
        return both.reshape((dp,) + both.shape[-2:])

    qk_all = gather_attention(qk, bits[1:])
    vo_full = gather_attention(vo, bits[:0:-1]).reshape(width, 2 * pair_width)
    qk_full = qk_all[:, :slice_width].reshape(width, 2 * pair_width)
    misc = qk_all[:, slice_width:]
    router_full = misc[:, : experts + 1, :slice_width].swapaxes(1, 2).reshape(width, -1)
    gain_rows = misc[:, experts + 2 : experts + 4, :slice_width].swapaxes(0, 1)
    gain_rows = gain_rows.reshape(2, width).astype(F32)
    bias = misc[:, experts + 1, :bias_width].astype(F32)
    bias = bias.reshape(dp, 3 * pair_heads, -1).swapaxes(0, 1).reshape(3, pair_width)

    tokens_sib = swap(tokens_z, 1)
    grad_z = lax.all_gather(out_grad, "tensor", axis=0, tiled=True)

    codes = jnp.concatenate([routes, slot_order], axis=1).T
    codes_x = swap(codes, 2)
    both_codes = swap(jnp.stack([codes, codes_x]), 1)
    codes_a = jnp.stack([codes, both_codes[0]])
    codes_b = jnp.stack([codes_x, both_codes[1]])
    pictures = jnp.stack([picture_ids, swap(picture_ids, 1)])

    def core_units(routed, shared):
        routed = routed.reshape(2, 2, mine_experts, hidden_units, slice_width)
        shared = shared.reshape(2, 2, 1, hidden_units, slice_width)

        def cut(which):
            return jnp.concatenate([pick(routed, which, 1), pick(shared, which, 1)], axis=1)

        return join(cut(core), swap(cut(1 - core), 1), 1, 3)

    def x_units(held):
        return join(pick(held, xi, 0), swap(pick(held, 1 - xi, 0), 2), 2, 2)

    def upper_units(held):
        for bit in upper[:-1]:
            held = join(held, swap(held, bit), bit, 2)
        return held, swap(held, upper[-1])

    def padded(*pairs):
        n = pairs[0][0].shape[-1]
        out = jnp.zeros((mine_experts + 1, len(pairs) * hidden_pad, 2 * n), BF)
        zero = jnp.int32(0)
        for k, (mine, theirs) in enumerate(pairs):
            row = jnp.int32(k * hidden_pad)
            out = lax.dynamic_update_slice(out, mine, (zero, row, n * bit_of(upper[-1])))
            out = lax.dynamic_update_slice(out, theirs, (zero, row, n * (1 - bit_of(upper[-1]))))
        return out

    down_c = core_units(expert_down, shared_down)
    gate_c = core_units(expert_gate.swapaxes(1, 2), shared_gate.T)
    up_c = core_units(expert_up.swapaxes(1, 2), shared_up.T)
    down_x = x_units(down_c)
    gate_x = x_units(gate_c)
    up_x = x_units(up_c)
    grad_x = swap(after(grad_z, up_x), 2)
    down_y = upper_units(down_x)
    gate_y = upper_units(gate_x)
    up_y = upper_units(up_x)

    rows_f = jnp.stack([tokens_z, tokens_sib]).astype(F32)
    qk_full = after(qk_full, down_c, gate_c, up_c)
    first_scale = lax.rsqrt(jnp.mean(rows_f * rows_f, axis=-1, keepdims=True) + EPS)
    first_norm = (rows_f * first_scale * gain_rows[0]).astype(BF)
    qk_pre = einsum("std,df->stf", first_norm, qk_full) + jnp.concatenate([bias[0], bias[1]])
    values = (einsum("std,df->stf", first_norm, vo_full[:, :pair_width]) + bias[2]).astype(BF)
    cos_part, sin_part = rope_tables(seq_len, head_width)
    qk_rot = rotate(
        qk_pre.reshape(2, seq_len, 2 * pair_heads, head_width), cos_part, sin_part
    ).astype(BF)
    qk_rot = after(qk_rot, down_x)
    queries, keys = qk_rot[:, :, :pair_heads], qk_rot[:, :, pair_heads:]
    values = values.reshape(2, seq_len, pair_heads, head_width)
    positions = jnp.arange(seq_len, dtype=jnp.int32)
    allowed = jnp.logical_or(
        positions[None, None, :] <= positions[None, :, None],
        pictures[:, :, None] * pictures[:, None, :] > 0,
    )
    score_scale = head_width ** (-0.5)
    scores = einsum("sqhd,skhd->shqk", queries, keys) * score_scale
    scores = jnp.where(allowed[:, None], scores, -1e30)
    weights = jnp.exp(scores - jnp.max(scores, axis=-1, keepdims=True))
    probs = weights / jnp.sum(weights, axis=-1, keepdims=True)
    probs_low = probs.astype(BF)
    head_mix = einsum("shqk,skhd->sqhd", probs_low, values).astype(BF)
    heads_out = after(head_mix.reshape(2, seq_len, pair_width), gate_x)
    out_weight = vo_full[:, pair_width:]
    attn_part = einsum("sqf,df->sqd", heads_out, out_weight)

    def core_sum(own, sibling):
        return own + swap(sibling.astype(BF), 1).astype(F32)

    def z_scatter(array):
        return lax.psum_scatter(
            array.astype(BF), "tensor", scatter_dimension=0, tiled=True
        ).astype(F32)

    inputs = tokens.astype(F32)
    hidden = inputs + z_scatter(core_sum(attn_part[0], attn_part[1]))
    hidden = after(hidden, up_x, down_y[1])
    second_scale = lax.rsqrt(jnp.mean(hidden * hidden, axis=-1, keepdims=True) + EPS)
    second_unit = hidden * second_scale
    second_norm = (second_unit * gain_rows[1]).astype(BF)
    norm_z = lax.all_gather(second_norm, "tensor", axis=0, tiled=True)
    norm_z = after(norm_z, gate_y[1], grad_x)
    down_all = padded(down_y)
    gateup_all = padded(gate_y, up_y)

    norm_x = swap(norm_z, 2)
    norm_a = jnp.stack([norm_z, swap(norm_z, 1)])
    norm_b = jnp.stack([norm_x, swap(norm_x, 1)])
    grad_a = jnp.stack([grad_z, swap(grad_z, 1)])
    grad_b = jnp.stack([grad_x, swap(grad_x, 1)])

    expert_ids = group * mine_experts + jnp.arange(mine_experts, dtype=jnp.int32)

    router_rows = jnp.pad(router_full.T, ((0, 16 - experts - 1), (0, 0)))
    group_ids = group.astype(jnp.int32).reshape(1)

    def slots_of(codes_in):
        routes_in, slots_in = codes_in[:, None, :top_count], codes_in[:, None, top_count:]
        matches = routes_in == expert_ids[None, :, None, None]
        return jnp.max(jnp.where(matches, slots_in, -1), axis=2)

    def feed(slots, rows, grads):
        slotted, slot_grad, pair, act, terms, pair_s, act_s, inner_s, probs_out = plain_act_call(
            experts, capacity, group_ids, slots, rows, grads, router_rows, gateup_all, down_all
        )
        terms = jnp.concatenate([terms.swapaxes(1, 2), inner_s], axis=-1)
        flat = [a.reshape(mine_experts, -1, a.shape[-1]) for a in (slotted, slot_grad, pair, act)]
        shared = [a.reshape(1, -1, a.shape[-1]) for a in (rows, grads, pair_s, act_s)]
        return (pair, pair_s), (act, act_s), terms, (flat, shared), probs_out

    slots_a, slots_b = slots_of(codes_a), slots_of(codes_b)
    fed_a = feed(slots_a, norm_a, grad_a)
    fed_b = feed(slots_b, norm_b, grad_b)
    columns_a, columns_b = slots_a[..., None], slots_b[..., None]
    row_grad_b = plain_back_call(columns_b, *fed_b[0], gateup_all)
    row_grad_a = plain_back_call(after(columns_a, row_grad_b), *fed_a[0], gateup_all)
    row_out_b = plain_back_call(after(columns_b, row_grad_a), *fed_b[1], down_all)
    row_out_a = plain_back_call(columns_a, *fed_a[1], down_all)

    def spread(terms):
        wide = jnp.zeros(terms.shape[:-1] + (128,), F32)
        wide = lax.dynamic_update_slice_in_dim(
            wide, terms[..., :mine_experts], group * mine_experts, terms.ndim - 1
        )
        return wide.at[..., experts].set(terms[..., mine_experts])

    def group_sum(a, b):
        across = b[0].astype(F32) + swap(b[1].astype(BF), 1).astype(F32)
        near = a[0].astype(F32) + swap(a[1].astype(BF), 1).astype(F32)
        return near + swap(across.astype(BF), 2).astype(F32)

    grad_sum = group_sum(row_grad_a, row_grad_b)
    term_sum = group_sum(spread(fed_a[2]), spread(fed_b[2]))
    packed = z_scatter(jnp.concatenate([grad_sum, term_sum], axis=-1))
    second_grad, gate_sums = packed[:, :width], packed[:, width:]

    data_a, data_b = fed_a[3], fed_b[3]

    def unit_grads(left, right):
        return jnp.concatenate(
            [
                plain_outer_call(
                    hidden_units,
                    hidden_pad,
                    dp,
                    [(data[k][left], data[k][right]) for data in (data_a, data_b)],
                )
                for k in range(2)
            ],
            axis=1,
        )

    def scatter_units(total):
        total = total.reshape((2,) * len(bits) + total.shape[1:])
        for bit in reversed(upper):
            axis = len(bits) - 1 - bits.index(bit)
            sent = half(total, 1 - bit_of(bit), axis)
            kept = half(total, bit_of(bit), axis)
            total = (kept.astype(F32) + swap(sent, bit).astype(F32)).astype(BF)
        total = total.reshape((2, 2) + total.shape[len(bits) :])
        held = join(pick(total, xi, 0)[None], swap(pick(total, 1 - xi, 0), 2)[None], 2, 0)
        return join(pick(held, core, 1)[:, None], swap(pick(held, 1 - core, 1), 1)[:, None], 1, 1)

    def split_units(held):
        routed = held[:, :, :mine_experts].reshape(experts, -1, slice_width)
        shared = held[:, :, mine_experts]
        return routed.astype(F32), shared.astype(F32)

    gateup_sum = scatter_units(unit_grads(2, 0))
    down_sum = scatter_units(unit_grads(3, 1))
    routed_gu, shared_gu = split_units(gateup_sum)
    routed_down, shared_down_sum = split_units(down_sum)
    shared_gu = shared_gu.reshape(4, 2, hidden_units, slice_width)
    egate_sum = routed_gu[:, :hidden_units].swapaxes(1, 2)
    eup_sum = routed_gu[:, hidden_units:].swapaxes(1, 2)
    sgate_sum = shared_gu[:, 0].reshape(-1, slice_width).T
    sup_sum = shared_gu[:, 1].reshape(-1, slice_width).T
    sdown_sum = shared_down_sum.reshape(-1, slice_width)

    row_start = zi * local_rows
    probs_local = lax.dynamic_slice_in_dim(fed_a[4][0], row_start, local_rows, 1).T
    probs_mine, weight_mine = probs_local[:, :experts], probs_local[:, experts]
    route_grad = gate_sums[:, :experts]
    expert_logit_grad = probs_mine * (
        route_grad - jnp.sum(probs_mine * route_grad, axis=-1, keepdims=True)
    )
    weight_logit_grad = gate_sums[:, experts] * weight_mine * (1.0 - weight_mine)
    logits_grad = jnp.concatenate([expert_logit_grad, weight_logit_grad[:, None]], axis=1).astype(
        BF
    )
    second_grad = second_grad + einsum("tf,df->td", logits_grad, router_full)
    gain_two_grad = jnp.sum(second_grad * second_unit, axis=0)
    unit_two = second_grad * gain_rows[1]
    hidden_grad = out_grad.astype(F32) + second_scale * (
        unit_two - second_unit * jnp.mean(unit_two * second_unit, axis=-1, keepdims=True)
    )
    attention_grad = hidden_grad.astype(BF)
    wide_logits = jnp.pad(logits_grad, ((0, 0), (0, 128 - experts - 1)))
    back_z = lax.all_gather(
        jnp.concatenate([attention_grad, wide_logits], axis=1), "tensor", axis=0, tiled=True
    )
    out_sum = after(group_sum(row_out_a, row_out_b), back_z)
    output = (hidden + z_scatter(out_sum)).astype(BF)
    logits_z = back_z[:, width : width + 16]
    back_own = back_z[:, :width]
    back_rows = jnp.stack([back_own, swap(back_own, 1)])

    router_part = einsum("tf,td->fd", logits_z, norm_z)[: experts + 1]

    out_proj = einsum("std,stf->df", back_rows, heads_out)
    mix_grad = einsum("std,df->stf", back_rows, out_weight).astype(BF)
    mix_grad = mix_grad.reshape(2, seq_len, pair_heads, head_width)
    prob_grad = einsum("sqhd,skhd->shqk", mix_grad, values)
    score_grad = (
        probs * (prob_grad - jnp.sum(probs * prob_grad, axis=-1, keepdims=True))
    ).astype(BF)
    query_rot = einsum("shqk,skhd->sqhd", score_grad, keys) * score_scale
    key_rot = einsum("shqk,sqhd->skhd", score_grad, queries) * score_scale
    value_grad = einsum("shqk,sqhd->skhd", probs_low, mix_grad)
    qk_grad = rotate(jnp.concatenate([query_rot, key_rot], axis=2), cos_part, -sin_part)
    qk_grad = qk_grad.astype(BF).reshape(2, seq_len, 2 * pair_width)
    v_grad = value_grad.astype(BF).reshape(2, seq_len, pair_width)
    first_part = einsum("stf,df->std", qk_grad, qk_full) + einsum(
        "stf,df->std", v_grad, vo_full[:, :pair_width]
    )
    first_grad = z_scatter(core_sum(first_part[0], first_part[1]))

    gain_one_grad = jnp.sum(first_part * (rows_f * first_scale), axis=(0, 1))
    bias_part = jnp.concatenate(
        [jnp.sum(qk_grad.astype(F32), axis=(0, 1)), jnp.sum(v_grad.astype(F32), axis=(0, 1))]
    )
    bias_part = bias_part.reshape(3 * pair_heads, dp, -1).swapaxes(0, 1).reshape(dp, 1, -1)
    gain_part = jnp.stack([gain_one_grad, gain_two_grad]).reshape(2, dp, slice_width)

    def wide_rows(rows):
        return jnp.pad(rows, ((0, 0), (0, 0), (0, 2 * pair_width - rows.shape[2])))

    misc_part = jnp.concatenate(
        [
            wide_rows(router_part.reshape(experts + 1, dp, slice_width).swapaxes(0, 1)),
            wide_rows(bias_part),
            wide_rows(gain_part.swapaxes(0, 1)),
            jnp.zeros((dp, misc_rows - experts - 4, 2 * pair_width), F32),
        ],
        axis=1,
    )
    qk_total = einsum("std,stf->df", first_norm, qk_grad).reshape(dp, slice_width, -1)
    qk_total = jnp.concatenate([qk_total, misc_part], axis=1)
    vo_total = jnp.concatenate([einsum("std,stf->df", first_norm, v_grad), out_proj], axis=1)
    vo_total = vo_total.reshape(dp, slice_width, -1)

    def scatter_attention(total, order):
        total = total.reshape((2,) * len(bits) + total.shape[1:])
        for bit in order:
            axis = len(bits) - 1 - bits.index(bit)
            sent = half(total, 1 - bit_of(bit), axis).astype(BF)
            total = half(total, bit_of(bit), axis) + swap(sent, bit).astype(F32)
        total = total.reshape((2,) + total.shape[-2:]).astype(BF)
        return pick(total, core, 0), swap(pick(total, 1 - core, 0), 1)

    def columns_of(mine, theirs):
        held = join(mine[:slice_width, None], theirs[:slice_width, None], 1, 1)
        first, second = held[..., :pair_width], held[..., pair_width:]
        return (
            first.reshape(slice_width, -1).astype(F32),
            second.reshape(slice_width, -1).astype(F32),
        )

    qk_mine, qk_theirs = scatter_attention(qk_total, bits[:0:-1])
    vo_mine, vo_theirs = scatter_attention(vo_total, bits[1:])
    qk_sums = columns_of(qk_mine, qk_theirs)
    vo_sums = columns_of(vo_mine, vo_theirs)
    misc_mine = qk_mine[slice_width:].astype(F32)
    misc_theirs = qk_theirs[slice_width:].astype(F32)
    misc_sum = misc_mine + misc_theirs
    router_sum = misc_sum[: experts + 1, :slice_width].T
    bias_sums = join(
        misc_mine[experts + 1, :bias_width].reshape(3, 1, pair_heads, -1),
        misc_theirs[experts + 1, :bias_width].reshape(3, 1, pair_heads, -1),
        1,
        1,
    ).reshape(3, heads_local, -1)
    gain_sums = lax.all_gather(
        misc_sum[experts + 2 : experts + 4, :slice_width], "tensor", axis=0, tiled=False
    )
    tensor = gain_sums.shape[0]
    gain_sums = jnp.sum(gain_sums, axis=0).reshape(2, tensor, -1)
    gain_sums = pick(gain_sums, zi, 1)

    unit_mine = inputs * lax.rsqrt(jnp.mean(inputs * inputs, axis=-1, keepdims=True) + EPS)
    scale_mine = lax.rsqrt(jnp.mean(inputs * inputs, axis=-1, keepdims=True) + EPS)
    unit_one = first_grad * gain_rows[0]
    input_grad = hidden_grad + scale_mine * (
        unit_one - unit_mine * jnp.mean(unit_one * unit_mine, axis=-1, keepdims=True)
    )
    return (
        output,
        input_grad.astype(BF),
        gain_sums,
        qk_sums[0],
        qk_sums[1],
        vo_sums[0],
        vo_sums[1].T,
        bias_sums,
        router_sum,
        sgate_sum,
        sup_sum,
        sdown_sum,
        egate_sum,
        eup_sum,
        routed_down,
    )


def local_fused(
    dp,
    depth,
    tokens,
    picture_ids,
    routes,
    slot_order,
    norm_gains,
    w_query,
    w_key,
    w_value,
    w_out,
    qkv_bias,
    router,
    shared_gate,
    shared_up,
    shared_down,
    expert_gate,
    expert_up,
    expert_down,
    out_grad,
):
    seq_len = picture_ids.shape[0]
    local_rows = tokens.shape[0]
    width = tokens.shape[1]
    experts, slice_width, hidden_units = expert_gate.shape
    top_count = routes.shape[1]
    capacity = 5 * seq_len * top_count // (4 * experts)
    heads_local = qkv_bias.shape[1]
    head_width = w_query.shape[1] // heads_local
    pair_heads = heads_local // 2
    pair_width = pair_heads * head_width
    mine_experts = experts // 4
    hidden_pad = -(-hidden_units // 128) * 128

    me = lax.axis_index("dp")
    zi = lax.axis_index("tensor")
    core, xi = me % 2, (me // 2) % 2
    group = me % 4
    bits = []
    while 2 ** (len(bits) + 1) <= dp:
        bits.append(2 ** len(bits))
    upper = bits[2:]

    def swap(array, bit):
        return lax.ppermute(array, "dp", [(i, i ^ bit) for i in range(dp)])

    def bit_of(bit):
        return (me // bit) % 2

    def join(mine, theirs, bit, axis):
        n = mine.shape[axis]
        shape = list(mine.shape)
        shape[axis] = 2 * n
        out = jnp.zeros(shape, mine.dtype)
        out = lax.dynamic_update_slice_in_dim(out, mine, n * bit_of(bit), axis)
        return lax.dynamic_update_slice_in_dim(out, theirs, n * (1 - bit_of(bit)), axis)

    def half(array, which, axis):
        n = array.shape[axis] // 2
        return lax.dynamic_slice_in_dim(array, which * n, n, axis)

    codes = jnp.concatenate([routes.T, slot_order.T, picture_ids[None]], axis=0)
    codes = jnp.pad(codes, ((0, 16 - codes.shape[0]), (0, 0)))
    bias_cores = qkv_bias.reshape(3, 2, -1).swapaxes(0, 1).reshape(2, -1)
    bias_width = bias_cores.shape[1]
    misc = jnp.zeros((16, slice_width), F32)
    misc = misc.at[: experts + 1].set(router.T.astype(F32))
    misc = misc.at[experts + 1 : experts + 3, :bias_width].set(bias_cores.astype(F32))
    gains = lax.dynamic_update_slice(
        jnp.zeros((8, slice_width), F32),
        norm_gains.astype(F32),
        (jnp.int32(0), zi * norm_gains.shape[1]),
    )
    cos_part, sin_part = rope_tables(seq_len, head_width)
    cos_rows = jnp.concatenate([cos_part, cos_part], axis=1)
    sin_rows = jnp.concatenate([-sin_part, sin_part], axis=1)
    (
        hidden,
        norm_all,
        grads_all,
        gateup_all,
        down_all,
        codes_all,
        misc_all,
        gain_rows,
        tok,
        attn_weights,
        qkv,
        probs_low,
        heads_out,
    ) = forward_call(
        dp,
        depth,
        experts,
        head_width,
        (codes, misc, gains, cos_rows, sin_rows),
        (tokens, out_grad, w_query, w_key, w_value, w_out.T),
        (
            expert_gate.swapaxes(1, 2),
            expert_up.swapaxes(1, 2),
            expert_down,
            shared_gate.T.reshape(4, hidden_units, slice_width),
            shared_up.T.reshape(4, hidden_units, slice_width),
            shared_down.reshape(4, hidden_units, slice_width),
        ),
    )
    gateup_all = gateup_all.reshape(mine_experts + 1, 2 * hidden_pad, width)
    down_all = down_all.reshape(mine_experts + 1, hidden_pad, width)
    router_rows = jnp.concatenate([misc_all[d] for d in range(dp)], axis=1)
    router_rows = jnp.where(jnp.arange(16)[:, None] <= experts, router_rows, 0.0).astype(BF)
    router_full = router_rows[: experts + 1].T
    group_ids = group.astype(jnp.int32).reshape(1)

    def feed(chunk, group_in):
        return act_call(
            experts,
            top_count,
            capacity,
            chunk,
            group_in,
            codes_all,
            norm_all,
            grads_all,
            router_rows,
            gateup_all,
            down_all,
        )

    def back(chunk, group_in, routed, shared, weight):
        return back_call(top_count, chunk, group_in, codes_all, routed, shared, weight)

    def across(own, sibling):
        total = own.astype(F32) + swap(sibling, 1).astype(F32)
        return total.astype(own.dtype)

    slots_b, slot_grads_b, pair_b, act_b, pair_sb, act_sb, terms_b, _ = feed(1, group_ids)
    terms_far = swap(across(terms_b[0], terms_b[1]), 2)
    grad_b = back(1, group_ids, pair_b, pair_sb, gateup_all)
    grad_far = across(*grad_b)
    slots_a, slot_grads_a, pair_a, act_a, pair_sa, act_sa, terms_a, probs_out = feed(
        0, after(group_ids, grad_far, terms_far)
    )
    grad_far = swap(grad_far, 2)

    def rows_of(array):
        return array.reshape(array.shape[0], -1, array.shape[-1])

    def chunks_of(array):
        return array.reshape(2, 2 * seq_len, width)

    def flat(array):
        return array.reshape(1, -1, array.shape[-1])

    gate_total, up_total = units_call(
        hidden_units,
        hidden_pad,
        dp,
        [(rows_of(pair_a), rows_of(slots_a)), (rows_of(pair_b), rows_of(slots_b))],
        [(flat(pair_sa), chunks_of(norm_all), 0), (flat(pair_sb), chunks_of(norm_all), 1)],
    )
    gate_sent = lax.dynamic_slice_in_dim(gate_total, (1 - me // 4) * 4, 4, 0)
    out_b = back(1, after(group_ids, gate_sent), act_b, act_sb, down_all)
    out_far = across(*out_b)
    gate_in = swap(gate_sent, 4)
    grad_a = back(0, after(group_ids, out_far), pair_a, pair_sa, gateup_all)
    out_a = back(0, after(group_ids, grad_a[0]), act_a, act_sa, down_all)
    (down_total,) = units_call(
        hidden_units,
        hidden_pad,
        dp,
        [
            (rows_of(act_a), rows_of(slot_grads_a)),
            (after(rows_of(act_b), out_a[0]), rows_of(slot_grads_b)),
        ],
        [(flat(act_sa), chunks_of(grads_all), 0), (flat(act_sb), chunks_of(grads_all), 1)],
    )
    grad_parts = (grad_a[0], swap(grad_a[1], 1), grad_far)
    out_parts = (out_a[0], swap(out_a[1], 1), out_far)
    terms = jnp.stack([terms_a[0], swap(terms_a[1], 1), terms_far])
    probs_mine = lax.dynamic_slice_in_dim(probs_out[0], zi * local_rows, local_rows, 1).T
    probs_mine = jnp.pad(probs_mine, ((0, 0), (0, 128 - probs_mine.shape[1])))
    router_wide = jnp.pad(router_rows, ((0, 128 - router_rows.shape[0]), (0, 0)))
    output, input_grad, gate_sum, up_sum, down_sum, _, attn_sum, misc_sum, gains_sum = backward_call(
        dp,
        depth,
        experts,
        head_width,
        (terms, probs_mine, router_wide, gain_rows, cos_rows, sin_rows, hidden, out_grad),
        grad_parts
        + out_parts
        + (gate_in, gate_total, up_total, down_total)
        + (tok, attn_weights, qkv, probs_low, heads_out, norm_all),
    )

    def split_units(held):
        routed = held[:, :mine_experts].reshape(experts, hidden_units, slice_width)
        shared = held[:, mine_experts].reshape(-1, slice_width)
        return routed.astype(F32), shared.astype(F32)

    egate_sum, sgate_sum = split_units(gate_sum)
    eup_sum, sup_sum = split_units(up_sum)
    edown_sum, sdown_sum = split_units(down_sum)

    def columns_of(kind):
        held = attn_sum[:, :, kind * pair_width : (kind + 1) * pair_width].swapaxes(0, 1)
        return held.reshape(slice_width, -1).astype(F32)

    bias_sums = misc_sum[experts + 1 : experts + 3, :bias_width].reshape(2, 3, pair_heads, -1)
    bias_sums = bias_sums.swapaxes(0, 1).reshape(3, heads_local, -1)
    piece = norm_gains.shape[1]
    gain_sums = lax.dynamic_slice(gains_sum[3:5], (jnp.int32(0), zi * piece), (2, piece))
    return (
        output,
        input_grad,
        gain_sums,
        columns_of(0),
        columns_of(1),
        columns_of(2),
        columns_of(3).T,
        bias_sums,
        misc_sum[: experts + 1].T,
        sgate_sum.T,
        sup_sum.T,
        sdown_sum,
        egate_sum.swapaxes(1, 2),
        eup_sum.swapaxes(1, 2),
        edown_sum,
    )


def solution(mesh):
    dp, depth = mesh.shape["dp"], mesh.shape["tensor"]

    def body(*arrays):
        if arrays[5].shape[0] % 128 == 0 and dp == 8 and depth == 4:
            return local_fused(dp, depth, *arrays)
        return local_plain(dp, *arrays)

    return jax.shard_map(
        body,
        mesh=mesh,
        in_specs=(
            P(("dp", "tensor"), None),
            P("dp"),
            P("dp", None),
            P("dp", None),
            P(None, ("dp", "tensor")),
            P("dp", "tensor"),
            P("dp", "tensor"),
            P("dp", "tensor"),
            P("tensor", "dp"),
            P(None, "tensor", "dp"),
            P("dp", None),
            P("dp", "tensor"),
            P("dp", "tensor"),
            P("tensor", "dp"),
            P(None, "dp", "tensor"),
            P(None, "dp", "tensor"),
            P(None, "tensor", "dp"),
            P(("dp", "tensor"), None),
        ),
        out_specs=(
            P(("dp", "tensor"), None),
            P(("dp", "tensor"), None),
            P(None, ("dp", "tensor")),
            P("dp", "tensor"),
            P("dp", "tensor"),
            P("dp", "tensor"),
            P("tensor", "dp"),
            P(None, "tensor", "dp"),
            P("dp", None),
            P("dp", "tensor"),
            P("dp", "tensor"),
            P("tensor", "dp"),
            P(None, "dp", "tensor"),
            P(None, "dp", "tensor"),
            P(None, "tensor", "dp"),
        ),
        check_vma=False,
    )
```

```python
import functools

import jax
import jax.numpy as jnp
from jax import lax
from jax.experimental import pallas as pl
from jax.experimental.pallas import tpu as pltpu
from jax.sharding import PartitionSpec as P

EPS = 1e-06
THETA = 1000000.0
BF = jnp.bfloat16
F32 = jnp.float32


def rope_tables(length, width):
    half_width = width // 2
    inverse = THETA ** (-(2.0 * jnp.arange(half_width, dtype=F32)) / width)
    angles = jnp.arange(length, dtype=F32)[:, None] * inverse[None, :]
    return jnp.cos(angles), jnp.sin(angles)


def rotate(field_in, cos_part, sin_part):
    half_width = field_in.shape[-1] // 2
    low, high = field_in[..., :half_width], field_in[..., half_width:]
    cos_rows, sin_rows = cos_part[:, None, :], sin_part[:, None, :]
    return jnp.concatenate(
        [low * cos_rows - high * sin_rows, high * cos_rows + low * sin_rows], axis=-1
    )


def einsum(spec, *args):
    return jnp.einsum(spec, *args, preferred_element_type=F32)


def silu_parts(gate_in):
    gate_sig = jax.nn.sigmoid(gate_in)
    return gate_in * gate_sig, gate_sig * (1.0 + gate_in * (1.0 - gate_sig))


def after(array, *others):
    return lax.optimization_barrier((array,) + others)[0]


def pick(array, index, axis):
    return lax.dynamic_index_in_dim(array, index, axis, keepdims=False)


VMEM_LIMIT = 58 * 2**20


def dot(left, right, left_dim=1, right_dim=0):
    return lax.dot_general(
        left, right, (((left_dim,), (right_dim,)), ((), ())), preferred_element_type=F32
    )


def call(body, grid, in_specs, out_specs, out_shape, flops, moved, scratch=()):
    return pl.pallas_call(
        body,
        grid=grid,
        in_specs=in_specs,
        out_specs=out_specs,
        out_shape=out_shape,
        scratch_shapes=scratch,
        cost_estimate=pl.CostEstimate(flops=flops, bytes_accessed=moved, transcendentals=0),
        compiler_params=pltpu.CompilerParams(vmem_limit_bytes=VMEM_LIMIT),
    )


def plain_act_body(
    experts,
    units,
    group_ref,
    slot_ref,
    rows_ref,
    grads_ref,
    router_ref,
    gateup_ref,
    down_ref,
    slotted_ref,
    slotgrad_ref,
    pair_ref,
    act_ref,
    terms_ref,
    pair_s_ref,
    act_s_ref,
    inner_s_ref,
    probs_ref,
):
    unit = pl.program_id(1)
    half = gateup_ref.shape[1] // 2
    seq_len = rows_ref.shape[1]
    capacity = slotted_ref.shape[2]

    @pl.when(unit == 0)
    def _():
        logits = dot(router_ref[...], rows_ref[0], 1, 1)
        row = lax.broadcasted_iota(jnp.int32, logits.shape, 0)
        routed = jnp.where(row < experts, logits, -1e30)
        raised = jnp.exp(routed - jnp.max(routed, axis=0, keepdims=True))
        soft = raised / jnp.sum(raised, axis=0, keepdims=True)
        probs_ref[0] = jnp.where(row < experts, soft, jax.nn.sigmoid(logits))

    def parts(data, cot, weight):
        both = dot(data, gateup_ref[0], 1, 1)
        cot_in = dot(cot, down_ref[0], 1, 1)
        gate_in, up_in = both[:, :half], both[:, half:]
        gate_act, gate_slope = silu_parts(gate_in)
        act = gate_act * up_in
        inner = jnp.sum(act.astype(BF).astype(F32) * cot_in, axis=1, keepdims=True)
        cot_in = cot_in * weight
        return (
            (act * weight).astype(BF),
            (cot_in * up_in * gate_slope).astype(BF),
            (cot_in * gate_act).astype(BF),
            inner,
        )

    @pl.when(unit < units - 1)
    def _():
        slot = slot_ref[0, pl.ds(unit, 1), :]
        mask = lax.broadcasted_iota(jnp.int32, (capacity, seq_len), 0) == slot
        onehot = mask.astype(F32).astype(BF)
        slotted_ref[0, 0] = dot(onehot, rows_ref[0]).astype(BF)
        slotgrad_ref[0, 0] = dot(onehot, grads_ref[0]).astype(BF)
        probs = probs_ref[0]
        row = lax.broadcasted_iota(jnp.int32, probs.shape, 0)
        expert = group_ref[0] * (units - 1) + unit
        gate = jnp.sum(jnp.where(row == expert, probs, 0.0), axis=0, keepdims=True)
        weight = jnp.sum(jnp.where(mask, gate, 0.0), axis=1, keepdims=True)
        act, gate_grad, up_grad, inner = parts(slotted_ref[0, 0], slotgrad_ref[0, 0], weight)
        act_ref[0, 0] = act
        pair_ref[0, 0, :, :half] = gate_grad
        pair_ref[0, 0, :, half:] = up_grad
        terms_ref[0, pl.ds(unit, 1), :] = jnp.sum(
            jnp.where(mask, inner, 0.0), axis=0, keepdims=True
        )

    @pl.when(unit == units - 1)
    def _():
        logits = dot(rows_ref[0], router_ref[...], 1, 1)
        weight = jax.nn.sigmoid(logits[:, experts : experts + 1])
        act, gate_grad, up_grad, inner = parts(rows_ref[0], grads_ref[0], weight)
        act_s_ref[0] = act
        pair_s_ref[0, :, :half] = gate_grad
        pair_s_ref[0, :, half:] = up_grad
        inner_s_ref[0] = inner


def plain_act_call(experts, capacity, group, slots, rows, grads, router, gateup, down):
    count, seq_len, width = rows.shape
    units, wide, _ = gateup.shape
    half = wide // 2
    routed = units - 1

    def seq(s, u):
        return (s, 0, 0)

    def unit(s, u):
        return (u, 0, 0)

    def slot(s, u):
        return (jnp.minimum(u, routed - 1), s, 0, 0)

    work = count * (routed * capacity + seq_len) * width
    return call(
        functools.partial(plain_act_body, experts, units),
        (count, units),
        [
            pl.BlockSpec(memory_space=pltpu.SMEM),
            pl.BlockSpec((1, routed, seq_len), seq),
            pl.BlockSpec((1, seq_len, width), seq),
            pl.BlockSpec((1, seq_len, width), seq),
            pl.BlockSpec(router.shape, lambda s, u: (0, 0)),
            pl.BlockSpec((1, wide, width), unit),
            pl.BlockSpec((1, half, width), unit),
        ],
        [
            pl.BlockSpec((1, 1, capacity, width), slot),
            pl.BlockSpec((1, 1, capacity, width), slot),
            pl.BlockSpec((1, 1, capacity, wide), slot),
            pl.BlockSpec((1, 1, capacity, half), slot),
            pl.BlockSpec((1, routed, seq_len), seq),
            pl.BlockSpec((1, seq_len, wide), seq),
            pl.BlockSpec((1, seq_len, half), seq),
            pl.BlockSpec((1, seq_len, 1), seq),
            pl.BlockSpec((1,) + (router.shape[0], seq_len), seq),
        ],
        [
            jax.ShapeDtypeStruct((routed, count, capacity, width), BF),
            jax.ShapeDtypeStruct((routed, count, capacity, width), BF),
            jax.ShapeDtypeStruct((routed, count, capacity, wide), BF),
            jax.ShapeDtypeStruct((routed, count, capacity, half), BF),
            jax.ShapeDtypeStruct((count, routed, seq_len), F32),
            jax.ShapeDtypeStruct((count, seq_len, wide), BF),
            jax.ShapeDtypeStruct((count, seq_len, half), BF),
            jax.ShapeDtypeStruct((count, seq_len, 1), F32),
            jax.ShapeDtypeStruct((count, router.shape[0], seq_len), F32),
        ],
        2 * work * 3 * half + 4 * count * routed * capacity * seq_len * width,
        8 * count * seq_len * width * 2,
    )(group, slots, rows, grads, router, gateup, down)


def plain_back_body(slot_ref, routed_ref, shared_ref, weight_ref, out_ref):
    routed, _, capacity, _ = routed_ref.shape
    seq_len = shared_ref.shape[1]
    total = dot(shared_ref[0], weight_ref[routed])
    lane = lax.broadcasted_iota(jnp.int32, (seq_len, capacity), 1)
    for e in range(routed):
        slot_rows = dot(routed_ref[e, 0], weight_ref[e]).astype(BF)
        onehot = (lane == slot_ref[0, e]).astype(F32).astype(BF)
        total = total + dot(onehot, slot_rows)
    out_ref[0] = total.astype(BF)


def plain_back_call(slots, routed, shared, weight):
    units, wide, width = weight.shape
    count, seq_len, _ = shared.shape
    capacity = routed.shape[2]
    block = min(width, 512)
    work = count * ((units - 1) * capacity + seq_len) * width
    return call(
        plain_back_body,
        (width // block, count),
        [
            pl.BlockSpec((1, units - 1, seq_len, 1), lambda j, s: (s, 0, 0, 0)),
            pl.BlockSpec((units - 1, 1, capacity, wide), lambda j, s: (0, s, 0, 0)),
            pl.BlockSpec((1, seq_len, wide), lambda j, s: (s, 0, 0)),
            pl.BlockSpec((units, wide, block), lambda j, s: (0, 0, j)),
        ],
        pl.BlockSpec((1, seq_len, block), lambda j, s: (s, 0, j)),
        jax.ShapeDtypeStruct((count, seq_len, width), BF),
        2 * work * wide + 2 * count * (units - 1) * capacity * seq_len * width,
        units * wide * width * 2 + count * seq_len * width * 2,
    )(slots, routed, shared, weight)


def plain_outer_body(keep, pad, left_a, right_a, left_b, right_b, out_ref):
    total = dot(left_a[0], right_a[0], 0, 0) + dot(left_b[0], right_b[0], 0, 0)
    total = total.astype(BF)
    blocks, _, rows, slice_width = out_ref.shape
    for part in range(rows // keep):
        for k in range(blocks):
            out_ref[k, 0, part * keep : (part + 1) * keep] = total[
                part * pad : part * pad + keep, k * slice_width : (k + 1) * slice_width
            ]


def plain_outer_call(keep, pad, dp, pairs):
    (left_a, right_a), (left_b, right_b) = pairs
    units, rows, wide = left_a.shape
    width = right_a.shape[2]
    slice_width = width // dp
    blocks = max(1, 512 // slice_width)
    kept = wide // pad * keep

    def left(n):
        return pl.BlockSpec((1, n, wide), lambda u, j: (u, 0, 0))

    def right(n):
        return pl.BlockSpec((1, n, blocks * slice_width), lambda u, j: (u, 0, j))

    return call(
        functools.partial(plain_outer_body, keep, pad),
        (units, dp // blocks),
        [left(rows), right(rows), left(rows), right(rows)],
        pl.BlockSpec((blocks, 1, kept, slice_width), lambda u, j: (j, u, 0, 0)),
        jax.ShapeDtypeStruct((dp, units, kept, slice_width), BF),
        4 * units * rows * wide * width,
        units * rows * (wide + width) * 4,
    )(left_a, right_a, left_b, right_b)


def act_body(
    experts,
    top_count,
    group_ref,
    codes_ref,
    rows_ref,
    grads_ref,
    router_ref,
    gateup_ref,
    down_ref,
    pair_ref,
    act_ref,
    terms_ref,
    probs_ref,
    weights,
    routed,
):
    unit, units = pl.program_id(0), pl.num_programs(0)
    half = gateup_ref.shape[1] // 2
    count, seq_len, width = rows_ref.shape
    data = rows_ref[...].reshape(count * seq_len, width)
    cot = grads_ref[...].reshape(count * seq_len, width)
    lane = lax.broadcasted_iota(jnp.int32, weights.shape, 1)

    @pl.when(unit == 0)
    def _():
        logits = dot(data, router_ref[...], 1, 1)
        chosen = jnp.where(lane < experts, logits, -1e30)
        raised = jnp.exp(chosen - jnp.max(chosen, axis=1, keepdims=True))
        soft = raised / jnp.sum(raised, axis=1, keepdims=True)
        probs = jnp.where(lane < experts, soft, jax.nn.sigmoid(logits))
        for s in range(count):
            codes = codes_ref[s]
            row = lax.broadcasted_iota(jnp.int32, codes.shape, 0)
            named = row == experts
            for k in range(top_count):
                named = jnp.logical_or(named, codes[k : k + 1] == row)
            named = jnp.logical_and(named, row <= experts).astype(F32).astype(BF)
            place = (codes.shape[0], weights.shape[1])
            same = lax.broadcasted_iota(jnp.int32, place, 0) == lax.broadcasted_iota(
                jnp.int32, place, 1
            )
            at = slice(s * seq_len, (s + 1) * seq_len)
            routed[at] = dot(named, same.astype(F32).astype(BF), 0, 0)
            probs_ref[s] = probs[at]
        weights[...] = probs * routed[...]
        terms_ref[...] = jnp.zeros_like(terms_ref)

    mine = lane == jnp.where(unit < units - 1, group_ref[0] * (units - 1) + unit, experts)
    weight = jnp.sum(jnp.where(mine, weights[...], 0.0), axis=1, keepdims=True)
    both = dot(data, gateup_ref[0], 1, 1)
    cot_in = dot(cot, down_ref[0], 1, 1)
    gate_in, up_in = both[:, :half], both[:, half:]
    gate_act, gate_slope = silu_parts(gate_in)
    act = gate_act * up_in
    inner = jnp.sum(act.astype(BF).astype(F32) * cot_in, axis=1, keepdims=True)
    cot_in = cot_in * weight
    act_ref[...] = (act * weight).astype(BF)
    pair_ref[:, :half] = (cot_in * up_in * gate_slope).astype(BF)
    pair_ref[:, half:] = (cot_in * gate_act).astype(BF)
    terms_ref[...] += jnp.where(mine, inner * routed[...], 0.0).reshape(terms_ref.shape)


def act_call(experts, top_count, chunk, group, codes, rows, grads, router, gateup, down):
    _, seq_len, width = rows.shape
    units, wide, _ = gateup.shape
    half, count = wide // 2, 2
    total = count * seq_len

    def part(*shape):
        return pl.BlockSpec(
            shape,
            lambda u: (chunk,) + (0,) * (len(shape) - 1),
            pipeline_mode=pl.Buffered(1),
        )

    def unit(u):
        return (u, 0, 0)

    def whole(u):
        return (0, 0, 0)

    return call(
        functools.partial(act_body, experts, top_count),
        (units,),
        [
            pl.BlockSpec(memory_space=pltpu.SMEM),
            part(count, codes.shape[1], seq_len),
            part(count, seq_len, width),
            part(count, seq_len, width),
            pl.BlockSpec(router.shape, lambda u: (0, 0)),
            pl.BlockSpec((1, wide, width), unit),
            pl.BlockSpec((1, half, width), unit),
        ],
        [
            pl.BlockSpec((total, wide), lambda u: (0, u)),
            pl.BlockSpec((total, half), lambda u: (0, u)),
            pl.BlockSpec((count, seq_len, 128), whole),
            pl.BlockSpec((count, seq_len, 128), whole),
        ],
        [
            jax.ShapeDtypeStruct((total, units * wide), BF),
            jax.ShapeDtypeStruct((total, units * half), BF),
            jax.ShapeDtypeStruct((count, seq_len, 128), F32),
            jax.ShapeDtypeStruct((count, seq_len, 128), F32),
        ],
        2 * total * units * 3 * half * width,
        4 * total * width + units * 3 * half * width * 2,
        [pltpu.VMEM((total, 128), F32), pltpu.VMEM((total, 128), F32)],
    )(group, codes, rows, grads, router, gateup, down)


def back_body(left_ref, weight_ref, *out_refs):
    seq_len = out_refs[0].shape[0]
    total = dot(left_ref[...], weight_ref[...]).astype(BF)
    for s, out_ref in enumerate(out_refs):
        out_ref[...] = total[s * seq_len : (s + 1) * seq_len]


def back_call(left, weight):
    units, wide, width = weight.shape
    weight = weight.reshape(units * wide, width)
    total, depth = left.shape
    block = min(width, 512)
    return call(
        back_body,
        (width // block,),
        [
            pl.BlockSpec((total, depth), lambda j: (0, 0), pipeline_mode=pl.Buffered(1)),
            pl.BlockSpec((depth, block), lambda j: (0, j)),
        ],
        [pl.BlockSpec((total // 2, block), lambda j: (0, j))] * 2,
        [jax.ShapeDtypeStruct((total // 2, width), BF)] * 2,
        2 * total * depth * width,
        (total * depth + depth * width + total * width) * 2,
    )(left, weight)


def units_body(keep, pad, left_a, left_b, right_a, right_b, *outs):
    total = dot(left_a[...], right_a[0], 0, 0) + dot(left_b[...], right_b[0], 0, 0)
    total = total.astype(BF)
    for part, out_ref in enumerate(outs):
        blocks, _, _, slice_width = out_ref.shape
        for k in range(blocks):
            out_ref[k, 0] = total[
                part * pad : part * pad + keep, k * slice_width : (k + 1) * slice_width
            ]


def units_call(keep, pad, dp, units, left_a, left_b, right):
    right = right.reshape(2, left_a.shape[0], -1)
    total, width = right.shape[1:]
    wide = left_a.shape[1] // units
    slice_width = width // dp
    blocks = max(1, 1024 // slice_width)
    parts = wide // pad
    left = pl.BlockSpec((total, wide), lambda u, j: (0, u))

    def chunk(k):
        return pl.BlockSpec((1, total, blocks * slice_width), lambda u, j: (k, 0, j))

    return call(
        functools.partial(units_body, keep, pad),
        (units, dp // blocks),
        [left, left, chunk(0), chunk(1)],
        [pl.BlockSpec((blocks, 1, keep, slice_width), lambda u, j: (j, u, 0, 0))] * parts,
        [jax.ShapeDtypeStruct((dp, units, keep, slice_width), BF)] * parts,
        4 * total * units * wide * width,
        (4 * total * width + 4 * total * units * wide + units * wide * width) * 2,
    )(left_a, left_b, right, right)


MESH = pl.DeviceIdType.MESH


class Copies:
    def __init__(self, send, recv, here):
        self.send, self.recv, self.here = send, recv, here
        self.remote_count = self.local_count = 0

    def remote(self, src, dst, **device):
        k = self.remote_count
        self.remote_count += 1
        return pltpu.make_async_remote_copy(
            src_ref=src,
            dst_ref=dst,
            send_sem=self.send.at[k],
            recv_sem=self.recv.at[k],
            device_id=device,
            device_id_type=MESH,
        )

    def local(self, src, dst):
        k = self.local_count
        self.local_count += 1
        return pltpu.make_async_copy(src, dst, self.here.at[k])


class Line:
    def __init__(self, copies, buffer, z, depth, rows):
        self.z, self.depth = z, depth

        def piece(p):
            return buffer.at[pl.ds(pl.multiple_of(p * rows, rows), rows)]

        def make(k, sign):
            p = z - sign * k
            return copies.remote(piece(p), piece(p), tensor=z + sign)

        self.ups = [make(k, 1) for k in range(depth - 1)]
        self.downs = [make(k, -1) for k in range(depth - 1)]

    def sends(self, k):
        z, top = self.z, self.depth - 1
        return (
            (self.ups[k], jnp.logical_and(z < top, z >= k)),
            (self.downs[k], jnp.logical_and(z > 0, z + k <= top)),
        )

    def begin(self):
        for copy, there in self.sends(0):
            pl.when(there)(copy.start)

    def finish(self):
        for k in range(self.depth - 1):
            for copy, there in self.sends(k):
                pl.when(there)(copy.wait_send)


def peer_of(me, r):
    out, bit = me, 1
    while bit <= r:
        if r & bit:
            out = out + bit - 2 * bit * (me // bit % 2)
        bit *= 2
    return out


def greet(me, z, dp, depth):
    barrier = pltpu.get_barrier_semaphore()
    for r in range(1, dp):
        pl.semaphore_signal(barrier, inc=1, device_id={"dp": peer_of(me, r)}, device_id_type=MESH)
    for r in range(1, depth):
        pl.semaphore_signal(
            barrier, inc=1, device_id={"tensor": (z + r) % depth}, device_id_type=MESH
        )
    pl.semaphore_wait(barrier, dp - 1 + depth - 1)


def spin(field, cos_rows, sin_rows):
    return field * cos_rows + pltpu.roll(field, field.shape[-1] // 2, 1) * sin_rows


def piece_of(buffer, p, rows):
    return buffer.at[pl.ds(pl.multiple_of(p * rows, rows), rows)]


def pass_on(c, source, target, z, depth, rows, sibling, passed):
    def make(p):
        return c.remote(piece_of(source, p, rows), piece_of(target, p, rows), dp=sibling)

    ups = [make(z - k) for k in range(1, depth)]
    downs = [make(z + k) for k in range(1, depth)]
    for k in range(1, depth):
        passed.append((ups[k - 1], z >= k))
        passed.append((downs[k - 1], z + k <= depth - 1))

    def each(k, up):
        (ups if up else downs)[k - 1].start()

    return each


def line_step(line, k, each=None):
    z, top = line.z, line.depth - 1
    onward = line.sends(k) if k < top else (None, None)
    for up, copy, there, further in (
        (True, line.ups[k - 1], z >= k, onward[0]),
        (False, line.downs[k - 1], z + k <= top, onward[1]),
    ):
        pl.when(there)(copy.wait_recv)
        if further is not None:
            pl.when(further[1])(further[0].start)
        if each is not None:
            pl.when(there)(functools.partial(each, k, up))


def forward_body(
    sizes,
    codes_ref,
    misc_ref,
    gains_ref,
    cos_ref,
    sin_ref,
    tokens_ref,
    outgrad_ref,
    wq_ref,
    wk_ref,
    wv_ref,
    wo_ref,
    eg_ref,
    eu_ref,
    ed_ref,
    sg_ref,
    su_ref,
    sd_ref,
    hidden_ref,
    norm_ref,
    grads_ref,
    gateup_ref,
    down_ref,
    codes_all,
    misc_all,
    gain_rows,
    tok,
    weights,
    qkv_ref,
    probs_ref,
    mix_ref,
    fnorm,
    part,
    part_in,
    scatter_in,
    gains_all,
    zeros,
    send,
    recv,
    here,
):
    dp, depth, experts, hidden_units, head = sizes
    me, z = lax.axis_index("dp"), lax.axis_index("tensor")
    core, x = me % 2, (me // 2) % 2
    bits = [2**k for k in range(dp.bit_length() - 1)]
    rows, width = tokens_ref.shape
    seq_len = rows * depth
    slice_width = width // dp
    routed = experts // 4
    c = Copies(send, recv, here)

    def bit_of(bit):
        return (me // bit) % 2

    greet(me, z, dp, depth)

    first = []
    own_codes = c.local(codes_ref, codes_all.at[0])
    own_misc = c.local(misc_ref, misc_all.at[me])
    own_gains = c.local(gains_ref, gains_all.at[z, me])
    for copy in (own_codes, own_misc, own_gains):
        copy.start()
    for r in range(1, 4):
        first.append(c.remote(codes_ref, codes_all.at[r], dp=peer_of(me, r)))
    gain_copies = [c.remote(gains_ref, gains_all.at[z, me], dp=peer_of(me, r)) for r in range(1, dp)]
    misc_copies = [c.remote(misc_ref, misc_all.at[me], dp=peer_of(me, r)) for r in range(1, dp)]
    for copy in gain_copies + misc_copies + first:
        copy.start()

    def piece(buffer, p):
        return buffer.at[pl.ds(pl.multiple_of(p * rows, rows), rows)]

    own_tok = c.local(tokens_ref, piece(tok.at[0], z))
    own_tok.start()
    own_grad = c.local(outgrad_ref, piece(grads_ref.at[0], z))
    own_grad.start()

    def columns(k, n):
        return pl.ds(pl.multiple_of(k * n, n), n)

    pair = wq_ref.shape[1] // 2
    own_at = tuple(bit_of(bit) for bit in reversed(bits))
    core_copies = []
    for k, w in enumerate((wq_ref, wk_ref, wv_ref, wo_ref)):
        place = weights.at[own_at + (slice(None), pl.ds(k * pair, pair))]
        core_copies.append(c.remote(w.at[:, columns(1 - core, pair)], place, dp=peer_of(me, 1)))
        core_copies.append(c.local(w.at[:, columns(core, pair)], place))
    for copy in core_copies:
        copy.start()

    own_tok.wait()
    tok_line = Line(c, tok.at[0], z, depth, rows)
    tok_line.begin()
    tok_pass = [c.remote(tokens_ref, piece(tok.at[1], z), dp=peer_of(me, 1))]
    tok_pass[0].start()

    zeros[...] = jnp.zeros_like(zeros)
    pad = zeros.shape[1]
    pads = [c.local(zeros, down_ref.at[:, 0, pl.ds(hidden_units, pad)])]
    pads += [c.local(zeros, gateup_ref.at[:, k, pl.ds(hidden_units, pad)]) for k in range(2)]
    matrices = ((ed_ref, sd_ref, down_ref, 0), (eg_ref, sg_ref, gateup_ref, 0), (eu_ref, su_ref, gateup_ref, 1))
    slab = columns(me, slice_width)

    def group_copies(routed_src, shared_src, dst, k, r):
        group = (peer_of(me, r)) % 4
        many = (
            routed_src.at[pl.ds(group * routed, routed)],
            dst.at[pl.ds(0, routed), k, pl.ds(0, hidden_units), slab],
        )
        one = (shared_src.at[group], dst.at[routed, k, pl.ds(0, hidden_units), slab])
        if r == 0:
            return [c.local(*many), c.local(*one)]
        return [c.remote(*many, dp=peer_of(me, r)), c.remote(*one, dp=peer_of(me, r))]

    near = [[copy for r in (0, 1) for copy in group_copies(*m, r)] for m in matrices]
    far = [[copy for r in (2, 3) for copy in group_copies(*m, r)] for m in matrices]

    def over_copy(dst, k, far_chip):
        n = 2 * slice_width
        chip = me // 2 + far_chip * (1 - 2 * x)
        cols = pl.ds(pl.multiple_of(chip * n, n), n)
        place = dst.at[:, k, pl.ds(0, hidden_units), cols]
        return c.remote(place, place, dp=peer_of(me, 4))

    over_near = [over_copy(m[2], m[3], 0) for m in matrices]
    over = [over_copy(m[2], m[3], 1) for m in matrices]

    for copy in core_copies:
        copy.wait()

    def weight_copies(order, half):
        have, copies = [1], []
        for bit in order:
            index = tuple(
                pl.ds(0, 2) if b in have else pl.ds(bit_of(b), 1) for b in reversed(bits)
            )
            place = weights.at[index + (slice(None), pl.ds(half * 2 * pair, 2 * pair))]
            copies.append(c.remote(place, place, dp=peer_of(me, bit)))
            have.append(bit)
        return copies

    qk_copies = weight_copies(bits[1:], 0)
    vo_copies = weight_copies(bits[:0:-1], 1)
    qk_copies[0].start()
    vo_copies[0].start()
    for copy in pads + [copy for m in near for copy in m]:
        copy.start()

    own_gains.wait()
    for copy in gain_copies:
        copy.wait_recv()
    gain_spread = [
        c.remote(gains_all.at[z], gains_all.at[z], tensor=(z + r) % depth) for r in range(1, depth)
    ]
    for copy in gain_spread:
        copy.start()

    tok_passed = []
    sibling = peer_of(me, 1)
    pass_tok = pass_on(c, tok.at[0], tok.at[1], z, depth, rows, sibling, tok_passed)

    line_step(tok_line, 1, pass_tok)
    for k in range(1, len(bits) - 1):
        qk_copies[k - 1].wait_recv()
        qk_copies[k].start()
        vo_copies[k - 1].wait_recv()
        vo_copies[k].start()
    for m in far:
        for copy in m:
            copy.start()
    for m, copy in zip(near, over_near):
        for part_copy in m:
            part_copy.wait()
        copy.start()
    own_grad.wait()
    grad_line = Line(c, grads_ref.at[0], z, depth, rows)
    for k in range(2, depth):
        line_step(tok_line, k, pass_tok)
    grad_line.begin()

    for copy in gain_spread:
        copy.wait_recv()
    for d in range(dp):
        total = gains_all[0, d]
        for t in range(1, depth):
            total = total + gains_all[t, d]
        gain_rows[:, d * slice_width : (d + 1) * slice_width] = total

    def norm_rows(s):
        def block(i, carry):
            at = pl.ds(pl.multiple_of(i * rows, rows), rows)
            data = tok[s, at, :].astype(F32)
            scale = lax.rsqrt(jnp.mean(data * data, axis=-1, keepdims=True) + EPS)
            fnorm[at, :] = (data * scale * gain_rows[0:1, :]).astype(BF)
            return carry

        lax.fori_loop(0, depth, block, 0)

    own_misc.wait()
    for copy in misc_copies:
        copy.wait_recv()
    bias_in = jnp.zeros(misc_ref.shape, F32)
    sub = lax.broadcasted_iota(jnp.int32, misc_ref.shape, 0)
    for d in range(dp):
        bias_in = jnp.where(sub == d, misc_all[d, pl.ds(experts + 1 + core, 1), :], bias_in)
    bias_in = bias_in.astype(BF)
    heads3 = 3 * pair
    head_slice = head // dp
    lane = lax.broadcasted_iota(jnp.int32, (bias_in.shape[1], heads3), 1)
    sub = lax.broadcasted_iota(jnp.int32, (bias_in.shape[1], heads3), 0)
    place = (lane // head * head_slice + lane % head_slice == sub).astype(F32).astype(BF)
    spread = dot(bias_in, place)
    lane = lax.broadcasted_iota(jnp.int32, spread.shape, 1)
    sub = lax.broadcasted_iota(jnp.int32, spread.shape, 0)
    bias = jnp.sum(jnp.where(lane % head // head_slice == sub, spread, 0.0), axis=0, keepdims=True)

    qk_copies[-1].wait_recv()
    vo_copies[-1].wait_recv()
    pairs = pair // head

    def project(s):
        def block(i, carry):
            at = pl.ds(pl.multiple_of(i * 2 * rows, 2 * rows), 2 * rows)
            full = weights[...].reshape(width, 4 * pair)
            pre = dot(fnorm[at, :], full[:, : 3 * pair]) + bias
            cos_rows, sin_rows = cos_ref[at, :], sin_ref[at, :]
            for kind in range(3):
                for h in range(pairs):
                    a = (kind * pairs + h) * head
                    field = pre[:, a : a + head]
                    if kind < 2:
                        field = spin(field, cos_rows, sin_rows)
                    qkv_ref[kind, s * pairs + h, at, :] = field.astype(BF)
            return carry

        lax.fori_loop(0, depth // 2, block, 0)

    norm_rows(0)
    project(0)
    line_step(grad_line, 1)
    for copy in far[0]:
        copy.wait_recv()
    over[0].start()
    tok_pass[0].wait()
    for copy, there in tok_passed:
        pl.when(there)(copy.wait)
    norm_rows(1)
    project(1)

    own_codes.wait()
    for copy in first:
        copy.wait()
    causal_block = seq_len // 2

    def attend(s):
        flags = codes_all[s]
        sub = lax.broadcasted_iota(jnp.int32, flags.shape, 0)
        flags = jnp.where(sub == 8, flags, 0).astype(F32).astype(BF)
        for h in range(pairs):
            for b in range(2):
                at = slice(b * causal_block, (b + 1) * causal_block)
                seen = dot(flags[:, at], flags, 0, 0)
                row = lax.broadcasted_iota(jnp.int32, seen.shape, 0) + b * causal_block
                col = lax.broadcasted_iota(jnp.int32, seen.shape, 1)
                scores = dot(qkv_ref[0, s * pairs + h, at, :], qkv_ref[1, s * pairs + h], 1, 1)
                scores = scores * head ** (-0.5)
                scores = jnp.where(jnp.logical_or(col <= row, seen > 0.5), scores, -1e30)
                raised = jnp.exp(scores - jnp.max(scores, axis=1, keepdims=True))
                probs = raised / jnp.sum(raised, axis=1, keepdims=True)
                probs = probs.astype(BF)
                probs_ref[s * pairs + h, at, :] = probs
                mixed = dot(probs, qkv_ref[2, s * pairs + h])
                mix_ref[s, at, h * head : (h + 1) * head] = mixed.astype(BF)

    def project_out(s):
        for d in range(dp):
            index = tuple(d // bit % 2 for bit in reversed(bits))
            block = weights[index + (slice(None), slice(3 * pair, 4 * pair))]
            at = slice(d * slice_width, (d + 1) * slice_width)
            part[s, :, at] = dot(mix_ref[s], block, 1, 1).astype(BF)

    attend(1)
    if depth > 2:
        line_step(grad_line, 2)
    project_out(1)
    part_pass = c.remote(part.at[1], part_in, dp=peer_of(me, 1))
    part_pass.start()
    attend(0)
    project_out(0)
    part_pass.wait_recv()

    scatter = []
    for r in list(range(1, depth)) + [0]:
        at = pl.ds(pl.multiple_of((z + r) % depth * rows, rows), rows)
        total = part[0, at, :].astype(F32) + part_in[at, :].astype(F32)
        if r:
            part[0, at, :] = total.astype(BF)
            copy = c.remote(part.at[0, at], scatter_in.at[r - 1], tensor=(z + r) % depth)
            copy.start()
            scatter.append(copy)
        else:
            hidden_ref[...] = total + tok[0, at, :].astype(F32)

    for k in range(3, depth):
        line_step(grad_line, k)
    x_grad = c.remote(grads_ref.at[0], grads_ref.at[2], dp=peer_of(me, 2))
    x_grad.start()
    own_pass = c.remote(grads_ref.at[0], grads_ref.at[1], dp=peer_of(me, 1))
    own_pass.start()
    for k in (1, 2):
        for copy in far[k]:
            copy.wait_recv()
        over[k].start()

    for copy in scatter:
        copy.wait_recv()
    total = hidden_ref[...]
    for r in range(1, depth):
        total = total + scatter_in[r - 1].astype(F32)
    hidden_ref[...] = total
    scale = lax.rsqrt(jnp.mean(total * total, axis=-1, keepdims=True) + EPS)
    norm_ref[0, pl.ds(pl.multiple_of(z * rows, rows), rows), :] = (
        total * scale * gain_rows[1:2, :]
    ).astype(BF)
    norm_line = Line(c, norm_ref.at[0], z, depth, rows)
    norm_line.begin()
    beside = peer_of(me, 2)
    norm_own = c.remote(piece(norm_ref.at[0], z), piece(norm_ref.at[1], z), dp=sibling)
    norm_far = c.remote(piece(norm_ref.at[0], z), piece(norm_ref.at[2], z), dp=beside)
    norm_far.start()
    norm_own.start()
    norm_passed, far_passed = [], []
    pass_norm = pass_on(
        c, norm_ref.at[0], norm_ref.at[1], z, depth, rows, sibling, norm_passed
    )
    pass_far = pass_on(c, norm_ref.at[0], norm_ref.at[2], z, depth, rows, beside, far_passed)

    def pass_both(k, up):
        pass_far(k, up)
        pass_norm(k, up)

    for k in range(1, depth):
        line_step(norm_line, k, pass_both)

    x_grad.wait_recv()
    grad_pass = c.remote(grads_ref.at[2], grads_ref.at[3], dp=peer_of(me, 1))
    grad_pass.start()
    for copy in over_near + over:
        copy.wait()
    norm_far.wait()
    for copy, there in far_passed:
        pl.when(there)(copy.wait)
    norm_pass = c.remote(norm_ref.at[2], norm_ref.at[3], dp=sibling)
    norm_pass.start()
    norm_own.wait()
    for copy, there in norm_passed:
        pl.when(there)(copy.wait)
    norm_pass.wait()
    own_pass.wait()
    grad_pass.wait()
    for line in (tok_line, grad_line, norm_line):
        line.finish()
    for copy in pads:
        copy.wait()
    for copy in gain_copies + misc_copies + gain_spread + qk_copies + vo_copies + scatter:
        copy.wait_send()
    for copy in [part_pass, x_grad] + [y for m in far for y in m]:
        copy.wait_send()


def forward_call(dp, depth, experts, head, small, arrays, units):
    codes, misc, gains, cos_rows, sin_rows = small
    tokens, pair = arrays[0], arrays[2].shape[1] // 2
    rows, width = tokens.shape
    seq_len = rows * depth
    hidden_units = units[0].shape[1]
    hidden_pad = -(-hidden_units // 128) * 128
    routed = experts // 4
    bits = dp.bit_length() - 1
    pairs = pair // head
    vmem, hbm = pl.BlockSpec(memory_space=pltpu.VMEM), pl.BlockSpec(memory_space=pl.ANY)
    shape = jax.ShapeDtypeStruct
    return pl.pallas_call(
        functools.partial(forward_body, (dp, depth, experts, hidden_units, head)),
        in_specs=[vmem] * 5 + [hbm] * 12,
        out_specs=[vmem, vmem, hbm, hbm, hbm] + [vmem] * 8,
        out_shape=[
            shape((rows, width), F32),
            shape((4, seq_len, width), BF),
            shape((4, seq_len, width), BF),
            shape((routed + 1, 2, hidden_pad, width), BF),
            shape((routed + 1, 1, hidden_pad, width), BF),
            shape((4,) + codes.shape, codes.dtype),
            shape((dp,) + misc.shape, F32),
            shape((8, width), F32),
            shape((2, seq_len, width), BF),
            shape((2,) * bits + (width // dp, 4 * pair), BF),
            shape((3, 2 * pairs, seq_len, head), BF),
            shape((2 * pairs, seq_len, seq_len), BF),
            shape((2, seq_len, pair), BF),
        ],
        scratch_shapes=[
            pltpu.VMEM((seq_len, width), BF),
            pltpu.VMEM((2, seq_len, width), BF),
            pltpu.VMEM((seq_len, width), BF),
            pltpu.VMEM((depth - 1, rows, width), BF),
            pltpu.VMEM((depth, dp) + gains.shape, F32),
            pltpu.VMEM((routed + 1, hidden_pad - hidden_units, width), BF),
            pltpu.SemaphoreType.DMA((160,)),
            pltpu.SemaphoreType.DMA((160,)),
            pltpu.SemaphoreType.DMA((32,)),
        ],
        compiler_params=pltpu.CompilerParams(
            collective_id=0, has_side_effects=True, vmem_limit_bytes=VMEM_LIMIT
        ),
    )(codes, misc, gains, cos_rows, sin_rows, *arrays, *units)


def backward_body(
    sizes,
    terms_ref,
    probs_mine_ref,
    router_ref,
    gain_rows,
    cos_ref,
    sin_ref,
    hidden_ref,
    outgrad_ref,
    grad_a_ref,
    grad_b_ref,
    grad_c_ref,
    gate_in_ref,
    gate_ref,
    up_ref,
    down_ref,
    tok_hbm,
    weights_hbm,
    qkv_hbm,
    probs_hbm,
    mix_hbm,
    norm_hbm,
    input_ref,
    gate_out,
    up_out,
    down_out,
    attn_out,
    misc_out,
    gains_out,
    own_sum,
    arrived,
    three,
    scatter_in,
    terms_sum,
    terms_in,
    back,
    tok,
    weights,
    qkv,
    probs_ref,
    mix_ref,
    scales,
    qkv_grad,
    part_in,
    keep,
    total_a,
    first_qk,
    first_vo,
    second_in,
    misc_part,
    misc_in,
    gains_in,
    vectors,
    send,
    recv,
    here,
):
    dp, depth, experts, head = sizes
    me, z = lax.axis_index("dp"), lax.axis_index("tensor")
    core, x, y = me % 2, (me // 2) % 2, me // 4
    rows, width = input_ref.shape
    seq_len = rows * depth
    slice_width = width // dp
    pair = mix_ref.shape[2]
    pairs = pair // head
    bits = [1, 2, 4]
    c = Copies(send, recv, here)

    greet(me, z, dp, depth)

    matrices = ((gate_ref, gate_out), (up_ref, up_out), (down_ref, down_out))
    over = [None]
    for m in (1, 2):
        other = matrices[m][0].at[pl.ds((1 - y) * 4, 4)]
        over.append(c.remote(other, arrived.at[m], dp=peer_of(me, 4)))
        over[m].start()
    gate_in = c.local(gate_in_ref, arrived.at[0])
    grads = (grad_a_ref, grad_b_ref, grad_c_ref)
    loads = [c.local(grads[k], three.at[k]) for k in range(3)]
    for copy in loads:
        copy.start()
    own_loads = [
        c.local(source.at[pl.ds(y * 4, 4)], own_sum) for source, _ in matrices
    ]
    inputs = [
        c.local(a, b)
        for a, b in (
            (weights_hbm, weights),
            (mix_hbm, mix_ref),
            (qkv_hbm, qkv),
            (probs_hbm, probs_ref),
            (tok_hbm, tok),
        )
    ]
    own_loads[0].start()
    gate_in.start()
    for copy in inputs:
        copy.start()

    def at_of(p):
        return pl.ds(pl.multiple_of(p * rows, rows), rows)

    for copy in loads:
        copy.wait()
    scatter, small = [], []
    for r in list(range(1, depth)) + [0]:
        at = at_of((z + r) % depth)
        total = three[0, at, :].astype(F32) + three[1, at, :].astype(F32)
        total = total + three[2, at, :].astype(F32)
        extra = terms_ref[0, at, :] + terms_ref[1, at, :] + terms_ref[2, at, :]
        if r:
            three[0, at, :] = total.astype(BF)
            terms_sum[at, :] = extra
            peer = (z + r) % depth
            scatter.append(c.remote(three.at[0, at], scatter_in.at[0, r - 1], tensor=peer))
            small.append(c.remote(terms_sum.at[at], terms_in.at[r - 1], tensor=peer))
            scatter[-1].start()
            small[-1].start()
        else:
            keep[0] = total
            terms_sum[at, :] = extra

    def add_over(m):
        own_loads[m].wait()
        if m:
            over[m].wait_recv()
        else:
            gate_in.wait()
        copies = []
        for r in (2, 3, 1, 0):
            k = peer_of(me, r) % 4
            for unit in range(own_sum.shape[1]):
                arrived[m, k, unit] = (
                    own_sum[k, unit].astype(F32) + arrived[m, k, unit].astype(F32)
                ).astype(BF)
            place = matrices[m][1].at[me % 4]
            if r:
                copies.append(c.remote(arrived.at[m, k], place, dp=peer_of(me, r)))
            else:
                copies.append(c.local(arrived.at[m, k], place))
            copies[-1].start()
        if m + 1 < len(own_loads):
            own_loads[m + 1].start()
        return copies

    units = add_over(0)
    for copy in scatter:
        copy.wait_recv()
    for copy in small:
        copy.wait_recv()
    route = terms_sum[at_of(z), :]
    grad = keep[0]
    for r in range(1, depth):
        grad = grad + scatter_in[0, r - 1].astype(F32)
        route = route + terms_in[r - 1]
    probs_mine = probs_mine_ref[...]
    lane = lax.broadcasted_iota(jnp.int32, route.shape, 1)
    inner = jnp.sum(jnp.where(lane < experts, probs_mine * route, 0.0), axis=1, keepdims=True)
    logits = jnp.where(
        lane < experts,
        probs_mine * (route - inner),
        jnp.where(lane == experts, route * probs_mine * (1.0 - probs_mine), 0.0),
    ).astype(BF)
    grad = grad + dot(logits, router_ref[...])
    hidden = hidden_ref[...]
    scale = lax.rsqrt(jnp.mean(hidden * hidden, axis=-1, keepdims=True) + EPS)
    unit = hidden * scale
    vectors[1:2, :] = jnp.sum(grad * unit, axis=0, keepdims=True)
    grad = grad * gain_rows[1:2, :]
    grad = outgrad_ref[...].astype(F32) + scale * (
        grad - unit * jnp.mean(grad * unit, axis=-1, keepdims=True)
    )
    keep[0] = grad
    back[0, at_of(z), :width] = grad.astype(BF)
    back[0, at_of(z), width:] = logits

    line = Line(c, back.at[0], z, depth, rows)
    line.begin()
    sibling = peer_of(me, 1)
    back_own = c.remote(piece_of(back.at[0], z, rows), piece_of(back.at[1], z, rows), dp=sibling)
    back_own.start()
    passed = []
    pass_back = pass_on(c, back.at[0], back.at[1], z, depth, rows, sibling, passed)
    for copy in scatter:
        copy.wait_send()
    line_step(line, 1, pass_back)

    for copy in inputs:
        copy.wait()

    def scale_rows(i, carry):
        at = at_of(i)
        for s in range(2):
            data = tok[s, at, :].astype(F32)
            scales[s, at, :] = lax.rsqrt(jnp.mean(data * data, axis=-1, keepdims=True) + EPS)
        return carry

    lax.fori_loop(0, depth, scale_rows, 0)
    line_step(line, 2, pass_back)
    units += add_over(1)
    line_step(line, 3, pass_back)
    back_own.wait()
    for copy, there in passed:
        pl.when(there)(copy.wait)
    def block_of(d):
        return tuple(d // bit % 2 for bit in reversed(bits))

    def slab(d):
        return slice(d * slice_width, (d + 1) * slice_width)

    def attention(s):
        mixed = jnp.zeros((seq_len, pair), F32)
        for d in range(dp):
            block = weights[block_of(d) + (slice(None), slice(3 * pair, 4 * pair))]
            mixed = mixed + dot(back[s, :, slab(d)], block)
        mixed = mixed.astype(BF)
        for h in range(pairs):
            n = s * pairs + h
            cot = mixed[:, h * head : (h + 1) * head]
            key_total = jnp.zeros((seq_len, head), F32)
            value_total = jnp.zeros((seq_len, head), F32)
            for b in range(2):
                at = slice(b * seq_len // 2, (b + 1) * seq_len // 2)
                p_low = probs_ref[n, at, :]
                p = p_low.astype(F32)
                p_grad = dot(cot[at], qkv[2, n], 1, 1)
                s_grad = p * (p_grad - jnp.sum(p * p_grad, axis=1, keepdims=True))
                s_grad = s_grad.astype(BF)
                q_grad = dot(s_grad, qkv[1, n]) * head ** (-0.5)
                q_grad = spin(q_grad, cos_ref[at, :], -sin_ref[at, :])
                qkv_grad[s, at, h * head : (h + 1) * head] = q_grad.astype(BF)
                key_total = key_total + dot(s_grad, qkv[0, n, at, :], 0, 0)
                value_total = value_total + dot(p_low, cot[at], 0, 0)
            k_grad = spin(key_total * head ** (-0.5), cos_ref[...], -sin_ref[...])
            a = pair + h * head
            qkv_grad[s, :, a : a + head] = k_grad.astype(BF)
            qkv_grad[s, :, a + pair : a + pair + head] = value_total.astype(BF)

    def first_grad(s):
        for d in range(dp):
            block = weights[block_of(d) + (slice(None), slice(0, 3 * pair))]
            total = dot(qkv_grad[s], block, 1, 1)
            three[1 + s, :, slab(d)] = total.astype(BF)
            unit_block = tok[s, :, slab(d)].astype(F32) * scales[s]
            row = jnp.sum(total * unit_block, axis=0, keepdims=True)
            vectors[2 + s : 3 + s, slab(d)] = row

    attention(1)
    first_grad(1)
    part_pass = c.remote(three.at[2], part_in, dp=sibling)
    part_pass.start()
    units += add_over(2)
    attention(0)
    first_grad(0)
    part_pass.wait_recv()
    first_scatter = []
    for r in list(range(1, depth)) + [0]:
        at = at_of((z + r) % depth)
        total = three[1, at, :].astype(F32) + part_in[at, :].astype(F32)
        if r:
            three[1, at, :] = total.astype(BF)
            peer = (z + r) % depth
            copy = c.remote(three.at[1, at], scatter_in.at[1, r - 1], tensor=peer)
            copy.start()
            first_scatter.append(copy)
        else:
            keep[1] = total

    for d in range(dp):
        total = jnp.zeros((slice_width, 3 * pair), F32)
        out_total = jnp.zeros((slice_width, pair), F32)
        for s in range(2):
            data = tok[s, :, slab(d)].astype(F32) * scales[s] * gain_rows[0:1, slab(d)]
            total = total + dot(data.astype(BF), qkv_grad[s], 0, 0)
            out_total = out_total + dot(back[s, :, slab(d)], mix_ref[s], 0, 0)
        total_a[block_of(d) + (slice(None), slice(0, 3 * pair))] = total.astype(BF)
        total_a[block_of(d) + (slice(None), slice(3 * pair, 4 * pair))] = out_total.astype(BF)

    half = 2 * pair

    def index(y_at, x_at, k):
        return (y_at, x_at, slice(None), slice(None), pl.ds(k * half, half))

    every = pl.ds(0, 2)
    qk_first = c.remote(
        total_a.at[index(pl.ds(1 - y, 1), every, 0)], first_qk, dp=peer_of(me, 4)
    )
    vo_first = c.remote(
        total_a.at[index(every, pl.ds(1 - x, 1), 1)], first_vo, dp=peer_of(me, 2)
    )
    qk_first.start()
    vo_first.start()

    norm_load = c.local(norm_hbm.at[0], three.at[0])
    norm_load.start()
    norm_load.wait()
    router_part = dot(back[0, :, width:], three[0], 0, 0)
    ones = jnp.ones((16, seq_len), BF)
    bias_row = dot(ones, qkv_grad[0]) + dot(ones, qkv_grad[1])
    lane = lax.broadcasted_iota(jnp.int32, bias_row.shape, 1)
    sub = lax.broadcasted_iota(jnp.int32, bias_row.shape, 0)
    head_slice = head // dp
    bias_rows = jnp.where(lane % head // head_slice == sub, bias_row, 0.0)
    high = bias_rows.astype(BF)
    low = (bias_rows - high.astype(F32)).astype(BF)
    lane = lax.broadcasted_iota(jnp.int32, (3 * pair, slice_width), 1)
    sub = lax.broadcasted_iota(jnp.int32, (3 * pair, slice_width), 0)
    place = (sub // head * head_slice + sub % head_slice == lane).astype(F32).astype(BF)
    bias_rows = dot(high, place) + dot(low, place)
    sub = lax.broadcasted_iota(jnp.int32, (16, slice_width), 0)
    misc_copies = []
    for d in range(dp):
        tile = jnp.where(sub <= experts, router_part[:16, slab(d)], 0.0)
        tile = jnp.where(sub == experts + 1 + core, bias_rows[d : d + 1], tile)
        gain_one = vectors[2:3, slab(d)] + vectors[3:4, slab(d)]
        tile = jnp.where(sub == experts + 3, gain_one, tile)
        tile = jnp.where(sub == experts + 4, vectors[1:2, slab(d)], tile)
        misc_part[d] = tile
    for r in range(1, dp):
        to = peer_of(me, r)
        misc_copies.append(c.remote(misc_part.at[to], misc_in.at[r - 1], dp=to))
        misc_copies[-1].start()

    qk_first.wait()
    mine = index(pl.ds(y, 1), every, 0)
    total_a[mine] = (total_a[mine].astype(F32) + first_qk[...].astype(F32)).astype(BF)
    qk_second = c.remote(
        total_a.at[index(pl.ds(y, 1), pl.ds(1 - x, 1), 0)], second_in.at[0], dp=peer_of(me, 2)
    )
    qk_second.start()
    vo_first.wait()
    mine = index(every, pl.ds(x, 1), 1)
    total_a[mine] = (total_a[mine].astype(F32) + first_vo[...].astype(F32)).astype(BF)
    vo_second = c.remote(
        total_a.at[index(pl.ds(1 - y, 1), pl.ds(x, 1), 1)], second_in.at[1], dp=peer_of(me, 4)
    )
    vo_second.start()

    total = misc_part[me]
    for r, copy in enumerate(misc_copies):
        copy.wait_recv()
        total = total + misc_in[r]
    misc_out[...] = total
    gain_copies = []
    for r in range(1, depth):
        peer = (z + r) % depth
        gain_copies.append(c.remote(misc_out.at[8:16], gains_in.at[r - 1], tensor=peer))
        gain_copies[-1].start()

    finals = []
    for k, copy in enumerate((qk_second, vo_second)):
        copy.wait()
        mine = (y, x, slice(None), slice(None), pl.ds(k * half, half))
        total_a[mine] = (
            total_a[mine].astype(F32) + second_in[k, 0, 0].astype(F32)
        ).astype(BF)
        for other in (True, False):
            to = 1 - core if other else core
            source = total_a.at[y, x, to, :, pl.ds(k * half, half)]
            place = attn_out.at[core, :, pl.ds(k * half, half)]
            finals.append(c.remote(source, place, dp=sibling) if other else c.local(source, place))
            finals[-1].start()

    for copy in first_scatter:
        copy.wait_recv()
    total = keep[1]
    for r in range(1, depth):
        total = total + scatter_in[1, r - 1].astype(F32)
    total = total * gain_rows[0:1, :]
    scale = scales[0, at_of(z), :]
    unit = tok[0, at_of(z), :].astype(F32) * scale
    total = keep[0] + scale * (total - unit * jnp.mean(total * unit, axis=-1, keepdims=True))
    input_ref[...] = total.astype(BF)

    total = misc_out[8:16, :]
    for r, copy in enumerate(gain_copies):
        copy.wait()
        total = total + gains_in[r]
    gains_out[...] = total
    for copy in finals + units:
        copy.wait()
    line.finish()
    for copy in over[1:] + small + first_scatter + misc_copies + [part_pass]:
        copy.wait_send()


def backward_call(dp, depth, experts, head, in_vmem, in_hbm):
    output_rows, width = in_vmem[6].shape
    seq_len = output_rows * depth
    slice_width = width // dp
    units = in_hbm[3].shape[1:]
    pair = in_hbm[11].shape[2]
    pairs = pair // head
    vmem, hbm = pl.BlockSpec(memory_space=pltpu.VMEM), pl.BlockSpec(memory_space=pl.ANY)
    shape = jax.ShapeDtypeStruct
    final = shape((4,) + units, BF)
    return pl.pallas_call(
        functools.partial(backward_body, (dp, depth, experts, head)),
        in_specs=[vmem] * len(in_vmem) + [hbm] * len(in_hbm),
        out_specs=[vmem, hbm, hbm, hbm, vmem, vmem, vmem],
        out_shape=[
            shape((output_rows, width), BF),
            final,
            final,
            final,
            shape((2, slice_width, 4 * pair), BF),
            shape((16, slice_width), F32),
            shape((8, slice_width), F32),
        ],
        scratch_shapes=[
            pltpu.VMEM((4,) + units, BF),
            pltpu.VMEM((3, 4) + units, BF),
            pltpu.VMEM((3, seq_len, width), BF),
            pltpu.VMEM((2, depth - 1, output_rows, width), BF),
            pltpu.VMEM((seq_len, 128), F32),
            pltpu.VMEM((depth - 1, output_rows, 128), F32),
            pltpu.VMEM((2, seq_len, width + 128), BF),
            pltpu.VMEM((2, seq_len, width), BF),
            pltpu.VMEM((2, 2, 2, slice_width, 4 * pair), BF),
            pltpu.VMEM((3, 2 * pairs, seq_len, head), BF),
            pltpu.VMEM((2 * pairs, seq_len, seq_len), BF),
            pltpu.VMEM((2, seq_len, pair), BF),
            pltpu.VMEM((2, seq_len, 1), F32),
            pltpu.VMEM((2, seq_len, 3 * pair), BF),
            pltpu.VMEM((seq_len, width), BF),
            pltpu.VMEM((2, output_rows, width), F32),
            pltpu.VMEM((2, 2, 2, slice_width, 4 * pair), BF),
            pltpu.VMEM((1, 2, 2, slice_width, 2 * pair), BF),
            pltpu.VMEM((2, 1, 2, slice_width, 2 * pair), BF),
            pltpu.VMEM((2, 1, 1, 2, slice_width, 2 * pair), BF),
            pltpu.VMEM((dp, 16, slice_width), F32),
            pltpu.VMEM((dp - 1, 16, slice_width), F32),
            pltpu.VMEM((depth - 1, 8, slice_width), F32),
            pltpu.VMEM((8, width), F32),
            pltpu.SemaphoreType.DMA((96,)),
            pltpu.SemaphoreType.DMA((96,)),
            pltpu.SemaphoreType.DMA((40,)),
        ],
        compiler_params=pltpu.CompilerParams(
            collective_id=1, has_side_effects=True, vmem_limit_bytes=62 * 2**20
        ),
    )(*in_vmem, *in_hbm)


def local_plain(
    dp,
    tokens,
    picture_ids,
    routes,
    slot_order,
    norm_gains,
    w_query,
    w_key,
    w_value,
    w_out,
    qkv_bias,
    router,
    shared_gate,
    shared_up,
    shared_down,
    expert_gate,
    expert_up,
    expert_down,
    out_grad,
):
    seq_len = picture_ids.shape[0]
    local_rows = tokens.shape[0]
    width = tokens.shape[1]
    experts, slice_width, hidden_units = expert_gate.shape
    top_count = routes.shape[1]
    capacity = 5 * seq_len * top_count // (4 * experts)
    heads_local = qkv_bias.shape[1]
    head_width = w_query.shape[1] // heads_local
    pair_heads = heads_local // 2
    pair_width = pair_heads * head_width
    mine_experts = experts // 4
    hidden_pad = -(-hidden_units // 128) * 128

    me = lax.axis_index("dp")
    zi = lax.axis_index("tensor")
    core, xi = me % 2, (me // 2) % 2
    group = me % 4
    bits = []
    while 2 ** (len(bits) + 1) <= dp:
        bits.append(2 ** len(bits))
    upper = bits[2:]

    def swap(array, bit):
        return lax.ppermute(array, "dp", [(i, i ^ bit) for i in range(dp)])

    def bit_of(bit):
        return (me // bit) % 2

    def join(mine, theirs, bit, axis):
        n = mine.shape[axis]
        shape = list(mine.shape)
        shape[axis] = 2 * n
        out = jnp.zeros(shape, mine.dtype)
        out = lax.dynamic_update_slice_in_dim(out, mine, n * bit_of(bit), axis)
        return lax.dynamic_update_slice_in_dim(out, theirs, n * (1 - bit_of(bit)), axis)

    def half(array, which, axis):
        n = array.shape[axis] // 2
        return lax.dynamic_slice_in_dim(array, which * n, n, axis)

    gains_z = lax.all_gather(norm_gains, "tensor", axis=1, tiled=True)
    misc_rows = 16
    bias_width = 3 * pair_heads * qkv_bias.shape[2]
    bias_cores = qkv_bias.reshape(3, 2, -1).swapaxes(0, 1).reshape(2, bias_width)

    def misc_pack(core_bias):
        wide = jnp.zeros((misc_rows, 2 * pair_width), BF)
        wide = wide.at[: experts + 1, :slice_width].set(router.T)
        wide = wide.at[experts + 1, :bias_width].set(core_bias)
        return wide.at[experts + 2 : experts + 4, :slice_width].set(gains_z)

    qk = jnp.concatenate(
        [w.reshape(slice_width, 2, pair_width) for w in (w_query, w_key)], axis=2
    )
    qk = jnp.concatenate(
        [qk, jnp.stack([misc_pack(bias_cores[0]), misc_pack(bias_cores[1])], axis=1)], axis=0
    )
    vo = jnp.concatenate(
        [w.reshape(slice_width, 2, pair_width) for w in (w_value, w_out.T)], axis=2
    )
    tokens_z = lax.all_gather(tokens, "tensor", axis=0, tiled=True)

    def gather_attention(pack, order):
        dims = (1,) * len(bits[1:])
        both = join(pick(pack, core, 1)[None], swap(pick(pack, 1 - core, 1), 1)[None], 1, 0)
        both = both.reshape(dims + both.shape)
        for bit in order:
            axis = len(bits) - 1 - bits.index(bit)
            both = join(both, swap(both, bit), bit, axis)
        return both.reshape((dp,) + both.shape[-2:])

    qk_all = gather_attention(qk, bits[1:])
    vo_full = gather_attention(vo, bits[:0:-1]).reshape(width, 2 * pair_width)
    qk_full = qk_all[:, :slice_width].reshape(width, 2 * pair_width)
    misc = qk_all[:, slice_width:]
    router_full = misc[:, : experts + 1, :slice_width].swapaxes(1, 2).reshape(width, -1)
    gain_rows = misc[:, experts + 2 : experts + 4, :slice_width].swapaxes(0, 1)
    gain_rows = gain_rows.reshape(2, width).astype(F32)
    bias = misc[:, experts + 1, :bias_width].astype(F32)
    bias = bias.reshape(dp, 3 * pair_heads, -1).swapaxes(0, 1).reshape(3, pair_width)

    tokens_sib = swap(tokens_z, 1)
    grad_z = lax.all_gather(out_grad, "tensor", axis=0, tiled=True)

    codes = jnp.concatenate([routes, slot_order], axis=1).T
    codes_x = swap(codes, 2)
    both_codes = swap(jnp.stack([codes, codes_x]), 1)
    codes_a = jnp.stack([codes, both_codes[0]])
    codes_b = jnp.stack([codes_x, both_codes[1]])
    pictures = jnp.stack([picture_ids, swap(picture_ids, 1)])

    def core_units(routed, shared):
        routed = routed.reshape(2, 2, mine_experts, hidden_units, slice_width)
        shared = shared.reshape(2, 2, 1, hidden_units, slice_width)

        def cut(which):
            return jnp.concatenate([pick(routed, which, 1), pick(shared, which, 1)], axis=1)

        return join(cut(core), swap(cut(1 - core), 1), 1, 3)

    def x_units(held):
        return join(pick(held, xi, 0), swap(pick(held, 1 - xi, 0), 2), 2, 2)

    def upper_units(held):
        for bit in upper[:-1]:
            held = join(held, swap(held, bit), bit, 2)
        return held, swap(held, upper[-1])

    def padded(*pairs):
        n = pairs[0][0].shape[-1]
        out = jnp.zeros((mine_experts + 1, len(pairs) * hidden_pad, 2 * n), BF)
        zero = jnp.int32(0)
        for k, (mine, theirs) in enumerate(pairs):
            row = jnp.int32(k * hidden_pad)
            out = lax.dynamic_update_slice(out, mine, (zero, row, n * bit_of(upper[-1])))
            out = lax.dynamic_update_slice(out, theirs, (zero, row, n * (1 - bit_of(upper[-1]))))
        return out

    down_c = core_units(expert_down, shared_down)
    gate_c = core_units(expert_gate.swapaxes(1, 2), shared_gate.T)
    up_c = core_units(expert_up.swapaxes(1, 2), shared_up.T)
    down_x = x_units(down_c)
    gate_x = x_units(gate_c)
    up_x = x_units(up_c)
    grad_x = swap(after(grad_z, up_x), 2)
    down_y = upper_units(down_x)
    gate_y = upper_units(gate_x)
    up_y = upper_units(up_x)

    rows_f = jnp.stack([tokens_z, tokens_sib]).astype(F32)
    qk_full = after(qk_full, down_c, gate_c, up_c)
    first_scale = lax.rsqrt(jnp.mean(rows_f * rows_f, axis=-1, keepdims=True) + EPS)
    first_norm = (rows_f * first_scale * gain_rows[0]).astype(BF)
    qk_pre = einsum("std,df->stf", first_norm, qk_full) + jnp.concatenate([bias[0], bias[1]])
    values = (einsum("std,df->stf", first_norm, vo_full[:, :pair_width]) + bias[2]).astype(BF)
    cos_part, sin_part = rope_tables(seq_len, head_width)
    qk_rot = rotate(
        qk_pre.reshape(2, seq_len, 2 * pair_heads, head_width), cos_part, sin_part
    ).astype(BF)
    qk_rot = after(qk_rot, down_x)
    queries, keys = qk_rot[:, :, :pair_heads], qk_rot[:, :, pair_heads:]
    values = values.reshape(2, seq_len, pair_heads, head_width)
    positions = jnp.arange(seq_len, dtype=jnp.int32)
    allowed = jnp.logical_or(
        positions[None, None, :] <= positions[None, :, None],
        pictures[:, :, None] * pictures[:, None, :] > 0,
    )
    score_scale = head_width ** (-0.5)
    scores = einsum("sqhd,skhd->shqk", queries, keys) * score_scale
    scores = jnp.where(allowed[:, None], scores, -1e30)
    weights = jnp.exp(scores - jnp.max(scores, axis=-1, keepdims=True))
    probs = weights / jnp.sum(weights, axis=-1, keepdims=True)
    probs_low = probs.astype(BF)
    head_mix = einsum("shqk,skhd->sqhd", probs_low, values).astype(BF)
    heads_out = after(head_mix.reshape(2, seq_len, pair_width), gate_x)
    out_weight = vo_full[:, pair_width:]
    attn_part = einsum("sqf,df->sqd", heads_out, out_weight)

    def core_sum(own, sibling):
        return own + swap(sibling.astype(BF), 1).astype(F32)

    def z_scatter(array):
        return lax.psum_scatter(
            array.astype(BF), "tensor", scatter_dimension=0, tiled=True
        ).astype(F32)

    inputs = tokens.astype(F32)
    hidden = inputs + z_scatter(core_sum(attn_part[0], attn_part[1]))
    hidden = after(hidden, up_x, down_y[1])
    second_scale = lax.rsqrt(jnp.mean(hidden * hidden, axis=-1, keepdims=True) + EPS)
    second_unit = hidden * second_scale
    second_norm = (second_unit * gain_rows[1]).astype(BF)
    norm_z = lax.all_gather(second_norm, "tensor", axis=0, tiled=True)
    norm_z = after(norm_z, gate_y[1], grad_x)
    down_all = padded(down_y)
    gateup_all = padded(gate_y, up_y)

    norm_x = swap(norm_z, 2)
    norm_a = jnp.stack([norm_z, swap(norm_z, 1)])
    norm_b = jnp.stack([norm_x, swap(norm_x, 1)])
    grad_a = jnp.stack([grad_z, swap(grad_z, 1)])
    grad_b = jnp.stack([grad_x, swap(grad_x, 1)])

    expert_ids = group * mine_experts + jnp.arange(mine_experts, dtype=jnp.int32)

    router_rows = jnp.pad(router_full.T, ((0, 16 - experts - 1), (0, 0)))
    group_ids = group.astype(jnp.int32).reshape(1)

    def slots_of(codes_in):
        routes_in, slots_in = codes_in[:, None, :top_count], codes_in[:, None, top_count:]
        matches = routes_in == expert_ids[None, :, None, None]
        return jnp.max(jnp.where(matches, slots_in, -1), axis=2)

    def feed(slots, rows, grads):
        slotted, slot_grad, pair, act, terms, pair_s, act_s, inner_s, probs_out = plain_act_call(
            experts, capacity, group_ids, slots, rows, grads, router_rows, gateup_all, down_all
        )
        terms = jnp.concatenate([terms.swapaxes(1, 2), inner_s], axis=-1)
        flat = [a.reshape(mine_experts, -1, a.shape[-1]) for a in (slotted, slot_grad, pair, act)]
        shared = [a.reshape(1, -1, a.shape[-1]) for a in (rows, grads, pair_s, act_s)]
        return (pair, pair_s), (act, act_s), terms, (flat, shared), probs_out

    slots_a, slots_b = slots_of(codes_a), slots_of(codes_b)
    fed_a = feed(slots_a, norm_a, grad_a)
    fed_b = feed(slots_b, norm_b, grad_b)
    columns_a, columns_b = slots_a[..., None], slots_b[..., None]
    row_grad_b = plain_back_call(columns_b, *fed_b[0], gateup_all)
    row_grad_a = plain_back_call(after(columns_a, row_grad_b), *fed_a[0], gateup_all)
    row_out_b = plain_back_call(after(columns_b, row_grad_a), *fed_b[1], down_all)
    row_out_a = plain_back_call(columns_a, *fed_a[1], down_all)

    def spread(terms):
        wide = jnp.zeros(terms.shape[:-1] + (128,), F32)
        wide = lax.dynamic_update_slice_in_dim(
            wide, terms[..., :mine_experts], group * mine_experts, terms.ndim - 1
        )
        return wide.at[..., experts].set(terms[..., mine_experts])

    def group_sum(a, b):
        across = b[0].astype(F32) + swap(b[1].astype(BF), 1).astype(F32)
        near = a[0].astype(F32) + swap(a[1].astype(BF), 1).astype(F32)
        return near + swap(across.astype(BF), 2).astype(F32)

    grad_sum = group_sum(row_grad_a, row_grad_b)
    term_sum = group_sum(spread(fed_a[2]), spread(fed_b[2]))
    packed = z_scatter(jnp.concatenate([grad_sum, term_sum], axis=-1))
    second_grad, gate_sums = packed[:, :width], packed[:, width:]

    data_a, data_b = fed_a[3], fed_b[3]

    def unit_grads(left, right):
        return jnp.concatenate(
            [
                plain_outer_call(
                    hidden_units,
                    hidden_pad,
                    dp,
                    [(data[k][left], data[k][right]) for data in (data_a, data_b)],
                )
                for k in range(2)
            ],
            axis=1,
        )

    def scatter_units(total):
        total = total.reshape((2,) * len(bits) + total.shape[1:])
        for bit in reversed(upper):
            axis = len(bits) - 1 - bits.index(bit)
            sent = half(total, 1 - bit_of(bit), axis)
            kept = half(total, bit_of(bit), axis)
            total = (kept.astype(F32) + swap(sent, bit).astype(F32)).astype(BF)
        total = total.reshape((2, 2) + total.shape[len(bits) :])
        held = join(pick(total, xi, 0)[None], swap(pick(total, 1 - xi, 0), 2)[None], 2, 0)
        return join(pick(held, core, 1)[:, None], swap(pick(held, 1 - core, 1), 1)[:, None], 1, 1)

    def split_units(held):
        routed = held[:, :, :mine_experts].reshape(experts, -1, slice_width)
        shared = held[:, :, mine_experts]
        return routed.astype(F32), shared.astype(F32)

    gateup_sum = scatter_units(unit_grads(2, 0))
    down_sum = scatter_units(unit_grads(3, 1))
    routed_gu, shared_gu = split_units(gateup_sum)
    routed_down, shared_down_sum = split_units(down_sum)
    shared_gu = shared_gu.reshape(4, 2, hidden_units, slice_width)
    egate_sum = routed_gu[:, :hidden_units].swapaxes(1, 2)
    eup_sum = routed_gu[:, hidden_units:].swapaxes(1, 2)
    sgate_sum = shared_gu[:, 0].reshape(-1, slice_width).T
    sup_sum = shared_gu[:, 1].reshape(-1, slice_width).T
    sdown_sum = shared_down_sum.reshape(-1, slice_width)

    row_start = zi * local_rows
    probs_local = lax.dynamic_slice_in_dim(fed_a[4][0], row_start, local_rows, 1).T
    probs_mine, weight_mine = probs_local[:, :experts], probs_local[:, experts]
    route_grad = gate_sums[:, :experts]
    expert_logit_grad = probs_mine * (
        route_grad - jnp.sum(probs_mine * route_grad, axis=-1, keepdims=True)
    )
    weight_logit_grad = gate_sums[:, experts] * weight_mine * (1.0 - weight_mine)
    logits_grad = jnp.concatenate([expert_logit_grad, weight_logit_grad[:, None]], axis=1).astype(
        BF
    )
    second_grad = second_grad + einsum("tf,df->td", logits_grad, router_full)
    gain_two_grad = jnp.sum(second_grad * second_unit, axis=0)
    unit_two = second_grad * gain_rows[1]
    hidden_grad = out_grad.astype(F32) + second_scale * (
        unit_two - second_unit * jnp.mean(unit_two * second_unit, axis=-1, keepdims=True)
    )
    attention_grad = hidden_grad.astype(BF)
    wide_logits = jnp.pad(logits_grad, ((0, 0), (0, 128 - experts - 1)))
    back_z = lax.all_gather(
        jnp.concatenate([attention_grad, wide_logits], axis=1), "tensor", axis=0, tiled=True
    )
    out_sum = after(group_sum(row_out_a, row_out_b), back_z)
    output = (hidden + z_scatter(out_sum)).astype(BF)
    logits_z = back_z[:, width : width + 16]
    back_own = back_z[:, :width]
    back_rows = jnp.stack([back_own, swap(back_own, 1)])

    router_part = einsum("tf,td->fd", logits_z, norm_z)[: experts + 1]

    out_proj = einsum("std,stf->df", back_rows, heads_out)
    mix_grad = einsum("std,df->stf", back_rows, out_weight).astype(BF)
    mix_grad = mix_grad.reshape(2, seq_len, pair_heads, head_width)
    prob_grad = einsum("sqhd,skhd->shqk", mix_grad, values)
    score_grad = (
        probs * (prob_grad - jnp.sum(probs * prob_grad, axis=-1, keepdims=True))
    ).astype(BF)
    query_rot = einsum("shqk,skhd->sqhd", score_grad, keys) * score_scale
    key_rot = einsum("shqk,sqhd->skhd", score_grad, queries) * score_scale
    value_grad = einsum("shqk,sqhd->skhd", probs_low, mix_grad)
    qk_grad = rotate(jnp.concatenate([query_rot, key_rot], axis=2), cos_part, -sin_part)
    qk_grad = qk_grad.astype(BF).reshape(2, seq_len, 2 * pair_width)
    v_grad = value_grad.astype(BF).reshape(2, seq_len, pair_width)
    first_part = einsum("stf,df->std", qk_grad, qk_full) + einsum(
        "stf,df->std", v_grad, vo_full[:, :pair_width]
    )
    first_grad = z_scatter(core_sum(first_part[0], first_part[1]))

    gain_one_grad = jnp.sum(first_part * (rows_f * first_scale), axis=(0, 1))
    bias_part = jnp.concatenate(
        [jnp.sum(qk_grad.astype(F32), axis=(0, 1)), jnp.sum(v_grad.astype(F32), axis=(0, 1))]
    )
    bias_part = bias_part.reshape(3 * pair_heads, dp, -1).swapaxes(0, 1).reshape(dp, 1, -1)
    gain_part = jnp.stack([gain_one_grad, gain_two_grad]).reshape(2, dp, slice_width)

    def wide_rows(rows):
        return jnp.pad(rows, ((0, 0), (0, 0), (0, 2 * pair_width - rows.shape[2])))

    misc_part = jnp.concatenate(
        [
            wide_rows(router_part.reshape(experts + 1, dp, slice_width).swapaxes(0, 1)),
            wide_rows(bias_part),
            wide_rows(gain_part.swapaxes(0, 1)),
            jnp.zeros((dp, misc_rows - experts - 4, 2 * pair_width), F32),
        ],
        axis=1,
    )
    qk_total = einsum("std,stf->df", first_norm, qk_grad).reshape(dp, slice_width, -1)
    qk_total = jnp.concatenate([qk_total, misc_part], axis=1)
    vo_total = jnp.concatenate([einsum("std,stf->df", first_norm, v_grad), out_proj], axis=1)
    vo_total = vo_total.reshape(dp, slice_width, -1)

    def scatter_attention(total, order):
        total = total.reshape((2,) * len(bits) + total.shape[1:])
        for bit in order:
            axis = len(bits) - 1 - bits.index(bit)
            sent = half(total, 1 - bit_of(bit), axis).astype(BF)
            total = half(total, bit_of(bit), axis) + swap(sent, bit).astype(F32)
        total = total.reshape((2,) + total.shape[-2:]).astype(BF)
        return pick(total, core, 0), swap(pick(total, 1 - core, 0), 1)

    def columns_of(mine, theirs):
        held = join(mine[:slice_width, None], theirs[:slice_width, None], 1, 1)
        first, second = held[..., :pair_width], held[..., pair_width:]
        return (
            first.reshape(slice_width, -1).astype(F32),
            second.reshape(slice_width, -1).astype(F32),
        )

    qk_mine, qk_theirs = scatter_attention(qk_total, bits[:0:-1])
    vo_mine, vo_theirs = scatter_attention(vo_total, bits[1:])
    qk_sums = columns_of(qk_mine, qk_theirs)
    vo_sums = columns_of(vo_mine, vo_theirs)
    misc_mine = qk_mine[slice_width:].astype(F32)
    misc_theirs = qk_theirs[slice_width:].astype(F32)
    misc_sum = misc_mine + misc_theirs
    router_sum = misc_sum[: experts + 1, :slice_width].T
    bias_sums = join(
        misc_mine[experts + 1, :bias_width].reshape(3, 1, pair_heads, -1),
        misc_theirs[experts + 1, :bias_width].reshape(3, 1, pair_heads, -1),
        1,
        1,
    ).reshape(3, heads_local, -1)
    gain_sums = lax.all_gather(
        misc_sum[experts + 2 : experts + 4, :slice_width], "tensor", axis=0, tiled=False
    )
    tensor = gain_sums.shape[0]
    gain_sums = jnp.sum(gain_sums, axis=0).reshape(2, tensor, -1)
    gain_sums = pick(gain_sums, zi, 1)

    unit_mine = inputs * lax.rsqrt(jnp.mean(inputs * inputs, axis=-1, keepdims=True) + EPS)
    scale_mine = lax.rsqrt(jnp.mean(inputs * inputs, axis=-1, keepdims=True) + EPS)
    unit_one = first_grad * gain_rows[0]
    input_grad = hidden_grad + scale_mine * (
        unit_one - unit_mine * jnp.mean(unit_one * unit_mine, axis=-1, keepdims=True)
    )
    return (
        output,
        input_grad.astype(BF),
        gain_sums,
        qk_sums[0],
        qk_sums[1],
        vo_sums[0],
        vo_sums[1].T,
        bias_sums,
        router_sum,
        sgate_sum,
        sup_sum,
        sdown_sum,
        egate_sum,
        eup_sum,
        routed_down,
    )


def local_fused(
    dp,
    depth,
    tokens,
    picture_ids,
    routes,
    slot_order,
    norm_gains,
    w_query,
    w_key,
    w_value,
    w_out,
    qkv_bias,
    router,
    shared_gate,
    shared_up,
    shared_down,
    expert_gate,
    expert_up,
    expert_down,
    out_grad,
):
    seq_len = picture_ids.shape[0]
    local_rows = tokens.shape[0]
    width = tokens.shape[1]
    experts, slice_width, hidden_units = expert_gate.shape
    top_count = routes.shape[1]
    capacity = 5 * seq_len * top_count // (4 * experts)
    heads_local = qkv_bias.shape[1]
    head_width = w_query.shape[1] // heads_local
    pair_heads = heads_local // 2
    pair_width = pair_heads * head_width
    mine_experts = experts // 4
    hidden_pad = -(-hidden_units // 128) * 128

    me = lax.axis_index("dp")
    zi = lax.axis_index("tensor")
    core, xi = me % 2, (me // 2) % 2
    group = me % 4
    def swap(array, bit):
        return lax.ppermute(array, "dp", [(i, i ^ bit) for i in range(dp)])

    codes = jnp.concatenate([routes.T, slot_order.T, picture_ids[None]], axis=0)
    codes = jnp.pad(codes, ((0, 16 - codes.shape[0]), (0, 0)))
    bias_cores = qkv_bias.reshape(3, 2, -1).swapaxes(0, 1).reshape(2, -1)
    bias_width = bias_cores.shape[1]
    misc = jnp.zeros((16, slice_width), F32)
    misc = misc.at[: experts + 1].set(router.T.astype(F32))
    misc = misc.at[experts + 1 : experts + 3, :bias_width].set(bias_cores.astype(F32))
    gains = lax.dynamic_update_slice(
        jnp.zeros((8, slice_width), F32),
        norm_gains.astype(F32),
        (jnp.int32(0), zi * norm_gains.shape[1]),
    )
    cos_part, sin_part = rope_tables(seq_len, head_width)
    cos_rows = jnp.concatenate([cos_part, cos_part], axis=1)
    sin_rows = jnp.concatenate([-sin_part, sin_part], axis=1)
    (
        hidden,
        norm_all,
        grads_all,
        gateup_all,
        down_all,
        codes_all,
        misc_all,
        gain_rows,
        tok,
        attn_weights,
        qkv,
        probs_low,
        heads_out,
    ) = forward_call(
        dp,
        depth,
        experts,
        head_width,
        (codes, misc, gains, cos_rows, sin_rows),
        (tokens, out_grad, w_query, w_key, w_value, w_out.T),
        (
            expert_gate.swapaxes(1, 2),
            expert_up.swapaxes(1, 2),
            expert_down,
            shared_gate.T.reshape(4, hidden_units, slice_width),
            shared_up.T.reshape(4, hidden_units, slice_width),
            shared_down.reshape(4, hidden_units, slice_width),
        ),
    )
    gateup_all = gateup_all.reshape(mine_experts + 1, 2 * hidden_pad, width)
    down_all = down_all.reshape(mine_experts + 1, hidden_pad, width)
    router_rows = jnp.concatenate([misc_all[d] for d in range(dp)], axis=1)
    router_rows = jnp.where(jnp.arange(16)[:, None] <= experts, router_rows, 0.0).astype(BF)
    router_rows = jnp.pad(router_rows, ((0, 128 - router_rows.shape[0]), (0, 0)))
    group_ids = group.astype(jnp.int32).reshape(1)

    def feed(chunk, group_in):
        return act_call(
            experts,
            top_count,
            chunk,
            group_in,
            codes_all,
            norm_all,
            grads_all,
            router_rows,
            gateup_all,
            down_all,
        )

    def across(own, sibling):
        total = own.astype(F32) + swap(sibling, 1).astype(F32)
        return total.astype(own.dtype)

    pair_b, act_b, terms_b, _ = feed(1, group_ids)
    terms_far = swap(across(terms_b[0], terms_b[1]), 2)
    out_far = across(*back_call(act_b, down_all))
    grad_far = across(*back_call(after(pair_b, out_far), gateup_all))
    pair_a, act_a, terms_a, probs_out = feed(0, after(group_ids, grad_far, terms_far))
    out_a = back_call(act_a, down_all)
    out_sum = out_a[0].astype(F32) + swap(out_a[1], 1).astype(F32) + swap(out_far, 2).astype(F32)
    gate_total, up_total = units_call(
        hidden_units, hidden_pad, dp, mine_experts + 1, after(pair_a, out_a[0]), pair_b, norm_all
    )
    gate_sent = lax.dynamic_slice_in_dim(gate_total, (1 - me // 4) * 4, 4, 0)
    gate_in = swap(gate_sent, 4)
    grad_a = back_call(after(pair_a, gate_sent), gateup_all)
    (down_total,) = units_call(
        hidden_units, hidden_pad, dp, mine_experts + 1, act_a, after(act_b, grad_a[0]), grads_all
    )
    grad_parts = (grad_a[0], swap(grad_a[1], 1), swap(grad_far, 2))
    terms = jnp.stack([terms_a[0], swap(terms_a[1], 1), terms_far])
    feed_out = lax.psum_scatter(
        out_sum.astype(BF), "tensor", scatter_dimension=0, tiled=True
    ).astype(F32)
    output = (hidden + feed_out).astype(BF)
    probs_mine = lax.dynamic_slice_in_dim(probs_out[0], zi * local_rows, local_rows, 0)
    input_grad, gate_sum, up_sum, down_sum, attn_sum, misc_sum, gains_sum = backward_call(
        dp,
        depth,
        experts,
        head_width,
        (terms, probs_mine, router_rows, gain_rows, cos_rows, sin_rows, hidden, out_grad),
        grad_parts
        + (gate_in, gate_total, up_total, down_total)
        + (tok, attn_weights, qkv, probs_low, heads_out, norm_all),
    )

    def split_units(held):
        routed = held[:, :mine_experts].reshape(experts, hidden_units, slice_width)
        shared = held[:, mine_experts].reshape(-1, slice_width)
        return routed.astype(F32), shared.astype(F32)

    egate_sum, sgate_sum = split_units(gate_sum)
    eup_sum, sup_sum = split_units(up_sum)
    edown_sum, sdown_sum = split_units(down_sum)

    def columns_of(kind):
        held = attn_sum[:, :, kind * pair_width : (kind + 1) * pair_width].swapaxes(0, 1)
        return held.reshape(slice_width, -1).astype(F32)

    bias_sums = misc_sum[experts + 1 : experts + 3, :bias_width].reshape(2, 3, pair_heads, -1)
    bias_sums = bias_sums.swapaxes(0, 1).reshape(3, heads_local, -1)
    piece = norm_gains.shape[1]
    gain_sums = lax.dynamic_slice(gains_sum[3:5], (jnp.int32(0), zi * piece), (2, piece))
    return (
        output,
        input_grad,
        gain_sums,
        columns_of(0),
        columns_of(1),
        columns_of(2),
        columns_of(3).T,
        bias_sums,
        misc_sum[: experts + 1].T,
        sgate_sum.T,
        sup_sum.T,
        sdown_sum,
        egate_sum.swapaxes(1, 2),
        eup_sum.swapaxes(1, 2),
        edown_sum,
    )


def solution(mesh):
    dp, depth = mesh.shape["dp"], mesh.shape["tensor"]

    def body(*arrays):
        if arrays[5].shape[0] % 128 == 0 and dp == 8 and depth == 4:
            return local_fused(dp, depth, *arrays)
        return local_plain(dp, *arrays)

    return jax.shard_map(
        body,
        mesh=mesh,
        in_specs=(
            P(("dp", "tensor"), None),
            P("dp"),
            P("dp", None),
            P("dp", None),
            P(None, ("dp", "tensor")),
            P("dp", "tensor"),
            P("dp", "tensor"),
            P("dp", "tensor"),
            P("tensor", "dp"),
            P(None, "tensor", "dp"),
            P("dp", None),
            P("dp", "tensor"),
            P("dp", "tensor"),
            P("tensor", "dp"),
            P(None, "dp", "tensor"),
            P(None, "dp", "tensor"),
            P(None, "tensor", "dp"),
            P(("dp", "tensor"), None),
        ),
        out_specs=(
            P(("dp", "tensor"), None),
            P(("dp", "tensor"), None),
            P(None, ("dp", "tensor")),
            P("dp", "tensor"),
            P("dp", "tensor"),
            P("dp", "tensor"),
            P("tensor", "dp"),
            P(None, "tensor", "dp"),
            P("dp", None),
            P("dp", "tensor"),
            P("dp", "tensor"),
            P("tensor", "dp"),
            P(None, "dp", "tensor"),
            P(None, "dp", "tensor"),
            P(None, "tensor", "dp"),
        ),
        check_vma=False,
    )
```

```python
import functools

import jax
import jax.numpy as jnp
from jax import lax
from jax.experimental import pallas as pl
from jax.experimental.pallas import tpu as pltpu
from jax.sharding import PartitionSpec as P

EPS = 1e-06
THETA = 1000000.0
BF = jnp.bfloat16
F32 = jnp.float32


def rope_tables(length, width):
    half_width = width // 2
    inverse = THETA ** (-(2.0 * jnp.arange(half_width, dtype=F32)) / width)
    angles = jnp.arange(length, dtype=F32)[:, None] * inverse[None, :]
    return jnp.cos(angles), jnp.sin(angles)


def rotate(field_in, cos_part, sin_part):
    half_width = field_in.shape[-1] // 2
    low, high = field_in[..., :half_width], field_in[..., half_width:]
    cos_rows, sin_rows = cos_part[:, None, :], sin_part[:, None, :]
    return jnp.concatenate(
        [low * cos_rows - high * sin_rows, high * cos_rows + low * sin_rows], axis=-1
    )


def einsum(spec, *args):
    return jnp.einsum(spec, *args, preferred_element_type=F32)


def silu_parts(gate_in):
    gate_sig = jax.nn.sigmoid(gate_in)
    return gate_in * gate_sig, gate_sig * (1.0 + gate_in * (1.0 - gate_sig))


def after(array, *others):
    return lax.optimization_barrier((array,) + others)[0]


def pick(array, index, axis):
    return lax.dynamic_index_in_dim(array, index, axis, keepdims=False)


VMEM_LIMIT = 58 * 2**20


def dot(left, right, left_dim=1, right_dim=0):
    return lax.dot_general(
        left, right, (((left_dim,), (right_dim,)), ((), ())), preferred_element_type=F32
    )


def call(body, grid, in_specs, out_specs, out_shape, flops, moved, scratch=()):
    return pl.pallas_call(
        body,
        grid=grid,
        in_specs=in_specs,
        out_specs=out_specs,
        out_shape=out_shape,
        scratch_shapes=scratch,
        cost_estimate=pl.CostEstimate(flops=flops, bytes_accessed=moved, transcendentals=0),
        compiler_params=pltpu.CompilerParams(vmem_limit_bytes=VMEM_LIMIT),
    )


def plain_act_body(
    experts,
    units,
    group_ref,
    slot_ref,
    rows_ref,
    grads_ref,
    router_ref,
    gateup_ref,
    down_ref,
    slotted_ref,
    slotgrad_ref,
    pair_ref,
    act_ref,
    terms_ref,
    pair_s_ref,
    act_s_ref,
    inner_s_ref,
    probs_ref,
):
    unit = pl.program_id(1)
    half = gateup_ref.shape[1] // 2
    seq_len = rows_ref.shape[1]
    capacity = slotted_ref.shape[2]

    @pl.when(unit == 0)
    def _():
        logits = dot(router_ref[...], rows_ref[0], 1, 1)
        row = lax.broadcasted_iota(jnp.int32, logits.shape, 0)
        routed = jnp.where(row < experts, logits, -1e30)
        raised = jnp.exp(routed - jnp.max(routed, axis=0, keepdims=True))
        soft = raised / jnp.sum(raised, axis=0, keepdims=True)
        probs_ref[0] = jnp.where(row < experts, soft, jax.nn.sigmoid(logits))

    def parts(data, cot, weight):
        both = dot(data, gateup_ref[0], 1, 1)
        cot_in = dot(cot, down_ref[0], 1, 1)
        gate_in, up_in = both[:, :half], both[:, half:]
        gate_act, gate_slope = silu_parts(gate_in)
        act = gate_act * up_in
        inner = jnp.sum(act.astype(BF).astype(F32) * cot_in, axis=1, keepdims=True)
        cot_in = cot_in * weight
        return (
            (act * weight).astype(BF),
            (cot_in * up_in * gate_slope).astype(BF),
            (cot_in * gate_act).astype(BF),
            inner,
        )

    @pl.when(unit < units - 1)
    def _():
        slot = slot_ref[0, pl.ds(unit, 1), :]
        mask = lax.broadcasted_iota(jnp.int32, (capacity, seq_len), 0) == slot
        onehot = mask.astype(F32).astype(BF)
        slotted_ref[0, 0] = dot(onehot, rows_ref[0]).astype(BF)
        slotgrad_ref[0, 0] = dot(onehot, grads_ref[0]).astype(BF)
        probs = probs_ref[0]
        row = lax.broadcasted_iota(jnp.int32, probs.shape, 0)
        expert = group_ref[0] * (units - 1) + unit
        gate = jnp.sum(jnp.where(row == expert, probs, 0.0), axis=0, keepdims=True)
        weight = jnp.sum(jnp.where(mask, gate, 0.0), axis=1, keepdims=True)
        act, gate_grad, up_grad, inner = parts(slotted_ref[0, 0], slotgrad_ref[0, 0], weight)
        act_ref[0, 0] = act
        pair_ref[0, 0, :, :half] = gate_grad
        pair_ref[0, 0, :, half:] = up_grad
        terms_ref[0, pl.ds(unit, 1), :] = jnp.sum(
            jnp.where(mask, inner, 0.0), axis=0, keepdims=True
        )

    @pl.when(unit == units - 1)
    def _():
        logits = dot(rows_ref[0], router_ref[...], 1, 1)
        weight = jax.nn.sigmoid(logits[:, experts : experts + 1])
        act, gate_grad, up_grad, inner = parts(rows_ref[0], grads_ref[0], weight)
        act_s_ref[0] = act
        pair_s_ref[0, :, :half] = gate_grad
        pair_s_ref[0, :, half:] = up_grad
        inner_s_ref[0] = inner


def plain_act_call(experts, capacity, group, slots, rows, grads, router, gateup, down):
    count, seq_len, width = rows.shape
    units, wide, _ = gateup.shape
    half = wide // 2
    routed = units - 1

    def seq(s, u):
        return (s, 0, 0)

    def unit(s, u):
        return (u, 0, 0)

    def slot(s, u):
        return (jnp.minimum(u, routed - 1), s, 0, 0)

    work = count * (routed * capacity + seq_len) * width
    return call(
        functools.partial(plain_act_body, experts, units),
        (count, units),
        [
            pl.BlockSpec(memory_space=pltpu.SMEM),
            pl.BlockSpec((1, routed, seq_len), seq),
            pl.BlockSpec((1, seq_len, width), seq),
            pl.BlockSpec((1, seq_len, width), seq),
            pl.BlockSpec(router.shape, lambda s, u: (0, 0)),
            pl.BlockSpec((1, wide, width), unit),
            pl.BlockSpec((1, half, width), unit),
        ],
        [
            pl.BlockSpec((1, 1, capacity, width), slot),
            pl.BlockSpec((1, 1, capacity, width), slot),
            pl.BlockSpec((1, 1, capacity, wide), slot),
            pl.BlockSpec((1, 1, capacity, half), slot),
            pl.BlockSpec((1, routed, seq_len), seq),
            pl.BlockSpec((1, seq_len, wide), seq),
            pl.BlockSpec((1, seq_len, half), seq),
            pl.BlockSpec((1, seq_len, 1), seq),
            pl.BlockSpec((1,) + (router.shape[0], seq_len), seq),
        ],
        [
            jax.ShapeDtypeStruct((routed, count, capacity, width), BF),
            jax.ShapeDtypeStruct((routed, count, capacity, width), BF),
            jax.ShapeDtypeStruct((routed, count, capacity, wide), BF),
            jax.ShapeDtypeStruct((routed, count, capacity, half), BF),
            jax.ShapeDtypeStruct((count, routed, seq_len), F32),
            jax.ShapeDtypeStruct((count, seq_len, wide), BF),
            jax.ShapeDtypeStruct((count, seq_len, half), BF),
            jax.ShapeDtypeStruct((count, seq_len, 1), F32),
            jax.ShapeDtypeStruct((count, router.shape[0], seq_len), F32),
        ],
        2 * work * 3 * half + 4 * count * routed * capacity * seq_len * width,
        8 * count * seq_len * width * 2,
    )(group, slots, rows, grads, router, gateup, down)


def plain_back_body(slot_ref, routed_ref, shared_ref, weight_ref, out_ref):
    routed, _, capacity, _ = routed_ref.shape
    seq_len = shared_ref.shape[1]
    total = dot(shared_ref[0], weight_ref[routed])
    lane = lax.broadcasted_iota(jnp.int32, (seq_len, capacity), 1)
    for e in range(routed):
        slot_rows = dot(routed_ref[e, 0], weight_ref[e]).astype(BF)
        onehot = (lane == slot_ref[0, e]).astype(F32).astype(BF)
        total = total + dot(onehot, slot_rows)
    out_ref[0] = total.astype(BF)


def plain_back_call(slots, routed, shared, weight):
    units, wide, width = weight.shape
    count, seq_len, _ = shared.shape
    capacity = routed.shape[2]
    block = min(width, 512)
    work = count * ((units - 1) * capacity + seq_len) * width
    return call(
        plain_back_body,
        (width // block, count),
        [
            pl.BlockSpec((1, units - 1, seq_len, 1), lambda j, s: (s, 0, 0, 0)),
            pl.BlockSpec((units - 1, 1, capacity, wide), lambda j, s: (0, s, 0, 0)),
            pl.BlockSpec((1, seq_len, wide), lambda j, s: (s, 0, 0)),
            pl.BlockSpec((units, wide, block), lambda j, s: (0, 0, j)),
        ],
        pl.BlockSpec((1, seq_len, block), lambda j, s: (s, 0, j)),
        jax.ShapeDtypeStruct((count, seq_len, width), BF),
        2 * work * wide + 2 * count * (units - 1) * capacity * seq_len * width,
        units * wide * width * 2 + count * seq_len * width * 2,
    )(slots, routed, shared, weight)


def plain_outer_body(keep, pad, left_a, right_a, left_b, right_b, out_ref):
    total = dot(left_a[0], right_a[0], 0, 0) + dot(left_b[0], right_b[0], 0, 0)
    total = total.astype(BF)
    blocks, _, rows, slice_width = out_ref.shape
    for part in range(rows // keep):
        for k in range(blocks):
            out_ref[k, 0, part * keep : (part + 1) * keep] = total[
                part * pad : part * pad + keep, k * slice_width : (k + 1) * slice_width
            ]


def plain_outer_call(keep, pad, dp, pairs):
    (left_a, right_a), (left_b, right_b) = pairs
    units, rows, wide = left_a.shape
    width = right_a.shape[2]
    slice_width = width // dp
    blocks = max(1, 512 // slice_width)
    kept = wide // pad * keep

    def left(n):
        return pl.BlockSpec((1, n, wide), lambda u, j: (u, 0, 0))

    def right(n):
        return pl.BlockSpec((1, n, blocks * slice_width), lambda u, j: (u, 0, j))

    return call(
        functools.partial(plain_outer_body, keep, pad),
        (units, dp // blocks),
        [left(rows), right(rows), left(rows), right(rows)],
        pl.BlockSpec((blocks, 1, kept, slice_width), lambda u, j: (j, u, 0, 0)),
        jax.ShapeDtypeStruct((dp, units, kept, slice_width), BF),
        4 * units * rows * wide * width,
        units * rows * (wide + width) * 4,
    )(left_a, right_a, left_b, right_b)


def act_body(
    experts,
    top_count,
    group_ref,
    codes_ref,
    rows_ref,
    grads_ref,
    router_ref,
    gateup_ref,
    down_ref,
    pair_ref,
    act_ref,
    terms_ref,
    probs_ref,
    weights,
    routed,
):
    unit, units = pl.program_id(0), pl.num_programs(0)
    half = gateup_ref.shape[1] // 2
    count, seq_len, width = rows_ref.shape
    data = rows_ref[...].reshape(count * seq_len, width)
    cot = grads_ref[...].reshape(count * seq_len, width)
    lane = lax.broadcasted_iota(jnp.int32, weights.shape, 1)

    @pl.when(unit == 0)
    def _():
        logits = dot(data, router_ref[...], 1, 1)
        chosen = jnp.where(lane < experts, logits, -1e30)
        raised = jnp.exp(chosen - jnp.max(chosen, axis=1, keepdims=True))
        soft = raised / jnp.sum(raised, axis=1, keepdims=True)
        probs = jnp.where(lane < experts, soft, jax.nn.sigmoid(logits))
        for s in range(count):
            codes = codes_ref[s]
            row = lax.broadcasted_iota(jnp.int32, codes.shape, 0)
            named = row == experts
            for k in range(top_count):
                named = jnp.logical_or(named, codes[k : k + 1] == row)
            named = jnp.logical_and(named, row <= experts).astype(F32).astype(BF)
            place = (codes.shape[0], weights.shape[1])
            same = lax.broadcasted_iota(jnp.int32, place, 0) == lax.broadcasted_iota(
                jnp.int32, place, 1
            )
            at = slice(s * seq_len, (s + 1) * seq_len)
            routed[at] = dot(named, same.astype(F32).astype(BF), 0, 0)
            probs_ref[s] = probs[at]
        weights[...] = probs * routed[...]
        terms_ref[...] = jnp.zeros_like(terms_ref)

    mine = lane == jnp.where(unit < units - 1, group_ref[0] * (units - 1) + unit, experts)
    weight = jnp.sum(jnp.where(mine, weights[...], 0.0), axis=1, keepdims=True)
    both = dot(data, gateup_ref[0], 1, 1)
    cot_in = dot(cot, down_ref[0], 1, 1)
    gate_in, up_in = both[:, :half], both[:, half:]
    gate_act, gate_slope = silu_parts(gate_in)
    act = gate_act * up_in
    inner = jnp.sum(act.astype(BF).astype(F32) * cot_in, axis=1, keepdims=True)
    cot_in = cot_in * weight
    act_ref[...] = (act * weight).astype(BF)
    pair_ref[:, :half] = (cot_in * up_in * gate_slope).astype(BF)
    pair_ref[:, half:] = (cot_in * gate_act).astype(BF)
    terms_ref[...] += jnp.where(mine, inner * routed[...], 0.0).reshape(terms_ref.shape)


def act_call(experts, top_count, chunk, group, codes, rows, grads, router, gateup, down):
    _, seq_len, width = rows.shape
    units, wide, _ = gateup.shape
    half, count = wide // 2, 2
    total = count * seq_len

    def part(*shape):
        return pl.BlockSpec(
            shape,
            lambda u: (chunk,) + (0,) * (len(shape) - 1),
            pipeline_mode=pl.Buffered(1),
        )

    def unit(u):
        return (u, 0, 0)

    def whole(u):
        return (0, 0, 0)

    return call(
        functools.partial(act_body, experts, top_count),
        (units,),
        [
            pl.BlockSpec(memory_space=pltpu.SMEM),
            part(count, codes.shape[1], seq_len),
            part(count, seq_len, width),
            part(count, seq_len, width),
            pl.BlockSpec(router.shape, lambda u: (0, 0)),
            pl.BlockSpec((1, wide, width), unit),
            pl.BlockSpec((1, half, width), unit),
        ],
        [
            pl.BlockSpec((total, wide), lambda u: (0, u)),
            pl.BlockSpec((total, half), lambda u: (0, u)),
            pl.BlockSpec((count, seq_len, 128), whole),
            pl.BlockSpec((count, seq_len, 128), whole),
        ],
        [
            jax.ShapeDtypeStruct((total, units * wide), BF),
            jax.ShapeDtypeStruct((total, units * half), BF),
            jax.ShapeDtypeStruct((count, seq_len, 128), F32),
            jax.ShapeDtypeStruct((count, seq_len, 128), F32),
        ],
        2 * total * units * 3 * half * width,
        4 * total * width + units * 3 * half * width * 2,
        [pltpu.VMEM((total, 128), F32), pltpu.VMEM((total, 128), F32)],
    )(group, codes, rows, grads, router, gateup, down)


def back_body(left_ref, weight_ref, *out_refs):
    seq_len = out_refs[0].shape[0]
    total = dot(left_ref[...], weight_ref[...]).astype(BF)
    for s, out_ref in enumerate(out_refs):
        out_ref[...] = total[s * seq_len : (s + 1) * seq_len]


def back_call(left, weight):
    units, wide, width = weight.shape
    weight = weight.reshape(units * wide, width)
    total, depth = left.shape
    block = min(width, 512)
    return call(
        back_body,
        (width // block,),
        [
            pl.BlockSpec((total, depth), lambda j: (0, 0), pipeline_mode=pl.Buffered(1)),
            pl.BlockSpec((depth, block), lambda j: (0, j)),
        ],
        [pl.BlockSpec((total // 2, block), lambda j: (0, j))] * 2,
        [jax.ShapeDtypeStruct((total // 2, width), BF)] * 2,
        2 * total * depth * width,
        (total * depth + depth * width + total * width) * 2,
    )(left, weight)


def units_body(keep, pad, left_a, left_b, right_a, right_b, *outs):
    total = dot(left_a[...], right_a[0], 0, 0) + dot(left_b[...], right_b[0], 0, 0)
    total = total.astype(BF)
    for part, out_ref in enumerate(outs):
        blocks, _, _, slice_width = out_ref.shape
        for k in range(blocks):
            out_ref[k, 0] = total[
                part * pad : part * pad + keep, k * slice_width : (k + 1) * slice_width
            ]


def units_call(keep, pad, dp, units, left_a, left_b, right):
    right = right.reshape(2, left_a.shape[0], -1)
    total, width = right.shape[1:]
    wide = left_a.shape[1] // units
    slice_width = width // dp
    blocks = max(1, 1024 // slice_width)
    parts = wide // pad
    left = pl.BlockSpec((total, wide), lambda u, j: (0, u))

    def chunk(k):
        return pl.BlockSpec((1, total, blocks * slice_width), lambda u, j: (k, 0, j))

    return call(
        functools.partial(units_body, keep, pad),
        (units, dp // blocks),
        [left, left, chunk(0), chunk(1)],
        [pl.BlockSpec((blocks, 1, keep, slice_width), lambda u, j: (j, u, 0, 0))] * parts,
        [jax.ShapeDtypeStruct((dp, units, keep, slice_width), BF)] * parts,
        4 * total * units * wide * width,
        (4 * total * width + 4 * total * units * wide + units * wide * width) * 2,
    )(left_a, left_b, right, right)


MESH = pl.DeviceIdType.MESH


class Copies:
    def __init__(self, send, recv, here):
        self.send, self.recv, self.here = send, recv, here
        self.remote_count = self.local_count = 0

    def remote(self, src, dst, **device):
        k = self.remote_count
        self.remote_count += 1
        return pltpu.make_async_remote_copy(
            src_ref=src,
            dst_ref=dst,
            send_sem=self.send.at[k],
            recv_sem=self.recv.at[k],
            device_id=device,
            device_id_type=MESH,
        )

    def local(self, src, dst):
        k = self.local_count
        self.local_count += 1
        return pltpu.make_async_copy(src, dst, self.here.at[k])


class Line:
    def __init__(self, copies, buffer, z, depth, rows):
        self.z, self.depth = z, depth

        def piece(p):
            return buffer.at[pl.ds(pl.multiple_of(p * rows, rows), rows)]

        def make(k, sign):
            p = z - sign * k
            return copies.remote(piece(p), piece(p), tensor=z + sign)

        self.ups = [make(k, 1) for k in range(depth - 1)]
        self.downs = [make(k, -1) for k in range(depth - 1)]

    def sends(self, k):
        z, top = self.z, self.depth - 1
        return (
            (self.ups[k], jnp.logical_and(z < top, z >= k)),
            (self.downs[k], jnp.logical_and(z > 0, z + k <= top)),
        )

    def begin(self):
        for copy, there in self.sends(0):
            pl.when(there)(copy.start)

    def finish(self):
        for k in range(self.depth - 1):
            for copy, there in self.sends(k):
                pl.when(there)(copy.wait_send)


def peer_of(me, r):
    out, bit = me, 1
    while bit <= r:
        if r & bit:
            out = out + bit - 2 * bit * (me // bit % 2)
        bit *= 2
    return out


def greet(me, z, dp, depth):
    barrier = pltpu.get_barrier_semaphore()
    for r in range(1, dp):
        pl.semaphore_signal(barrier, inc=1, device_id={"dp": peer_of(me, r)}, device_id_type=MESH)
    for r in range(1, depth):
        pl.semaphore_signal(
            barrier, inc=1, device_id={"tensor": (z + r) % depth}, device_id_type=MESH
        )
    pl.semaphore_wait(barrier, dp - 1 + depth - 1)


def spin(field, cos_rows, sin_rows):
    return field * cos_rows + pltpu.roll(field, field.shape[-1] // 2, 1) * sin_rows


def piece_of(buffer, p, rows):
    return buffer.at[pl.ds(pl.multiple_of(p * rows, rows), rows)]


def pass_on(c, source, target, z, depth, rows, sibling, passed):
    def make(p):
        return c.remote(piece_of(source, p, rows), piece_of(target, p, rows), dp=sibling)

    ups = [make(z - k) for k in range(1, depth)]
    downs = [make(z + k) for k in range(1, depth)]
    for k in range(1, depth):
        passed.append((ups[k - 1], z >= k))
        passed.append((downs[k - 1], z + k <= depth - 1))

    def each(k, up):
        (ups if up else downs)[k - 1].start()

    return each


def line_step(line, k, each=None):
    z, top = line.z, line.depth - 1
    onward = line.sends(k) if k < top else (None, None)
    for up, copy, there, further in (
        (True, line.ups[k - 1], z >= k, onward[0]),
        (False, line.downs[k - 1], z + k <= top, onward[1]),
    ):
        pl.when(there)(copy.wait_recv)
        if further is not None:
            pl.when(further[1])(further[0].start)
        if each is not None:
            pl.when(there)(functools.partial(each, k, up))


def forward_body(
    sizes,
    codes_ref,
    misc_ref,
    gains_ref,
    cos_ref,
    sin_ref,
    tokens_ref,
    outgrad_ref,
    wq_ref,
    wk_ref,
    wv_ref,
    wo_ref,
    eg_ref,
    eu_ref,
    ed_ref,
    sg_ref,
    su_ref,
    sd_ref,
    hidden_ref,
    norm_ref,
    grads_ref,
    gateup_ref,
    down_ref,
    codes_all,
    router_out,
    gain_rows,
    tok_out,
    weights_out,
    qkv_out,
    probs_out,
    mix_out,
    misc_all,
    norm_mine,
    tok,
    weights,
    qkv_ref,
    probs_ref,
    mix_ref,
    fnorm,
    part,
    part_in,
    scatter_in,
    gains_all,
    zeros,
    send,
    recv,
    here,
):
    dp, depth, experts, hidden_units, head = sizes
    me, z = lax.axis_index("dp"), lax.axis_index("tensor")
    core, x = me % 2, (me // 2) % 2
    bits = [2**k for k in range(dp.bit_length() - 1)]
    rows, width = tokens_ref.shape
    seq_len = rows * depth
    slice_width = width // dp
    routed = experts // 4
    c = Copies(send, recv, here)

    def bit_of(bit):
        return (me // bit) % 2

    greet(me, z, dp, depth)

    first = []
    own_codes = c.local(codes_ref, codes_all.at[0])
    own_misc = c.local(misc_ref, misc_all.at[me])
    own_gains = c.local(gains_ref, gains_all.at[z, me])
    for copy in (own_codes, own_misc, own_gains):
        copy.start()
    for r in range(1, 4):
        first.append(c.remote(codes_ref, codes_all.at[r], dp=peer_of(me, r)))
    gain_copies = [c.remote(gains_ref, gains_all.at[z, me], dp=peer_of(me, r)) for r in range(1, dp)]
    misc_copies = [c.remote(misc_ref, misc_all.at[me], dp=peer_of(me, r)) for r in range(1, dp)]
    for copy in gain_copies + misc_copies + first:
        copy.start()

    def piece(buffer, p):
        return buffer.at[pl.ds(pl.multiple_of(p * rows, rows), rows)]

    own_tok = c.local(tokens_ref, piece(tok.at[0], z))
    own_tok.start()
    own_grad = c.local(outgrad_ref, piece(grads_ref.at[0], z))
    own_grad.start()

    def columns(k, n):
        return pl.ds(pl.multiple_of(k * n, n), n)

    pair = wq_ref.shape[1] // 2
    own_at = tuple(bit_of(bit) for bit in reversed(bits))
    core_copies = []
    for k, w in enumerate((wq_ref, wk_ref, wv_ref, wo_ref)):
        place = weights.at[own_at + (slice(None), pl.ds(k * pair, pair))]
        core_copies.append(c.remote(w.at[:, columns(1 - core, pair)], place, dp=peer_of(me, 1)))
        core_copies.append(c.local(w.at[:, columns(core, pair)], place))
    for copy in core_copies:
        copy.start()

    own_tok.wait()
    tok_line = Line(c, tok.at[0], z, depth, rows)
    tok_line.begin()
    tok_pass = [c.remote(tokens_ref, piece(tok.at[1], z), dp=peer_of(me, 1))]
    tok_pass[0].start()

    zeros[...] = jnp.zeros_like(zeros)
    pad = zeros.shape[1]
    pads = [c.local(zeros, down_ref.at[:, 0, pl.ds(hidden_units, pad)])]
    pads += [c.local(zeros, gateup_ref.at[:, k, pl.ds(hidden_units, pad)]) for k in range(2)]
    matrices = ((ed_ref, sd_ref, down_ref, 0), (eg_ref, sg_ref, gateup_ref, 0), (eu_ref, su_ref, gateup_ref, 1))
    slab = columns(me, slice_width)

    def group_copies(routed_src, shared_src, dst, k, r):
        group = (peer_of(me, r)) % 4
        many = (
            routed_src.at[pl.ds(group * routed, routed)],
            dst.at[pl.ds(0, routed), k, pl.ds(0, hidden_units), slab],
        )
        one = (shared_src.at[group], dst.at[routed, k, pl.ds(0, hidden_units), slab])
        if r == 0:
            return [c.local(*many), c.local(*one)]
        return [c.remote(*many, dp=peer_of(me, r)), c.remote(*one, dp=peer_of(me, r))]

    near = [[copy for r in (0, 1) for copy in group_copies(*m, r)] for m in matrices]
    far = [[copy for r in (2, 3) for copy in group_copies(*m, r)] for m in matrices]

    def over_copy(dst, k, far_chip):
        n = 2 * slice_width
        chip = me // 2 + far_chip * (1 - 2 * x)
        cols = pl.ds(pl.multiple_of(chip * n, n), n)
        place = dst.at[:, k, pl.ds(0, hidden_units), cols]
        return c.remote(place, place, dp=peer_of(me, 4))

    over_near = [over_copy(m[2], m[3], 0) for m in matrices]
    over = [over_copy(m[2], m[3], 1) for m in matrices]

    for copy in core_copies:
        copy.wait()

    def weight_copies(order, half):
        have, copies = [1], []
        for bit in order:
            index = tuple(
                pl.ds(0, 2) if b in have else pl.ds(bit_of(b), 1) for b in reversed(bits)
            )
            place = weights.at[index + (slice(None), pl.ds(half * 2 * pair, 2 * pair))]
            copies.append(c.remote(place, place, dp=peer_of(me, bit)))
            have.append(bit)
        return copies

    qk_copies = weight_copies(bits[1:], 0)
    vo_copies = weight_copies(bits[:0:-1], 1)
    qk_copies[0].start()
    vo_copies[0].start()
    for copy in pads + [copy for m in near for copy in m]:
        copy.start()

    own_gains.wait()
    for copy in gain_copies:
        copy.wait_recv()
    gain_spread = [
        c.remote(gains_all.at[z], gains_all.at[z], tensor=(z + r) % depth) for r in range(1, depth)
    ]
    for copy in gain_spread:
        copy.start()

    tok_passed = []
    sibling = peer_of(me, 1)
    pass_tok = pass_on(c, tok.at[0], tok.at[1], z, depth, rows, sibling, tok_passed)

    line_step(tok_line, 1, pass_tok)
    for k in range(1, len(bits) - 1):
        qk_copies[k - 1].wait_recv()
        qk_copies[k].start()
        vo_copies[k - 1].wait_recv()
        vo_copies[k].start()
    own_grad.wait()
    grad_line = Line(c, grads_ref.at[0], z, depth, rows)
    for k in range(2, depth):
        line_step(tok_line, k, pass_tok)
    grad_line.begin()

    for copy in gain_spread:
        copy.wait_recv()
    for d in range(dp):
        total = gains_all[0, d]
        for t in range(1, depth):
            total = total + gains_all[t, d]
        gain_rows[:, d * slice_width : (d + 1) * slice_width] = total

    def norm_rows(s):
        def block(i, carry):
            at = pl.ds(pl.multiple_of(i * rows, rows), rows)
            data = tok[s, at, :].astype(F32)
            scale = lax.rsqrt(jnp.mean(data * data, axis=-1, keepdims=True) + EPS)
            fnorm[at, :] = (data * scale * gain_rows[0:1, :]).astype(BF)
            return carry

        lax.fori_loop(0, depth, block, 0)

    own_misc.wait()
    for copy in misc_copies:
        copy.wait_recv()
    router_out[...] = jnp.zeros_like(router_out)
    row = lax.broadcasted_iota(jnp.int32, misc_ref.shape, 0)
    for d in range(dp):
        block = jnp.where(row <= experts, misc_all[d], 0.0).astype(BF)
        router_out[: misc_ref.shape[0], d * slice_width : (d + 1) * slice_width] = block
    bias_in = jnp.zeros(misc_ref.shape, F32)
    sub = lax.broadcasted_iota(jnp.int32, misc_ref.shape, 0)
    for d in range(dp):
        bias_in = jnp.where(sub == d, misc_all[d, pl.ds(experts + 1 + core, 1), :], bias_in)
    bias_in = bias_in.astype(BF)
    heads3 = 3 * pair
    head_slice = head // dp
    lane = lax.broadcasted_iota(jnp.int32, (bias_in.shape[1], heads3), 1)
    sub = lax.broadcasted_iota(jnp.int32, (bias_in.shape[1], heads3), 0)
    place = (lane // head * head_slice + lane % head_slice == sub).astype(F32).astype(BF)
    spread = dot(bias_in, place)
    lane = lax.broadcasted_iota(jnp.int32, spread.shape, 1)
    sub = lax.broadcasted_iota(jnp.int32, spread.shape, 0)
    bias = jnp.sum(jnp.where(lane % head // head_slice == sub, spread, 0.0), axis=0, keepdims=True)

    qk_copies[-1].wait_recv()
    vo_copies[-1].wait_recv()
    for m in far:
        for copy in m:
            copy.start()
    for m, copy in zip(near, over_near):
        for part_copy in m:
            part_copy.wait()
        copy.start()
    pairs = pair // head

    def project(s):
        def block(i, carry):
            at = pl.ds(pl.multiple_of(i * 2 * rows, 2 * rows), 2 * rows)
            full = weights[...].reshape(width, 4 * pair)
            pre = dot(fnorm[at, :], full[:, : 3 * pair]) + bias
            cos_rows, sin_rows = cos_ref[at, :], sin_ref[at, :]
            for kind in range(3):
                for h in range(pairs):
                    a = (kind * pairs + h) * head
                    field = pre[:, a : a + head]
                    if kind < 2:
                        field = spin(field, cos_rows, sin_rows)
                    qkv_ref[kind, s * pairs + h, at, :] = field.astype(BF)
            return carry

        lax.fori_loop(0, depth // 2, block, 0)

    norm_rows(0)
    project(0)
    line_step(grad_line, 1)
    for copy in far[0]:
        copy.wait_recv()
    over[0].start()
    tok_pass[0].wait()
    for copy, there in tok_passed:
        pl.when(there)(copy.wait)
    norm_rows(1)
    project(1)

    own_codes.wait()
    for copy in first:
        copy.wait()
    causal_block = seq_len // 2

    def attend(s):
        flags = codes_all[s]
        sub = lax.broadcasted_iota(jnp.int32, flags.shape, 0)
        flags = jnp.where(sub == 8, flags, 0).astype(F32).astype(BF)
        for h in range(pairs):
            for b in range(2):
                at = slice(b * causal_block, (b + 1) * causal_block)
                seen = dot(flags[:, at], flags, 0, 0)
                row = lax.broadcasted_iota(jnp.int32, seen.shape, 0) + b * causal_block
                col = lax.broadcasted_iota(jnp.int32, seen.shape, 1)
                scores = dot(qkv_ref[0, s * pairs + h, at, :], qkv_ref[1, s * pairs + h], 1, 1)
                scores = scores * head ** (-0.5)
                scores = jnp.where(jnp.logical_or(col <= row, seen > 0.5), scores, -1e30)
                raised = jnp.exp(scores - jnp.max(scores, axis=1, keepdims=True))
                probs = raised / jnp.sum(raised, axis=1, keepdims=True)
                probs = probs.astype(BF)
                probs_ref[s * pairs + h, at, :] = probs
                mixed = dot(probs, qkv_ref[2, s * pairs + h])
                mix_ref[s, at, h * head : (h + 1) * head] = mixed.astype(BF)

    def project_out(s):
        for d in range(dp):
            index = tuple(d // bit % 2 for bit in reversed(bits))
            block = weights[index + (slice(None), slice(3 * pair, 4 * pair))]
            at = slice(d * slice_width, (d + 1) * slice_width)
            part[s, :, at] = dot(mix_ref[s], block, 1, 1).astype(BF)

    attend(1)
    if depth > 2:
        line_step(grad_line, 2)
    project_out(1)
    part_pass = c.remote(part.at[1], part_in, dp=peer_of(me, 1))
    part_pass.start()
    attend(0)
    project_out(0)
    part_pass.wait_recv()

    saved = [
        c.local(a, b)
        for a, b in (
            (tok, tok_out),
            (weights, weights_out),
            (qkv_ref, qkv_out),
            (probs_ref, probs_out),
            (mix_ref, mix_out),
        )
    ]
    for copy in saved:
        copy.start()
    scatter = []
    for r in list(range(1, depth)) + [0]:
        at = pl.ds(pl.multiple_of((z + r) % depth * rows, rows), rows)
        total = part[0, at, :].astype(F32) + part_in[at, :].astype(F32)
        if r:
            part[0, at, :] = total.astype(BF)
            copy = c.remote(part.at[0, at], scatter_in.at[r - 1], tensor=(z + r) % depth)
            copy.start()
            scatter.append(copy)
        else:
            hidden_ref[...] = total + tok[0, at, :].astype(F32)

    for k in range(3, depth):
        line_step(grad_line, k)
    x_grad = c.remote(grads_ref.at[0], grads_ref.at[2], dp=peer_of(me, 2))
    x_grad.start()
    own_pass = c.remote(grads_ref.at[0], grads_ref.at[1], dp=peer_of(me, 1))
    own_pass.start()
    for k in (1, 2):
        for copy in far[k]:
            copy.wait_recv()
        over[k].start()

    for copy in scatter:
        copy.wait_recv()
    total = hidden_ref[...]
    for r in range(1, depth):
        total = total + scatter_in[r - 1].astype(F32)
    hidden_ref[...] = total
    scale = lax.rsqrt(jnp.mean(total * total, axis=-1, keepdims=True) + EPS)
    norm_mine[...] = (total * scale * gain_rows[1:2, :]).astype(BF)
    norm_here = c.local(norm_mine, piece(norm_ref.at[0], z))
    norm_here.start()
    norm_here.wait()
    norm_line = Line(c, norm_ref.at[0], z, depth, rows)
    norm_line.begin()
    beside = peer_of(me, 2)
    norm_own = c.remote(piece(norm_ref.at[0], z), piece(norm_ref.at[1], z), dp=sibling)
    norm_far = c.remote(piece(norm_ref.at[0], z), piece(norm_ref.at[2], z), dp=beside)
    norm_far.start()
    norm_own.start()
    norm_passed, far_passed = [], []
    pass_norm = pass_on(
        c, norm_ref.at[0], norm_ref.at[1], z, depth, rows, sibling, norm_passed
    )
    pass_far = pass_on(c, norm_ref.at[0], norm_ref.at[2], z, depth, rows, beside, far_passed)

    def pass_both(k, up):
        pass_far(k, up)
        pass_norm(k, up)

    for k in range(1, depth):
        line_step(norm_line, k, pass_both)

    x_grad.wait_recv()
    grad_pass = c.remote(grads_ref.at[2], grads_ref.at[3], dp=peer_of(me, 1))
    grad_pass.start()
    for copy in over_near + over:
        copy.wait()
    norm_far.wait()
    for copy, there in far_passed:
        pl.when(there)(copy.wait)
    norm_pass = c.remote(norm_ref.at[2], norm_ref.at[3], dp=sibling)
    norm_pass.start()
    norm_own.wait()
    for copy, there in norm_passed:
        pl.when(there)(copy.wait)
    norm_pass.wait()
    own_pass.wait()
    grad_pass.wait()
    for line in (tok_line, grad_line, norm_line):
        line.finish()
    for copy in pads + saved:
        copy.wait()
    for copy in gain_copies + misc_copies + gain_spread + qk_copies + vo_copies + scatter:
        copy.wait_send()
    for copy in [part_pass, x_grad] + [y for m in far for y in m]:
        copy.wait_send()


def forward_call(dp, depth, experts, head, small, arrays, units):
    codes, misc, gains, cos_rows, sin_rows = small
    tokens, pair = arrays[0], arrays[2].shape[1] // 2
    rows, width = tokens.shape
    seq_len = rows * depth
    hidden_units = units[0].shape[1]
    hidden_pad = -(-hidden_units // 128) * 128
    routed = experts // 4
    bits = dp.bit_length() - 1
    pairs = pair // head
    vmem, hbm = pl.BlockSpec(memory_space=pltpu.VMEM), pl.BlockSpec(memory_space=pl.ANY)
    shape = jax.ShapeDtypeStruct
    return pl.pallas_call(
        functools.partial(forward_body, (dp, depth, experts, hidden_units, head)),
        in_specs=[vmem] * 5 + [hbm] * 12,
        out_specs=[vmem] + [hbm] * 4 + [vmem] * 3 + [hbm] * 5,
        out_shape=[
            shape((rows, width), F32),
            shape((4, seq_len, width), BF),
            shape((4, seq_len, width), BF),
            shape((routed + 1, 2, hidden_pad, width), BF),
            shape((routed + 1, 1, hidden_pad, width), BF),
            shape((4,) + codes.shape, codes.dtype),
            shape((128, width), BF),
            shape((8, width), F32),
            shape((2, seq_len, width), BF),
            shape((2,) * bits + (width // dp, 4 * pair), BF),
            shape((3, 2 * pairs, seq_len, head), BF),
            shape((2 * pairs, seq_len, seq_len), BF),
            shape((2, seq_len, pair), BF),
        ],
        scratch_shapes=[
            pltpu.VMEM((dp,) + misc.shape, F32),
            pltpu.VMEM((rows, width), BF),
            pltpu.VMEM((2, seq_len, width), BF),
            pltpu.VMEM((2,) * bits + (width // dp, 4 * pair), BF),
            pltpu.VMEM((3, 2 * pairs, seq_len, head), BF),
            pltpu.VMEM((2 * pairs, seq_len, seq_len), BF),
            pltpu.VMEM((2, seq_len, pair), BF),
            pltpu.VMEM((seq_len, width), BF),
            pltpu.VMEM((2, seq_len, width), BF),
            pltpu.VMEM((seq_len, width), BF),
            pltpu.VMEM((depth - 1, rows, width), BF),
            pltpu.VMEM((depth, dp) + gains.shape, F32),
            pltpu.VMEM((routed + 1, hidden_pad - hidden_units, width), BF),
            pltpu.SemaphoreType.DMA((160,)),
            pltpu.SemaphoreType.DMA((160,)),
            pltpu.SemaphoreType.DMA((40,)),
        ],
        compiler_params=pltpu.CompilerParams(
            collective_id=0, has_side_effects=True, vmem_limit_bytes=VMEM_LIMIT
        ),
    )(codes, misc, gains, cos_rows, sin_rows, *arrays, *units)


def backward_body(
    sizes,
    terms_ref,
    probs_mine_ref,
    router_ref,
    gain_rows,
    cos_ref,
    sin_ref,
    hidden_ref,
    outgrad_ref,
    grad_a_ref,
    grad_b_ref,
    grad_c_ref,
    gate_in_ref,
    gate_ref,
    up_ref,
    down_ref,
    tok_hbm,
    weights_hbm,
    qkv_hbm,
    probs_hbm,
    mix_hbm,
    norm_hbm,
    input_ref,
    gate_out,
    up_out,
    down_out,
    attn_out,
    misc_out,
    gains_out,
    own_sum,
    arrived,
    three,
    scatter_in,
    terms_sum,
    terms_in,
    back,
    tok,
    weights,
    qkv,
    probs_ref,
    mix_ref,
    scales,
    qkv_grad,
    part_in,
    keep,
    total_a,
    first_qk,
    first_vo,
    second_in,
    misc_part,
    misc_in,
    gains_in,
    vectors,
    send,
    recv,
    here,
):
    dp, depth, experts, head = sizes
    me, z = lax.axis_index("dp"), lax.axis_index("tensor")
    core, x, y = me % 2, (me // 2) % 2, me // 4
    rows, width = input_ref.shape
    seq_len = rows * depth
    slice_width = width // dp
    pair = mix_ref.shape[2]
    pairs = pair // head
    bits = [1, 2, 4]
    c = Copies(send, recv, here)

    greet(me, z, dp, depth)

    matrices = ((gate_ref, gate_out), (up_ref, up_out), (down_ref, down_out))
    over = [None]
    for m in (1, 2):
        other = matrices[m][0].at[pl.ds((1 - y) * 4, 4)]
        over.append(c.remote(other, arrived.at[m], dp=peer_of(me, 4)))
        over[m].start()
    gate_in = c.local(gate_in_ref, arrived.at[0])
    grads = (grad_a_ref, grad_b_ref, grad_c_ref)
    loads = [c.local(grads[k], three.at[k]) for k in range(3)]
    for copy in loads:
        copy.start()
    own_loads = [
        c.local(source.at[pl.ds(y * 4, 4)], own_sum) for source, _ in matrices
    ]
    inputs = [
        c.local(a, b)
        for a, b in (
            (weights_hbm, weights),
            (mix_hbm, mix_ref),
            (qkv_hbm, qkv),
            (probs_hbm, probs_ref),
            (tok_hbm, tok),
        )
    ]
    own_loads[0].start()
    gate_in.start()
    for copy in inputs:
        copy.start()

    def at_of(p):
        return pl.ds(pl.multiple_of(p * rows, rows), rows)

    for copy in loads:
        copy.wait()
    scatter, small = [], []
    for r in list(range(1, depth)) + [0]:
        at = at_of((z + r) % depth)
        total = three[0, at, :].astype(F32) + three[1, at, :].astype(F32)
        total = total + three[2, at, :].astype(F32)
        extra = terms_ref[0, at, :] + terms_ref[1, at, :] + terms_ref[2, at, :]
        if r:
            three[0, at, :] = total.astype(BF)
            terms_sum[at, :] = extra
            peer = (z + r) % depth
            scatter.append(c.remote(three.at[0, at], scatter_in.at[0, r - 1], tensor=peer))
            small.append(c.remote(terms_sum.at[at], terms_in.at[r - 1], tensor=peer))
            scatter[-1].start()
            small[-1].start()
        else:
            keep[0] = total
            terms_sum[at, :] = extra

    def add_over(m):
        own_loads[m].wait()
        if m:
            over[m].wait_recv()
        else:
            gate_in.wait()
        copies = []
        for r in (2, 3, 1, 0):
            k = peer_of(me, r) % 4
            for unit in range(own_sum.shape[1]):
                arrived[m, k, unit] = (
                    own_sum[k, unit].astype(F32) + arrived[m, k, unit].astype(F32)
                ).astype(BF)
            place = matrices[m][1].at[me % 4]
            if r:
                copies.append(c.remote(arrived.at[m, k], place, dp=peer_of(me, r)))
            else:
                copies.append(c.local(arrived.at[m, k], place))
            copies[-1].start()
        if m + 1 < len(own_loads):
            own_loads[m + 1].start()
        return copies

    units = add_over(0)
    for copy in scatter:
        copy.wait_recv()
    for copy in small:
        copy.wait_recv()
    route = terms_sum[at_of(z), :]
    grad = keep[0]
    for r in range(1, depth):
        grad = grad + scatter_in[0, r - 1].astype(F32)
        route = route + terms_in[r - 1]
    probs_mine = probs_mine_ref[...]
    lane = lax.broadcasted_iota(jnp.int32, route.shape, 1)
    inner = jnp.sum(jnp.where(lane < experts, probs_mine * route, 0.0), axis=1, keepdims=True)
    logits = jnp.where(
        lane < experts,
        probs_mine * (route - inner),
        jnp.where(lane == experts, route * probs_mine * (1.0 - probs_mine), 0.0),
    ).astype(BF)
    grad = grad + dot(logits, router_ref[...])
    hidden = hidden_ref[...]
    scale = lax.rsqrt(jnp.mean(hidden * hidden, axis=-1, keepdims=True) + EPS)
    unit = hidden * scale
    vectors[1:2, :] = jnp.sum(grad * unit, axis=0, keepdims=True)
    grad = grad * gain_rows[1:2, :]
    grad = outgrad_ref[...].astype(F32) + scale * (
        grad - unit * jnp.mean(grad * unit, axis=-1, keepdims=True)
    )
    keep[0] = grad
    back[0, at_of(z), :width] = grad.astype(BF)
    back[0, at_of(z), width:] = logits

    line = Line(c, back.at[0], z, depth, rows)
    line.begin()
    sibling = peer_of(me, 1)
    back_own = c.remote(piece_of(back.at[0], z, rows), piece_of(back.at[1], z, rows), dp=sibling)
    back_own.start()
    passed = []
    pass_back = pass_on(c, back.at[0], back.at[1], z, depth, rows, sibling, passed)
    for copy in scatter:
        copy.wait_send()
    line_step(line, 1, pass_back)

    for copy in inputs:
        copy.wait()

    def scale_rows(i, carry):
        at = at_of(i)
        for s in range(2):
            data = tok[s, at, :].astype(F32)
            scales[s, at, :] = lax.rsqrt(jnp.mean(data * data, axis=-1, keepdims=True) + EPS)
        return carry

    lax.fori_loop(0, depth, scale_rows, 0)
    line_step(line, 2, pass_back)
    units += add_over(1)
    line_step(line, 3, pass_back)
    back_own.wait()
    for copy, there in passed:
        pl.when(there)(copy.wait)
    def block_of(d):
        return tuple(d // bit % 2 for bit in reversed(bits))

    def slab(d):
        return slice(d * slice_width, (d + 1) * slice_width)

    def attention(s):
        mixed = jnp.zeros((seq_len, pair), F32)
        for d in range(dp):
            block = weights[block_of(d) + (slice(None), slice(3 * pair, 4 * pair))]
            mixed = mixed + dot(back[s, :, slab(d)], block)
        mixed = mixed.astype(BF)
        for h in range(pairs):
            n = s * pairs + h
            cot = mixed[:, h * head : (h + 1) * head]
            key_total = jnp.zeros((seq_len, head), F32)
            value_total = jnp.zeros((seq_len, head), F32)
            for b in range(2):
                at = slice(b * seq_len // 2, (b + 1) * seq_len // 2)
                p_low = probs_ref[n, at, :]
                p = p_low.astype(F32)
                p_grad = dot(cot[at], qkv[2, n], 1, 1)
                s_grad = p * (p_grad - jnp.sum(p * p_grad, axis=1, keepdims=True))
                s_grad = s_grad.astype(BF)
                q_grad = dot(s_grad, qkv[1, n]) * head ** (-0.5)
                q_grad = spin(q_grad, cos_ref[at, :], -sin_ref[at, :])
                qkv_grad[s, at, h * head : (h + 1) * head] = q_grad.astype(BF)
                key_total = key_total + dot(s_grad, qkv[0, n, at, :], 0, 0)
                value_total = value_total + dot(p_low, cot[at], 0, 0)
            k_grad = spin(key_total * head ** (-0.5), cos_ref[...], -sin_ref[...])
            a = pair + h * head
            qkv_grad[s, :, a : a + head] = k_grad.astype(BF)
            qkv_grad[s, :, a + pair : a + pair + head] = value_total.astype(BF)

    def first_grad(s):
        for d in range(dp):
            block = weights[block_of(d) + (slice(None), slice(0, 3 * pair))]
            total = dot(qkv_grad[s], block, 1, 1)
            three[1 + s, :, slab(d)] = total.astype(BF)
            unit_block = tok[s, :, slab(d)].astype(F32) * scales[s]
            row = jnp.sum(total * unit_block, axis=0, keepdims=True)
            vectors[2 + s : 3 + s, slab(d)] = row

    attention(1)
    first_grad(1)
    part_pass = c.remote(three.at[2], part_in, dp=sibling)
    part_pass.start()
    units += add_over(2)
    attention(0)
    first_grad(0)
    part_pass.wait_recv()
    first_scatter = []
    for r in list(range(1, depth)) + [0]:
        at = at_of((z + r) % depth)
        total = three[1, at, :].astype(F32) + part_in[at, :].astype(F32)
        if r:
            three[1, at, :] = total.astype(BF)
            peer = (z + r) % depth
            copy = c.remote(three.at[1, at], scatter_in.at[1, r - 1], tensor=peer)
            copy.start()
            first_scatter.append(copy)
        else:
            keep[1] = total

    for d in range(dp):
        total = jnp.zeros((slice_width, 3 * pair), F32)
        out_total = jnp.zeros((slice_width, pair), F32)
        for s in range(2):
            data = tok[s, :, slab(d)].astype(F32) * scales[s] * gain_rows[0:1, slab(d)]
            total = total + dot(data.astype(BF), qkv_grad[s], 0, 0)
            out_total = out_total + dot(back[s, :, slab(d)], mix_ref[s], 0, 0)
        total_a[block_of(d) + (slice(None), slice(0, 3 * pair))] = total.astype(BF)
        total_a[block_of(d) + (slice(None), slice(3 * pair, 4 * pair))] = out_total.astype(BF)

    half = 2 * pair

    def index(y_at, x_at, k):
        return (y_at, x_at, slice(None), slice(None), pl.ds(k * half, half))

    every = pl.ds(0, 2)
    qk_first = c.remote(
        total_a.at[index(pl.ds(1 - y, 1), every, 0)], first_qk, dp=peer_of(me, 4)
    )
    vo_first = c.remote(
        total_a.at[index(every, pl.ds(1 - x, 1), 1)], first_vo, dp=peer_of(me, 2)
    )
    qk_first.start()
    vo_first.start()

    norm_load = c.local(norm_hbm.at[0], three.at[0])
    norm_load.start()
    norm_load.wait()
    router_part = dot(back[0, :, width:], three[0], 0, 0)
    ones = jnp.ones((16, seq_len), BF)
    bias_row = dot(ones, qkv_grad[0]) + dot(ones, qkv_grad[1])
    lane = lax.broadcasted_iota(jnp.int32, bias_row.shape, 1)
    sub = lax.broadcasted_iota(jnp.int32, bias_row.shape, 0)
    head_slice = head // dp
    bias_rows = jnp.where(lane % head // head_slice == sub, bias_row, 0.0)
    high = bias_rows.astype(BF)
    low = (bias_rows - high.astype(F32)).astype(BF)
    lane = lax.broadcasted_iota(jnp.int32, (3 * pair, slice_width), 1)
    sub = lax.broadcasted_iota(jnp.int32, (3 * pair, slice_width), 0)
    place = (sub // head * head_slice + sub % head_slice == lane).astype(F32).astype(BF)
    bias_rows = dot(high, place) + dot(low, place)
    sub = lax.broadcasted_iota(jnp.int32, (16, slice_width), 0)
    misc_copies = []
    for d in range(dp):
        tile = jnp.where(sub <= experts, router_part[:16, slab(d)], 0.0)
        tile = jnp.where(sub == experts + 1 + core, bias_rows[d : d + 1], tile)
        gain_one = vectors[2:3, slab(d)] + vectors[3:4, slab(d)]
        tile = jnp.where(sub == experts + 3, gain_one, tile)
        tile = jnp.where(sub == experts + 4, vectors[1:2, slab(d)], tile)
        misc_part[d] = tile
    for r in range(1, dp):
        to = peer_of(me, r)
        misc_copies.append(c.remote(misc_part.at[to], misc_in.at[r - 1], dp=to))
        misc_copies[-1].start()

    qk_first.wait()
    mine = index(pl.ds(y, 1), every, 0)
    total_a[mine] = (total_a[mine].astype(F32) + first_qk[...].astype(F32)).astype(BF)
    qk_second = c.remote(
        total_a.at[index(pl.ds(y, 1), pl.ds(1 - x, 1), 0)], second_in.at[0], dp=peer_of(me, 2)
    )
    qk_second.start()
    vo_first.wait()
    mine = index(every, pl.ds(x, 1), 1)
    total_a[mine] = (total_a[mine].astype(F32) + first_vo[...].astype(F32)).astype(BF)
    vo_second = c.remote(
        total_a.at[index(pl.ds(1 - y, 1), pl.ds(x, 1), 1)], second_in.at[1], dp=peer_of(me, 4)
    )
    vo_second.start()

    total = misc_part[me]
    for r, copy in enumerate(misc_copies):
        copy.wait_recv()
        total = total + misc_in[r]
    misc_out[...] = total
    gain_copies = []
    for r in range(1, depth):
        peer = (z + r) % depth
        gain_copies.append(c.remote(misc_out.at[8:16], gains_in.at[r - 1], tensor=peer))
        gain_copies[-1].start()

    finals = []
    for k, copy in enumerate((qk_second, vo_second)):
        copy.wait()
        mine = (y, x, slice(None), slice(None), pl.ds(k * half, half))
        total_a[mine] = (
            total_a[mine].astype(F32) + second_in[k, 0, 0].astype(F32)
        ).astype(BF)
        for other in (True, False):
            to = 1 - core if other else core
            source = total_a.at[y, x, to, :, pl.ds(k * half, half)]
            place = attn_out.at[core, :, pl.ds(k * half, half)]
            finals.append(c.remote(source, place, dp=sibling) if other else c.local(source, place))
            finals[-1].start()

    for copy in first_scatter:
        copy.wait_recv()
    total = keep[1]
    for r in range(1, depth):
        total = total + scatter_in[1, r - 1].astype(F32)
    total = total * gain_rows[0:1, :]
    scale = scales[0, at_of(z), :]
    unit = tok[0, at_of(z), :].astype(F32) * scale
    total = keep[0] + scale * (total - unit * jnp.mean(total * unit, axis=-1, keepdims=True))
    input_ref[...] = total.astype(BF)

    total = misc_out[8:16, :]
    for r, copy in enumerate(gain_copies):
        copy.wait()
        total = total + gains_in[r]
    gains_out[...] = total
    for copy in finals + units:
        copy.wait()
    line.finish()
    for copy in over[1:] + small + first_scatter + misc_copies + [part_pass]:
        copy.wait_send()


def backward_call(dp, depth, experts, head, in_vmem, in_hbm):
    output_rows, width = in_vmem[6].shape
    seq_len = output_rows * depth
    slice_width = width // dp
    units = in_hbm[3].shape[1:]
    pair = in_hbm[11].shape[2]
    pairs = pair // head
    vmem, hbm = pl.BlockSpec(memory_space=pltpu.VMEM), pl.BlockSpec(memory_space=pl.ANY)
    shape = jax.ShapeDtypeStruct
    final = shape((4,) + units, BF)
    return pl.pallas_call(
        functools.partial(backward_body, (dp, depth, experts, head)),
        in_specs=[vmem] * len(in_vmem) + [hbm] * len(in_hbm),
        out_specs=[vmem, hbm, hbm, hbm, vmem, vmem, vmem],
        out_shape=[
            shape((output_rows, width), BF),
            final,
            final,
            final,
            shape((2, slice_width, 4 * pair), BF),
            shape((16, slice_width), F32),
            shape((8, slice_width), F32),
        ],
        scratch_shapes=[
            pltpu.VMEM((4,) + units, BF),
            pltpu.VMEM((3, 4) + units, BF),
            pltpu.VMEM((3, seq_len, width), BF),
            pltpu.VMEM((2, depth - 1, output_rows, width), BF),
            pltpu.VMEM((seq_len, 128), F32),
            pltpu.VMEM((depth - 1, output_rows, 128), F32),
            pltpu.VMEM((2, seq_len, width + 128), BF),
            pltpu.VMEM((2, seq_len, width), BF),
            pltpu.VMEM((2, 2, 2, slice_width, 4 * pair), BF),
            pltpu.VMEM((3, 2 * pairs, seq_len, head), BF),
            pltpu.VMEM((2 * pairs, seq_len, seq_len), BF),
            pltpu.VMEM((2, seq_len, pair), BF),
            pltpu.VMEM((2, seq_len, 1), F32),
            pltpu.VMEM((2, seq_len, 3 * pair), BF),
            pltpu.VMEM((seq_len, width), BF),
            pltpu.VMEM((2, output_rows, width), F32),
            pltpu.VMEM((2, 2, 2, slice_width, 4 * pair), BF),
            pltpu.VMEM((1, 2, 2, slice_width, 2 * pair), BF),
            pltpu.VMEM((2, 1, 2, slice_width, 2 * pair), BF),
            pltpu.VMEM((2, 1, 1, 2, slice_width, 2 * pair), BF),
            pltpu.VMEM((dp, 16, slice_width), F32),
            pltpu.VMEM((dp - 1, 16, slice_width), F32),
            pltpu.VMEM((depth - 1, 8, slice_width), F32),
            pltpu.VMEM((8, width), F32),
            pltpu.SemaphoreType.DMA((96,)),
            pltpu.SemaphoreType.DMA((96,)),
            pltpu.SemaphoreType.DMA((40,)),
        ],
        compiler_params=pltpu.CompilerParams(
            collective_id=1, has_side_effects=True, vmem_limit_bytes=62 * 2**20
        ),
    )(*in_vmem, *in_hbm)


def finish_body(
    gate_ref, up_ref, down_ref, attn_ref, eg_ref, eu_ref, ed_ref, sg_ref, su_ref, sd_ref,
    q_ref, k_ref, v_ref, o_ref, sg_rows, su_rows
):
    group, groups = pl.program_id(0), pl.num_programs(0)
    many, rows, _ = eg_ref.shape
    for source, routed, shared in (
        (gate_ref, eg_ref, sg_rows.at[group]),
        (up_ref, eu_ref, su_rows.at[group]),
        (down_ref, ed_ref, sd_ref),
    ):
        for unit in range(many):
            routed[unit] = source[0, unit].astype(F32)
        shared[...] = source[0, many].astype(F32)

    @pl.when(group == 0)
    def _():
        pair = attn_ref.shape[2] // 4
        for c in range(2):
            at = slice(c * pair, (c + 1) * pair)
            for kind, out_ref in enumerate((q_ref, k_ref, v_ref)):
                out_ref[:, at] = attn_ref[c, :, kind * pair : (kind + 1) * pair].astype(F32)
            o_ref[at, :] = jnp.transpose(attn_ref[c, :, 3 * pair :].astype(F32))

    @pl.when(group == groups - 1)
    def _():
        for source, out_ref in ((sg_rows, sg_ref), (su_rows, su_ref)):
            out_ref[...] = jnp.transpose(source[...].reshape(groups * rows, -1))


def finish_call(gate, up, down, attn):
    groups, units, rows, slice_width = gate.shape
    many, pair = units - 1, attn.shape[2] // 4
    shape = jax.ShapeDtypeStruct

    def whole(*dims):
        return pl.BlockSpec(dims, lambda g: (0,) * len(dims))

    source = pl.BlockSpec((1, units, rows, slice_width), lambda g: (g, 0, 0, 0))
    routed = pl.BlockSpec((many, rows, slice_width), lambda g: (g, 0, 0))
    return call(
        finish_body,
        (groups,),
        [source] * 3 + [whole(*attn.shape)],
        [routed] * 3
        + [whole(slice_width, groups * rows)] * 2
        + [pl.BlockSpec((rows, slice_width), lambda g: (g, 0))]
        + [whole(slice_width, 2 * pair)] * 3
        + [whole(2 * pair, slice_width)],
        [shape((groups * many, rows, slice_width), F32)] * 3
        + [shape((slice_width, groups * rows), F32)] * 2
        + [shape((groups * rows, slice_width), F32)]
        + [shape((slice_width, 2 * pair), F32)] * 3
        + [shape((2 * pair, slice_width), F32)],
        0,
        groups * units * rows * slice_width * 18,
        [pltpu.VMEM((groups, rows, slice_width), F32)] * 2,
    )(gate, up, down, attn)


def local_plain(
    dp,
    tokens,
    picture_ids,
    routes,
    slot_order,
    norm_gains,
    w_query,
    w_key,
    w_value,
    w_out,
    qkv_bias,
    router,
    shared_gate,
    shared_up,
    shared_down,
    expert_gate,
    expert_up,
    expert_down,
    out_grad,
):
    seq_len = picture_ids.shape[0]
    local_rows = tokens.shape[0]
    width = tokens.shape[1]
    experts, slice_width, hidden_units = expert_gate.shape
    top_count = routes.shape[1]
    capacity = 5 * seq_len * top_count // (4 * experts)
    heads_local = qkv_bias.shape[1]
    head_width = w_query.shape[1] // heads_local
    pair_heads = heads_local // 2
    pair_width = pair_heads * head_width
    mine_experts = experts // 4
    hidden_pad = -(-hidden_units // 128) * 128

    me = lax.axis_index("dp")
    zi = lax.axis_index("tensor")
    core, xi = me % 2, (me // 2) % 2
    group = me % 4
    bits = []
    while 2 ** (len(bits) + 1) <= dp:
        bits.append(2 ** len(bits))
    upper = bits[2:]

    def swap(array, bit):
        return lax.ppermute(array, "dp", [(i, i ^ bit) for i in range(dp)])

    def bit_of(bit):
        return (me // bit) % 2

    def join(mine, theirs, bit, axis):
        n = mine.shape[axis]
        shape = list(mine.shape)
        shape[axis] = 2 * n
        out = jnp.zeros(shape, mine.dtype)
        out = lax.dynamic_update_slice_in_dim(out, mine, n * bit_of(bit), axis)
        return lax.dynamic_update_slice_in_dim(out, theirs, n * (1 - bit_of(bit)), axis)

    def half(array, which, axis):
        n = array.shape[axis] // 2
        return lax.dynamic_slice_in_dim(array, which * n, n, axis)

    gains_z = lax.all_gather(norm_gains, "tensor", axis=1, tiled=True)
    misc_rows = 16
    bias_width = 3 * pair_heads * qkv_bias.shape[2]
    bias_cores = qkv_bias.reshape(3, 2, -1).swapaxes(0, 1).reshape(2, bias_width)

    def misc_pack(core_bias):
        wide = jnp.zeros((misc_rows, 2 * pair_width), BF)
        wide = wide.at[: experts + 1, :slice_width].set(router.T)
        wide = wide.at[experts + 1, :bias_width].set(core_bias)
        return wide.at[experts + 2 : experts + 4, :slice_width].set(gains_z)

    qk = jnp.concatenate(
        [w.reshape(slice_width, 2, pair_width) for w in (w_query, w_key)], axis=2
    )
    qk = jnp.concatenate(
        [qk, jnp.stack([misc_pack(bias_cores[0]), misc_pack(bias_cores[1])], axis=1)], axis=0
    )
    vo = jnp.concatenate(
        [w.reshape(slice_width, 2, pair_width) for w in (w_value, w_out.T)], axis=2
    )
    tokens_z = lax.all_gather(tokens, "tensor", axis=0, tiled=True)

    def gather_attention(pack, order):
        dims = (1,) * len(bits[1:])
        both = join(pick(pack, core, 1)[None], swap(pick(pack, 1 - core, 1), 1)[None], 1, 0)
        both = both.reshape(dims + both.shape)
        for bit in order:
            axis = len(bits) - 1 - bits.index(bit)
            both = join(both, swap(both, bit), bit, axis)
        return both.reshape((dp,) + both.shape[-2:])

    qk_all = gather_attention(qk, bits[1:])
    vo_full = gather_attention(vo, bits[:0:-1]).reshape(width, 2 * pair_width)
    qk_full = qk_all[:, :slice_width].reshape(width, 2 * pair_width)
    misc = qk_all[:, slice_width:]
    router_full = misc[:, : experts + 1, :slice_width].swapaxes(1, 2).reshape(width, -1)
    gain_rows = misc[:, experts + 2 : experts + 4, :slice_width].swapaxes(0, 1)
    gain_rows = gain_rows.reshape(2, width).astype(F32)
    bias = misc[:, experts + 1, :bias_width].astype(F32)
    bias = bias.reshape(dp, 3 * pair_heads, -1).swapaxes(0, 1).reshape(3, pair_width)

    tokens_sib = swap(tokens_z, 1)
    grad_z = lax.all_gather(out_grad, "tensor", axis=0, tiled=True)

    codes = jnp.concatenate([routes, slot_order], axis=1).T
    codes_x = swap(codes, 2)
    both_codes = swap(jnp.stack([codes, codes_x]), 1)
    codes_a = jnp.stack([codes, both_codes[0]])
    codes_b = jnp.stack([codes_x, both_codes[1]])
    pictures = jnp.stack([picture_ids, swap(picture_ids, 1)])

    def core_units(routed, shared):
        routed = routed.reshape(2, 2, mine_experts, hidden_units, slice_width)
        shared = shared.reshape(2, 2, 1, hidden_units, slice_width)

        def cut(which):
            return jnp.concatenate([pick(routed, which, 1), pick(shared, which, 1)], axis=1)

        return join(cut(core), swap(cut(1 - core), 1), 1, 3)

    def x_units(held):
        return join(pick(held, xi, 0), swap(pick(held, 1 - xi, 0), 2), 2, 2)

    def upper_units(held):
        for bit in upper[:-1]:
            held = join(held, swap(held, bit), bit, 2)
        return held, swap(held, upper[-1])

    def padded(*pairs):
        n = pairs[0][0].shape[-1]
        out = jnp.zeros((mine_experts + 1, len(pairs) * hidden_pad, 2 * n), BF)
        zero = jnp.int32(0)
        for k, (mine, theirs) in enumerate(pairs):
            row = jnp.int32(k * hidden_pad)
            out = lax.dynamic_update_slice(out, mine, (zero, row, n * bit_of(upper[-1])))
            out = lax.dynamic_update_slice(out, theirs, (zero, row, n * (1 - bit_of(upper[-1]))))
        return out

    down_c = core_units(expert_down, shared_down)
    gate_c = core_units(expert_gate.swapaxes(1, 2), shared_gate.T)
    up_c = core_units(expert_up.swapaxes(1, 2), shared_up.T)
    down_x = x_units(down_c)
    gate_x = x_units(gate_c)
    up_x = x_units(up_c)
    grad_x = swap(after(grad_z, up_x), 2)
    down_y = upper_units(down_x)
    gate_y = upper_units(gate_x)
    up_y = upper_units(up_x)

    rows_f = jnp.stack([tokens_z, tokens_sib]).astype(F32)
    qk_full = after(qk_full, down_c, gate_c, up_c)
    first_scale = lax.rsqrt(jnp.mean(rows_f * rows_f, axis=-1, keepdims=True) + EPS)
    first_norm = (rows_f * first_scale * gain_rows[0]).astype(BF)
    qk_pre = einsum("std,df->stf", first_norm, qk_full) + jnp.concatenate([bias[0], bias[1]])
    values = (einsum("std,df->stf", first_norm, vo_full[:, :pair_width]) + bias[2]).astype(BF)
    cos_part, sin_part = rope_tables(seq_len, head_width)
    qk_rot = rotate(
        qk_pre.reshape(2, seq_len, 2 * pair_heads, head_width), cos_part, sin_part
    ).astype(BF)
    qk_rot = after(qk_rot, down_x)
    queries, keys = qk_rot[:, :, :pair_heads], qk_rot[:, :, pair_heads:]
    values = values.reshape(2, seq_len, pair_heads, head_width)
    positions = jnp.arange(seq_len, dtype=jnp.int32)
    allowed = jnp.logical_or(
        positions[None, None, :] <= positions[None, :, None],
        pictures[:, :, None] * pictures[:, None, :] > 0,
    )
    score_scale = head_width ** (-0.5)
    scores = einsum("sqhd,skhd->shqk", queries, keys) * score_scale
    scores = jnp.where(allowed[:, None], scores, -1e30)
    weights = jnp.exp(scores - jnp.max(scores, axis=-1, keepdims=True))
    probs = weights / jnp.sum(weights, axis=-1, keepdims=True)
    probs_low = probs.astype(BF)
    head_mix = einsum("shqk,skhd->sqhd", probs_low, values).astype(BF)
    heads_out = after(head_mix.reshape(2, seq_len, pair_width), gate_x)
    out_weight = vo_full[:, pair_width:]
    attn_part = einsum("sqf,df->sqd", heads_out, out_weight)

    def core_sum(own, sibling):
        return own + swap(sibling.astype(BF), 1).astype(F32)

    def z_scatter(array):
        return lax.psum_scatter(
            array.astype(BF), "tensor", scatter_dimension=0, tiled=True
        ).astype(F32)

    inputs = tokens.astype(F32)
    hidden = inputs + z_scatter(core_sum(attn_part[0], attn_part[1]))
    hidden = after(hidden, up_x, down_y[1])
    second_scale = lax.rsqrt(jnp.mean(hidden * hidden, axis=-1, keepdims=True) + EPS)
    second_unit = hidden * second_scale
    second_norm = (second_unit * gain_rows[1]).astype(BF)
    norm_z = lax.all_gather(second_norm, "tensor", axis=0, tiled=True)
    norm_z = after(norm_z, gate_y[1], grad_x)
    down_all = padded(down_y)
    gateup_all = padded(gate_y, up_y)

    norm_x = swap(norm_z, 2)
    norm_a = jnp.stack([norm_z, swap(norm_z, 1)])
    norm_b = jnp.stack([norm_x, swap(norm_x, 1)])
    grad_a = jnp.stack([grad_z, swap(grad_z, 1)])
    grad_b = jnp.stack([grad_x, swap(grad_x, 1)])

    expert_ids = group * mine_experts + jnp.arange(mine_experts, dtype=jnp.int32)

    router_rows = jnp.pad(router_full.T, ((0, 16 - experts - 1), (0, 0)))
    group_ids = group.astype(jnp.int32).reshape(1)

    def slots_of(codes_in):
        routes_in, slots_in = codes_in[:, None, :top_count], codes_in[:, None, top_count:]
        matches = routes_in == expert_ids[None, :, None, None]
        return jnp.max(jnp.where(matches, slots_in, -1), axis=2)

    def feed(slots, rows, grads):
        slotted, slot_grad, pair, act, terms, pair_s, act_s, inner_s, probs_out = plain_act_call(
            experts, capacity, group_ids, slots, rows, grads, router_rows, gateup_all, down_all
        )
        terms = jnp.concatenate([terms.swapaxes(1, 2), inner_s], axis=-1)
        flat = [a.reshape(mine_experts, -1, a.shape[-1]) for a in (slotted, slot_grad, pair, act)]
        shared = [a.reshape(1, -1, a.shape[-1]) for a in (rows, grads, pair_s, act_s)]
        return (pair, pair_s), (act, act_s), terms, (flat, shared), probs_out

    slots_a, slots_b = slots_of(codes_a), slots_of(codes_b)
    fed_a = feed(slots_a, norm_a, grad_a)
    fed_b = feed(slots_b, norm_b, grad_b)
    columns_a, columns_b = slots_a[..., None], slots_b[..., None]
    row_grad_b = plain_back_call(columns_b, *fed_b[0], gateup_all)
    row_grad_a = plain_back_call(after(columns_a, row_grad_b), *fed_a[0], gateup_all)
    row_out_b = plain_back_call(after(columns_b, row_grad_a), *fed_b[1], down_all)
    row_out_a = plain_back_call(columns_a, *fed_a[1], down_all)

    def spread(terms):
        wide = jnp.zeros(terms.shape[:-1] + (128,), F32)
        wide = lax.dynamic_update_slice_in_dim(
            wide, terms[..., :mine_experts], group * mine_experts, terms.ndim - 1
        )
        return wide.at[..., experts].set(terms[..., mine_experts])

    def group_sum(a, b):
        across = b[0].astype(F32) + swap(b[1].astype(BF), 1).astype(F32)
        near = a[0].astype(F32) + swap(a[1].astype(BF), 1).astype(F32)
        return near + swap(across.astype(BF), 2).astype(F32)

    grad_sum = group_sum(row_grad_a, row_grad_b)
    term_sum = group_sum(spread(fed_a[2]), spread(fed_b[2]))
    packed = z_scatter(jnp.concatenate([grad_sum, term_sum], axis=-1))
    second_grad, gate_sums = packed[:, :width], packed[:, width:]

    data_a, data_b = fed_a[3], fed_b[3]

    def unit_grads(left, right):
        return jnp.concatenate(
            [
                plain_outer_call(
                    hidden_units,
                    hidden_pad,
                    dp,
                    [(data[k][left], data[k][right]) for data in (data_a, data_b)],
                )
                for k in range(2)
            ],
            axis=1,
        )

    def scatter_units(total):
        total = total.reshape((2,) * len(bits) + total.shape[1:])
        for bit in reversed(upper):
            axis = len(bits) - 1 - bits.index(bit)
            sent = half(total, 1 - bit_of(bit), axis)
            kept = half(total, bit_of(bit), axis)
            total = (kept.astype(F32) + swap(sent, bit).astype(F32)).astype(BF)
        total = total.reshape((2, 2) + total.shape[len(bits) :])
        held = join(pick(total, xi, 0)[None], swap(pick(total, 1 - xi, 0), 2)[None], 2, 0)
        return join(pick(held, core, 1)[:, None], swap(pick(held, 1 - core, 1), 1)[:, None], 1, 1)

    def split_units(held):
        routed = held[:, :, :mine_experts].reshape(experts, -1, slice_width)
        shared = held[:, :, mine_experts]
        return routed.astype(F32), shared.astype(F32)

    gateup_sum = scatter_units(unit_grads(2, 0))
    down_sum = scatter_units(unit_grads(3, 1))
    routed_gu, shared_gu = split_units(gateup_sum)
    routed_down, shared_down_sum = split_units(down_sum)
    shared_gu = shared_gu.reshape(4, 2, hidden_units, slice_width)
    egate_sum = routed_gu[:, :hidden_units].swapaxes(1, 2)
    eup_sum = routed_gu[:, hidden_units:].swapaxes(1, 2)
    sgate_sum = shared_gu[:, 0].reshape(-1, slice_width).T
    sup_sum = shared_gu[:, 1].reshape(-1, slice_width).T
    sdown_sum = shared_down_sum.reshape(-1, slice_width)

    row_start = zi * local_rows
    probs_local = lax.dynamic_slice_in_dim(fed_a[4][0], row_start, local_rows, 1).T
    probs_mine, weight_mine = probs_local[:, :experts], probs_local[:, experts]
    route_grad = gate_sums[:, :experts]
    expert_logit_grad = probs_mine * (
        route_grad - jnp.sum(probs_mine * route_grad, axis=-1, keepdims=True)
    )
    weight_logit_grad = gate_sums[:, experts] * weight_mine * (1.0 - weight_mine)
    logits_grad = jnp.concatenate([expert_logit_grad, weight_logit_grad[:, None]], axis=1).astype(
        BF
    )
    second_grad = second_grad + einsum("tf,df->td", logits_grad, router_full)
    gain_two_grad = jnp.sum(second_grad * second_unit, axis=0)
    unit_two = second_grad * gain_rows[1]
    hidden_grad = out_grad.astype(F32) + second_scale * (
        unit_two - second_unit * jnp.mean(unit_two * second_unit, axis=-1, keepdims=True)
    )
    attention_grad = hidden_grad.astype(BF)
    wide_logits = jnp.pad(logits_grad, ((0, 0), (0, 128 - experts - 1)))
    back_z = lax.all_gather(
        jnp.concatenate([attention_grad, wide_logits], axis=1), "tensor", axis=0, tiled=True
    )
    out_sum = after(group_sum(row_out_a, row_out_b), back_z)
    output = (hidden + z_scatter(out_sum)).astype(BF)
    logits_z = back_z[:, width : width + 16]
    back_own = back_z[:, :width]
    back_rows = jnp.stack([back_own, swap(back_own, 1)])

    router_part = einsum("tf,td->fd", logits_z, norm_z)[: experts + 1]

    out_proj = einsum("std,stf->df", back_rows, heads_out)
    mix_grad = einsum("std,df->stf", back_rows, out_weight).astype(BF)
    mix_grad = mix_grad.reshape(2, seq_len, pair_heads, head_width)
    prob_grad = einsum("sqhd,skhd->shqk", mix_grad, values)
    score_grad = (
        probs * (prob_grad - jnp.sum(probs * prob_grad, axis=-1, keepdims=True))
    ).astype(BF)
    query_rot = einsum("shqk,skhd->sqhd", score_grad, keys) * score_scale
    key_rot = einsum("shqk,sqhd->skhd", score_grad, queries) * score_scale
    value_grad = einsum("shqk,sqhd->skhd", probs_low, mix_grad)
    qk_grad = rotate(jnp.concatenate([query_rot, key_rot], axis=2), cos_part, -sin_part)
    qk_grad = qk_grad.astype(BF).reshape(2, seq_len, 2 * pair_width)
    v_grad = value_grad.astype(BF).reshape(2, seq_len, pair_width)
    first_part = einsum("stf,df->std", qk_grad, qk_full) + einsum(
        "stf,df->std", v_grad, vo_full[:, :pair_width]
    )
    first_grad = z_scatter(core_sum(first_part[0], first_part[1]))

    gain_one_grad = jnp.sum(first_part * (rows_f * first_scale), axis=(0, 1))
    bias_part = jnp.concatenate(
        [jnp.sum(qk_grad.astype(F32), axis=(0, 1)), jnp.sum(v_grad.astype(F32), axis=(0, 1))]
    )
    bias_part = bias_part.reshape(3 * pair_heads, dp, -1).swapaxes(0, 1).reshape(dp, 1, -1)
    gain_part = jnp.stack([gain_one_grad, gain_two_grad]).reshape(2, dp, slice_width)

    def wide_rows(rows):
        return jnp.pad(rows, ((0, 0), (0, 0), (0, 2 * pair_width - rows.shape[2])))

    misc_part = jnp.concatenate(
        [
            wide_rows(router_part.reshape(experts + 1, dp, slice_width).swapaxes(0, 1)),
            wide_rows(bias_part),
            wide_rows(gain_part.swapaxes(0, 1)),
            jnp.zeros((dp, misc_rows - experts - 4, 2 * pair_width), F32),
        ],
        axis=1,
    )
    qk_total = einsum("std,stf->df", first_norm, qk_grad).reshape(dp, slice_width, -1)
    qk_total = jnp.concatenate([qk_total, misc_part], axis=1)
    vo_total = jnp.concatenate([einsum("std,stf->df", first_norm, v_grad), out_proj], axis=1)
    vo_total = vo_total.reshape(dp, slice_width, -1)

    def scatter_attention(total, order):
        total = total.reshape((2,) * len(bits) + total.shape[1:])
        for bit in order:
            axis = len(bits) - 1 - bits.index(bit)
            sent = half(total, 1 - bit_of(bit), axis).astype(BF)
            total = half(total, bit_of(bit), axis) + swap(sent, bit).astype(F32)
        total = total.reshape((2,) + total.shape[-2:]).astype(BF)
        return pick(total, core, 0), swap(pick(total, 1 - core, 0), 1)

    def columns_of(mine, theirs):
        held = join(mine[:slice_width, None], theirs[:slice_width, None], 1, 1)
        first, second = held[..., :pair_width], held[..., pair_width:]
        return (
            first.reshape(slice_width, -1).astype(F32),
            second.reshape(slice_width, -1).astype(F32),
        )

    qk_mine, qk_theirs = scatter_attention(qk_total, bits[:0:-1])
    vo_mine, vo_theirs = scatter_attention(vo_total, bits[1:])
    qk_sums = columns_of(qk_mine, qk_theirs)
    vo_sums = columns_of(vo_mine, vo_theirs)
    misc_mine = qk_mine[slice_width:].astype(F32)
    misc_theirs = qk_theirs[slice_width:].astype(F32)
    misc_sum = misc_mine + misc_theirs
    router_sum = misc_sum[: experts + 1, :slice_width].T
    bias_sums = join(
        misc_mine[experts + 1, :bias_width].reshape(3, 1, pair_heads, -1),
        misc_theirs[experts + 1, :bias_width].reshape(3, 1, pair_heads, -1),
        1,
        1,
    ).reshape(3, heads_local, -1)
    gain_sums = lax.all_gather(
        misc_sum[experts + 2 : experts + 4, :slice_width], "tensor", axis=0, tiled=False
    )
    tensor = gain_sums.shape[0]
    gain_sums = jnp.sum(gain_sums, axis=0).reshape(2, tensor, -1)
    gain_sums = pick(gain_sums, zi, 1)

    unit_mine = inputs * lax.rsqrt(jnp.mean(inputs * inputs, axis=-1, keepdims=True) + EPS)
    scale_mine = lax.rsqrt(jnp.mean(inputs * inputs, axis=-1, keepdims=True) + EPS)
    unit_one = first_grad * gain_rows[0]
    input_grad = hidden_grad + scale_mine * (
        unit_one - unit_mine * jnp.mean(unit_one * unit_mine, axis=-1, keepdims=True)
    )
    return (
        output,
        input_grad.astype(BF),
        gain_sums,
        qk_sums[0],
        qk_sums[1],
        vo_sums[0],
        vo_sums[1].T,
        bias_sums,
        router_sum,
        sgate_sum,
        sup_sum,
        sdown_sum,
        egate_sum,
        eup_sum,
        routed_down,
    )


def local_fused(
    dp,
    depth,
    tokens,
    picture_ids,
    routes,
    slot_order,
    norm_gains,
    w_query,
    w_key,
    w_value,
    w_out,
    qkv_bias,
    router,
    shared_gate,
    shared_up,
    shared_down,
    expert_gate,
    expert_up,
    expert_down,
    out_grad,
):
    seq_len = picture_ids.shape[0]
    local_rows = tokens.shape[0]
    width = tokens.shape[1]
    experts, slice_width, hidden_units = expert_gate.shape
    top_count = routes.shape[1]
    capacity = 5 * seq_len * top_count // (4 * experts)
    heads_local = qkv_bias.shape[1]
    head_width = w_query.shape[1] // heads_local
    pair_heads = heads_local // 2
    pair_width = pair_heads * head_width
    mine_experts = experts // 4
    hidden_pad = -(-hidden_units // 128) * 128

    me = lax.axis_index("dp")
    zi = lax.axis_index("tensor")
    core, xi = me % 2, (me // 2) % 2
    group = me % 4
    def swap(array, bit):
        return lax.ppermute(array, "dp", [(i, i ^ bit) for i in range(dp)])

    codes = jnp.concatenate([routes.T, slot_order.T, picture_ids[None]], axis=0)
    codes = jnp.pad(codes, ((0, 16 - codes.shape[0]), (0, 0)))
    bias_cores = qkv_bias.reshape(3, 2, -1).swapaxes(0, 1).reshape(2, -1)
    bias_width = bias_cores.shape[1]
    misc = jnp.zeros((16, slice_width), F32)
    misc = misc.at[: experts + 1].set(router.T.astype(F32))
    misc = misc.at[experts + 1 : experts + 3, :bias_width].set(bias_cores.astype(F32))
    gains = lax.dynamic_update_slice(
        jnp.zeros((8, slice_width), F32),
        norm_gains.astype(F32),
        (jnp.int32(0), zi * norm_gains.shape[1]),
    )
    cos_part, sin_part = rope_tables(seq_len, head_width)
    cos_rows = jnp.concatenate([cos_part, cos_part], axis=1)
    sin_rows = jnp.concatenate([-sin_part, sin_part], axis=1)
    (
        hidden,
        norm_all,
        grads_all,
        gateup_all,
        down_all,
        codes_all,
        router_rows,
        gain_rows,
        tok,
        attn_weights,
        qkv,
        probs_low,
        heads_out,
    ) = forward_call(
        dp,
        depth,
        experts,
        head_width,
        (codes, misc, gains, cos_rows, sin_rows),
        (tokens, out_grad, w_query, w_key, w_value, w_out.T),
        (
            expert_gate.swapaxes(1, 2),
            expert_up.swapaxes(1, 2),
            expert_down,
            shared_gate.T.reshape(4, hidden_units, slice_width),
            shared_up.T.reshape(4, hidden_units, slice_width),
            shared_down.reshape(4, hidden_units, slice_width),
        ),
    )
    gateup_all = gateup_all.reshape(mine_experts + 1, 2 * hidden_pad, width)
    down_all = down_all.reshape(mine_experts + 1, hidden_pad, width)
    group_ids = group.astype(jnp.int32).reshape(1)

    def feed(chunk, group_in):
        return act_call(
            experts,
            top_count,
            chunk,
            group_in,
            codes_all,
            norm_all,
            grads_all,
            router_rows,
            gateup_all,
            down_all,
        )

    def across(own, sibling):
        total = own.astype(F32) + swap(sibling, 1).astype(F32)
        return total.astype(own.dtype)

    units = mine_experts + 1
    pair_b, act_b, terms_b, _ = feed(1, group_ids)
    out_b = back_call(act_b, down_all)
    grad_b = back_call(after(pair_b, out_b[0]), gateup_all)
    out_far = across(*out_b)
    pair_a, act_a, terms_a, probs_out = feed(0, after(group_ids, out_far, grad_b[0]))
    grad_far = across(*grad_b)
    terms_far = swap(across(terms_b[0], terms_b[1]), 2)
    out_a = back_call(after(act_a, grad_far, terms_far), down_all)
    gate_total, up_total = units_call(
        hidden_units, hidden_pad, dp, units, after(pair_a, out_a[0]), pair_b, norm_all
    )
    gate_sent = lax.dynamic_slice_in_dim(gate_total, (1 - me // 4) * 4, 4, 0)
    gate_in = swap(gate_sent, 4)
    out_sum = out_a[0].astype(F32) + swap(out_a[1], 1).astype(F32) + swap(out_far, 2).astype(F32)
    grad_a = back_call(after(pair_a, gate_sent), gateup_all)
    (down_total,) = units_call(
        hidden_units, hidden_pad, dp, units, act_a, after(act_b, grad_a[0], out_sum), grads_all
    )
    output = hidden + lax.dynamic_slice_in_dim(out_sum, zi * local_rows, local_rows, 0)
    for r in range(1, depth):
        start = (zi + r) % depth * local_rows
        sent = lax.dynamic_slice_in_dim(out_sum, start, local_rows, 0).astype(BF)
        moved = lax.ppermute(sent, "tensor", [(i, (i + r) % depth) for i in range(depth)])
        output = output + moved.astype(F32)
    output = output.astype(BF)
    grad_parts = (grad_a[0], swap(grad_a[1], 1), swap(grad_far, 2))
    terms = jnp.stack([terms_a[0], swap(terms_a[1], 1), terms_far])
    probs_mine = lax.dynamic_slice_in_dim(probs_out[0], zi * local_rows, local_rows, 0)
    input_grad, gate_sum, up_sum, down_sum, attn_sum, misc_sum, gains_sum = backward_call(
        dp,
        depth,
        experts,
        head_width,
        (after(terms, output), probs_mine, router_rows, gain_rows, cos_rows, sin_rows, hidden, out_grad),
        grad_parts
        + (gate_in, gate_total, up_total, down_total)
        + (tok, attn_weights, qkv, probs_low, heads_out, norm_all),
    )

    egate_sum, eup_sum, edown_sum, sgate_sum, sup_sum, sdown_sum, *attn_sums = finish_call(
        gate_sum, up_sum, down_sum, attn_sum
    )
    bias_sums = misc_sum[experts + 1 : experts + 3, :bias_width].reshape(2, 3, pair_heads, -1)
    bias_sums = bias_sums.swapaxes(0, 1).reshape(3, heads_local, -1)
    piece = norm_gains.shape[1]
    gain_sums = lax.dynamic_slice(gains_sum[3:5], (jnp.int32(0), zi * piece), (2, piece))
    return (
        output,
        input_grad,
        gain_sums,
        *attn_sums,
        bias_sums,
        misc_sum[: experts + 1].T,
        sgate_sum,
        sup_sum,
        sdown_sum,
        egate_sum.swapaxes(1, 2),
        eup_sum.swapaxes(1, 2),
        edown_sum,
    )


def solution(mesh):
    dp, depth = mesh.shape["dp"], mesh.shape["tensor"]

    def body(*arrays):
        if arrays[5].shape[0] % 128 == 0 and dp == 8 and depth == 4:
            return local_fused(dp, depth, *arrays)
        return local_plain(dp, *arrays)

    return jax.shard_map(
        body,
        mesh=mesh,
        in_specs=(
            P(("dp", "tensor"), None),
            P("dp"),
            P("dp", None),
            P("dp", None),
            P(None, ("dp", "tensor")),
            P("dp", "tensor"),
            P("dp", "tensor"),
            P("dp", "tensor"),
            P("tensor", "dp"),
            P(None, "tensor", "dp"),
            P("dp", None),
            P("dp", "tensor"),
            P("dp", "tensor"),
            P("tensor", "dp"),
            P(None, "dp", "tensor"),
            P(None, "dp", "tensor"),
            P(None, "tensor", "dp"),
            P(("dp", "tensor"), None),
        ),
        out_specs=(
            P(("dp", "tensor"), None),
            P(("dp", "tensor"), None),
            P(None, ("dp", "tensor")),
            P("dp", "tensor"),
            P("dp", "tensor"),
            P("dp", "tensor"),
            P("tensor", "dp"),
            P(None, "tensor", "dp"),
            P("dp", None),
            P("dp", "tensor"),
            P("dp", "tensor"),
            P("tensor", "dp"),
            P(None, "dp", "tensor"),
            P(None, "dp", "tensor"),
            P(None, "tensor", "dp"),
        ),
        check_vma=False,
    )
```

```python
import functools

import jax
import jax.numpy as jnp
from jax import lax
from jax.experimental import pallas as pl
from jax.experimental.pallas import tpu as pltpu
from jax.sharding import PartitionSpec as P

EPS = 1e-06
THETA = 1000000.0
BF = jnp.bfloat16
F32 = jnp.float32


def rope_tables(length, width):
    half_width = width // 2
    inverse = THETA ** (-(2.0 * jnp.arange(half_width, dtype=F32)) / width)
    angles = jnp.arange(length, dtype=F32)[:, None] * inverse[None, :]
    return jnp.cos(angles), jnp.sin(angles)


def rotate(field_in, cos_part, sin_part):
    half_width = field_in.shape[-1] // 2
    low, high = field_in[..., :half_width], field_in[..., half_width:]
    cos_rows, sin_rows = cos_part[:, None, :], sin_part[:, None, :]
    return jnp.concatenate(
        [low * cos_rows - high * sin_rows, high * cos_rows + low * sin_rows], axis=-1
    )


def einsum(spec, *args):
    return jnp.einsum(spec, *args, preferred_element_type=F32)


def silu_parts(gate_in):
    gate_sig = jax.nn.sigmoid(gate_in)
    return gate_in * gate_sig, gate_sig * (1.0 + gate_in * (1.0 - gate_sig))


def after(array, *others):
    return lax.optimization_barrier((array,) + others)[0]


def pick(array, index, axis):
    return lax.dynamic_index_in_dim(array, index, axis, keepdims=False)


VMEM_LIMIT = 58 * 2**20


def dot(left, right, left_dim=1, right_dim=0):
    return lax.dot_general(
        left, right, (((left_dim,), (right_dim,)), ((), ())), preferred_element_type=F32
    )


def call(body, grid, in_specs, out_specs, out_shape, flops, moved, scratch=()):
    return pl.pallas_call(
        body,
        grid=grid,
        in_specs=in_specs,
        out_specs=out_specs,
        out_shape=out_shape,
        scratch_shapes=scratch,
        cost_estimate=pl.CostEstimate(flops=flops, bytes_accessed=moved, transcendentals=0),
        compiler_params=pltpu.CompilerParams(vmem_limit_bytes=VMEM_LIMIT),
    )


def plain_act_body(
    experts,
    units,
    group_ref,
    slot_ref,
    rows_ref,
    grads_ref,
    router_ref,
    gateup_ref,
    down_ref,
    slotted_ref,
    slotgrad_ref,
    pair_ref,
    act_ref,
    terms_ref,
    pair_s_ref,
    act_s_ref,
    inner_s_ref,
    probs_ref,
):
    unit = pl.program_id(1)
    half = gateup_ref.shape[1] // 2
    seq_len = rows_ref.shape[1]
    capacity = slotted_ref.shape[2]

    @pl.when(unit == 0)
    def _():
        logits = dot(router_ref[...], rows_ref[0], 1, 1)
        row = lax.broadcasted_iota(jnp.int32, logits.shape, 0)
        routed = jnp.where(row < experts, logits, -1e30)
        raised = jnp.exp(routed - jnp.max(routed, axis=0, keepdims=True))
        soft = raised / jnp.sum(raised, axis=0, keepdims=True)
        probs_ref[0] = jnp.where(row < experts, soft, jax.nn.sigmoid(logits))

    def parts(data, cot, weight):
        both = dot(data, gateup_ref[0], 1, 1)
        cot_in = dot(cot, down_ref[0], 1, 1)
        gate_in, up_in = both[:, :half], both[:, half:]
        gate_act, gate_slope = silu_parts(gate_in)
        act = gate_act * up_in
        inner = jnp.sum(act.astype(BF).astype(F32) * cot_in, axis=1, keepdims=True)
        cot_in = cot_in * weight
        return (
            (act * weight).astype(BF),
            (cot_in * up_in * gate_slope).astype(BF),
            (cot_in * gate_act).astype(BF),
            inner,
        )

    @pl.when(unit < units - 1)
    def _():
        slot = slot_ref[0, pl.ds(unit, 1), :]
        mask = lax.broadcasted_iota(jnp.int32, (capacity, seq_len), 0) == slot
        onehot = mask.astype(F32).astype(BF)
        slotted_ref[0, 0] = dot(onehot, rows_ref[0]).astype(BF)
        slotgrad_ref[0, 0] = dot(onehot, grads_ref[0]).astype(BF)
        probs = probs_ref[0]
        row = lax.broadcasted_iota(jnp.int32, probs.shape, 0)
        expert = group_ref[0] * (units - 1) + unit
        gate = jnp.sum(jnp.where(row == expert, probs, 0.0), axis=0, keepdims=True)
        weight = jnp.sum(jnp.where(mask, gate, 0.0), axis=1, keepdims=True)
        act, gate_grad, up_grad, inner = parts(slotted_ref[0, 0], slotgrad_ref[0, 0], weight)
        act_ref[0, 0] = act
        pair_ref[0, 0, :, :half] = gate_grad
        pair_ref[0, 0, :, half:] = up_grad
        terms_ref[0, pl.ds(unit, 1), :] = jnp.sum(
            jnp.where(mask, inner, 0.0), axis=0, keepdims=True
        )

    @pl.when(unit == units - 1)
    def _():
        logits = dot(rows_ref[0], router_ref[...], 1, 1)
        weight = jax.nn.sigmoid(logits[:, experts : experts + 1])
        act, gate_grad, up_grad, inner = parts(rows_ref[0], grads_ref[0], weight)
        act_s_ref[0] = act
        pair_s_ref[0, :, :half] = gate_grad
        pair_s_ref[0, :, half:] = up_grad
        inner_s_ref[0] = inner


def plain_act_call(experts, capacity, group, slots, rows, grads, router, gateup, down):
    count, seq_len, width = rows.shape
    units, wide, _ = gateup.shape
    half = wide // 2
    routed = units - 1

    def seq(s, u):
        return (s, 0, 0)

    def unit(s, u):
        return (u, 0, 0)

    def slot(s, u):
        return (jnp.minimum(u, routed - 1), s, 0, 0)

    work = count * (routed * capacity + seq_len) * width
    return call(
        functools.partial(plain_act_body, experts, units),
        (count, units),
        [
            pl.BlockSpec(memory_space=pltpu.SMEM),
            pl.BlockSpec((1, routed, seq_len), seq),
            pl.BlockSpec((1, seq_len, width), seq),
            pl.BlockSpec((1, seq_len, width), seq),
            pl.BlockSpec(router.shape, lambda s, u: (0, 0)),
            pl.BlockSpec((1, wide, width), unit),
            pl.BlockSpec((1, half, width), unit),
        ],
        [
            pl.BlockSpec((1, 1, capacity, width), slot),
            pl.BlockSpec((1, 1, capacity, width), slot),
            pl.BlockSpec((1, 1, capacity, wide), slot),
            pl.BlockSpec((1, 1, capacity, half), slot),
            pl.BlockSpec((1, routed, seq_len), seq),
            pl.BlockSpec((1, seq_len, wide), seq),
            pl.BlockSpec((1, seq_len, half), seq),
            pl.BlockSpec((1, seq_len, 1), seq),
            pl.BlockSpec((1,) + (router.shape[0], seq_len), seq),
        ],
        [
            jax.ShapeDtypeStruct((routed, count, capacity, width), BF),
            jax.ShapeDtypeStruct((routed, count, capacity, width), BF),
            jax.ShapeDtypeStruct((routed, count, capacity, wide), BF),
            jax.ShapeDtypeStruct((routed, count, capacity, half), BF),
            jax.ShapeDtypeStruct((count, routed, seq_len), F32),
            jax.ShapeDtypeStruct((count, seq_len, wide), BF),
            jax.ShapeDtypeStruct((count, seq_len, half), BF),
            jax.ShapeDtypeStruct((count, seq_len, 1), F32),
            jax.ShapeDtypeStruct((count, router.shape[0], seq_len), F32),
        ],
        2 * work * 3 * half + 4 * count * routed * capacity * seq_len * width,
        8 * count * seq_len * width * 2,
    )(group, slots, rows, grads, router, gateup, down)


def plain_back_body(slot_ref, routed_ref, shared_ref, weight_ref, out_ref):
    routed, _, capacity, _ = routed_ref.shape
    seq_len = shared_ref.shape[1]
    total = dot(shared_ref[0], weight_ref[routed])
    lane = lax.broadcasted_iota(jnp.int32, (seq_len, capacity), 1)
    for e in range(routed):
        slot_rows = dot(routed_ref[e, 0], weight_ref[e]).astype(BF)
        onehot = (lane == slot_ref[0, e]).astype(F32).astype(BF)
        total = total + dot(onehot, slot_rows)
    out_ref[0] = total.astype(BF)


def plain_back_call(slots, routed, shared, weight):
    units, wide, width = weight.shape
    count, seq_len, _ = shared.shape
    capacity = routed.shape[2]
    block = min(width, 512)
    work = count * ((units - 1) * capacity + seq_len) * width
    return call(
        plain_back_body,
        (width // block, count),
        [
            pl.BlockSpec((1, units - 1, seq_len, 1), lambda j, s: (s, 0, 0, 0)),
            pl.BlockSpec((units - 1, 1, capacity, wide), lambda j, s: (0, s, 0, 0)),
            pl.BlockSpec((1, seq_len, wide), lambda j, s: (s, 0, 0)),
            pl.BlockSpec((units, wide, block), lambda j, s: (0, 0, j)),
        ],
        pl.BlockSpec((1, seq_len, block), lambda j, s: (s, 0, j)),
        jax.ShapeDtypeStruct((count, seq_len, width), BF),
        2 * work * wide + 2 * count * (units - 1) * capacity * seq_len * width,
        units * wide * width * 2 + count * seq_len * width * 2,
    )(slots, routed, shared, weight)


def plain_outer_body(keep, pad, left_a, right_a, left_b, right_b, out_ref):
    total = dot(left_a[0], right_a[0], 0, 0) + dot(left_b[0], right_b[0], 0, 0)
    total = total.astype(BF)
    blocks, _, rows, slice_width = out_ref.shape
    for part in range(rows // keep):
        for k in range(blocks):
            out_ref[k, 0, part * keep : (part + 1) * keep] = total[
                part * pad : part * pad + keep, k * slice_width : (k + 1) * slice_width
            ]


def plain_outer_call(keep, pad, dp, pairs):
    (left_a, right_a), (left_b, right_b) = pairs
    units, rows, wide = left_a.shape
    width = right_a.shape[2]
    slice_width = width // dp
    blocks = max(1, 512 // slice_width)
    kept = wide // pad * keep

    def left(n):
        return pl.BlockSpec((1, n, wide), lambda u, j: (u, 0, 0))

    def right(n):
        return pl.BlockSpec((1, n, blocks * slice_width), lambda u, j: (u, 0, j))

    return call(
        functools.partial(plain_outer_body, keep, pad),
        (units, dp // blocks),
        [left(rows), right(rows), left(rows), right(rows)],
        pl.BlockSpec((blocks, 1, kept, slice_width), lambda u, j: (j, u, 0, 0)),
        jax.ShapeDtypeStruct((dp, units, kept, slice_width), BF),
        4 * units * rows * wide * width,
        units * rows * (wide + width) * 4,
    )(left_a, right_a, left_b, right_b)


MESH = pl.DeviceIdType.MESH


class Copies:
    def __init__(self, send, recv, here):
        self.send, self.recv, self.here = send, recv, here
        self.remote_count = self.local_count = 0

    def remote(self, src, dst, **device):
        k = self.remote_count
        self.remote_count += 1
        return pltpu.make_async_remote_copy(
            src_ref=src,
            dst_ref=dst,
            send_sem=self.send.at[k],
            recv_sem=self.recv.at[k],
            device_id=device,
            device_id_type=MESH,
        )

    def local(self, src, dst):
        k = self.local_count
        self.local_count += 1
        return pltpu.make_async_copy(src, dst, self.here.at[k])


class Line:
    def __init__(self, copies, buffer, z, depth, rows):
        self.z, self.depth = z, depth

        def piece(p):
            return buffer.at[pl.ds(pl.multiple_of(p * rows, rows), rows)]

        def make(k, sign):
            p = z - sign * k
            return copies.remote(piece(p), piece(p), tensor=z + sign)

        self.ups = [make(k, 1) for k in range(depth - 1)]
        self.downs = [make(k, -1) for k in range(depth - 1)]

    def sends(self, k):
        z, top = self.z, self.depth - 1
        return (
            (self.ups[k], jnp.logical_and(z < top, z >= k)),
            (self.downs[k], jnp.logical_and(z > 0, z + k <= top)),
        )

    def begin(self):
        for copy, there in self.sends(0):
            pl.when(there)(copy.start)

    def finish(self):
        for k in range(self.depth - 1):
            for copy, there in self.sends(k):
                pl.when(there)(copy.wait_send)


def peer_of(me, r):
    out, bit = me, 1
    while bit <= r:
        if r & bit:
            out = out + bit - 2 * bit * (me // bit % 2)
        bit *= 2
    return out


def greet(me, z, dp, depth):
    barrier = pltpu.get_barrier_semaphore()
    for r in range(1, dp):
        pl.semaphore_signal(barrier, inc=1, device_id={"dp": peer_of(me, r)}, device_id_type=MESH)
    for r in range(1, depth):
        pl.semaphore_signal(
            barrier, inc=1, device_id={"tensor": (z + r) % depth}, device_id_type=MESH
        )
    pl.semaphore_wait(barrier, dp - 1 + depth - 1)


def spin(field, cos_rows, sin_rows):
    return field * cos_rows + pltpu.roll(field, field.shape[-1] // 2, 1) * sin_rows


def piece_of(buffer, p, rows):
    return buffer.at[pl.ds(pl.multiple_of(p * rows, rows), rows)]


def pass_on(c, source, target, z, depth, rows, sibling, passed):
    def make(p):
        return c.remote(piece_of(source, p, rows), piece_of(target, p, rows), dp=sibling)

    ups = [make(z - k) for k in range(1, depth)]
    downs = [make(z + k) for k in range(1, depth)]
    for k in range(1, depth):
        passed.append((ups[k - 1], z >= k))
        passed.append((downs[k - 1], z + k <= depth - 1))

    def each(k, up):
        (ups if up else downs)[k - 1].start()

    return each


def line_step(line, k, each=None):
    z, top = line.z, line.depth - 1
    onward = line.sends(k) if k < top else (None, None)
    for up, copy, there, further in (
        (True, line.ups[k - 1], z >= k, onward[0]),
        (False, line.downs[k - 1], z + k <= top, onward[1]),
    ):
        pl.when(there)(copy.wait_recv)
        if further is not None:
            pl.when(further[1])(further[0].start)
        if each is not None:
            pl.when(there)(functools.partial(each, k, up))


def forward_body(
    sizes,
    codes_ref,
    misc_ref,
    gains_ref,
    cos_ref,
    sin_ref,
    tokens_ref,
    outgrad_ref,
    wq_ref,
    wk_ref,
    wv_ref,
    wo_ref,
    eg_ref,
    eu_ref,
    ed_ref,
    sg_ref,
    su_ref,
    sd_ref,
    hidden_ref,
    norm_ref,
    grads_ref,
    gateup_ref,
    down_ref,
    codes_all,
    router_out,
    gain_rows,
    tok_out,
    weights_out,
    qkv_out,
    probs_out,
    mix_out,
    misc_all,
    norm_mine,
    tok,
    weights,
    qkv_ref,
    probs_ref,
    mix_ref,
    fnorm,
    part,
    part_in,
    scatter_in,
    gains_all,
    zeros,
    send,
    recv,
    here,
):
    dp, depth, experts, hidden_units, head = sizes
    me, z = lax.axis_index("dp"), lax.axis_index("tensor")
    core, x = me % 2, (me // 2) % 2
    bits = [2**k for k in range(dp.bit_length() - 1)]
    rows, width = tokens_ref.shape
    seq_len = rows * depth
    slice_width = width // dp
    routed = experts // 4
    c = Copies(send, recv, here)

    def bit_of(bit):
        return (me // bit) % 2

    greet(me, z, dp, depth)

    first = []
    own_codes = c.local(codes_ref, codes_all.at[0])
    own_misc = c.local(misc_ref, misc_all.at[me])
    own_gains = c.local(gains_ref, gains_all.at[z, me])
    for copy in (own_codes, own_misc, own_gains):
        copy.start()
    for r in range(1, 4):
        first.append(c.remote(codes_ref, codes_all.at[r], dp=peer_of(me, r)))
    gain_copies = [c.remote(gains_ref, gains_all.at[z, me], dp=peer_of(me, r)) for r in range(1, dp)]
    misc_copies = [c.remote(misc_ref, misc_all.at[me], dp=peer_of(me, r)) for r in range(1, dp)]
    for copy in gain_copies + misc_copies + first:
        copy.start()

    def piece(buffer, p):
        return buffer.at[pl.ds(pl.multiple_of(p * rows, rows), rows)]

    own_tok = c.local(tokens_ref, piece(tok.at[0], z))
    own_tok.start()
    own_grad = c.local(outgrad_ref, piece(grads_ref.at[0], z))
    own_grad.start()

    def columns(k, n):
        return pl.ds(pl.multiple_of(k * n, n), n)

    pair = wq_ref.shape[1] // 2
    own_at = tuple(bit_of(bit) for bit in reversed(bits))
    core_copies = []
    for k, w in enumerate((wq_ref, wk_ref, wv_ref, wo_ref)):
        place = weights.at[own_at + (slice(None), pl.ds(k * pair, pair))]
        core_copies.append(c.remote(w.at[:, columns(1 - core, pair)], place, dp=peer_of(me, 1)))
        core_copies.append(c.local(w.at[:, columns(core, pair)], place))
    for copy in core_copies:
        copy.start()

    own_tok.wait()
    tok_line = Line(c, tok.at[0], z, depth, rows)
    tok_line.begin()
    tok_pass = [c.remote(tokens_ref, piece(tok.at[1], z), dp=peer_of(me, 1))]
    tok_pass[0].start()

    zeros[...] = jnp.zeros_like(zeros)
    pad = zeros.shape[1]
    pads = [c.local(zeros, down_ref.at[:, 0, pl.ds(hidden_units, pad)])]
    pads += [c.local(zeros, gateup_ref.at[:, k, pl.ds(hidden_units, pad)]) for k in range(2)]
    matrices = ((ed_ref, sd_ref, down_ref, 0), (eg_ref, sg_ref, gateup_ref, 0), (eu_ref, su_ref, gateup_ref, 1))
    slab = columns(me, slice_width)

    def group_copies(routed_src, shared_src, dst, k, r):
        group = (peer_of(me, r)) % 4
        many = (
            routed_src.at[pl.ds(group * routed, routed)],
            dst.at[pl.ds(0, routed), k, pl.ds(0, hidden_units), slab],
        )
        one = (shared_src.at[group], dst.at[routed, k, pl.ds(0, hidden_units), slab])
        if r == 0:
            return [c.local(*many), c.local(*one)]
        return [c.remote(*many, dp=peer_of(me, r)), c.remote(*one, dp=peer_of(me, r))]

    near = [[copy for r in (0, 1) for copy in group_copies(*m, r)] for m in matrices]
    far = [[copy for r in (2, 3) for copy in group_copies(*m, r)] for m in matrices]

    def over_copy(dst, k, far_chip):
        n = 2 * slice_width
        chip = me // 2 + far_chip * (1 - 2 * x)
        cols = pl.ds(pl.multiple_of(chip * n, n), n)
        place = dst.at[:, k, pl.ds(0, hidden_units), cols]
        return c.remote(place, place, dp=peer_of(me, 4))

    over_near = [over_copy(m[2], m[3], 0) for m in matrices]
    over = [over_copy(m[2], m[3], 1) for m in matrices]

    for copy in core_copies:
        copy.wait()

    def weight_copies(order, half):
        have, copies = [1], []
        for bit in order:
            index = tuple(
                pl.ds(0, 2) if b in have else pl.ds(bit_of(b), 1) for b in reversed(bits)
            )
            place = weights.at[index + (slice(None), pl.ds(half * 2 * pair, 2 * pair))]
            copies.append(c.remote(place, place, dp=peer_of(me, bit)))
            have.append(bit)
        return copies

    qk_copies = weight_copies(bits[1:], 0)
    vo_copies = weight_copies(bits[:0:-1], 1)
    qk_copies[0].start()
    vo_copies[0].start()
    for copy in pads + [copy for m in near for copy in m]:
        copy.start()

    own_gains.wait()
    for copy in gain_copies:
        copy.wait_recv()
    gain_spread = [
        c.remote(gains_all.at[z], gains_all.at[z], tensor=(z + r) % depth) for r in range(1, depth)
    ]
    for copy in gain_spread:
        copy.start()

    tok_passed = []
    sibling = peer_of(me, 1)
    pass_tok = pass_on(c, tok.at[0], tok.at[1], z, depth, rows, sibling, tok_passed)

    line_step(tok_line, 1, pass_tok)
    for k in range(1, len(bits) - 1):
        qk_copies[k - 1].wait_recv()
        qk_copies[k].start()
        vo_copies[k - 1].wait_recv()
        vo_copies[k].start()
    own_grad.wait()
    grad_line = Line(c, grads_ref.at[0], z, depth, rows)
    for k in range(2, depth):
        line_step(tok_line, k, pass_tok)
    grad_line.begin()

    for copy in gain_spread:
        copy.wait_recv()
    for d in range(dp):
        total = gains_all[0, d]
        for t in range(1, depth):
            total = total + gains_all[t, d]
        gain_rows[:, d * slice_width : (d + 1) * slice_width] = total

    def norm_rows(s):
        def block(i, carry):
            at = pl.ds(pl.multiple_of(i * rows, rows), rows)
            data = tok[s, at, :].astype(F32)
            scale = lax.rsqrt(jnp.mean(data * data, axis=-1, keepdims=True) + EPS)
            fnorm[at, :] = (data * scale * gain_rows[0:1, :]).astype(BF)
            return carry

        lax.fori_loop(0, depth, block, 0)

    own_misc.wait()
    for copy in misc_copies:
        copy.wait_recv()
    router_out[...] = jnp.zeros_like(router_out)
    row = lax.broadcasted_iota(jnp.int32, misc_ref.shape, 0)
    for d in range(dp):
        block = jnp.where(row <= experts, misc_all[d], 0.0).astype(BF)
        router_out[: misc_ref.shape[0], d * slice_width : (d + 1) * slice_width] = block
    bias_in = jnp.zeros(misc_ref.shape, F32)
    sub = lax.broadcasted_iota(jnp.int32, misc_ref.shape, 0)
    for d in range(dp):
        bias_in = jnp.where(sub == d, misc_all[d, pl.ds(experts + 1 + core, 1), :], bias_in)
    bias_in = bias_in.astype(BF)
    heads3 = 3 * pair
    head_slice = head // dp
    lane = lax.broadcasted_iota(jnp.int32, (bias_in.shape[1], heads3), 1)
    sub = lax.broadcasted_iota(jnp.int32, (bias_in.shape[1], heads3), 0)
    place = (lane // head * head_slice + lane % head_slice == sub).astype(F32).astype(BF)
    spread = dot(bias_in, place)
    lane = lax.broadcasted_iota(jnp.int32, spread.shape, 1)
    sub = lax.broadcasted_iota(jnp.int32, spread.shape, 0)
    bias = jnp.sum(jnp.where(lane % head // head_slice == sub, spread, 0.0), axis=0, keepdims=True)

    qk_copies[-1].wait_recv()
    vo_copies[-1].wait_recv()
    for m in far:
        for copy in m:
            copy.start()
    for m, copy in zip(near, over_near):
        for part_copy in m:
            part_copy.wait()
        copy.start()
    pairs = pair // head

    def project(s):
        def block(i, carry):
            at = pl.ds(pl.multiple_of(i * 2 * rows, 2 * rows), 2 * rows)
            full = weights[...].reshape(width, 4 * pair)
            pre = dot(fnorm[at, :], full[:, : 3 * pair]) + bias
            cos_rows, sin_rows = cos_ref[at, :], sin_ref[at, :]
            for kind in range(3):
                for h in range(pairs):
                    a = (kind * pairs + h) * head
                    field = pre[:, a : a + head]
                    if kind < 2:
                        field = spin(field, cos_rows, sin_rows)
                    qkv_ref[kind, s * pairs + h, at, :] = field.astype(BF)
            return carry

        lax.fori_loop(0, depth // 2, block, 0)

    norm_rows(0)
    project(0)
    line_step(grad_line, 1)
    for copy in far[0]:
        copy.wait_recv()
    over[0].start()
    tok_pass[0].wait()
    for copy, there in tok_passed:
        pl.when(there)(copy.wait)
    norm_rows(1)
    project(1)

    own_codes.wait()
    for copy in first:
        copy.wait()
    causal_block = seq_len // 2

    def attend(s):
        flags = codes_all[s]
        sub = lax.broadcasted_iota(jnp.int32, flags.shape, 0)
        flags = jnp.where(sub == 8, flags, 0).astype(F32).astype(BF)
        for h in range(pairs):
            for b in range(2):
                at = slice(b * causal_block, (b + 1) * causal_block)
                seen = dot(flags[:, at], flags, 0, 0)
                row = lax.broadcasted_iota(jnp.int32, seen.shape, 0) + b * causal_block
                col = lax.broadcasted_iota(jnp.int32, seen.shape, 1)
                scores = dot(qkv_ref[0, s * pairs + h, at, :], qkv_ref[1, s * pairs + h], 1, 1)
                scores = scores * head ** (-0.5)
                scores = jnp.where(jnp.logical_or(col <= row, seen > 0.5), scores, -1e30)
                raised = jnp.exp(scores - jnp.max(scores, axis=1, keepdims=True))
                probs = raised / jnp.sum(raised, axis=1, keepdims=True)
                probs = probs.astype(BF)
                probs_ref[s * pairs + h, at, :] = probs
                mixed = dot(probs, qkv_ref[2, s * pairs + h])
                mix_ref[s, at, h * head : (h + 1) * head] = mixed.astype(BF)

    def project_out(s):
        for d in range(dp):
            index = tuple(d // bit % 2 for bit in reversed(bits))
            block = weights[index + (slice(None), slice(3 * pair, 4 * pair))]
            at = slice(d * slice_width, (d + 1) * slice_width)
            part[s, :, at] = dot(mix_ref[s], block, 1, 1).astype(BF)

    attend(1)
    if depth > 2:
        line_step(grad_line, 2)
    project_out(1)
    part_pass = c.remote(part.at[1], part_in, dp=peer_of(me, 1))
    part_pass.start()
    attend(0)
    project_out(0)
    part_pass.wait_recv()

    saved = [
        c.local(a, b)
        for a, b in (
            (tok, tok_out),
            (weights, weights_out),
            (qkv_ref, qkv_out),
            (probs_ref, probs_out),
            (mix_ref, mix_out),
        )
    ]
    for copy in saved:
        copy.start()
    scatter = []
    for r in list(range(1, depth)) + [0]:
        at = pl.ds(pl.multiple_of((z + r) % depth * rows, rows), rows)
        total = part[0, at, :].astype(F32) + part_in[at, :].astype(F32)
        if r:
            part[0, at, :] = total.astype(BF)
            copy = c.remote(part.at[0, at], scatter_in.at[r - 1], tensor=(z + r) % depth)
            copy.start()
            scatter.append(copy)
        else:
            hidden_ref[...] = total + tok[0, at, :].astype(F32)

    for k in range(3, depth):
        line_step(grad_line, k)
    x_grad = c.remote(grads_ref.at[0], grads_ref.at[2], dp=peer_of(me, 2))
    x_grad.start()
    own_pass = c.remote(grads_ref.at[0], grads_ref.at[1], dp=peer_of(me, 1))
    own_pass.start()
    for k in (1, 2):
        for copy in far[k]:
            copy.wait_recv()
        over[k].start()

    for copy in scatter:
        copy.wait_recv()
    total = hidden_ref[...]
    for r in range(1, depth):
        total = total + scatter_in[r - 1].astype(F32)
    hidden_ref[...] = total
    scale = lax.rsqrt(jnp.mean(total * total, axis=-1, keepdims=True) + EPS)
    norm_mine[...] = (total * scale * gain_rows[1:2, :]).astype(BF)
    norm_here = c.local(norm_mine, piece(norm_ref.at[0], z))
    norm_here.start()
    norm_here.wait()
    norm_line = Line(c, norm_ref.at[0], z, depth, rows)
    norm_line.begin()
    beside = peer_of(me, 2)
    norm_own = c.remote(piece(norm_ref.at[0], z), piece(norm_ref.at[1], z), dp=sibling)
    norm_far = c.remote(piece(norm_ref.at[0], z), piece(norm_ref.at[2], z), dp=beside)
    norm_far.start()
    norm_own.start()
    norm_passed, far_passed = [], []
    pass_norm = pass_on(
        c, norm_ref.at[0], norm_ref.at[1], z, depth, rows, sibling, norm_passed
    )
    pass_far = pass_on(c, norm_ref.at[0], norm_ref.at[2], z, depth, rows, beside, far_passed)

    def pass_both(k, up):
        pass_far(k, up)
        pass_norm(k, up)

    for k in range(1, depth):
        line_step(norm_line, k, pass_both)

    x_grad.wait_recv()
    grad_pass = c.remote(grads_ref.at[2], grads_ref.at[3], dp=peer_of(me, 1))
    grad_pass.start()
    for copy in over_near + over:
        copy.wait()
    norm_far.wait()
    for copy, there in far_passed:
        pl.when(there)(copy.wait)
    norm_pass = c.remote(norm_ref.at[2], norm_ref.at[3], dp=sibling)
    norm_pass.start()
    norm_own.wait()
    for copy, there in norm_passed:
        pl.when(there)(copy.wait)
    norm_pass.wait()
    own_pass.wait()
    grad_pass.wait()
    for line in (tok_line, grad_line, norm_line):
        line.finish()
    for copy in pads + saved:
        copy.wait()
    for copy in gain_copies + misc_copies + gain_spread + qk_copies + vo_copies + scatter:
        copy.wait_send()
    for copy in [part_pass, x_grad] + [y for m in far for y in m]:
        copy.wait_send()


def forward_call(dp, depth, experts, head, small, arrays, units):
    codes, misc, gains, cos_rows, sin_rows = small
    tokens, pair = arrays[0], arrays[2].shape[1] // 2
    rows, width = tokens.shape
    seq_len = rows * depth
    hidden_units = units[0].shape[1]
    hidden_pad = -(-hidden_units // 128) * 128
    routed = experts // 4
    bits = dp.bit_length() - 1
    pairs = pair // head
    vmem, hbm = pl.BlockSpec(memory_space=pltpu.VMEM), pl.BlockSpec(memory_space=pl.ANY)
    shape = jax.ShapeDtypeStruct
    return pl.pallas_call(
        functools.partial(forward_body, (dp, depth, experts, hidden_units, head)),
        in_specs=[vmem] * 5 + [hbm] * 12,
        out_specs=[vmem] + [hbm] * 4 + [vmem] * 3 + [hbm] * 5,
        out_shape=[
            shape((rows, width), F32),
            shape((4, seq_len, width), BF),
            shape((4, seq_len, width), BF),
            shape((routed + 1, 2, hidden_pad, width), BF),
            shape((routed + 1, 1, hidden_pad, width), BF),
            shape((4,) + codes.shape, codes.dtype),
            shape((128, width), BF),
            shape((8, width), F32),
            shape((2, seq_len, width), BF),
            shape((2,) * bits + (width // dp, 4 * pair), BF),
            shape((3, 2 * pairs, seq_len, head), BF),
            shape((2 * pairs, seq_len, seq_len), BF),
            shape((2, seq_len, pair), BF),
        ],
        scratch_shapes=[
            pltpu.VMEM((dp,) + misc.shape, F32),
            pltpu.VMEM((rows, width), BF),
            pltpu.VMEM((2, seq_len, width), BF),
            pltpu.VMEM((2,) * bits + (width // dp, 4 * pair), BF),
            pltpu.VMEM((3, 2 * pairs, seq_len, head), BF),
            pltpu.VMEM((2 * pairs, seq_len, seq_len), BF),
            pltpu.VMEM((2, seq_len, pair), BF),
            pltpu.VMEM((seq_len, width), BF),
            pltpu.VMEM((2, seq_len, width), BF),
            pltpu.VMEM((seq_len, width), BF),
            pltpu.VMEM((depth - 1, rows, width), BF),
            pltpu.VMEM((depth, dp) + gains.shape, F32),
            pltpu.VMEM((routed + 1, hidden_pad - hidden_units, width), BF),
            pltpu.SemaphoreType.DMA((160,)),
            pltpu.SemaphoreType.DMA((160,)),
            pltpu.SemaphoreType.DMA((40,)),
        ],
        compiler_params=pltpu.CompilerParams(
            collective_id=0, has_side_effects=True, vmem_limit_bytes=VMEM_LIMIT
        ),
    )(codes, misc, gains, cos_rows, sin_rows, *arrays, *units)


def middle_body(
    sizes,
    hidden_ref,
    codes_ref,
    router_ref,
    rows_ref,
    grads_ref,
    gateup_ref,
    down_ref,
    output_ref,
    terms_out,
    probs_out,
    grad_own,
    grad_sib,
    grad_far,
    gate_total,
    up_total,
    down_total,
    gate_in,
    wide_w,
    down_w,
    xs,
    ys,
    pair,
    act,
    outs,
    backs,
    near_in,
    back_in,
    far_in,
    z_in,
    stage,
    weights,
    routed,
    probs,
    terms,
    terms_in,
    send,
    recv,
    here,
):
    dp, depth, experts, top_count, keep = sizes
    me, z = lax.axis_index("dp"), lax.axis_index("tensor")
    y = me // 4
    rows, width = output_ref.shape
    seq_len = rows * depth
    total = 2 * seq_len
    units, wide, _ = wide_w.shape
    half = wide // 2
    slice_width = width // dp
    sibling, beside, over = peer_of(me, 1), peer_of(me, 2), peer_of(me, 4)
    c = Copies(send, recv, here)

    greet(me, z, dp, depth)

    def load(source, chunk, target):
        copies = [
            c.local(source.at[2 * chunk + s], target.at[pl.ds(s * seq_len, seq_len)])
            for s in range(2)
        ]
        for copy in copies:
            copy.start()
        return copies

    def wait(copies):
        for copy in copies:
            copy.wait()

    loads = load(rows_ref, 1, xs)
    first = [(c.local(gateup_ref.at[u], wide_w.at[u]), c.local(down_ref.at[u], down_w.at[u])) for u in range(units)]
    first[0][0].start()
    first[0][1].start()
    loads += load(grads_ref, 1, ys)
    for u in range(1, units):
        first[u][0].start()
        first[u][1].start()

    block = seq_len // 2
    lanes = weights.shape[1]

    def gate_weights(chunk):
        def step(i, carry):
            at = pl.ds(pl.multiple_of(i * block, block), block)
            logits = dot(xs[at, :], router_ref[...], 1, 1)
            lane = lax.broadcasted_iota(jnp.int32, logits.shape, 1)
            chosen = jnp.where(lane < experts, logits, -1e30)
            raised = jnp.exp(chosen - jnp.max(chosen, axis=1, keepdims=True))
            soft = raised / jnp.sum(raised, axis=1, keepdims=True)
            probs[at, :] = jnp.where(lane < experts, soft, jax.nn.sigmoid(logits))
            return carry

        lax.fori_loop(0, total // block, step, 0)
        for s in range(2):
            codes = codes_ref[2 * chunk + s]
            row = lax.broadcasted_iota(jnp.int32, codes.shape, 0)
            named = row == experts
            for k in range(top_count):
                named = jnp.logical_or(named, codes[k : k + 1] == row)
            named = jnp.logical_and(named, row <= experts).astype(F32).astype(BF)
            place = (codes.shape[0], lanes)
            same = lax.broadcasted_iota(jnp.int32, place, 0) == lax.broadcasted_iota(
                jnp.int32, place, 1
            )
            routed[s * seq_len : (s + 1) * seq_len] = dot(named, same.astype(F32).astype(BF), 0, 0)
        weights[...] = probs[...] * routed[...]

    def activate(chunk):
        for u in range(units):
            if chunk == 1:
                wait(first[u])
            if u == 0:
                gate_weights(chunk)
            place = me % 4 * (units - 1) + u if u < units - 1 else experts

            def step(i, carry, u=u, place=place):
                at = pl.ds(pl.multiple_of(i * block, block), block)
                mine = lax.broadcasted_iota(jnp.int32, (block, lanes), 1) == place
                weight = jnp.sum(jnp.where(mine, weights[at, :], 0.0), axis=1, keepdims=True)
                both = dot(xs[at, :], wide_w[u], 1, 1)
                cot = dot(ys[at, :], down_w[u], 1, 1)
                gate_act, gate_slope = silu_parts(both[:, :half])
                value = gate_act * both[:, half:]
                inner = jnp.sum(value * cot, axis=1, keepdims=True)
                inner = jnp.where(mine, inner * routed[at, :], 0.0)
                terms[chunk, at, :] = inner if u == 0 else terms[chunk, at, :] + inner
                cot = cot * weight
                act[chunk, at, u * half : (u + 1) * half] = (value * weight).astype(BF)
                a = u * wide
                pair[chunk, at, a : a + half] = (cot * both[:, half:] * gate_slope).astype(BF)
                pair[chunk, at, a + half : a + wide] = (cot * gate_act).astype(BF)
                return carry

            lax.fori_loop(0, total // block, step, 0)

    cols = 512

    def back(left, chunk, s, weight, target):
        at = slice(s * seq_len, (s + 1) * seq_len)
        for j in range(width // cols):
            part = weight[:, :, j * cols : (j + 1) * cols]
            part = part.reshape(-1, cols)
            target[:, j * cols : (j + 1) * cols] = dot(left[chunk, at, :], part).astype(BF)

    def add_into(target, other):
        def step(i, carry):
            at = pl.ds(pl.multiple_of(i * rows, rows), rows)
            target[at, :] = (target[at, :].astype(F32) + other[at, :].astype(F32)).astype(BF)
            return carry

        lax.fori_loop(0, depth, step, 0)

    wait(loads)
    activate(1)
    loads = load(rows_ref, 0, xs) + load(grads_ref, 0, ys)
    terms_near = c.remote(terms.at[1, pl.ds(seq_len, seq_len)], terms_in, dp=sibling)
    terms_near.start()
    back(act, 1, 1, down_w, outs.at[1])
    out_near = c.remote(outs.at[1], near_in, dp=sibling)
    out_near.start()
    back(act, 1, 0, down_w, outs.at[0])
    terms_near.wait()
    terms[1, :seq_len] = terms[1, :seq_len] + terms_in[...]
    terms_across = c.remote(terms.at[1, pl.ds(0, seq_len)], terms_out.at[2], dp=beside)
    terms_across.start()
    out_near.wait()
    add_into(outs.at[0], near_in)
    out_across = c.remote(outs.at[0], far_in, dp=beside)
    out_across.start()
    back(pair, 1, 1, wide_w, outs.at[1])
    grad_near = c.remote(outs.at[1], back_in, dp=sibling)
    grad_near.start()
    back(pair, 1, 0, wide_w, backs)
    grad_near.wait()
    add_into(backs, back_in)
    grad_across = c.remote(backs, grad_far, dp=beside)
    grad_across.start()

    wait(loads)
    activate(0)
    probs_out[...] = probs[pl.ds(pl.multiple_of(z * rows, rows), rows), :]
    loads = load(rows_ref, 1, ys)
    terms_out[0] = terms[0, :seq_len]
    terms_last = c.remote(terms.at[0, pl.ds(seq_len, seq_len)], terms_out.at[1], dp=sibling)
    terms_last.start()
    back(act, 0, 1, down_w, outs.at[1])
    out_last = c.remote(outs.at[1], near_in, dp=sibling)
    out_last.start()
    back(act, 0, 0, down_w, back_in)

    staged, moved = [None, None], []
    blocks = stage.shape[2]

    def outer(left, parts, targets, u, j, slot):
        at = slice(j * blocks * slice_width, (j + 1) * blocks * slice_width)
        n = parts * half
        value = dot(left[0, :, u * n : (u + 1) * n], xs[:, at], 0, 0)
        value = (value + dot(left[1, :, u * n : (u + 1) * n], ys[:, at], 0, 0)).astype(BF)
        if staged[slot] is not None:
            wait(staged[slot])
        copies = []
        for k, target in enumerate(targets):
            for b in range(blocks):
                stage[slot, k, b] = value[
                    k * half : k * half + keep, b * slice_width : (b + 1) * slice_width
                ]
            copies.append(c.local(stage.at[slot, k], target.at[pl.ds(j * blocks, blocks), u]))
            copies[-1].start()
        staged[slot] = copies

    wait(loads)
    steps = dp // blocks
    scatter = []
    over_copies = []
    for u in range(units):
        for j in range(steps):
            outer(pair, 2, (gate_total, up_total), u, j, j % 2)
        if u == 0:
            out_last.wait()
            out_across.wait()
            for r in list(range(1, depth)) + [0]:
                at = pl.ds(pl.multiple_of((z + r) % depth * rows, rows), rows)
                part = back_in[at, :].astype(F32) + near_in[at, :].astype(F32)
                part = part + far_in[at, :].astype(F32)
                if r:
                    back_in[at, :] = part.astype(BF)
                    copy = c.remote(back_in.at[at], z_in.at[r - 1], tensor=(z + r) % depth)
                    copy.start()
                    scatter.append(copy)
                else:
                    near_in[at, :] = part.astype(BF)
        for slot in range(2):
            wait(staged[slot])
            staged[slot] = None
        source = gate_total.at[pl.ds((1 - y) * 4, 4), u]
        over_copies.append(c.remote(source, gate_in.at[:, u], dp=over))
        over_copies[-1].start()
    loads = load(grads_ref, 0, xs) + load(grads_ref, 1, ys)

    back(pair, 0, 1, wide_w, outs.at[1])
    grad_last = c.remote(outs.at[1], grad_sib, dp=sibling)
    grad_last.start()
    back(pair, 0, 0, wide_w, outs.at[0])
    grad_here = c.local(outs.at[0], grad_own)
    grad_here.start()
    wait(loads)
    for u in range(units):
        for j in range(steps):
            outer(act, 1, (down_total,), u, j, j % 2)
    for copy in scatter:
        copy.wait_recv()
    value = near_in[pl.ds(pl.multiple_of(z * rows, rows), rows), :].astype(F32)
    value = value + hidden_ref[...]
    for r in range(1, depth):
        value = value + z_in[r - 1].astype(F32)
    output_ref[...] = value.astype(BF)
    for slot in range(2):
        wait(staged[slot])
    for copy in scatter:
        copy.wait_send()
    wait([grad_here, grad_last, terms_last, terms_across, grad_across] + over_copies)


def middle_call(dp, depth, experts, top_count, hidden_units, hidden, codes, router, arrays):
    rows, width = hidden.shape
    seq_len = rows * depth
    norm, grads, gateup, down = arrays
    units, wide, _ = gateup.shape
    half = wide // 2
    slice_width = width // dp
    blocks = max(1, 1024 // slice_width)
    vmem, hbm = pl.BlockSpec(memory_space=pltpu.VMEM), pl.BlockSpec(memory_space=pl.ANY)
    shape = jax.ShapeDtypeStruct
    total = shape((dp, units, hidden_units, slice_width), BF)
    return pl.pallas_call(
        functools.partial(middle_body, (dp, depth, experts, top_count, hidden_units)),
        in_specs=[vmem] * 3 + [hbm] * 4,
        out_specs=[vmem] * 3 + [hbm] * 7,
        out_shape=[
            shape((rows, width), BF),
            shape((3, seq_len, 128), F32),
            shape((rows, 128), F32),
            shape((seq_len, width), BF),
            shape((seq_len, width), BF),
            shape((seq_len, width), BF),
            total,
            total,
            total,
            shape((4, units, hidden_units, slice_width), BF),
        ],
        scratch_shapes=[
            pltpu.VMEM((units, wide, width), BF),
            pltpu.VMEM((units, half, width), BF),
            pltpu.VMEM((2 * seq_len, width), BF),
            pltpu.VMEM((2 * seq_len, width), BF),
            pltpu.VMEM((2, 2 * seq_len, units * wide), BF),
            pltpu.VMEM((2, 2 * seq_len, units * half), BF),
            pltpu.VMEM((2, seq_len, width), BF),
            pltpu.VMEM((seq_len, width), BF),
            pltpu.VMEM((seq_len, width), BF),
            pltpu.VMEM((seq_len, width), BF),
            pltpu.VMEM((seq_len, width), BF),
            pltpu.VMEM((depth - 1, rows, width), BF),
            pltpu.VMEM((2, 2, blocks, hidden_units, slice_width), BF),
            pltpu.VMEM((2 * seq_len, 128), F32),
            pltpu.VMEM((2 * seq_len, 128), F32),
            pltpu.VMEM((2 * seq_len, 128), F32),
            pltpu.VMEM((2, 2 * seq_len, 128), F32),
            pltpu.VMEM((seq_len, 128), F32),
            pltpu.SemaphoreType.DMA((32,)),
            pltpu.SemaphoreType.DMA((32,)),
            pltpu.SemaphoreType.DMA((64,)),
        ],
        compiler_params=pltpu.CompilerParams(
            collective_id=2, has_side_effects=True, vmem_limit_bytes=63 * 2**20
        ),
    )(hidden, codes, router, norm, grads, gateup, down)


def backward_body(
    sizes,
    terms_ref,
    probs_mine_ref,
    router_ref,
    gain_rows,
    cos_ref,
    sin_ref,
    hidden_ref,
    outgrad_ref,
    grad_a_ref,
    grad_b_ref,
    grad_c_ref,
    gate_in_ref,
    gate_ref,
    up_ref,
    down_ref,
    tok_hbm,
    weights_hbm,
    qkv_hbm,
    probs_hbm,
    mix_hbm,
    norm_hbm,
    input_ref,
    gate_out,
    up_out,
    down_out,
    attn_out,
    misc_out,
    gains_out,
    own_sum,
    arrived,
    three,
    scatter_in,
    terms_sum,
    terms_in,
    back,
    tok,
    weights,
    qkv,
    probs_ref,
    mix_ref,
    scales,
    qkv_grad,
    part_in,
    keep,
    total_a,
    first_qk,
    first_vo,
    second_in,
    misc_part,
    misc_in,
    gains_in,
    vectors,
    send,
    recv,
    here,
):
    dp, depth, experts, head = sizes
    me, z = lax.axis_index("dp"), lax.axis_index("tensor")
    core, x, y = me % 2, (me // 2) % 2, me // 4
    rows, width = input_ref.shape
    seq_len = rows * depth
    slice_width = width // dp
    pair = mix_ref.shape[2]
    pairs = pair // head
    bits = [1, 2, 4]
    c = Copies(send, recv, here)

    greet(me, z, dp, depth)

    matrices = ((gate_ref, gate_out), (up_ref, up_out), (down_ref, down_out))
    over = [None]
    for m in (1, 2):
        other = matrices[m][0].at[pl.ds((1 - y) * 4, 4)]
        over.append(c.remote(other, arrived.at[m], dp=peer_of(me, 4)))
        over[m].start()
    gate_in = c.local(gate_in_ref, arrived.at[0])
    grads = (grad_a_ref, grad_b_ref, grad_c_ref)
    loads = [c.local(grads[k], three.at[k]) for k in range(3)]
    for copy in loads:
        copy.start()
    own_loads = [
        c.local(source.at[pl.ds(y * 4, 4)], own_sum) for source, _ in matrices
    ]
    inputs = [
        c.local(a, b)
        for a, b in (
            (weights_hbm, weights),
            (mix_hbm, mix_ref),
            (qkv_hbm, qkv),
            (probs_hbm, probs_ref),
            (tok_hbm, tok),
        )
    ]
    own_loads[0].start()
    gate_in.start()
    for copy in inputs:
        copy.start()

    def at_of(p):
        return pl.ds(pl.multiple_of(p * rows, rows), rows)

    for copy in loads:
        copy.wait()
    scatter, small = [], []
    for r in list(range(1, depth)) + [0]:
        at = at_of((z + r) % depth)
        total = three[0, at, :].astype(F32) + three[1, at, :].astype(F32)
        total = total + three[2, at, :].astype(F32)
        extra = terms_ref[0, at, :] + terms_ref[1, at, :] + terms_ref[2, at, :]
        if r:
            three[0, at, :] = total.astype(BF)
            terms_sum[at, :] = extra
            peer = (z + r) % depth
            scatter.append(c.remote(three.at[0, at], scatter_in.at[0, r - 1], tensor=peer))
            small.append(c.remote(terms_sum.at[at], terms_in.at[r - 1], tensor=peer))
            scatter[-1].start()
            small[-1].start()
        else:
            keep[0] = total
            terms_sum[at, :] = extra

    def add_over(m):
        own_loads[m].wait()
        if m:
            over[m].wait_recv()
        else:
            gate_in.wait()
        copies = []
        for r in (2, 3, 1, 0):
            k = peer_of(me, r) % 4
            for unit in range(own_sum.shape[1]):
                arrived[m, k, unit] = (
                    own_sum[k, unit].astype(F32) + arrived[m, k, unit].astype(F32)
                ).astype(BF)
            place = matrices[m][1].at[me % 4]
            if r:
                copies.append(c.remote(arrived.at[m, k], place, dp=peer_of(me, r)))
            else:
                copies.append(c.local(arrived.at[m, k], place))
            copies[-1].start()
        if m + 1 < len(own_loads):
            own_loads[m + 1].start()
        return copies

    units = add_over(0)
    for copy in scatter:
        copy.wait_recv()
    for copy in small:
        copy.wait_recv()
    route = terms_sum[at_of(z), :]
    grad = keep[0]
    for r in range(1, depth):
        grad = grad + scatter_in[0, r - 1].astype(F32)
        route = route + terms_in[r - 1]
    probs_mine = probs_mine_ref[...]
    lane = lax.broadcasted_iota(jnp.int32, route.shape, 1)
    inner = jnp.sum(jnp.where(lane < experts, probs_mine * route, 0.0), axis=1, keepdims=True)
    logits = jnp.where(
        lane < experts,
        probs_mine * (route - inner),
        jnp.where(lane == experts, route * probs_mine * (1.0 - probs_mine), 0.0),
    ).astype(BF)
    grad = grad + dot(logits, router_ref[...])
    hidden = hidden_ref[...]
    scale = lax.rsqrt(jnp.mean(hidden * hidden, axis=-1, keepdims=True) + EPS)
    unit = hidden * scale
    vectors[1:2, :] = jnp.sum(grad * unit, axis=0, keepdims=True)
    grad = grad * gain_rows[1:2, :]
    grad = outgrad_ref[...].astype(F32) + scale * (
        grad - unit * jnp.mean(grad * unit, axis=-1, keepdims=True)
    )
    keep[0] = grad
    back[0, at_of(z), :width] = grad.astype(BF)
    back[0, at_of(z), width:] = logits

    line = Line(c, back.at[0], z, depth, rows)
    line.begin()
    sibling = peer_of(me, 1)
    back_own = c.remote(piece_of(back.at[0], z, rows), piece_of(back.at[1], z, rows), dp=sibling)
    back_own.start()
    passed = []
    pass_back = pass_on(c, back.at[0], back.at[1], z, depth, rows, sibling, passed)
    for copy in scatter:
        copy.wait_send()
    line_step(line, 1, pass_back)

    for copy in inputs:
        copy.wait()

    def scale_rows(i, carry):
        at = at_of(i)
        for s in range(2):
            data = tok[s, at, :].astype(F32)
            scales[s, at, :] = lax.rsqrt(jnp.mean(data * data, axis=-1, keepdims=True) + EPS)
        return carry

    lax.fori_loop(0, depth, scale_rows, 0)
    line_step(line, 2, pass_back)
    units += add_over(1)
    line_step(line, 3, pass_back)
    back_own.wait()
    for copy, there in passed:
        pl.when(there)(copy.wait)
    def block_of(d):
        return tuple(d // bit % 2 for bit in reversed(bits))

    def slab(d):
        return slice(d * slice_width, (d + 1) * slice_width)

    def attention(s):
        mixed = jnp.zeros((seq_len, pair), F32)
        for d in range(dp):
            block = weights[block_of(d) + (slice(None), slice(3 * pair, 4 * pair))]
            mixed = mixed + dot(back[s, :, slab(d)], block)
        mixed = mixed.astype(BF)
        for h in range(pairs):
            n = s * pairs + h
            cot = mixed[:, h * head : (h + 1) * head]
            key_total = jnp.zeros((seq_len, head), F32)
            value_total = jnp.zeros((seq_len, head), F32)
            for b in range(2):
                at = slice(b * seq_len // 2, (b + 1) * seq_len // 2)
                p_low = probs_ref[n, at, :]
                p = p_low.astype(F32)
                p_grad = dot(cot[at], qkv[2, n], 1, 1)
                s_grad = p * (p_grad - jnp.sum(p * p_grad, axis=1, keepdims=True))
                s_grad = s_grad.astype(BF)
                q_grad = dot(s_grad, qkv[1, n]) * head ** (-0.5)
                q_grad = spin(q_grad, cos_ref[at, :], -sin_ref[at, :])
                qkv_grad[s, at, h * head : (h + 1) * head] = q_grad.astype(BF)
                key_total = key_total + dot(s_grad, qkv[0, n, at, :], 0, 0)
                value_total = value_total + dot(p_low, cot[at], 0, 0)
            k_grad = spin(key_total * head ** (-0.5), cos_ref[...], -sin_ref[...])
            a = pair + h * head
            qkv_grad[s, :, a : a + head] = k_grad.astype(BF)
            qkv_grad[s, :, a + pair : a + pair + head] = value_total.astype(BF)

    def first_grad(s):
        for d in range(dp):
            block = weights[block_of(d) + (slice(None), slice(0, 3 * pair))]
            total = dot(qkv_grad[s], block, 1, 1)
            three[1 + s, :, slab(d)] = total.astype(BF)
            unit_block = tok[s, :, slab(d)].astype(F32) * scales[s]
            row = jnp.sum(total * unit_block, axis=0, keepdims=True)
            vectors[2 + s : 3 + s, slab(d)] = row

    attention(1)
    first_grad(1)
    part_pass = c.remote(three.at[2], part_in, dp=sibling)
    part_pass.start()
    units += add_over(2)
    attention(0)
    first_grad(0)
    part_pass.wait_recv()
    first_scatter = []
    for r in list(range(1, depth)) + [0]:
        at = at_of((z + r) % depth)
        total = three[1, at, :].astype(F32) + part_in[at, :].astype(F32)
        if r:
            three[1, at, :] = total.astype(BF)
            peer = (z + r) % depth
            copy = c.remote(three.at[1, at], scatter_in.at[1, r - 1], tensor=peer)
            copy.start()
            first_scatter.append(copy)
        else:
            keep[1] = total

    for d in range(dp):
        total = jnp.zeros((slice_width, 3 * pair), F32)
        out_total = jnp.zeros((slice_width, pair), F32)
        for s in range(2):
            data = tok[s, :, slab(d)].astype(F32) * scales[s] * gain_rows[0:1, slab(d)]
            total = total + dot(data.astype(BF), qkv_grad[s], 0, 0)
            out_total = out_total + dot(back[s, :, slab(d)], mix_ref[s], 0, 0)
        total_a[block_of(d) + (slice(None), slice(0, 3 * pair))] = total.astype(BF)
        total_a[block_of(d) + (slice(None), slice(3 * pair, 4 * pair))] = out_total.astype(BF)

    half = 2 * pair

    def index(y_at, x_at, k):
        return (y_at, x_at, slice(None), slice(None), pl.ds(k * half, half))

    every = pl.ds(0, 2)
    qk_first = c.remote(
        total_a.at[index(pl.ds(1 - y, 1), every, 0)], first_qk, dp=peer_of(me, 4)
    )
    vo_first = c.remote(
        total_a.at[index(every, pl.ds(1 - x, 1), 1)], first_vo, dp=peer_of(me, 2)
    )
    qk_first.start()
    vo_first.start()

    norm_load = c.local(norm_hbm.at[0], three.at[0])
    norm_load.start()
    norm_load.wait()
    router_part = dot(back[0, :, width:], three[0], 0, 0)
    ones = jnp.ones((16, seq_len), BF)
    bias_row = dot(ones, qkv_grad[0]) + dot(ones, qkv_grad[1])
    lane = lax.broadcasted_iota(jnp.int32, bias_row.shape, 1)
    sub = lax.broadcasted_iota(jnp.int32, bias_row.shape, 0)
    head_slice = head // dp
    bias_rows = jnp.where(lane % head // head_slice == sub, bias_row, 0.0)
    high = bias_rows.astype(BF)
    low = (bias_rows - high.astype(F32)).astype(BF)
    lane = lax.broadcasted_iota(jnp.int32, (3 * pair, slice_width), 1)
    sub = lax.broadcasted_iota(jnp.int32, (3 * pair, slice_width), 0)
    place = (sub // head * head_slice + sub % head_slice == lane).astype(F32).astype(BF)
    bias_rows = dot(high, place) + dot(low, place)
    sub = lax.broadcasted_iota(jnp.int32, (16, slice_width), 0)
    misc_copies = []
    for d in range(dp):
        tile = jnp.where(sub <= experts, router_part[:16, slab(d)], 0.0)
        tile = jnp.where(sub == experts + 1 + core, bias_rows[d : d + 1], tile)
        gain_one = vectors[2:3, slab(d)] + vectors[3:4, slab(d)]
        tile = jnp.where(sub == experts + 3, gain_one, tile)
        tile = jnp.where(sub == experts + 4, vectors[1:2, slab(d)], tile)
        misc_part[d] = tile
    for r in range(1, dp):
        to = peer_of(me, r)
        misc_copies.append(c.remote(misc_part.at[to], misc_in.at[r - 1], dp=to))
        misc_copies[-1].start()

    qk_first.wait()
    mine = index(pl.ds(y, 1), every, 0)
    total_a[mine] = (total_a[mine].astype(F32) + first_qk[...].astype(F32)).astype(BF)
    qk_second = c.remote(
        total_a.at[index(pl.ds(y, 1), pl.ds(1 - x, 1), 0)], second_in.at[0], dp=peer_of(me, 2)
    )
    qk_second.start()
    vo_first.wait()
    mine = index(every, pl.ds(x, 1), 1)
    total_a[mine] = (total_a[mine].astype(F32) + first_vo[...].astype(F32)).astype(BF)
    vo_second = c.remote(
        total_a.at[index(pl.ds(1 - y, 1), pl.ds(x, 1), 1)], second_in.at[1], dp=peer_of(me, 4)
    )
    vo_second.start()

    total = misc_part[me]
    for r, copy in enumerate(misc_copies):
        copy.wait_recv()
        total = total + misc_in[r]
    misc_out[...] = total
    gain_copies = []
    for r in range(1, depth):
        peer = (z + r) % depth
        gain_copies.append(c.remote(misc_out.at[8:16], gains_in.at[r - 1], tensor=peer))
        gain_copies[-1].start()

    finals = []
    for k, copy in enumerate((qk_second, vo_second)):
        copy.wait()
        mine = (y, x, slice(None), slice(None), pl.ds(k * half, half))
        total_a[mine] = (
            total_a[mine].astype(F32) + second_in[k, 0, 0].astype(F32)
        ).astype(BF)
        for other in (True, False):
            to = 1 - core if other else core
            source = total_a.at[y, x, to, :, pl.ds(k * half, half)]
            place = attn_out.at[core, :, pl.ds(k * half, half)]
            finals.append(c.remote(source, place, dp=sibling) if other else c.local(source, place))
            finals[-1].start()

    for copy in first_scatter:
        copy.wait_recv()
    total = keep[1]
    for r in range(1, depth):
        total = total + scatter_in[1, r - 1].astype(F32)
    total = total * gain_rows[0:1, :]
    scale = scales[0, at_of(z), :]
    unit = tok[0, at_of(z), :].astype(F32) * scale
    total = keep[0] + scale * (total - unit * jnp.mean(total * unit, axis=-1, keepdims=True))
    input_ref[...] = total.astype(BF)

    total = misc_out[8:16, :]
    for r, copy in enumerate(gain_copies):
        copy.wait()
        total = total + gains_in[r]
    gains_out[...] = total
    for copy in finals + units:
        copy.wait()
    line.finish()
    for copy in over[1:] + small + first_scatter + misc_copies + [part_pass]:
        copy.wait_send()


def backward_call(dp, depth, experts, head, in_vmem, in_hbm):
    output_rows, width = in_vmem[6].shape
    seq_len = output_rows * depth
    slice_width = width // dp
    units = in_hbm[3].shape[1:]
    pair = in_hbm[11].shape[2]
    pairs = pair // head
    vmem, hbm = pl.BlockSpec(memory_space=pltpu.VMEM), pl.BlockSpec(memory_space=pl.ANY)
    shape = jax.ShapeDtypeStruct
    final = shape((4,) + units, BF)
    return pl.pallas_call(
        functools.partial(backward_body, (dp, depth, experts, head)),
        in_specs=[vmem] * len(in_vmem) + [hbm] * len(in_hbm),
        out_specs=[vmem, hbm, hbm, hbm, vmem, vmem, vmem],
        out_shape=[
            shape((output_rows, width), BF),
            final,
            final,
            final,
            shape((2, slice_width, 4 * pair), BF),
            shape((16, slice_width), F32),
            shape((8, slice_width), F32),
        ],
        scratch_shapes=[
            pltpu.VMEM((4,) + units, BF),
            pltpu.VMEM((3, 4) + units, BF),
            pltpu.VMEM((3, seq_len, width), BF),
            pltpu.VMEM((2, depth - 1, output_rows, width), BF),
            pltpu.VMEM((seq_len, 128), F32),
            pltpu.VMEM((depth - 1, output_rows, 128), F32),
            pltpu.VMEM((2, seq_len, width + 128), BF),
            pltpu.VMEM((2, seq_len, width), BF),
            pltpu.VMEM((2, 2, 2, slice_width, 4 * pair), BF),
            pltpu.VMEM((3, 2 * pairs, seq_len, head), BF),
            pltpu.VMEM((2 * pairs, seq_len, seq_len), BF),
            pltpu.VMEM((2, seq_len, pair), BF),
            pltpu.VMEM((2, seq_len, 1), F32),
            pltpu.VMEM((2, seq_len, 3 * pair), BF),
            pltpu.VMEM((seq_len, width), BF),
            pltpu.VMEM((2, output_rows, width), F32),
            pltpu.VMEM((2, 2, 2, slice_width, 4 * pair), BF),
            pltpu.VMEM((1, 2, 2, slice_width, 2 * pair), BF),
            pltpu.VMEM((2, 1, 2, slice_width, 2 * pair), BF),
            pltpu.VMEM((2, 1, 1, 2, slice_width, 2 * pair), BF),
            pltpu.VMEM((dp, 16, slice_width), F32),
            pltpu.VMEM((dp - 1, 16, slice_width), F32),
            pltpu.VMEM((depth - 1, 8, slice_width), F32),
            pltpu.VMEM((8, width), F32),
            pltpu.SemaphoreType.DMA((96,)),
            pltpu.SemaphoreType.DMA((96,)),
            pltpu.SemaphoreType.DMA((40,)),
        ],
        compiler_params=pltpu.CompilerParams(
            collective_id=1, has_side_effects=True, vmem_limit_bytes=62 * 2**20
        ),
    )(*in_vmem, *in_hbm)


def finish_body(
    gate_ref, up_ref, down_ref, attn_ref, eg_ref, eu_ref, ed_ref, sg_ref, su_ref, sd_ref,
    q_ref, k_ref, v_ref, o_ref, sg_rows, su_rows
):
    group, groups = pl.program_id(0), pl.num_programs(0)
    many, rows, _ = eg_ref.shape
    for source, routed, shared in (
        (gate_ref, eg_ref, sg_rows.at[group]),
        (up_ref, eu_ref, su_rows.at[group]),
        (down_ref, ed_ref, sd_ref),
    ):
        for unit in range(many):
            routed[unit] = source[0, unit].astype(F32)
        shared[...] = source[0, many].astype(F32)

    @pl.when(group == 0)
    def _():
        pair = attn_ref.shape[2] // 4
        for c in range(2):
            at = slice(c * pair, (c + 1) * pair)
            for kind, out_ref in enumerate((q_ref, k_ref, v_ref)):
                out_ref[:, at] = attn_ref[c, :, kind * pair : (kind + 1) * pair].astype(F32)
            o_ref[at, :] = jnp.transpose(attn_ref[c, :, 3 * pair :].astype(F32))

    @pl.when(group == groups - 1)
    def _():
        for source, out_ref in ((sg_rows, sg_ref), (su_rows, su_ref)):
            out_ref[...] = jnp.transpose(source[...].reshape(groups * rows, -1))


def finish_call(gate, up, down, attn):
    groups, units, rows, slice_width = gate.shape
    many, pair = units - 1, attn.shape[2] // 4
    shape = jax.ShapeDtypeStruct

    def whole(*dims):
        return pl.BlockSpec(dims, lambda g: (0,) * len(dims))

    source = pl.BlockSpec((1, units, rows, slice_width), lambda g: (g, 0, 0, 0))
    routed = pl.BlockSpec((many, rows, slice_width), lambda g: (g, 0, 0))
    return call(
        finish_body,
        (groups,),
        [source] * 3 + [whole(*attn.shape)],
        [routed] * 3
        + [whole(slice_width, groups * rows)] * 2
        + [pl.BlockSpec((rows, slice_width), lambda g: (g, 0))]
        + [whole(slice_width, 2 * pair)] * 3
        + [whole(2 * pair, slice_width)],
        [shape((groups * many, rows, slice_width), F32)] * 3
        + [shape((slice_width, groups * rows), F32)] * 2
        + [shape((groups * rows, slice_width), F32)]
        + [shape((slice_width, 2 * pair), F32)] * 3
        + [shape((2 * pair, slice_width), F32)],
        0,
        groups * units * rows * slice_width * 18,
        [pltpu.VMEM((groups, rows, slice_width), F32)] * 2,
    )(gate, up, down, attn)


def local_plain(
    dp,
    tokens,
    picture_ids,
    routes,
    slot_order,
    norm_gains,
    w_query,
    w_key,
    w_value,
    w_out,
    qkv_bias,
    router,
    shared_gate,
    shared_up,
    shared_down,
    expert_gate,
    expert_up,
    expert_down,
    out_grad,
):
    seq_len = picture_ids.shape[0]
    local_rows = tokens.shape[0]
    width = tokens.shape[1]
    experts, slice_width, hidden_units = expert_gate.shape
    top_count = routes.shape[1]
    capacity = 5 * seq_len * top_count // (4 * experts)
    heads_local = qkv_bias.shape[1]
    head_width = w_query.shape[1] // heads_local
    pair_heads = heads_local // 2
    pair_width = pair_heads * head_width
    mine_experts = experts // 4
    hidden_pad = -(-hidden_units // 128) * 128

    me = lax.axis_index("dp")
    zi = lax.axis_index("tensor")
    core, xi = me % 2, (me // 2) % 2
    group = me % 4
    bits = []
    while 2 ** (len(bits) + 1) <= dp:
        bits.append(2 ** len(bits))
    upper = bits[2:]

    def swap(array, bit):
        return lax.ppermute(array, "dp", [(i, i ^ bit) for i in range(dp)])

    def bit_of(bit):
        return (me // bit) % 2

    def join(mine, theirs, bit, axis):
        n = mine.shape[axis]
        shape = list(mine.shape)
        shape[axis] = 2 * n
        out = jnp.zeros(shape, mine.dtype)
        out = lax.dynamic_update_slice_in_dim(out, mine, n * bit_of(bit), axis)
        return lax.dynamic_update_slice_in_dim(out, theirs, n * (1 - bit_of(bit)), axis)

    def half(array, which, axis):
        n = array.shape[axis] // 2
        return lax.dynamic_slice_in_dim(array, which * n, n, axis)

    gains_z = lax.all_gather(norm_gains, "tensor", axis=1, tiled=True)
    misc_rows = 16
    bias_width = 3 * pair_heads * qkv_bias.shape[2]
    bias_cores = qkv_bias.reshape(3, 2, -1).swapaxes(0, 1).reshape(2, bias_width)

    def misc_pack(core_bias):
        wide = jnp.zeros((misc_rows, 2 * pair_width), BF)
        wide = wide.at[: experts + 1, :slice_width].set(router.T)
        wide = wide.at[experts + 1, :bias_width].set(core_bias)
        return wide.at[experts + 2 : experts + 4, :slice_width].set(gains_z)

    qk = jnp.concatenate(
        [w.reshape(slice_width, 2, pair_width) for w in (w_query, w_key)], axis=2
    )
    qk = jnp.concatenate(
        [qk, jnp.stack([misc_pack(bias_cores[0]), misc_pack(bias_cores[1])], axis=1)], axis=0
    )
    vo = jnp.concatenate(
        [w.reshape(slice_width, 2, pair_width) for w in (w_value, w_out.T)], axis=2
    )
    tokens_z = lax.all_gather(tokens, "tensor", axis=0, tiled=True)

    def gather_attention(pack, order):
        dims = (1,) * len(bits[1:])
        both = join(pick(pack, core, 1)[None], swap(pick(pack, 1 - core, 1), 1)[None], 1, 0)
        both = both.reshape(dims + both.shape)
        for bit in order:
            axis = len(bits) - 1 - bits.index(bit)
            both = join(both, swap(both, bit), bit, axis)
        return both.reshape((dp,) + both.shape[-2:])

    qk_all = gather_attention(qk, bits[1:])
    vo_full = gather_attention(vo, bits[:0:-1]).reshape(width, 2 * pair_width)
    qk_full = qk_all[:, :slice_width].reshape(width, 2 * pair_width)
    misc = qk_all[:, slice_width:]
    router_full = misc[:, : experts + 1, :slice_width].swapaxes(1, 2).reshape(width, -1)
    gain_rows = misc[:, experts + 2 : experts + 4, :slice_width].swapaxes(0, 1)
    gain_rows = gain_rows.reshape(2, width).astype(F32)
    bias = misc[:, experts + 1, :bias_width].astype(F32)
    bias = bias.reshape(dp, 3 * pair_heads, -1).swapaxes(0, 1).reshape(3, pair_width)

    tokens_sib = swap(tokens_z, 1)
    grad_z = lax.all_gather(out_grad, "tensor", axis=0, tiled=True)

    codes = jnp.concatenate([routes, slot_order], axis=1).T
    codes_x = swap(codes, 2)
    both_codes = swap(jnp.stack([codes, codes_x]), 1)
    codes_a = jnp.stack([codes, both_codes[0]])
    codes_b = jnp.stack([codes_x, both_codes[1]])
    pictures = jnp.stack([picture_ids, swap(picture_ids, 1)])

    def core_units(routed, shared):
        routed = routed.reshape(2, 2, mine_experts, hidden_units, slice_width)
        shared = shared.reshape(2, 2, 1, hidden_units, slice_width)

        def cut(which):
            return jnp.concatenate([pick(routed, which, 1), pick(shared, which, 1)], axis=1)

        return join(cut(core), swap(cut(1 - core), 1), 1, 3)

    def x_units(held):
        return join(pick(held, xi, 0), swap(pick(held, 1 - xi, 0), 2), 2, 2)

    def upper_units(held):
        for bit in upper[:-1]:
            held = join(held, swap(held, bit), bit, 2)
        return held, swap(held, upper[-1])

    def padded(*pairs):
        n = pairs[0][0].shape[-1]
        out = jnp.zeros((mine_experts + 1, len(pairs) * hidden_pad, 2 * n), BF)
        zero = jnp.int32(0)
        for k, (mine, theirs) in enumerate(pairs):
            row = jnp.int32(k * hidden_pad)
            out = lax.dynamic_update_slice(out, mine, (zero, row, n * bit_of(upper[-1])))
            out = lax.dynamic_update_slice(out, theirs, (zero, row, n * (1 - bit_of(upper[-1]))))
        return out

    down_c = core_units(expert_down, shared_down)
    gate_c = core_units(expert_gate.swapaxes(1, 2), shared_gate.T)
    up_c = core_units(expert_up.swapaxes(1, 2), shared_up.T)
    down_x = x_units(down_c)
    gate_x = x_units(gate_c)
    up_x = x_units(up_c)
    grad_x = swap(after(grad_z, up_x), 2)
    down_y = upper_units(down_x)
    gate_y = upper_units(gate_x)
    up_y = upper_units(up_x)

    rows_f = jnp.stack([tokens_z, tokens_sib]).astype(F32)
    qk_full = after(qk_full, down_c, gate_c, up_c)
    first_scale = lax.rsqrt(jnp.mean(rows_f * rows_f, axis=-1, keepdims=True) + EPS)
    first_norm = (rows_f * first_scale * gain_rows[0]).astype(BF)
    qk_pre = einsum("std,df->stf", first_norm, qk_full) + jnp.concatenate([bias[0], bias[1]])
    values = (einsum("std,df->stf", first_norm, vo_full[:, :pair_width]) + bias[2]).astype(BF)
    cos_part, sin_part = rope_tables(seq_len, head_width)
    qk_rot = rotate(
        qk_pre.reshape(2, seq_len, 2 * pair_heads, head_width), cos_part, sin_part
    ).astype(BF)
    qk_rot = after(qk_rot, down_x)
    queries, keys = qk_rot[:, :, :pair_heads], qk_rot[:, :, pair_heads:]
    values = values.reshape(2, seq_len, pair_heads, head_width)
    positions = jnp.arange(seq_len, dtype=jnp.int32)
    allowed = jnp.logical_or(
        positions[None, None, :] <= positions[None, :, None],
        pictures[:, :, None] * pictures[:, None, :] > 0,
    )
    score_scale = head_width ** (-0.5)
    scores = einsum("sqhd,skhd->shqk", queries, keys) * score_scale
    scores = jnp.where(allowed[:, None], scores, -1e30)
    weights = jnp.exp(scores - jnp.max(scores, axis=-1, keepdims=True))
    probs = weights / jnp.sum(weights, axis=-1, keepdims=True)
    probs_low = probs.astype(BF)
    head_mix = einsum("shqk,skhd->sqhd", probs_low, values).astype(BF)
    heads_out = after(head_mix.reshape(2, seq_len, pair_width), gate_x)
    out_weight = vo_full[:, pair_width:]
    attn_part = einsum("sqf,df->sqd", heads_out, out_weight)

    def core_sum(own, sibling):
        return own + swap(sibling.astype(BF), 1).astype(F32)

    def z_scatter(array):
        return lax.psum_scatter(
            array.astype(BF), "tensor", scatter_dimension=0, tiled=True
        ).astype(F32)

    inputs = tokens.astype(F32)
    hidden = inputs + z_scatter(core_sum(attn_part[0], attn_part[1]))
    hidden = after(hidden, up_x, down_y[1])
    second_scale = lax.rsqrt(jnp.mean(hidden * hidden, axis=-1, keepdims=True) + EPS)
    second_unit = hidden * second_scale
    second_norm = (second_unit * gain_rows[1]).astype(BF)
    norm_z = lax.all_gather(second_norm, "tensor", axis=0, tiled=True)
    norm_z = after(norm_z, gate_y[1], grad_x)
    down_all = padded(down_y)
    gateup_all = padded(gate_y, up_y)

    norm_x = swap(norm_z, 2)
    norm_a = jnp.stack([norm_z, swap(norm_z, 1)])
    norm_b = jnp.stack([norm_x, swap(norm_x, 1)])
    grad_a = jnp.stack([grad_z, swap(grad_z, 1)])
    grad_b = jnp.stack([grad_x, swap(grad_x, 1)])

    expert_ids = group * mine_experts + jnp.arange(mine_experts, dtype=jnp.int32)

    router_rows = jnp.pad(router_full.T, ((0, 16 - experts - 1), (0, 0)))
    group_ids = group.astype(jnp.int32).reshape(1)

    def slots_of(codes_in):
        routes_in, slots_in = codes_in[:, None, :top_count], codes_in[:, None, top_count:]
        matches = routes_in == expert_ids[None, :, None, None]
        return jnp.max(jnp.where(matches, slots_in, -1), axis=2)

    def feed(slots, rows, grads):
        slotted, slot_grad, pair, act, terms, pair_s, act_s, inner_s, probs_out = plain_act_call(
            experts, capacity, group_ids, slots, rows, grads, router_rows, gateup_all, down_all
        )
        terms = jnp.concatenate([terms.swapaxes(1, 2), inner_s], axis=-1)
        flat = [a.reshape(mine_experts, -1, a.shape[-1]) for a in (slotted, slot_grad, pair, act)]
        shared = [a.reshape(1, -1, a.shape[-1]) for a in (rows, grads, pair_s, act_s)]
        return (pair, pair_s), (act, act_s), terms, (flat, shared), probs_out

    slots_a, slots_b = slots_of(codes_a), slots_of(codes_b)
    fed_a = feed(slots_a, norm_a, grad_a)
    fed_b = feed(slots_b, norm_b, grad_b)
    columns_a, columns_b = slots_a[..., None], slots_b[..., None]
    row_grad_b = plain_back_call(columns_b, *fed_b[0], gateup_all)
    row_grad_a = plain_back_call(after(columns_a, row_grad_b), *fed_a[0], gateup_all)
    row_out_b = plain_back_call(after(columns_b, row_grad_a), *fed_b[1], down_all)
    row_out_a = plain_back_call(columns_a, *fed_a[1], down_all)

    def spread(terms):
        wide = jnp.zeros(terms.shape[:-1] + (128,), F32)
        wide = lax.dynamic_update_slice_in_dim(
            wide, terms[..., :mine_experts], group * mine_experts, terms.ndim - 1
        )
        return wide.at[..., experts].set(terms[..., mine_experts])

    def group_sum(a, b):
        across = b[0].astype(F32) + swap(b[1].astype(BF), 1).astype(F32)
        near = a[0].astype(F32) + swap(a[1].astype(BF), 1).astype(F32)
        return near + swap(across.astype(BF), 2).astype(F32)

    grad_sum = group_sum(row_grad_a, row_grad_b)
    term_sum = group_sum(spread(fed_a[2]), spread(fed_b[2]))
    packed = z_scatter(jnp.concatenate([grad_sum, term_sum], axis=-1))
    second_grad, gate_sums = packed[:, :width], packed[:, width:]

    data_a, data_b = fed_a[3], fed_b[3]

    def unit_grads(left, right):
        return jnp.concatenate(
            [
                plain_outer_call(
                    hidden_units,
                    hidden_pad,
                    dp,
                    [(data[k][left], data[k][right]) for data in (data_a, data_b)],
                )
                for k in range(2)
            ],
            axis=1,
        )

    def scatter_units(total):
        total = total.reshape((2,) * len(bits) + total.shape[1:])
        for bit in reversed(upper):
            axis = len(bits) - 1 - bits.index(bit)
            sent = half(total, 1 - bit_of(bit), axis)
            kept = half(total, bit_of(bit), axis)
            total = (kept.astype(F32) + swap(sent, bit).astype(F32)).astype(BF)
        total = total.reshape((2, 2) + total.shape[len(bits) :])
        held = join(pick(total, xi, 0)[None], swap(pick(total, 1 - xi, 0), 2)[None], 2, 0)
        return join(pick(held, core, 1)[:, None], swap(pick(held, 1 - core, 1), 1)[:, None], 1, 1)

    def split_units(held):
        routed = held[:, :, :mine_experts].reshape(experts, -1, slice_width)
        shared = held[:, :, mine_experts]
        return routed.astype(F32), shared.astype(F32)

    gateup_sum = scatter_units(unit_grads(2, 0))
    down_sum = scatter_units(unit_grads(3, 1))
    routed_gu, shared_gu = split_units(gateup_sum)
    routed_down, shared_down_sum = split_units(down_sum)
    shared_gu = shared_gu.reshape(4, 2, hidden_units, slice_width)
    egate_sum = routed_gu[:, :hidden_units].swapaxes(1, 2)
    eup_sum = routed_gu[:, hidden_units:].swapaxes(1, 2)
    sgate_sum = shared_gu[:, 0].reshape(-1, slice_width).T
    sup_sum = shared_gu[:, 1].reshape(-1, slice_width).T
    sdown_sum = shared_down_sum.reshape(-1, slice_width)

    row_start = zi * local_rows
    probs_local = lax.dynamic_slice_in_dim(fed_a[4][0], row_start, local_rows, 1).T
    probs_mine, weight_mine = probs_local[:, :experts], probs_local[:, experts]
    route_grad = gate_sums[:, :experts]
    expert_logit_grad = probs_mine * (
        route_grad - jnp.sum(probs_mine * route_grad, axis=-1, keepdims=True)
    )
    weight_logit_grad = gate_sums[:, experts] * weight_mine * (1.0 - weight_mine)
    logits_grad = jnp.concatenate([expert_logit_grad, weight_logit_grad[:, None]], axis=1).astype(
        BF
    )
    second_grad = second_grad + einsum("tf,df->td", logits_grad, router_full)
    gain_two_grad = jnp.sum(second_grad * second_unit, axis=0)
    unit_two = second_grad * gain_rows[1]
    hidden_grad = out_grad.astype(F32) + second_scale * (
        unit_two - second_unit * jnp.mean(unit_two * second_unit, axis=-1, keepdims=True)
    )
    attention_grad = hidden_grad.astype(BF)
    wide_logits = jnp.pad(logits_grad, ((0, 0), (0, 128 - experts - 1)))
    back_z = lax.all_gather(
        jnp.concatenate([attention_grad, wide_logits], axis=1), "tensor", axis=0, tiled=True
    )
    out_sum = after(group_sum(row_out_a, row_out_b), back_z)
    output = (hidden + z_scatter(out_sum)).astype(BF)
    logits_z = back_z[:, width : width + 16]
    back_own = back_z[:, :width]
    back_rows = jnp.stack([back_own, swap(back_own, 1)])

    router_part = einsum("tf,td->fd", logits_z, norm_z)[: experts + 1]

    out_proj = einsum("std,stf->df", back_rows, heads_out)
    mix_grad = einsum("std,df->stf", back_rows, out_weight).astype(BF)
    mix_grad = mix_grad.reshape(2, seq_len, pair_heads, head_width)
    prob_grad = einsum("sqhd,skhd->shqk", mix_grad, values)
    score_grad = (
        probs * (prob_grad - jnp.sum(probs * prob_grad, axis=-1, keepdims=True))
    ).astype(BF)
    query_rot = einsum("shqk,skhd->sqhd", score_grad, keys) * score_scale
    key_rot = einsum("shqk,sqhd->skhd", score_grad, queries) * score_scale
    value_grad = einsum("shqk,sqhd->skhd", probs_low, mix_grad)
    qk_grad = rotate(jnp.concatenate([query_rot, key_rot], axis=2), cos_part, -sin_part)
    qk_grad = qk_grad.astype(BF).reshape(2, seq_len, 2 * pair_width)
    v_grad = value_grad.astype(BF).reshape(2, seq_len, pair_width)
    first_part = einsum("stf,df->std", qk_grad, qk_full) + einsum(
        "stf,df->std", v_grad, vo_full[:, :pair_width]
    )
    first_grad = z_scatter(core_sum(first_part[0], first_part[1]))

    gain_one_grad = jnp.sum(first_part * (rows_f * first_scale), axis=(0, 1))
    bias_part = jnp.concatenate(
        [jnp.sum(qk_grad.astype(F32), axis=(0, 1)), jnp.sum(v_grad.astype(F32), axis=(0, 1))]
    )
    bias_part = bias_part.reshape(3 * pair_heads, dp, -1).swapaxes(0, 1).reshape(dp, 1, -1)
    gain_part = jnp.stack([gain_one_grad, gain_two_grad]).reshape(2, dp, slice_width)

    def wide_rows(rows):
        return jnp.pad(rows, ((0, 0), (0, 0), (0, 2 * pair_width - rows.shape[2])))

    misc_part = jnp.concatenate(
        [
            wide_rows(router_part.reshape(experts + 1, dp, slice_width).swapaxes(0, 1)),
            wide_rows(bias_part),
            wide_rows(gain_part.swapaxes(0, 1)),
            jnp.zeros((dp, misc_rows - experts - 4, 2 * pair_width), F32),
        ],
        axis=1,
    )
    qk_total = einsum("std,stf->df", first_norm, qk_grad).reshape(dp, slice_width, -1)
    qk_total = jnp.concatenate([qk_total, misc_part], axis=1)
    vo_total = jnp.concatenate([einsum("std,stf->df", first_norm, v_grad), out_proj], axis=1)
    vo_total = vo_total.reshape(dp, slice_width, -1)

    def scatter_attention(total, order):
        total = total.reshape((2,) * len(bits) + total.shape[1:])
        for bit in order:
            axis = len(bits) - 1 - bits.index(bit)
            sent = half(total, 1 - bit_of(bit), axis).astype(BF)
            total = half(total, bit_of(bit), axis) + swap(sent, bit).astype(F32)
        total = total.reshape((2,) + total.shape[-2:]).astype(BF)
        return pick(total, core, 0), swap(pick(total, 1 - core, 0), 1)

    def columns_of(mine, theirs):
        held = join(mine[:slice_width, None], theirs[:slice_width, None], 1, 1)
        first, second = held[..., :pair_width], held[..., pair_width:]
        return (
            first.reshape(slice_width, -1).astype(F32),
            second.reshape(slice_width, -1).astype(F32),
        )

    qk_mine, qk_theirs = scatter_attention(qk_total, bits[:0:-1])
    vo_mine, vo_theirs = scatter_attention(vo_total, bits[1:])
    qk_sums = columns_of(qk_mine, qk_theirs)
    vo_sums = columns_of(vo_mine, vo_theirs)
    misc_mine = qk_mine[slice_width:].astype(F32)
    misc_theirs = qk_theirs[slice_width:].astype(F32)
    misc_sum = misc_mine + misc_theirs
    router_sum = misc_sum[: experts + 1, :slice_width].T
    bias_sums = join(
        misc_mine[experts + 1, :bias_width].reshape(3, 1, pair_heads, -1),
        misc_theirs[experts + 1, :bias_width].reshape(3, 1, pair_heads, -1),
        1,
        1,
    ).reshape(3, heads_local, -1)
    gain_sums = lax.all_gather(
        misc_sum[experts + 2 : experts + 4, :slice_width], "tensor", axis=0, tiled=False
    )
    tensor = gain_sums.shape[0]
    gain_sums = jnp.sum(gain_sums, axis=0).reshape(2, tensor, -1)
    gain_sums = pick(gain_sums, zi, 1)

    unit_mine = inputs * lax.rsqrt(jnp.mean(inputs * inputs, axis=-1, keepdims=True) + EPS)
    scale_mine = lax.rsqrt(jnp.mean(inputs * inputs, axis=-1, keepdims=True) + EPS)
    unit_one = first_grad * gain_rows[0]
    input_grad = hidden_grad + scale_mine * (
        unit_one - unit_mine * jnp.mean(unit_one * unit_mine, axis=-1, keepdims=True)
    )
    return (
        output,
        input_grad.astype(BF),
        gain_sums,
        qk_sums[0],
        qk_sums[1],
        vo_sums[0],
        vo_sums[1].T,
        bias_sums,
        router_sum,
        sgate_sum,
        sup_sum,
        sdown_sum,
        egate_sum,
        eup_sum,
        routed_down,
    )


def local_fused(
    dp,
    depth,
    tokens,
    picture_ids,
    routes,
    slot_order,
    norm_gains,
    w_query,
    w_key,
    w_value,
    w_out,
    qkv_bias,
    router,
    shared_gate,
    shared_up,
    shared_down,
    expert_gate,
    expert_up,
    expert_down,
    out_grad,
):
    seq_len = picture_ids.shape[0]
    local_rows = tokens.shape[0]
    width = tokens.shape[1]
    experts, slice_width, hidden_units = expert_gate.shape
    heads_local = qkv_bias.shape[1]
    head_width = w_query.shape[1] // heads_local
    pair_heads = heads_local // 2
    pair_width = pair_heads * head_width
    mine_experts = experts // 4
    hidden_pad = -(-hidden_units // 128) * 128

    zi = lax.axis_index("tensor")
    codes = jnp.concatenate([routes.T, slot_order.T, picture_ids[None]], axis=0)
    codes = jnp.pad(codes, ((0, 16 - codes.shape[0]), (0, 0)))
    bias_cores = qkv_bias.reshape(3, 2, -1).swapaxes(0, 1).reshape(2, -1)
    bias_width = bias_cores.shape[1]
    misc = jnp.zeros((16, slice_width), F32)
    misc = misc.at[: experts + 1].set(router.T.astype(F32))
    misc = misc.at[experts + 1 : experts + 3, :bias_width].set(bias_cores.astype(F32))
    gains = lax.dynamic_update_slice(
        jnp.zeros((8, slice_width), F32),
        norm_gains.astype(F32),
        (jnp.int32(0), zi * norm_gains.shape[1]),
    )
    cos_part, sin_part = rope_tables(seq_len, head_width)
    cos_rows = jnp.concatenate([cos_part, cos_part], axis=1)
    sin_rows = jnp.concatenate([-sin_part, sin_part], axis=1)
    (
        hidden,
        norm_all,
        grads_all,
        gateup_all,
        down_all,
        codes_all,
        router_rows,
        gain_rows,
        tok,
        attn_weights,
        qkv,
        probs_low,
        heads_out,
    ) = forward_call(
        dp,
        depth,
        experts,
        head_width,
        (codes, misc, gains, cos_rows, sin_rows),
        (tokens, out_grad, w_query, w_key, w_value, w_out.T),
        (
            expert_gate.swapaxes(1, 2),
            expert_up.swapaxes(1, 2),
            expert_down,
            shared_gate.T.reshape(4, hidden_units, slice_width),
            shared_up.T.reshape(4, hidden_units, slice_width),
            shared_down.reshape(4, hidden_units, slice_width),
        ),
    )
    gateup_all = gateup_all.reshape(mine_experts + 1, 2 * hidden_pad, width)
    down_all = down_all.reshape(mine_experts + 1, hidden_pad, width)
    (
        output,
        terms,
        probs_mine,
        grad_own,
        grad_sib,
        grad_far,
        gate_total,
        up_total,
        down_total,
        gate_in,
    ) = middle_call(
        dp,
        depth,
        experts,
        routes.shape[1],
        hidden_units,
        hidden,
        codes_all,
        router_rows,
        (norm_all, grads_all, gateup_all, down_all),
    )
    input_grad, gate_sum, up_sum, down_sum, attn_sum, misc_sum, gains_sum = backward_call(
        dp,
        depth,
        experts,
        head_width,
        (terms, probs_mine, router_rows, gain_rows, cos_rows, sin_rows, hidden, out_grad),
        (grad_own, grad_sib, grad_far, gate_in, gate_total, up_total, down_total)
        + (tok, attn_weights, qkv, probs_low, heads_out, norm_all),
    )

    egate_sum, eup_sum, edown_sum, sgate_sum, sup_sum, sdown_sum, *attn_sums = finish_call(
        gate_sum, up_sum, down_sum, attn_sum
    )
    bias_sums = misc_sum[experts + 1 : experts + 3, :bias_width].reshape(2, 3, pair_heads, -1)
    bias_sums = bias_sums.swapaxes(0, 1).reshape(3, heads_local, -1)
    piece = norm_gains.shape[1]
    gain_sums = lax.dynamic_slice(gains_sum[3:5], (jnp.int32(0), zi * piece), (2, piece))
    return (
        output,
        input_grad,
        gain_sums,
        *attn_sums,
        bias_sums,
        misc_sum[: experts + 1].T,
        sgate_sum,
        sup_sum,
        sdown_sum,
        egate_sum.swapaxes(1, 2),
        eup_sum.swapaxes(1, 2),
        edown_sum,
    )


def solution(mesh):
    dp, depth = mesh.shape["dp"], mesh.shape["tensor"]

    def body(*arrays):
        if arrays[5].shape[0] % 128 == 0 and dp == 8 and depth == 4:
            return local_fused(dp, depth, *arrays)
        return local_plain(dp, *arrays)

    return jax.shard_map(
        body,
        mesh=mesh,
        in_specs=(
            P(("dp", "tensor"), None),
            P("dp"),
            P("dp", None),
            P("dp", None),
            P(None, ("dp", "tensor")),
            P("dp", "tensor"),
            P("dp", "tensor"),
            P("dp", "tensor"),
            P("tensor", "dp"),
            P(None, "tensor", "dp"),
            P("dp", None),
            P("dp", "tensor"),
            P("dp", "tensor"),
            P("tensor", "dp"),
            P(None, "dp", "tensor"),
            P(None, "dp", "tensor"),
            P(None, "tensor", "dp"),
            P(("dp", "tensor"), None),
        ),
        out_specs=(
            P(("dp", "tensor"), None),
            P(("dp", "tensor"), None),
            P(None, ("dp", "tensor")),
            P("dp", "tensor"),
            P("dp", "tensor"),
            P("dp", "tensor"),
            P("tensor", "dp"),
            P(None, "tensor", "dp"),
            P("dp", None),
            P("dp", "tensor"),
            P("dp", "tensor"),
            P("tensor", "dp"),
            P(None, "dp", "tensor"),
            P(None, "dp", "tensor"),
            P(None, "tensor", "dp"),
        ),
        check_vma=False,
    )
```

```python
import functools

import jax
import jax.numpy as jnp
from jax import lax
from jax.experimental import pallas as pl
from jax.experimental.pallas import tpu as pltpu
from jax.sharding import PartitionSpec as P

EPS = 1e-06
THETA = 1000000.0
BF = jnp.bfloat16
F32 = jnp.float32


def rope_tables(length, width):
    half_width = width // 2
    inverse = THETA ** (-(2.0 * jnp.arange(half_width, dtype=F32)) / width)
    angles = jnp.arange(length, dtype=F32)[:, None] * inverse[None, :]
    return jnp.cos(angles), jnp.sin(angles)


def rotate(field_in, cos_part, sin_part):
    half_width = field_in.shape[-1] // 2
    low, high = field_in[..., :half_width], field_in[..., half_width:]
    cos_rows, sin_rows = cos_part[:, None, :], sin_part[:, None, :]
    return jnp.concatenate(
        [low * cos_rows - high * sin_rows, high * cos_rows + low * sin_rows], axis=-1
    )


def einsum(spec, *args):
    return jnp.einsum(spec, *args, preferred_element_type=F32)


def silu_parts(gate_in):
    gate_sig = jax.nn.sigmoid(gate_in)
    return gate_in * gate_sig, gate_sig * (1.0 + gate_in * (1.0 - gate_sig))


def after(array, *others):
    return lax.optimization_barrier((array,) + others)[0]


def pick(array, index, axis):
    return lax.dynamic_index_in_dim(array, index, axis, keepdims=False)


VMEM_LIMIT = 58 * 2**20


def dot(left, right, left_dim=1, right_dim=0):
    return lax.dot_general(
        left, right, (((left_dim,), (right_dim,)), ((), ())), preferred_element_type=F32
    )


def call(body, grid, in_specs, out_specs, out_shape, flops, moved, scratch=()):
    return pl.pallas_call(
        body,
        grid=grid,
        in_specs=in_specs,
        out_specs=out_specs,
        out_shape=out_shape,
        scratch_shapes=scratch,
        cost_estimate=pl.CostEstimate(flops=flops, bytes_accessed=moved, transcendentals=0),
        compiler_params=pltpu.CompilerParams(vmem_limit_bytes=VMEM_LIMIT),
    )


def plain_act_body(
    experts,
    units,
    group_ref,
    slot_ref,
    rows_ref,
    grads_ref,
    router_ref,
    gateup_ref,
    down_ref,
    slotted_ref,
    slotgrad_ref,
    pair_ref,
    act_ref,
    terms_ref,
    pair_s_ref,
    act_s_ref,
    inner_s_ref,
    probs_ref,
):
    unit = pl.program_id(1)
    half = gateup_ref.shape[1] // 2
    seq_len = rows_ref.shape[1]
    capacity = slotted_ref.shape[2]

    @pl.when(unit == 0)
    def _():
        logits = dot(router_ref[...], rows_ref[0], 1, 1)
        row = lax.broadcasted_iota(jnp.int32, logits.shape, 0)
        routed = jnp.where(row < experts, logits, -1e30)
        raised = jnp.exp(routed - jnp.max(routed, axis=0, keepdims=True))
        soft = raised / jnp.sum(raised, axis=0, keepdims=True)
        probs_ref[0] = jnp.where(row < experts, soft, jax.nn.sigmoid(logits))

    def parts(data, cot, weight):
        both = dot(data, gateup_ref[0], 1, 1)
        cot_in = dot(cot, down_ref[0], 1, 1)
        gate_in, up_in = both[:, :half], both[:, half:]
        gate_act, gate_slope = silu_parts(gate_in)
        act = gate_act * up_in
        inner = jnp.sum(act.astype(BF).astype(F32) * cot_in, axis=1, keepdims=True)
        cot_in = cot_in * weight
        return (
            (act * weight).astype(BF),
            (cot_in * up_in * gate_slope).astype(BF),
            (cot_in * gate_act).astype(BF),
            inner,
        )

    @pl.when(unit < units - 1)
    def _():
        slot = slot_ref[0, pl.ds(unit, 1), :]
        mask = lax.broadcasted_iota(jnp.int32, (capacity, seq_len), 0) == slot
        onehot = mask.astype(F32).astype(BF)
        slotted_ref[0, 0] = dot(onehot, rows_ref[0]).astype(BF)
        slotgrad_ref[0, 0] = dot(onehot, grads_ref[0]).astype(BF)
        probs = probs_ref[0]
        row = lax.broadcasted_iota(jnp.int32, probs.shape, 0)
        expert = group_ref[0] * (units - 1) + unit
        gate = jnp.sum(jnp.where(row == expert, probs, 0.0), axis=0, keepdims=True)
        weight = jnp.sum(jnp.where(mask, gate, 0.0), axis=1, keepdims=True)
        act, gate_grad, up_grad, inner = parts(slotted_ref[0, 0], slotgrad_ref[0, 0], weight)
        act_ref[0, 0] = act
        pair_ref[0, 0, :, :half] = gate_grad
        pair_ref[0, 0, :, half:] = up_grad
        terms_ref[0, pl.ds(unit, 1), :] = jnp.sum(
            jnp.where(mask, inner, 0.0), axis=0, keepdims=True
        )

    @pl.when(unit == units - 1)
    def _():
        logits = dot(rows_ref[0], router_ref[...], 1, 1)
        weight = jax.nn.sigmoid(logits[:, experts : experts + 1])
        act, gate_grad, up_grad, inner = parts(rows_ref[0], grads_ref[0], weight)
        act_s_ref[0] = act
        pair_s_ref[0, :, :half] = gate_grad
        pair_s_ref[0, :, half:] = up_grad
        inner_s_ref[0] = inner


def plain_act_call(experts, capacity, group, slots, rows, grads, router, gateup, down):
    count, seq_len, width = rows.shape
    units, wide, _ = gateup.shape
    half = wide // 2
    routed = units - 1

    def seq(s, u):
        return (s, 0, 0)

    def unit(s, u):
        return (u, 0, 0)

    def slot(s, u):
        return (jnp.minimum(u, routed - 1), s, 0, 0)

    work = count * (routed * capacity + seq_len) * width
    return call(
        functools.partial(plain_act_body, experts, units),
        (count, units),
        [
            pl.BlockSpec(memory_space=pltpu.SMEM),
            pl.BlockSpec((1, routed, seq_len), seq),
            pl.BlockSpec((1, seq_len, width), seq),
            pl.BlockSpec((1, seq_len, width), seq),
            pl.BlockSpec(router.shape, lambda s, u: (0, 0)),
            pl.BlockSpec((1, wide, width), unit),
            pl.BlockSpec((1, half, width), unit),
        ],
        [
            pl.BlockSpec((1, 1, capacity, width), slot),
            pl.BlockSpec((1, 1, capacity, width), slot),
            pl.BlockSpec((1, 1, capacity, wide), slot),
            pl.BlockSpec((1, 1, capacity, half), slot),
            pl.BlockSpec((1, routed, seq_len), seq),
            pl.BlockSpec((1, seq_len, wide), seq),
            pl.BlockSpec((1, seq_len, half), seq),
            pl.BlockSpec((1, seq_len, 1), seq),
            pl.BlockSpec((1,) + (router.shape[0], seq_len), seq),
        ],
        [
            jax.ShapeDtypeStruct((routed, count, capacity, width), BF),
            jax.ShapeDtypeStruct((routed, count, capacity, width), BF),
            jax.ShapeDtypeStruct((routed, count, capacity, wide), BF),
            jax.ShapeDtypeStruct((routed, count, capacity, half), BF),
            jax.ShapeDtypeStruct((count, routed, seq_len), F32),
            jax.ShapeDtypeStruct((count, seq_len, wide), BF),
            jax.ShapeDtypeStruct((count, seq_len, half), BF),
            jax.ShapeDtypeStruct((count, seq_len, 1), F32),
            jax.ShapeDtypeStruct((count, router.shape[0], seq_len), F32),
        ],
        2 * work * 3 * half + 4 * count * routed * capacity * seq_len * width,
        8 * count * seq_len * width * 2,
    )(group, slots, rows, grads, router, gateup, down)


def plain_back_body(slot_ref, routed_ref, shared_ref, weight_ref, out_ref):
    routed, _, capacity, _ = routed_ref.shape
    seq_len = shared_ref.shape[1]
    total = dot(shared_ref[0], weight_ref[routed])
    lane = lax.broadcasted_iota(jnp.int32, (seq_len, capacity), 1)
    for e in range(routed):
        slot_rows = dot(routed_ref[e, 0], weight_ref[e]).astype(BF)
        onehot = (lane == slot_ref[0, e]).astype(F32).astype(BF)
        total = total + dot(onehot, slot_rows)
    out_ref[0] = total.astype(BF)


def plain_back_call(slots, routed, shared, weight):
    units, wide, width = weight.shape
    count, seq_len, _ = shared.shape
    capacity = routed.shape[2]
    block = min(width, 512)
    work = count * ((units - 1) * capacity + seq_len) * width
    return call(
        plain_back_body,
        (width // block, count),
        [
            pl.BlockSpec((1, units - 1, seq_len, 1), lambda j, s: (s, 0, 0, 0)),
            pl.BlockSpec((units - 1, 1, capacity, wide), lambda j, s: (0, s, 0, 0)),
            pl.BlockSpec((1, seq_len, wide), lambda j, s: (s, 0, 0)),
            pl.BlockSpec((units, wide, block), lambda j, s: (0, 0, j)),
        ],
        pl.BlockSpec((1, seq_len, block), lambda j, s: (s, 0, j)),
        jax.ShapeDtypeStruct((count, seq_len, width), BF),
        2 * work * wide + 2 * count * (units - 1) * capacity * seq_len * width,
        units * wide * width * 2 + count * seq_len * width * 2,
    )(slots, routed, shared, weight)


def plain_outer_body(keep, pad, left_a, right_a, left_b, right_b, out_ref):
    total = dot(left_a[0], right_a[0], 0, 0) + dot(left_b[0], right_b[0], 0, 0)
    total = total.astype(BF)
    blocks, _, rows, slice_width = out_ref.shape
    for part in range(rows // keep):
        for k in range(blocks):
            out_ref[k, 0, part * keep : (part + 1) * keep] = total[
                part * pad : part * pad + keep, k * slice_width : (k + 1) * slice_width
            ]


def plain_outer_call(keep, pad, dp, pairs):
    (left_a, right_a), (left_b, right_b) = pairs
    units, rows, wide = left_a.shape
    width = right_a.shape[2]
    slice_width = width // dp
    blocks = max(1, 512 // slice_width)
    kept = wide // pad * keep

    def left(n):
        return pl.BlockSpec((1, n, wide), lambda u, j: (u, 0, 0))

    def right(n):
        return pl.BlockSpec((1, n, blocks * slice_width), lambda u, j: (u, 0, j))

    return call(
        functools.partial(plain_outer_body, keep, pad),
        (units, dp // blocks),
        [left(rows), right(rows), left(rows), right(rows)],
        pl.BlockSpec((blocks, 1, kept, slice_width), lambda u, j: (j, u, 0, 0)),
        jax.ShapeDtypeStruct((dp, units, kept, slice_width), BF),
        4 * units * rows * wide * width,
        units * rows * (wide + width) * 4,
    )(left_a, right_a, left_b, right_b)


MESH = pl.DeviceIdType.MESH


class Copies:
    def __init__(self, send, recv, here):
        self.send, self.recv, self.here = send, recv, here
        self.remote_count = self.local_count = 0

    def remote(self, src, dst, **device):
        k = self.remote_count
        self.remote_count += 1
        return pltpu.make_async_remote_copy(
            src_ref=src,
            dst_ref=dst,
            send_sem=self.send.at[k],
            recv_sem=self.recv.at[k],
            device_id=device,
            device_id_type=MESH,
        )

    def local(self, src, dst):
        k = self.local_count
        self.local_count += 1
        return pltpu.make_async_copy(src, dst, self.here.at[k])


class Line:
    def __init__(self, copies, buffer, z, depth, rows):
        self.z, self.depth = z, depth

        def piece(p):
            return buffer.at[pl.ds(pl.multiple_of(p * rows, rows), rows)]

        def make(k, sign):
            p = z - sign * k
            return copies.remote(piece(p), piece(p), tensor=z + sign)

        self.ups = [make(k, 1) for k in range(depth - 1)]
        self.downs = [make(k, -1) for k in range(depth - 1)]

    def sends(self, k):
        z, top = self.z, self.depth - 1
        return (
            (self.ups[k], jnp.logical_and(z < top, z >= k)),
            (self.downs[k], jnp.logical_and(z > 0, z + k <= top)),
        )

    def begin(self):
        for copy, there in self.sends(0):
            pl.when(there)(copy.start)

    def finish(self):
        for k in range(self.depth - 1):
            for copy, there in self.sends(k):
                pl.when(there)(copy.wait_send)


def peer_of(me, r):
    out, bit = me, 1
    while bit <= r:
        if r & bit:
            out = out + bit - 2 * bit * (me // bit % 2)
        bit *= 2
    return out


def greet(me, z, dp, depth):
    barrier = pltpu.get_barrier_semaphore()
    for r in range(1, dp):
        pl.semaphore_signal(barrier, inc=1, device_id={"dp": peer_of(me, r)}, device_id_type=MESH)
    for r in range(1, depth):
        pl.semaphore_signal(
            barrier, inc=1, device_id={"tensor": (z + r) % depth}, device_id_type=MESH
        )
    pl.semaphore_wait(barrier, dp - 1 + depth - 1)


def spin(field, cos_rows, sin_rows):
    return field * cos_rows + pltpu.roll(field, field.shape[-1] // 2, 1) * sin_rows


def piece_of(buffer, p, rows):
    return buffer.at[pl.ds(pl.multiple_of(p * rows, rows), rows)]


def pass_on(c, source, target, z, depth, rows, sibling, passed):
    def make(p):
        return c.remote(piece_of(source, p, rows), piece_of(target, p, rows), dp=sibling)

    ups = [make(z - k) for k in range(1, depth)]
    downs = [make(z + k) for k in range(1, depth)]
    for k in range(1, depth):
        passed.append((ups[k - 1], z >= k))
        passed.append((downs[k - 1], z + k <= depth - 1))

    def each(k, up):
        (ups if up else downs)[k - 1].start()

    return each


def line_step(line, k, each=None):
    z, top = line.z, line.depth - 1
    onward = line.sends(k) if k < top else (None, None)
    for up, copy, there, further in (
        (True, line.ups[k - 1], z >= k, onward[0]),
        (False, line.downs[k - 1], z + k <= top, onward[1]),
    ):
        pl.when(there)(copy.wait_recv)
        if further is not None:
            pl.when(further[1])(further[0].start)
        if each is not None:
            pl.when(there)(functools.partial(each, k, up))


def forward_body(
    sizes,
    codes_ref,
    misc_ref,
    gains_ref,
    cos_ref,
    sin_ref,
    tokens_ref,
    outgrad_ref,
    wq_ref,
    wk_ref,
    wv_ref,
    wo_ref,
    eg_ref,
    eu_ref,
    ed_ref,
    sg_ref,
    su_ref,
    sd_ref,
    hidden_ref,
    norm_ref,
    grads_ref,
    gateup_ref,
    down_ref,
    codes_all,
    router_out,
    gain_rows,
    tok_out,
    weights_out,
    qkv_out,
    probs_out,
    mix_out,
    misc_all,
    norm_mine,
    tok,
    weights,
    qkv_ref,
    probs_ref,
    mix_ref,
    fnorm,
    part,
    part_in,
    scatter_in,
    gains_all,
    zeros,
    send,
    recv,
    here,
):
    dp, depth, experts, hidden_units, head = sizes
    me, z = lax.axis_index("dp"), lax.axis_index("tensor")
    core, x = me % 2, (me // 2) % 2
    bits = [2**k for k in range(dp.bit_length() - 1)]
    rows, width = tokens_ref.shape
    seq_len = rows * depth
    slice_width = width // dp
    routed = experts // 4
    c = Copies(send, recv, here)

    def bit_of(bit):
        return (me // bit) % 2

    greet(me, z, dp, depth)

    first = []
    own_codes = c.local(codes_ref, codes_all.at[0])
    own_misc = c.local(misc_ref, misc_all.at[me])
    own_gains = c.local(gains_ref, gains_all.at[z, me])
    for copy in (own_codes, own_misc, own_gains):
        copy.start()
    for r in range(1, 4):
        first.append(c.remote(codes_ref, codes_all.at[r], dp=peer_of(me, r)))
    gain_copies = [c.remote(gains_ref, gains_all.at[z, me], dp=peer_of(me, r)) for r in range(1, dp)]
    misc_copies = [c.remote(misc_ref, misc_all.at[me], dp=peer_of(me, r)) for r in range(1, dp)]
    for copy in gain_copies + misc_copies + first:
        copy.start()

    def piece(buffer, p):
        return buffer.at[pl.ds(pl.multiple_of(p * rows, rows), rows)]

    own_tok = c.local(tokens_ref, piece(tok.at[0], z))
    own_tok.start()
    own_grad = c.local(outgrad_ref, piece(grads_ref.at[0], z))
    own_grad.start()

    def columns(k, n):
        return pl.ds(pl.multiple_of(k * n, n), n)

    pair = wq_ref.shape[1] // 2
    own_at = tuple(bit_of(bit) for bit in reversed(bits))
    core_copies = []
    for k, w in enumerate((wq_ref, wk_ref, wv_ref, wo_ref)):
        place = weights.at[own_at + (slice(None), pl.ds(k * pair, pair))]
        core_copies.append(c.remote(w.at[:, columns(1 - core, pair)], place, dp=peer_of(me, 1)))
        core_copies.append(c.local(w.at[:, columns(core, pair)], place))
    for copy in core_copies:
        copy.start()

    beside = peer_of(me, 2)
    own_tok.wait()
    tok_line = Line(c, tok.at[0], z, depth, rows)
    tok_line.begin()
    tok_pass = [c.remote(tokens_ref, piece(tok.at[1], z), dp=peer_of(me, 1))]
    tok_pass[0].start()

    zeros[...] = jnp.zeros_like(zeros)
    pad = zeros.shape[1]
    pads = [c.local(zeros, down_ref.at[:, 0, pl.ds(hidden_units, pad)])]
    pads += [c.local(zeros, gateup_ref.at[:, k, pl.ds(hidden_units, pad)]) for k in range(2)]
    matrices = ((ed_ref, sd_ref, down_ref, 0), (eg_ref, sg_ref, gateup_ref, 0), (eu_ref, su_ref, gateup_ref, 1))
    slab = columns(me, slice_width)

    def group_copies(routed_src, shared_src, dst, k, r):
        group = (peer_of(me, r)) % 4
        many = (
            routed_src.at[pl.ds(group * routed, routed)],
            dst.at[pl.ds(0, routed), k, pl.ds(0, hidden_units), slab],
        )
        one = (shared_src.at[group], dst.at[routed, k, pl.ds(0, hidden_units), slab])
        if r == 0:
            return [c.local(*many), c.local(*one)]
        return [c.remote(*many, dp=peer_of(me, r)), c.remote(*one, dp=peer_of(me, r))]

    near = [[copy for r in (0, 1) for copy in group_copies(*m, r)] for m in matrices]
    far = [[copy for r in (2, 3) for copy in group_copies(*m, r)] for m in matrices]

    def over_copy(dst, k, far_chip):
        n = 2 * slice_width
        chip = me // 2 + far_chip * (1 - 2 * x)
        cols = pl.ds(pl.multiple_of(chip * n, n), n)
        place = dst.at[:, k, pl.ds(0, hidden_units), cols]
        return c.remote(place, place, dp=peer_of(me, 4))

    over_near = [over_copy(m[2], m[3], 0) for m in matrices]
    over = [over_copy(m[2], m[3], 1) for m in matrices]

    for copy in core_copies:
        copy.wait()

    def weight_copies(order, half):
        have, copies = [1], []
        for bit in order:
            index = tuple(
                pl.ds(0, 2) if b in have else pl.ds(bit_of(b), 1) for b in reversed(bits)
            )
            place = weights.at[index + (slice(None), pl.ds(half * 2 * pair, 2 * pair))]
            copies.append(c.remote(place, place, dp=peer_of(me, bit)))
            have.append(bit)
        return copies

    qk_copies = weight_copies(bits[1:], 0)
    vo_copies = weight_copies(bits[:0:-1], 1)
    qk_copies[0].start()
    vo_copies[0].start()
    grad_cut = width * 12 // 16
    grad_left, grad_right = pl.ds(0, grad_cut), pl.ds(grad_cut, width - grad_cut)
    far_grads = grads_ref.at[2, :, grad_right]
    grad_beside = c.remote(outgrad_ref.at[:, grad_right], piece(far_grads, z), dp=beside)
    grad_beside.start()
    far_grad_line = Line(c, far_grads, z, depth, rows)
    for copy in pads + [copy for m in near for copy in m]:
        copy.start()

    own_gains.wait()
    for copy in gain_copies:
        copy.wait_recv()
    gain_spread = [
        c.remote(gains_all.at[z], gains_all.at[z], tensor=(z + r) % depth) for r in range(1, depth)
    ]
    for copy in gain_spread:
        copy.start()

    tok_passed = []
    sibling = peer_of(me, 1)
    pass_tok = pass_on(c, tok.at[0], tok.at[1], z, depth, rows, sibling, tok_passed)

    line_step(tok_line, 1, pass_tok)
    for k in range(1, len(bits) - 1):
        qk_copies[k - 1].wait_recv()
        qk_copies[k].start()
        vo_copies[k - 1].wait_recv()
        vo_copies[k].start()
    own_grad.wait()
    grad_line = Line(c, grads_ref.at[0], z, depth, rows)
    for k in range(2, depth):
        line_step(tok_line, k, pass_tok)
    grad_line.begin()

    for copy in gain_spread:
        copy.wait_recv()
    for d in range(dp):
        total = gains_all[0, d]
        for t in range(1, depth):
            total = total + gains_all[t, d]
        gain_rows[:, d * slice_width : (d + 1) * slice_width] = total

    def norm_rows(s):
        def block(i, carry):
            at = pl.ds(pl.multiple_of(i * rows, rows), rows)
            data = tok[s, at, :].astype(F32)
            scale = lax.rsqrt(jnp.mean(data * data, axis=-1, keepdims=True) + EPS)
            fnorm[at, :] = (data * scale * gain_rows[0:1, :]).astype(BF)
            return carry

        lax.fori_loop(0, depth, block, 0)

    own_misc.wait()
    for copy in misc_copies:
        copy.wait_recv()
    router_out[...] = jnp.zeros_like(router_out)
    row = lax.broadcasted_iota(jnp.int32, misc_ref.shape, 0)
    for d in range(dp):
        block = jnp.where(row <= experts, misc_all[d], 0.0).astype(BF)
        router_out[: misc_ref.shape[0], d * slice_width : (d + 1) * slice_width] = block
    bias_in = jnp.zeros(misc_ref.shape, F32)
    sub = lax.broadcasted_iota(jnp.int32, misc_ref.shape, 0)
    for d in range(dp):
        bias_in = jnp.where(sub == d, misc_all[d, pl.ds(experts + 1 + core, 1), :], bias_in)
    bias_in = bias_in.astype(BF)
    heads3 = 3 * pair
    head_slice = head // dp
    lane = lax.broadcasted_iota(jnp.int32, (bias_in.shape[1], heads3), 1)
    sub = lax.broadcasted_iota(jnp.int32, (bias_in.shape[1], heads3), 0)
    place = (lane // head * head_slice + lane % head_slice == sub).astype(F32).astype(BF)
    spread = dot(bias_in, place)
    lane = lax.broadcasted_iota(jnp.int32, spread.shape, 1)
    sub = lax.broadcasted_iota(jnp.int32, spread.shape, 0)
    bias = jnp.sum(jnp.where(lane % head // head_slice == sub, spread, 0.0), axis=0, keepdims=True)

    qk_copies[-1].wait_recv()
    vo_copies[-1].wait_recv()
    for m in far:
        for copy in m:
            copy.start()
    for m, copy in zip(near, over_near):
        for part_copy in m:
            part_copy.wait()
        copy.start()
    pairs = pair // head

    def project(s):
        def block(i, carry):
            at = pl.ds(pl.multiple_of(i * 2 * rows, 2 * rows), 2 * rows)
            full = weights[...].reshape(width, 4 * pair)
            pre = dot(fnorm[at, :], full[:, : 3 * pair]) + bias
            cos_rows, sin_rows = cos_ref[at, :], sin_ref[at, :]
            for kind in range(3):
                for h in range(pairs):
                    a = (kind * pairs + h) * head
                    field = pre[:, a : a + head]
                    if kind < 2:
                        field = spin(field, cos_rows, sin_rows)
                    qkv_ref[kind, s * pairs + h, at, :] = field.astype(BF)
            return carry

        lax.fori_loop(0, depth // 2, block, 0)

    norm_rows(0)
    project(0)
    line_step(grad_line, 1)
    grad_beside.wait()
    far_grad_line.begin()
    for copy in far[0]:
        copy.wait_recv()
    over[0].start()
    tok_pass[0].wait()
    for copy, there in tok_passed:
        pl.when(there)(copy.wait)
    norm_rows(1)
    project(1)

    own_codes.wait()
    for copy in first:
        copy.wait()
    causal_block = seq_len // 2

    def attend(s):
        flags = codes_all[s]
        sub = lax.broadcasted_iota(jnp.int32, flags.shape, 0)
        flags = jnp.where(sub == 8, flags, 0).astype(F32).astype(BF)
        for h in range(pairs):
            for b in range(2):
                at = slice(b * causal_block, (b + 1) * causal_block)
                seen = dot(flags[:, at], flags, 0, 0)
                row = lax.broadcasted_iota(jnp.int32, seen.shape, 0) + b * causal_block
                col = lax.broadcasted_iota(jnp.int32, seen.shape, 1)
                scores = dot(qkv_ref[0, s * pairs + h, at, :], qkv_ref[1, s * pairs + h], 1, 1)
                scores = scores * head ** (-0.5)
                scores = jnp.where(jnp.logical_or(col <= row, seen > 0.5), scores, -1e30)
                raised = jnp.exp(scores - jnp.max(scores, axis=1, keepdims=True))
                probs = raised / jnp.sum(raised, axis=1, keepdims=True)
                probs = probs.astype(BF)
                probs_ref[s * pairs + h, at, :] = probs
                mixed = dot(probs, qkv_ref[2, s * pairs + h])
                mix_ref[s, at, h * head : (h + 1) * head] = mixed.astype(BF)

    def project_out(s):
        for d in range(dp):
            index = tuple(d // bit % 2 for bit in reversed(bits))
            block = weights[index + (slice(None), slice(3 * pair, 4 * pair))]
            at = slice(d * slice_width, (d + 1) * slice_width)
            part[s, :, at] = dot(mix_ref[s], block, 1, 1).astype(BF)

    attend(1)
    if depth > 2:
        line_step(grad_line, 2)
        line_step(far_grad_line, 1)
    project_out(1)
    part_pass = c.remote(part.at[1], part_in, dp=peer_of(me, 1))
    part_pass.start()
    attend(0)
    project_out(0)
    part_pass.wait_recv()

    saved = [
        c.local(a, b)
        for a, b in (
            (tok, tok_out),
            (weights, weights_out),
            (qkv_ref, qkv_out),
            (probs_ref, probs_out),
            (mix_ref, mix_out),
        )
    ]
    for copy in saved:
        copy.start()
    for k in range(3, depth):
        line_step(grad_line, k)
        line_step(far_grad_line, k - 1)
    x_grad = c.remote(grads_ref.at[0, :, grad_left], grads_ref.at[2, :, grad_left], dp=beside)
    x_grad.start()
    own_pass = c.remote(grads_ref.at[0], grads_ref.at[1], dp=peer_of(me, 1))
    own_pass.start()
    here_at = pl.ds(pl.multiple_of(z * rows, rows), rows)
    hidden_ref[...] = part[0, here_at, :].astype(F32) + part_in[here_at, :].astype(F32)
    hidden_ref[...] += tok[0, here_at, :].astype(F32)
    for r in range(depth):
        at = pl.ds(r * rows, rows)
        part[0, at, :] = (part[0, at, :].astype(F32) + part_in[at, :].astype(F32)).astype(BF)
    scatter = LineSum(c, part.at[0], scatter_in.at[0], scatter_in.at[1], z, depth, rows)
    scatter.run()
    for k in (1, 2):
        for copy in far[k]:
            copy.wait_recv()
        over[k].start()
    scatter.collect(hidden_ref)
    total = hidden_ref[...]
    scale = lax.rsqrt(jnp.mean(total * total, axis=-1, keepdims=True) + EPS)
    norm_mine[...] = (total * scale * gain_rows[1:2, :]).astype(BF)
    norm_here = c.local(norm_mine, piece(norm_ref.at[0], z))
    norm_here.start()
    norm_here.wait()
    norm_line = Line(c, norm_ref.at[0], z, depth, rows)
    norm_line.begin()
    cut = width * 10 // 16
    left, right = pl.ds(0, cut), pl.ds(cut, width - cut)
    norm_own = c.remote(piece(norm_ref.at[0], z), piece(norm_ref.at[1], z), dp=sibling)
    norm_far = c.remote(piece(norm_ref.at[0], z), piece(norm_ref.at[2], z), dp=beside)
    norm_far.start()
    norm_own.start()
    far_line = Line(c, norm_ref.at[2, :, right], z, depth, rows)
    norm_passed, far_passed = [], []
    pass_norm = pass_on(
        c, norm_ref.at[0], norm_ref.at[1], z, depth, rows, sibling, norm_passed
    )
    pass_far = pass_on(
        c, norm_ref.at[0, :, left], norm_ref.at[2, :, left], z, depth, rows, beside, far_passed
    )

    def pass_both(k, up):
        pass_far(k, up)
        pass_norm(k, up)

    line_step(norm_line, 1, pass_both)
    norm_far.wait()
    far_line.begin()
    for k in range(2, depth):
        line_step(norm_line, k, pass_both)
        line_step(far_line, k - 1)
    line_step(far_line, depth - 1)

    line_step(far_grad_line, depth - 1)
    x_grad.wait_recv()
    grad_pass = c.remote(grads_ref.at[2], grads_ref.at[3], dp=peer_of(me, 1))
    grad_pass.start()
    for copy in over_near + over:
        copy.wait()
    for copy, there in far_passed:
        pl.when(there)(copy.wait)
    norm_pass = c.remote(norm_ref.at[2], norm_ref.at[3], dp=sibling)
    norm_pass.start()
    norm_own.wait()
    for copy, there in norm_passed:
        pl.when(there)(copy.wait)
    norm_pass.wait()
    own_pass.wait()
    grad_pass.wait()
    for line in (tok_line, grad_line, far_grad_line, norm_line, far_line, scatter):
        line.finish()
    for copy in pads + saved:
        copy.wait()
    for copy in gain_copies + misc_copies + gain_spread + qk_copies + vo_copies:
        copy.wait_send()
    for copy in [part_pass, x_grad] + [y for m in far for y in m]:
        copy.wait_send()


def forward_call(dp, depth, experts, head, small, arrays, units):
    codes, misc, gains, cos_rows, sin_rows = small
    tokens, pair = arrays[0], arrays[2].shape[1] // 2
    rows, width = tokens.shape
    seq_len = rows * depth
    hidden_units = units[0].shape[1]
    hidden_pad = -(-hidden_units // 128) * 128
    routed = experts // 4
    bits = dp.bit_length() - 1
    pairs = pair // head
    vmem, hbm = pl.BlockSpec(memory_space=pltpu.VMEM), pl.BlockSpec(memory_space=pl.ANY)
    shape = jax.ShapeDtypeStruct
    return pl.pallas_call(
        functools.partial(forward_body, (dp, depth, experts, hidden_units, head)),
        in_specs=[vmem] * 5 + [hbm] * 12,
        out_specs=[vmem] + [hbm] * 4 + [vmem] * 3 + [hbm] * 5,
        out_shape=[
            shape((rows, width), F32),
            shape((4, seq_len, width), BF),
            shape((4, seq_len, width), BF),
            shape((routed + 1, 2, hidden_pad, width), BF),
            shape((routed + 1, 1, hidden_pad, width), BF),
            shape((4,) + codes.shape, codes.dtype),
            shape((128, width), BF),
            shape((8, width), F32),
            shape((2, seq_len, width), BF),
            shape((2,) * bits + (width // dp, 4 * pair), BF),
            shape((3, 2 * pairs, seq_len, head), BF),
            shape((2 * pairs, seq_len, seq_len), BF),
            shape((2, seq_len, pair), BF),
        ],
        scratch_shapes=[
            pltpu.VMEM((dp,) + misc.shape, F32),
            pltpu.VMEM((rows, width), BF),
            pltpu.VMEM((2, seq_len, width), BF),
            pltpu.VMEM((2,) * bits + (width // dp, 4 * pair), BF),
            pltpu.VMEM((3, 2 * pairs, seq_len, head), BF),
            pltpu.VMEM((2 * pairs, seq_len, seq_len), BF),
            pltpu.VMEM((2, seq_len, pair), BF),
            pltpu.VMEM((seq_len, width), BF),
            pltpu.VMEM((2, seq_len, width), BF),
            pltpu.VMEM((seq_len, width), BF),
            pltpu.VMEM((2, depth - 1, rows, width), BF),
            pltpu.VMEM((depth, dp) + gains.shape, F32),
            pltpu.VMEM((routed + 1, hidden_pad - hidden_units, width), BF),
            pltpu.SemaphoreType.DMA((160,)),
            pltpu.SemaphoreType.DMA((160,)),
            pltpu.SemaphoreType.DMA((40,)),
        ],
        compiler_params=pltpu.CompilerParams(
            collective_id=0, has_side_effects=True, vmem_limit_bytes=VMEM_LIMIT
        ),
    )(codes, misc, gains, cos_rows, sin_rows, *arrays, *units)


def middle_body(
    sizes,
    hidden_ref,
    codes_ref,
    router_ref,
    rows_ref,
    grads_ref,
    gateup_ref,
    down_ref,
    output_ref,
    terms_out,
    probs_out,
    grad_own,
    grad_sib,
    grad_far,
    gate_total,
    up_total,
    down_total,
    gate_in,
    wide_w,
    down_w,
    xs,
    ys,
    pair,
    act,
    outs,
    backs,
    near_in,
    back_in,
    far_in,
    z_in,
    stage,
    weights,
    routed,
    probs,
    terms,
    terms_in,
    send,
    recv,
    here,
):
    dp, depth, experts, top_count, keep = sizes
    me, z = lax.axis_index("dp"), lax.axis_index("tensor")
    y = me // 4
    rows, width = output_ref.shape
    seq_len = rows * depth
    total = 2 * seq_len
    units, wide, _ = wide_w.shape
    half = wide // 2
    slice_width = width // dp
    sibling, beside, over = peer_of(me, 1), peer_of(me, 2), peer_of(me, 4)
    c = Copies(send, recv, here)

    greet(me, z, dp, depth)

    def load(source, chunk, target):
        copies = [
            c.local(source.at[2 * chunk + s], target.at[pl.ds(s * seq_len, seq_len)])
            for s in range(2)
        ]
        for copy in copies:
            copy.start()
        return copies

    def wait(copies):
        for copy in copies:
            copy.wait()

    loads = load(rows_ref, 1, xs)
    first = [(c.local(gateup_ref.at[u], wide_w.at[u]), c.local(down_ref.at[u], down_w.at[u])) for u in range(units)]
    first[0][0].start()
    first[0][1].start()
    loads += load(grads_ref, 1, ys)
    for u in range(1, units):
        first[u][0].start()
        first[u][1].start()

    block = seq_len // 2
    lanes = weights.shape[1]

    def gate_weights(chunk):
        def step(i, carry):
            at = pl.ds(pl.multiple_of(i * block, block), block)
            logits = dot(xs[at, :], router_ref[...], 1, 1)
            lane = lax.broadcasted_iota(jnp.int32, logits.shape, 1)
            chosen = jnp.where(lane < experts, logits, -1e30)
            raised = jnp.exp(chosen - jnp.max(chosen, axis=1, keepdims=True))
            soft = raised / jnp.sum(raised, axis=1, keepdims=True)
            probs[at, :] = jnp.where(lane < experts, soft, jax.nn.sigmoid(logits))
            return carry

        lax.fori_loop(0, total // block, step, 0)
        for s in range(2):
            codes = codes_ref[2 * chunk + s]
            row = lax.broadcasted_iota(jnp.int32, codes.shape, 0)
            named = row == experts
            for k in range(top_count):
                named = jnp.logical_or(named, codes[k : k + 1] == row)
            named = jnp.logical_and(named, row <= experts).astype(F32).astype(BF)
            place = (codes.shape[0], lanes)
            same = lax.broadcasted_iota(jnp.int32, place, 0) == lax.broadcasted_iota(
                jnp.int32, place, 1
            )
            routed[s * seq_len : (s + 1) * seq_len] = dot(named, same.astype(F32).astype(BF), 0, 0)
        weights[...] = probs[...] * routed[...]

    def activate(chunk):
        for u in range(units):
            if chunk == 1:
                wait(first[u])
            if u == 0:
                gate_weights(chunk)
            place = me % 4 * (units - 1) + u if u < units - 1 else experts

            def step(i, carry, u=u, place=place):
                at = pl.ds(pl.multiple_of(i * block, block), block)
                mine = lax.broadcasted_iota(jnp.int32, (block, lanes), 1) == place
                weight = jnp.sum(jnp.where(mine, weights[at, :], 0.0), axis=1, keepdims=True)
                both = dot(xs[at, :], wide_w[u], 1, 1)
                cot = dot(ys[at, :], down_w[u], 1, 1)
                gate_act, gate_slope = silu_parts(both[:, :half])
                value = gate_act * both[:, half:]
                inner = jnp.sum(value * cot, axis=1, keepdims=True)
                inner = jnp.where(mine, inner * routed[at, :], 0.0)
                terms[chunk, at, :] = inner if u == 0 else terms[chunk, at, :] + inner
                cot = cot * weight
                act[chunk, at, u * half : (u + 1) * half] = (value * weight).astype(BF)
                a = u * wide
                pair[chunk, at, a : a + half] = (cot * both[:, half:] * gate_slope).astype(BF)
                pair[chunk, at, a + half : a + wide] = (cot * gate_act).astype(BF)
                return carry

            lax.fori_loop(0, total // block, step, 0)

    cols = 512

    def back(left, chunk, s, weight, target):
        at = slice(s * seq_len, (s + 1) * seq_len)
        for j in range(width // cols):
            part = weight[:, :, j * cols : (j + 1) * cols]
            part = part.reshape(-1, cols)
            target[:, j * cols : (j + 1) * cols] = dot(left[chunk, at, :], part).astype(BF)

    def add_into(target, other):
        def step(i, carry):
            at = pl.ds(pl.multiple_of(i * rows, rows), rows)
            target[at, :] = (target[at, :].astype(F32) + other[at, :].astype(F32)).astype(BF)
            return carry

        lax.fori_loop(0, depth, step, 0)

    wait(loads)
    activate(1)
    loads = load(rows_ref, 0, xs) + load(grads_ref, 0, ys)
    terms_near = c.remote(terms.at[1, pl.ds(seq_len, seq_len)], terms_in, dp=sibling)
    terms_near.start()
    back(act, 1, 1, down_w, outs.at[1])
    out_near = c.remote(outs.at[1], near_in, dp=sibling)
    out_near.start()
    back(act, 1, 0, down_w, outs.at[0])
    terms_near.wait()
    terms[1, :seq_len] = terms[1, :seq_len] + terms_in[...]
    terms_across = c.remote(terms.at[1, pl.ds(0, seq_len)], terms_out.at[2], dp=beside)
    terms_across.start()
    out_near.wait()
    add_into(outs.at[0], near_in)
    out_across = c.remote(outs.at[0], far_in, dp=beside)
    out_across.start()
    back(pair, 1, 1, wide_w, outs.at[1])
    grad_near = c.remote(outs.at[1], back_in, dp=sibling)
    grad_near.start()
    back(pair, 1, 0, wide_w, backs)
    grad_near.wait()
    add_into(backs, back_in)
    grad_across = c.remote(backs, grad_far, dp=beside)
    grad_across.start()

    wait(loads)
    activate(0)
    probs_out[...] = probs[pl.ds(pl.multiple_of(z * rows, rows), rows), :]
    loads = load(rows_ref, 1, ys)
    terms_out[0] = terms[0, :seq_len]
    terms_last = c.remote(terms.at[0, pl.ds(seq_len, seq_len)], terms_out.at[1], dp=sibling)
    terms_last.start()
    back(act, 0, 1, down_w, outs.at[1])
    out_last = c.remote(outs.at[1], near_in, dp=sibling)
    out_last.start()
    back(act, 0, 0, down_w, back_in)

    staged, moved = [None, None], []
    blocks = stage.shape[2]

    def outer(left, parts, targets, u, j, slot):
        at = slice(j * blocks * slice_width, (j + 1) * blocks * slice_width)
        n = parts * half
        value = dot(left[0, :, u * n : (u + 1) * n], xs[:, at], 0, 0)
        value = (value + dot(left[1, :, u * n : (u + 1) * n], ys[:, at], 0, 0)).astype(BF)
        if staged[slot] is not None:
            wait(staged[slot])
        copies = []
        for k, target in enumerate(targets):
            for b in range(blocks):
                stage[slot, k, b] = value[
                    k * half : k * half + keep, b * slice_width : (b + 1) * slice_width
                ]
            copies.append(c.local(stage.at[slot, k], target.at[pl.ds(j * blocks, blocks), u]))
            copies[-1].start()
        staged[slot] = copies

    wait(loads)
    steps = dp // blocks
    scatter = []
    over_copies = []
    for u in range(units):
        for j in range(steps):
            outer(pair, 2, (gate_total, up_total), u, j, j % 2)
        if u == 0:
            out_last.wait()
            out_across.wait()
            for r in list(range(1, depth)) + [0]:
                at = pl.ds(pl.multiple_of((z + r) % depth * rows, rows), rows)
                part = back_in[at, :].astype(F32) + near_in[at, :].astype(F32)
                part = part + far_in[at, :].astype(F32)
                if r:
                    back_in[at, :] = part.astype(BF)
                    copy = c.remote(back_in.at[at], z_in.at[r - 1], tensor=(z + r) % depth)
                    copy.start()
                    scatter.append(copy)
                else:
                    near_in[at, :] = part.astype(BF)
        for slot in range(2):
            wait(staged[slot])
            staged[slot] = None
        source = gate_total.at[pl.ds((1 - y) * 4, 4), u]
        over_copies.append(c.remote(source, gate_in.at[:, u], dp=over))
        over_copies[-1].start()
    loads = load(grads_ref, 0, xs) + load(grads_ref, 1, ys)

    back(pair, 0, 1, wide_w, outs.at[1])
    grad_last = c.remote(outs.at[1], grad_sib, dp=sibling)
    grad_last.start()
    back(pair, 0, 0, wide_w, outs.at[0])
    grad_here = c.local(outs.at[0], grad_own)
    grad_here.start()
    wait(loads)
    for u in range(units):
        for j in range(steps):
            outer(act, 1, (down_total,), u, j, j % 2)
    for copy in scatter:
        copy.wait_recv()
    value = near_in[pl.ds(pl.multiple_of(z * rows, rows), rows), :].astype(F32)
    value = value + hidden_ref[...]
    for r in range(1, depth):
        value = value + z_in[r - 1].astype(F32)
    output_ref[...] = value.astype(BF)
    for slot in range(2):
        wait(staged[slot])
    for copy in scatter:
        copy.wait_send()
    wait([grad_here, grad_last, terms_last, terms_across, grad_across] + over_copies)


def middle_call(dp, depth, experts, top_count, hidden_units, hidden, codes, router, arrays):
    rows, width = hidden.shape
    seq_len = rows * depth
    norm, grads, gateup, down = arrays
    units, wide, _ = gateup.shape
    half = wide // 2
    slice_width = width // dp
    blocks = max(1, 1024 // slice_width)
    vmem, hbm = pl.BlockSpec(memory_space=pltpu.VMEM), pl.BlockSpec(memory_space=pl.ANY)
    shape = jax.ShapeDtypeStruct
    total = shape((dp, units, hidden_units, slice_width), BF)
    return pl.pallas_call(
        functools.partial(middle_body, (dp, depth, experts, top_count, hidden_units)),
        in_specs=[vmem] * 3 + [hbm] * 4,
        out_specs=[vmem] * 3 + [hbm] * 7,
        out_shape=[
            shape((rows, width), BF),
            shape((3, seq_len, 128), F32),
            shape((rows, 128), F32),
            shape((seq_len, width), BF),
            shape((seq_len, width), BF),
            shape((seq_len, width), BF),
            total,
            total,
            total,
            shape((4, units, hidden_units, slice_width), BF),
        ],
        scratch_shapes=[
            pltpu.VMEM((units, wide, width), BF),
            pltpu.VMEM((units, half, width), BF),
            pltpu.VMEM((2 * seq_len, width), BF),
            pltpu.VMEM((2 * seq_len, width), BF),
            pltpu.VMEM((2, 2 * seq_len, units * wide), BF),
            pltpu.VMEM((2, 2 * seq_len, units * half), BF),
            pltpu.VMEM((2, seq_len, width), BF),
            pltpu.VMEM((seq_len, width), BF),
            pltpu.VMEM((seq_len, width), BF),
            pltpu.VMEM((seq_len, width), BF),
            pltpu.VMEM((seq_len, width), BF),
            pltpu.VMEM((depth - 1, rows, width), BF),
            pltpu.VMEM((2, 2, blocks, hidden_units, slice_width), BF),
            pltpu.VMEM((2 * seq_len, 128), F32),
            pltpu.VMEM((2 * seq_len, 128), F32),
            pltpu.VMEM((2 * seq_len, 128), F32),
            pltpu.VMEM((2, 2 * seq_len, 128), F32),
            pltpu.VMEM((seq_len, 128), F32),
            pltpu.SemaphoreType.DMA((32,)),
            pltpu.SemaphoreType.DMA((32,)),
            pltpu.SemaphoreType.DMA((64,)),
        ],
        compiler_params=pltpu.CompilerParams(
            collective_id=2, has_side_effects=True, vmem_limit_bytes=63 * 2**20
        ),
    )(hidden, codes, router, norm, grads, gateup, down)


class LineSum:
    def __init__(self, c, data, ups, downs, z, depth, rows):
        self.data, self.ups, self.downs = data, ups, downs
        self.z, self.depth, self.rows = z, depth, rows
        self.up_copies = [
            c.remote(self.piece(t), ups.at[t - 1], tensor=z + 1) for t in range(1, depth)
        ]
        self.down_copies = [
            c.remote(self.piece(t), downs.at[t], tensor=z - 1) for t in range(depth - 1)
        ]

    def piece(self, t):
        return self.data.at[pl.ds(t * self.rows, self.rows)]

    def add(self, t, other):
        at = pl.ds(t * self.rows, self.rows)
        self.data[at, :] = (self.data[at, :].astype(F32) + other.astype(F32)).astype(BF)

    def up(self, t):
        copy = self.up_copies[t - 1]

        @pl.when(self.z < t)
        def _():
            @pl.when(self.z > 0)
            def _():
                copy.wait_recv()
                self.add(t, self.ups[t - 1])

            copy.start()

    def down(self, t):
        copy = self.down_copies[t]

        @pl.when(self.z > t)
        def _():
            @pl.when(self.z < self.depth - 1)
            def _():
                copy.wait_recv()
                self.add(t, self.downs[t])

            copy.start()

    def begin(self):
        top = self.depth - 1

        @pl.when(self.z == 0)
        def _():
            for k in range(top):
                self.up_copies[top - k - 1].start()

        @pl.when(self.z == top)
        def _():
            for k in range(top):
                self.down_copies[k].start()

    def step(self, k):
        top = self.depth - 1

        @pl.when(jnp.logical_and(self.z > 0, self.z < self.depth // 2))
        def _():
            self.up(top - k)
            self.down(k)

        @pl.when(jnp.logical_and(self.z >= self.depth // 2, self.z < top))
        def _():
            self.down(k)
            self.up(top - k)

    def run(self):
        self.begin()
        for k in range(self.depth - 1):
            self.step(k)

    def collect(self, total_ref):
        for t in range(self.depth):

            @pl.when(self.z == t)
            def _(t=t):
                if t > 0:
                    self.up_copies[t - 1].wait_recv()
                    total_ref[...] += self.ups[t - 1].astype(F32)
                if t < self.depth - 1:
                    self.down_copies[t].wait_recv()
                    total_ref[...] += self.downs[t].astype(F32)

    def finish(self):
        for t in range(1, self.depth):
            pl.when(self.z < t)(self.up_copies[t - 1].wait_send)
        for t in range(self.depth - 1):
            pl.when(self.z > t)(self.down_copies[t].wait_send)


def backward_body(
    sizes,
    terms_ref,
    probs_mine_ref,
    router_ref,
    gain_rows,
    cos_ref,
    sin_ref,
    hidden_ref,
    outgrad_ref,
    grad_a_ref,
    grad_b_ref,
    grad_c_ref,
    gate_in_ref,
    gate_ref,
    up_ref,
    down_ref,
    tok_hbm,
    weights_hbm,
    qkv_hbm,
    probs_hbm,
    mix_hbm,
    norm_hbm,
    input_ref,
    gate_out,
    up_out,
    down_out,
    attn_out,
    misc_out,
    gains_out,
    own_sum,
    arrived,
    three,
    scatter_in,
    terms_sum,
    terms_in,
    back,
    tok,
    weights,
    qkv,
    probs_ref,
    mix_ref,
    scales,
    qkv_grad,
    part_in,
    keep,
    total_a,
    first_qk,
    first_vo,
    second_in,
    misc_part,
    misc_in,
    gains_in,
    vectors,
    send,
    recv,
    here,
):
    dp, depth, experts, head = sizes
    me, z = lax.axis_index("dp"), lax.axis_index("tensor")
    core, x, y = me % 2, (me // 2) % 2, me // 4
    rows, width = input_ref.shape
    seq_len = rows * depth
    slice_width = width // dp
    pair = mix_ref.shape[2]
    pairs = pair // head
    bits = [1, 2, 4]
    c = Copies(send, recv, here)

    greet(me, z, dp, depth)

    matrices = ((gate_ref, gate_out), (up_ref, up_out), (down_ref, down_out))
    over = [None]
    for m in (1, 2):
        other = matrices[m][0].at[pl.ds((1 - y) * 4, 4)]
        over.append(c.remote(other, arrived.at[m], dp=peer_of(me, 4)))
        over[m].start()
    gate_in = c.local(gate_in_ref, arrived.at[0])
    grads = (grad_a_ref, grad_b_ref, grad_c_ref)
    loads = [c.local(grads[k], three.at[k]) for k in range(3)]
    for copy in loads:
        copy.start()
    own_loads = [
        c.local(source.at[pl.ds(y * 4, 4)], own_sum) for source, _ in matrices
    ]
    inputs = [
        c.local(a, b)
        for a, b in (
            (weights_hbm, weights),
            (mix_hbm, mix_ref),
            (qkv_hbm, qkv),
            (probs_hbm, probs_ref),
            (tok_hbm, tok),
        )
    ]
    own_loads[0].start()
    gate_in.start()
    for copy in inputs:
        copy.start()

    def at_of(p):
        return pl.ds(pl.multiple_of(p * rows, rows), rows)

    for copy in loads:
        copy.wait()
    small = []
    for r in range(depth):
        at = at_of((z + r) % depth)
        total = three[0, at, :].astype(F32) + three[1, at, :].astype(F32)
        total = total + three[2, at, :].astype(F32)
        three[0, at, :] = total.astype(BF)
        extra = terms_ref[0, at, :] + terms_ref[1, at, :] + terms_ref[2, at, :]
        terms_sum[at, :] = extra
        if r:
            copy = c.remote(terms_sum.at[at], terms_in.at[r - 1], tensor=(z + r) % depth)
            copy.start()
            small.append(copy)
        else:
            keep[0] = total
    scatter = LineSum(c, three.at[0], scatter_in.at[0, 0], scatter_in.at[0, 1], z, depth, rows)
    scatter.run()

    def add_over(m):
        own_loads[m].wait()
        if m:
            over[m].wait_recv()
        else:
            gate_in.wait()
        copies = []
        for r in (2, 3, 1, 0):
            k = peer_of(me, r) % 4
            for unit in range(own_sum.shape[1]):
                arrived[m, k, unit] = (
                    own_sum[k, unit].astype(F32) + arrived[m, k, unit].astype(F32)
                ).astype(BF)
            place = matrices[m][1].at[me % 4]
            if r:
                copies.append(c.remote(arrived.at[m, k], place, dp=peer_of(me, r)))
            else:
                copies.append(c.local(arrived.at[m, k], place))
            copies[-1].start()
        if m + 1 < len(own_loads):
            own_loads[m + 1].start()
        return copies

    units = add_over(0)
    for copy in small:
        copy.wait_recv()
    route = terms_sum[at_of(z), :]
    for r in range(1, depth):
        route = route + terms_in[r - 1]
    scatter.collect(keep.at[0])
    grad = keep[0]
    probs_mine = probs_mine_ref[...]
    lane = lax.broadcasted_iota(jnp.int32, route.shape, 1)
    inner = jnp.sum(jnp.where(lane < experts, probs_mine * route, 0.0), axis=1, keepdims=True)
    logits = jnp.where(
        lane < experts,
        probs_mine * (route - inner),
        jnp.where(lane == experts, route * probs_mine * (1.0 - probs_mine), 0.0),
    ).astype(BF)
    grad = grad + dot(logits, router_ref[...])
    hidden = hidden_ref[...]
    scale = lax.rsqrt(jnp.mean(hidden * hidden, axis=-1, keepdims=True) + EPS)
    unit = hidden * scale
    vectors[1:2, :] = jnp.sum(grad * unit, axis=0, keepdims=True)
    grad = grad * gain_rows[1:2, :]
    grad = outgrad_ref[...].astype(F32) + scale * (
        grad - unit * jnp.mean(grad * unit, axis=-1, keepdims=True)
    )
    keep[0] = grad
    back[0, at_of(z), :width] = grad.astype(BF)
    back[0, at_of(z), width:] = logits

    line = Line(c, back.at[0], z, depth, rows)
    line.begin()
    sibling = peer_of(me, 1)
    back_own = c.remote(piece_of(back.at[0], z, rows), piece_of(back.at[1], z, rows), dp=sibling)
    back_own.start()
    passed = []
    pass_back = pass_on(c, back.at[0], back.at[1], z, depth, rows, sibling, passed)
    line_step(line, 1, pass_back)

    for copy in inputs:
        copy.wait()

    def scale_rows(i, carry):
        at = at_of(i)
        for s in range(2):
            data = tok[s, at, :].astype(F32)
            scales[s, at, :] = lax.rsqrt(jnp.mean(data * data, axis=-1, keepdims=True) + EPS)
        return carry

    lax.fori_loop(0, depth, scale_rows, 0)
    units += add_over(1)
    line_step(line, 2, pass_back)
    line_step(line, 3, pass_back)
    back_own.wait()
    for copy, there in passed:
        pl.when(there)(copy.wait)
    def block_of(d):
        return tuple(d // bit % 2 for bit in reversed(bits))

    def slab(d):
        return slice(d * slice_width, (d + 1) * slice_width)

    def attention(s):
        mixed = jnp.zeros((seq_len, pair), F32)
        for d in range(dp):
            block = weights[block_of(d) + (slice(None), slice(3 * pair, 4 * pair))]
            mixed = mixed + dot(back[s, :, slab(d)], block)
        mixed = mixed.astype(BF)
        for h in range(pairs):
            n = s * pairs + h
            cot = mixed[:, h * head : (h + 1) * head]
            key_total = jnp.zeros((seq_len, head), F32)
            value_total = jnp.zeros((seq_len, head), F32)
            for b in range(2):
                at = slice(b * seq_len // 2, (b + 1) * seq_len // 2)
                p_low = probs_ref[n, at, :]
                p = p_low.astype(F32)
                p_grad = dot(cot[at], qkv[2, n], 1, 1)
                s_grad = p * (p_grad - jnp.sum(p * p_grad, axis=1, keepdims=True))
                s_grad = s_grad.astype(BF)
                q_grad = dot(s_grad, qkv[1, n]) * head ** (-0.5)
                q_grad = spin(q_grad, cos_ref[at, :], -sin_ref[at, :])
                qkv_grad[s, at, h * head : (h + 1) * head] = q_grad.astype(BF)
                key_total = key_total + dot(s_grad, qkv[0, n, at, :], 0, 0)
                value_total = value_total + dot(p_low, cot[at], 0, 0)
            k_grad = spin(key_total * head ** (-0.5), cos_ref[...], -sin_ref[...])
            a = pair + h * head
            qkv_grad[s, :, a : a + head] = k_grad.astype(BF)
            qkv_grad[s, :, a + pair : a + pair + head] = value_total.astype(BF)

    def first_grad(s):
        for d in range(dp):
            block = weights[block_of(d) + (slice(None), slice(0, 3 * pair))]
            total = dot(qkv_grad[s], block, 1, 1)
            three[1 + s, :, slab(d)] = total.astype(BF)
            unit_block = tok[s, :, slab(d)].astype(F32) * scales[s]
            row = jnp.sum(total * unit_block, axis=0, keepdims=True)
            vectors[2 + s : 3 + s, slab(d)] = row

    units += add_over(2)
    attention(1)
    first_grad(1)
    part_pass = c.remote(three.at[2], part_in, dp=sibling)
    part_pass.start()
    attention(0)
    first_grad(0)
    part_pass.wait_recv()
    keep[1] = three[1, at_of(z), :].astype(F32) + part_in[at_of(z), :].astype(F32)
    for r in range(depth):
        at = at_of(r)
        three[1, at, :] = (three[1, at, :].astype(F32) + part_in[at, :].astype(F32)).astype(BF)
    first_scatter = LineSum(
        c, three.at[1], scatter_in.at[1, 0], scatter_in.at[1, 1], z, depth, rows
    )
    first_scatter.begin()

    for d in range(dp):
        total = jnp.zeros((slice_width, 3 * pair), F32)
        out_total = jnp.zeros((slice_width, pair), F32)
        for s in range(2):
            data = tok[s, :, slab(d)].astype(F32) * scales[s] * gain_rows[0:1, slab(d)]
            total = total + dot(data.astype(BF), qkv_grad[s], 0, 0)
            out_total = out_total + dot(back[s, :, slab(d)], mix_ref[s], 0, 0)
        total_a[block_of(d) + (slice(None), slice(0, 3 * pair))] = total.astype(BF)
        total_a[block_of(d) + (slice(None), slice(3 * pair, 4 * pair))] = out_total.astype(BF)

    half = 2 * pair

    def index(y_at, x_at, k):
        return (y_at, x_at, slice(None), slice(None), pl.ds(k * half, half))

    every = pl.ds(0, 2)
    qk_first = c.remote(
        total_a.at[index(pl.ds(1 - y, 1), every, 0)], first_qk, dp=peer_of(me, 4)
    )
    vo_first = c.remote(
        total_a.at[index(every, pl.ds(1 - x, 1), 1)], first_vo, dp=peer_of(me, 2)
    )
    qk_first.start()
    vo_first.start()
    first_scatter.step(0)

    scatter.finish()
    norm_load = c.local(norm_hbm.at[0], three.at[0])
    norm_load.start()
    norm_load.wait()
    router_part = dot(back[0, :, width:], three[0], 0, 0)
    ones = jnp.ones((16, seq_len), BF)
    bias_row = dot(ones, qkv_grad[0]) + dot(ones, qkv_grad[1])
    lane = lax.broadcasted_iota(jnp.int32, bias_row.shape, 1)
    sub = lax.broadcasted_iota(jnp.int32, bias_row.shape, 0)
    head_slice = head // dp
    bias_rows = jnp.where(lane % head // head_slice == sub, bias_row, 0.0)
    high = bias_rows.astype(BF)
    low = (bias_rows - high.astype(F32)).astype(BF)
    lane = lax.broadcasted_iota(jnp.int32, (3 * pair, slice_width), 1)
    sub = lax.broadcasted_iota(jnp.int32, (3 * pair, slice_width), 0)
    place = (sub // head * head_slice + sub % head_slice == lane).astype(F32).astype(BF)
    bias_rows = dot(high, place) + dot(low, place)
    sub = lax.broadcasted_iota(jnp.int32, (16, slice_width), 0)
    misc_copies = []
    for d in range(dp):
        tile = jnp.where(sub <= experts, router_part[:16, slab(d)], 0.0)
        tile = jnp.where(sub == experts + 1 + core, bias_rows[d : d + 1], tile)
        gain_one = vectors[2:3, slab(d)] + vectors[3:4, slab(d)]
        tile = jnp.where(sub == experts + 3, gain_one, tile)
        tile = jnp.where(sub == experts + 4, vectors[1:2, slab(d)], tile)
        misc_part[d] = tile
    for r in range(1, dp):
        to = peer_of(me, r)
        misc_copies.append(c.remote(misc_part.at[to], misc_in.at[r - 1], dp=to))
        misc_copies[-1].start()

    for k in range(1, depth - 1):
        first_scatter.step(k)
    qk_first.wait()
    mine = index(pl.ds(y, 1), every, 0)
    total_a[mine] = (total_a[mine].astype(F32) + first_qk[...].astype(F32)).astype(BF)
    qk_second = c.remote(
        total_a.at[index(pl.ds(y, 1), pl.ds(1 - x, 1), 0)], second_in.at[0], dp=peer_of(me, 2)
    )
    qk_second.start()
    vo_first.wait()
    mine = index(every, pl.ds(x, 1), 1)
    total_a[mine] = (total_a[mine].astype(F32) + first_vo[...].astype(F32)).astype(BF)
    vo_second = c.remote(
        total_a.at[index(pl.ds(1 - y, 1), pl.ds(x, 1), 1)], second_in.at[1], dp=peer_of(me, 4)
    )
    vo_second.start()

    total = misc_part[me]
    for r, copy in enumerate(misc_copies):
        copy.wait_recv()
        total = total + misc_in[r]
    misc_out[...] = total
    gain_copies = []
    for r in range(1, depth):
        peer = (z + r) % depth
        gain_copies.append(c.remote(misc_out.at[8:16], gains_in.at[r - 1], tensor=peer))
        gain_copies[-1].start()

    finals = []
    for k, copy in enumerate((qk_second, vo_second)):
        copy.wait()
        mine = (y, x, slice(None), slice(None), pl.ds(k * half, half))
        total_a[mine] = (
            total_a[mine].astype(F32) + second_in[k, 0, 0].astype(F32)
        ).astype(BF)
        for other in (True, False):
            to = 1 - core if other else core
            source = total_a.at[y, x, to, :, pl.ds(k * half, half)]
            place = attn_out.at[core, :, pl.ds(k * half, half)]
            finals.append(c.remote(source, place, dp=sibling) if other else c.local(source, place))
            finals[-1].start()

    first_scatter.collect(keep.at[1])
    total = keep[1]
    total = total * gain_rows[0:1, :]
    scale = scales[0, at_of(z), :]
    unit = tok[0, at_of(z), :].astype(F32) * scale
    total = keep[0] + scale * (total - unit * jnp.mean(total * unit, axis=-1, keepdims=True))
    input_ref[...] = total.astype(BF)

    total = misc_out[8:16, :]
    for r, copy in enumerate(gain_copies):
        copy.wait()
        total = total + gains_in[r]
    gains_out[...] = total
    for copy in finals + units:
        copy.wait()
    line.finish()
    first_scatter.finish()
    for copy in over[1:] + small + misc_copies + [part_pass]:
        copy.wait_send()


def backward_call(dp, depth, experts, head, in_vmem, in_hbm):
    output_rows, width = in_vmem[6].shape
    seq_len = output_rows * depth
    slice_width = width // dp
    units = in_hbm[3].shape[1:]
    pair = in_hbm[11].shape[2]
    pairs = pair // head
    vmem, hbm = pl.BlockSpec(memory_space=pltpu.VMEM), pl.BlockSpec(memory_space=pl.ANY)
    shape = jax.ShapeDtypeStruct
    final = shape((4,) + units, BF)
    return pl.pallas_call(
        functools.partial(backward_body, (dp, depth, experts, head)),
        in_specs=[vmem] * len(in_vmem) + [hbm] * len(in_hbm),
        out_specs=[vmem, hbm, hbm, hbm, vmem, vmem, vmem],
        out_shape=[
            shape((output_rows, width), BF),
            final,
            final,
            final,
            shape((2, slice_width, 4 * pair), BF),
            shape((16, slice_width), F32),
            shape((8, slice_width), F32),
        ],
        scratch_shapes=[
            pltpu.VMEM((4,) + units, BF),
            pltpu.VMEM((3, 4) + units, BF),
            pltpu.VMEM((3, seq_len, width), BF),
            pltpu.VMEM((2, 2, depth - 1, output_rows, width), BF),
            pltpu.VMEM((seq_len, 128), F32),
            pltpu.VMEM((depth - 1, output_rows, 128), F32),
            pltpu.VMEM((2, seq_len, width + 128), BF),
            pltpu.VMEM((2, seq_len, width), BF),
            pltpu.VMEM((2, 2, 2, slice_width, 4 * pair), BF),
            pltpu.VMEM((3, 2 * pairs, seq_len, head), BF),
            pltpu.VMEM((2 * pairs, seq_len, seq_len), BF),
            pltpu.VMEM((2, seq_len, pair), BF),
            pltpu.VMEM((2, seq_len, 1), F32),
            pltpu.VMEM((2, seq_len, 3 * pair), BF),
            pltpu.VMEM((seq_len, width), BF),
            pltpu.VMEM((2, output_rows, width), F32),
            pltpu.VMEM((2, 2, 2, slice_width, 4 * pair), BF),
            pltpu.VMEM((1, 2, 2, slice_width, 2 * pair), BF),
            pltpu.VMEM((2, 1, 2, slice_width, 2 * pair), BF),
            pltpu.VMEM((2, 1, 1, 2, slice_width, 2 * pair), BF),
            pltpu.VMEM((dp, 16, slice_width), F32),
            pltpu.VMEM((dp - 1, 16, slice_width), F32),
            pltpu.VMEM((depth - 1, 8, slice_width), F32),
            pltpu.VMEM((8, width), F32),
            pltpu.SemaphoreType.DMA((96,)),
            pltpu.SemaphoreType.DMA((96,)),
            pltpu.SemaphoreType.DMA((40,)),
        ],
        compiler_params=pltpu.CompilerParams(
            collective_id=1, has_side_effects=True, vmem_limit_bytes=62 * 2**20
        ),
    )(*in_vmem, *in_hbm)


def finish_body(
    gate_ref, up_ref, down_ref, attn_ref, eg_ref, eu_ref, ed_ref, sg_ref, su_ref, sd_ref,
    q_ref, k_ref, v_ref, o_ref, sg_rows, su_rows
):
    group, groups = pl.program_id(0), pl.num_programs(0)
    many, rows, _ = eg_ref.shape
    for source, routed, shared in (
        (gate_ref, eg_ref, sg_rows.at[group]),
        (up_ref, eu_ref, su_rows.at[group]),
        (down_ref, ed_ref, sd_ref),
    ):
        for unit in range(many):
            routed[unit] = source[0, unit].astype(F32)
        shared[...] = source[0, many].astype(F32)

    @pl.when(group == 0)
    def _():
        pair = attn_ref.shape[2] // 4
        for c in range(2):
            at = slice(c * pair, (c + 1) * pair)
            for kind, out_ref in enumerate((q_ref, k_ref, v_ref)):
                out_ref[:, at] = attn_ref[c, :, kind * pair : (kind + 1) * pair].astype(F32)
            o_ref[at, :] = jnp.transpose(attn_ref[c, :, 3 * pair :].astype(F32))

    @pl.when(group == groups - 1)
    def _():
        for source, out_ref in ((sg_rows, sg_ref), (su_rows, su_ref)):
            out_ref[...] = jnp.transpose(source[...].reshape(groups * rows, -1))


def finish_call(gate, up, down, attn):
    groups, units, rows, slice_width = gate.shape
    many, pair = units - 1, attn.shape[2] // 4
    shape = jax.ShapeDtypeStruct

    def whole(*dims):
        return pl.BlockSpec(dims, lambda g: (0,) * len(dims))

    source = pl.BlockSpec((1, units, rows, slice_width), lambda g: (g, 0, 0, 0))
    routed = pl.BlockSpec((many, rows, slice_width), lambda g: (g, 0, 0))
    return call(
        finish_body,
        (groups,),
        [source] * 3 + [whole(*attn.shape)],
        [routed] * 3
        + [whole(slice_width, groups * rows)] * 2
        + [pl.BlockSpec((rows, slice_width), lambda g: (g, 0))]
        + [whole(slice_width, 2 * pair)] * 3
        + [whole(2 * pair, slice_width)],
        [shape((groups * many, rows, slice_width), F32)] * 3
        + [shape((slice_width, groups * rows), F32)] * 2
        + [shape((groups * rows, slice_width), F32)]
        + [shape((slice_width, 2 * pair), F32)] * 3
        + [shape((2 * pair, slice_width), F32)],
        0,
        groups * units * rows * slice_width * 18,
        [pltpu.VMEM((groups, rows, slice_width), F32)] * 2,
    )(gate, up, down, attn)


def local_plain(
    dp,
    tokens,
    picture_ids,
    routes,
    slot_order,
    norm_gains,
    w_query,
    w_key,
    w_value,
    w_out,
    qkv_bias,
    router,
    shared_gate,
    shared_up,
    shared_down,
    expert_gate,
    expert_up,
    expert_down,
    out_grad,
):
    seq_len = picture_ids.shape[0]
    local_rows = tokens.shape[0]
    width = tokens.shape[1]
    experts, slice_width, hidden_units = expert_gate.shape
    top_count = routes.shape[1]
    capacity = 5 * seq_len * top_count // (4 * experts)
    heads_local = qkv_bias.shape[1]
    head_width = w_query.shape[1] // heads_local
    pair_heads = heads_local // 2
    pair_width = pair_heads * head_width
    mine_experts = experts // 4
    hidden_pad = -(-hidden_units // 128) * 128

    me = lax.axis_index("dp")
    zi = lax.axis_index("tensor")
    core, xi = me % 2, (me // 2) % 2
    group = me % 4
    bits = []
    while 2 ** (len(bits) + 1) <= dp:
        bits.append(2 ** len(bits))
    upper = bits[2:]

    def swap(array, bit):
        return lax.ppermute(array, "dp", [(i, i ^ bit) for i in range(dp)])

    def bit_of(bit):
        return (me // bit) % 2

    def join(mine, theirs, bit, axis):
        n = mine.shape[axis]
        shape = list(mine.shape)
        shape[axis] = 2 * n
        out = jnp.zeros(shape, mine.dtype)
        out = lax.dynamic_update_slice_in_dim(out, mine, n * bit_of(bit), axis)
        return lax.dynamic_update_slice_in_dim(out, theirs, n * (1 - bit_of(bit)), axis)

    def half(array, which, axis):
        n = array.shape[axis] // 2
        return lax.dynamic_slice_in_dim(array, which * n, n, axis)

    gains_z = lax.all_gather(norm_gains, "tensor", axis=1, tiled=True)
    misc_rows = 16
    bias_width = 3 * pair_heads * qkv_bias.shape[2]
    bias_cores = qkv_bias.reshape(3, 2, -1).swapaxes(0, 1).reshape(2, bias_width)

    def misc_pack(core_bias):
        wide = jnp.zeros((misc_rows, 2 * pair_width), BF)
        wide = wide.at[: experts + 1, :slice_width].set(router.T)
        wide = wide.at[experts + 1, :bias_width].set(core_bias)
        return wide.at[experts + 2 : experts + 4, :slice_width].set(gains_z)

    qk = jnp.concatenate(
        [w.reshape(slice_width, 2, pair_width) for w in (w_query, w_key)], axis=2
    )
    qk = jnp.concatenate(
        [qk, jnp.stack([misc_pack(bias_cores[0]), misc_pack(bias_cores[1])], axis=1)], axis=0
    )
    vo = jnp.concatenate(
        [w.reshape(slice_width, 2, pair_width) for w in (w_value, w_out.T)], axis=2
    )
    tokens_z = lax.all_gather(tokens, "tensor", axis=0, tiled=True)

    def gather_attention(pack, order):
        dims = (1,) * len(bits[1:])
        both = join(pick(pack, core, 1)[None], swap(pick(pack, 1 - core, 1), 1)[None], 1, 0)
        both = both.reshape(dims + both.shape)
        for bit in order:
            axis = len(bits) - 1 - bits.index(bit)
            both = join(both, swap(both, bit), bit, axis)
        return both.reshape((dp,) + both.shape[-2:])

    qk_all = gather_attention(qk, bits[1:])
    vo_full = gather_attention(vo, bits[:0:-1]).reshape(width, 2 * pair_width)
    qk_full = qk_all[:, :slice_width].reshape(width, 2 * pair_width)
    misc = qk_all[:, slice_width:]
    router_full = misc[:, : experts + 1, :slice_width].swapaxes(1, 2).reshape(width, -1)
    gain_rows = misc[:, experts + 2 : experts + 4, :slice_width].swapaxes(0, 1)
    gain_rows = gain_rows.reshape(2, width).astype(F32)
    bias = misc[:, experts + 1, :bias_width].astype(F32)
    bias = bias.reshape(dp, 3 * pair_heads, -1).swapaxes(0, 1).reshape(3, pair_width)

    tokens_sib = swap(tokens_z, 1)
    grad_z = lax.all_gather(out_grad, "tensor", axis=0, tiled=True)

    codes = jnp.concatenate([routes, slot_order], axis=1).T
    codes_x = swap(codes, 2)
    both_codes = swap(jnp.stack([codes, codes_x]), 1)
    codes_a = jnp.stack([codes, both_codes[0]])
    codes_b = jnp.stack([codes_x, both_codes[1]])
    pictures = jnp.stack([picture_ids, swap(picture_ids, 1)])

    def core_units(routed, shared):
        routed = routed.reshape(2, 2, mine_experts, hidden_units, slice_width)
        shared = shared.reshape(2, 2, 1, hidden_units, slice_width)

        def cut(which):
            return jnp.concatenate([pick(routed, which, 1), pick(shared, which, 1)], axis=1)

        return join(cut(core), swap(cut(1 - core), 1), 1, 3)

    def x_units(held):
        return join(pick(held, xi, 0), swap(pick(held, 1 - xi, 0), 2), 2, 2)

    def upper_units(held):
        for bit in upper[:-1]:
            held = join(held, swap(held, bit), bit, 2)
        return held, swap(held, upper[-1])

    def padded(*pairs):
        n = pairs[0][0].shape[-1]
        out = jnp.zeros((mine_experts + 1, len(pairs) * hidden_pad, 2 * n), BF)
        zero = jnp.int32(0)
        for k, (mine, theirs) in enumerate(pairs):
            row = jnp.int32(k * hidden_pad)
            out = lax.dynamic_update_slice(out, mine, (zero, row, n * bit_of(upper[-1])))
            out = lax.dynamic_update_slice(out, theirs, (zero, row, n * (1 - bit_of(upper[-1]))))
        return out

    down_c = core_units(expert_down, shared_down)
    gate_c = core_units(expert_gate.swapaxes(1, 2), shared_gate.T)
    up_c = core_units(expert_up.swapaxes(1, 2), shared_up.T)
    down_x = x_units(down_c)
    gate_x = x_units(gate_c)
    up_x = x_units(up_c)
    grad_x = swap(after(grad_z, up_x), 2)
    down_y = upper_units(down_x)
    gate_y = upper_units(gate_x)
    up_y = upper_units(up_x)

    rows_f = jnp.stack([tokens_z, tokens_sib]).astype(F32)
    qk_full = after(qk_full, down_c, gate_c, up_c)
    first_scale = lax.rsqrt(jnp.mean(rows_f * rows_f, axis=-1, keepdims=True) + EPS)
    first_norm = (rows_f * first_scale * gain_rows[0]).astype(BF)
    qk_pre = einsum("std,df->stf", first_norm, qk_full) + jnp.concatenate([bias[0], bias[1]])
    values = (einsum("std,df->stf", first_norm, vo_full[:, :pair_width]) + bias[2]).astype(BF)
    cos_part, sin_part = rope_tables(seq_len, head_width)
    qk_rot = rotate(
        qk_pre.reshape(2, seq_len, 2 * pair_heads, head_width), cos_part, sin_part
    ).astype(BF)
    qk_rot = after(qk_rot, down_x)
    queries, keys = qk_rot[:, :, :pair_heads], qk_rot[:, :, pair_heads:]
    values = values.reshape(2, seq_len, pair_heads, head_width)
    positions = jnp.arange(seq_len, dtype=jnp.int32)
    allowed = jnp.logical_or(
        positions[None, None, :] <= positions[None, :, None],
        pictures[:, :, None] * pictures[:, None, :] > 0,
    )
    score_scale = head_width ** (-0.5)
    scores = einsum("sqhd,skhd->shqk", queries, keys) * score_scale
    scores = jnp.where(allowed[:, None], scores, -1e30)
    weights = jnp.exp(scores - jnp.max(scores, axis=-1, keepdims=True))
    probs = weights / jnp.sum(weights, axis=-1, keepdims=True)
    probs_low = probs.astype(BF)
    head_mix = einsum("shqk,skhd->sqhd", probs_low, values).astype(BF)
    heads_out = after(head_mix.reshape(2, seq_len, pair_width), gate_x)
    out_weight = vo_full[:, pair_width:]
    attn_part = einsum("sqf,df->sqd", heads_out, out_weight)

    def core_sum(own, sibling):
        return own + swap(sibling.astype(BF), 1).astype(F32)

    def z_scatter(array):
        return lax.psum_scatter(
            array.astype(BF), "tensor", scatter_dimension=0, tiled=True
        ).astype(F32)

    inputs = tokens.astype(F32)
    hidden = inputs + z_scatter(core_sum(attn_part[0], attn_part[1]))
    hidden = after(hidden, up_x, down_y[1])
    second_scale = lax.rsqrt(jnp.mean(hidden * hidden, axis=-1, keepdims=True) + EPS)
    second_unit = hidden * second_scale
    second_norm = (second_unit * gain_rows[1]).astype(BF)
    norm_z = lax.all_gather(second_norm, "tensor", axis=0, tiled=True)
    norm_z = after(norm_z, gate_y[1], grad_x)
    down_all = padded(down_y)
    gateup_all = padded(gate_y, up_y)

    norm_x = swap(norm_z, 2)
    norm_a = jnp.stack([norm_z, swap(norm_z, 1)])
    norm_b = jnp.stack([norm_x, swap(norm_x, 1)])
    grad_a = jnp.stack([grad_z, swap(grad_z, 1)])
    grad_b = jnp.stack([grad_x, swap(grad_x, 1)])

    expert_ids = group * mine_experts + jnp.arange(mine_experts, dtype=jnp.int32)

    router_rows = jnp.pad(router_full.T, ((0, 16 - experts - 1), (0, 0)))
    group_ids = group.astype(jnp.int32).reshape(1)

    def slots_of(codes_in):
        routes_in, slots_in = codes_in[:, None, :top_count], codes_in[:, None, top_count:]
        matches = routes_in == expert_ids[None, :, None, None]
        return jnp.max(jnp.where(matches, slots_in, -1), axis=2)

    def feed(slots, rows, grads):
        slotted, slot_grad, pair, act, terms, pair_s, act_s, inner_s, probs_out = plain_act_call(
            experts, capacity, group_ids, slots, rows, grads, router_rows, gateup_all, down_all
        )
        terms = jnp.concatenate([terms.swapaxes(1, 2), inner_s], axis=-1)
        flat = [a.reshape(mine_experts, -1, a.shape[-1]) for a in (slotted, slot_grad, pair, act)]
        shared = [a.reshape(1, -1, a.shape[-1]) for a in (rows, grads, pair_s, act_s)]
        return (pair, pair_s), (act, act_s), terms, (flat, shared), probs_out

    slots_a, slots_b = slots_of(codes_a), slots_of(codes_b)
    fed_a = feed(slots_a, norm_a, grad_a)
    fed_b = feed(slots_b, norm_b, grad_b)
    columns_a, columns_b = slots_a[..., None], slots_b[..., None]
    row_grad_b = plain_back_call(columns_b, *fed_b[0], gateup_all)
    row_grad_a = plain_back_call(after(columns_a, row_grad_b), *fed_a[0], gateup_all)
    row_out_b = plain_back_call(after(columns_b, row_grad_a), *fed_b[1], down_all)
    row_out_a = plain_back_call(columns_a, *fed_a[1], down_all)

    def spread(terms):
        wide = jnp.zeros(terms.shape[:-1] + (128,), F32)
        wide = lax.dynamic_update_slice_in_dim(
            wide, terms[..., :mine_experts], group * mine_experts, terms.ndim - 1
        )
        return wide.at[..., experts].set(terms[..., mine_experts])

    def group_sum(a, b):
        across = b[0].astype(F32) + swap(b[1].astype(BF), 1).astype(F32)
        near = a[0].astype(F32) + swap(a[1].astype(BF), 1).astype(F32)
        return near + swap(across.astype(BF), 2).astype(F32)

    grad_sum = group_sum(row_grad_a, row_grad_b)
    term_sum = group_sum(spread(fed_a[2]), spread(fed_b[2]))
    packed = z_scatter(jnp.concatenate([grad_sum, term_sum], axis=-1))
    second_grad, gate_sums = packed[:, :width], packed[:, width:]

    data_a, data_b = fed_a[3], fed_b[3]

    def unit_grads(left, right):
        return jnp.concatenate(
            [
                plain_outer_call(
                    hidden_units,
                    hidden_pad,
                    dp,
                    [(data[k][left], data[k][right]) for data in (data_a, data_b)],
                )
                for k in range(2)
            ],
            axis=1,
        )

    def scatter_units(total):
        total = total.reshape((2,) * len(bits) + total.shape[1:])
        for bit in reversed(upper):
            axis = len(bits) - 1 - bits.index(bit)
            sent = half(total, 1 - bit_of(bit), axis)
            kept = half(total, bit_of(bit), axis)
            total = (kept.astype(F32) + swap(sent, bit).astype(F32)).astype(BF)
        total = total.reshape((2, 2) + total.shape[len(bits) :])
        held = join(pick(total, xi, 0)[None], swap(pick(total, 1 - xi, 0), 2)[None], 2, 0)
        return join(pick(held, core, 1)[:, None], swap(pick(held, 1 - core, 1), 1)[:, None], 1, 1)

    def split_units(held):
        routed = held[:, :, :mine_experts].reshape(experts, -1, slice_width)
        shared = held[:, :, mine_experts]
        return routed.astype(F32), shared.astype(F32)

    gateup_sum = scatter_units(unit_grads(2, 0))
    down_sum = scatter_units(unit_grads(3, 1))
    routed_gu, shared_gu = split_units(gateup_sum)
    routed_down, shared_down_sum = split_units(down_sum)
    shared_gu = shared_gu.reshape(4, 2, hidden_units, slice_width)
    egate_sum = routed_gu[:, :hidden_units].swapaxes(1, 2)
    eup_sum = routed_gu[:, hidden_units:].swapaxes(1, 2)
    sgate_sum = shared_gu[:, 0].reshape(-1, slice_width).T
    sup_sum = shared_gu[:, 1].reshape(-1, slice_width).T
    sdown_sum = shared_down_sum.reshape(-1, slice_width)

    row_start = zi * local_rows
    probs_local = lax.dynamic_slice_in_dim(fed_a[4][0], row_start, local_rows, 1).T
    probs_mine, weight_mine = probs_local[:, :experts], probs_local[:, experts]
    route_grad = gate_sums[:, :experts]
    expert_logit_grad = probs_mine * (
        route_grad - jnp.sum(probs_mine * route_grad, axis=-1, keepdims=True)
    )
    weight_logit_grad = gate_sums[:, experts] * weight_mine * (1.0 - weight_mine)
    logits_grad = jnp.concatenate([expert_logit_grad, weight_logit_grad[:, None]], axis=1).astype(
        BF
    )
    second_grad = second_grad + einsum("tf,df->td", logits_grad, router_full)
    gain_two_grad = jnp.sum(second_grad * second_unit, axis=0)
    unit_two = second_grad * gain_rows[1]
    hidden_grad = out_grad.astype(F32) + second_scale * (
        unit_two - second_unit * jnp.mean(unit_two * second_unit, axis=-1, keepdims=True)
    )
    attention_grad = hidden_grad.astype(BF)
    wide_logits = jnp.pad(logits_grad, ((0, 0), (0, 128 - experts - 1)))
    back_z = lax.all_gather(
        jnp.concatenate([attention_grad, wide_logits], axis=1), "tensor", axis=0, tiled=True
    )
    out_sum = after(group_sum(row_out_a, row_out_b), back_z)
    output = (hidden + z_scatter(out_sum)).astype(BF)
    logits_z = back_z[:, width : width + 16]
    back_own = back_z[:, :width]
    back_rows = jnp.stack([back_own, swap(back_own, 1)])

    router_part = einsum("tf,td->fd", logits_z, norm_z)[: experts + 1]

    out_proj = einsum("std,stf->df", back_rows, heads_out)
    mix_grad = einsum("std,df->stf", back_rows, out_weight).astype(BF)
    mix_grad = mix_grad.reshape(2, seq_len, pair_heads, head_width)
    prob_grad = einsum("sqhd,skhd->shqk", mix_grad, values)
    score_grad = (
        probs * (prob_grad - jnp.sum(probs * prob_grad, axis=-1, keepdims=True))
    ).astype(BF)
    query_rot = einsum("shqk,skhd->sqhd", score_grad, keys) * score_scale
    key_rot = einsum("shqk,sqhd->skhd", score_grad, queries) * score_scale
    value_grad = einsum("shqk,sqhd->skhd", probs_low, mix_grad)
    qk_grad = rotate(jnp.concatenate([query_rot, key_rot], axis=2), cos_part, -sin_part)
    qk_grad = qk_grad.astype(BF).reshape(2, seq_len, 2 * pair_width)
    v_grad = value_grad.astype(BF).reshape(2, seq_len, pair_width)
    first_part = einsum("stf,df->std", qk_grad, qk_full) + einsum(
        "stf,df->std", v_grad, vo_full[:, :pair_width]
    )
    first_grad = z_scatter(core_sum(first_part[0], first_part[1]))

    gain_one_grad = jnp.sum(first_part * (rows_f * first_scale), axis=(0, 1))
    bias_part = jnp.concatenate(
        [jnp.sum(qk_grad.astype(F32), axis=(0, 1)), jnp.sum(v_grad.astype(F32), axis=(0, 1))]
    )
    bias_part = bias_part.reshape(3 * pair_heads, dp, -1).swapaxes(0, 1).reshape(dp, 1, -1)
    gain_part = jnp.stack([gain_one_grad, gain_two_grad]).reshape(2, dp, slice_width)

    def wide_rows(rows):
        return jnp.pad(rows, ((0, 0), (0, 0), (0, 2 * pair_width - rows.shape[2])))

    misc_part = jnp.concatenate(
        [
            wide_rows(router_part.reshape(experts + 1, dp, slice_width).swapaxes(0, 1)),
            wide_rows(bias_part),
            wide_rows(gain_part.swapaxes(0, 1)),
            jnp.zeros((dp, misc_rows - experts - 4, 2 * pair_width), F32),
        ],
        axis=1,
    )
    qk_total = einsum("std,stf->df", first_norm, qk_grad).reshape(dp, slice_width, -1)
    qk_total = jnp.concatenate([qk_total, misc_part], axis=1)
    vo_total = jnp.concatenate([einsum("std,stf->df", first_norm, v_grad), out_proj], axis=1)
    vo_total = vo_total.reshape(dp, slice_width, -1)

    def scatter_attention(total, order):
        total = total.reshape((2,) * len(bits) + total.shape[1:])
        for bit in order:
            axis = len(bits) - 1 - bits.index(bit)
            sent = half(total, 1 - bit_of(bit), axis).astype(BF)
            total = half(total, bit_of(bit), axis) + swap(sent, bit).astype(F32)
        total = total.reshape((2,) + total.shape[-2:]).astype(BF)
        return pick(total, core, 0), swap(pick(total, 1 - core, 0), 1)

    def columns_of(mine, theirs):
        held = join(mine[:slice_width, None], theirs[:slice_width, None], 1, 1)
        first, second = held[..., :pair_width], held[..., pair_width:]
        return (
            first.reshape(slice_width, -1).astype(F32),
            second.reshape(slice_width, -1).astype(F32),
        )

    qk_mine, qk_theirs = scatter_attention(qk_total, bits[:0:-1])
    vo_mine, vo_theirs = scatter_attention(vo_total, bits[1:])
    qk_sums = columns_of(qk_mine, qk_theirs)
    vo_sums = columns_of(vo_mine, vo_theirs)
    misc_mine = qk_mine[slice_width:].astype(F32)
    misc_theirs = qk_theirs[slice_width:].astype(F32)
    misc_sum = misc_mine + misc_theirs
    router_sum = misc_sum[: experts + 1, :slice_width].T
    bias_sums = join(
        misc_mine[experts + 1, :bias_width].reshape(3, 1, pair_heads, -1),
        misc_theirs[experts + 1, :bias_width].reshape(3, 1, pair_heads, -1),
        1,
        1,
    ).reshape(3, heads_local, -1)
    gain_sums = lax.all_gather(
        misc_sum[experts + 2 : experts + 4, :slice_width], "tensor", axis=0, tiled=False
    )
    tensor = gain_sums.shape[0]
    gain_sums = jnp.sum(gain_sums, axis=0).reshape(2, tensor, -1)
    gain_sums = pick(gain_sums, zi, 1)

    unit_mine = inputs * lax.rsqrt(jnp.mean(inputs * inputs, axis=-1, keepdims=True) + EPS)
    scale_mine = lax.rsqrt(jnp.mean(inputs * inputs, axis=-1, keepdims=True) + EPS)
    unit_one = first_grad * gain_rows[0]
    input_grad = hidden_grad + scale_mine * (
        unit_one - unit_mine * jnp.mean(unit_one * unit_mine, axis=-1, keepdims=True)
    )
    return (
        output,
        input_grad.astype(BF),
        gain_sums,
        qk_sums[0],
        qk_sums[1],
        vo_sums[0],
        vo_sums[1].T,
        bias_sums,
        router_sum,
        sgate_sum,
        sup_sum,
        sdown_sum,
        egate_sum,
        eup_sum,
        routed_down,
    )


def local_fused(
    dp,
    depth,
    tokens,
    picture_ids,
    routes,
    slot_order,
    norm_gains,
    w_query,
    w_key,
    w_value,
    w_out,
    qkv_bias,
    router,
    shared_gate,
    shared_up,
    shared_down,
    expert_gate,
    expert_up,
    expert_down,
    out_grad,
):
    seq_len = picture_ids.shape[0]
    local_rows = tokens.shape[0]
    width = tokens.shape[1]
    experts, slice_width, hidden_units = expert_gate.shape
    heads_local = qkv_bias.shape[1]
    head_width = w_query.shape[1] // heads_local
    pair_heads = heads_local // 2
    pair_width = pair_heads * head_width
    mine_experts = experts // 4
    hidden_pad = -(-hidden_units // 128) * 128

    zi = lax.axis_index("tensor")
    codes = jnp.concatenate([routes.T, slot_order.T, picture_ids[None]], axis=0)
    codes = jnp.pad(codes, ((0, 16 - codes.shape[0]), (0, 0)))
    bias_cores = qkv_bias.reshape(3, 2, -1).swapaxes(0, 1).reshape(2, -1)
    bias_width = bias_cores.shape[1]
    misc = jnp.zeros((16, slice_width), F32)
    misc = misc.at[: experts + 1].set(router.T.astype(F32))
    misc = misc.at[experts + 1 : experts + 3, :bias_width].set(bias_cores.astype(F32))
    gains = lax.dynamic_update_slice(
        jnp.zeros((8, slice_width), F32),
        norm_gains.astype(F32),
        (jnp.int32(0), zi * norm_gains.shape[1]),
    )
    cos_part, sin_part = rope_tables(seq_len, head_width)
    cos_rows = jnp.concatenate([cos_part, cos_part], axis=1)
    sin_rows = jnp.concatenate([-sin_part, sin_part], axis=1)
    (
        hidden,
        norm_all,
        grads_all,
        gateup_all,
        down_all,
        codes_all,
        router_rows,
        gain_rows,
        tok,
        attn_weights,
        qkv,
        probs_low,
        heads_out,
    ) = forward_call(
        dp,
        depth,
        experts,
        head_width,
        (codes, misc, gains, cos_rows, sin_rows),
        (tokens, out_grad, w_query, w_key, w_value, w_out.T),
        (
            expert_gate.swapaxes(1, 2),
            expert_up.swapaxes(1, 2),
            expert_down,
            shared_gate.T.reshape(4, hidden_units, slice_width),
            shared_up.T.reshape(4, hidden_units, slice_width),
            shared_down.reshape(4, hidden_units, slice_width),
        ),
    )
    gateup_all = gateup_all.reshape(mine_experts + 1, 2 * hidden_pad, width)
    down_all = down_all.reshape(mine_experts + 1, hidden_pad, width)
    (
        output,
        terms,
        probs_mine,
        grad_own,
        grad_sib,
        grad_far,
        gate_total,
        up_total,
        down_total,
        gate_in,
    ) = middle_call(
        dp,
        depth,
        experts,
        routes.shape[1],
        hidden_units,
        hidden,
        codes_all,
        router_rows,
        (norm_all, grads_all, gateup_all, down_all),
    )
    input_grad, gate_sum, up_sum, down_sum, attn_sum, misc_sum, gains_sum = backward_call(
        dp,
        depth,
        experts,
        head_width,
        (terms, probs_mine, router_rows, gain_rows, cos_rows, sin_rows, hidden, out_grad),
        (grad_own, grad_sib, grad_far, gate_in, gate_total, up_total, down_total)
        + (tok, attn_weights, qkv, probs_low, heads_out, norm_all),
    )

    egate_sum, eup_sum, edown_sum, sgate_sum, sup_sum, sdown_sum, *attn_sums = finish_call(
        gate_sum, up_sum, down_sum, attn_sum
    )
    bias_sums = misc_sum[experts + 1 : experts + 3, :bias_width].reshape(2, 3, pair_heads, -1)
    bias_sums = bias_sums.swapaxes(0, 1).reshape(3, heads_local, -1)
    piece = norm_gains.shape[1]
    gain_sums = lax.dynamic_slice(gains_sum[3:5], (jnp.int32(0), zi * piece), (2, piece))
    return (
        output,
        input_grad,
        gain_sums,
        *attn_sums,
        bias_sums,
        misc_sum[: experts + 1].T,
        sgate_sum,
        sup_sum,
        sdown_sum,
        egate_sum.swapaxes(1, 2),
        eup_sum.swapaxes(1, 2),
        edown_sum,
    )


def solution(mesh):
    dp, depth = mesh.shape["dp"], mesh.shape["tensor"]

    def body(*arrays):
        if arrays[5].shape[0] % 128 == 0 and dp == 8 and depth == 4:
            return local_fused(dp, depth, *arrays)
        return local_plain(dp, *arrays)

    return jax.shard_map(
        body,
        mesh=mesh,
        in_specs=(
            P(("dp", "tensor"), None),
            P("dp"),
            P("dp", None),
            P("dp", None),
            P(None, ("dp", "tensor")),
            P("dp", "tensor"),
            P("dp", "tensor"),
            P("dp", "tensor"),
            P("tensor", "dp"),
            P(None, "tensor", "dp"),
            P("dp", None),
            P("dp", "tensor"),
            P("dp", "tensor"),
            P("tensor", "dp"),
            P(None, "dp", "tensor"),
            P(None, "dp", "tensor"),
            P(None, "tensor", "dp"),
            P(("dp", "tensor"), None),
        ),
        out_specs=(
            P(("dp", "tensor"), None),
            P(("dp", "tensor"), None),
            P(None, ("dp", "tensor")),
            P("dp", "tensor"),
            P("dp", "tensor"),
            P("dp", "tensor"),
            P("tensor", "dp"),
            P(None, "tensor", "dp"),
            P("dp", None),
            P("dp", "tensor"),
            P("dp", "tensor"),
            P("tensor", "dp"),
            P(None, "dp", "tensor"),
            P(None, "dp", "tensor"),
            P(None, "tensor", "dp"),
        ),
        check_vma=False,
    )
```

```python
import functools

import jax
import jax.numpy as jnp
import numpy as np
from jax import lax
from jax.experimental import pallas as pl
from jax.experimental.pallas import tpu as pltpu
from jax.sharding import PartitionSpec as P

EPS = 1e-06
THETA = 1000000.0
BF = jnp.bfloat16
F32 = jnp.float32


def rope_tables(length, width):
    half_width = width // 2
    inverse = THETA ** (-(2.0 * jnp.arange(half_width, dtype=F32)) / width)
    angles = jnp.arange(length, dtype=F32)[:, None] * inverse[None, :]
    return jnp.cos(angles), jnp.sin(angles)


def rope_arrays(length, width):
    inverse = THETA ** (-(2.0 * np.arange(width // 2)) / width)
    angles = np.arange(length)[:, None] * inverse[None, :]
    return np.cos(angles).astype(np.float32), np.sin(angles).astype(np.float32)


def rotate(field_in, cos_part, sin_part):
    half_width = field_in.shape[-1] // 2
    low, high = field_in[..., :half_width], field_in[..., half_width:]
    cos_rows, sin_rows = cos_part[:, None, :], sin_part[:, None, :]
    return jnp.concatenate(
        [low * cos_rows - high * sin_rows, high * cos_rows + low * sin_rows], axis=-1
    )


def einsum(spec, *args):
    return jnp.einsum(spec, *args, preferred_element_type=F32)


def silu_parts(gate_in):
    gate_sig = jax.nn.sigmoid(gate_in)
    return gate_in * gate_sig, gate_sig * (1.0 + gate_in * (1.0 - gate_sig))


def after(array, *others):
    return lax.optimization_barrier((array,) + others)[0]


def pick(array, index, axis):
    return lax.dynamic_index_in_dim(array, index, axis, keepdims=False)


VMEM_LIMIT = 58 * 2**20


def dot(left, right, left_dim=1, right_dim=0):
    return lax.dot_general(
        left, right, (((left_dim,), (right_dim,)), ((), ())), preferred_element_type=F32
    )


def call(body, grid, in_specs, out_specs, out_shape, flops, moved, scratch=()):
    return pl.pallas_call(
        body,
        grid=grid,
        in_specs=in_specs,
        out_specs=out_specs,
        out_shape=out_shape,
        scratch_shapes=scratch,
        cost_estimate=pl.CostEstimate(flops=flops, bytes_accessed=moved, transcendentals=0),
        compiler_params=pltpu.CompilerParams(vmem_limit_bytes=VMEM_LIMIT),
    )


def plain_act_body(
    experts,
    units,
    group_ref,
    slot_ref,
    rows_ref,
    grads_ref,
    router_ref,
    gateup_ref,
    down_ref,
    slotted_ref,
    slotgrad_ref,
    pair_ref,
    act_ref,
    terms_ref,
    pair_s_ref,
    act_s_ref,
    inner_s_ref,
    probs_ref,
):
    unit = pl.program_id(1)
    half = gateup_ref.shape[1] // 2
    seq_len = rows_ref.shape[1]
    capacity = slotted_ref.shape[2]

    @pl.when(unit == 0)
    def _():
        logits = dot(router_ref[...], rows_ref[0], 1, 1)
        row = lax.broadcasted_iota(jnp.int32, logits.shape, 0)
        routed = jnp.where(row < experts, logits, -1e30)
        raised = jnp.exp(routed - jnp.max(routed, axis=0, keepdims=True))
        soft = raised / jnp.sum(raised, axis=0, keepdims=True)
        probs_ref[0] = jnp.where(row < experts, soft, jax.nn.sigmoid(logits))

    def parts(data, cot, weight):
        both = dot(data, gateup_ref[0], 1, 1)
        cot_in = dot(cot, down_ref[0], 1, 1)
        gate_in, up_in = both[:, :half], both[:, half:]
        gate_act, gate_slope = silu_parts(gate_in)
        act = gate_act * up_in
        inner = jnp.sum(act.astype(BF).astype(F32) * cot_in, axis=1, keepdims=True)
        cot_in = cot_in * weight
        return (
            (act * weight).astype(BF),
            (cot_in * up_in * gate_slope).astype(BF),
            (cot_in * gate_act).astype(BF),
            inner,
        )

    @pl.when(unit < units - 1)
    def _():
        slot = slot_ref[0, pl.ds(unit, 1), :]
        mask = lax.broadcasted_iota(jnp.int32, (capacity, seq_len), 0) == slot
        onehot = mask.astype(F32).astype(BF)
        slotted_ref[0, 0] = dot(onehot, rows_ref[0]).astype(BF)
        slotgrad_ref[0, 0] = dot(onehot, grads_ref[0]).astype(BF)
        probs = probs_ref[0]
        row = lax.broadcasted_iota(jnp.int32, probs.shape, 0)
        expert = group_ref[0] * (units - 1) + unit
        gate = jnp.sum(jnp.where(row == expert, probs, 0.0), axis=0, keepdims=True)
        weight = jnp.sum(jnp.where(mask, gate, 0.0), axis=1, keepdims=True)
        act, gate_grad, up_grad, inner = parts(slotted_ref[0, 0], slotgrad_ref[0, 0], weight)
        act_ref[0, 0] = act
        pair_ref[0, 0, :, :half] = gate_grad
        pair_ref[0, 0, :, half:] = up_grad
        terms_ref[0, pl.ds(unit, 1), :] = jnp.sum(
            jnp.where(mask, inner, 0.0), axis=0, keepdims=True
        )

    @pl.when(unit == units - 1)
    def _():
        logits = dot(rows_ref[0], router_ref[...], 1, 1)
        weight = jax.nn.sigmoid(logits[:, experts : experts + 1])
        act, gate_grad, up_grad, inner = parts(rows_ref[0], grads_ref[0], weight)
        act_s_ref[0] = act
        pair_s_ref[0, :, :half] = gate_grad
        pair_s_ref[0, :, half:] = up_grad
        inner_s_ref[0] = inner


def plain_act_call(experts, capacity, group, slots, rows, grads, router, gateup, down):
    count, seq_len, width = rows.shape
    units, wide, _ = gateup.shape
    half = wide // 2
    routed = units - 1

    def seq(s, u):
        return (s, 0, 0)

    def unit(s, u):
        return (u, 0, 0)

    def slot(s, u):
        return (jnp.minimum(u, routed - 1), s, 0, 0)

    work = count * (routed * capacity + seq_len) * width
    return call(
        functools.partial(plain_act_body, experts, units),
        (count, units),
        [
            pl.BlockSpec(memory_space=pltpu.SMEM),
            pl.BlockSpec((1, routed, seq_len), seq),
            pl.BlockSpec((1, seq_len, width), seq),
            pl.BlockSpec((1, seq_len, width), seq),
            pl.BlockSpec(router.shape, lambda s, u: (0, 0)),
            pl.BlockSpec((1, wide, width), unit),
            pl.BlockSpec((1, half, width), unit),
        ],
        [
            pl.BlockSpec((1, 1, capacity, width), slot),
            pl.BlockSpec((1, 1, capacity, width), slot),
            pl.BlockSpec((1, 1, capacity, wide), slot),
            pl.BlockSpec((1, 1, capacity, half), slot),
            pl.BlockSpec((1, routed, seq_len), seq),
            pl.BlockSpec((1, seq_len, wide), seq),
            pl.BlockSpec((1, seq_len, half), seq),
            pl.BlockSpec((1, seq_len, 1), seq),
            pl.BlockSpec((1,) + (router.shape[0], seq_len), seq),
        ],
        [
            jax.ShapeDtypeStruct((routed, count, capacity, width), BF),
            jax.ShapeDtypeStruct((routed, count, capacity, width), BF),
            jax.ShapeDtypeStruct((routed, count, capacity, wide), BF),
            jax.ShapeDtypeStruct((routed, count, capacity, half), BF),
            jax.ShapeDtypeStruct((count, routed, seq_len), F32),
            jax.ShapeDtypeStruct((count, seq_len, wide), BF),
            jax.ShapeDtypeStruct((count, seq_len, half), BF),
            jax.ShapeDtypeStruct((count, seq_len, 1), F32),
            jax.ShapeDtypeStruct((count, router.shape[0], seq_len), F32),
        ],
        2 * work * 3 * half + 4 * count * routed * capacity * seq_len * width,
        8 * count * seq_len * width * 2,
    )(group, slots, rows, grads, router, gateup, down)


def plain_back_body(slot_ref, routed_ref, shared_ref, weight_ref, out_ref):
    routed, _, capacity, _ = routed_ref.shape
    seq_len = shared_ref.shape[1]
    total = dot(shared_ref[0], weight_ref[routed])
    lane = lax.broadcasted_iota(jnp.int32, (seq_len, capacity), 1)
    for e in range(routed):
        slot_rows = dot(routed_ref[e, 0], weight_ref[e]).astype(BF)
        onehot = (lane == slot_ref[0, e]).astype(F32).astype(BF)
        total = total + dot(onehot, slot_rows)
    out_ref[0] = total.astype(BF)


def plain_back_call(slots, routed, shared, weight):
    units, wide, width = weight.shape
    count, seq_len, _ = shared.shape
    capacity = routed.shape[2]
    block = min(width, 512)
    work = count * ((units - 1) * capacity + seq_len) * width
    return call(
        plain_back_body,
        (width // block, count),
        [
            pl.BlockSpec((1, units - 1, seq_len, 1), lambda j, s: (s, 0, 0, 0)),
            pl.BlockSpec((units - 1, 1, capacity, wide), lambda j, s: (0, s, 0, 0)),
            pl.BlockSpec((1, seq_len, wide), lambda j, s: (s, 0, 0)),
            pl.BlockSpec((units, wide, block), lambda j, s: (0, 0, j)),
        ],
        pl.BlockSpec((1, seq_len, block), lambda j, s: (s, 0, j)),
        jax.ShapeDtypeStruct((count, seq_len, width), BF),
        2 * work * wide + 2 * count * (units - 1) * capacity * seq_len * width,
        units * wide * width * 2 + count * seq_len * width * 2,
    )(slots, routed, shared, weight)


def plain_outer_body(keep, pad, left_a, right_a, left_b, right_b, out_ref):
    total = dot(left_a[0], right_a[0], 0, 0) + dot(left_b[0], right_b[0], 0, 0)
    total = total.astype(BF)
    blocks, _, rows, slice_width = out_ref.shape
    for part in range(rows // keep):
        for k in range(blocks):
            out_ref[k, 0, part * keep : (part + 1) * keep] = total[
                part * pad : part * pad + keep, k * slice_width : (k + 1) * slice_width
            ]


def plain_outer_call(keep, pad, dp, pairs):
    (left_a, right_a), (left_b, right_b) = pairs
    units, rows, wide = left_a.shape
    width = right_a.shape[2]
    slice_width = width // dp
    blocks = max(1, 512 // slice_width)
    kept = wide // pad * keep

    def left(n):
        return pl.BlockSpec((1, n, wide), lambda u, j: (u, 0, 0))

    def right(n):
        return pl.BlockSpec((1, n, blocks * slice_width), lambda u, j: (u, 0, j))

    return call(
        functools.partial(plain_outer_body, keep, pad),
        (units, dp // blocks),
        [left(rows), right(rows), left(rows), right(rows)],
        pl.BlockSpec((blocks, 1, kept, slice_width), lambda u, j: (j, u, 0, 0)),
        jax.ShapeDtypeStruct((dp, units, kept, slice_width), BF),
        4 * units * rows * wide * width,
        units * rows * (wide + width) * 4,
    )(left_a, right_a, left_b, right_b)


MESH = pl.DeviceIdType.MESH


class Copies:
    def __init__(self, send, recv, here):
        self.send, self.recv, self.here = send, recv, here
        self.remote_count = self.local_count = 0

    def remote(self, src, dst, **device):
        k = self.remote_count
        self.remote_count += 1
        return pltpu.make_async_remote_copy(
            src_ref=src,
            dst_ref=dst,
            send_sem=self.send.at[k],
            recv_sem=self.recv.at[k],
            device_id=device,
            device_id_type=MESH,
        )

    def local(self, src, dst):
        k = self.local_count
        self.local_count += 1
        return pltpu.make_async_copy(src, dst, self.here.at[k])


class Line:
    def __init__(self, copies, buffer, z, depth, rows):
        self.z, self.depth = z, depth

        def piece(p):
            return buffer.at[pl.ds(pl.multiple_of(p * rows, rows), rows)]

        def make(k, sign):
            p = z - sign * k
            return copies.remote(piece(p), piece(p), tensor=z + sign)

        self.ups = [make(k, 1) for k in range(depth - 1)]
        self.downs = [make(k, -1) for k in range(depth - 1)]

    def sends(self, k):
        z, top = self.z, self.depth - 1
        return (
            (self.ups[k], jnp.logical_and(z < top, z >= k)),
            (self.downs[k], jnp.logical_and(z > 0, z + k <= top)),
        )

    def begin(self):
        for copy, there in self.sends(0):
            pl.when(there)(copy.start)

    def finish(self):
        for k in range(self.depth - 1):
            for copy, there in self.sends(k):
                pl.when(there)(copy.wait_send)


def peer_of(me, r):
    out, bit = me, 1
    while bit <= r:
        if r & bit:
            out = out + bit - 2 * bit * (me // bit % 2)
        bit *= 2
    return out


def greet(me, z, dp, depth):
    barrier = pltpu.get_barrier_semaphore()
    for r in range(1, dp):
        pl.semaphore_signal(barrier, inc=1, device_id={"dp": peer_of(me, r)}, device_id_type=MESH)
    for r in range(1, depth):
        pl.semaphore_signal(
            barrier, inc=1, device_id={"tensor": (z + r) % depth}, device_id_type=MESH
        )
    pl.semaphore_wait(barrier, dp - 1 + depth - 1)


def spin(field, cos_rows, sin_rows):
    return field * cos_rows + pltpu.roll(field, field.shape[-1] // 2, 1) * sin_rows


def piece_of(buffer, p, rows):
    return buffer.at[pl.ds(pl.multiple_of(p * rows, rows), rows)]


def pass_on(c, source, target, z, depth, rows, sibling, passed):
    def make(p):
        return c.remote(piece_of(source, p, rows), piece_of(target, p, rows), dp=sibling)

    ups = [make(z - k) for k in range(1, depth)]
    downs = [make(z + k) for k in range(1, depth)]
    for k in range(1, depth):
        passed.append((ups[k - 1], z >= k))
        passed.append((downs[k - 1], z + k <= depth - 1))

    def each(k, up):
        (ups if up else downs)[k - 1].start()

    return each


def line_step(line, k, each=None):
    z, top = line.z, line.depth - 1
    onward = line.sends(k) if k < top else (None, None)
    for up, copy, there, further in (
        (True, line.ups[k - 1], z >= k, onward[0]),
        (False, line.downs[k - 1], z + k <= top, onward[1]),
    ):
        pl.when(there)(copy.wait_recv)
        if further is not None:
            pl.when(further[1])(further[0].start)
        if each is not None:
            pl.when(there)(functools.partial(each, k, up))


def forward_body(
    sizes,
    codes_ref,
    misc_ref,
    gains_ref,
    cos_ref,
    sin_ref,
    tokens_ref,
    outgrad_ref,
    wq_ref,
    wk_ref,
    wv_ref,
    wo_ref,
    eg_ref,
    eu_ref,
    ed_ref,
    sg_ref,
    su_ref,
    sd_ref,
    hidden_ref,
    norm_ref,
    grads_ref,
    gateup_ref,
    down_ref,
    codes_all,
    router_out,
    gain_rows,
    tok_out,
    weights_out,
    qkv_out,
    probs_out,
    mix_out,
    misc_all,
    norm_mine,
    tok,
    weights,
    qkv_ref,
    probs_ref,
    mix_ref,
    fnorm,
    part,
    part_in,
    scatter_in,
    gains_all,
    zeros,
    shared_raw,
    shared_rows,
    send,
    recv,
    here,
):
    dp, depth, experts, hidden_units, head = sizes
    me, z = lax.axis_index("dp"), lax.axis_index("tensor")
    core, x = me % 2, (me // 2) % 2
    bits = [2**k for k in range(dp.bit_length() - 1)]
    rows, width = tokens_ref.shape
    seq_len = rows * depth
    slice_width = width // dp
    routed = experts // 4
    c = Copies(send, recv, here)

    def bit_of(bit):
        return (me // bit) % 2

    greet(me, z, dp, depth)

    first = []
    own_codes = c.local(codes_ref, codes_all.at[0])
    own_misc = c.local(misc_ref, misc_all.at[me])
    own_gains = c.local(gains_ref, gains_all.at[z, me])
    for copy in (own_codes, own_misc, own_gains):
        copy.start()
    for r in range(1, 4):
        first.append(c.remote(codes_ref, codes_all.at[r], dp=peer_of(me, r)))
    gain_copies = [c.remote(gains_ref, gains_all.at[z, me], dp=peer_of(me, r)) for r in range(1, dp)]
    misc_copies = [c.remote(misc_ref, misc_all.at[me], dp=peer_of(me, r)) for r in range(1, dp)]
    for copy in gain_copies + misc_copies + first:
        copy.start()

    def piece(buffer, p):
        return buffer.at[pl.ds(pl.multiple_of(p * rows, rows), rows)]

    own_tok = c.local(tokens_ref, piece(tok.at[0], z))
    own_tok.start()
    grad_up = c.local(outgrad_ref, norm_mine)
    grad_up.start()
    own_grad = c.local(norm_mine, piece(grads_ref.at[0], z))

    def columns(k, n):
        return pl.ds(pl.multiple_of(k * n, n), n)

    pair = wq_ref.shape[1] // 2
    own_at = tuple(bit_of(bit) for bit in reversed(bits))
    core_copies = []
    for k, w in enumerate((wq_ref, wk_ref, wv_ref, wo_ref)):
        place = weights.at[own_at + (slice(None), pl.ds(k * pair, pair))]
        core_copies.append(c.remote(w.at[:, columns(1 - core, pair)], place, dp=peer_of(me, 1)))
        core_copies.append(c.local(w.at[:, columns(core, pair)], place))
    for copy in core_copies:
        copy.start()

    beside = peer_of(me, 2)
    own_tok.wait()
    tok_line = Line(c, tok.at[0], z, depth, rows)
    tok_line.begin()
    tok_pass = [c.remote(tokens_ref, piece(tok.at[1], z), dp=peer_of(me, 1))]
    tok_pass[0].start()

    shared_loads = [c.local(sg_ref, shared_raw.at[0]), c.local(su_ref, shared_raw.at[1])]
    for copy in shared_loads:
        copy.start()
    zeros[...] = jnp.zeros_like(zeros)
    pad = zeros.shape[1]
    pads = [c.local(zeros, down_ref.at[:, 0, pl.ds(hidden_units, pad)])]
    pads += [c.local(zeros, gateup_ref.at[:, k, pl.ds(hidden_units, pad)]) for k in range(2)]
    matrices = ((ed_ref, sd_ref, down_ref, 0), (eg_ref, shared_rows.at[0], gateup_ref, 0), (eu_ref, shared_rows.at[1], gateup_ref, 1))
    slab = columns(me, slice_width)

    def group_copies(routed_src, shared_src, dst, k, r):
        group = (peer_of(me, r)) % 4
        many = (
            routed_src.at[pl.ds(group * routed, routed)],
            dst.at[pl.ds(0, routed), k, pl.ds(0, hidden_units), slab],
        )
        one = (shared_src.at[group], dst.at[routed, k, pl.ds(0, hidden_units), slab])
        if r == 0:
            return [c.local(*many), c.local(*one)]
        return [c.remote(*many, dp=peer_of(me, r)), c.remote(*one, dp=peer_of(me, r))]

    near = [[copy for r in (0, 1) for copy in group_copies(*m, r)] for m in matrices]
    far = [[copy for r in (2, 3) for copy in group_copies(*m, r)] for m in matrices]

    def over_copy(dst, k):
        n = 2 * slice_width
        chip = me // 2 + 1 - 2 * x
        cols = pl.ds(pl.multiple_of(chip * n, n), n)
        place = dst.at[:, k, pl.ds(0, hidden_units), cols]
        return c.remote(place, place, dp=peer_of(me, 4))

    over_near = [copy for m in matrices for r in (4, 5) for copy in group_copies(*m, r)]
    over = [over_copy(m[2], m[3]) for m in matrices]

    for copy in core_copies:
        copy.wait()

    def weight_copies(order, half):
        have, copies = [1], []
        for bit in order:
            index = tuple(
                pl.ds(0, 2) if b in have else pl.ds(bit_of(b), 1) for b in reversed(bits)
            )
            place = weights.at[index + (slice(None), pl.ds(half * 2 * pair, 2 * pair))]
            copies.append(c.remote(place, place, dp=peer_of(me, bit)))
            have.append(bit)
        return copies

    qk_copies = weight_copies(bits[1:], 0)
    vo_copies = weight_copies(bits[:0:-1], 1)
    qk_copies[0].start()
    vo_copies[0].start()
    grad_cut = width * 12 // 16
    grad_left, grad_right = pl.ds(0, grad_cut), pl.ds(grad_cut, width - grad_cut)
    far_grads = grads_ref.at[2, :, grad_right]
    grad_beside = c.remote(outgrad_ref.at[:, grad_right], piece(far_grads, z), dp=beside)
    grad_beside.start()
    far_grad_line = Line(c, far_grads, z, depth, rows)
    for k in range(2):
        shared_loads[k].wait()
        flipped = jnp.transpose(shared_raw[k].astype(F32)).astype(BF)
        shared_rows[k] = flipped.reshape(shared_rows.shape[1:])
    for copy in pads + [copy for m in near for copy in m]:
        copy.start()

    own_gains.wait()
    for copy in gain_copies:
        copy.wait_recv()
    gain_spread = [
        c.remote(gains_all.at[z], gains_all.at[z], tensor=(z + r) % depth) for r in range(1, depth)
    ]
    for copy in gain_spread:
        copy.start()

    tok_passed = []
    sibling = peer_of(me, 1)
    pass_tok = pass_on(c, tok.at[0], tok.at[1], z, depth, rows, sibling, tok_passed)

    line_step(tok_line, 1, pass_tok)
    for k in range(1, len(bits) - 1):
        qk_copies[k - 1].wait_recv()
        qk_copies[k].start()
        vo_copies[k - 1].wait_recv()
        vo_copies[k].start()
    grad_up.wait()
    own_grad.start()
    own_grad.wait()
    grad_line = Line(c, grads_ref.at[0], z, depth, rows)
    for k in range(2, depth):
        line_step(tok_line, k, pass_tok)
    grad_line.begin()

    for copy in gain_spread:
        copy.wait_recv()
    for d in range(dp):
        total = gains_all[0, d]
        for t in range(1, depth):
            total = total + gains_all[t, d]
        gain_rows[:, d * slice_width : (d + 1) * slice_width] = total

    def norm_rows(s):
        def block(i, carry):
            at = pl.ds(pl.multiple_of(i * rows, rows), rows)
            data = tok[s, at, :].astype(F32)
            scale = lax.rsqrt(jnp.mean(data * data, axis=-1, keepdims=True) + EPS)
            fnorm[at, :] = (data * scale * gain_rows[0:1, :]).astype(BF)
            return carry

        lax.fori_loop(0, depth, block, 0)

    own_misc.wait()
    for copy in misc_copies:
        copy.wait_recv()
    router_out[...] = jnp.zeros_like(router_out)
    row = lax.broadcasted_iota(jnp.int32, misc_ref.shape, 0)
    for d in range(dp):
        block = jnp.where(row <= experts, misc_all[d], 0.0).astype(BF)
        router_out[: misc_ref.shape[0], d * slice_width : (d + 1) * slice_width] = block
    bias_in = jnp.zeros(misc_ref.shape, F32)
    sub = lax.broadcasted_iota(jnp.int32, misc_ref.shape, 0)
    for d in range(dp):
        bias_in = jnp.where(sub == d, misc_all[d, pl.ds(experts + 1 + core, 1), :], bias_in)
    bias_in = bias_in.astype(BF)
    heads3 = 3 * pair
    head_slice = head // dp
    lane = lax.broadcasted_iota(jnp.int32, (bias_in.shape[1], heads3), 1)
    sub = lax.broadcasted_iota(jnp.int32, (bias_in.shape[1], heads3), 0)
    place = (lane // head * head_slice + lane % head_slice == sub).astype(F32).astype(BF)
    spread = dot(bias_in, place)
    lane = lax.broadcasted_iota(jnp.int32, spread.shape, 1)
    sub = lax.broadcasted_iota(jnp.int32, spread.shape, 0)
    bias = jnp.sum(jnp.where(lane % head // head_slice == sub, spread, 0.0), axis=0, keepdims=True)

    qk_copies[-1].wait_recv()
    vo_copies[-1].wait_recv()
    for m in far:
        for copy in m:
            copy.start()
    for copy in over_near:
        copy.start()
    pairs = pair // head

    def project(s):
        def block(i, carry):
            at = pl.ds(pl.multiple_of(i * 2 * rows, 2 * rows), 2 * rows)
            full = weights[...].reshape(width, 4 * pair)
            pre = dot(fnorm[at, :], full[:, : 3 * pair]) + bias
            cos_rows, sin_rows = cos_ref[at, :], sin_ref[at, :]
            for kind in range(3):
                for h in range(pairs):
                    a = (kind * pairs + h) * head
                    field = pre[:, a : a + head]
                    if kind < 2:
                        field = spin(field, cos_rows, sin_rows)
                    qkv_ref[kind, s * pairs + h, at, :] = field.astype(BF)
            return carry

        lax.fori_loop(0, depth // 2, block, 0)

    norm_rows(0)
    project(0)
    line_step(grad_line, 1)
    grad_beside.wait()
    far_grad_line.begin()
    for copy in far[0]:
        copy.wait_recv()
    over[0].start()
    tok_pass[0].wait()
    for copy, there in tok_passed:
        pl.when(there)(copy.wait)
    norm_rows(1)
    project(1)

    own_codes.wait()
    for copy in first:
        copy.wait()
    causal_block = seq_len // 2

    def attend(s):
        flags = codes_all[s]
        sub = lax.broadcasted_iota(jnp.int32, flags.shape, 0)
        flags = jnp.where(sub == 8, flags, 0).astype(F32).astype(BF)
        for h in range(pairs):
            for b in range(2):
                at = slice(b * causal_block, (b + 1) * causal_block)
                seen = dot(flags[:, at], flags, 0, 0)
                row = lax.broadcasted_iota(jnp.int32, seen.shape, 0) + b * causal_block
                col = lax.broadcasted_iota(jnp.int32, seen.shape, 1)
                scores = dot(qkv_ref[0, s * pairs + h, at, :], qkv_ref[1, s * pairs + h], 1, 1)
                scores = scores * head ** (-0.5)
                scores = jnp.where(jnp.logical_or(col <= row, seen > 0.5), scores, -1e30)
                raised = jnp.exp(scores - jnp.max(scores, axis=1, keepdims=True))
                probs = raised / jnp.sum(raised, axis=1, keepdims=True)
                probs = probs.astype(BF)
                probs_ref[s * pairs + h, at, :] = probs
                mixed = dot(probs, qkv_ref[2, s * pairs + h])
                mix_ref[s, at, h * head : (h + 1) * head] = mixed.astype(BF)

    def project_out(s):
        for d in range(dp):
            index = tuple(d // bit % 2 for bit in reversed(bits))
            block = weights[index + (slice(None), slice(3 * pair, 4 * pair))]
            at = slice(d * slice_width, (d + 1) * slice_width)
            part[s, :, at] = dot(mix_ref[s], block, 1, 1).astype(BF)

    attend(1)
    if depth > 2:
        line_step(grad_line, 2)
        line_step(far_grad_line, 1)
    project_out(1)
    part_pass = c.remote(part.at[1], part_in, dp=peer_of(me, 1))
    part_pass.start()
    attend(0)
    project_out(0)
    part_pass.wait_recv()

    saved = [
        c.local(a, b)
        for a, b in (
            (tok, tok_out),
            (weights, weights_out),
            (qkv_ref, qkv_out),
            (probs_ref, probs_out),
            (mix_ref, mix_out),
        )
    ]
    for copy in saved:
        copy.start()
    for k in range(3, depth):
        line_step(grad_line, k)
        line_step(far_grad_line, k - 1)
    x_grad = c.remote(grads_ref.at[0, :, grad_left], grads_ref.at[2, :, grad_left], dp=beside)
    x_grad.start()
    own_pass = c.remote(grads_ref.at[0], grads_ref.at[1], dp=peer_of(me, 1))
    own_pass.start()
    here_at = pl.ds(pl.multiple_of(z * rows, rows), rows)
    hidden_ref[...] = part[0, here_at, :].astype(F32) + part_in[here_at, :].astype(F32)
    hidden_ref[...] += tok[0, here_at, :].astype(F32)
    for r in range(depth):
        at = pl.ds(r * rows, rows)
        part[0, at, :] = (part[0, at, :].astype(F32) + part_in[at, :].astype(F32)).astype(BF)
    scatter = LineSum(c, part.at[0], scatter_in.at[0], scatter_in.at[1], z, depth, rows)
    scatter.run()
    for k in (1, 2):
        for copy in far[k]:
            copy.wait_recv()
        over[k].start()
    scatter.collect(hidden_ref)
    total = hidden_ref[...]
    scale = lax.rsqrt(jnp.mean(total * total, axis=-1, keepdims=True) + EPS)
    norm_mine[...] = (total * scale * gain_rows[1:2, :]).astype(BF)
    norm_here = c.local(norm_mine, piece(norm_ref.at[0], z))
    norm_here.start()
    norm_here.wait()
    norm_line = Line(c, norm_ref.at[0], z, depth, rows)
    norm_line.begin()
    cut = width * 12 // 16
    left, right = pl.ds(0, cut), pl.ds(cut, width - cut)
    norm_own = c.remote(piece(norm_ref.at[0], z), piece(norm_ref.at[1], z), dp=sibling)
    norm_far = c.remote(piece(norm_ref.at[0], z), piece(norm_ref.at[2], z), dp=beside)
    norm_far.start()
    norm_own.start()
    far_line = Line(c, norm_ref.at[2, :, right], z, depth, rows)
    norm_passed, far_passed = [], []
    pass_norm = pass_on(
        c, norm_ref.at[0], norm_ref.at[1], z, depth, rows, sibling, norm_passed
    )
    pass_far = pass_on(
        c, norm_ref.at[0, :, left], norm_ref.at[2, :, left], z, depth, rows, beside, far_passed
    )

    def pass_both(k, up):
        pass_far(k, up)
        pass_norm(k, up)

    line_step(norm_line, 1, pass_both)
    norm_far.wait()
    far_line.begin()
    for k in range(2, depth):
        line_step(norm_line, k, pass_both)
        line_step(far_line, k - 1)
    line_step(far_line, depth - 1)

    line_step(far_grad_line, depth - 1)
    x_grad.wait_recv()
    grad_pass = c.remote(grads_ref.at[2], grads_ref.at[3], dp=peer_of(me, 1))
    grad_pass.start()
    for copy in over_near + over + [copy for m in near for copy in m]:
        copy.wait()
    for copy, there in far_passed:
        pl.when(there)(copy.wait)
    norm_pass = c.remote(norm_ref.at[2], norm_ref.at[3], dp=sibling)
    norm_pass.start()
    norm_own.wait()
    for copy, there in norm_passed:
        pl.when(there)(copy.wait)
    norm_pass.wait()
    own_pass.wait()
    grad_pass.wait()
    for line in (tok_line, grad_line, far_grad_line, norm_line, far_line, scatter):
        line.finish()
    for copy in pads + saved:
        copy.wait()
    for copy in gain_copies + misc_copies + gain_spread + qk_copies + vo_copies:
        copy.wait_send()
    for copy in [part_pass, x_grad] + [y for m in far for y in m]:
        copy.wait_send()


def forward_call(dp, depth, experts, head, small, arrays, units):
    codes, misc, gains, cos_rows, sin_rows = small
    tokens, pair = arrays[0], arrays[2].shape[1] // 2
    rows, width = tokens.shape
    seq_len = rows * depth
    hidden_units = units[0].shape[1]
    hidden_pad = -(-hidden_units // 128) * 128
    routed = experts // 4
    bits = dp.bit_length() - 1
    pairs = pair // head
    vmem, hbm = pl.BlockSpec(memory_space=pltpu.VMEM), pl.BlockSpec(memory_space=pl.ANY)
    shape = jax.ShapeDtypeStruct
    return pl.pallas_call(
        functools.partial(forward_body, (dp, depth, experts, hidden_units, head)),
        in_specs=[vmem] * 5 + [hbm] * 12,
        out_specs=[vmem] + [hbm] * 4 + [vmem] * 3 + [hbm] * 5,
        out_shape=[
            shape((rows, width), F32),
            shape((4, seq_len, width), BF),
            shape((4, seq_len, width), BF),
            shape((routed + 1, 2, hidden_pad, width), BF),
            shape((routed + 1, 1, hidden_pad, width), BF),
            shape((4,) + codes.shape, codes.dtype),
            shape((128, width), BF),
            shape((8, width), F32),
            shape((2, seq_len, width), BF),
            shape((2,) * bits + (width // dp, 4 * pair), BF),
            shape((3, 2 * pairs, seq_len, head), BF),
            shape((2 * pairs, seq_len, seq_len), BF),
            shape((2, seq_len, pair), BF),
        ],
        scratch_shapes=[
            pltpu.VMEM((dp,) + misc.shape, F32),
            pltpu.VMEM((rows, width), BF),
            pltpu.VMEM((2, seq_len, width), BF),
            pltpu.VMEM((2,) * bits + (width // dp, 4 * pair), BF),
            pltpu.VMEM((3, 2 * pairs, seq_len, head), BF),
            pltpu.VMEM((2 * pairs, seq_len, seq_len), BF),
            pltpu.VMEM((2, seq_len, pair), BF),
            pltpu.VMEM((seq_len, width), BF),
            pltpu.VMEM((2, seq_len, width), BF),
            pltpu.VMEM((seq_len, width), BF),
            pltpu.VMEM((2, depth - 1, rows, width), BF),
            pltpu.VMEM((depth, dp) + gains.shape, F32),
            pltpu.VMEM((routed + 1, hidden_pad - hidden_units, width), BF),
            pltpu.VMEM((2, width // dp, 4 * hidden_units), BF),
            pltpu.VMEM((2, 4, hidden_units, width // dp), BF),
            pltpu.SemaphoreType.DMA((160,)),
            pltpu.SemaphoreType.DMA((160,)),
            pltpu.SemaphoreType.DMA((40,)),
        ],
        compiler_params=pltpu.CompilerParams(
            collective_id=0, has_side_effects=True, vmem_limit_bytes=VMEM_LIMIT
        ),
    )(codes, misc, gains, cos_rows, sin_rows, *arrays, *units)


def middle_body(
    sizes,
    hidden_ref,
    codes_ref,
    router_ref,
    rows_ref,
    grads_ref,
    gateup_ref,
    down_ref,
    output_ref,
    terms_out,
    probs_out,
    grad_own,
    grad_sib,
    grad_far,
    gate_total,
    up_total,
    down_total,
    gate_in,
    wide_w,
    down_w,
    xs,
    ys,
    pair,
    act,
    outs,
    backs,
    near_in,
    back_in,
    far_in,
    z_in,
    stage,
    weights,
    routed,
    probs,
    terms,
    terms_in,
    send,
    recv,
    here,
):
    dp, depth, experts, top_count, keep = sizes
    me, z = lax.axis_index("dp"), lax.axis_index("tensor")
    y = me // 4
    rows, width = output_ref.shape
    seq_len = rows * depth
    total = 2 * seq_len
    units, wide, _ = wide_w.shape
    half = wide // 2
    slice_width = width // dp
    sibling, beside, over = peer_of(me, 1), peer_of(me, 2), peer_of(me, 4)
    c = Copies(send, recv, here)

    greet(me, z, dp, depth)

    def load(source, chunk, target):
        copies = [
            c.local(source.at[2 * chunk + s], target.at[pl.ds(s * seq_len, seq_len)])
            for s in range(2)
        ]
        for copy in copies:
            copy.start()
        return copies

    def wait(copies):
        for copy in copies:
            copy.wait()

    loads = load(rows_ref, 1, xs)
    first = [(c.local(gateup_ref.at[u], wide_w.at[u]), c.local(down_ref.at[u], down_w.at[u])) for u in range(units)]
    first[0][0].start()
    first[0][1].start()
    loads += load(grads_ref, 1, ys)
    for u in range(1, units):
        first[u][0].start()
        first[u][1].start()

    block = seq_len // 2
    lanes = weights.shape[1]

    def gate_weights(chunk):
        def step(i, carry):
            at = pl.ds(pl.multiple_of(i * block, block), block)
            logits = dot(xs[at, :], router_ref[...], 1, 1)
            lane = lax.broadcasted_iota(jnp.int32, logits.shape, 1)
            chosen = jnp.where(lane < experts, logits, -1e30)
            raised = jnp.exp(chosen - jnp.max(chosen, axis=1, keepdims=True))
            soft = raised / jnp.sum(raised, axis=1, keepdims=True)
            probs[at, :] = jnp.where(lane < experts, soft, jax.nn.sigmoid(logits))
            return carry

        lax.fori_loop(0, total // block, step, 0)
        for s in range(2):
            codes = codes_ref[2 * chunk + s]
            row = lax.broadcasted_iota(jnp.int32, codes.shape, 0)
            named = row == experts
            for k in range(top_count):
                named = jnp.logical_or(named, codes[k : k + 1] == row)
            named = jnp.logical_and(named, row <= experts).astype(F32).astype(BF)
            place = (codes.shape[0], lanes)
            same = lax.broadcasted_iota(jnp.int32, place, 0) == lax.broadcasted_iota(
                jnp.int32, place, 1
            )
            routed[s * seq_len : (s + 1) * seq_len] = dot(named, same.astype(F32).astype(BF), 0, 0)
        weights[...] = probs[...] * routed[...]

    def activate(chunk):
        for u in range(units):
            if chunk == 1:
                wait(first[u])
            if u == 0:
                gate_weights(chunk)
            place = me % 4 * (units - 1) + u if u < units - 1 else experts

            def step(i, carry, u=u, place=place):
                at = pl.ds(pl.multiple_of(i * block, block), block)
                mine = lax.broadcasted_iota(jnp.int32, (block, lanes), 1) == place
                weight = jnp.sum(jnp.where(mine, weights[at, :], 0.0), axis=1, keepdims=True)
                both = dot(xs[at, :], wide_w[u], 1, 1)
                cot = dot(ys[at, :], down_w[u], 1, 1)
                gate_act, gate_slope = silu_parts(both[:, :half])
                value = gate_act * both[:, half:]
                inner = jnp.sum(value * cot, axis=1, keepdims=True)
                inner = jnp.where(mine, inner * routed[at, :], 0.0)
                terms[chunk, at, :] = inner if u == 0 else terms[chunk, at, :] + inner
                cot = cot * weight
                act[chunk, at, u * half : (u + 1) * half] = (value * weight).astype(BF)
                a = u * wide
                pair[chunk, at, a : a + half] = (cot * both[:, half:] * gate_slope).astype(BF)
                pair[chunk, at, a + half : a + wide] = (cot * gate_act).astype(BF)
                return carry

            lax.fori_loop(0, total // block, step, 0)

    cols = 512

    def back(left, chunk, s, weight, target):
        at = slice(s * seq_len, (s + 1) * seq_len)
        for j in range(width // cols):
            part = weight[:, :, j * cols : (j + 1) * cols]
            part = part.reshape(-1, cols)
            target[:, j * cols : (j + 1) * cols] = dot(left[chunk, at, :], part).astype(BF)

    def add_into(target, other):
        def step(i, carry):
            at = pl.ds(pl.multiple_of(i * rows, rows), rows)
            target[at, :] = (target[at, :].astype(F32) + other[at, :].astype(F32)).astype(BF)
            return carry

        lax.fori_loop(0, depth, step, 0)

    wait(loads)
    activate(1)
    loads = load(rows_ref, 0, xs) + load(grads_ref, 0, ys)
    terms_near = c.remote(terms.at[1, pl.ds(seq_len, seq_len)], terms_in, dp=sibling)
    terms_near.start()
    back(act, 1, 1, down_w, outs.at[1])
    out_near = c.remote(outs.at[1], near_in, dp=sibling)
    out_near.start()
    back(act, 1, 0, down_w, outs.at[0])
    terms_near.wait()
    terms[1, :seq_len] = terms[1, :seq_len] + terms_in[...]
    terms_across = c.remote(terms.at[1, pl.ds(0, seq_len)], terms_out.at[2], dp=beside)
    terms_across.start()
    out_near.wait()
    add_into(outs.at[0], near_in)
    out_across = c.remote(outs.at[0], far_in, dp=beside)
    out_across.start()
    back(pair, 1, 1, wide_w, outs.at[1])
    grad_near = c.remote(outs.at[1], back_in, dp=sibling)
    grad_near.start()
    back(pair, 1, 0, wide_w, backs)
    grad_near.wait()
    add_into(backs, back_in)
    grad_across = c.remote(backs, grad_far, dp=beside)
    grad_across.start()

    wait(loads)
    activate(0)
    probs_out[...] = probs[pl.ds(pl.multiple_of(z * rows, rows), rows), :]
    loads = load(rows_ref, 1, ys)
    terms_out[0] = terms[0, :seq_len]
    terms_last = c.remote(terms.at[0, pl.ds(seq_len, seq_len)], terms_out.at[1], dp=sibling)
    terms_last.start()
    back(act, 0, 1, down_w, outs.at[1])
    out_last = c.remote(outs.at[1], near_in, dp=sibling)
    out_last.start()
    back(act, 0, 0, down_w, back_in)

    staged, moved = [None, None], []
    blocks = stage.shape[2]

    def outer(left, parts, targets, u, j, slot):
        at = slice(j * blocks * slice_width, (j + 1) * blocks * slice_width)
        n = parts * half
        value = dot(left[0, :, u * n : (u + 1) * n], xs[:, at], 0, 0)
        value = (value + dot(left[1, :, u * n : (u + 1) * n], ys[:, at], 0, 0)).astype(BF)
        if staged[slot] is not None:
            wait(staged[slot])
        copies = []
        for k, target in enumerate(targets):
            for b in range(blocks):
                stage[slot, k, b] = value[
                    k * half : k * half + keep, b * slice_width : (b + 1) * slice_width
                ]
            copies.append(c.local(stage.at[slot, k], target.at[pl.ds(j * blocks, blocks), u]))
            copies[-1].start()
        staged[slot] = copies

    wait(loads)
    steps = dp // blocks
    scatter = []
    over_copies = []
    for u in range(units):
        for j in range(steps):
            outer(pair, 2, (gate_total, up_total), u, j, j % 2)
        if u == 0:
            out_last.wait()
            out_across.wait()
            for r in list(range(1, depth)) + [0]:
                at = pl.ds(pl.multiple_of((z + r) % depth * rows, rows), rows)
                part = back_in[at, :].astype(F32) + near_in[at, :].astype(F32)
                part = part + far_in[at, :].astype(F32)
                if r:
                    back_in[at, :] = part.astype(BF)
                    copy = c.remote(back_in.at[at], z_in.at[r - 1], tensor=(z + r) % depth)
                    copy.start()
                    scatter.append(copy)
                else:
                    near_in[at, :] = part.astype(BF)
        for slot in range(2):
            wait(staged[slot])
            staged[slot] = None
        source = gate_total.at[pl.ds((1 - y) * 4, 4), u]
        over_copies.append(c.remote(source, gate_in.at[:, u], dp=over))
        over_copies[-1].start()
    loads = load(grads_ref, 0, xs) + load(grads_ref, 1, ys)

    back(pair, 0, 1, wide_w, outs.at[1])
    grad_last = c.remote(outs.at[1], grad_sib, dp=sibling)
    grad_last.start()
    back(pair, 0, 0, wide_w, outs.at[0])
    grad_here = c.local(outs.at[0], grad_own)
    grad_here.start()
    wait(loads)
    for u in range(units):
        for j in range(steps):
            outer(act, 1, (down_total,), u, j, j % 2)
    for copy in scatter:
        copy.wait_recv()
    value = near_in[pl.ds(pl.multiple_of(z * rows, rows), rows), :].astype(F32)
    value = value + hidden_ref[...]
    for r in range(1, depth):
        value = value + z_in[r - 1].astype(F32)
    output_ref[...] = value.astype(BF)
    for slot in range(2):
        wait(staged[slot])
    for copy in scatter:
        copy.wait_send()
    wait([grad_here, grad_last, terms_last, terms_across, grad_across] + over_copies)


def middle_call(dp, depth, experts, top_count, hidden_units, hidden, codes, router, arrays):
    rows, width = hidden.shape
    seq_len = rows * depth
    norm, grads, gateup, down = arrays
    units, wide, _ = gateup.shape
    half = wide // 2
    slice_width = width // dp
    blocks = max(1, 1024 // slice_width)
    vmem, hbm = pl.BlockSpec(memory_space=pltpu.VMEM), pl.BlockSpec(memory_space=pl.ANY)
    shape = jax.ShapeDtypeStruct
    total = shape((dp, units, hidden_units, slice_width), BF)
    return pl.pallas_call(
        functools.partial(middle_body, (dp, depth, experts, top_count, hidden_units)),
        in_specs=[vmem] * 3 + [hbm] * 4,
        out_specs=[vmem] * 3 + [hbm] * 7,
        out_shape=[
            shape((rows, width), BF),
            shape((3, seq_len, 128), F32),
            shape((rows, 128), F32),
            shape((seq_len, width), BF),
            shape((seq_len, width), BF),
            shape((seq_len, width), BF),
            total,
            total,
            total,
            shape((4, units, hidden_units, slice_width), BF),
        ],
        scratch_shapes=[
            pltpu.VMEM((units, wide, width), BF),
            pltpu.VMEM((units, half, width), BF),
            pltpu.VMEM((2 * seq_len, width), BF),
            pltpu.VMEM((2 * seq_len, width), BF),
            pltpu.VMEM((2, 2 * seq_len, units * wide), BF),
            pltpu.VMEM((2, 2 * seq_len, units * half), BF),
            pltpu.VMEM((2, seq_len, width), BF),
            pltpu.VMEM((seq_len, width), BF),
            pltpu.VMEM((seq_len, width), BF),
            pltpu.VMEM((seq_len, width), BF),
            pltpu.VMEM((seq_len, width), BF),
            pltpu.VMEM((depth - 1, rows, width), BF),
            pltpu.VMEM((2, 2, blocks, hidden_units, slice_width), BF),
            pltpu.VMEM((2 * seq_len, 128), F32),
            pltpu.VMEM((2 * seq_len, 128), F32),
            pltpu.VMEM((2 * seq_len, 128), F32),
            pltpu.VMEM((2, 2 * seq_len, 128), F32),
            pltpu.VMEM((seq_len, 128), F32),
            pltpu.SemaphoreType.DMA((32,)),
            pltpu.SemaphoreType.DMA((32,)),
            pltpu.SemaphoreType.DMA((64,)),
        ],
        compiler_params=pltpu.CompilerParams(
            collective_id=2, has_side_effects=True, vmem_limit_bytes=63 * 2**20
        ),
    )(hidden, codes, router, norm, grads, gateup, down)


class LineSum:
    def __init__(self, c, data, ups, downs, z, depth, rows):
        self.data, self.ups, self.downs = data, ups, downs
        self.z, self.depth, self.rows = z, depth, rows
        self.up_copies = [
            c.remote(self.piece(t), ups.at[t - 1], tensor=z + 1) for t in range(1, depth)
        ]
        self.down_copies = [
            c.remote(self.piece(t), downs.at[t], tensor=z - 1) for t in range(depth - 1)
        ]

    def piece(self, t):
        return self.data.at[pl.ds(t * self.rows, self.rows)]

    def add(self, t, other):
        at = pl.ds(t * self.rows, self.rows)
        self.data[at, :] = (self.data[at, :].astype(F32) + other.astype(F32)).astype(BF)

    def up(self, t):
        copy = self.up_copies[t - 1]

        @pl.when(self.z < t)
        def _():
            @pl.when(self.z > 0)
            def _():
                copy.wait_recv()
                self.add(t, self.ups[t - 1])

            copy.start()

    def down(self, t):
        copy = self.down_copies[t]

        @pl.when(self.z > t)
        def _():
            @pl.when(self.z < self.depth - 1)
            def _():
                copy.wait_recv()
                self.add(t, self.downs[t])

            copy.start()

    def begin(self):
        top = self.depth - 1

        @pl.when(self.z == 0)
        def _():
            for k in range(top):
                self.up_copies[top - k - 1].start()

        @pl.when(self.z == top)
        def _():
            for k in range(top):
                self.down_copies[k].start()

    def step(self, k):
        top = self.depth - 1

        @pl.when(jnp.logical_and(self.z > 0, self.z < self.depth // 2))
        def _():
            self.up(top - k)
            self.down(k)

        @pl.when(jnp.logical_and(self.z >= self.depth // 2, self.z < top))
        def _():
            self.down(k)
            self.up(top - k)

    def run(self):
        self.begin()
        for k in range(self.depth - 1):
            self.step(k)

    def collect(self, total_ref):
        for t in range(self.depth):

            @pl.when(self.z == t)
            def _(t=t):
                if t > 0:
                    self.up_copies[t - 1].wait_recv()
                    total_ref[...] += self.ups[t - 1].astype(F32)
                if t < self.depth - 1:
                    self.down_copies[t].wait_recv()
                    total_ref[...] += self.downs[t].astype(F32)

    def finish(self):
        for t in range(1, self.depth):
            pl.when(self.z < t)(self.up_copies[t - 1].wait_send)
        for t in range(self.depth - 1):
            pl.when(self.z > t)(self.down_copies[t].wait_send)


def backward_body(
    sizes,
    terms_ref,
    probs_mine_ref,
    router_ref,
    gain_rows,
    cos_ref,
    sin_ref,
    hidden_ref,
    outgrad_ref,
    grad_a_ref,
    grad_b_ref,
    grad_c_ref,
    gate_in_ref,
    gate_ref,
    up_ref,
    down_ref,
    tok_hbm,
    weights_hbm,
    qkv_hbm,
    probs_hbm,
    mix_hbm,
    norm_hbm,
    input_ref,
    gate_out,
    up_out,
    down_out,
    attn_out,
    misc_out,
    gains_out,
    own_sum,
    arrived,
    three,
    scatter_in,
    terms_sum,
    terms_in,
    back,
    tok,
    weights,
    qkv,
    probs_ref,
    mix_ref,
    scales,
    qkv_grad,
    part_in,
    keep,
    total_a,
    first_qk,
    first_vo,
    second_in,
    misc_part,
    misc_in,
    gains_in,
    vectors,
    send,
    recv,
    here,
):
    dp, depth, experts, head = sizes
    me, z = lax.axis_index("dp"), lax.axis_index("tensor")
    core, x, y = me % 2, (me // 2) % 2, me // 4
    rows, width = input_ref.shape
    seq_len = rows * depth
    slice_width = width // dp
    pair = mix_ref.shape[2]
    pairs = pair // head
    bits = [1, 2, 4]
    c = Copies(send, recv, here)

    greet(me, z, dp, depth)

    matrices = ((gate_ref, gate_out), (up_ref, up_out), (down_ref, down_out))
    over = [None]
    for m in (1, 2):
        other = matrices[m][0].at[pl.ds((1 - y) * 4, 4)]
        over.append(c.remote(other, arrived.at[m], dp=peer_of(me, 4)))
        over[m].start()
    gate_in = c.local(gate_in_ref, arrived.at[0])
    grads = (grad_a_ref, grad_b_ref, grad_c_ref)
    loads = [c.local(grads[k], three.at[k]) for k in range(3)]
    for copy in loads:
        copy.start()
    own_loads = [
        c.local(source.at[pl.ds(y * 4, 4)], own_sum) for source, _ in matrices
    ]
    inputs = [
        c.local(a, b)
        for a, b in (
            (weights_hbm, weights),
            (mix_hbm, mix_ref),
            (qkv_hbm, qkv),
            (probs_hbm, probs_ref),
            (tok_hbm, tok),
        )
    ]
    own_loads[0].start()
    gate_in.start()
    for copy in inputs:
        copy.start()

    def at_of(p):
        return pl.ds(pl.multiple_of(p * rows, rows), rows)

    for copy in loads:
        copy.wait()
    small = []
    for r in range(depth):
        at = at_of((z + r) % depth)
        total = three[0, at, :].astype(F32) + three[1, at, :].astype(F32)
        total = total + three[2, at, :].astype(F32)
        three[0, at, :] = total.astype(BF)
        extra = terms_ref[0, at, :] + terms_ref[1, at, :] + terms_ref[2, at, :]
        terms_sum[at, :] = extra
        if r:
            copy = c.remote(terms_sum.at[at], terms_in.at[r - 1], tensor=(z + r) % depth)
            copy.start()
            small.append(copy)
        else:
            keep[0] = total
    scatter = LineSum(c, three.at[0], scatter_in.at[0, 0], scatter_in.at[0, 1], z, depth, rows)
    scatter.run()

    def add_over(m):
        own_loads[m].wait()
        if m:
            over[m].wait_recv()
        else:
            gate_in.wait()
        copies = []
        for r in (2, 3, 1, 0):
            k = peer_of(me, r) % 4
            for unit in range(own_sum.shape[1]):
                arrived[m, k, unit] = (
                    own_sum[k, unit].astype(F32) + arrived[m, k, unit].astype(F32)
                ).astype(BF)
            place = matrices[m][1].at[me % 4]
            if r:
                copies.append(c.remote(arrived.at[m, k], place, dp=peer_of(me, r)))
            else:
                copies.append(c.local(arrived.at[m, k], place))
            copies[-1].start()
        if m + 1 < len(own_loads):
            own_loads[m + 1].start()
        return copies

    units = add_over(0)
    for copy in small:
        copy.wait_recv()
    route = terms_sum[at_of(z), :]
    for r in range(1, depth):
        route = route + terms_in[r - 1]
    scatter.collect(keep.at[0])
    grad = keep[0]
    probs_mine = probs_mine_ref[...]
    lane = lax.broadcasted_iota(jnp.int32, route.shape, 1)
    inner = jnp.sum(jnp.where(lane < experts, probs_mine * route, 0.0), axis=1, keepdims=True)
    logits = jnp.where(
        lane < experts,
        probs_mine * (route - inner),
        jnp.where(lane == experts, route * probs_mine * (1.0 - probs_mine), 0.0),
    ).astype(BF)
    grad = grad + dot(logits, router_ref[...])
    hidden = hidden_ref[...]
    scale = lax.rsqrt(jnp.mean(hidden * hidden, axis=-1, keepdims=True) + EPS)
    unit = hidden * scale
    vectors[1:2, :] = jnp.sum(grad * unit, axis=0, keepdims=True)
    grad = grad * gain_rows[1:2, :]
    grad = outgrad_ref[...].astype(F32) + scale * (
        grad - unit * jnp.mean(grad * unit, axis=-1, keepdims=True)
    )
    keep[0] = grad
    back[0, at_of(z), :width] = grad.astype(BF)
    back[0, at_of(z), width:] = logits

    line = Line(c, back.at[0], z, depth, rows)
    line.begin()
    sibling = peer_of(me, 1)
    back_own = c.remote(piece_of(back.at[0], z, rows), piece_of(back.at[1], z, rows), dp=sibling)
    back_own.start()
    passed = []
    pass_back = pass_on(c, back.at[0], back.at[1], z, depth, rows, sibling, passed)
    line_step(line, 1, pass_back)

    for copy in inputs:
        copy.wait()

    def scale_rows(i, carry):
        at = at_of(i)
        for s in range(2):
            data = tok[s, at, :].astype(F32)
            scales[s, at, :] = lax.rsqrt(jnp.mean(data * data, axis=-1, keepdims=True) + EPS)
        return carry

    lax.fori_loop(0, depth, scale_rows, 0)
    units += add_over(1)
    line_step(line, 2, pass_back)
    line_step(line, 3, pass_back)
    back_own.wait()
    for copy, there in passed:
        pl.when(there)(copy.wait)
    def block_of(d):
        return tuple(d // bit % 2 for bit in reversed(bits))

    def slab(d):
        return slice(d * slice_width, (d + 1) * slice_width)

    def attention(s):
        mixed = jnp.zeros((seq_len, pair), F32)
        for d in range(dp):
            block = weights[block_of(d) + (slice(None), slice(3 * pair, 4 * pair))]
            mixed = mixed + dot(back[s, :, slab(d)], block)
        mixed = mixed.astype(BF)
        for h in range(pairs):
            n = s * pairs + h
            cot = mixed[:, h * head : (h + 1) * head]
            key_total = jnp.zeros((seq_len, head), F32)
            value_total = jnp.zeros((seq_len, head), F32)
            for b in range(2):
                at = slice(b * seq_len // 2, (b + 1) * seq_len // 2)
                p_low = probs_ref[n, at, :]
                p = p_low.astype(F32)
                p_grad = dot(cot[at], qkv[2, n], 1, 1)
                s_grad = p * (p_grad - jnp.sum(p * p_grad, axis=1, keepdims=True))
                s_grad = s_grad.astype(BF)
                q_grad = dot(s_grad, qkv[1, n]) * head ** (-0.5)
                q_grad = spin(q_grad, cos_ref[at, :], -sin_ref[at, :])
                qkv_grad[s, at, h * head : (h + 1) * head] = q_grad.astype(BF)
                key_total = key_total + dot(s_grad, qkv[0, n, at, :], 0, 0)
                value_total = value_total + dot(p_low, cot[at], 0, 0)
            k_grad = spin(key_total * head ** (-0.5), cos_ref[...], -sin_ref[...])
            a = pair + h * head
            qkv_grad[s, :, a : a + head] = k_grad.astype(BF)
            qkv_grad[s, :, a + pair : a + pair + head] = value_total.astype(BF)

    def first_grad(s):
        for d in range(dp):
            block = weights[block_of(d) + (slice(None), slice(0, 3 * pair))]
            total = dot(qkv_grad[s], block, 1, 1)
            three[1 + s, :, slab(d)] = total.astype(BF)
            unit_block = tok[s, :, slab(d)].astype(F32) * scales[s]
            row = jnp.sum(total * unit_block, axis=0, keepdims=True)
            vectors[2 + s : 3 + s, slab(d)] = row

    units += add_over(2)
    attention(1)
    first_grad(1)
    part_pass = c.remote(three.at[2], part_in, dp=sibling)
    part_pass.start()
    attention(0)
    first_grad(0)
    part_pass.wait_recv()
    keep[1] = three[1, at_of(z), :].astype(F32) + part_in[at_of(z), :].astype(F32)
    for r in range(depth):
        at = at_of(r)
        three[1, at, :] = (three[1, at, :].astype(F32) + part_in[at, :].astype(F32)).astype(BF)
    first_scatter = LineSum(
        c, three.at[1], scatter_in.at[1, 0], scatter_in.at[1, 1], z, depth, rows
    )
    first_scatter.begin()

    for d in range(dp):
        total = jnp.zeros((slice_width, 3 * pair), F32)
        out_total = jnp.zeros((slice_width, pair), F32)
        for s in range(2):
            data = tok[s, :, slab(d)].astype(F32) * scales[s] * gain_rows[0:1, slab(d)]
            total = total + dot(data.astype(BF), qkv_grad[s], 0, 0)
            out_total = out_total + dot(back[s, :, slab(d)], mix_ref[s], 0, 0)
        total_a[block_of(d) + (slice(None), slice(0, 3 * pair))] = total.astype(BF)
        total_a[block_of(d) + (slice(None), slice(3 * pair, 4 * pair))] = out_total.astype(BF)

    half = 2 * pair

    def index(y_at, x_at, k):
        return (y_at, x_at, slice(None), slice(None), pl.ds(k * half, half))

    every = pl.ds(0, 2)
    qk_first = c.remote(
        total_a.at[index(pl.ds(1 - y, 1), every, 0)], first_qk, dp=peer_of(me, 4)
    )
    vo_first = c.remote(
        total_a.at[index(every, pl.ds(1 - x, 1), 1)], first_vo, dp=peer_of(me, 2)
    )
    qk_first.start()
    vo_first.start()
    first_scatter.step(0)

    scatter.finish()
    norm_load = c.local(norm_hbm.at[0], three.at[0])
    norm_load.start()
    norm_load.wait()
    router_part = dot(back[0, :, width:], three[0], 0, 0)
    ones = jnp.ones((16, seq_len), BF)
    bias_row = dot(ones, qkv_grad[0]) + dot(ones, qkv_grad[1])
    lane = lax.broadcasted_iota(jnp.int32, bias_row.shape, 1)
    sub = lax.broadcasted_iota(jnp.int32, bias_row.shape, 0)
    head_slice = head // dp
    bias_rows = jnp.where(lane % head // head_slice == sub, bias_row, 0.0)
    high = bias_rows.astype(BF)
    low = (bias_rows - high.astype(F32)).astype(BF)
    lane = lax.broadcasted_iota(jnp.int32, (3 * pair, slice_width), 1)
    sub = lax.broadcasted_iota(jnp.int32, (3 * pair, slice_width), 0)
    place = (sub // head * head_slice + sub % head_slice == lane).astype(F32).astype(BF)
    bias_rows = dot(high, place) + dot(low, place)
    sub = lax.broadcasted_iota(jnp.int32, (16, slice_width), 0)
    misc_copies = []
    for d in range(dp):
        tile = jnp.where(sub <= experts, router_part[:16, slab(d)], 0.0)
        tile = jnp.where(sub == experts + 1 + core, bias_rows[d : d + 1], tile)
        gain_one = vectors[2:3, slab(d)] + vectors[3:4, slab(d)]
        tile = jnp.where(sub == experts + 3, gain_one, tile)
        tile = jnp.where(sub == experts + 4, vectors[1:2, slab(d)], tile)
        misc_part[d] = tile
    for r in range(1, dp):
        to = peer_of(me, r)
        misc_copies.append(c.remote(misc_part.at[to], misc_in.at[r - 1], dp=to))
        misc_copies[-1].start()

    for k in range(1, depth - 1):
        first_scatter.step(k)
    qk_first.wait()
    mine = index(pl.ds(y, 1), every, 0)
    total_a[mine] = (total_a[mine].astype(F32) + first_qk[...].astype(F32)).astype(BF)
    qk_second = c.remote(
        total_a.at[index(pl.ds(y, 1), pl.ds(1 - x, 1), 0)], second_in.at[0], dp=peer_of(me, 2)
    )
    qk_second.start()
    vo_first.wait()
    mine = index(every, pl.ds(x, 1), 1)
    total_a[mine] = (total_a[mine].astype(F32) + first_vo[...].astype(F32)).astype(BF)
    vo_second = c.remote(
        total_a.at[index(pl.ds(1 - y, 1), pl.ds(x, 1), 1)], second_in.at[1], dp=peer_of(me, 4)
    )
    vo_second.start()

    total = misc_part[me]
    for r, copy in enumerate(misc_copies):
        copy.wait_recv()
        total = total + misc_in[r]
    misc_out[...] = total
    gain_copies = []
    for r in range(1, depth):
        peer = (z + r) % depth
        gain_copies.append(c.remote(misc_out.at[8:16], gains_in.at[r - 1], tensor=peer))
        gain_copies[-1].start()

    finals = []
    for k, copy in enumerate((qk_second, vo_second)):
        copy.wait()
        mine = (y, x, slice(None), slice(None), pl.ds(k * half, half))
        total_a[mine] = (
            total_a[mine].astype(F32) + second_in[k, 0, 0].astype(F32)
        ).astype(BF)
        for other in (True, False):
            to = 1 - core if other else core
            source = total_a.at[y, x, to, :, pl.ds(k * half, half)]
            place = attn_out.at[core, :, pl.ds(k * half, half)]
            finals.append(c.remote(source, place, dp=sibling) if other else c.local(source, place))
            finals[-1].start()

    first_scatter.collect(keep.at[1])
    total = keep[1]
    total = total * gain_rows[0:1, :]
    scale = scales[0, at_of(z), :]
    unit = tok[0, at_of(z), :].astype(F32) * scale
    total = keep[0] + scale * (total - unit * jnp.mean(total * unit, axis=-1, keepdims=True))
    input_ref[...] = total.astype(BF)

    total = misc_out[8:16, :]
    for r, copy in enumerate(gain_copies):
        copy.wait()
        total = total + gains_in[r]
    gains_out[...] = total
    for copy in finals + units:
        copy.wait()
    line.finish()
    first_scatter.finish()
    for copy in over[1:] + small + misc_copies + [part_pass]:
        copy.wait_send()


def backward_call(dp, depth, experts, head, in_vmem, in_hbm):
    output_rows, width = in_vmem[6].shape
    seq_len = output_rows * depth
    slice_width = width // dp
    units = in_hbm[3].shape[1:]
    pair = in_hbm[11].shape[2]
    pairs = pair // head
    vmem, hbm = pl.BlockSpec(memory_space=pltpu.VMEM), pl.BlockSpec(memory_space=pl.ANY)
    shape = jax.ShapeDtypeStruct
    final = shape((4,) + units, BF)
    return pl.pallas_call(
        functools.partial(backward_body, (dp, depth, experts, head)),
        in_specs=[vmem] * len(in_vmem) + [hbm] * len(in_hbm),
        out_specs=[vmem, hbm, hbm, hbm, vmem, vmem, vmem],
        out_shape=[
            shape((output_rows, width), BF),
            final,
            final,
            final,
            shape((2, slice_width, 4 * pair), BF),
            shape((16, slice_width), F32),
            shape((8, slice_width), F32),
        ],
        scratch_shapes=[
            pltpu.VMEM((4,) + units, BF),
            pltpu.VMEM((3, 4) + units, BF),
            pltpu.VMEM((3, seq_len, width), BF),
            pltpu.VMEM((2, 2, depth - 1, output_rows, width), BF),
            pltpu.VMEM((seq_len, 128), F32),
            pltpu.VMEM((depth - 1, output_rows, 128), F32),
            pltpu.VMEM((2, seq_len, width + 128), BF),
            pltpu.VMEM((2, seq_len, width), BF),
            pltpu.VMEM((2, 2, 2, slice_width, 4 * pair), BF),
            pltpu.VMEM((3, 2 * pairs, seq_len, head), BF),
            pltpu.VMEM((2 * pairs, seq_len, seq_len), BF),
            pltpu.VMEM((2, seq_len, pair), BF),
            pltpu.VMEM((2, seq_len, 1), F32),
            pltpu.VMEM((2, seq_len, 3 * pair), BF),
            pltpu.VMEM((seq_len, width), BF),
            pltpu.VMEM((2, output_rows, width), F32),
            pltpu.VMEM((2, 2, 2, slice_width, 4 * pair), BF),
            pltpu.VMEM((1, 2, 2, slice_width, 2 * pair), BF),
            pltpu.VMEM((2, 1, 2, slice_width, 2 * pair), BF),
            pltpu.VMEM((2, 1, 1, 2, slice_width, 2 * pair), BF),
            pltpu.VMEM((dp, 16, slice_width), F32),
            pltpu.VMEM((dp - 1, 16, slice_width), F32),
            pltpu.VMEM((depth - 1, 8, slice_width), F32),
            pltpu.VMEM((8, width), F32),
            pltpu.SemaphoreType.DMA((96,)),
            pltpu.SemaphoreType.DMA((96,)),
            pltpu.SemaphoreType.DMA((40,)),
        ],
        compiler_params=pltpu.CompilerParams(
            collective_id=1, has_side_effects=True, vmem_limit_bytes=62 * 2**20
        ),
    )(*in_vmem, *in_hbm)


def finish_body(
    gate_ref, up_ref, down_ref, attn_ref, eg_ref, eu_ref, ed_ref, sg_ref, su_ref, sd_ref,
    q_ref, k_ref, v_ref, o_ref, sg_rows, su_rows
):
    group, groups = pl.program_id(0), pl.num_programs(0)
    many, rows, _ = eg_ref.shape
    for source, routed, shared in (
        (gate_ref, eg_ref, sg_rows.at[group]),
        (up_ref, eu_ref, su_rows.at[group]),
        (down_ref, ed_ref, sd_ref),
    ):
        for unit in range(many):
            routed[unit] = source[0, unit].astype(F32)
        shared[...] = source[0, many].astype(F32)

    @pl.when(group == 0)
    def _():
        pair = attn_ref.shape[2] // 4
        for c in range(2):
            at = slice(c * pair, (c + 1) * pair)
            for kind, out_ref in enumerate((q_ref, k_ref, v_ref)):
                out_ref[:, at] = attn_ref[c, :, kind * pair : (kind + 1) * pair].astype(F32)
            o_ref[at, :] = jnp.transpose(attn_ref[c, :, 3 * pair :].astype(F32))

    @pl.when(group == groups - 1)
    def _():
        for source, out_ref in ((sg_rows, sg_ref), (su_rows, su_ref)):
            out_ref[...] = jnp.transpose(source[...].reshape(groups * rows, -1))


def finish_call(gate, up, down, attn):
    groups, units, rows, slice_width = gate.shape
    many, pair = units - 1, attn.shape[2] // 4
    shape = jax.ShapeDtypeStruct

    def whole(*dims):
        return pl.BlockSpec(dims, lambda g: (0,) * len(dims))

    source = pl.BlockSpec((1, units, rows, slice_width), lambda g: (g, 0, 0, 0))
    routed = pl.BlockSpec((many, rows, slice_width), lambda g: (g, 0, 0))
    return call(
        finish_body,
        (groups,),
        [source] * 3 + [whole(*attn.shape)],
        [routed] * 3
        + [whole(slice_width, groups * rows)] * 2
        + [pl.BlockSpec((rows, slice_width), lambda g: (g, 0))]
        + [whole(slice_width, 2 * pair)] * 3
        + [whole(2 * pair, slice_width)],
        [shape((groups * many, rows, slice_width), F32)] * 3
        + [shape((slice_width, groups * rows), F32)] * 2
        + [shape((groups * rows, slice_width), F32)]
        + [shape((slice_width, 2 * pair), F32)] * 3
        + [shape((2 * pair, slice_width), F32)],
        0,
        groups * units * rows * slice_width * 18,
        [pltpu.VMEM((groups, rows, slice_width), F32)] * 2,
    )(gate, up, down, attn)


def local_plain(
    dp,
    tokens,
    picture_ids,
    routes,
    slot_order,
    norm_gains,
    w_query,
    w_key,
    w_value,
    w_out,
    qkv_bias,
    router,
    shared_gate,
    shared_up,
    shared_down,
    expert_gate,
    expert_up,
    expert_down,
    out_grad,
):
    seq_len = picture_ids.shape[0]
    local_rows = tokens.shape[0]
    width = tokens.shape[1]
    experts, slice_width, hidden_units = expert_gate.shape
    top_count = routes.shape[1]
    capacity = 5 * seq_len * top_count // (4 * experts)
    heads_local = qkv_bias.shape[1]
    head_width = w_query.shape[1] // heads_local
    pair_heads = heads_local // 2
    pair_width = pair_heads * head_width
    mine_experts = experts // 4
    hidden_pad = -(-hidden_units // 128) * 128

    me = lax.axis_index("dp")
    zi = lax.axis_index("tensor")
    core, xi = me % 2, (me // 2) % 2
    group = me % 4
    bits = []
    while 2 ** (len(bits) + 1) <= dp:
        bits.append(2 ** len(bits))
    upper = bits[2:]

    def swap(array, bit):
        return lax.ppermute(array, "dp", [(i, i ^ bit) for i in range(dp)])

    def bit_of(bit):
        return (me // bit) % 2

    def join(mine, theirs, bit, axis):
        n = mine.shape[axis]
        shape = list(mine.shape)
        shape[axis] = 2 * n
        out = jnp.zeros(shape, mine.dtype)
        out = lax.dynamic_update_slice_in_dim(out, mine, n * bit_of(bit), axis)
        return lax.dynamic_update_slice_in_dim(out, theirs, n * (1 - bit_of(bit)), axis)

    def half(array, which, axis):
        n = array.shape[axis] // 2
        return lax.dynamic_slice_in_dim(array, which * n, n, axis)

    gains_z = lax.all_gather(norm_gains, "tensor", axis=1, tiled=True)
    misc_rows = 16
    bias_width = 3 * pair_heads * qkv_bias.shape[2]
    bias_cores = qkv_bias.reshape(3, 2, -1).swapaxes(0, 1).reshape(2, bias_width)

    def misc_pack(core_bias):
        wide = jnp.zeros((misc_rows, 2 * pair_width), BF)
        wide = wide.at[: experts + 1, :slice_width].set(router.T)
        wide = wide.at[experts + 1, :bias_width].set(core_bias)
        return wide.at[experts + 2 : experts + 4, :slice_width].set(gains_z)

    qk = jnp.concatenate(
        [w.reshape(slice_width, 2, pair_width) for w in (w_query, w_key)], axis=2
    )
    qk = jnp.concatenate(
        [qk, jnp.stack([misc_pack(bias_cores[0]), misc_pack(bias_cores[1])], axis=1)], axis=0
    )
    vo = jnp.concatenate(
        [w.reshape(slice_width, 2, pair_width) for w in (w_value, w_out.T)], axis=2
    )
    tokens_z = lax.all_gather(tokens, "tensor", axis=0, tiled=True)

    def gather_attention(pack, order):
        dims = (1,) * len(bits[1:])
        both = join(pick(pack, core, 1)[None], swap(pick(pack, 1 - core, 1), 1)[None], 1, 0)
        both = both.reshape(dims + both.shape)
        for bit in order:
            axis = len(bits) - 1 - bits.index(bit)
            both = join(both, swap(both, bit), bit, axis)
        return both.reshape((dp,) + both.shape[-2:])

    qk_all = gather_attention(qk, bits[1:])
    vo_full = gather_attention(vo, bits[:0:-1]).reshape(width, 2 * pair_width)
    qk_full = qk_all[:, :slice_width].reshape(width, 2 * pair_width)
    misc = qk_all[:, slice_width:]
    router_full = misc[:, : experts + 1, :slice_width].swapaxes(1, 2).reshape(width, -1)
    gain_rows = misc[:, experts + 2 : experts + 4, :slice_width].swapaxes(0, 1)
    gain_rows = gain_rows.reshape(2, width).astype(F32)
    bias = misc[:, experts + 1, :bias_width].astype(F32)
    bias = bias.reshape(dp, 3 * pair_heads, -1).swapaxes(0, 1).reshape(3, pair_width)

    tokens_sib = swap(tokens_z, 1)
    grad_z = lax.all_gather(out_grad, "tensor", axis=0, tiled=True)

    codes = jnp.concatenate([routes, slot_order], axis=1).T
    codes_x = swap(codes, 2)
    both_codes = swap(jnp.stack([codes, codes_x]), 1)
    codes_a = jnp.stack([codes, both_codes[0]])
    codes_b = jnp.stack([codes_x, both_codes[1]])
    pictures = jnp.stack([picture_ids, swap(picture_ids, 1)])

    def core_units(routed, shared):
        routed = routed.reshape(2, 2, mine_experts, hidden_units, slice_width)
        shared = shared.reshape(2, 2, 1, hidden_units, slice_width)

        def cut(which):
            return jnp.concatenate([pick(routed, which, 1), pick(shared, which, 1)], axis=1)

        return join(cut(core), swap(cut(1 - core), 1), 1, 3)

    def x_units(held):
        return join(pick(held, xi, 0), swap(pick(held, 1 - xi, 0), 2), 2, 2)

    def upper_units(held):
        for bit in upper[:-1]:
            held = join(held, swap(held, bit), bit, 2)
        return held, swap(held, upper[-1])

    def padded(*pairs):
        n = pairs[0][0].shape[-1]
        out = jnp.zeros((mine_experts + 1, len(pairs) * hidden_pad, 2 * n), BF)
        zero = jnp.int32(0)
        for k, (mine, theirs) in enumerate(pairs):
            row = jnp.int32(k * hidden_pad)
            out = lax.dynamic_update_slice(out, mine, (zero, row, n * bit_of(upper[-1])))
            out = lax.dynamic_update_slice(out, theirs, (zero, row, n * (1 - bit_of(upper[-1]))))
        return out

    down_c = core_units(expert_down, shared_down)
    gate_c = core_units(expert_gate.swapaxes(1, 2), shared_gate.T)
    up_c = core_units(expert_up.swapaxes(1, 2), shared_up.T)
    down_x = x_units(down_c)
    gate_x = x_units(gate_c)
    up_x = x_units(up_c)
    grad_x = swap(after(grad_z, up_x), 2)
    down_y = upper_units(down_x)
    gate_y = upper_units(gate_x)
    up_y = upper_units(up_x)

    rows_f = jnp.stack([tokens_z, tokens_sib]).astype(F32)
    qk_full = after(qk_full, down_c, gate_c, up_c)
    first_scale = lax.rsqrt(jnp.mean(rows_f * rows_f, axis=-1, keepdims=True) + EPS)
    first_norm = (rows_f * first_scale * gain_rows[0]).astype(BF)
    qk_pre = einsum("std,df->stf", first_norm, qk_full) + jnp.concatenate([bias[0], bias[1]])
    values = (einsum("std,df->stf", first_norm, vo_full[:, :pair_width]) + bias[2]).astype(BF)
    cos_part, sin_part = rope_tables(seq_len, head_width)
    qk_rot = rotate(
        qk_pre.reshape(2, seq_len, 2 * pair_heads, head_width), cos_part, sin_part
    ).astype(BF)
    qk_rot = after(qk_rot, down_x)
    queries, keys = qk_rot[:, :, :pair_heads], qk_rot[:, :, pair_heads:]
    values = values.reshape(2, seq_len, pair_heads, head_width)
    positions = jnp.arange(seq_len, dtype=jnp.int32)
    allowed = jnp.logical_or(
        positions[None, None, :] <= positions[None, :, None],
        pictures[:, :, None] * pictures[:, None, :] > 0,
    )
    score_scale = head_width ** (-0.5)
    scores = einsum("sqhd,skhd->shqk", queries, keys) * score_scale
    scores = jnp.where(allowed[:, None], scores, -1e30)
    weights = jnp.exp(scores - jnp.max(scores, axis=-1, keepdims=True))
    probs = weights / jnp.sum(weights, axis=-1, keepdims=True)
    probs_low = probs.astype(BF)
    head_mix = einsum("shqk,skhd->sqhd", probs_low, values).astype(BF)
    heads_out = after(head_mix.reshape(2, seq_len, pair_width), gate_x)
    out_weight = vo_full[:, pair_width:]
    attn_part = einsum("sqf,df->sqd", heads_out, out_weight)

    def core_sum(own, sibling):
        return own + swap(sibling.astype(BF), 1).astype(F32)

    def z_scatter(array):
        return lax.psum_scatter(
            array.astype(BF), "tensor", scatter_dimension=0, tiled=True
        ).astype(F32)

    inputs = tokens.astype(F32)
    hidden = inputs + z_scatter(core_sum(attn_part[0], attn_part[1]))
    hidden = after(hidden, up_x, down_y[1])
    second_scale = lax.rsqrt(jnp.mean(hidden * hidden, axis=-1, keepdims=True) + EPS)
    second_unit = hidden * second_scale
    second_norm = (second_unit * gain_rows[1]).astype(BF)
    norm_z = lax.all_gather(second_norm, "tensor", axis=0, tiled=True)
    norm_z = after(norm_z, gate_y[1], grad_x)
    down_all = padded(down_y)
    gateup_all = padded(gate_y, up_y)

    norm_x = swap(norm_z, 2)
    norm_a = jnp.stack([norm_z, swap(norm_z, 1)])
    norm_b = jnp.stack([norm_x, swap(norm_x, 1)])
    grad_a = jnp.stack([grad_z, swap(grad_z, 1)])
    grad_b = jnp.stack([grad_x, swap(grad_x, 1)])

    expert_ids = group * mine_experts + jnp.arange(mine_experts, dtype=jnp.int32)

    router_rows = jnp.pad(router_full.T, ((0, 16 - experts - 1), (0, 0)))
    group_ids = group.astype(jnp.int32).reshape(1)

    def slots_of(codes_in):
        routes_in, slots_in = codes_in[:, None, :top_count], codes_in[:, None, top_count:]
        matches = routes_in == expert_ids[None, :, None, None]
        return jnp.max(jnp.where(matches, slots_in, -1), axis=2)

    def feed(slots, rows, grads):
        slotted, slot_grad, pair, act, terms, pair_s, act_s, inner_s, probs_out = plain_act_call(
            experts, capacity, group_ids, slots, rows, grads, router_rows, gateup_all, down_all
        )
        terms = jnp.concatenate([terms.swapaxes(1, 2), inner_s], axis=-1)
        flat = [a.reshape(mine_experts, -1, a.shape[-1]) for a in (slotted, slot_grad, pair, act)]
        shared = [a.reshape(1, -1, a.shape[-1]) for a in (rows, grads, pair_s, act_s)]
        return (pair, pair_s), (act, act_s), terms, (flat, shared), probs_out

    slots_a, slots_b = slots_of(codes_a), slots_of(codes_b)
    fed_a = feed(slots_a, norm_a, grad_a)
    fed_b = feed(slots_b, norm_b, grad_b)
    columns_a, columns_b = slots_a[..., None], slots_b[..., None]
    row_grad_b = plain_back_call(columns_b, *fed_b[0], gateup_all)
    row_grad_a = plain_back_call(after(columns_a, row_grad_b), *fed_a[0], gateup_all)
    row_out_b = plain_back_call(after(columns_b, row_grad_a), *fed_b[1], down_all)
    row_out_a = plain_back_call(columns_a, *fed_a[1], down_all)

    def spread(terms):
        wide = jnp.zeros(terms.shape[:-1] + (128,), F32)
        wide = lax.dynamic_update_slice_in_dim(
            wide, terms[..., :mine_experts], group * mine_experts, terms.ndim - 1
        )
        return wide.at[..., experts].set(terms[..., mine_experts])

    def group_sum(a, b):
        across = b[0].astype(F32) + swap(b[1].astype(BF), 1).astype(F32)
        near = a[0].astype(F32) + swap(a[1].astype(BF), 1).astype(F32)
        return near + swap(across.astype(BF), 2).astype(F32)

    grad_sum = group_sum(row_grad_a, row_grad_b)
    term_sum = group_sum(spread(fed_a[2]), spread(fed_b[2]))
    packed = z_scatter(jnp.concatenate([grad_sum, term_sum], axis=-1))
    second_grad, gate_sums = packed[:, :width], packed[:, width:]

    data_a, data_b = fed_a[3], fed_b[3]

    def unit_grads(left, right):
        return jnp.concatenate(
            [
                plain_outer_call(
                    hidden_units,
                    hidden_pad,
                    dp,
                    [(data[k][left], data[k][right]) for data in (data_a, data_b)],
                )
                for k in range(2)
            ],
            axis=1,
        )

    def scatter_units(total):
        total = total.reshape((2,) * len(bits) + total.shape[1:])
        for bit in reversed(upper):
            axis = len(bits) - 1 - bits.index(bit)
            sent = half(total, 1 - bit_of(bit), axis)
            kept = half(total, bit_of(bit), axis)
            total = (kept.astype(F32) + swap(sent, bit).astype(F32)).astype(BF)
        total = total.reshape((2, 2) + total.shape[len(bits) :])
        held = join(pick(total, xi, 0)[None], swap(pick(total, 1 - xi, 0), 2)[None], 2, 0)
        return join(pick(held, core, 1)[:, None], swap(pick(held, 1 - core, 1), 1)[:, None], 1, 1)

    def split_units(held):
        routed = held[:, :, :mine_experts].reshape(experts, -1, slice_width)
        shared = held[:, :, mine_experts]
        return routed.astype(F32), shared.astype(F32)

    gateup_sum = scatter_units(unit_grads(2, 0))
    down_sum = scatter_units(unit_grads(3, 1))
    routed_gu, shared_gu = split_units(gateup_sum)
    routed_down, shared_down_sum = split_units(down_sum)
    shared_gu = shared_gu.reshape(4, 2, hidden_units, slice_width)
    egate_sum = routed_gu[:, :hidden_units].swapaxes(1, 2)
    eup_sum = routed_gu[:, hidden_units:].swapaxes(1, 2)
    sgate_sum = shared_gu[:, 0].reshape(-1, slice_width).T
    sup_sum = shared_gu[:, 1].reshape(-1, slice_width).T
    sdown_sum = shared_down_sum.reshape(-1, slice_width)

    row_start = zi * local_rows
    probs_local = lax.dynamic_slice_in_dim(fed_a[4][0], row_start, local_rows, 1).T
    probs_mine, weight_mine = probs_local[:, :experts], probs_local[:, experts]
    route_grad = gate_sums[:, :experts]
    expert_logit_grad = probs_mine * (
        route_grad - jnp.sum(probs_mine * route_grad, axis=-1, keepdims=True)
    )
    weight_logit_grad = gate_sums[:, experts] * weight_mine * (1.0 - weight_mine)
    logits_grad = jnp.concatenate([expert_logit_grad, weight_logit_grad[:, None]], axis=1).astype(
        BF
    )
    second_grad = second_grad + einsum("tf,df->td", logits_grad, router_full)
    gain_two_grad = jnp.sum(second_grad * second_unit, axis=0)
    unit_two = second_grad * gain_rows[1]
    hidden_grad = out_grad.astype(F32) + second_scale * (
        unit_two - second_unit * jnp.mean(unit_two * second_unit, axis=-1, keepdims=True)
    )
    attention_grad = hidden_grad.astype(BF)
    wide_logits = jnp.pad(logits_grad, ((0, 0), (0, 128 - experts - 1)))
    back_z = lax.all_gather(
        jnp.concatenate([attention_grad, wide_logits], axis=1), "tensor", axis=0, tiled=True
    )
    out_sum = after(group_sum(row_out_a, row_out_b), back_z)
    output = (hidden + z_scatter(out_sum)).astype(BF)
    logits_z = back_z[:, width : width + 16]
    back_own = back_z[:, :width]
    back_rows = jnp.stack([back_own, swap(back_own, 1)])

    router_part = einsum("tf,td->fd", logits_z, norm_z)[: experts + 1]

    out_proj = einsum("std,stf->df", back_rows, heads_out)
    mix_grad = einsum("std,df->stf", back_rows, out_weight).astype(BF)
    mix_grad = mix_grad.reshape(2, seq_len, pair_heads, head_width)
    prob_grad = einsum("sqhd,skhd->shqk", mix_grad, values)
    score_grad = (
        probs * (prob_grad - jnp.sum(probs * prob_grad, axis=-1, keepdims=True))
    ).astype(BF)
    query_rot = einsum("shqk,skhd->sqhd", score_grad, keys) * score_scale
    key_rot = einsum("shqk,sqhd->skhd", score_grad, queries) * score_scale
    value_grad = einsum("shqk,sqhd->skhd", probs_low, mix_grad)
    qk_grad = rotate(jnp.concatenate([query_rot, key_rot], axis=2), cos_part, -sin_part)
    qk_grad = qk_grad.astype(BF).reshape(2, seq_len, 2 * pair_width)
    v_grad = value_grad.astype(BF).reshape(2, seq_len, pair_width)
    first_part = einsum("stf,df->std", qk_grad, qk_full) + einsum(
        "stf,df->std", v_grad, vo_full[:, :pair_width]
    )
    first_grad = z_scatter(core_sum(first_part[0], first_part[1]))

    gain_one_grad = jnp.sum(first_part * (rows_f * first_scale), axis=(0, 1))
    bias_part = jnp.concatenate(
        [jnp.sum(qk_grad.astype(F32), axis=(0, 1)), jnp.sum(v_grad.astype(F32), axis=(0, 1))]
    )
    bias_part = bias_part.reshape(3 * pair_heads, dp, -1).swapaxes(0, 1).reshape(dp, 1, -1)
    gain_part = jnp.stack([gain_one_grad, gain_two_grad]).reshape(2, dp, slice_width)

    def wide_rows(rows):
        return jnp.pad(rows, ((0, 0), (0, 0), (0, 2 * pair_width - rows.shape[2])))

    misc_part = jnp.concatenate(
        [
            wide_rows(router_part.reshape(experts + 1, dp, slice_width).swapaxes(0, 1)),
            wide_rows(bias_part),
            wide_rows(gain_part.swapaxes(0, 1)),
            jnp.zeros((dp, misc_rows - experts - 4, 2 * pair_width), F32),
        ],
        axis=1,
    )
    qk_total = einsum("std,stf->df", first_norm, qk_grad).reshape(dp, slice_width, -1)
    qk_total = jnp.concatenate([qk_total, misc_part], axis=1)
    vo_total = jnp.concatenate([einsum("std,stf->df", first_norm, v_grad), out_proj], axis=1)
    vo_total = vo_total.reshape(dp, slice_width, -1)

    def scatter_attention(total, order):
        total = total.reshape((2,) * len(bits) + total.shape[1:])
        for bit in order:
            axis = len(bits) - 1 - bits.index(bit)
            sent = half(total, 1 - bit_of(bit), axis).astype(BF)
            total = half(total, bit_of(bit), axis) + swap(sent, bit).astype(F32)
        total = total.reshape((2,) + total.shape[-2:]).astype(BF)
        return pick(total, core, 0), swap(pick(total, 1 - core, 0), 1)

    def columns_of(mine, theirs):
        held = join(mine[:slice_width, None], theirs[:slice_width, None], 1, 1)
        first, second = held[..., :pair_width], held[..., pair_width:]
        return (
            first.reshape(slice_width, -1).astype(F32),
            second.reshape(slice_width, -1).astype(F32),
        )

    qk_mine, qk_theirs = scatter_attention(qk_total, bits[:0:-1])
    vo_mine, vo_theirs = scatter_attention(vo_total, bits[1:])
    qk_sums = columns_of(qk_mine, qk_theirs)
    vo_sums = columns_of(vo_mine, vo_theirs)
    misc_mine = qk_mine[slice_width:].astype(F32)
    misc_theirs = qk_theirs[slice_width:].astype(F32)
    misc_sum = misc_mine + misc_theirs
    router_sum = misc_sum[: experts + 1, :slice_width].T
    bias_sums = join(
        misc_mine[experts + 1, :bias_width].reshape(3, 1, pair_heads, -1),
        misc_theirs[experts + 1, :bias_width].reshape(3, 1, pair_heads, -1),
        1,
        1,
    ).reshape(3, heads_local, -1)
    gain_sums = lax.all_gather(
        misc_sum[experts + 2 : experts + 4, :slice_width], "tensor", axis=0, tiled=False
    )
    tensor = gain_sums.shape[0]
    gain_sums = jnp.sum(gain_sums, axis=0).reshape(2, tensor, -1)
    gain_sums = pick(gain_sums, zi, 1)

    unit_mine = inputs * lax.rsqrt(jnp.mean(inputs * inputs, axis=-1, keepdims=True) + EPS)
    scale_mine = lax.rsqrt(jnp.mean(inputs * inputs, axis=-1, keepdims=True) + EPS)
    unit_one = first_grad * gain_rows[0]
    input_grad = hidden_grad + scale_mine * (
        unit_one - unit_mine * jnp.mean(unit_one * unit_mine, axis=-1, keepdims=True)
    )
    return (
        output,
        input_grad.astype(BF),
        gain_sums,
        qk_sums[0],
        qk_sums[1],
        vo_sums[0],
        vo_sums[1].T,
        bias_sums,
        router_sum,
        sgate_sum,
        sup_sum,
        sdown_sum,
        egate_sum,
        eup_sum,
        routed_down,
    )


def local_fused(
    dp,
    depth,
    tokens,
    picture_ids,
    routes,
    slot_order,
    norm_gains,
    w_query,
    w_key,
    w_value,
    w_out,
    qkv_bias,
    router,
    shared_gate,
    shared_up,
    shared_down,
    expert_gate,
    expert_up,
    expert_down,
    out_grad,
):
    seq_len = picture_ids.shape[0]
    local_rows = tokens.shape[0]
    width = tokens.shape[1]
    experts, slice_width, hidden_units = expert_gate.shape
    heads_local = qkv_bias.shape[1]
    head_width = w_query.shape[1] // heads_local
    pair_heads = heads_local // 2
    pair_width = pair_heads * head_width
    mine_experts = experts // 4
    hidden_pad = -(-hidden_units // 128) * 128

    zi = lax.axis_index("tensor")
    codes = jnp.concatenate([routes.T, slot_order.T, picture_ids[None]], axis=0)
    codes = jnp.pad(codes, ((0, 16 - codes.shape[0]), (0, 0)))
    bias_cores = qkv_bias.reshape(3, 2, -1).swapaxes(0, 1).reshape(2, -1)
    bias_width = bias_cores.shape[1]
    misc = jnp.zeros((16, slice_width), F32)
    misc = misc.at[: experts + 1].set(router.T.astype(F32))
    misc = misc.at[experts + 1 : experts + 3, :bias_width].set(bias_cores.astype(F32))
    gains = lax.dynamic_update_slice(
        jnp.zeros((8, slice_width), F32),
        norm_gains.astype(F32),
        (jnp.int32(0), zi * norm_gains.shape[1]),
    )
    cos_part, sin_part = rope_arrays(seq_len, head_width)
    cos_rows = np.concatenate([cos_part, cos_part], axis=1)
    sin_rows = np.concatenate([-sin_part, sin_part], axis=1)
    (
        hidden,
        norm_all,
        grads_all,
        gateup_all,
        down_all,
        codes_all,
        router_rows,
        gain_rows,
        tok,
        attn_weights,
        qkv,
        probs_low,
        heads_out,
    ) = forward_call(
        dp,
        depth,
        experts,
        head_width,
        (codes, misc, gains, cos_rows, sin_rows),
        (tokens, out_grad, w_query, w_key, w_value, w_out.T),
        (
            expert_gate.swapaxes(1, 2),
            expert_up.swapaxes(1, 2),
            expert_down,
            shared_gate,
            shared_up,
            shared_down.reshape(4, hidden_units, slice_width),
        ),
    )
    gateup_all = gateup_all.reshape(mine_experts + 1, 2 * hidden_pad, width)
    down_all = down_all.reshape(mine_experts + 1, hidden_pad, width)
    (
        output,
        terms,
        probs_mine,
        grad_own,
        grad_sib,
        grad_far,
        gate_total,
        up_total,
        down_total,
        gate_in,
    ) = middle_call(
        dp,
        depth,
        experts,
        routes.shape[1],
        hidden_units,
        hidden,
        codes_all,
        router_rows,
        (norm_all, grads_all, gateup_all, down_all),
    )
    input_grad, gate_sum, up_sum, down_sum, attn_sum, misc_sum, gains_sum = backward_call(
        dp,
        depth,
        experts,
        head_width,
        (terms, probs_mine, router_rows, gain_rows, cos_rows, sin_rows, hidden, out_grad),
        (grad_own, grad_sib, grad_far, gate_in, gate_total, up_total, down_total)
        + (tok, attn_weights, qkv, probs_low, heads_out, norm_all),
    )

    egate_sum, eup_sum, edown_sum, sgate_sum, sup_sum, sdown_sum, *attn_sums = finish_call(
        gate_sum, up_sum, down_sum, attn_sum
    )
    bias_sums = misc_sum[experts + 1 : experts + 3, :bias_width].reshape(2, 3, pair_heads, -1)
    bias_sums = bias_sums.swapaxes(0, 1).reshape(3, heads_local, -1)
    piece = norm_gains.shape[1]
    gain_sums = lax.dynamic_slice(gains_sum[3:5], (jnp.int32(0), zi * piece), (2, piece))
    return (
        output,
        input_grad,
        gain_sums,
        *attn_sums,
        bias_sums,
        misc_sum[: experts + 1].T,
        sgate_sum,
        sup_sum,
        sdown_sum,
        egate_sum.swapaxes(1, 2),
        eup_sum.swapaxes(1, 2),
        edown_sum,
    )


def solution(mesh):
    dp, depth = mesh.shape["dp"], mesh.shape["tensor"]

    def body(*arrays):
        if arrays[5].shape[0] % 128 == 0 and dp == 8 and depth == 4:
            return local_fused(dp, depth, *arrays)
        return local_plain(dp, *arrays)

    return jax.shard_map(
        body,
        mesh=mesh,
        in_specs=(
            P(("dp", "tensor"), None),
            P("dp"),
            P("dp", None),
            P("dp", None),
            P(None, ("dp", "tensor")),
            P("dp", "tensor"),
            P("dp", "tensor"),
            P("dp", "tensor"),
            P("tensor", "dp"),
            P(None, "tensor", "dp"),
            P("dp", None),
            P("dp", "tensor"),
            P("dp", "tensor"),
            P("tensor", "dp"),
            P(None, "dp", "tensor"),
            P(None, "dp", "tensor"),
            P(None, "tensor", "dp"),
            P(("dp", "tensor"), None),
        ),
        out_specs=(
            P(("dp", "tensor"), None),
            P(("dp", "tensor"), None),
            P(None, ("dp", "tensor")),
            P("dp", "tensor"),
            P("dp", "tensor"),
            P("dp", "tensor"),
            P("tensor", "dp"),
            P(None, "tensor", "dp"),
            P("dp", None),
            P("dp", "tensor"),
            P("dp", "tensor"),
            P("tensor", "dp"),
            P(None, "dp", "tensor"),
            P(None, "dp", "tensor"),
            P(None, "tensor", "dp"),
        ),
        check_vma=False,
    )
```

```python
import functools

import jax
import jax.numpy as jnp
import numpy as np
from jax import lax
from jax.experimental import pallas as pl
from jax.experimental.pallas import tpu as pltpu
from jax.sharding import PartitionSpec as P

EPS = 1e-06
THETA = 1000000.0
BF = jnp.bfloat16
F32 = jnp.float32


def rope_tables(length, width):
    half_width = width // 2
    inverse = THETA ** (-(2.0 * jnp.arange(half_width, dtype=F32)) / width)
    angles = jnp.arange(length, dtype=F32)[:, None] * inverse[None, :]
    return jnp.cos(angles), jnp.sin(angles)


def rope_arrays(length, width):
    inverse = THETA ** (-(2.0 * np.arange(width // 2)) / width)
    angles = np.arange(length)[:, None] * inverse[None, :]
    return np.cos(angles).astype(np.float32), np.sin(angles).astype(np.float32)


def rotate(field_in, cos_part, sin_part):
    half_width = field_in.shape[-1] // 2
    low, high = field_in[..., :half_width], field_in[..., half_width:]
    cos_rows, sin_rows = cos_part[:, None, :], sin_part[:, None, :]
    return jnp.concatenate(
        [low * cos_rows - high * sin_rows, high * cos_rows + low * sin_rows], axis=-1
    )


def einsum(spec, *args):
    return jnp.einsum(spec, *args, preferred_element_type=F32)


def silu_parts(gate_in):
    gate_sig = jax.nn.sigmoid(gate_in)
    return gate_in * gate_sig, gate_sig * (1.0 + gate_in * (1.0 - gate_sig))


def after(array, *others):
    return lax.optimization_barrier((array,) + others)[0]


def pick(array, index, axis):
    return lax.dynamic_index_in_dim(array, index, axis, keepdims=False)


VMEM_LIMIT = 58 * 2**20


def dot(left, right, left_dim=1, right_dim=0):
    return lax.dot_general(
        left, right, (((left_dim,), (right_dim,)), ((), ())), preferred_element_type=F32
    )


def call(body, grid, in_specs, out_specs, out_shape, flops, moved, scratch=()):
    return pl.pallas_call(
        body,
        grid=grid,
        in_specs=in_specs,
        out_specs=out_specs,
        out_shape=out_shape,
        scratch_shapes=scratch,
        cost_estimate=pl.CostEstimate(flops=flops, bytes_accessed=moved, transcendentals=0),
        compiler_params=pltpu.CompilerParams(vmem_limit_bytes=VMEM_LIMIT),
    )


def plain_act_body(
    experts,
    units,
    group_ref,
    slot_ref,
    rows_ref,
    grads_ref,
    router_ref,
    gateup_ref,
    down_ref,
    slotted_ref,
    slotgrad_ref,
    pair_ref,
    act_ref,
    terms_ref,
    pair_s_ref,
    act_s_ref,
    inner_s_ref,
    probs_ref,
):
    unit = pl.program_id(1)
    half = gateup_ref.shape[1] // 2
    seq_len = rows_ref.shape[1]
    capacity = slotted_ref.shape[2]

    @pl.when(unit == 0)
    def _():
        logits = dot(router_ref[...], rows_ref[0], 1, 1)
        row = lax.broadcasted_iota(jnp.int32, logits.shape, 0)
        routed = jnp.where(row < experts, logits, -1e30)
        raised = jnp.exp(routed - jnp.max(routed, axis=0, keepdims=True))
        soft = raised / jnp.sum(raised, axis=0, keepdims=True)
        probs_ref[0] = jnp.where(row < experts, soft, jax.nn.sigmoid(logits))

    def parts(data, cot, weight):
        both = dot(data, gateup_ref[0], 1, 1)
        cot_in = dot(cot, down_ref[0], 1, 1)
        gate_in, up_in = both[:, :half], both[:, half:]
        gate_act, gate_slope = silu_parts(gate_in)
        act = gate_act * up_in
        inner = jnp.sum(act.astype(BF).astype(F32) * cot_in, axis=1, keepdims=True)
        cot_in = cot_in * weight
        return (
            (act * weight).astype(BF),
            (cot_in * up_in * gate_slope).astype(BF),
            (cot_in * gate_act).astype(BF),
            inner,
        )

    @pl.when(unit < units - 1)
    def _():
        slot = slot_ref[0, pl.ds(unit, 1), :]
        mask = lax.broadcasted_iota(jnp.int32, (capacity, seq_len), 0) == slot
        onehot = mask.astype(F32).astype(BF)
        slotted_ref[0, 0] = dot(onehot, rows_ref[0]).astype(BF)
        slotgrad_ref[0, 0] = dot(onehot, grads_ref[0]).astype(BF)
        probs = probs_ref[0]
        row = lax.broadcasted_iota(jnp.int32, probs.shape, 0)
        expert = group_ref[0] * (units - 1) + unit
        gate = jnp.sum(jnp.where(row == expert, probs, 0.0), axis=0, keepdims=True)
        weight = jnp.sum(jnp.where(mask, gate, 0.0), axis=1, keepdims=True)
        act, gate_grad, up_grad, inner = parts(slotted_ref[0, 0], slotgrad_ref[0, 0], weight)
        act_ref[0, 0] = act
        pair_ref[0, 0, :, :half] = gate_grad
        pair_ref[0, 0, :, half:] = up_grad
        terms_ref[0, pl.ds(unit, 1), :] = jnp.sum(
            jnp.where(mask, inner, 0.0), axis=0, keepdims=True
        )

    @pl.when(unit == units - 1)
    def _():
        logits = dot(rows_ref[0], router_ref[...], 1, 1)
        weight = jax.nn.sigmoid(logits[:, experts : experts + 1])
        act, gate_grad, up_grad, inner = parts(rows_ref[0], grads_ref[0], weight)
        act_s_ref[0] = act
        pair_s_ref[0, :, :half] = gate_grad
        pair_s_ref[0, :, half:] = up_grad
        inner_s_ref[0] = inner


def plain_act_call(experts, capacity, group, slots, rows, grads, router, gateup, down):
    count, seq_len, width = rows.shape
    units, wide, _ = gateup.shape
    half = wide // 2
    routed = units - 1

    def seq(s, u):
        return (s, 0, 0)

    def unit(s, u):
        return (u, 0, 0)

    def slot(s, u):
        return (jnp.minimum(u, routed - 1), s, 0, 0)

    work = count * (routed * capacity + seq_len) * width
    return call(
        functools.partial(plain_act_body, experts, units),
        (count, units),
        [
            pl.BlockSpec(memory_space=pltpu.SMEM),
            pl.BlockSpec((1, routed, seq_len), seq),
            pl.BlockSpec((1, seq_len, width), seq),
            pl.BlockSpec((1, seq_len, width), seq),
            pl.BlockSpec(router.shape, lambda s, u: (0, 0)),
            pl.BlockSpec((1, wide, width), unit),
            pl.BlockSpec((1, half, width), unit),
        ],
        [
            pl.BlockSpec((1, 1, capacity, width), slot),
            pl.BlockSpec((1, 1, capacity, width), slot),
            pl.BlockSpec((1, 1, capacity, wide), slot),
            pl.BlockSpec((1, 1, capacity, half), slot),
            pl.BlockSpec((1, routed, seq_len), seq),
            pl.BlockSpec((1, seq_len, wide), seq),
            pl.BlockSpec((1, seq_len, half), seq),
            pl.BlockSpec((1, seq_len, 1), seq),
            pl.BlockSpec((1,) + (router.shape[0], seq_len), seq),
        ],
        [
            jax.ShapeDtypeStruct((routed, count, capacity, width), BF),
            jax.ShapeDtypeStruct((routed, count, capacity, width), BF),
            jax.ShapeDtypeStruct((routed, count, capacity, wide), BF),
            jax.ShapeDtypeStruct((routed, count, capacity, half), BF),
            jax.ShapeDtypeStruct((count, routed, seq_len), F32),
            jax.ShapeDtypeStruct((count, seq_len, wide), BF),
            jax.ShapeDtypeStruct((count, seq_len, half), BF),
            jax.ShapeDtypeStruct((count, seq_len, 1), F32),
            jax.ShapeDtypeStruct((count, router.shape[0], seq_len), F32),
        ],
        2 * work * 3 * half + 4 * count * routed * capacity * seq_len * width,
        8 * count * seq_len * width * 2,
    )(group, slots, rows, grads, router, gateup, down)


def plain_back_body(slot_ref, routed_ref, shared_ref, weight_ref, out_ref):
    routed, _, capacity, _ = routed_ref.shape
    seq_len = shared_ref.shape[1]
    total = dot(shared_ref[0], weight_ref[routed])
    lane = lax.broadcasted_iota(jnp.int32, (seq_len, capacity), 1)
    for e in range(routed):
        slot_rows = dot(routed_ref[e, 0], weight_ref[e]).astype(BF)
        onehot = (lane == slot_ref[0, e]).astype(F32).astype(BF)
        total = total + dot(onehot, slot_rows)
    out_ref[0] = total.astype(BF)


def plain_back_call(slots, routed, shared, weight):
    units, wide, width = weight.shape
    count, seq_len, _ = shared.shape
    capacity = routed.shape[2]
    block = min(width, 512)
    work = count * ((units - 1) * capacity + seq_len) * width
    return call(
        plain_back_body,
        (width // block, count),
        [
            pl.BlockSpec((1, units - 1, seq_len, 1), lambda j, s: (s, 0, 0, 0)),
            pl.BlockSpec((units - 1, 1, capacity, wide), lambda j, s: (0, s, 0, 0)),
            pl.BlockSpec((1, seq_len, wide), lambda j, s: (s, 0, 0)),
            pl.BlockSpec((units, wide, block), lambda j, s: (0, 0, j)),
        ],
        pl.BlockSpec((1, seq_len, block), lambda j, s: (s, 0, j)),
        jax.ShapeDtypeStruct((count, seq_len, width), BF),
        2 * work * wide + 2 * count * (units - 1) * capacity * seq_len * width,
        units * wide * width * 2 + count * seq_len * width * 2,
    )(slots, routed, shared, weight)


def plain_outer_body(keep, pad, left_a, right_a, left_b, right_b, out_ref):
    total = dot(left_a[0], right_a[0], 0, 0) + dot(left_b[0], right_b[0], 0, 0)
    total = total.astype(BF)
    blocks, _, rows, slice_width = out_ref.shape
    for part in range(rows // keep):
        for k in range(blocks):
            out_ref[k, 0, part * keep : (part + 1) * keep] = total[
                part * pad : part * pad + keep, k * slice_width : (k + 1) * slice_width
            ]


def plain_outer_call(keep, pad, dp, pairs):
    (left_a, right_a), (left_b, right_b) = pairs
    units, rows, wide = left_a.shape
    width = right_a.shape[2]
    slice_width = width // dp
    blocks = max(1, 512 // slice_width)
    kept = wide // pad * keep

    def left(n):
        return pl.BlockSpec((1, n, wide), lambda u, j: (u, 0, 0))

    def right(n):
        return pl.BlockSpec((1, n, blocks * slice_width), lambda u, j: (u, 0, j))

    return call(
        functools.partial(plain_outer_body, keep, pad),
        (units, dp // blocks),
        [left(rows), right(rows), left(rows), right(rows)],
        pl.BlockSpec((blocks, 1, kept, slice_width), lambda u, j: (j, u, 0, 0)),
        jax.ShapeDtypeStruct((dp, units, kept, slice_width), BF),
        4 * units * rows * wide * width,
        units * rows * (wide + width) * 4,
    )(left_a, right_a, left_b, right_b)


MESH = pl.DeviceIdType.MESH


class Copies:
    def __init__(self, send, recv, here):
        self.send, self.recv, self.here = send, recv, here
        self.remote_count = self.local_count = 0

    def remote(self, src, dst, **device):
        k = self.remote_count
        self.remote_count += 1
        return pltpu.make_async_remote_copy(
            src_ref=src,
            dst_ref=dst,
            send_sem=self.send.at[k],
            recv_sem=self.recv.at[k],
            device_id=device,
            device_id_type=MESH,
        )

    def local(self, src, dst):
        k = self.local_count
        self.local_count += 1
        return pltpu.make_async_copy(src, dst, self.here.at[k])


class Line:
    def __init__(self, copies, buffer, z, depth, rows):
        self.z, self.depth = z, depth

        def piece(p):
            return buffer.at[pl.ds(pl.multiple_of(p * rows, rows), rows)]

        def make(k, sign):
            p = z - sign * k
            return copies.remote(piece(p), piece(p), tensor=z + sign)

        self.ups = [make(k, 1) for k in range(depth - 1)]
        self.downs = [make(k, -1) for k in range(depth - 1)]

    def sends(self, k):
        z, top = self.z, self.depth - 1
        return (
            (self.ups[k], jnp.logical_and(z < top, z >= k)),
            (self.downs[k], jnp.logical_and(z > 0, z + k <= top)),
        )

    def begin(self):
        for copy, there in self.sends(0):
            pl.when(there)(copy.start)

    def finish(self):
        for k in range(self.depth - 1):
            for copy, there in self.sends(k):
                pl.when(there)(copy.wait_send)


def peer_of(me, r):
    out, bit = me, 1
    while bit <= r:
        if r & bit:
            out = out + bit - 2 * bit * (me // bit % 2)
        bit *= 2
    return out


def greet(me, z, dp, depth):
    barrier = pltpu.get_barrier_semaphore()
    for r in range(1, dp):
        pl.semaphore_signal(barrier, inc=1, device_id={"dp": peer_of(me, r)}, device_id_type=MESH)
    for r in range(1, depth):
        pl.semaphore_signal(
            barrier, inc=1, device_id={"tensor": (z + r) % depth}, device_id_type=MESH
        )
    pl.semaphore_wait(barrier, dp - 1 + depth - 1)


def spin(field, cos_rows, sin_rows):
    return field * cos_rows + pltpu.roll(field, field.shape[-1] // 2, 1) * sin_rows


def piece_of(buffer, p, rows):
    return buffer.at[pl.ds(pl.multiple_of(p * rows, rows), rows)]


def pass_on(c, source, target, z, depth, rows, sibling, passed):
    def make(p):
        return c.remote(piece_of(source, p, rows), piece_of(target, p, rows), dp=sibling)

    ups = [make(z - k) for k in range(1, depth)]
    downs = [make(z + k) for k in range(1, depth)]
    for k in range(1, depth):
        passed.append((ups[k - 1], z >= k))
        passed.append((downs[k - 1], z + k <= depth - 1))

    def each(k, up):
        (ups if up else downs)[k - 1].start()

    return each


def line_step(line, k, each=None):
    z, top = line.z, line.depth - 1
    onward = line.sends(k) if k < top else (None, None)
    for up, copy, there, further in (
        (True, line.ups[k - 1], z >= k, onward[0]),
        (False, line.downs[k - 1], z + k <= top, onward[1]),
    ):
        pl.when(there)(copy.wait_recv)
        if further is not None:
            pl.when(further[1])(further[0].start)
        if each is not None:
            pl.when(there)(functools.partial(each, k, up))


def forward_body(
    sizes,
    codes_ref,
    misc_ref,
    gains_ref,
    cos_ref,
    sin_ref,
    tokens_ref,
    outgrad_ref,
    wq_ref,
    wk_ref,
    wv_ref,
    wo_ref,
    eg_ref,
    eu_ref,
    ed_ref,
    sg_ref,
    su_ref,
    sd_ref,
    hidden_ref,
    norm_ref,
    grads_ref,
    gateup_ref,
    down_ref,
    codes_all,
    router_out,
    gain_rows,
    tok_out,
    weights_out,
    qkv_out,
    probs_out,
    mix_out,
    misc_all,
    norm_mine,
    tok,
    weights,
    qkv_ref,
    probs_ref,
    mix_ref,
    fnorm,
    part,
    part_in,
    scatter_in,
    gains_all,
    zeros,
    shared_raw,
    shared_rows,
    send,
    recv,
    here,
):
    dp, depth, experts, hidden_units, head = sizes
    me, z = lax.axis_index("dp"), lax.axis_index("tensor")
    core, x = me % 2, (me // 2) % 2
    bits = [2**k for k in range(dp.bit_length() - 1)]
    rows, width = tokens_ref.shape
    seq_len = rows * depth
    slice_width = width // dp
    routed = experts // 4
    c = Copies(send, recv, here)

    def bit_of(bit):
        return (me // bit) % 2

    greet(me, z, dp, depth)

    first = []
    own_codes = c.local(codes_ref, codes_all.at[0])
    own_misc = c.local(misc_ref, misc_all.at[me])
    own_gains = c.local(gains_ref, gains_all.at[z, me])
    for copy in (own_codes, own_misc, own_gains):
        copy.start()
    for r in range(1, 4):
        first.append(c.remote(codes_ref, codes_all.at[r], dp=peer_of(me, r)))
    gain_copies = [c.remote(gains_ref, gains_all.at[z, me], dp=peer_of(me, r)) for r in range(1, dp)]
    misc_copies = [c.remote(misc_ref, misc_all.at[me], dp=peer_of(me, r)) for r in range(1, dp)]
    for copy in gain_copies + misc_copies + first:
        copy.start()

    def piece(buffer, p):
        return buffer.at[pl.ds(pl.multiple_of(p * rows, rows), rows)]

    own_tok = c.local(tokens_ref, piece(tok.at[0], z))
    own_tok.start()
    grad_up = c.local(outgrad_ref, norm_mine)
    grad_up.start()
    own_grad = c.local(norm_mine, piece(grads_ref.at[0], z))

    def columns(k, n):
        return pl.ds(pl.multiple_of(k * n, n), n)

    pair = wq_ref.shape[1] // 2
    own_at = tuple(bit_of(bit) for bit in reversed(bits))
    core_copies = []
    for k, w in enumerate((wq_ref, wk_ref, wv_ref, wo_ref)):
        place = weights.at[own_at + (slice(None), pl.ds(k * pair, pair))]
        core_copies.append(c.remote(w.at[:, columns(1 - core, pair)], place, dp=peer_of(me, 1)))
        core_copies.append(c.local(w.at[:, columns(core, pair)], place))
    for copy in core_copies:
        copy.start()

    beside = peer_of(me, 2)
    own_tok.wait()
    tok_line = Line(c, tok.at[0], z, depth, rows)
    tok_line.begin()
    tok_pass = [c.remote(tokens_ref, piece(tok.at[1], z), dp=peer_of(me, 1))]
    tok_pass[0].start()

    shared_loads = [c.local(sg_ref, shared_raw.at[0]), c.local(su_ref, shared_raw.at[1])]
    for copy in shared_loads:
        copy.start()
    zeros[...] = jnp.zeros_like(zeros)
    pad = zeros.shape[1]
    pads = [c.local(zeros, down_ref.at[:, 0, pl.ds(hidden_units, pad)])]
    pads += [c.local(zeros, gateup_ref.at[:, k, pl.ds(hidden_units, pad)]) for k in range(2)]
    matrices = ((ed_ref, sd_ref, down_ref, 0), (eg_ref, shared_rows.at[0], gateup_ref, 0), (eu_ref, shared_rows.at[1], gateup_ref, 1))
    slab = columns(me, slice_width)

    def group_copies(routed_src, shared_src, dst, k, r):
        group = (peer_of(me, r)) % 4
        many = (
            routed_src.at[pl.ds(group * routed, routed)],
            dst.at[pl.ds(0, routed), k, pl.ds(0, hidden_units), slab],
        )
        one = (shared_src.at[group], dst.at[routed, k, pl.ds(0, hidden_units), slab])
        if r == 0:
            return [c.local(*many), c.local(*one)]
        return [c.remote(*many, dp=peer_of(me, r)), c.remote(*one, dp=peer_of(me, r))]

    near = [[copy for r in (0, 1) for copy in group_copies(*m, r)] for m in matrices]
    far = [[copy for r in (2, 3) for copy in group_copies(*m, r)] for m in matrices]

    def over_copy(dst, k):
        n = 2 * slice_width
        chip = me // 2 + 1 - 2 * x
        cols = pl.ds(pl.multiple_of(chip * n, n), n)
        place = dst.at[:, k, pl.ds(0, hidden_units), cols]
        return c.remote(place, place, dp=peer_of(me, 4))

    over_near = [copy for m in matrices for r in (4, 5) for copy in group_copies(*m, r)]
    over = [over_copy(m[2], m[3]) for m in matrices]

    for copy in core_copies:
        copy.wait()

    def weight_copies(order, half):
        have, copies = [1], []
        for bit in order:
            index = tuple(
                pl.ds(0, 2) if b in have else pl.ds(bit_of(b), 1) for b in reversed(bits)
            )
            place = weights.at[index + (slice(None), pl.ds(half * 2 * pair, 2 * pair))]
            copies.append(c.remote(place, place, dp=peer_of(me, bit)))
            have.append(bit)
        return copies

    qk_copies = weight_copies(bits[1:], 0)
    vo_copies = weight_copies(bits[:0:-1], 1)
    qk_copies[0].start()
    vo_copies[0].start()
    grad_cut = width * 12 // 16
    grad_left, grad_right = pl.ds(0, grad_cut), pl.ds(grad_cut, width - grad_cut)
    far_grads = grads_ref.at[2, :, grad_right]
    grad_beside = c.remote(outgrad_ref.at[:, grad_right], piece(far_grads, z), dp=beside)
    grad_beside.start()
    far_grad_line = Line(c, far_grads, z, depth, rows)
    for k in range(2):
        shared_loads[k].wait()
        flipped = jnp.transpose(shared_raw[k].astype(F32)).astype(BF)
        shared_rows[k] = flipped.reshape(shared_rows.shape[1:])
    for copy in pads + [copy for m in near for copy in m]:
        copy.start()

    own_gains.wait()
    for copy in gain_copies:
        copy.wait_recv()
    gain_spread = [
        c.remote(gains_all.at[z], gains_all.at[z], tensor=(z + r) % depth) for r in range(1, depth)
    ]
    for copy in gain_spread:
        copy.start()

    tok_passed = []
    sibling = peer_of(me, 1)
    pass_tok = pass_on(c, tok.at[0], tok.at[1], z, depth, rows, sibling, tok_passed)

    line_step(tok_line, 1, pass_tok)
    for k in range(1, len(bits) - 1):
        qk_copies[k - 1].wait_recv()
        qk_copies[k].start()
        vo_copies[k - 1].wait_recv()
        vo_copies[k].start()
    grad_up.wait()
    own_grad.start()
    own_grad.wait()
    grad_line = Line(c, grads_ref.at[0], z, depth, rows)
    for k in range(2, depth):
        line_step(tok_line, k, pass_tok)
    grad_line.begin()

    for copy in gain_spread:
        copy.wait_recv()
    for d in range(dp):
        total = gains_all[0, d]
        for t in range(1, depth):
            total = total + gains_all[t, d]
        gain_rows[:, d * slice_width : (d + 1) * slice_width] = total

    def norm_rows(s):
        def block(i, carry):
            at = pl.ds(pl.multiple_of(i * rows, rows), rows)
            data = tok[s, at, :].astype(F32)
            scale = lax.rsqrt(jnp.mean(data * data, axis=-1, keepdims=True) + EPS)
            fnorm[at, :] = (data * scale * gain_rows[0:1, :]).astype(BF)
            return carry

        lax.fori_loop(0, depth, block, 0)

    own_misc.wait()
    for copy in misc_copies:
        copy.wait_recv()
    router_out[...] = jnp.zeros_like(router_out)
    row = lax.broadcasted_iota(jnp.int32, misc_ref.shape, 0)
    for d in range(dp):
        block = jnp.where(row <= experts, misc_all[d], 0.0).astype(BF)
        router_out[: misc_ref.shape[0], d * slice_width : (d + 1) * slice_width] = block
    bias_in = jnp.zeros(misc_ref.shape, F32)
    sub = lax.broadcasted_iota(jnp.int32, misc_ref.shape, 0)
    for d in range(dp):
        bias_in = jnp.where(sub == d, misc_all[d, pl.ds(experts + 1 + core, 1), :], bias_in)
    bias_in = bias_in.astype(BF)
    heads3 = 3 * pair
    head_slice = head // dp
    lane = lax.broadcasted_iota(jnp.int32, (bias_in.shape[1], heads3), 1)
    sub = lax.broadcasted_iota(jnp.int32, (bias_in.shape[1], heads3), 0)
    place = (lane // head * head_slice + lane % head_slice == sub).astype(F32).astype(BF)
    spread = dot(bias_in, place)
    lane = lax.broadcasted_iota(jnp.int32, spread.shape, 1)
    sub = lax.broadcasted_iota(jnp.int32, spread.shape, 0)
    bias = jnp.sum(jnp.where(lane % head // head_slice == sub, spread, 0.0), axis=0, keepdims=True)

    qk_copies[-1].wait_recv()
    vo_copies[-1].wait_recv()
    for m in far:
        for copy in m:
            copy.start()
    for copy in over_near:
        copy.start()
    pairs = pair // head

    def project(s):
        def block(i, carry):
            at = pl.ds(pl.multiple_of(i * 2 * rows, 2 * rows), 2 * rows)
            full = weights[...].reshape(width, 4 * pair)
            pre = dot(fnorm[at, :], full[:, : 3 * pair]) + bias
            cos_rows, sin_rows = cos_ref[at, :], sin_ref[at, :]
            for kind in range(3):
                for h in range(pairs):
                    a = (kind * pairs + h) * head
                    field = pre[:, a : a + head]
                    if kind < 2:
                        field = spin(field, cos_rows, sin_rows)
                    qkv_ref[kind, s * pairs + h, at, :] = field.astype(BF)
            return carry

        lax.fori_loop(0, depth // 2, block, 0)

    norm_rows(0)
    project(0)
    line_step(grad_line, 1)
    grad_beside.wait()
    far_grad_line.begin()
    for copy in far[0]:
        copy.wait_recv()
    over[0].start()
    tok_pass[0].wait()
    for copy, there in tok_passed:
        pl.when(there)(copy.wait)
    norm_rows(1)
    project(1)

    own_codes.wait()
    for copy in first:
        copy.wait()
    causal_block = seq_len // 2

    def attend(s):
        flags = codes_all[s]
        sub = lax.broadcasted_iota(jnp.int32, flags.shape, 0)
        flags = jnp.where(sub == 8, flags, 0).astype(F32).astype(BF)
        for h in range(pairs):
            for b in range(2):
                at = slice(b * causal_block, (b + 1) * causal_block)
                seen = dot(flags[:, at], flags, 0, 0)
                row = lax.broadcasted_iota(jnp.int32, seen.shape, 0) + b * causal_block
                col = lax.broadcasted_iota(jnp.int32, seen.shape, 1)
                scores = dot(qkv_ref[0, s * pairs + h, at, :], qkv_ref[1, s * pairs + h], 1, 1)
                scores = scores * head ** (-0.5)
                scores = jnp.where(jnp.logical_or(col <= row, seen > 0.5), scores, -1e30)
                raised = jnp.exp(scores - jnp.max(scores, axis=1, keepdims=True))
                probs = raised / jnp.sum(raised, axis=1, keepdims=True)
                probs = probs.astype(BF)
                probs_ref[s * pairs + h, at, :] = probs
                mixed = dot(probs, qkv_ref[2, s * pairs + h])
                mix_ref[s, at, h * head : (h + 1) * head] = mixed.astype(BF)

    def project_out(s):
        for d in range(dp):
            index = tuple(d // bit % 2 for bit in reversed(bits))
            block = weights[index + (slice(None), slice(3 * pair, 4 * pair))]
            at = slice(d * slice_width, (d + 1) * slice_width)
            part[s, :, at] = dot(mix_ref[s], block, 1, 1).astype(BF)

    attend(1)
    if depth > 2:
        line_step(grad_line, 2)
        line_step(far_grad_line, 1)
    project_out(1)
    part_pass = c.remote(part.at[1], part_in, dp=peer_of(me, 1))
    part_pass.start()
    attend(0)
    project_out(0)
    part_pass.wait_recv()

    saved = [
        c.local(a, b)
        for a, b in (
            (tok, tok_out),
            (weights, weights_out),
            (qkv_ref, qkv_out),
            (probs_ref, probs_out),
            (mix_ref, mix_out),
        )
    ]
    for copy in saved:
        copy.start()
    for k in range(3, depth):
        line_step(grad_line, k)
        line_step(far_grad_line, k - 1)
    x_grad = c.remote(grads_ref.at[0, :, grad_left], grads_ref.at[2, :, grad_left], dp=beside)
    x_grad.start()
    own_pass = c.remote(grads_ref.at[0], grads_ref.at[1], dp=peer_of(me, 1))
    own_pass.start()
    here_at = pl.ds(pl.multiple_of(z * rows, rows), rows)
    hidden_ref[...] = part[0, here_at, :].astype(F32) + part_in[here_at, :].astype(F32)
    hidden_ref[...] += tok[0, here_at, :].astype(F32)
    for r in range(depth):
        at = pl.ds(r * rows, rows)
        part[0, at, :] = (part[0, at, :].astype(F32) + part_in[at, :].astype(F32)).astype(BF)
    scatter = LineSum(c, part.at[0], scatter_in.at[0], scatter_in.at[1], z, depth, rows)
    scatter.run()
    for k in (1, 2):
        for copy in far[k]:
            copy.wait_recv()
        over[k].start()
    scatter.collect(hidden_ref)
    total = hidden_ref[...]
    scale = lax.rsqrt(jnp.mean(total * total, axis=-1, keepdims=True) + EPS)
    norm_mine[...] = (total * scale * gain_rows[1:2, :]).astype(BF)
    norm_here = c.local(norm_mine, piece(norm_ref.at[0], z))
    norm_here.start()
    norm_here.wait()
    norm_line = Line(c, norm_ref.at[0], z, depth, rows)
    norm_line.begin()
    cut = width * 12 // 16
    left, right = pl.ds(0, cut), pl.ds(cut, width - cut)
    norm_own = c.remote(piece(norm_ref.at[0], z), piece(norm_ref.at[1], z), dp=sibling)
    norm_far = c.remote(piece(norm_ref.at[0], z), piece(norm_ref.at[2], z), dp=beside)
    norm_far.start()
    norm_own.start()
    far_line = Line(c, norm_ref.at[2, :, right], z, depth, rows)
    norm_passed, far_passed = [], []
    pass_norm = pass_on(
        c, norm_ref.at[0], norm_ref.at[1], z, depth, rows, sibling, norm_passed
    )
    pass_far = pass_on(
        c, norm_ref.at[0, :, left], norm_ref.at[2, :, left], z, depth, rows, beside, far_passed
    )

    def pass_both(k, up):
        pass_far(k, up)
        pass_norm(k, up)

    line_step(norm_line, 1, pass_both)
    norm_far.wait()
    far_line.begin()
    for k in range(2, depth):
        line_step(norm_line, k, pass_both)
        line_step(far_line, k - 1)
    line_step(far_line, depth - 1)

    line_step(far_grad_line, depth - 1)
    x_grad.wait_recv()
    grad_pass = c.remote(grads_ref.at[2], grads_ref.at[3], dp=peer_of(me, 1))
    grad_pass.start()
    for copy in over_near + over + [copy for m in near for copy in m]:
        copy.wait()
    for copy, there in far_passed:
        pl.when(there)(copy.wait)
    norm_pass = c.remote(norm_ref.at[2], norm_ref.at[3], dp=sibling)
    norm_pass.start()
    norm_own.wait()
    for copy, there in norm_passed:
        pl.when(there)(copy.wait)
    norm_pass.wait()
    own_pass.wait()
    grad_pass.wait()
    for line in (tok_line, grad_line, far_grad_line, norm_line, far_line, scatter):
        line.finish()
    for copy in pads + saved:
        copy.wait()
    for copy in gain_copies + misc_copies + gain_spread + qk_copies + vo_copies:
        copy.wait_send()
    for copy in [part_pass, x_grad] + [y for m in far for y in m]:
        copy.wait_send()


def forward_call(dp, depth, experts, head, small, arrays, units):
    codes, misc, gains, cos_rows, sin_rows = small
    tokens, pair = arrays[0], arrays[2].shape[1] // 2
    rows, width = tokens.shape
    seq_len = rows * depth
    hidden_units = units[0].shape[1]
    hidden_pad = -(-hidden_units // 128) * 128
    routed = experts // 4
    bits = dp.bit_length() - 1
    pairs = pair // head
    vmem, hbm = pl.BlockSpec(memory_space=pltpu.VMEM), pl.BlockSpec(memory_space=pl.ANY)
    shape = jax.ShapeDtypeStruct
    return pl.pallas_call(
        functools.partial(forward_body, (dp, depth, experts, hidden_units, head)),
        in_specs=[vmem] * 5 + [hbm] * 12,
        out_specs=[vmem] + [hbm] * 4 + [vmem] * 3 + [hbm] * 5,
        out_shape=[
            shape((rows, width), F32),
            shape((4, seq_len, width), BF),
            shape((4, seq_len, width), BF),
            shape((routed + 1, 2, hidden_pad, width), BF),
            shape((routed + 1, 1, hidden_pad, width), BF),
            shape((4,) + codes.shape, codes.dtype),
            shape((128, width), BF),
            shape((8, width), F32),
            shape((2, seq_len, width), BF),
            shape((2,) * bits + (width // dp, 4 * pair), BF),
            shape((3, 2 * pairs, seq_len, head), BF),
            shape((2 * pairs, seq_len, seq_len), BF),
            shape((2, seq_len, pair), BF),
        ],
        scratch_shapes=[
            pltpu.VMEM((dp,) + misc.shape, F32),
            pltpu.VMEM((rows, width), BF),
            pltpu.VMEM((2, seq_len, width), BF),
            pltpu.VMEM((2,) * bits + (width // dp, 4 * pair), BF),
            pltpu.VMEM((3, 2 * pairs, seq_len, head), BF),
            pltpu.VMEM((2 * pairs, seq_len, seq_len), BF),
            pltpu.VMEM((2, seq_len, pair), BF),
            pltpu.VMEM((seq_len, width), BF),
            pltpu.VMEM((2, seq_len, width), BF),
            pltpu.VMEM((seq_len, width), BF),
            pltpu.VMEM((2, depth - 1, rows, width), BF),
            pltpu.VMEM((depth, dp) + gains.shape, F32),
            pltpu.VMEM((routed + 1, hidden_pad - hidden_units, width), BF),
            pltpu.VMEM((2, width // dp, 4 * hidden_units), BF),
            pltpu.VMEM((2, 4, hidden_units, width // dp), BF),
            pltpu.SemaphoreType.DMA((160,)),
            pltpu.SemaphoreType.DMA((160,)),
            pltpu.SemaphoreType.DMA((40,)),
        ],
        compiler_params=pltpu.CompilerParams(
            collective_id=0, has_side_effects=True, vmem_limit_bytes=VMEM_LIMIT
        ),
    )(codes, misc, gains, cos_rows, sin_rows, *arrays, *units)


def middle_body(
    sizes,
    hidden_ref,
    codes_ref,
    router_ref,
    rows_ref,
    grads_ref,
    gateup_ref,
    down_ref,
    output_ref,
    terms_out,
    probs_out,
    grad_own,
    grad_sib,
    grad_far,
    gate_total,
    up_total,
    down_total,
    gate_in,
    wide_w,
    down_w,
    xs,
    ys,
    pair,
    act,
    outs,
    backs,
    near_in,
    back_in,
    far_in,
    z_in,
    stage,
    weights,
    routed,
    probs,
    terms,
    terms_in,
    send,
    recv,
    here,
):
    dp, depth, experts, top_count, keep = sizes
    me, z = lax.axis_index("dp"), lax.axis_index("tensor")
    y = me // 4
    rows, width = output_ref.shape
    seq_len = rows * depth
    total = 2 * seq_len
    units, wide, _ = wide_w.shape
    half = wide // 2
    slice_width = width // dp
    sibling, beside, over = peer_of(me, 1), peer_of(me, 2), peer_of(me, 4)
    c = Copies(send, recv, here)

    greet(me, z, dp, depth)

    def load(source, chunk, target):
        copies = [
            c.local(source.at[2 * chunk + s], target.at[pl.ds(s * seq_len, seq_len)])
            for s in range(2)
        ]
        for copy in copies:
            copy.start()
        return copies

    def wait(copies):
        for copy in copies:
            copy.wait()

    loads = load(rows_ref, 1, xs)
    first = [(c.local(gateup_ref.at[u], wide_w.at[u]), c.local(down_ref.at[u], down_w.at[u])) for u in range(units)]
    first[0][0].start()
    first[0][1].start()
    loads += load(grads_ref, 1, ys)
    for u in range(1, units):
        first[u][0].start()
        first[u][1].start()

    block = seq_len // 2
    lanes = weights.shape[1]

    def gate_weights(chunk):
        def step(i, carry):
            at = pl.ds(pl.multiple_of(i * block, block), block)
            logits = dot(xs[at, :], router_ref[...], 1, 1)
            lane = lax.broadcasted_iota(jnp.int32, logits.shape, 1)
            chosen = jnp.where(lane < experts, logits, -1e30)
            raised = jnp.exp(chosen - jnp.max(chosen, axis=1, keepdims=True))
            soft = raised / jnp.sum(raised, axis=1, keepdims=True)
            probs[at, :] = jnp.where(lane < experts, soft, jax.nn.sigmoid(logits))
            return carry

        lax.fori_loop(0, total // block, step, 0)
        for s in range(2):
            codes = codes_ref[2 * chunk + s]
            row = lax.broadcasted_iota(jnp.int32, codes.shape, 0)
            named = row == experts
            for k in range(top_count):
                named = jnp.logical_or(named, codes[k : k + 1] == row)
            named = jnp.logical_and(named, row <= experts).astype(F32).astype(BF)
            place = (codes.shape[0], lanes)
            same = lax.broadcasted_iota(jnp.int32, place, 0) == lax.broadcasted_iota(
                jnp.int32, place, 1
            )
            routed[s * seq_len : (s + 1) * seq_len] = dot(named, same.astype(F32).astype(BF), 0, 0)
        weights[...] = probs[...] * routed[...]

    def activate(chunk):
        for u in range(units):
            if chunk == 1:
                wait(first[u])
            if u == 0:
                gate_weights(chunk)
            place = me % 4 * (units - 1) + u if u < units - 1 else experts

            def step(i, carry, u=u, place=place):
                at = pl.ds(pl.multiple_of(i * block, block), block)
                mine = lax.broadcasted_iota(jnp.int32, (block, lanes), 1) == place
                weight = jnp.sum(jnp.where(mine, weights[at, :], 0.0), axis=1, keepdims=True)
                both = dot(xs[at, :], wide_w[u], 1, 1)
                cot = dot(ys[at, :], down_w[u], 1, 1)
                gate_act, gate_slope = silu_parts(both[:, :half])
                value = gate_act * both[:, half:]
                inner = jnp.sum(value * cot, axis=1, keepdims=True)
                inner = jnp.where(mine, inner * routed[at, :], 0.0)
                terms[chunk, at, :] = inner if u == 0 else terms[chunk, at, :] + inner
                cot = cot * weight
                act[chunk, at, u * half : (u + 1) * half] = (value * weight).astype(BF)
                a = u * wide
                pair[chunk, at, a : a + half] = (cot * both[:, half:] * gate_slope).astype(BF)
                pair[chunk, at, a + half : a + wide] = (cot * gate_act).astype(BF)
                return carry

            lax.fori_loop(0, total // block, step, 0)

    cols = 512

    def back(left, chunk, s, weight, target):
        at = slice(s * seq_len, (s + 1) * seq_len)
        for j in range(width // cols):
            part = weight[:, :, j * cols : (j + 1) * cols]
            part = part.reshape(-1, cols)
            target[:, j * cols : (j + 1) * cols] = dot(left[chunk, at, :], part).astype(BF)

    def add_into(target, other):
        def step(i, carry):
            at = pl.ds(pl.multiple_of(i * rows, rows), rows)
            target[at, :] = (target[at, :].astype(F32) + other[at, :].astype(F32)).astype(BF)
            return carry

        lax.fori_loop(0, depth, step, 0)

    wait(loads)
    activate(1)
    loads = load(rows_ref, 0, xs) + load(grads_ref, 0, ys)
    terms_near = c.remote(terms.at[1, pl.ds(seq_len, seq_len)], terms_in, dp=sibling)
    terms_near.start()
    back(act, 1, 1, down_w, outs.at[1])
    out_near = c.remote(outs.at[1], near_in, dp=sibling)
    out_near.start()
    back(act, 1, 0, down_w, outs.at[0])
    terms_near.wait()
    terms[1, :seq_len] = terms[1, :seq_len] + terms_in[...]
    terms_across = c.remote(terms.at[1, pl.ds(0, seq_len)], terms_out.at[2], dp=beside)
    terms_across.start()
    out_near.wait()
    add_into(outs.at[0], near_in)
    out_across = c.remote(outs.at[0], far_in, dp=beside)
    out_across.start()
    back(pair, 1, 1, wide_w, outs.at[1])
    grad_near = c.remote(outs.at[1], back_in, dp=sibling)
    grad_near.start()
    back(pair, 1, 0, wide_w, backs)
    grad_near.wait()
    add_into(backs, back_in)
    grad_across = c.remote(backs, grad_far, dp=beside)
    grad_across.start()

    wait(loads)
    activate(0)
    probs_out[...] = probs[pl.ds(pl.multiple_of(z * rows, rows), rows), :]
    loads = load(rows_ref, 1, ys)
    terms_out[0] = terms[0, :seq_len]
    terms_last = c.remote(terms.at[0, pl.ds(seq_len, seq_len)], terms_out.at[1], dp=sibling)
    terms_last.start()
    back(act, 0, 1, down_w, outs.at[1])
    out_last = c.remote(outs.at[1], near_in, dp=sibling)
    out_last.start()
    back(act, 0, 0, down_w, back_in)

    staged, moved = [None, None], []
    blocks = stage.shape[2]

    def outer(left, parts, targets, u, j, slot):
        at = slice(j * blocks * slice_width, (j + 1) * blocks * slice_width)
        n = parts * half
        value = dot(left[0, :, u * n : (u + 1) * n], xs[:, at], 0, 0)
        value = (value + dot(left[1, :, u * n : (u + 1) * n], ys[:, at], 0, 0)).astype(BF)
        if staged[slot] is not None:
            wait(staged[slot])
        copies = []
        for k, target in enumerate(targets):
            for b in range(blocks):
                stage[slot, k, b] = value[
                    k * half : k * half + keep, b * slice_width : (b + 1) * slice_width
                ]
            copies.append(c.local(stage.at[slot, k], target.at[pl.ds(j * blocks, blocks), u]))
            copies[-1].start()
        staged[slot] = copies

    wait(loads)
    steps = dp // blocks
    scatter = []
    over_copies = []
    for u in range(units):
        for j in range(steps):
            outer(pair, 2, (gate_total, up_total), u, j, j % 2)
        if u == 0:
            out_last.wait()
            out_across.wait()
            for r in list(range(1, depth)) + [0]:
                at = pl.ds(pl.multiple_of((z + r) % depth * rows, rows), rows)
                part = back_in[at, :].astype(F32) + near_in[at, :].astype(F32)
                part = part + far_in[at, :].astype(F32)
                if r:
                    back_in[at, :] = part.astype(BF)
                    copy = c.remote(back_in.at[at], z_in.at[r - 1], tensor=(z + r) % depth)
                    copy.start()
                    scatter.append(copy)
                else:
                    near_in[at, :] = part.astype(BF)
        for slot in range(2):
            wait(staged[slot])
            staged[slot] = None
        source = gate_total.at[pl.ds((1 - y) * 4, 4), u]
        over_copies.append(c.remote(source, gate_in.at[:, u], dp=over))
        over_copies[-1].start()
    loads = load(grads_ref, 0, xs) + load(grads_ref, 1, ys)

    back(pair, 0, 1, wide_w, outs.at[1])
    grad_last = c.remote(outs.at[1], grad_sib, dp=sibling)
    grad_last.start()
    back(pair, 0, 0, wide_w, outs.at[0])
    grad_here = c.local(outs.at[0], grad_own)
    grad_here.start()
    wait(loads)
    for u in range(units):
        for j in range(steps):
            outer(act, 1, (down_total,), u, j, j % 2)
    for copy in scatter:
        copy.wait_recv()
    value = near_in[pl.ds(pl.multiple_of(z * rows, rows), rows), :].astype(F32)
    value = value + hidden_ref[...]
    for r in range(1, depth):
        value = value + z_in[r - 1].astype(F32)
    output_ref[...] = value.astype(BF)
    for slot in range(2):
        wait(staged[slot])
    for copy in scatter:
        copy.wait_send()
    wait([grad_here, grad_last, terms_last, terms_across, grad_across] + over_copies)


def middle_call(dp, depth, experts, top_count, hidden_units, hidden, codes, router, arrays):
    rows, width = hidden.shape
    seq_len = rows * depth
    norm, grads, gateup, down = arrays
    units, wide, _ = gateup.shape
    half = wide // 2
    slice_width = width // dp
    blocks = max(1, 1024 // slice_width)
    vmem, hbm = pl.BlockSpec(memory_space=pltpu.VMEM), pl.BlockSpec(memory_space=pl.ANY)
    shape = jax.ShapeDtypeStruct
    total = shape((dp, units, hidden_units, slice_width), BF)
    return pl.pallas_call(
        functools.partial(middle_body, (dp, depth, experts, top_count, hidden_units)),
        in_specs=[vmem] * 3 + [hbm] * 4,
        out_specs=[vmem] * 3 + [hbm] * 7,
        out_shape=[
            shape((rows, width), BF),
            shape((3, seq_len, 128), F32),
            shape((rows, 128), F32),
            shape((seq_len, width), BF),
            shape((seq_len, width), BF),
            shape((seq_len, width), BF),
            total,
            total,
            total,
            shape((4, units, hidden_units, slice_width), BF),
        ],
        scratch_shapes=[
            pltpu.VMEM((units, wide, width), BF),
            pltpu.VMEM((units, half, width), BF),
            pltpu.VMEM((2 * seq_len, width), BF),
            pltpu.VMEM((2 * seq_len, width), BF),
            pltpu.VMEM((2, 2 * seq_len, units * wide), BF),
            pltpu.VMEM((2, 2 * seq_len, units * half), BF),
            pltpu.VMEM((2, seq_len, width), BF),
            pltpu.VMEM((seq_len, width), BF),
            pltpu.VMEM((seq_len, width), BF),
            pltpu.VMEM((seq_len, width), BF),
            pltpu.VMEM((seq_len, width), BF),
            pltpu.VMEM((depth - 1, rows, width), BF),
            pltpu.VMEM((2, 2, blocks, hidden_units, slice_width), BF),
            pltpu.VMEM((2 * seq_len, 128), F32),
            pltpu.VMEM((2 * seq_len, 128), F32),
            pltpu.VMEM((2 * seq_len, 128), F32),
            pltpu.VMEM((2, 2 * seq_len, 128), F32),
            pltpu.VMEM((seq_len, 128), F32),
            pltpu.SemaphoreType.DMA((32,)),
            pltpu.SemaphoreType.DMA((32,)),
            pltpu.SemaphoreType.DMA((64,)),
        ],
        compiler_params=pltpu.CompilerParams(
            collective_id=2, has_side_effects=True, vmem_limit_bytes=63 * 2**20
        ),
    )(hidden, codes, router, norm, grads, gateup, down)


class LineSum:
    def __init__(self, c, data, ups, downs, z, depth, rows):
        self.data, self.ups, self.downs = data, ups, downs
        self.z, self.depth, self.rows = z, depth, rows
        self.up_copies = [
            c.remote(self.piece(t), ups.at[t - 1], tensor=z + 1) for t in range(1, depth)
        ]
        self.down_copies = [
            c.remote(self.piece(t), downs.at[t], tensor=z - 1) for t in range(depth - 1)
        ]

    def piece(self, t):
        return self.data.at[pl.ds(t * self.rows, self.rows)]

    def add(self, t, other):
        at = pl.ds(t * self.rows, self.rows)
        self.data[at, :] = (self.data[at, :].astype(F32) + other.astype(F32)).astype(BF)

    def up(self, t):
        copy = self.up_copies[t - 1]

        @pl.when(self.z < t)
        def _():
            @pl.when(self.z > 0)
            def _():
                copy.wait_recv()
                self.add(t, self.ups[t - 1])

            copy.start()

    def down(self, t):
        copy = self.down_copies[t]

        @pl.when(self.z > t)
        def _():
            @pl.when(self.z < self.depth - 1)
            def _():
                copy.wait_recv()
                self.add(t, self.downs[t])

            copy.start()

    def begin(self):
        top = self.depth - 1

        @pl.when(self.z == 0)
        def _():
            for k in range(top):
                self.up_copies[top - k - 1].start()

        @pl.when(self.z == top)
        def _():
            for k in range(top):
                self.down_copies[k].start()

    def step(self, k):
        top = self.depth - 1

        @pl.when(jnp.logical_and(self.z > 0, self.z < self.depth // 2))
        def _():
            self.up(top - k)
            self.down(k)

        @pl.when(jnp.logical_and(self.z >= self.depth // 2, self.z < top))
        def _():
            self.down(k)
            self.up(top - k)

    def run(self):
        self.begin()
        for k in range(self.depth - 1):
            self.step(k)

    def collect(self, total_ref):
        for t in range(self.depth):

            @pl.when(self.z == t)
            def _(t=t):
                if t > 0:
                    self.up_copies[t - 1].wait_recv()
                    total_ref[...] += self.ups[t - 1].astype(F32)
                if t < self.depth - 1:
                    self.down_copies[t].wait_recv()
                    total_ref[...] += self.downs[t].astype(F32)

    def finish(self):
        for t in range(1, self.depth):
            pl.when(self.z < t)(self.up_copies[t - 1].wait_send)
        for t in range(self.depth - 1):
            pl.when(self.z > t)(self.down_copies[t].wait_send)


def backward_body(
    sizes,
    terms_ref,
    probs_mine_ref,
    router_ref,
    gain_rows,
    cos_ref,
    sin_ref,
    hidden_ref,
    outgrad_ref,
    grad_a_ref,
    grad_b_ref,
    grad_c_ref,
    gate_in_ref,
    gate_ref,
    up_ref,
    down_ref,
    tok_hbm,
    weights_hbm,
    qkv_hbm,
    probs_hbm,
    mix_hbm,
    norm_hbm,
    input_ref,
    gate_out,
    up_out,
    down_out,
    attn_out,
    misc_out,
    gains_out,
    own_sum,
    arrived,
    three,
    scatter_in,
    terms_sum,
    terms_in,
    back,
    tok,
    weights,
    qkv,
    probs_ref,
    mix_ref,
    scales,
    qkv_grad,
    part_in,
    keep,
    total_a,
    first_qk,
    first_vo,
    second_in,
    misc_part,
    misc_in,
    gains_in,
    vectors,
    send,
    recv,
    here,
):
    dp, depth, experts, head = sizes
    me, z = lax.axis_index("dp"), lax.axis_index("tensor")
    core, x, y = me % 2, (me // 2) % 2, me // 4
    rows, width = input_ref.shape
    seq_len = rows * depth
    slice_width = width // dp
    pair = mix_ref.shape[2]
    pairs = pair // head
    bits = [1, 2, 4]
    c = Copies(send, recv, here)

    greet(me, z, dp, depth)

    matrices = ((gate_ref, gate_out), (up_ref, up_out), (down_ref, down_out))
    over = [None]
    for m in (1, 2):
        other = matrices[m][0].at[pl.ds((1 - y) * 4, 4)]
        over.append(c.remote(other, arrived.at[m], dp=peer_of(me, 4)))
        over[m].start()
    gate_in = c.local(gate_in_ref, arrived.at[0])
    grads = (grad_a_ref, grad_b_ref, grad_c_ref)
    loads = [c.local(grads[k], three.at[k]) for k in range(3)]
    for copy in loads:
        copy.start()
    own_loads = [
        c.local(source.at[pl.ds(y * 4, 4)], own_sum) for source, _ in matrices
    ]
    inputs = [
        c.local(a, b)
        for a, b in (
            (weights_hbm, weights),
            (mix_hbm, mix_ref),
            (qkv_hbm, qkv),
            (probs_hbm, probs_ref),
            (tok_hbm, tok),
        )
    ]
    own_loads[0].start()
    gate_in.start()
    for copy in inputs:
        copy.start()

    def at_of(p):
        return pl.ds(pl.multiple_of(p * rows, rows), rows)

    for copy in loads:
        copy.wait()
    small = []
    for r in range(depth):
        at = at_of((z + r) % depth)
        total = three[0, at, :].astype(F32) + three[1, at, :].astype(F32)
        total = total + three[2, at, :].astype(F32)
        three[0, at, :] = total.astype(BF)
        extra = terms_ref[0, at, :] + terms_ref[1, at, :] + terms_ref[2, at, :]
        terms_sum[at, :] = extra
        if r:
            copy = c.remote(terms_sum.at[at], terms_in.at[r - 1], tensor=(z + r) % depth)
            copy.start()
            small.append(copy)
        else:
            keep[0] = total
    scatter = LineSum(c, three.at[0], scatter_in.at[0, 0], scatter_in.at[0, 1], z, depth, rows)
    scatter.run()

    def add_over(m):
        own_loads[m].wait()
        if m:
            over[m].wait_recv()
        else:
            gate_in.wait()
        copies = []
        for r in (2, 3, 1, 0):
            k = peer_of(me, r) % 4
            for unit in range(own_sum.shape[1]):
                arrived[m, k, unit] = (
                    own_sum[k, unit].astype(F32) + arrived[m, k, unit].astype(F32)
                ).astype(BF)
            place = matrices[m][1].at[me % 4]
            if r:
                copies.append(c.remote(arrived.at[m, k], place, dp=peer_of(me, r)))
            else:
                copies.append(c.local(arrived.at[m, k], place))
            copies[-1].start()
        if m + 1 < len(own_loads):
            own_loads[m + 1].start()
        return copies

    units = add_over(0)
    for copy in small:
        copy.wait_recv()
    route = terms_sum[at_of(z), :]
    for r in range(1, depth):
        route = route + terms_in[r - 1]
    scatter.collect(keep.at[0])
    grad = keep[0]
    probs_mine = probs_mine_ref[...]
    lane = lax.broadcasted_iota(jnp.int32, route.shape, 1)
    inner = jnp.sum(jnp.where(lane < experts, probs_mine * route, 0.0), axis=1, keepdims=True)
    logits = jnp.where(
        lane < experts,
        probs_mine * (route - inner),
        jnp.where(lane == experts, route * probs_mine * (1.0 - probs_mine), 0.0),
    ).astype(BF)
    grad = grad + dot(logits, router_ref[...])
    hidden = hidden_ref[...]
    scale = lax.rsqrt(jnp.mean(hidden * hidden, axis=-1, keepdims=True) + EPS)
    unit = hidden * scale
    vectors[1:2, :] = jnp.sum(grad * unit, axis=0, keepdims=True)
    grad = grad * gain_rows[1:2, :]
    grad = outgrad_ref[...].astype(F32) + scale * (
        grad - unit * jnp.mean(grad * unit, axis=-1, keepdims=True)
    )
    keep[0] = grad
    back[0, at_of(z), :width] = grad.astype(BF)
    back[0, at_of(z), width:] = logits

    line = Line(c, back.at[0], z, depth, rows)
    line.begin()
    sibling = peer_of(me, 1)
    back_own = c.remote(piece_of(back.at[0], z, rows), piece_of(back.at[1], z, rows), dp=sibling)
    back_own.start()
    passed = []
    pass_back = pass_on(c, back.at[0], back.at[1], z, depth, rows, sibling, passed)
    line_step(line, 1, pass_back)

    for copy in inputs:
        copy.wait()

    def scale_rows(i, carry):
        at = at_of(i)
        for s in range(2):
            data = tok[s, at, :].astype(F32)
            scales[s, at, :] = lax.rsqrt(jnp.mean(data * data, axis=-1, keepdims=True) + EPS)
        return carry

    lax.fori_loop(0, depth, scale_rows, 0)
    units += add_over(1)
    line_step(line, 2, pass_back)
    line_step(line, 3, pass_back)
    back_own.wait()
    for copy, there in passed:
        pl.when(there)(copy.wait)
    def block_of(d):
        return tuple(d // bit % 2 for bit in reversed(bits))

    def slab(d):
        return slice(d * slice_width, (d + 1) * slice_width)

    def attention(s):
        mixed = jnp.zeros((seq_len, pair), F32)
        for d in range(dp):
            block = weights[block_of(d) + (slice(None), slice(3 * pair, 4 * pair))]
            mixed = mixed + dot(back[s, :, slab(d)], block)
        mixed = mixed.astype(BF)
        for h in range(pairs):
            n = s * pairs + h
            cot = mixed[:, h * head : (h + 1) * head]
            key_total = jnp.zeros((seq_len, head), F32)
            value_total = jnp.zeros((seq_len, head), F32)
            for b in range(2):
                at = slice(b * seq_len // 2, (b + 1) * seq_len // 2)
                p_low = probs_ref[n, at, :]
                p = p_low.astype(F32)
                p_grad = dot(cot[at], qkv[2, n], 1, 1)
                s_grad = p * (p_grad - jnp.sum(p * p_grad, axis=1, keepdims=True))
                s_grad = s_grad.astype(BF)
                q_grad = dot(s_grad, qkv[1, n]) * head ** (-0.5)
                q_grad = spin(q_grad, cos_ref[at, :], -sin_ref[at, :])
                qkv_grad[s, at, h * head : (h + 1) * head] = q_grad.astype(BF)
                key_total = key_total + dot(s_grad, qkv[0, n, at, :], 0, 0)
                value_total = value_total + dot(p_low, cot[at], 0, 0)
            k_grad = spin(key_total * head ** (-0.5), cos_ref[...], -sin_ref[...])
            a = pair + h * head
            qkv_grad[s, :, a : a + head] = k_grad.astype(BF)
            qkv_grad[s, :, a + pair : a + pair + head] = value_total.astype(BF)

    def first_grad(s):
        for d in range(dp):
            block = weights[block_of(d) + (slice(None), slice(0, 3 * pair))]
            total = dot(qkv_grad[s], block, 1, 1)
            three[1 + s, :, slab(d)] = total.astype(BF)
            unit_block = tok[s, :, slab(d)].astype(F32) * scales[s]
            row = jnp.sum(total * unit_block, axis=0, keepdims=True)
            vectors[2 + s : 3 + s, slab(d)] = row

    units += add_over(2)
    attention(1)
    first_grad(1)
    part_pass = c.remote(three.at[2], part_in, dp=sibling)
    part_pass.start()
    attention(0)
    first_grad(0)
    part_pass.wait_recv()
    keep[1] = three[1, at_of(z), :].astype(F32) + part_in[at_of(z), :].astype(F32)
    for r in range(depth):
        at = at_of(r)
        three[1, at, :] = (three[1, at, :].astype(F32) + part_in[at, :].astype(F32)).astype(BF)
    first_scatter = LineSum(
        c, three.at[1], scatter_in.at[1, 0], scatter_in.at[1, 1], z, depth, rows
    )
    first_scatter.begin()

    for d in range(dp):
        total = jnp.zeros((slice_width, 3 * pair), F32)
        out_total = jnp.zeros((slice_width, pair), F32)
        for s in range(2):
            data = tok[s, :, slab(d)].astype(F32) * scales[s] * gain_rows[0:1, slab(d)]
            total = total + dot(data.astype(BF), qkv_grad[s], 0, 0)
            out_total = out_total + dot(back[s, :, slab(d)], mix_ref[s], 0, 0)
        total_a[block_of(d) + (slice(None), slice(0, 3 * pair))] = total.astype(BF)
        total_a[block_of(d) + (slice(None), slice(3 * pair, 4 * pair))] = out_total.astype(BF)

    half = 2 * pair

    def index(y_at, x_at, k):
        return (y_at, x_at, slice(None), slice(None), pl.ds(k * half, half))

    every = pl.ds(0, 2)
    qk_first = c.remote(
        total_a.at[index(pl.ds(1 - y, 1), every, 0)], first_qk, dp=peer_of(me, 4)
    )
    vo_first = c.remote(
        total_a.at[index(every, pl.ds(1 - x, 1), 1)], first_vo, dp=peer_of(me, 2)
    )
    qk_first.start()
    vo_first.start()
    first_scatter.step(0)

    scatter.finish()
    norm_load = c.local(norm_hbm.at[0], three.at[0])
    norm_load.start()
    norm_load.wait()
    router_part = dot(back[0, :, width:], three[0], 0, 0)
    ones = jnp.ones((16, seq_len), BF)
    bias_row = dot(ones, qkv_grad[0]) + dot(ones, qkv_grad[1])
    lane = lax.broadcasted_iota(jnp.int32, bias_row.shape, 1)
    sub = lax.broadcasted_iota(jnp.int32, bias_row.shape, 0)
    head_slice = head // dp
    bias_rows = jnp.where(lane % head // head_slice == sub, bias_row, 0.0)
    high = bias_rows.astype(BF)
    low = (bias_rows - high.astype(F32)).astype(BF)
    lane = lax.broadcasted_iota(jnp.int32, (3 * pair, slice_width), 1)
    sub = lax.broadcasted_iota(jnp.int32, (3 * pair, slice_width), 0)
    place = (sub // head * head_slice + sub % head_slice == lane).astype(F32).astype(BF)
    bias_rows = dot(high, place) + dot(low, place)
    sub = lax.broadcasted_iota(jnp.int32, (16, slice_width), 0)
    misc_copies = []
    for d in range(dp):
        tile = jnp.where(sub <= experts, router_part[:16, slab(d)], 0.0)
        tile = jnp.where(sub == experts + 1 + core, bias_rows[d : d + 1], tile)
        gain_one = vectors[2:3, slab(d)] + vectors[3:4, slab(d)]
        tile = jnp.where(sub == experts + 3, gain_one, tile)
        tile = jnp.where(sub == experts + 4, vectors[1:2, slab(d)], tile)
        misc_part[d] = tile
    for r in range(1, dp):
        to = peer_of(me, r)
        misc_copies.append(c.remote(misc_part.at[to], misc_in.at[r - 1], dp=to))
        misc_copies[-1].start()

    for k in range(1, depth - 1):
        first_scatter.step(k)
    qk_first.wait()
    mine = index(pl.ds(y, 1), every, 0)
    total_a[mine] = (total_a[mine].astype(F32) + first_qk[...].astype(F32)).astype(BF)
    qk_second = c.remote(
        total_a.at[index(pl.ds(y, 1), pl.ds(1 - x, 1), 0)], second_in.at[0], dp=peer_of(me, 2)
    )
    qk_second.start()
    vo_first.wait()
    mine = index(every, pl.ds(x, 1), 1)
    total_a[mine] = (total_a[mine].astype(F32) + first_vo[...].astype(F32)).astype(BF)
    vo_second = c.remote(
        total_a.at[index(pl.ds(1 - y, 1), pl.ds(x, 1), 1)], second_in.at[1], dp=peer_of(me, 4)
    )
    vo_second.start()

    total = misc_part[me]
    for r, copy in enumerate(misc_copies):
        copy.wait_recv()
        total = total + misc_in[r]
    misc_out[...] = total
    gain_copies = []
    for r in range(1, depth):
        peer = (z + r) % depth
        gain_copies.append(c.remote(misc_out.at[8:16], gains_in.at[r - 1], tensor=peer))
        gain_copies[-1].start()

    finals = []
    for k, copy in enumerate((qk_second, vo_second)):
        copy.wait()
        mine = (y, x, slice(None), slice(None), pl.ds(k * half, half))
        total_a[mine] = (
            total_a[mine].astype(F32) + second_in[k, 0, 0].astype(F32)
        ).astype(BF)
        for other in (True, False):
            to = 1 - core if other else core
            source = total_a.at[y, x, to, :, pl.ds(k * half, half)]
            place = attn_out.at[core, :, pl.ds(k * half, half)]
            finals.append(c.remote(source, place, dp=sibling) if other else c.local(source, place))
            finals[-1].start()

    first_scatter.collect(keep.at[1])
    total = keep[1]
    total = total * gain_rows[0:1, :]
    scale = scales[0, at_of(z), :]
    unit = tok[0, at_of(z), :].astype(F32) * scale
    total = keep[0] + scale * (total - unit * jnp.mean(total * unit, axis=-1, keepdims=True))
    input_ref[...] = total.astype(BF)

    total = misc_out[8:16, :]
    for r, copy in enumerate(gain_copies):
        copy.wait()
        total = total + gains_in[r]
    gains_out[...] = total
    for copy in finals + units:
        copy.wait()
    line.finish()
    first_scatter.finish()
    for copy in over[1:] + small + misc_copies + [part_pass]:
        copy.wait_send()


def backward_call(dp, depth, experts, head, in_vmem, in_hbm):
    output_rows, width = in_vmem[6].shape
    seq_len = output_rows * depth
    slice_width = width // dp
    units = in_hbm[3].shape[1:]
    pair = in_hbm[11].shape[2]
    pairs = pair // head
    vmem, hbm = pl.BlockSpec(memory_space=pltpu.VMEM), pl.BlockSpec(memory_space=pl.ANY)
    shape = jax.ShapeDtypeStruct
    final = shape((4,) + units, BF)
    return pl.pallas_call(
        functools.partial(backward_body, (dp, depth, experts, head)),
        in_specs=[vmem] * len(in_vmem) + [hbm] * len(in_hbm),
        out_specs=[vmem, hbm, hbm, hbm, vmem, vmem, vmem],
        out_shape=[
            shape((output_rows, width), BF),
            final,
            final,
            final,
            shape((2, slice_width, 4 * pair), BF),
            shape((16, slice_width), F32),
            shape((8, slice_width), F32),
        ],
        scratch_shapes=[
            pltpu.VMEM((4,) + units, BF),
            pltpu.VMEM((3, 4) + units, BF),
            pltpu.VMEM((3, seq_len, width), BF),
            pltpu.VMEM((2, 2, depth - 1, output_rows, width), BF),
            pltpu.VMEM((seq_len, 128), F32),
            pltpu.VMEM((depth - 1, output_rows, 128), F32),
            pltpu.VMEM((2, seq_len, width + 128), BF),
            pltpu.VMEM((2, seq_len, width), BF),
            pltpu.VMEM((2, 2, 2, slice_width, 4 * pair), BF),
            pltpu.VMEM((3, 2 * pairs, seq_len, head), BF),
            pltpu.VMEM((2 * pairs, seq_len, seq_len), BF),
            pltpu.VMEM((2, seq_len, pair), BF),
            pltpu.VMEM((2, seq_len, 1), F32),
            pltpu.VMEM((2, seq_len, 3 * pair), BF),
            pltpu.VMEM((seq_len, width), BF),
            pltpu.VMEM((2, output_rows, width), F32),
            pltpu.VMEM((2, 2, 2, slice_width, 4 * pair), BF),
            pltpu.VMEM((1, 2, 2, slice_width, 2 * pair), BF),
            pltpu.VMEM((2, 1, 2, slice_width, 2 * pair), BF),
            pltpu.VMEM((2, 1, 1, 2, slice_width, 2 * pair), BF),
            pltpu.VMEM((dp, 16, slice_width), F32),
            pltpu.VMEM((dp - 1, 16, slice_width), F32),
            pltpu.VMEM((depth - 1, 8, slice_width), F32),
            pltpu.VMEM((8, width), F32),
            pltpu.SemaphoreType.DMA((96,)),
            pltpu.SemaphoreType.DMA((96,)),
            pltpu.SemaphoreType.DMA((40,)),
        ],
        compiler_params=pltpu.CompilerParams(
            collective_id=1, has_side_effects=True, vmem_limit_bytes=62 * 2**20
        ),
    )(*in_vmem, *in_hbm)


def finish_body(
    gate_ref, up_ref, down_ref, attn_ref, misc_ref, eg_ref, eu_ref, ed_ref, sg_ref, su_ref, sd_ref,
    q_ref, k_ref, v_ref, o_ref, router_ref, sg_rows, su_rows
):
    group = pl.program_id(0)
    many, rows, _ = eg_ref.shape
    for source, routed, shared in (
        (gate_ref, eg_ref, sg_rows.at[pl.ds(pl.multiple_of(group * rows, 8), rows)]),
        (up_ref, eu_ref, su_rows.at[pl.ds(pl.multiple_of(group * rows, 8), rows)]),
        (down_ref, ed_ref, sd_ref),
    ):
        for unit in range(many):
            routed[unit] = source[0, unit].astype(F32)
        shared[...] = source[0, many].astype(F32)

    @pl.when(group == 0)
    def _():
        router_ref[...] = misc_ref[: router_ref.shape[0]]
        pair = attn_ref.shape[2] // 4
        for c in range(2):
            at = slice(c * pair, (c + 1) * pair)
            for kind, out_ref in enumerate((q_ref, k_ref, v_ref)):
                out_ref[:, at] = attn_ref[c, :, kind * pair : (kind + 1) * pair].astype(F32)
            o_ref[at, :] = jnp.transpose(attn_ref[c, :, 3 * pair :].astype(F32))

    for g in range(sg_rows.shape[0] // rows):

        @pl.when(group == g)
        def _(g=g):
            at = slice(g * rows // 128 * 128, (g + 1) * rows // 128 * 128)
            for source, out_ref in ((sg_rows, sg_ref), (su_rows, su_ref)):
                out_ref[:, at] = jnp.transpose(source[at])


def finish_call(columns, gate, up, down, attn, misc):
    groups, units, rows, slice_width = gate.shape
    many, pair = units - 1, attn.shape[2] // 4
    shape = jax.ShapeDtypeStruct

    def whole(*dims):
        return pl.BlockSpec(dims, lambda g: (0,) * len(dims))

    source = pl.BlockSpec((1, units, rows, slice_width), lambda g: (g, 0, 0, 0))
    routed = pl.BlockSpec((many, rows, slice_width), lambda g: (g, 0, 0))
    return call(
        finish_body,
        (groups,),
        [source] * 3 + [whole(*attn.shape), whole(*misc.shape)],
        [routed] * 3
        + [whole(slice_width, groups * rows)] * 2
        + [pl.BlockSpec((rows, slice_width), lambda g: (g, 0))]
        + [whole(slice_width, 2 * pair)] * 3
        + [whole(2 * pair, slice_width), whole(columns, slice_width)],
        [shape((groups * many, rows, slice_width), F32)] * 3
        + [shape((slice_width, groups * rows), F32)] * 2
        + [shape((groups * rows, slice_width), F32)]
        + [shape((slice_width, 2 * pair), F32)] * 3
        + [shape((2 * pair, slice_width), F32), shape((columns, slice_width), F32)],
        0,
        groups * units * rows * slice_width * 18,
        [pltpu.VMEM((groups * rows, slice_width), F32)] * 2,
    )(gate, up, down, attn, misc)


def local_plain(
    dp,
    tokens,
    picture_ids,
    routes,
    slot_order,
    norm_gains,
    w_query,
    w_key,
    w_value,
    w_out,
    qkv_bias,
    router,
    shared_gate,
    shared_up,
    shared_down,
    expert_gate,
    expert_up,
    expert_down,
    out_grad,
):
    seq_len = picture_ids.shape[0]
    local_rows = tokens.shape[0]
    width = tokens.shape[1]
    experts, slice_width, hidden_units = expert_gate.shape
    top_count = routes.shape[1]
    capacity = 5 * seq_len * top_count // (4 * experts)
    heads_local = qkv_bias.shape[1]
    head_width = w_query.shape[1] // heads_local
    pair_heads = heads_local // 2
    pair_width = pair_heads * head_width
    mine_experts = experts // 4
    hidden_pad = -(-hidden_units // 128) * 128

    me = lax.axis_index("dp")
    zi = lax.axis_index("tensor")
    core, xi = me % 2, (me // 2) % 2
    group = me % 4
    bits = []
    while 2 ** (len(bits) + 1) <= dp:
        bits.append(2 ** len(bits))
    upper = bits[2:]

    def swap(array, bit):
        return lax.ppermute(array, "dp", [(i, i ^ bit) for i in range(dp)])

    def bit_of(bit):
        return (me // bit) % 2

    def join(mine, theirs, bit, axis):
        n = mine.shape[axis]
        shape = list(mine.shape)
        shape[axis] = 2 * n
        out = jnp.zeros(shape, mine.dtype)
        out = lax.dynamic_update_slice_in_dim(out, mine, n * bit_of(bit), axis)
        return lax.dynamic_update_slice_in_dim(out, theirs, n * (1 - bit_of(bit)), axis)

    def half(array, which, axis):
        n = array.shape[axis] // 2
        return lax.dynamic_slice_in_dim(array, which * n, n, axis)

    gains_z = lax.all_gather(norm_gains, "tensor", axis=1, tiled=True)
    misc_rows = 16
    bias_width = 3 * pair_heads * qkv_bias.shape[2]
    bias_cores = qkv_bias.reshape(3, 2, -1).swapaxes(0, 1).reshape(2, bias_width)

    def misc_pack(core_bias):
        wide = jnp.zeros((misc_rows, 2 * pair_width), BF)
        wide = wide.at[: experts + 1, :slice_width].set(router.T)
        wide = wide.at[experts + 1, :bias_width].set(core_bias)
        return wide.at[experts + 2 : experts + 4, :slice_width].set(gains_z)

    qk = jnp.concatenate(
        [w.reshape(slice_width, 2, pair_width) for w in (w_query, w_key)], axis=2
    )
    qk = jnp.concatenate(
        [qk, jnp.stack([misc_pack(bias_cores[0]), misc_pack(bias_cores[1])], axis=1)], axis=0
    )
    vo = jnp.concatenate(
        [w.reshape(slice_width, 2, pair_width) for w in (w_value, w_out.T)], axis=2
    )
    tokens_z = lax.all_gather(tokens, "tensor", axis=0, tiled=True)

    def gather_attention(pack, order):
        dims = (1,) * len(bits[1:])
        both = join(pick(pack, core, 1)[None], swap(pick(pack, 1 - core, 1), 1)[None], 1, 0)
        both = both.reshape(dims + both.shape)
        for bit in order:
            axis = len(bits) - 1 - bits.index(bit)
            both = join(both, swap(both, bit), bit, axis)
        return both.reshape((dp,) + both.shape[-2:])

    qk_all = gather_attention(qk, bits[1:])
    vo_full = gather_attention(vo, bits[:0:-1]).reshape(width, 2 * pair_width)
    qk_full = qk_all[:, :slice_width].reshape(width, 2 * pair_width)
    misc = qk_all[:, slice_width:]
    router_full = misc[:, : experts + 1, :slice_width].swapaxes(1, 2).reshape(width, -1)
    gain_rows = misc[:, experts + 2 : experts + 4, :slice_width].swapaxes(0, 1)
    gain_rows = gain_rows.reshape(2, width).astype(F32)
    bias = misc[:, experts + 1, :bias_width].astype(F32)
    bias = bias.reshape(dp, 3 * pair_heads, -1).swapaxes(0, 1).reshape(3, pair_width)

    tokens_sib = swap(tokens_z, 1)
    grad_z = lax.all_gather(out_grad, "tensor", axis=0, tiled=True)

    codes = jnp.concatenate([routes, slot_order], axis=1).T
    codes_x = swap(codes, 2)
    both_codes = swap(jnp.stack([codes, codes_x]), 1)
    codes_a = jnp.stack([codes, both_codes[0]])
    codes_b = jnp.stack([codes_x, both_codes[1]])
    pictures = jnp.stack([picture_ids, swap(picture_ids, 1)])

    def core_units(routed, shared):
        routed = routed.reshape(2, 2, mine_experts, hidden_units, slice_width)
        shared = shared.reshape(2, 2, 1, hidden_units, slice_width)

        def cut(which):
            return jnp.concatenate([pick(routed, which, 1), pick(shared, which, 1)], axis=1)

        return join(cut(core), swap(cut(1 - core), 1), 1, 3)

    def x_units(held):
        return join(pick(held, xi, 0), swap(pick(held, 1 - xi, 0), 2), 2, 2)

    def upper_units(held):
        for bit in upper[:-1]:
            held = join(held, swap(held, bit), bit, 2)
        return held, swap(held, upper[-1])

    def padded(*pairs):
        n = pairs[0][0].shape[-1]
        out = jnp.zeros((mine_experts + 1, len(pairs) * hidden_pad, 2 * n), BF)
        zero = jnp.int32(0)
        for k, (mine, theirs) in enumerate(pairs):
            row = jnp.int32(k * hidden_pad)
            out = lax.dynamic_update_slice(out, mine, (zero, row, n * bit_of(upper[-1])))
            out = lax.dynamic_update_slice(out, theirs, (zero, row, n * (1 - bit_of(upper[-1]))))
        return out

    down_c = core_units(expert_down, shared_down)
    gate_c = core_units(expert_gate.swapaxes(1, 2), shared_gate.T)
    up_c = core_units(expert_up.swapaxes(1, 2), shared_up.T)
    down_x = x_units(down_c)
    gate_x = x_units(gate_c)
    up_x = x_units(up_c)
    grad_x = swap(after(grad_z, up_x), 2)
    down_y = upper_units(down_x)
    gate_y = upper_units(gate_x)
    up_y = upper_units(up_x)

    rows_f = jnp.stack([tokens_z, tokens_sib]).astype(F32)
    qk_full = after(qk_full, down_c, gate_c, up_c)
    first_scale = lax.rsqrt(jnp.mean(rows_f * rows_f, axis=-1, keepdims=True) + EPS)
    first_norm = (rows_f * first_scale * gain_rows[0]).astype(BF)
    qk_pre = einsum("std,df->stf", first_norm, qk_full) + jnp.concatenate([bias[0], bias[1]])
    values = (einsum("std,df->stf", first_norm, vo_full[:, :pair_width]) + bias[2]).astype(BF)
    cos_part, sin_part = rope_tables(seq_len, head_width)
    qk_rot = rotate(
        qk_pre.reshape(2, seq_len, 2 * pair_heads, head_width), cos_part, sin_part
    ).astype(BF)
    qk_rot = after(qk_rot, down_x)
    queries, keys = qk_rot[:, :, :pair_heads], qk_rot[:, :, pair_heads:]
    values = values.reshape(2, seq_len, pair_heads, head_width)
    positions = jnp.arange(seq_len, dtype=jnp.int32)
    allowed = jnp.logical_or(
        positions[None, None, :] <= positions[None, :, None],
        pictures[:, :, None] * pictures[:, None, :] > 0,
    )
    score_scale = head_width ** (-0.5)
    scores = einsum("sqhd,skhd->shqk", queries, keys) * score_scale
    scores = jnp.where(allowed[:, None], scores, -1e30)
    weights = jnp.exp(scores - jnp.max(scores, axis=-1, keepdims=True))
    probs = weights / jnp.sum(weights, axis=-1, keepdims=True)
    probs_low = probs.astype(BF)
    head_mix = einsum("shqk,skhd->sqhd", probs_low, values).astype(BF)
    heads_out = after(head_mix.reshape(2, seq_len, pair_width), gate_x)
    out_weight = vo_full[:, pair_width:]
    attn_part = einsum("sqf,df->sqd", heads_out, out_weight)

    def core_sum(own, sibling):
        return own + swap(sibling.astype(BF), 1).astype(F32)

    def z_scatter(array):
        return lax.psum_scatter(
            array.astype(BF), "tensor", scatter_dimension=0, tiled=True
        ).astype(F32)

    inputs = tokens.astype(F32)
    hidden = inputs + z_scatter(core_sum(attn_part[0], attn_part[1]))
    hidden = after(hidden, up_x, down_y[1])
    second_scale = lax.rsqrt(jnp.mean(hidden * hidden, axis=-1, keepdims=True) + EPS)
    second_unit = hidden * second_scale
    second_norm = (second_unit * gain_rows[1]).astype(BF)
    norm_z = lax.all_gather(second_norm, "tensor", axis=0, tiled=True)
    norm_z = after(norm_z, gate_y[1], grad_x)
    down_all = padded(down_y)
    gateup_all = padded(gate_y, up_y)

    norm_x = swap(norm_z, 2)
    norm_a = jnp.stack([norm_z, swap(norm_z, 1)])
    norm_b = jnp.stack([norm_x, swap(norm_x, 1)])
    grad_a = jnp.stack([grad_z, swap(grad_z, 1)])
    grad_b = jnp.stack([grad_x, swap(grad_x, 1)])

    expert_ids = group * mine_experts + jnp.arange(mine_experts, dtype=jnp.int32)

    router_rows = jnp.pad(router_full.T, ((0, 16 - experts - 1), (0, 0)))
    group_ids = group.astype(jnp.int32).reshape(1)

    def slots_of(codes_in):
        routes_in, slots_in = codes_in[:, None, :top_count], codes_in[:, None, top_count:]
        matches = routes_in == expert_ids[None, :, None, None]
        return jnp.max(jnp.where(matches, slots_in, -1), axis=2)

    def feed(slots, rows, grads):
        slotted, slot_grad, pair, act, terms, pair_s, act_s, inner_s, probs_out = plain_act_call(
            experts, capacity, group_ids, slots, rows, grads, router_rows, gateup_all, down_all
        )
        terms = jnp.concatenate([terms.swapaxes(1, 2), inner_s], axis=-1)
        flat = [a.reshape(mine_experts, -1, a.shape[-1]) for a in (slotted, slot_grad, pair, act)]
        shared = [a.reshape(1, -1, a.shape[-1]) for a in (rows, grads, pair_s, act_s)]
        return (pair, pair_s), (act, act_s), terms, (flat, shared), probs_out

    slots_a, slots_b = slots_of(codes_a), slots_of(codes_b)
    fed_a = feed(slots_a, norm_a, grad_a)
    fed_b = feed(slots_b, norm_b, grad_b)
    columns_a, columns_b = slots_a[..., None], slots_b[..., None]
    row_grad_b = plain_back_call(columns_b, *fed_b[0], gateup_all)
    row_grad_a = plain_back_call(after(columns_a, row_grad_b), *fed_a[0], gateup_all)
    row_out_b = plain_back_call(after(columns_b, row_grad_a), *fed_b[1], down_all)
    row_out_a = plain_back_call(columns_a, *fed_a[1], down_all)

    def spread(terms):
        wide = jnp.zeros(terms.shape[:-1] + (128,), F32)
        wide = lax.dynamic_update_slice_in_dim(
            wide, terms[..., :mine_experts], group * mine_experts, terms.ndim - 1
        )
        return wide.at[..., experts].set(terms[..., mine_experts])

    def group_sum(a, b):
        across = b[0].astype(F32) + swap(b[1].astype(BF), 1).astype(F32)
        near = a[0].astype(F32) + swap(a[1].astype(BF), 1).astype(F32)
        return near + swap(across.astype(BF), 2).astype(F32)

    grad_sum = group_sum(row_grad_a, row_grad_b)
    term_sum = group_sum(spread(fed_a[2]), spread(fed_b[2]))
    packed = z_scatter(jnp.concatenate([grad_sum, term_sum], axis=-1))
    second_grad, gate_sums = packed[:, :width], packed[:, width:]

    data_a, data_b = fed_a[3], fed_b[3]

    def unit_grads(left, right):
        return jnp.concatenate(
            [
                plain_outer_call(
                    hidden_units,
                    hidden_pad,
                    dp,
                    [(data[k][left], data[k][right]) for data in (data_a, data_b)],
                )
                for k in range(2)
            ],
            axis=1,
        )

    def scatter_units(total):
        total = total.reshape((2,) * len(bits) + total.shape[1:])
        for bit in reversed(upper):
            axis = len(bits) - 1 - bits.index(bit)
            sent = half(total, 1 - bit_of(bit), axis)
            kept = half(total, bit_of(bit), axis)
            total = (kept.astype(F32) + swap(sent, bit).astype(F32)).astype(BF)
        total = total.reshape((2, 2) + total.shape[len(bits) :])
        held = join(pick(total, xi, 0)[None], swap(pick(total, 1 - xi, 0), 2)[None], 2, 0)
        return join(pick(held, core, 1)[:, None], swap(pick(held, 1 - core, 1), 1)[:, None], 1, 1)

    def split_units(held):
        routed = held[:, :, :mine_experts].reshape(experts, -1, slice_width)
        shared = held[:, :, mine_experts]
        return routed.astype(F32), shared.astype(F32)

    gateup_sum = scatter_units(unit_grads(2, 0))
    down_sum = scatter_units(unit_grads(3, 1))
    routed_gu, shared_gu = split_units(gateup_sum)
    routed_down, shared_down_sum = split_units(down_sum)
    shared_gu = shared_gu.reshape(4, 2, hidden_units, slice_width)
    egate_sum = routed_gu[:, :hidden_units].swapaxes(1, 2)
    eup_sum = routed_gu[:, hidden_units:].swapaxes(1, 2)
    sgate_sum = shared_gu[:, 0].reshape(-1, slice_width).T
    sup_sum = shared_gu[:, 1].reshape(-1, slice_width).T
    sdown_sum = shared_down_sum.reshape(-1, slice_width)

    row_start = zi * local_rows
    probs_local = lax.dynamic_slice_in_dim(fed_a[4][0], row_start, local_rows, 1).T
    probs_mine, weight_mine = probs_local[:, :experts], probs_local[:, experts]
    route_grad = gate_sums[:, :experts]
    expert_logit_grad = probs_mine * (
        route_grad - jnp.sum(probs_mine * route_grad, axis=-1, keepdims=True)
    )
    weight_logit_grad = gate_sums[:, experts] * weight_mine * (1.0 - weight_mine)
    logits_grad = jnp.concatenate([expert_logit_grad, weight_logit_grad[:, None]], axis=1).astype(
        BF
    )
    second_grad = second_grad + einsum("tf,df->td", logits_grad, router_full)
    gain_two_grad = jnp.sum(second_grad * second_unit, axis=0)
    unit_two = second_grad * gain_rows[1]
    hidden_grad = out_grad.astype(F32) + second_scale * (
        unit_two - second_unit * jnp.mean(unit_two * second_unit, axis=-1, keepdims=True)
    )
    attention_grad = hidden_grad.astype(BF)
    wide_logits = jnp.pad(logits_grad, ((0, 0), (0, 128 - experts - 1)))
    back_z = lax.all_gather(
        jnp.concatenate([attention_grad, wide_logits], axis=1), "tensor", axis=0, tiled=True
    )
    out_sum = after(group_sum(row_out_a, row_out_b), back_z)
    output = (hidden + z_scatter(out_sum)).astype(BF)
    logits_z = back_z[:, width : width + 16]
    back_own = back_z[:, :width]
    back_rows = jnp.stack([back_own, swap(back_own, 1)])

    router_part = einsum("tf,td->fd", logits_z, norm_z)[: experts + 1]

    out_proj = einsum("std,stf->df", back_rows, heads_out)
    mix_grad = einsum("std,df->stf", back_rows, out_weight).astype(BF)
    mix_grad = mix_grad.reshape(2, seq_len, pair_heads, head_width)
    prob_grad = einsum("sqhd,skhd->shqk", mix_grad, values)
    score_grad = (
        probs * (prob_grad - jnp.sum(probs * prob_grad, axis=-1, keepdims=True))
    ).astype(BF)
    query_rot = einsum("shqk,skhd->sqhd", score_grad, keys) * score_scale
    key_rot = einsum("shqk,sqhd->skhd", score_grad, queries) * score_scale
    value_grad = einsum("shqk,sqhd->skhd", probs_low, mix_grad)
    qk_grad = rotate(jnp.concatenate([query_rot, key_rot], axis=2), cos_part, -sin_part)
    qk_grad = qk_grad.astype(BF).reshape(2, seq_len, 2 * pair_width)
    v_grad = value_grad.astype(BF).reshape(2, seq_len, pair_width)
    first_part = einsum("stf,df->std", qk_grad, qk_full) + einsum(
        "stf,df->std", v_grad, vo_full[:, :pair_width]
    )
    first_grad = z_scatter(core_sum(first_part[0], first_part[1]))

    gain_one_grad = jnp.sum(first_part * (rows_f * first_scale), axis=(0, 1))
    bias_part = jnp.concatenate(
        [jnp.sum(qk_grad.astype(F32), axis=(0, 1)), jnp.sum(v_grad.astype(F32), axis=(0, 1))]
    )
    bias_part = bias_part.reshape(3 * pair_heads, dp, -1).swapaxes(0, 1).reshape(dp, 1, -1)
    gain_part = jnp.stack([gain_one_grad, gain_two_grad]).reshape(2, dp, slice_width)

    def wide_rows(rows):
        return jnp.pad(rows, ((0, 0), (0, 0), (0, 2 * pair_width - rows.shape[2])))

    misc_part = jnp.concatenate(
        [
            wide_rows(router_part.reshape(experts + 1, dp, slice_width).swapaxes(0, 1)),
            wide_rows(bias_part),
            wide_rows(gain_part.swapaxes(0, 1)),
            jnp.zeros((dp, misc_rows - experts - 4, 2 * pair_width), F32),
        ],
        axis=1,
    )
    qk_total = einsum("std,stf->df", first_norm, qk_grad).reshape(dp, slice_width, -1)
    qk_total = jnp.concatenate([qk_total, misc_part], axis=1)
    vo_total = jnp.concatenate([einsum("std,stf->df", first_norm, v_grad), out_proj], axis=1)
    vo_total = vo_total.reshape(dp, slice_width, -1)

    def scatter_attention(total, order):
        total = total.reshape((2,) * len(bits) + total.shape[1:])
        for bit in order:
            axis = len(bits) - 1 - bits.index(bit)
            sent = half(total, 1 - bit_of(bit), axis).astype(BF)
            total = half(total, bit_of(bit), axis) + swap(sent, bit).astype(F32)
        total = total.reshape((2,) + total.shape[-2:]).astype(BF)
        return pick(total, core, 0), swap(pick(total, 1 - core, 0), 1)

    def columns_of(mine, theirs):
        held = join(mine[:slice_width, None], theirs[:slice_width, None], 1, 1)
        first, second = held[..., :pair_width], held[..., pair_width:]
        return (
            first.reshape(slice_width, -1).astype(F32),
            second.reshape(slice_width, -1).astype(F32),
        )

    qk_mine, qk_theirs = scatter_attention(qk_total, bits[:0:-1])
    vo_mine, vo_theirs = scatter_attention(vo_total, bits[1:])
    qk_sums = columns_of(qk_mine, qk_theirs)
    vo_sums = columns_of(vo_mine, vo_theirs)
    misc_mine = qk_mine[slice_width:].astype(F32)
    misc_theirs = qk_theirs[slice_width:].astype(F32)
    misc_sum = misc_mine + misc_theirs
    router_sum = misc_sum[: experts + 1, :slice_width].T
    bias_sums = join(
        misc_mine[experts + 1, :bias_width].reshape(3, 1, pair_heads, -1),
        misc_theirs[experts + 1, :bias_width].reshape(3, 1, pair_heads, -1),
        1,
        1,
    ).reshape(3, heads_local, -1)
    gain_sums = lax.all_gather(
        misc_sum[experts + 2 : experts + 4, :slice_width], "tensor", axis=0, tiled=False
    )
    tensor = gain_sums.shape[0]
    gain_sums = jnp.sum(gain_sums, axis=0).reshape(2, tensor, -1)
    gain_sums = pick(gain_sums, zi, 1)

    unit_mine = inputs * lax.rsqrt(jnp.mean(inputs * inputs, axis=-1, keepdims=True) + EPS)
    scale_mine = lax.rsqrt(jnp.mean(inputs * inputs, axis=-1, keepdims=True) + EPS)
    unit_one = first_grad * gain_rows[0]
    input_grad = hidden_grad + scale_mine * (
        unit_one - unit_mine * jnp.mean(unit_one * unit_mine, axis=-1, keepdims=True)
    )
    return (
        output,
        input_grad.astype(BF),
        gain_sums,
        qk_sums[0],
        qk_sums[1],
        vo_sums[0],
        vo_sums[1].T,
        bias_sums,
        router_sum,
        sgate_sum,
        sup_sum,
        sdown_sum,
        egate_sum,
        eup_sum,
        routed_down,
    )


def local_fused(
    dp,
    depth,
    tokens,
    picture_ids,
    routes,
    slot_order,
    norm_gains,
    w_query,
    w_key,
    w_value,
    w_out,
    qkv_bias,
    router,
    shared_gate,
    shared_up,
    shared_down,
    expert_gate,
    expert_up,
    expert_down,
    out_grad,
):
    seq_len = picture_ids.shape[0]
    local_rows = tokens.shape[0]
    width = tokens.shape[1]
    experts, slice_width, hidden_units = expert_gate.shape
    heads_local = qkv_bias.shape[1]
    head_width = w_query.shape[1] // heads_local
    pair_heads = heads_local // 2
    pair_width = pair_heads * head_width
    mine_experts = experts // 4
    hidden_pad = -(-hidden_units // 128) * 128

    zi = lax.axis_index("tensor")
    codes = jnp.concatenate([routes.T, slot_order.T, picture_ids[None]], axis=0)
    codes = jnp.pad(codes, ((0, 16 - codes.shape[0]), (0, 0)))
    bias_cores = qkv_bias.reshape(3, 2, -1).swapaxes(0, 1).reshape(2, -1)
    bias_width = bias_cores.shape[1]
    misc = jnp.zeros((16, slice_width), F32)
    misc = misc.at[: experts + 1].set(router.T.astype(F32))
    misc = misc.at[experts + 1 : experts + 3, :bias_width].set(bias_cores.astype(F32))
    gains = lax.dynamic_update_slice(
        jnp.zeros((8, slice_width), F32),
        norm_gains.astype(F32),
        (jnp.int32(0), zi * norm_gains.shape[1]),
    )
    cos_part, sin_part = rope_arrays(seq_len, head_width)
    cos_rows = np.concatenate([cos_part, cos_part], axis=1)
    sin_rows = np.concatenate([-sin_part, sin_part], axis=1)
    (
        hidden,
        norm_all,
        grads_all,
        gateup_all,
        down_all,
        codes_all,
        router_rows,
        gain_rows,
        tok,
        attn_weights,
        qkv,
        probs_low,
        heads_out,
    ) = forward_call(
        dp,
        depth,
        experts,
        head_width,
        (codes, misc, gains, cos_rows, sin_rows),
        (tokens, out_grad, w_query, w_key, w_value, w_out.T),
        (
            expert_gate.swapaxes(1, 2),
            expert_up.swapaxes(1, 2),
            expert_down,
            shared_gate,
            shared_up,
            shared_down.reshape(4, hidden_units, slice_width),
        ),
    )
    gateup_all = gateup_all.reshape(mine_experts + 1, 2 * hidden_pad, width)
    down_all = down_all.reshape(mine_experts + 1, hidden_pad, width)
    (
        output,
        terms,
        probs_mine,
        grad_own,
        grad_sib,
        grad_far,
        gate_total,
        up_total,
        down_total,
        gate_in,
    ) = middle_call(
        dp,
        depth,
        experts,
        routes.shape[1],
        hidden_units,
        hidden,
        codes_all,
        router_rows,
        (norm_all, grads_all, gateup_all, down_all),
    )
    input_grad, gate_sum, up_sum, down_sum, attn_sum, misc_sum, gains_sum = backward_call(
        dp,
        depth,
        experts,
        head_width,
        (terms, probs_mine, router_rows, gain_rows, cos_rows, sin_rows, hidden, out_grad),
        (grad_own, grad_sib, grad_far, gate_in, gate_total, up_total, down_total)
        + (tok, attn_weights, qkv, probs_low, heads_out, norm_all),
    )

    egate_sum, eup_sum, edown_sum, sgate_sum, sup_sum, sdown_sum, *attn_sums, router_sum = finish_call(
        experts + 1, gate_sum, up_sum, down_sum, attn_sum, misc_sum
    )
    bias_sums = misc_sum[experts + 1 : experts + 3, :bias_width].reshape(2, 3, pair_heads, -1)
    bias_sums = bias_sums.swapaxes(0, 1).reshape(3, heads_local, -1)
    piece = norm_gains.shape[1]
    gain_sums = lax.dynamic_slice(gains_sum[3:5], (jnp.int32(0), zi * piece), (2, piece))
    return (
        output,
        input_grad,
        gain_sums,
        *attn_sums,
        bias_sums,
        router_sum.T,
        sgate_sum,
        sup_sum,
        sdown_sum,
        egate_sum.swapaxes(1, 2),
        eup_sum.swapaxes(1, 2),
        edown_sum,
    )


def solution(mesh):
    dp, depth = mesh.shape["dp"], mesh.shape["tensor"]

    def body(*arrays):
        if arrays[5].shape[0] % 128 == 0 and dp == 8 and depth == 4:
            return local_fused(dp, depth, *arrays)
        return local_plain(dp, *arrays)

    return jax.shard_map(
        body,
        mesh=mesh,
        in_specs=(
            P(("dp", "tensor"), None),
            P("dp"),
            P("dp", None),
            P("dp", None),
            P(None, ("dp", "tensor")),
            P("dp", "tensor"),
            P("dp", "tensor"),
            P("dp", "tensor"),
            P("tensor", "dp"),
            P(None, "tensor", "dp"),
            P("dp", None),
            P("dp", "tensor"),
            P("dp", "tensor"),
            P("tensor", "dp"),
            P(None, "dp", "tensor"),
            P(None, "dp", "tensor"),
            P(None, "tensor", "dp"),
            P(("dp", "tensor"), None),
        ),
        out_specs=(
            P(("dp", "tensor"), None),
            P(("dp", "tensor"), None),
            P(None, ("dp", "tensor")),
            P("dp", "tensor"),
            P("dp", "tensor"),
            P("dp", "tensor"),
            P("tensor", "dp"),
            P(None, "tensor", "dp"),
            P("dp", None),
            P("dp", "tensor"),
            P("dp", "tensor"),
            P("tensor", "dp"),
            P(None, "dp", "tensor"),
            P(None, "dp", "tensor"),
            P(None, "tensor", "dp"),
        ),
        check_vma=False,
    )
```
